32 devices in a mesh: dp: 8 (over z, x), tensor: 4 (over y, core).
Axes of the slice: x: 2, y: 2, z: 4, core: 2. Of those that a mesh axis runs over, the one named last changes fastest.
Arguments:
- clips: bfloat16 [8, 16, 256, 768], P('dp', 'tensor'), may hold values from -6 to 6
- cotangent: bfloat16 [8, 16, 256, 768], P('dp', 'tensor'), may hold values from -6 to 6
- timesteps: int32 [8], P('dp'), may hold values from 0 to 999
- labels: int32 [8], P('dp'), may hold values from 0 to 100
- time_table: float32 [1000, 768], replicated, may hold values from -5 to 5
- class_table: float32 [101, 768], replicated, may hold values from -5 to 5
- attention_weights: float32 [2, 4, 768, 768], P(None, None, 'dp', 'tensor'), may hold values from -0.21650635 to 0.21650635
- attention_first: float32 [2, 4, 768, 768], P(None, None, 'dp', 'tensor'), may hold values from -32 to 32
- attention_second: float32 [2, 4, 768, 768], P(None, None, 'dp', 'tensor'), may hold values from 1.47456 to 23.59296
- ffn_weights: float32 [2, 2, 768, 3072], P(None, None, 'dp', 'tensor'), may hold values from -0.21875 to 0.21875
- ffn_first: float32 [2, 2, 768, 3072], P(None, None, 'dp', 'tensor'), may hold values from -32 to 32
- ffn_second: float32 [2, 2, 768, 3072], P(None, None, 'dp', 'tensor'), may hold values from 1.47456 to 23.59296
- modulation_weights: float32 [2, 768, 4608], P(None, ('dp', 'tensor')), may hold values from -0.21875 to 0.21875
- modulation_first: float32 [2, 768, 4608], P(None, ('dp', 'tensor')), may hold values from -32 to 32
- modulation_second: float32 [2, 768, 4608], P(None, ('dp', 'tensor')), may hold values from 1.47456 to 23.59296
- bias_vectors: float32 [2, 10752], P(None, ('dp', 'tensor')), may hold values from -1 to 1
- bias_first: float32 [2, 10752], P(None, ('dp', 'tensor')), may hold values from -32 to 32
- bias_second: float32 [2, 10752], P(None, ('dp', 'tensor')), may hold values from 1.47456 to 23.59296
Outputs:
- output: bfloat16 [8, 16, 256, 768], P('dp', 'tensor')
- input_grad: float32 [8, 16, 256, 768], P('dp', 'tensor')
- cond_grad: float32 [8, 768], P('dp')
- attention_new: float32 [2, 4, 768, 768], P(None, None, 'dp', 'tensor')
- attention_first_new: float32 [2, 4, 768, 768], P(None, None, 'dp', 'tensor')
- attention_second_new: float32 [2, 4, 768, 768], P(None, None, 'dp', 'tensor')
- attention_copy: bfloat16 [2, 4, 768, 768], P(None, None, 'dp', 'tensor')
- ffn_new: float32 [2, 2, 768, 3072], P(None, None, 'dp', 'tensor')
- ffn_first_new: float32 [2, 2, 768, 3072], P(None, None, 'dp', 'tensor')
- ffn_second_new: float32 [2, 2, 768, 3072], P(None, None, 'dp', 'tensor')
- ffn_copy: bfloat16 [2, 2, 768, 3072], P(None, None, 'dp', 'tensor')
- modulation_new: float32 [2, 768, 4608], P(None, ('dp', 'tensor'))
- modulation_first_new: float32 [2, 768, 4608], P(None, ('dp', 'tensor'))
- modulation_second_new: float32 [2, 768, 4608], P(None, ('dp', 'tensor'))
- modulation_copy: bfloat16 [2, 768, 4608], P(None, ('dp', 'tensor'))
- bias_new: float32 [2, 10752], P(None, ('dp', 'tensor'))
- bias_first_new: float32 [2, 10752], P(None, ('dp', 'tensor'))
- bias_second_new: float32 [2, 10752], P(None, ('dp', 'tensor'))
- bias_copy: bfloat16 [2, 10752], P(None, ('dp', 'tensor'))
The draws below stay inside these ranges and needn't reach their ends.
All inputs are finite; a program needn't handle non-finite values.
Results may differ from the reference program's by a relative error of at most 0.018.
Values may be sent and summed in bfloat16 or wider, within the bound.
A program may use at most 320 MiB of HBM per device.

```python
import math
import jax
import jax.numpy as jnp
from jax import lax

D = 768
HD = 64
FF = 3072
NSTEPS = 1000
NCLASS = 101
FRAMES = 16
PATCHES = 256
LAYERS = 2
STEP = 10
CLIPS = 8
NB = 10752


def draw_attention_weights(key, part):
    key = jax.random.fold_in(key, 17)
    base = jax.random.truncated_normal(key, -2.0, 2.0, (LAYERS, 4, D, D), jnp.float32)
    factor = jnp.concatenate([jnp.ones((3,), jnp.float32), jnp.full((1,), 3.0, jnp.float32)]).reshape(1, 4, 1, 1)
    return base * factor / jnp.sqrt(jnp.float32(D))


def set_ends(values, key, low, largest):
    longest = values.shape.index(max(values.shape))
    spots = []
    for shift in (0, 1):
        where = [jax.random.randint(jax.random.fold_in(key, axis), (), 0, length) for axis, length in enumerate(values.shape)]
        where[longest] = (where[longest] + shift) % values.shape[longest]
        spots.append(tuple(where))
    return values.at[spots[0]].set(low).at[spots[1]].set(largest)


def levels(key, extent, shards, smallest, largest):
    def one(position, blocks):
        draws = jax.random.uniform(jax.random.fold_in(jax.random.fold_in(key, 6), position), (blocks,), jnp.float32, smallest / len(shards), largest / len(shards))
        return jnp.repeat(jnp.exp(draws), extent[position] // blocks).reshape((-1,) + (1,) * (len(extent) - position - 1))

    level = one(*shards[0])
    for cut in shards[1:]:
        level = level * one(*cut)
    return level


def noise(key, dims, scale, limit, shards=(), kind=jnp.bfloat16):
    values = scale * jax.random.normal(key, dims, jnp.float32)
    if shards:
        values = values * levels(key, dims, shards, -0.22, 0.18)
    return jnp.clip(values, -limit, limit).astype(kind)


def setup_inputs(seed: int = 0) -> dict:
    seeds = jax.random.split(jax.random.key(seed), 19)
    clips = noise(seeds[0], (CLIPS, FRAMES, PATCHES, D), 1.0, 6.0, ((0, 8), (1, 4)))
    cotangent = noise(seeds[1], (CLIPS, FRAMES, PATCHES, D), 1.0, 6.0, ((0, 8), (1, 4)))
    timesteps = set_ends(jax.random.randint(seeds[2], (CLIPS,), 0, NSTEPS), jax.random.fold_in(seeds[2], 1), 0, NSTEPS - 1).astype(jnp.int32)
    labels = set_ends(jax.random.randint(seeds[3], (CLIPS,), 0, NCLASS), jax.random.fold_in(seeds[3], 1), 0, NCLASS - 1).astype(jnp.int32)
    time_table = noise(seeds[4], (NSTEPS, D), 0.7, 5.0, (), jnp.float32)
    class_table = noise(seeds[5], (NCLASS, D), 0.7, 5.0, (), jnp.float32)
    attention_weights = draw_attention_weights(jax.random.fold_in(seeds[18], 71), 0)
    attention_first = noise(seeds[7], (LAYERS, 4, D, D), (0.033 * (CLIPS * FRAMES * PATCHES) ** 0.5), 32.0, ((2, 8), (3, 4)), jnp.float32)
    attention_second = jnp.clip(jnp.exp(math.log(23.59296) - 2.7725887 * jax.random.uniform(seeds[8], (LAYERS, 4, D, D), jnp.float32) ** levels(seeds[8], (LAYERS, 4, D, D), ((2, 8), (3, 4)), -0.2, 0.2)), 1.47456, 23.59296)
    ffn_weights = noise(seeds[9], (LAYERS, 2, D, FF), D ** -0.5, 0.21875, ((2, 8), (3, 4)), jnp.float32)
    ffn_first = noise(seeds[10], (LAYERS, 2, D, FF), (0.033 * (CLIPS * FRAMES * PATCHES) ** 0.5), 32.0, ((2, 8), (3, 4)), jnp.float32)
    ffn_second = jnp.clip(jnp.exp(math.log(23.59296) - 2.7725887 * jax.random.uniform(seeds[11], (LAYERS, 2, D, FF), jnp.float32) ** levels(seeds[11], (LAYERS, 2, D, FF), ((2, 8), (3, 4)), -0.2, 0.2)), 1.47456, 23.59296)
    modulation_weights = noise(seeds[12], (LAYERS, D, 6 * D), D ** -0.5, 0.21875, ((1, 32),), jnp.float32)
    modulation_first = noise(seeds[13], (LAYERS, D, 6 * D), (0.033 * (CLIPS * FRAMES * PATCHES) ** 0.5), 32.0, ((1, 32),), jnp.float32)
    modulation_second = jnp.clip(jnp.exp(math.log(23.59296) - 2.7725887 * jax.random.uniform(seeds[14], (LAYERS, D, 6 * D), jnp.float32) ** levels(seeds[14], (LAYERS, D, 6 * D), ((1, 32),), -0.2, 0.2)), 1.47456, 23.59296)
    bias_vectors = noise(seeds[15], (LAYERS, NB), 0.2, 1.0, ((1, 32),), jnp.float32)
    bias_first = noise(seeds[16], (LAYERS, NB), (0.033 * (CLIPS * FRAMES * PATCHES) ** 0.5), 32.0, ((1, 32),), jnp.float32)
    bias_second = jnp.clip(jnp.exp(math.log(23.59296) - 2.7725887 * jax.random.uniform(seeds[17], (LAYERS, NB), jnp.float32) ** levels(seeds[17], (LAYERS, NB), ((1, 32),), -0.2, 0.2)), 1.47456, 23.59296)
    return {"clips": clips, "cotangent": cotangent, "timesteps": timesteps, "labels": labels, "time_table": time_table, "class_table": class_table, "attention_weights": attention_weights, "attention_first": attention_first, "attention_second": attention_second, "ffn_weights": ffn_weights, "ffn_first": ffn_first, "ffn_second": ffn_second, "modulation_weights": modulation_weights, "modulation_first": modulation_first, "modulation_second": modulation_second, "bias_vectors": bias_vectors, "bias_first": bias_first, "bias_second": bias_second}


BETA_ONE = 0.9
BETA_TWO = 0.999
ADAM_EPS = 1e-08
MATRIX_RATE = 0.04
VECTOR_RATE = 0.2
MATRIX_DECAY = 0.1
NORM_EPS = 1e-06

@jax.custom_vjp
def low(v):
    return lax.optimization_barrier(v.astype(jnp.bfloat16)).astype(jnp.float32)

@jax.custom_vjp
def low_back(v):
    return v

def low_keep(v):
    return (low(v), None)

def low_pass(kept, grad):
    return (grad,)

def back_keep(v):
    return (v, None)

def back_low(kept, grad):
    return (low(grad),)
low.defvjp(low_keep, low_pass)
low_back.defvjp(back_keep, back_low)

def precise(form, left, right):
    return jnp.einsum(form, left, right, precision=lax.Precision.HIGHEST)

def modulate_norm(stream, shift, scale):
    average = lax.optimization_barrier(jnp.mean(stream, axis=-1, keepdims=True))
    centred = stream - average
    spread = lax.optimization_barrier(jnp.mean(centred * centred, axis=-1, keepdims=True))
    return centred * lax.rsqrt(spread + NORM_EPS) * (1.0 + scale) + shift

def einsum_forms(temporal):
    if temporal:
        return ('fphd,gphd->phfg', 'phfg,gphd->fphd')
    return ('fphd,fqhd->fhpq', 'fhpq,fqhd->fphd')

def block(stream, modrow, attention, ffn, bias, temporal):
    frames, patches, width = stream.shape
    hidden_width = ffn.shape[-1]
    rows = modrow.reshape(6, width)
    normed = low(modulate_norm(stream, rows[0], rows[1]))
    head_size = HD
    head_shape = (frames, patches, width // head_size, head_size)
    query = precise('fpd,de->fpe', normed, attention[0]) + bias[0:width]
    key = precise('fpd,de->fpe', normed, attention[1])
    value = precise('fpd,de->fpe', normed, attention[2]) + bias[width:2 * width]
    query = low(low_back(query)).reshape(head_shape)
    key = low(low_back(key)).reshape(head_shape)
    value = low(low_back(value)).reshape(head_shape)
    score_form, mix_form = einsum_forms(temporal)
    scores = low_back(precise(score_form, query, key) * head_size ** (-0.5))
    highest = lax.optimization_barrier(jnp.max(scores, axis=-1, keepdims=True))
    raised = jnp.exp(scores - highest)
    probs = low(raised / lax.optimization_barrier(jnp.sum(raised, axis=-1, keepdims=True)))
    mixed = low(low_back(precise(mix_form, probs, value))).reshape(frames, patches, width)
    branch = low_back(precise('fpj,ij->fpi', mixed, attention[3]) + bias[2 * width:3 * width])
    middle = stream + rows[2] * branch
    normed_second = low(modulate_norm(middle, rows[3], rows[4]))
    hidden = low_back(precise('fpd,dh->fph', normed_second, ffn[0]) + bias[3 * width:3 * width + hidden_width])
    active = low(jax.nn.gelu(hidden, approximate=True))
    down = low_back(precise('fph,dh->fpd', active, ffn[1]) + bias[3 * width + hidden_width:4 * width + hidden_width])
    return middle + rows[5] * down

def forward(inputs, embed, attention_weights, ffn_weights, modulation_weights, bias_vectors):
    attention = low(attention_weights)
    ffn = low(ffn_weights)
    modulation = low(modulation_weights)
    bias = low(bias_vectors)
    cond_act = low(jax.nn.silu(embed))
    width = inputs.shape[-1]
    mod_start = 4 * width + ffn.shape[-1]
    layers = attention.shape[0]
    mods = jnp.stack([low_back(jnp.dot(cond_act, modulation[layer], precision=lax.Precision.HIGHEST) + bias[layer, mod_start:]) for layer in range(layers)], axis=1)

    def clip_pass(item):
        stream, modclip = item
        for layer in range(layers):
            stream = block(stream, modclip[layer], attention[layer], ffn[layer], bias[layer], layer % 2 == 1)
        return stream
    return lax.map(jax.checkpoint(clip_pass), (inputs, mods))

def adam_update(weight, first, second, grad, rate, decay):
    first_new = BETA_ONE * first + (1.0 - BETA_ONE) * grad
    second_new = BETA_TWO * second + (1.0 - BETA_TWO) * grad * grad
    corrected = first_new / (1.0 - BETA_ONE ** STEP) / (jnp.sqrt(second_new / (1.0 - BETA_TWO ** STEP)) + ADAM_EPS)
    weight_new = weight - rate * (corrected + decay * weight)
    return (weight_new, first_new, second_new, weight_new.astype(jnp.bfloat16))

def reference(clips, cotangent, timesteps, labels, time_table, class_table, attention_weights, attention_first, attention_second, ffn_weights, ffn_first, ffn_second, modulation_weights, modulation_first, modulation_second, bias_vectors, bias_first, bias_second):
    embed = time_table[timesteps] + class_table[labels]
    result, pull = jax.vjp(forward, clips.astype(jnp.float32), embed, attention_weights, ffn_weights, modulation_weights, bias_vectors)
    input_grad, cond_grad, attention_grad, ffn_grad, modulation_grad, bias_grad = pull(cotangent.astype(jnp.float32))
    attention_new, attention_first_new, attention_second_new, attention_copy = adam_update(attention_weights, attention_first, attention_second, attention_grad, MATRIX_RATE, MATRIX_DECAY)
    ffn_new, ffn_first_new, ffn_second_new, ffn_copy = adam_update(ffn_weights, ffn_first, ffn_second, ffn_grad, MATRIX_RATE, MATRIX_DECAY)
    modulation_new, modulation_first_new, modulation_second_new, modulation_copy = adam_update(modulation_weights, modulation_first, modulation_second, modulation_grad, MATRIX_RATE, MATRIX_DECAY)
    bias_new, bias_first_new, bias_second_new, bias_copy = adam_update(bias_vectors, bias_first, bias_second, bias_grad, VECTOR_RATE, 0.0)
    return (result.astype(jnp.bfloat16), input_grad, cond_grad, attention_new, attention_first_new, attention_second_new, attention_copy, ffn_new, ffn_first_new, ffn_second_new, ffn_copy, modulation_new, modulation_first_new, modulation_second_new, modulation_copy, bias_new, bias_first_new, bias_second_new, bias_copy)
```

```python
from functools import partial

import jax
import jax.numpy as jnp
from jax import lax
from jax.sharding import PartitionSpec as P

HD = 64
STEP = 10
BETA_ONE = 0.9
BETA_TWO = 0.999
ADAM_EPS = 1e-08
MATRIX_RATE = 0.04
VECTOR_RATE = 0.2
MATRIX_DECAY = 0.1
NORM_EPS = 1e-06
BOTH = ("dp", "tensor")


def einsum_forms(temporal):
    if temporal:
        return ("fphd,gphd->phfg", "phfg,gphd->fphd", "phfg,fphd->gphd")
    return ("fphd,fqhd->fhpq", "fhpq,fqhd->fphd", "fhpq,fphd->fqhd")


def modulate_norm(stream, shift, scale):
    average = jnp.mean(stream, axis=-1, keepdims=True)
    centred = stream - average
    spread = jnp.mean(centred * centred, axis=-1, keepdims=True)
    return centred * lax.rsqrt(spread + NORM_EPS) * (1.0 + scale) + shift


def attend(query, key, value, temporal):
    score_form, mix_form, back_form = einsum_forms(temporal)
    scale = query.shape[-1] ** (-0.5)
    scores = jnp.einsum(score_form, query, key, preferred_element_type=jnp.float32) * scale
    highest = jnp.max(scores, axis=-1, keepdims=True)
    raised = jnp.exp(scores - highest)
    total = jnp.sum(raised, axis=-1, keepdims=True)
    probs = (raised / total).astype(jnp.bfloat16)
    mixed = jnp.einsum(mix_form, probs, value, preferred_element_type=jnp.float32)
    return mixed.astype(jnp.bfloat16), highest + jnp.log(total)


def attend_back(query, key, value, logsum, grad_mixed, temporal):
    score_form, mix_form, back_form = einsum_forms(temporal)
    scale = query.shape[-1] ** (-0.5)
    scores = jnp.einsum(score_form, query, key, preferred_element_type=jnp.float32) * scale
    probs = jnp.exp(scores - logsum)
    grad_probs = jnp.einsum(score_form, grad_mixed, value, preferred_element_type=jnp.float32)
    grad_value = jnp.einsum(
        back_form, probs.astype(jnp.bfloat16), grad_mixed, preferred_element_type=jnp.float32
    )
    inner = jnp.sum(grad_probs * probs, axis=-1, keepdims=True)
    grad_scores = (probs * (grad_probs - inner)).astype(jnp.bfloat16)
    grad_query = jnp.einsum(mix_form, grad_scores, key, preferred_element_type=jnp.float32) * scale
    grad_key = jnp.einsum(back_form, grad_scores, query, preferred_element_type=jnp.float32) * scale
    return (grad_query, grad_key, grad_value)


def dot32(form, left, right):
    return jnp.einsum(form, left, right, preferred_element_type=jnp.float32)


def layer_forward(stream, mod, weights, bias, temporal):
    packed, up, down_w = weights
    ranks, width = packed.shape[0], packed.shape[1]
    cols = packed.shape[2] // 4
    frames, patches = stream.shape[:2]
    hidden_width = ranks * up.shape[2]
    normed = modulate_norm(stream, mod[0], mod[1]).astype(jnp.bfloat16)
    projected = dot32("fpd,tde->fpte", normed, packed[:, :, : 3 * cols])
    heads = (frames, patches, width // HD, HD)
    flat = (frames, patches, width)
    query = projected[..., :cols].reshape(flat) + bias[:width]
    key = projected[..., cols : 2 * cols].reshape(flat)
    value = projected[..., 2 * cols :].reshape(flat) + bias[width : 2 * width]
    query, key, value = (v.astype(jnp.bfloat16).reshape(heads) for v in (query, key, value))
    mixed, logsum = attend(query, key, value, temporal)
    mixed = mixed.reshape(frames, patches, ranks, cols)
    branch = dot32("fptj,tij->fpi", mixed, packed[:, :, 3 * cols :]) + bias[2 * width : 3 * width]
    middle = stream + mod[2] * branch
    second = modulate_norm(middle, mod[3], mod[4]).astype(jnp.bfloat16)
    bias_up = bias[3 * width : 3 * width + hidden_width].reshape(ranks, -1)
    hidden = dot32("fpd,tdh->fpth", second, up) + bias_up
    active = jax.nn.gelu(hidden, approximate=True).astype(jnp.bfloat16)
    bias_down = bias[3 * width + hidden_width : 4 * width + hidden_width]
    down = dot32("fpth,tdh->fpd", active, down_w) + bias_down
    result = middle + mod[5] * down
    saved = (stream, normed, query, key, value, logsum, mixed, branch, middle, second, hidden, active, down)
    return result, saved


def layer_backward(saved, grad_result, mod, weights, temporal):
    stream, normed, query, key, value, logsum, mixed, branch, middle, second, hidden, active, down = saved
    packed, up, down_w = weights
    ranks, width = packed.shape[0], packed.shape[1]
    cols = packed.shape[2] // 4
    frames, patches = stream.shape[:2]
    tokens = (0, 1)
    grad_down = (mod[5] * grad_result).astype(jnp.bfloat16)
    grad_gate_ffn = jnp.sum(grad_result * down, axis=tokens)
    grad_active = dot32("fpd,tdh->fpth", grad_down, down_w)
    gelu_value, gelu_pull = jax.vjp(partial(jax.nn.gelu, approximate=True), hidden)
    grad_hidden = gelu_pull(grad_active)[0].astype(jnp.bfloat16)
    grad_up_w = dot32("fpd,fpth->tdh", second, grad_hidden)
    grad_down_w = dot32("fpd,fpth->tdh", grad_down, active)
    grad_second = dot32("fpth,tdh->fpd", grad_hidden, up)
    second_value, second_pull = jax.vjp(modulate_norm, middle, mod[3], mod[4])
    grad_middle, grad_shift_ffn, grad_scale_ffn = second_pull(grad_second)
    grad_middle = grad_middle + grad_result
    grad_branch = (mod[2] * grad_middle).astype(jnp.bfloat16)
    grad_gate_attn = jnp.sum(grad_middle * branch, axis=tokens)
    grad_mixed = dot32("fpi,tij->fptj", grad_branch, packed[:, :, 3 * cols :]).astype(jnp.bfloat16)
    grad_out_w = dot32("fpi,fptj->tij", grad_branch, mixed)
    grads = attend_back(query, key, value, logsum, grad_mixed.reshape(query.shape), temporal)
    grad_project = jnp.concatenate(
        [g.astype(jnp.bfloat16).reshape(frames, patches, ranks, cols) for g in grads], axis=-1
    )
    grad_project_w = dot32("fpd,fpte->tde", normed, grad_project)
    grad_normed = dot32("fpte,tde->fpd", grad_project, packed[:, :, : 3 * cols])
    first_value, first_pull = jax.vjp(modulate_norm, stream, mod[0], mod[1])
    grad_stream, grad_shift_attn, grad_scale_attn = first_pull(grad_normed)
    grad_stream = grad_stream + grad_middle
    grad_mod = jnp.concatenate(
        [grad_shift_attn, grad_scale_attn, grad_gate_attn, grad_shift_ffn, grad_scale_ffn, grad_gate_ffn]
    )
    grad_weights = jnp.stack(
        [jnp.concatenate([grad_project_w, grad_out_w], axis=-1), grad_up_w, grad_down_w]
    )
    token_sum = lambda v: jnp.sum(v, axis=tokens, dtype=jnp.float32).reshape(-1)
    grad_bias = jnp.concatenate(
        [
            token_sum(grad_project[..., :cols]),
            token_sum(grad_project[..., 2 * cols :]),
            token_sum(grad_branch),
            token_sum(grad_hidden),
            token_sum(grad_down),
        ]
    )
    return grad_stream, grad_mod, grad_weights, grad_bias


def adam_update(weight, first, second, grad, rate, decay):
    first_new = BETA_ONE * first + (1.0 - BETA_ONE) * grad
    second_new = BETA_TWO * second + (1.0 - BETA_TWO) * grad * grad
    corrected = (
        first_new
        / (1.0 - BETA_ONE**STEP)
        / (jnp.sqrt(second_new / (1.0 - BETA_TWO**STEP)) + ADAM_EPS)
    )
    weight_new = weight - rate * (corrected + decay * weight)
    return (weight_new, first_new, second_new, weight_new.astype(jnp.bfloat16))


def to_patches(stream):
    return lax.all_to_all(stream, "tensor", split_axis=1, concat_axis=0, tiled=True)


def to_frames(stream):
    return lax.all_to_all(stream, "tensor", split_axis=0, concat_axis=1, tiled=True)


def gather_weights(shard):
    kinds, rows, width = shard.shape
    whole = lax.all_gather(shard, ("tensor", "dp"), axis=1, tiled=True)
    return whole.reshape(kinds, -1, lax.axis_size("dp") * rows, width)


def scatter_weights(grads):
    kinds, ranks, width, cols = grads.shape
    flat = grads.reshape(kinds, ranks * width, cols)
    return lax.psum_scatter(flat, ("tensor", "dp"), scatter_dimension=1, tiled=True)


def per_device(
    clips, cotangent, timesteps, labels, time_table, class_table,
    attention_weights, attention_first, attention_second,
    ffn_weights, ffn_first, ffn_second,
    modulation_weights, modulation_first, modulation_second,
    bias_vectors, bias_first, bias_second,
):
    layers, _, rows, cols = attention_weights.shape
    width = clips.shape[-1]
    mod_rows = modulation_weights.shape[1]
    bias_cols = bias_vectors.shape[1]
    dp, tp = lax.axis_size("dp"), lax.axis_size("tensor")
    position = lax.axis_index("dp") * tp + lax.axis_index("tensor")
    embed = time_table[timesteps] + class_table[labels]
    cond_act = jax.nn.silu(embed).astype(jnp.bfloat16)
    low = bias_vectors.astype(jnp.bfloat16).reshape(-1)
    row = jnp.concatenate([cond_act[0], low])
    row = jnp.pad(row, (0, -row.shape[0] % 128)).reshape(1, -1, 128)
    gathered = lax.all_gather(row, BOTH, axis=0, tiled=True).reshape(dp * tp, -1)
    cond_all = gathered[::tp, :width]
    bias_low = gathered[:, width : width + layers * bias_cols].reshape(dp * tp, layers, bias_cols)
    bias_low = bias_low.transpose(1, 0, 2).reshape(layers, -1).astype(jnp.float32)
    cond_rows = lax.dynamic_slice_in_dim(cond_all, position * mod_rows, mod_rows, axis=1)
    modulation_low = modulation_weights.astype(jnp.bfloat16)
    mod_part = dot32("ck,lke->cle", cond_rows, modulation_low)
    mod_part = lax.psum_scatter(mod_part, "dp", scatter_dimension=0, tiled=True)
    mod = lax.psum(mod_part, "tensor")[0]
    mod_width = mod.shape[-1]
    mod = (mod + bias_low[:, -mod_width:]).reshape(layers, 6, width)

    weights = []
    for layer in range(layers):
        packed = attention_weights[layer].transpose(1, 0, 2).reshape(1, rows, 4 * cols)
        shard = jnp.concatenate([packed, ffn_weights[layer]], axis=0).astype(jnp.bfloat16)
        weights.append(gather_weights(shard))

    cotangent_patches = to_patches(cotangent[0])
    current = clips[0].astype(jnp.float32)
    saves = []
    for layer in range(layers):
        if layer % 2:
            current = to_patches(current)
        current, saved = layer_forward(current, mod[layer], weights[layer], bias_low[layer], layer % 2 == 1)
        if layer % 2:
            if layer == layers - 1:
                current = current.astype(jnp.bfloat16)
            current = to_frames(current)
        saves.append(saved)
    output = current.astype(jnp.bfloat16)[None]
    grad = cotangent_patches if layers % 2 == 0 else cotangent[0]
    grad = grad.astype(jnp.float32)
    small = [None] * layers
    weight_grads = [None] * layers
    for layer in reversed(range(layers)):
        if layer % 2 and layer != layers - 1:
            grad = to_patches(grad)
        grad, grad_mod, grad_w, grad_bias = layer_backward(
            saves[layer], grad, mod[layer], weights[layer], layer % 2 == 1
        )
        if layer % 2:
            grad = to_frames(grad)
        weight_grads[layer] = scatter_weights(grad_w.astype(jnp.bfloat16)).astype(jnp.float32)
        small[layer] = jnp.concatenate([grad_bias, grad_mod])
    input_grad = grad[None]

    small = lax.psum(jnp.stack(small), "tensor")
    token_width = small.shape[1] - mod_width
    small = lax.all_gather(small.reshape(1, -1, 128), "dp", axis=0, tiled=True).reshape(dp, layers, -1)
    grad_mod_low = small[..., token_width:].astype(jnp.bfloat16)
    grad_bias_all = jnp.concatenate(
        [small[..., :token_width], grad_mod_low.astype(jnp.float32)], axis=-1
    ).sum(axis=0)
    grad_bias = lax.dynamic_slice_in_dim(grad_bias_all, position * bias_cols, bias_cols, axis=1)
    grad_mod_weight = dot32("ck,cle->lke", cond_rows, grad_mod_low)
    grad_act = dot32("cle,lke->ck", grad_mod_low, modulation_low)
    grad_act = lax.all_gather(grad_act, BOTH, axis=0)
    grad_act = lax.dynamic_index_in_dim(grad_act, lax.axis_index("dp"), axis=1, keepdims=False)
    silu_value, silu_pull = jax.vjp(jax.nn.silu, embed)
    cond_grad = silu_pull(grad_act.reshape(1, width))[0]

    grads = jnp.stack(weight_grads)
    grad_attention = grads[:, 0].reshape(layers, rows, 4, cols).transpose(0, 2, 1, 3)
    grad_ffn = grads[:, 1:]
    return (output, input_grad, cond_grad) + (
        adam_update(attention_weights, attention_first, attention_second, grad_attention, MATRIX_RATE, MATRIX_DECAY)
        + adam_update(ffn_weights, ffn_first, ffn_second, grad_ffn, MATRIX_RATE, MATRIX_DECAY)
        + adam_update(modulation_weights, modulation_first, modulation_second, grad_mod_weight, MATRIX_RATE, MATRIX_DECAY)
        + adam_update(bias_vectors, bias_first, bias_second, grad_bias, VECTOR_RATE, 0.0)
    )


def solution(mesh):
    tokens = P("dp", "tensor", None, None)
    matrix = P(None, None, "dp", "tensor")
    modulation = P(None, BOTH, None)
    vector = P(None, BOTH)
    return jax.shard_map(
        per_device,
        mesh=mesh,
        in_specs=(tokens, tokens, P("dp"), P("dp"), P(), P())
        + (matrix,) * 6 + (modulation,) * 3 + (vector,) * 3,
        out_specs=(tokens, tokens, P("dp", None)) + (matrix,) * 8 + (modulation,) * 4 + (vector,) * 4,
        check_vma=False,
    )
```

```python
from functools import partial

import jax
import jax.numpy as jnp
from jax import lax
from jax.experimental import pallas as pl
from jax.experimental.pallas import tpu as pltpu
from jax.sharding import PartitionSpec as P

HD = 64
PAIR = 128
BLOCK = 256
SPLIT = 4
STEP = 10
BETA_ONE = 0.9
BETA_TWO = 0.999
ADAM_EPS = 1e-08
MATRIX_RATE = 0.04
VECTOR_RATE = 0.2
MATRIX_DECAY = 0.1
NORM_EPS = 1e-06
GELU_A = (2.0 / 3.141592653589793) ** 0.5
GELU_B = 0.044715
BLOCKED = -1e30
VMEM_LIMIT = 56 * 1024 * 1024
BOTH = ("dp", "tensor")


def mm(left, right, dims=((1,), (0,))):
    return lax.dot_general(left, right, (dims, ((), ())), preferred_element_type=jnp.float32)


def norm_parts(value):
    average = jnp.mean(value, axis=-1, keepdims=True)
    centred = value - average
    spread = jnp.mean(centred * centred, axis=-1, keepdims=True)
    inverse = lax.rsqrt(spread + NORM_EPS)
    return centred * inverse, inverse


def norm_back(grad, shape, inverse):
    first = jnp.mean(grad, axis=-1, keepdims=True)
    second = jnp.mean(grad * shape, axis=-1, keepdims=True)
    return inverse * (grad - first - shape * second)


def rows_of(ref):
    value = ref[...]
    return value.reshape(-1, value.shape[-1])


def put(ref, value):
    ref[...] = value.reshape(ref.shape).astype(ref.dtype)


def add_rows(ref, index, value):
    ref[pl.ds(index, 1), :] += jnp.sum(value, axis=0, keepdims=True)


def half_masks(rows):
    lane = lax.broadcasted_iota(jnp.int32, (rows, PAIR), 1)
    return lane < HD


def same_patch(tokens, stride):
    row = lax.broadcasted_iota(jnp.int32, (tokens, tokens), 0)
    column = lax.broadcasted_iota(jnp.int32, (tokens, tokens), 1)
    return lax.rem(row, stride) == lax.rem(column, stride)


def attention_forward_kernel(
    stride, stream_ref, mod_ref, bias_ref, weight_ref,
    query_ref, key_ref, value_ref, mixed_ref, branch_ref, middle_ref,
):
    stream = rows_of(stream_ref).astype(jnp.float32)
    tokens, width = stream.shape
    shape, _ = norm_parts(stream)
    normed = (shape * (1.0 + mod_ref[1:2]) + mod_ref[0:1]).astype(jnp.bfloat16)
    query = (mm(normed, weight_ref[0]) + bias_ref[0:1]).astype(jnp.bfloat16)
    put(query_ref, query)
    key = mm(normed, weight_ref[1]).astype(jnp.bfloat16)
    put(key_ref, key)
    value = (mm(normed, weight_ref[2]) + bias_ref[1:2]).astype(jnp.bfloat16)
    put(value_ref, value)
    lower = half_masks(tokens)
    allowed = same_patch(tokens, stride) if stride else None
    mixed = []
    for start in range(0, width, PAIR):
        part = slice(start, start + PAIR)
        pair = query[:, part].astype(jnp.float32) * HD**-0.5
        outs = []
        for keep in (lower, ~lower):
            chosen = jnp.where(keep, pair, 0.0).astype(jnp.bfloat16)
            scores = mm(chosen, key[:, part], ((1,), (1,)))
            if stride:
                scores = jnp.where(allowed, scores, BLOCKED)
            raised = jnp.exp(scores - jnp.max(scores, axis=-1, keepdims=True))
            total = jnp.sum(raised, axis=-1, keepdims=True)
            probs = (raised / total).astype(jnp.bfloat16)
            outs.append(mm(probs, value[:, part]))
        mixed.append(jnp.where(lower, outs[0], outs[1]).astype(jnp.bfloat16))
    mixed = jnp.concatenate(mixed, axis=1)
    put(mixed_ref, mixed)
    branch = mm(mixed, weight_ref[3], ((1,), (1,))) + bias_ref[2:3]
    put(branch_ref, branch)
    put(middle_ref, stream + mod_ref[2:3] * branch)


def gelu_parts(value):
    square = value * value
    bent = jnp.tanh(value * (GELU_A + (GELU_A * GELU_B) * square))
    half = 0.5 * (1.0 + bent)
    slope = half + (0.5 * value) * (1.0 - bent * bent) * (GELU_A + (3.0 * GELU_A * GELU_B) * square)
    return value * half, slope


def ffn_forward_kernel(
    split, middle_ref, mod_ref, bias_ref, bias_up_ref, up_ref, down_ref,
    hidden_ref, branch_ref, result_ref, second_ref, total_ref,
):
    step = pl.program_id(0)
    tokens = middle_ref.shape[0]
    chunk = tokens // split

    @pl.when(step == 0)
    def _():
        def norm_chunk(index, carry):
            rows = pl.ds(pl.multiple_of(index * chunk, chunk), chunk)
            shape, _ = norm_parts(middle_ref[rows, :])
            second_ref[rows, :] = (shape * (1.0 + mod_ref[4:5]) + mod_ref[3:4]).astype(jnp.bfloat16)
            return carry

        lax.fori_loop(0, split, norm_chunk, 0)

    def one(index, carry):
        rows = pl.ds(pl.multiple_of(index * chunk, chunk), chunk)
        hidden = mm(second_ref[rows, :], up_ref[0]) + bias_up_ref[0]
        hidden_ref[0, rows, :] = hidden.astype(jnp.bfloat16)
        active, _ = gelu_parts(hidden)
        part = mm(active.astype(jnp.bfloat16), down_ref[0], ((1,), (1,)))
        total_ref[rows, :] = jnp.where(step == 0, 0.0, total_ref[rows, :]) + part
        return carry

    lax.fori_loop(0, split, one, 0)

    @pl.when(step == pl.num_programs(0) - 1)
    def _():
        for index in range(split):
            rows = slice(index * chunk, (index + 1) * chunk)
            down = total_ref[rows, :] + bias_ref[3:4]
            branch_ref[rows, :] = down.astype(jnp.bfloat16)
            result = middle_ref[rows, :] + mod_ref[5:6] * down
            store_frame(result_ref, index, chunk, result)


def store_frame(ref, index, chunk, value):
    if len(ref.shape) == 2:
        ref[index * chunk : (index + 1) * chunk, :] = value.astype(ref.dtype)
    else:
        ref[:, index] = value.reshape(ref.shape[0], ref.shape[2], ref.shape[3]).astype(ref.dtype)


def load_frame(ref, index, chunk):
    if len(ref.shape) == 2:
        return ref[index * chunk : (index + 1) * chunk, :].astype(jnp.float32)
    value = ref[:, index]
    return value.reshape(chunk, value.shape[-1]).astype(jnp.float32)


def ffn_backward_kernel(
    split, grad_ref, middle_ref, branch_ref, hidden_ref, mod_ref, up_ref, down_ref,
    grad_middle_ref, weight_grad_ref, up_sum_ref, sums_ref,
    second_ref, low_ref, active_ref, slope_ref, total_ref,
):
    step = pl.program_id(0)
    tokens, width = middle_ref.shape
    chunk = tokens // split

    @pl.when(step == 0)
    def _():
        sums_ref[...] = jnp.zeros_like(sums_ref)
        for index in range(split):
            rows = slice(index * chunk, (index + 1) * chunk)
            grad = load_frame(grad_ref, index, chunk)
            low = (mod_ref[5:6] * grad).astype(jnp.bfloat16)
            low_ref[rows, :] = low
            add_rows(sums_ref, 0, low.astype(jnp.float32))
            add_rows(sums_ref, 3, grad * branch_ref[rows, :].astype(jnp.float32))
            shape, _ = norm_parts(middle_ref[rows, :])
            second_ref[rows, :] = (shape * (1.0 + mod_ref[4:5]) + mod_ref[3:4]).astype(jnp.bfloat16)

    up_sum_ref[...] = jnp.zeros_like(up_sum_ref)

    def one(index, carry):
        rows = pl.ds(pl.multiple_of(index * chunk, chunk), chunk)
        active, slope = gelu_parts(hidden_ref[0, rows, :].astype(jnp.float32))
        active_ref[rows, :] = active.astype(jnp.bfloat16)
        low = (mm(low_ref[rows, :], down_ref[0]) * slope).astype(jnp.bfloat16)
        slope_ref[rows, :] = low
        up_sum_ref[0] += jnp.sum(low.astype(jnp.float32), axis=0, keepdims=True)
        part = mm(low, up_ref[0], ((1,), (1,)))
        total_ref[rows, :] = jnp.where(step == 0, 0.0, total_ref[rows, :]) + part
        return carry

    lax.fori_loop(0, split, one, 0)

    def weights(index, carry):
        part = pl.ds(pl.multiple_of(index * BLOCK, BLOCK), BLOCK)
        weight_grad_ref[0, 0, part, :] = mm(second_ref[:, part], slope_ref[...], ((0,), (0,))).astype(
            jnp.bfloat16
        )
        weight_grad_ref[1, 0, part, :] = mm(low_ref[:, part], active_ref[...], ((0,), (0,))).astype(
            jnp.bfloat16
        )
        return carry

    lax.fori_loop(0, width // BLOCK, weights, 0)

    @pl.when(step == pl.num_programs(0) - 1)
    def _():
        for index in range(split):
            rows = slice(index * chunk, (index + 1) * chunk)
            shape, inverse = norm_parts(middle_ref[rows, :])
            grad = total_ref[rows, :]
            add_rows(sums_ref, 1, grad)
            add_rows(sums_ref, 2, grad * shape)
            back = norm_back(grad * (1.0 + mod_ref[4:5]), shape, inverse)
            grad_middle_ref[rows, :] = load_frame(grad_ref, index, chunk) + back


def attention_backward_kernel(
    stride, grad_ref, stream_ref, query_ref, key_ref, value_ref, mixed_ref, branch_ref,
    mod_ref, weight_ref,
    grad_stream_ref, weight_grad_ref, sums_ref,
    left_ref, right_ref,
):
    step = pl.program_id(0)
    grad_middle = rows_of(grad_ref)
    tokens, width = grad_middle.shape
    stream = rows_of(stream_ref).astype(jnp.float32)
    shape, inverse = norm_parts(stream)
    rows = pl.ds(pl.multiple_of(step * tokens, tokens), tokens)

    @pl.when(step == 0)
    def _():
        sums_ref[...] = jnp.zeros_like(sums_ref)

    normed = (shape * (1.0 + mod_ref[1:2]) + mod_ref[0:1]).astype(jnp.bfloat16)
    low = (mod_ref[2:3] * grad_middle).astype(jnp.bfloat16)
    left_ref[0, rows, :] = normed
    left_ref[1, rows, :] = low
    right_ref[3, rows, :] = rows_of(mixed_ref)
    add_rows(sums_ref, 2, low.astype(jnp.float32))
    add_rows(sums_ref, 5, grad_middle * rows_of(branch_ref).astype(jnp.float32))
    grad_mixed = mm(low, weight_ref[3]).astype(jnp.bfloat16)
    query, key, value = rows_of(query_ref), rows_of(key_ref), rows_of(value_ref)
    lower = half_masks(tokens)
    allowed = same_patch(tokens, stride) if stride else None
    scale = HD**-0.5
    grads = ([], [], [])
    for start in range(0, width, PAIR):
        part = slice(start, start + PAIR)
        query_pair, mixed_pair = query[:, part], grad_mixed[:, part]
        query_wide, mixed_wide = query_pair.astype(jnp.float32), mixed_pair.astype(jnp.float32)
        outs = ([], [], [])
        for keep in (lower, ~lower):
            chosen = jnp.where(keep, query_wide * scale, 0.0).astype(jnp.bfloat16)
            scores = mm(key[:, part], chosen, ((1,), (1,)))
            if stride:
                scores = jnp.where(allowed, scores, BLOCKED)
            raised = jnp.exp(scores - jnp.max(scores, axis=0, keepdims=True))
            probs = raised * (1.0 / jnp.sum(raised, axis=0, keepdims=True))
            taken = jnp.where(keep, mixed_wide, 0.0).astype(jnp.bfloat16)
            grad_probs = mm(value[:, part], taken, ((1,), (1,)))
            inner = jnp.sum(grad_probs * probs, axis=0, keepdims=True)
            grad_scores = (probs * (grad_probs - inner)).astype(jnp.bfloat16)
            outs[0].append(mm(grad_scores, key[:, part], ((0,), (0,))))
            outs[1].append(mm(grad_scores, query_pair))
            outs[2].append(mm(probs.astype(jnp.bfloat16), mixed_pair))
        for kind, factor in enumerate((scale, scale, 1.0)):
            merged = jnp.where(lower, outs[kind][0], outs[kind][1]) * factor
            grads[kind].append(merged.astype(jnp.bfloat16))
    grad_normed = None
    for kind in range(3):
        whole = jnp.concatenate(grads[kind], axis=1)
        right_ref[kind, rows, :] = whole
        if kind != 1:
            add_rows(sums_ref, kind // 2, whole.astype(jnp.float32))
        term = mm(whole, weight_ref[kind], ((1,), (1,)))
        grad_normed = term if grad_normed is None else grad_normed + term
    add_rows(sums_ref, 3, grad_normed)
    add_rows(sums_ref, 4, grad_normed * shape)
    back = norm_back(grad_normed * (1.0 + mod_ref[1:2]), shape, inverse)
    put(grad_stream_ref, grad_middle + back)

    @pl.when(step == pl.num_programs(0) - 1)
    def _():
        def weights(index, carry):
            part = pl.ds(pl.multiple_of(index * BLOCK, BLOCK), BLOCK)
            for kind in range(4):
                side = left_ref[kind // 3, :, part]
                weight_grad_ref[kind, part, :] = mm(side, right_ref[kind], ((0,), (0,))).astype(
                    jnp.bfloat16
                )
            return carry

        lax.fori_loop(0, width // BLOCK, weights, 0)


def fixed(shape):
    return pl.BlockSpec(shape, lambda step: (0,) * len(shape))


def kernel_params():
    return pltpu.CompilerParams(vmem_limit_bytes=VMEM_LIMIT, dimension_semantics=("arbitrary",))


def cost(flops, moved, raised=0):
    return pl.CostEstimate(flops=int(flops), bytes_accessed=int(moved), transcendentals=int(raised))


def group_spec(shape):
    return pl.BlockSpec((shape[0], 1, shape[2], shape[3]), lambda step: (0, step, 0, 0))


def attention_forward(stream, mod, bias, weight, stride):
    shape = stream.shape
    width = shape[-1]
    tokens = shape[0] * shape[1] * shape[2]
    spec = group_spec(shape)
    low = jax.ShapeDtypeStruct(shape, jnp.bfloat16)
    wide = jax.ShapeDtypeStruct(shape, jnp.float32)
    return pl.pallas_call(
        partial(attention_forward_kernel, stride),
        grid=(shape[1],),
        in_specs=[spec, fixed(mod.shape), fixed(bias.shape), fixed(weight.shape)],
        out_specs=[spec] * 6,
        out_shape=[low, low, low, low, low, wide],
        compiler_params=kernel_params(),
        cost_estimate=cost(8 * tokens * width * width * 1.5, tokens * width * 16 + weight.size * 2),
        name="attention_forward",
    )(stream, mod, bias, weight)


def ffn_forward(middle, mod, bias, bias_up, up, down, result_shape, result_type):
    tokens, width = middle.shape
    ranks, _, part = up.shape
    whole = fixed((tokens, width))
    block = pl.BlockSpec((1, width, part), lambda step: (step, 0, 0))
    vector = pl.BlockSpec((1, 1, part), lambda step: (step, 0, 0))
    return pl.pallas_call(
        partial(ffn_forward_kernel, SPLIT),
        grid=(ranks,),
        in_specs=[whole, fixed(mod.shape), fixed(bias.shape), vector, block, block],
        out_specs=[pl.BlockSpec((1, tokens, part), lambda step: (step, 0, 0)), whole, fixed(result_shape)],
        out_shape=[
            jax.ShapeDtypeStruct((ranks, tokens, part), jnp.bfloat16),
            jax.ShapeDtypeStruct((tokens, width), jnp.bfloat16),
            jax.ShapeDtypeStruct(result_shape, result_type),
        ],
        scratch_shapes=[
            pltpu.VMEM((tokens, width), jnp.bfloat16),
            pltpu.VMEM((tokens, width), jnp.float32),
        ],
        compiler_params=kernel_params(),
        cost_estimate=cost(4 * tokens * up.size * 1.2, tokens * width * 14 + up.size * 4, tokens * ranks * part),
        name="ffn_forward",
    )(middle, mod, bias, bias_up, up, down)


def ffn_backward(grad, middle, branch, hidden, mod, up, down):
    tokens, width = middle.shape
    ranks, _, part = up.shape
    whole = fixed((tokens, width))
    block = pl.BlockSpec((1, width, part), lambda step: (step, 0, 0))
    return pl.pallas_call(
        partial(ffn_backward_kernel, SPLIT),
        grid=(ranks,),
        in_specs=[
            fixed(grad.shape), whole, whole,
            pl.BlockSpec((1, tokens, part), lambda step: (step, 0, 0)),
            fixed(mod.shape), block, block,
        ],
        out_specs=[
            whole,
            pl.BlockSpec((2, 1, width, part), lambda step: (0, step, 0, 0)),
            pl.BlockSpec((1, 1, part), lambda step: (step, 0, 0)),
            fixed((4, width)),
        ],
        out_shape=[
            jax.ShapeDtypeStruct((tokens, width), jnp.float32),
            jax.ShapeDtypeStruct((2, ranks, width, part), jnp.bfloat16),
            jax.ShapeDtypeStruct((ranks, 1, part), jnp.float32),
            jax.ShapeDtypeStruct((4, width), jnp.float32),
        ],
        scratch_shapes=[
            pltpu.VMEM((tokens, width), jnp.bfloat16),
            pltpu.VMEM((tokens, width), jnp.bfloat16),
            pltpu.VMEM((tokens, part), jnp.bfloat16),
            pltpu.VMEM((tokens, part), jnp.bfloat16),
            pltpu.VMEM((tokens, width), jnp.float32),
        ],
        compiler_params=kernel_params(),
        cost_estimate=cost(8 * tokens * up.size * 1.2, tokens * width * 20 + up.size * 8, tokens * ranks * part),
        name="ffn_backward",
    )(grad, middle, branch, hidden, mod, up, down)


def attention_backward(grad, stream, saved, mod, weight, stride, result_type):
    shape = stream.shape
    width = shape[-1]
    tokens = shape[0] * shape[1] * shape[2]
    spec = group_spec(shape)
    return pl.pallas_call(
        partial(attention_backward_kernel, stride),
        grid=(shape[1],),
        in_specs=[spec] * 7 + [fixed(mod.shape), fixed(weight.shape)],
        out_specs=[spec, fixed(weight.shape), fixed((6, width))],
        out_shape=[
            jax.ShapeDtypeStruct(shape, result_type),
            jax.ShapeDtypeStruct(weight.shape, jnp.bfloat16),
            jax.ShapeDtypeStruct((6, width), jnp.float32),
        ],
        scratch_shapes=[
            pltpu.VMEM((2, tokens, width), jnp.bfloat16),
            pltpu.VMEM((4, tokens, width), jnp.bfloat16),
        ],
        compiler_params=kernel_params(),
        cost_estimate=cost(16 * tokens * width * width * 1.5, tokens * width * 20 + weight.size * 4),
        name="attention_backward",
    )(grad, stream, *saved, mod, weight)


def adam_update(weight, first, second, grad, rate, decay):
    first_new = BETA_ONE * first + (1.0 - BETA_ONE) * grad
    second_new = BETA_TWO * second + (1.0 - BETA_TWO) * grad * grad
    corrected = (
        first_new
        / (1.0 - BETA_ONE**STEP)
        / (jnp.sqrt(second_new / (1.0 - BETA_TWO**STEP)) + ADAM_EPS)
    )
    weight_new = weight - rate * (corrected + decay * weight)
    return (weight_new, first_new, second_new, weight_new.astype(jnp.bfloat16))


def dot32(form, left, right):
    return jnp.einsum(form, left, right, preferred_element_type=jnp.float32)


def exchange(blocks):
    return lax.all_to_all(blocks, "tensor", split_axis=0, concat_axis=0, tiled=True)


def gather_weights(shard):
    kinds, rows, width = shard.shape
    whole = lax.all_gather(shard, ("tensor", "dp"), axis=1, tiled=True)
    return whole.reshape(kinds, -1, lax.axis_size("dp") * rows, width)


def scatter_weights(grads):
    kinds, ranks, width, cols = grads.shape
    flat = grads.reshape(kinds, ranks * width, cols)
    return lax.psum_scatter(flat, ("tensor", "dp"), scatter_dimension=1, tiled=True)


def per_device(
    clips, cotangent, timesteps, labels, time_table, class_table,
    attention_weights, attention_first, attention_second,
    ffn_weights, ffn_first, ffn_second,
    modulation_weights, modulation_first, modulation_second,
    bias_vectors, bias_first, bias_second,
):
    layers, kinds, rows, cols = attention_weights.shape
    _, frames, patches, width = clips.shape
    mod_rows = modulation_weights.shape[1]
    bias_cols = bias_vectors.shape[1]
    dp, tp = lax.axis_size("dp"), lax.axis_size("tensor")
    position = lax.axis_index("dp") * tp + lax.axis_index("tensor")
    tokens = frames * patches
    strip = patches // (tp * frames)
    blocks = (tp, frames, frames * strip, width)
    pieces = (tp * frames, frames, strip, width)

    embed = time_table[timesteps] + class_table[labels]
    cond_act = jax.nn.silu(embed).astype(jnp.bfloat16)
    low = bias_vectors.astype(jnp.bfloat16).reshape(-1)
    row = jnp.concatenate([cond_act[0], low])
    row = jnp.pad(row, (0, -row.shape[0] % 128)).reshape(1, -1, 128)
    gathered = lax.all_gather(row, BOTH, axis=0, tiled=True).reshape(dp * tp, -1)
    cond_all = gathered[::tp, :width]
    bias_low = gathered[:, width : width + layers * bias_cols].reshape(dp * tp, layers, bias_cols)
    bias_low = bias_low.transpose(1, 0, 2).reshape(layers, -1).astype(jnp.float32)
    cond_rows = lax.dynamic_slice_in_dim(cond_all, position * mod_rows, mod_rows, axis=1)
    modulation_low = modulation_weights.astype(jnp.bfloat16)
    mod_part = dot32("ck,lke->cle", cond_rows, modulation_low)
    mod_part = lax.psum_scatter(mod_part, "dp", scatter_dimension=0, tiled=True)
    mod = lax.psum(mod_part, "tensor")[0]
    mod_width = mod.shape[-1]
    mod = (mod + bias_low[:, -mod_width:]).reshape(layers, 6, width)
    hidden_width = bias_low.shape[1] - mod_width - 4 * width
    bias_rows = jnp.concatenate(
        [bias_low[:, : 3 * width], bias_low[:, 3 * width + hidden_width : 4 * width + hidden_width]], axis=1
    ).reshape(layers, 4, width)
    bias_up = bias_low[:, 3 * width : 3 * width + hidden_width].reshape(layers, tp, 1, -1)

    attention, ffn = [], []
    for layer in range(layers):
        packed = attention_weights[layer].transpose(1, 0, 2).reshape(1, rows, kinds * cols)
        packed = gather_weights(packed.astype(jnp.bfloat16))
        packed = packed.reshape(tp, width, kinds, cols).transpose(2, 1, 0, 3).reshape(kinds, width, width)
        attention.append(packed)
        ffn.append(gather_weights(ffn_weights[layer].astype(jnp.bfloat16)))

    by_patch = lambda v: v.reshape(frames, tp * frames, strip, width).transpose(1, 0, 2, 3)
    cot = exchange(by_patch(cotangent[0]).reshape(blocks))

    def forward(layer, stream, stride, result_shape):
        query, key, value, mixed, branch, middle = attention_forward(
            stream, mod[layer], bias_rows[layer], attention[layer], stride
        )
        middle = middle.reshape(tokens, width)
        hidden, down, result = ffn_forward(
            middle, mod[layer], bias_rows[layer], bias_up[layer], ffn[layer][0], ffn[layer][1],
            result_shape, jnp.bfloat16,
        )
        return result, ((query, key, value, mixed, branch), middle, hidden, down)

    def backward(layer, grad, stream, saved, stride, result_type):
        heads, middle, hidden, down = saved
        grad_middle, ffn_grad, up_sum, low_sums = ffn_backward(
            grad, middle, down, hidden, mod[layer], ffn[layer][0], ffn[layer][1]
        )
        ffn_grad = scatter_weights(ffn_grad)
        grad, attention_grad, sums = attention_backward(
            grad_middle.reshape(stream.shape), stream, heads, mod[layer], attention[layer], stride, result_type
        )
        packed = attention_grad.reshape(kinds, width, tp, cols).transpose(2, 1, 0, 3)
        packed = scatter_weights(packed.reshape(1, tp, width, kinds * cols))
        attention_grad = packed.reshape(rows, kinds, cols).transpose(1, 0, 2)
        small = jnp.concatenate(
            [sums[:3].reshape(-1), up_sum.reshape(-1), low_sums[0], sums[3:].reshape(-1), low_sums[1:].reshape(-1)]
        )
        return grad, attention_grad, ffn_grad, small

    first = clips[0].reshape(1, frames, patches, width)
    second, saved_first = forward(0, first, 0, pieces)
    second = exchange(second.reshape(blocks))
    result, saved_second = forward(1, second, strip, (tokens, width))
    result = exchange(result.reshape(blocks)).reshape(pieces)
    output = result.transpose(1, 0, 2, 3).reshape(clips.shape)

    grad, attention_b, ffn_b, small_b = backward(
        1, cot.reshape(tokens, width), second, saved_second, strip, jnp.bfloat16
    )
    grad = exchange(grad).reshape(pieces)
    grad, attention_a, ffn_a, small_a = backward(0, grad, first, saved_first, 0, jnp.float32)
    input_grad = grad.reshape(clips.shape)

    small = lax.psum(jnp.stack([small_a, small_b]), "tensor")
    token_width = small.shape[1] - mod_width
    small = lax.all_gather(small.reshape(1, -1, 128), "dp", axis=0, tiled=True).reshape(dp, layers, -1)
    grad_mod_low = small[..., token_width:].astype(jnp.bfloat16)
    grad_bias_all = jnp.concatenate(
        [small[..., :token_width], grad_mod_low.astype(jnp.float32)], axis=-1
    ).sum(axis=0)
    grad_bias = lax.dynamic_slice_in_dim(grad_bias_all, position * bias_cols, bias_cols, axis=1)
    grad_mod_weight = dot32("ck,cle->lke", cond_rows, grad_mod_low)
    grad_act = dot32("cle,lke->ck", grad_mod_low, modulation_low)
    grad_act = lax.all_gather(grad_act, BOTH, axis=0)
    grad_act = lax.dynamic_index_in_dim(grad_act, lax.axis_index("dp"), axis=1, keepdims=False)
    silu_value, silu_pull = jax.vjp(jax.nn.silu, embed)
    cond_grad = silu_pull(grad_act.reshape(1, width))[0]

    grad_attention = jnp.stack([attention_a, attention_b]).astype(jnp.float32)
    grad_ffn = jnp.stack([ffn_a, ffn_b]).astype(jnp.float32)
    return (output, input_grad, cond_grad) + (
        adam_update(attention_weights, attention_first, attention_second, grad_attention, MATRIX_RATE, MATRIX_DECAY)
        + adam_update(ffn_weights, ffn_first, ffn_second, grad_ffn, MATRIX_RATE, MATRIX_DECAY)
        + adam_update(modulation_weights, modulation_first, modulation_second, grad_mod_weight, MATRIX_RATE, MATRIX_DECAY)
        + adam_update(bias_vectors, bias_first, bias_second, grad_bias, VECTOR_RATE, 0.0)
    )


def solution(mesh):
    tokens = P("dp", "tensor", None, None)
    matrix = P(None, None, "dp", "tensor")
    modulation = P(None, BOTH, None)
    vector = P(None, BOTH)
    return jax.shard_map(
        per_device,
        mesh=mesh,
        in_specs=(tokens, tokens, P("dp"), P("dp"), P(), P())
        + (matrix,) * 6 + (modulation,) * 3 + (vector,) * 3,
        out_specs=(tokens, tokens, P("dp", None)) + (matrix,) * 8 + (modulation,) * 4 + (vector,) * 4,
        check_vma=False,
    )
```

```python
from functools import partial

import jax
import jax.numpy as jnp
from jax import lax
from jax.experimental import pallas as pl
from jax.experimental.pallas import tpu as pltpu
from jax.sharding import PartitionSpec as P

HD = 64
PAIR = 128
BLOCK = 256
SPLIT = 4
STEP = 10
BETA_ONE = 0.9
BETA_TWO = 0.999
ADAM_EPS = 1e-08
MATRIX_RATE = 0.04
VECTOR_RATE = 0.2
MATRIX_DECAY = 0.1
NORM_EPS = 1e-06
GELU_A = (2.0 / 3.141592653589793) ** 0.5
GELU_B = 0.044715
BLOCKED = -1e30
VMEM_LIMIT = 56 * 1024 * 1024
BOTH = ("dp", "tensor")


def mm(left, right, dims=((1,), (0,))):
    return lax.dot_general(left, right, (dims, ((), ())), preferred_element_type=jnp.float32)


def norm_parts(value):
    average = jnp.mean(value, axis=-1, keepdims=True)
    centred = value - average
    spread = jnp.mean(centred * centred, axis=-1, keepdims=True)
    inverse = lax.rsqrt(spread + NORM_EPS)
    return centred * inverse, inverse


def norm_back(grad, shape, inverse):
    first = jnp.mean(grad, axis=-1, keepdims=True)
    second = jnp.mean(grad * shape, axis=-1, keepdims=True)
    return inverse * (grad - first - shape * second)


def rows_of(ref):
    value = ref[...]
    return value.reshape(-1, value.shape[-1])


def put(ref, value):
    ref[...] = value.reshape(ref.shape).astype(ref.dtype)


def add_rows(ref, index, value):
    ref[pl.ds(index, 1), :] += jnp.sum(value, axis=0, keepdims=True)


def half_masks(rows):
    lane = lax.broadcasted_iota(jnp.int32, (rows, PAIR), 1)
    return lane < HD


def same_patch(tokens, stride):
    row = lax.broadcasted_iota(jnp.int32, (tokens, tokens), 0)
    column = lax.broadcasted_iota(jnp.int32, (tokens, tokens), 1)
    return lax.rem(row, stride) == lax.rem(column, stride)


def swap_halves(value):
    return pltpu.roll(value, HD, 1)


def start_loads(sources, kind, target, semaphores):
    if len(sources) == 1:
        for rank in range(target.shape[0]):
            pltpu.make_async_copy(sources[0].at[kind, rank], target.at[rank], semaphores.at[rank]).start()
        return
    far, near, rows = sources[0].shape[2], 2, sources[0].shape[4]
    device, rank = lax.axis_index("dp"), lax.axis_index("tensor")
    for core, source in enumerate(sources):
        for row in range(2):
            for side in range(2):
                for back in range(far):
                    where = lax.rem(device // near + far - back, far) * near + (device % near + side) % near
                    owner = (rank // 2 + row) % 2 * 2 + (rank % 2 + core) % 2
                    pltpu.make_async_copy(
                        source.at[row, side, back, kind],
                        target.at[owner, pl.ds(pl.multiple_of(where * rows, rows), rows)],
                        semaphores.at[owner],
                    ).start()


def wait_loads(target, semaphores, rank):
    pltpu.make_async_copy(target.at[rank], target.at[rank], semaphores.at[rank]).wait()


def softmax_rows(scores, axis):
    raised = jnp.exp(scores - jnp.max(scores, axis=axis, keepdims=True))
    return raised * (1.0 / jnp.sum(raised, axis=axis, keepdims=True))


def attention_forward_kernel(stride, count, *refs):
    sources = refs[:count]
    (stream_ref, mod_ref, bias_ref, bias_out_ref,
     project_ref, mixed_ref, branch_ref, middle_ref, weight_ref, semaphores) = refs[count:]
    ranks = weight_ref.shape[0]

    @pl.when(pl.program_id(0) == 0)
    def _():
        start_loads(sources, 0, weight_ref, semaphores)

    stream = rows_of(stream_ref).astype(jnp.float32)
    tokens, width = stream.shape
    shape, _ = norm_parts(stream)
    normed = (shape * (1.0 + mod_ref[1:2]) + mod_ref[0:1]).astype(jnp.bfloat16)
    lower = half_masks(tokens)
    allowed = same_patch(tokens, stride) if stride else None

    @pl.when(pl.program_id(0) == 0)
    def _():
        for rank in range(ranks):
            wait_loads(weight_ref, semaphores, rank)

    def one_head(chosen, key, value):
        scores = mm(chosen.astype(jnp.bfloat16), key, ((1,), (1,)))
        if stride:
            scores = jnp.where(allowed, scores, BLOCKED)
        return mm(softmax_rows(scores, -1).astype(jnp.bfloat16), value)

    branch = None
    for rank in range(ranks):
        project = (mm(normed, weight_ref[rank, :, : 5 * PAIR]) + bias_ref[rank]).astype(jnp.bfloat16)
        project_ref[rank] = project.reshape(project_ref.shape[1:])
        query = project[:, :PAIR].astype(jnp.float32) * HD**-0.5
        key, value = project[:, PAIR : 2 * PAIR], project[:, 2 * PAIR : 3 * PAIR]
        first = one_head(jnp.where(lower, query, 0.0), key, value)
        second = one_head(jnp.where(lower, 0.0, query), key, value)
        both = project[:, 3 * PAIR : 4 * PAIR].astype(jnp.float32)
        last = one_head(
            jnp.where(lower, both * HD**-0.5, 0.0),
            swap_halves(both).astype(jnp.bfloat16),
            project[:, 4 * PAIR : 5 * PAIR],
        )
        mixed = jnp.concatenate(
            [jnp.where(lower, 0.0, swap_halves(last)), jnp.where(lower, first, second)], axis=1
        ).astype(jnp.bfloat16)
        mixed_ref[rank] = mixed.reshape(mixed_ref.shape[1:])
        term = mm(mixed, weight_ref[rank, :, 4 * PAIR :], ((1,), (1,)))
        branch = term if branch is None else branch + term
    branch = branch + bias_out_ref[...]
    put(branch_ref, branch)
    put(middle_ref, stream + mod_ref[2:3] * branch)


def gelu_parts(value):
    square = value * value
    bent = jnp.tanh(value * (GELU_A + (GELU_A * GELU_B) * square))
    half = 0.5 * (1.0 + bent)
    slope = half + (0.5 * value) * (1.0 - bent * bent) * (GELU_A + (3.0 * GELU_A * GELU_B) * square)
    return value * half, slope


def ffn_forward_kernel(split, count, *refs):
    sources = refs[:count]
    (middle_ref, mod_ref, bias_ref, bias_up_ref,
     hidden_ref, branch_ref, result_ref,
     up_ref, down_ref, up_semaphores, down_semaphores, second_ref, total_ref) = refs[count:]
    step = pl.program_id(0)
    tokens = middle_ref.shape[0]
    chunk = tokens // split

    @pl.when(step == 0)
    def _():
        start_loads(sources, 0, up_ref, up_semaphores)
        start_loads(sources, 1, down_ref, down_semaphores)

        def norm_chunk(index, carry):
            rows = pl.ds(pl.multiple_of(index * chunk, chunk), chunk)
            shape, _ = norm_parts(middle_ref[rows, :])
            second_ref[rows, :] = (shape * (1.0 + mod_ref[4:5]) + mod_ref[3:4]).astype(jnp.bfloat16)
            return carry

        lax.fori_loop(0, split, norm_chunk, 0)

    wait_loads(up_ref, up_semaphores, step)
    wait_loads(down_ref, down_semaphores, step)

    def one(index, carry):
        rows = pl.ds(pl.multiple_of(index * chunk, chunk), chunk)
        hidden = mm(second_ref[rows, :], up_ref[step]) + bias_up_ref[0]
        hidden_ref[0, rows, :] = hidden.astype(jnp.bfloat16)
        active, _ = gelu_parts(hidden)
        part = mm(active.astype(jnp.bfloat16), down_ref[step], ((1,), (1,)))
        total_ref[rows, :] = jnp.where(step == 0, 0.0, total_ref[rows, :]) + part
        return carry

    lax.fori_loop(0, split, one, 0)

    @pl.when(step == pl.num_programs(0) - 1)
    def _():
        for index in range(split):
            rows = slice(index * chunk, (index + 1) * chunk)
            down = total_ref[rows, :] + bias_ref[...]
            branch_ref[rows, :] = down.astype(jnp.bfloat16)
            result = middle_ref[rows, :] + mod_ref[5:6] * down
            store_frame(result_ref, index, chunk, result)


def store_frame(ref, index, chunk, value):
    if len(ref.shape) == 2:
        ref[index * chunk : (index + 1) * chunk, :] = value.astype(ref.dtype)
    else:
        ref[:, index] = value.reshape(ref.shape[0], ref.shape[2], ref.shape[3]).astype(ref.dtype)


def load_frame(ref, index, chunk):
    if len(ref.shape) == 2:
        return ref[index * chunk : (index + 1) * chunk, :].astype(jnp.float32)
    value = ref[:, index]
    return value.reshape(chunk, value.shape[-1]).astype(jnp.float32)


def ffn_backward_kernel(split, count, *refs):
    sources = refs[:count]
    (grad_ref, middle_ref, branch_ref, hidden_ref, mod_ref,
     grad_middle_ref, weight_grad_ref, up_sum_ref, sums_ref,
     up_ref, down_ref, up_semaphores, down_semaphores,
     second_ref, low_ref, active_ref, slope_ref, total_ref) = refs[count:]
    step = pl.program_id(0)
    tokens, width = middle_ref.shape
    chunk = tokens // split

    @pl.when(step == 0)
    def _():
        start_loads(sources, 0, up_ref, up_semaphores)
        start_loads(sources, 1, down_ref, down_semaphores)
        sums_ref[...] = jnp.zeros_like(sums_ref)
        for index in range(split):
            rows = slice(index * chunk, (index + 1) * chunk)
            grad = load_frame(grad_ref, index, chunk)
            low = (mod_ref[5:6] * grad).astype(jnp.bfloat16)
            low_ref[rows, :] = low
            add_rows(sums_ref, 0, low.astype(jnp.float32))
            add_rows(sums_ref, 3, grad * branch_ref[rows, :].astype(jnp.float32))
            shape, _ = norm_parts(middle_ref[rows, :])
            second_ref[rows, :] = (shape * (1.0 + mod_ref[4:5]) + mod_ref[3:4]).astype(jnp.bfloat16)

    up_sum_ref[...] = jnp.zeros_like(up_sum_ref)
    wait_loads(up_ref, up_semaphores, step)
    wait_loads(down_ref, down_semaphores, step)

    def one(index, carry):
        rows = pl.ds(pl.multiple_of(index * chunk, chunk), chunk)
        active, slope = gelu_parts(hidden_ref[0, rows, :].astype(jnp.float32))
        active_ref[rows, :] = active.astype(jnp.bfloat16)
        low = (mm(low_ref[rows, :], down_ref[step]) * slope).astype(jnp.bfloat16)
        slope_ref[rows, :] = low
        up_sum_ref[0] += jnp.sum(low.astype(jnp.float32), axis=0, keepdims=True)
        part = mm(low, up_ref[step], ((1,), (1,)))
        total_ref[rows, :] = jnp.where(step == 0, 0.0, total_ref[rows, :]) + part
        return carry

    lax.fori_loop(0, split, one, 0)

    def weights(index, carry):
        part = pl.ds(pl.multiple_of(index * BLOCK, BLOCK), BLOCK)
        weight_grad_ref[0, 0, part, :] = mm(second_ref[:, part], slope_ref[...], ((0,), (0,))).astype(
            jnp.bfloat16
        )
        weight_grad_ref[1, 0, part, :] = mm(low_ref[:, part], active_ref[...], ((0,), (0,))).astype(
            jnp.bfloat16
        )
        return carry

    lax.fori_loop(0, width // BLOCK, weights, 0)

    @pl.when(step == pl.num_programs(0) - 1)
    def _():
        for index in range(split):
            rows = slice(index * chunk, (index + 1) * chunk)
            shape, inverse = norm_parts(middle_ref[rows, :])
            grad = total_ref[rows, :]
            add_rows(sums_ref, 1, grad)
            add_rows(sums_ref, 2, grad * shape)
            back = norm_back(grad * (1.0 + mod_ref[4:5]), shape, inverse)
            grad_middle_ref[rows, :] = load_frame(grad_ref, index, chunk) + back


def attention_backward_kernel(stride, count, *refs):
    sources = refs[:count]
    (grad_ref, stream_ref, project_ref, mixed_ref, branch_ref, mod_ref,
     grad_stream_ref, weight_grad_ref, sums_ref, project_sum_ref,
     weight_ref, semaphores, left_ref, right_ref, outer_ref) = refs[count:]
    step = pl.program_id(0)
    ranks = weight_ref.shape[0]

    @pl.when(step == 0)
    def _():
        start_loads(sources, 0, weight_ref, semaphores)
        sums_ref[...] = jnp.zeros_like(sums_ref)
        project_sum_ref[...] = jnp.zeros_like(project_sum_ref)

    grad_middle = rows_of(grad_ref)
    tokens, width = grad_middle.shape
    stream = rows_of(stream_ref).astype(jnp.float32)
    shape, inverse = norm_parts(stream)
    rows = pl.ds(pl.multiple_of(step * tokens, tokens), tokens)
    normed = (shape * (1.0 + mod_ref[1:2]) + mod_ref[0:1]).astype(jnp.bfloat16)
    low = (mod_ref[2:3] * grad_middle).astype(jnp.bfloat16)
    left_ref[0, rows, :] = normed
    left_ref[1, rows, :] = low
    add_rows(sums_ref, 0, low.astype(jnp.float32))
    add_rows(sums_ref, 3, grad_middle * rows_of(branch_ref).astype(jnp.float32))
    lower = half_masks(tokens)
    allowed = same_patch(tokens, stride) if stride else None
    scale = HD**-0.5

    @pl.when(step == 0)
    def _():
        for rank in range(ranks):
            wait_loads(weight_ref, semaphores, rank)

    def one_head(chosen, key, value, taken):
        scores = mm(key, chosen.astype(jnp.bfloat16), ((1,), (1,)))
        if stride:
            scores = jnp.where(allowed, scores, BLOCKED)
        probs = softmax_rows(scores, 0)
        grad_probs = mm(value, taken.astype(jnp.bfloat16), ((1,), (1,)))
        inner = jnp.sum(grad_probs * probs, axis=0, keepdims=True)
        return probs.astype(jnp.bfloat16), (probs * (grad_probs - inner)).astype(jnp.bfloat16)

    grad_normed = None
    for rank in range(ranks):
        project = project_ref[rank].reshape(tokens, 5 * PAIR)
        mixed = mixed_ref[rank].reshape(tokens, 2 * PAIR)
        outer_ref[rank, rows, :] = mixed
        grad_mixed = mm(low, weight_ref[rank, :, 4 * PAIR :]).astype(jnp.bfloat16)
        query, key, value = (project[:, n * PAIR : (n + 1) * PAIR] for n in range(3))
        query_wide = query.astype(jnp.float32) * scale
        pair = grad_mixed[:, PAIR:]
        pair_wide = pair.astype(jnp.float32)
        outs = []
        for keep in (lower, ~lower):
            probs, grad_scores = one_head(
                jnp.where(keep, query_wide, 0.0), key, value, jnp.where(keep, pair_wide, 0.0)
            )
            outs.append(
                (mm(grad_scores, key, ((0,), (0,))), mm(grad_scores, query), mm(probs, pair))
            )
        parts = [
            jnp.where(lower, one, two) * factor
            for one, two, factor in zip(outs[0], outs[1], (scale, scale, 1.0))
        ]
        both = project[:, 3 * PAIR : 4 * PAIR].astype(jnp.float32)
        swapped = swap_halves(both).astype(jnp.bfloat16)
        single = swap_halves(grad_mixed[:, :PAIR].astype(jnp.float32))
        probs, grad_scores = one_head(
            jnp.where(lower, both * scale, 0.0),
            swapped,
            project[:, 4 * PAIR :],
            jnp.where(lower, single, 0.0),
        )
        parts.append(
            jnp.where(lower, mm(grad_scores, swapped, ((0,), (0,))), mm(grad_scores, swapped)) * scale
        )
        parts.append(jnp.where(lower, mm(probs, single.astype(jnp.bfloat16)), 0.0))
        whole = jnp.concatenate(parts, axis=1).astype(jnp.bfloat16)
        right_ref[rank, rows, :] = whole
        add_rows(project_sum_ref, rank, whole.astype(jnp.float32))
        term = mm(whole, weight_ref[rank, :, : 5 * PAIR], ((1,), (1,)))
        grad_normed = term if grad_normed is None else grad_normed + term
    add_rows(sums_ref, 1, grad_normed)
    add_rows(sums_ref, 2, grad_normed * shape)
    back = norm_back(grad_normed * (1.0 + mod_ref[1:2]), shape, inverse)
    put(grad_stream_ref, grad_middle + back)

    @pl.when(step == pl.num_programs(0) - 1)
    def _():
        def weights(rank, carry):
            def block(index, inner):
                part = pl.ds(pl.multiple_of(index * BLOCK, BLOCK), BLOCK)
                inside = mm(left_ref[0, :, part], right_ref[rank], ((0,), (0,)))
                outside = mm(left_ref[1, :, part], outer_ref[rank], ((0,), (0,)))
                weight_grad_ref[rank, part, : 4 * PAIR] = inside[:, : 4 * PAIR].astype(jnp.bfloat16)
                weight_grad_ref[rank, part, 4 * PAIR : 5 * PAIR] = (
                    inside[:, 4 * PAIR :] + outside[:, :PAIR]
                ).astype(jnp.bfloat16)
                weight_grad_ref[rank, part, 5 * PAIR :] = outside[:, PAIR:].astype(jnp.bfloat16)
                return inner

            return lax.fori_loop(0, width // BLOCK, block, carry)

        lax.fori_loop(0, ranks, weights, 0)


def fixed(shape):
    return pl.BlockSpec(shape, lambda step: (0,) * len(shape))


def kernel_params():
    return pltpu.CompilerParams(vmem_limit_bytes=VMEM_LIMIT, dimension_semantics=("arbitrary",))


def cost(flops, moved, raised=0):
    return pl.CostEstimate(flops=int(flops), bytes_accessed=int(moved), transcendentals=int(raised))


def group_spec(shape):
    return pl.BlockSpec((shape[0], 1, shape[2], shape[3]), lambda step: (0, step, 0, 0))


def anywhere(sources):
    return [pl.BlockSpec(memory_space=pl.ANY)] * len(sources)


def rank_spec(shape):
    return pl.BlockSpec((shape[0], shape[1], 1) + shape[3:], lambda step: (0, 0, step, 0, 0))


def attention_forward(sources, stream, mod, bias, bias_out, stride):
    shape = stream.shape
    width = shape[-1]
    ranks = bias.shape[0]
    tokens = shape[0] * shape[1] * shape[2]
    spec = group_spec(shape)
    low = jax.ShapeDtypeStruct(shape, jnp.bfloat16)
    wide = jax.ShapeDtypeStruct(shape, jnp.float32)
    project = jax.ShapeDtypeStruct((ranks,) + shape[:3] + (5 * PAIR,), jnp.bfloat16)
    mixed = jax.ShapeDtypeStruct((ranks,) + shape[:3] + (2 * PAIR,), jnp.bfloat16)
    return pl.pallas_call(
        partial(attention_forward_kernel, stride, len(sources)),
        grid=(shape[1],),
        in_specs=anywhere(sources) + [spec, fixed(mod.shape), fixed(bias.shape), fixed(bias_out.shape)],
        out_specs=[rank_spec(project.shape), rank_spec(mixed.shape), spec, spec],
        out_shape=[project, mixed, low, wide],
        scratch_shapes=[
            pltpu.VMEM((ranks, width, 6 * PAIR), jnp.bfloat16),
            pltpu.SemaphoreType.DMA((ranks,)),
        ],
        compiler_params=kernel_params(),
        cost_estimate=cost(8 * tokens * width * width * 1.5, tokens * width * 16),
        name="attention_forward",
    )(*sources, stream, mod, bias, bias_out)


def ffn_weights_scratch(ranks, width, part):
    return [
        pltpu.VMEM((ranks, width, part), jnp.bfloat16),
        pltpu.VMEM((ranks, width, part), jnp.bfloat16),
        pltpu.SemaphoreType.DMA((ranks,)),
        pltpu.SemaphoreType.DMA((ranks,)),
    ]


def ffn_forward(sources, middle, mod, bias_down, bias_up, result_shape, result_type):
    tokens, width = middle.shape
    ranks, _, part = bias_up.shape
    whole = fixed((tokens, width))
    return pl.pallas_call(
        partial(ffn_forward_kernel, SPLIT, len(sources)),
        grid=(ranks,),
        in_specs=anywhere(sources) + [
            whole, fixed(mod.shape), fixed(bias_down.shape),
            pl.BlockSpec((1, 1, part), lambda step: (step, 0, 0)),
        ],
        out_specs=[pl.BlockSpec((1, tokens, part), lambda step: (step, 0, 0)), whole, fixed(result_shape)],
        out_shape=[
            jax.ShapeDtypeStruct((ranks, tokens, part), jnp.bfloat16),
            jax.ShapeDtypeStruct((tokens, width), jnp.bfloat16),
            jax.ShapeDtypeStruct(result_shape, result_type),
        ],
        scratch_shapes=ffn_weights_scratch(ranks, width, part) + [
            pltpu.VMEM((tokens, width), jnp.bfloat16),
            pltpu.VMEM((tokens, width), jnp.float32),
        ],
        compiler_params=kernel_params(),
        cost_estimate=cost(4.8 * tokens * width * ranks * part, tokens * width * 14, tokens * ranks * part),
        name="ffn_forward",
    )(*sources, middle, mod, bias_down, bias_up)


def ffn_backward(sources, grad, middle, branch, hidden, mod):
    tokens, width = middle.shape
    ranks, _, part = hidden.shape
    whole = fixed((tokens, width))
    return pl.pallas_call(
        partial(ffn_backward_kernel, SPLIT, len(sources)),
        grid=(ranks,),
        in_specs=anywhere(sources) + [
            fixed(grad.shape), whole, whole,
            pl.BlockSpec((1, tokens, part), lambda step: (step, 0, 0)),
            fixed(mod.shape),
        ],
        out_specs=[
            whole,
            pl.BlockSpec((2, 1, width, part), lambda step: (0, step, 0, 0)),
            pl.BlockSpec((1, 1, part), lambda step: (step, 0, 0)),
            fixed((4, width)),
        ],
        out_shape=[
            jax.ShapeDtypeStruct((tokens, width), jnp.float32),
            jax.ShapeDtypeStruct((2, ranks, width, part), jnp.bfloat16),
            jax.ShapeDtypeStruct((ranks, 1, part), jnp.float32),
            jax.ShapeDtypeStruct((4, width), jnp.float32),
        ],
        scratch_shapes=ffn_weights_scratch(ranks, width, part) + [
            pltpu.VMEM((tokens, width), jnp.bfloat16),
            pltpu.VMEM((tokens, width), jnp.bfloat16),
            pltpu.VMEM((tokens, part), jnp.bfloat16),
            pltpu.VMEM((tokens, part), jnp.bfloat16),
            pltpu.VMEM((tokens, width), jnp.float32),
        ],
        compiler_params=kernel_params(),
        cost_estimate=cost(9.6 * tokens * width * ranks * part, tokens * width * 20, tokens * ranks * part),
        name="ffn_backward",
    )(*sources, grad, middle, branch, hidden, mod)


def attention_backward(sources, grad, stream, saved, mod, stride, result_type):
    project, mixed, branch = saved
    shape = stream.shape
    width = shape[-1]
    ranks = project.shape[0]
    tokens = shape[0] * shape[1] * shape[2]
    spec = group_spec(shape)
    return pl.pallas_call(
        partial(attention_backward_kernel, stride, len(sources)),
        grid=(shape[1],),
        in_specs=anywhere(sources) + [
            spec, spec, rank_spec(project.shape), rank_spec(mixed.shape), spec, fixed(mod.shape),
        ],
        out_specs=[
            spec, fixed((ranks, width, 6 * PAIR)), fixed((4, width)), fixed((ranks, 5 * PAIR)),
        ],
        out_shape=[
            jax.ShapeDtypeStruct(shape, result_type),
            jax.ShapeDtypeStruct((ranks, width, 6 * PAIR), jnp.bfloat16),
            jax.ShapeDtypeStruct((4, width), jnp.float32),
            jax.ShapeDtypeStruct((ranks, 5 * PAIR), jnp.float32),
        ],
        scratch_shapes=[
            pltpu.VMEM((ranks, width, 6 * PAIR), jnp.bfloat16),
            pltpu.SemaphoreType.DMA((ranks,)),
            pltpu.VMEM((2, tokens, width), jnp.bfloat16),
            pltpu.VMEM((ranks, tokens, 5 * PAIR), jnp.bfloat16),
            pltpu.VMEM((ranks, tokens, 2 * PAIR), jnp.bfloat16),
        ],
        compiler_params=kernel_params(),
        cost_estimate=cost(16 * tokens * width * width * 1.5, tokens * width * 20),
        name="attention_backward",
    )(*sources, grad, stream, project, mixed, branch, mod)


def pack_heads(block):
    query, key, value, outer = block
    return jnp.concatenate(
        [query[:, :PAIR], key[:, :PAIR], value[:, :PAIR], query[:, PAIR:], key[:, PAIR:],
         value[:, PAIR:], outer[:, PAIR:], outer[:, :PAIR]], axis=1
    )


def unpack_heads(packed):
    part = lambda start, size: packed[:, start : start + size]
    join = lambda first, last: jnp.concatenate([part(first, PAIR), part(last, HD)], axis=1)
    return jnp.stack(
        [join(0, 3 * PAIR), join(PAIR, 3 * PAIR + HD), join(2 * PAIR, 4 * PAIR), join(5 * PAIR, 4 * PAIR + HD)]
    )


def pack_bias(query, value, ranks):
    query, value = query.reshape(ranks, -1), value.reshape(ranks, -1)
    none = jnp.zeros((ranks, PAIR), query.dtype)
    return jnp.concatenate(
        [query[:, :PAIR], none, value[:, :PAIR], query[:, PAIR:], none[:, :HD], value[:, PAIR:], none[:, :HD]],
        axis=1,
    )[:, None]


def unpack_bias(sums):
    query = jnp.concatenate([sums[:, :PAIR], sums[:, 3 * PAIR : 3 * PAIR + HD]], axis=1)
    value = jnp.concatenate([sums[:, 2 * PAIR : 3 * PAIR], sums[:, 4 * PAIR : 4 * PAIR + HD]], axis=1)
    return query.reshape(-1), value.reshape(-1)


def adam_update(weight, first, second, grad, rate, decay):
    first_new = BETA_ONE * first + (1.0 - BETA_ONE) * grad
    second_new = BETA_TWO * second + (1.0 - BETA_TWO) * grad * grad
    corrected = (
        first_new
        / (1.0 - BETA_ONE**STEP)
        / (jnp.sqrt(second_new / (1.0 - BETA_TWO**STEP)) + ADAM_EPS)
    )
    weight_new = weight - rate * (corrected + decay * weight)
    return (weight_new, first_new, second_new, weight_new.astype(jnp.bfloat16))


def dot32(form, left, right):
    return jnp.einsum(form, left, right, preferred_element_type=jnp.float32)


def exchange(blocks):
    return lax.all_to_all(blocks, "tensor", split_axis=0, concat_axis=0, tiled=True)


def flip(value, axis, bit):
    count = lax.axis_size(axis)
    return lax.ppermute(value, axis, [(n, n ^ bit) for n in range(count)])


def far_shift(value, shift):
    far = lax.axis_size("dp") // 2
    return lax.ppermute(
        value, "dp", [(2 * n + side, 2 * ((n + shift) % far) + side) for n in range(far) for side in range(2)]
    )


def add_low(left, right):
    return (left.astype(jnp.float32) + right.astype(jnp.float32)).astype(jnp.bfloat16)


def pick(value, index, axis):
    return lax.dynamic_index_in_dim(value, index, axis, keepdims=False)


def in_pieces(rows):
    return rows % 16 == 0


def gather_weights(shard, after):
    kinds, rows, width = shard.shape
    if not in_pieces(rows):
        whole = lax.all_gather(shard, ("tensor", "dp"), axis=1, tiled=True)
        return (whole.reshape(kinds, -1, lax.axis_size("dp") * rows, width),), after
    if after is not None:
        shard, _ = lax.optimization_barrier((shard, after))
    far = lax.axis_size("dp") // 2
    line = [shard] + [far_shift(shard, shift) for shift in range(1, far)]
    half = far // 2
    mine = jnp.stack(line)
    over_side = flip(mine, "dp", 1)
    over_row = flip(mine, "tensor", 2)
    across = jnp.concatenate([flip(over_side[:half], "tensor", 2), flip(over_row[half:], "dp", 1)])
    own = jnp.stack([jnp.stack([mine, over_side]), jnp.stack([over_row, across])])
    return (own, flip(own, "tensor", 1)), line[-1]


def scatter_weights(grads):
    kinds, ranks, width, cols = grads.shape
    dp = lax.axis_size("dp")
    rows = width // dp
    if not in_pieces(rows):
        flat = grads.reshape(kinds, ranks * width, cols)
        return lax.psum_scatter(flat, ("tensor", "dp"), scatter_dimension=1, tiled=True)
    far, half = dp // 2, dp // 4
    device, rank = lax.axis_index("dp"), lax.axis_index("tensor")
    place, side, row, core = device // 2, device % 2, rank // 2, rank % 2
    grads = grads.reshape(kinds, 2, 2, far, 2, rows, cols)
    grads = add_low(pick(grads, core, 2), flip(pick(grads, 1 - core, 2), "tensor", 1))
    first, last = grads[:, :, :half], grads[:, :, half:]
    first = add_low(pick(first, side, 3), flip(pick(first, 1 - side, 3), "dp", 1))
    last = add_low(pick(last, row, 1), flip(pick(last, 1 - row, 1), "tensor", 2))
    first = add_low(pick(first, row, 1), flip(pick(first, 1 - row, 1), "tensor", 2))
    last = add_low(pick(last, side, 2), flip(pick(last, 1 - side, 2), "dp", 1))
    line = jnp.concatenate([first, last], axis=1)
    total = pick(line, place, 1).astype(jnp.float32)
    for shift in range(1, far):
        total = total + far_shift(pick(line, (place + shift) % far, 1), shift).astype(jnp.float32)
    return total


def per_device(
    clips, cotangent, timesteps, labels, time_table, class_table,
    attention_weights, attention_first, attention_second,
    ffn_weights, ffn_first, ffn_second,
    modulation_weights, modulation_first, modulation_second,
    bias_vectors, bias_first, bias_second,
):
    layers, kinds, rows, cols = attention_weights.shape
    _, frames, patches, width = clips.shape
    mod_rows = modulation_weights.shape[1]
    bias_cols = bias_vectors.shape[1]
    dp, tp = lax.axis_size("dp"), lax.axis_size("tensor")
    position = lax.axis_index("dp") * tp + lax.axis_index("tensor")
    tokens = frames * patches
    strip = patches // (tp * frames)
    blocks = (tp, frames, frames * strip, width)
    pieces = (tp * frames, frames, strip, width)

    embed = time_table[timesteps] + class_table[labels]
    cond_act = jax.nn.silu(embed).astype(jnp.bfloat16)
    low = bias_vectors.astype(jnp.bfloat16).reshape(-1)
    row = jnp.concatenate([cond_act[0], low])
    row = jnp.pad(row, (0, -row.shape[0] % 128)).reshape(1, -1, 128)
    gathered = lax.all_gather(row, BOTH, axis=0, tiled=True).reshape(dp * tp, -1)
    cond_all = gathered[::tp, :width]
    bias_low = gathered[:, width : width + layers * bias_cols].reshape(dp * tp, layers, bias_cols)
    bias_low = bias_low.transpose(1, 0, 2).reshape(layers, -1).astype(jnp.float32)
    cond_rows = lax.dynamic_slice_in_dim(cond_all, position * mod_rows, mod_rows, axis=1)
    modulation_low = modulation_weights.astype(jnp.bfloat16)
    mod_part = dot32("ck,lke->cle", cond_rows, modulation_low)
    mod_part = lax.psum_scatter(mod_part, "dp", scatter_dimension=0, tiled=True)
    mod = lax.psum(mod_part, "tensor")[0]
    mod_width = mod.shape[-1]
    mod = (mod + bias_low[:, -mod_width:]).reshape(layers, 6, width)
    hidden_width = bias_low.shape[1] - mod_width - 4 * width
    bias_up = bias_low[:, 3 * width : 3 * width + hidden_width].reshape(layers, tp, 1, -1)
    bias_out = bias_low[:, None, 2 * width : 3 * width]
    bias_down = bias_low[:, None, 3 * width + hidden_width : 4 * width + hidden_width]
    bias_project = [
        pack_bias(bias_low[layer, :width], bias_low[layer, width : 2 * width], tp) for layer in range(layers)
    ]

    attention, ffn, after = [], [], None
    for layer in range(layers):
        packed = pack_heads(attention_weights[layer].astype(jnp.bfloat16))[None]
        packed, after = gather_weights(packed, after)
        attention.append(packed)
        wide, after = gather_weights(ffn_weights[layer].astype(jnp.bfloat16), after)
        ffn.append(wide)

    by_patch = lambda v: v.reshape(frames, tp * frames, strip, width).transpose(1, 0, 2, 3)
    cot = exchange(by_patch(cotangent[0]).reshape(blocks))

    def forward(layer, stream, stride, result_shape):
        project, mixed, branch, middle = attention_forward(
            attention[layer], stream, mod[layer], bias_project[layer], bias_out[layer], stride
        )
        middle = middle.reshape(tokens, width)
        hidden, down, result = ffn_forward(
            ffn[layer], middle, mod[layer], bias_down[layer], bias_up[layer], result_shape, jnp.bfloat16
        )
        return result, ((project, mixed, branch), middle, hidden, down)

    def backward(layer, grad, stream, saved, stride, result_type):
        heads, middle, hidden, down = saved
        grad_middle, ffn_grad, up_sum, low_sums = ffn_backward(
            ffn[layer], grad, middle, down, hidden, mod[layer]
        )
        ffn_grad = scatter_weights(ffn_grad)
        grad, attention_grad, sums, project_sum = attention_backward(
            attention[layer], grad_middle.reshape(stream.shape), stream, heads, mod[layer], stride, result_type
        )
        attention_grad = unpack_heads(scatter_weights(attention_grad[None])[0])
        small = jnp.concatenate(
            [*unpack_bias(project_sum), sums[0], up_sum.reshape(-1), low_sums[0],
             sums[1:].reshape(-1), low_sums[1:].reshape(-1)]
        )
        return grad, attention_grad, ffn_grad, small

    first = clips[0].reshape(1, frames, patches, width)
    second, saved_first = forward(0, first, 0, pieces)
    second = exchange(second.reshape(blocks))
    result, saved_second = forward(1, second, strip, (tokens, width))
    result = exchange(result.reshape(blocks)).reshape(pieces)
    output = result.transpose(1, 0, 2, 3).reshape(clips.shape)

    grad, attention_b, ffn_b, small_b = backward(
        1, cot.reshape(tokens, width), second, saved_second, strip, jnp.bfloat16
    )
    grad = exchange(grad).reshape(pieces)
    grad, attention_a, ffn_a, small_a = backward(0, grad, first, saved_first, 0, jnp.float32)
    input_grad = grad.reshape(clips.shape)

    small = lax.psum(jnp.stack([small_a, small_b]), "tensor")
    token_width = small.shape[1] - mod_width
    small = lax.all_gather(small.reshape(1, -1, 128), "dp", axis=0, tiled=True).reshape(dp, layers, -1)
    grad_mod_low = small[..., token_width:].astype(jnp.bfloat16)
    grad_bias_all = jnp.concatenate(
        [small[..., :token_width], grad_mod_low.astype(jnp.float32)], axis=-1
    ).sum(axis=0)
    grad_bias = lax.dynamic_slice_in_dim(grad_bias_all, position * bias_cols, bias_cols, axis=1)
    grad_mod_weight = dot32("ck,cle->lke", cond_rows, grad_mod_low)
    grad_act = dot32("cle,lke->ck", grad_mod_low, modulation_low)
    grad_act = lax.all_gather(grad_act, BOTH, axis=0)
    grad_act = lax.dynamic_index_in_dim(grad_act, lax.axis_index("dp"), axis=1, keepdims=False)
    silu_value, silu_pull = jax.vjp(jax.nn.silu, embed)
    cond_grad = silu_pull(grad_act.reshape(1, width))[0]

    grad_attention = jnp.stack([attention_a, attention_b]).astype(jnp.float32)
    grad_ffn = jnp.stack([ffn_a, ffn_b]).astype(jnp.float32)
    return (output, input_grad, cond_grad) + (
        adam_update(attention_weights, attention_first, attention_second, grad_attention, MATRIX_RATE, MATRIX_DECAY)
        + adam_update(ffn_weights, ffn_first, ffn_second, grad_ffn, MATRIX_RATE, MATRIX_DECAY)
        + adam_update(modulation_weights, modulation_first, modulation_second, grad_mod_weight, MATRIX_RATE, MATRIX_DECAY)
        + adam_update(bias_vectors, bias_first, bias_second, grad_bias, VECTOR_RATE, 0.0)
    )


def solution(mesh):
    tokens = P("dp", "tensor", None, None)
    matrix = P(None, None, "dp", "tensor")
    modulation = P(None, BOTH, None)
    vector = P(None, BOTH)
    return jax.shard_map(
        per_device,
        mesh=mesh,
        in_specs=(tokens, tokens, P("dp"), P("dp"), P(), P())
        + (matrix,) * 6 + (modulation,) * 3 + (vector,) * 3,
        out_specs=(tokens, tokens, P("dp", None)) + (matrix,) * 8 + (modulation,) * 4 + (vector,) * 4,
        check_vma=False,
    )
```

```python
from functools import partial

import jax
import jax.numpy as jnp
from jax import lax
from jax.experimental import pallas as pl
from jax.experimental.pallas import tpu as pltpu
from jax.sharding import PartitionSpec as P

HD = 64
PAIR = 128
BLOCK = 256
SPLIT = 4
STEP = 10
BETA_ONE = 0.9
BETA_TWO = 0.999
ADAM_EPS = 1e-08
MATRIX_RATE = 0.04
VECTOR_RATE = 0.2
MATRIX_DECAY = 0.1
NORM_EPS = 1e-06
GELU_A = (2.0 / 3.141592653589793) ** 0.5
GELU_B = 0.044715
BLOCKED = -1e30
VMEM_LIMIT = 56 * 1024 * 1024
BOTH = ("dp", "tensor")


def mm(left, right, dims=((1,), (0,))):
    return lax.dot_general(left, right, (dims, ((), ())), preferred_element_type=jnp.float32)


def norm_parts(value):
    average = jnp.mean(value, axis=-1, keepdims=True)
    centred = value - average
    spread = jnp.mean(centred * centred, axis=-1, keepdims=True)
    inverse = lax.rsqrt(spread + NORM_EPS)
    return centred * inverse, inverse


def norm_back(grad, shape, inverse):
    first = jnp.mean(grad, axis=-1, keepdims=True)
    second = jnp.mean(grad * shape, axis=-1, keepdims=True)
    return inverse * (grad - first - shape * second)


def rows_of(ref):
    value = ref[...]
    return value.reshape(-1, value.shape[-1])


def put(ref, value):
    ref[...] = value.reshape(ref.shape).astype(ref.dtype)


def add_rows(ref, index, value):
    ref[pl.ds(index, 1), :] += jnp.sum(value, axis=0, keepdims=True)


def half_masks(rows):
    lane = lax.broadcasted_iota(jnp.int32, (rows, PAIR), 1)
    return lane < HD


def same_patch(tokens, stride):
    row = lax.broadcasted_iota(jnp.int32, (tokens, tokens), 0)
    column = lax.broadcasted_iota(jnp.int32, (tokens, tokens), 1)
    return lax.rem(row, stride) == lax.rem(column, stride)


def swap_halves(value):
    return pltpu.roll(value, HD, 1)


def start_loads(sources, kind, target, semaphores):
    if len(sources) == 1:
        for rank in range(target.shape[0]):
            pltpu.make_async_copy(sources[0].at[kind, rank], target.at[rank], semaphores.at[rank]).start()
        return
    far, near, rows = sources[0].shape[2], 2, sources[0].shape[4]
    device, rank = lax.axis_index("dp"), lax.axis_index("tensor")
    for core, source in enumerate(sources):
        for row in range(2):
            for side in range(2):
                for back in range(far):
                    where = lax.rem(device // near + far - back, far) * near + (device % near + side) % near
                    owner = (rank // 2 + row) % 2 * 2 + (rank % 2 + core) % 2
                    pltpu.make_async_copy(
                        source.at[row, side, back, kind],
                        target.at[owner, pl.ds(pl.multiple_of(where * rows, rows), rows)],
                        semaphores.at[owner],
                    ).start()


def wait_loads(target, semaphores, rank):
    pltpu.make_async_copy(target.at[rank], target.at[rank], semaphores.at[rank]).wait()


def softmax_rows(scores, axis):
    raised = jnp.exp(scores - jnp.max(scores, axis=axis, keepdims=True))
    return raised * (1.0 / jnp.sum(raised, axis=axis, keepdims=True))


def attention_forward_kernel(stride, count, *refs):
    sources = refs[:count]
    (stream_ref, mod_ref, bias_ref, bias_out_ref,
     project_ref, mixed_ref, branch_ref, middle_ref, weight_ref, semaphores) = refs[count:]
    ranks = weight_ref.shape[0]

    @pl.when(pl.program_id(0) == 0)
    def _():
        start_loads(sources, 0, weight_ref, semaphores)

    stream = rows_of(stream_ref).astype(jnp.float32)
    tokens, width = stream.shape
    shape, _ = norm_parts(stream)
    normed = (shape * (1.0 + mod_ref[1:2]) + mod_ref[0:1]).astype(jnp.bfloat16)
    lower = half_masks(tokens)
    allowed = same_patch(tokens, stride) if stride else None

    @pl.when(pl.program_id(0) == 0)
    def _():
        for rank in range(ranks):
            wait_loads(weight_ref, semaphores, rank)

    def one_head(chosen, key, value):
        scores = mm(chosen.astype(jnp.bfloat16), key, ((1,), (1,)))
        if stride:
            scores = jnp.where(allowed, scores, BLOCKED)
        return mm(softmax_rows(scores, -1).astype(jnp.bfloat16), value)

    branch = None
    for rank in range(ranks):
        project = (mm(normed, weight_ref[rank, :, : 5 * PAIR]) + bias_ref[rank]).astype(jnp.bfloat16)
        project_ref[rank] = project.reshape(project_ref.shape[1:])
        query = project[:, :PAIR].astype(jnp.float32) * HD**-0.5
        key, value = project[:, PAIR : 2 * PAIR], project[:, 2 * PAIR : 3 * PAIR]
        first = one_head(jnp.where(lower, query, 0.0), key, value)
        second = one_head(jnp.where(lower, 0.0, query), key, value)
        both = project[:, 3 * PAIR : 4 * PAIR].astype(jnp.float32)
        last = one_head(
            jnp.where(lower, both * HD**-0.5, 0.0),
            swap_halves(both).astype(jnp.bfloat16),
            project[:, 4 * PAIR : 5 * PAIR],
        )
        mixed = jnp.concatenate(
            [jnp.where(lower, 0.0, swap_halves(last)), jnp.where(lower, first, second)], axis=1
        ).astype(jnp.bfloat16)
        mixed_ref[rank] = mixed.reshape(mixed_ref.shape[1:])
        term = mm(mixed, weight_ref[rank, :, 4 * PAIR :], ((1,), (1,)))
        branch = term if branch is None else branch + term
    branch = branch + bias_out_ref[...]
    put(branch_ref, branch)
    put(middle_ref, stream + mod_ref[2:3] * branch)


def gelu_parts(value):
    square = value * value
    bent = jnp.tanh(value * (GELU_A + (GELU_A * GELU_B) * square))
    half = 0.5 * (1.0 + bent)
    slope = half + (0.5 * value) * (1.0 - bent * bent) * (GELU_A + (3.0 * GELU_A * GELU_B) * square)
    return value * half, slope


def ffn_forward_kernel(split, count, *refs):
    sources = refs[:count]
    (middle_ref, mod_ref, bias_ref, bias_up_ref,
     hidden_ref, branch_ref, result_ref,
     up_ref, down_ref, up_semaphores, down_semaphores, second_ref, total_ref) = refs[count:]
    step = pl.program_id(0)
    tokens = middle_ref.shape[0]
    chunk = tokens // split

    @pl.when(step == 0)
    def _():
        start_loads(sources, 0, up_ref, up_semaphores)
        start_loads(sources, 1, down_ref, down_semaphores)

        def norm_chunk(index, carry):
            rows = pl.ds(pl.multiple_of(index * chunk, chunk), chunk)
            shape, _ = norm_parts(middle_ref[rows, :])
            second_ref[rows, :] = (shape * (1.0 + mod_ref[4:5]) + mod_ref[3:4]).astype(jnp.bfloat16)
            return carry

        lax.fori_loop(0, split, norm_chunk, 0)

    wait_loads(up_ref, up_semaphores, step)
    wait_loads(down_ref, down_semaphores, step)

    def one(index, carry):
        rows = pl.ds(pl.multiple_of(index * chunk, chunk), chunk)
        hidden = mm(second_ref[rows, :], up_ref[step]) + bias_up_ref[0]
        hidden_ref[0, rows, :] = hidden.astype(jnp.bfloat16)
        active, _ = gelu_parts(hidden)
        part = mm(active.astype(jnp.bfloat16), down_ref[step], ((1,), (1,)))
        total_ref[rows, :] = jnp.where(step == 0, 0.0, total_ref[rows, :]) + part
        return carry

    lax.fori_loop(0, split, one, 0)

    @pl.when(step == pl.num_programs(0) - 1)
    def _():
        for index in range(split):
            rows = slice(index * chunk, (index + 1) * chunk)
            down = total_ref[rows, :] + bias_ref[...]
            branch_ref[rows, :] = down.astype(jnp.bfloat16)
            result = middle_ref[rows, :] + mod_ref[5:6] * down
            store_frame(result_ref, index, chunk, result)


def store_frame(ref, index, chunk, value):
    if len(ref.shape) == 2:
        ref[index * chunk : (index + 1) * chunk, :] = value.astype(ref.dtype)
    else:
        ref[:, index] = value.reshape(ref.shape[0], ref.shape[2], ref.shape[3]).astype(ref.dtype)


def load_frame(ref, index, chunk):
    if len(ref.shape) == 2:
        return ref[index * chunk : (index + 1) * chunk, :].astype(jnp.float32)
    value = ref[:, index]
    return value.reshape(chunk, value.shape[-1]).astype(jnp.float32)


def ffn_backward_kernel(split, count, *refs):
    sources = refs[:count]
    (grad_ref, middle_ref, branch_ref, hidden_ref, mod_ref,
     grad_middle_ref, weight_grad_ref, up_sum_ref, sums_ref,
     up_ref, down_ref, up_semaphores, down_semaphores,
     second_ref, low_ref, active_ref, slope_ref, total_ref) = refs[count:]
    step = pl.program_id(0)
    tokens, width = middle_ref.shape
    chunk = tokens // split

    @pl.when(step == 0)
    def _():
        start_loads(sources, 0, up_ref, up_semaphores)
        start_loads(sources, 1, down_ref, down_semaphores)
        sums_ref[...] = jnp.zeros_like(sums_ref)
        for index in range(split):
            rows = slice(index * chunk, (index + 1) * chunk)
            grad = load_frame(grad_ref, index, chunk)
            low = (mod_ref[5:6] * grad).astype(jnp.bfloat16)
            low_ref[rows, :] = low
            add_rows(sums_ref, 0, low.astype(jnp.float32))
            add_rows(sums_ref, 3, grad * branch_ref[rows, :].astype(jnp.float32))
            shape, _ = norm_parts(middle_ref[rows, :])
            second_ref[rows, :] = (shape * (1.0 + mod_ref[4:5]) + mod_ref[3:4]).astype(jnp.bfloat16)

    up_sum_ref[...] = jnp.zeros_like(up_sum_ref)
    wait_loads(up_ref, up_semaphores, step)
    wait_loads(down_ref, down_semaphores, step)

    def one(index, carry):
        rows = pl.ds(pl.multiple_of(index * chunk, chunk), chunk)
        active, slope = gelu_parts(hidden_ref[0, rows, :].astype(jnp.float32))
        active_ref[rows, :] = active.astype(jnp.bfloat16)
        low = (mm(low_ref[rows, :], down_ref[step]) * slope).astype(jnp.bfloat16)
        slope_ref[rows, :] = low
        up_sum_ref[0] += jnp.sum(low.astype(jnp.float32), axis=0, keepdims=True)
        part = mm(low, up_ref[step], ((1,), (1,)))
        total_ref[rows, :] = jnp.where(step == 0, 0.0, total_ref[rows, :]) + part
        return carry

    lax.fori_loop(0, split, one, 0)

    def weights(index, carry):
        part = pl.ds(pl.multiple_of(index * BLOCK, BLOCK), BLOCK)
        weight_grad_ref[0, 0, part, :] = mm(second_ref[:, part], slope_ref[...], ((0,), (0,))).astype(
            jnp.bfloat16
        )
        weight_grad_ref[1, 0, part, :] = mm(low_ref[:, part], active_ref[...], ((0,), (0,))).astype(
            jnp.bfloat16
        )
        return carry

    lax.fori_loop(0, width // BLOCK, weights, 0)

    @pl.when(step == pl.num_programs(0) - 1)
    def _():
        for index in range(split):
            rows = slice(index * chunk, (index + 1) * chunk)
            shape, inverse = norm_parts(middle_ref[rows, :])
            grad = total_ref[rows, :]
            add_rows(sums_ref, 1, grad)
            add_rows(sums_ref, 2, grad * shape)
            back = norm_back(grad * (1.0 + mod_ref[4:5]), shape, inverse)
            grad_middle_ref[rows, :] = load_frame(grad_ref, index, chunk) + back


def attention_backward_kernel(stride, count, *refs):
    sources = refs[:count]
    (grad_ref, stream_ref, project_ref, mixed_ref, branch_ref, mod_ref,
     grad_stream_ref, weight_grad_ref, sums_ref, project_sum_ref,
     weight_ref, semaphores, left_ref, right_ref, outer_ref) = refs[count:]
    step = pl.program_id(0)
    ranks = weight_ref.shape[0]

    @pl.when(step == 0)
    def _():
        start_loads(sources, 0, weight_ref, semaphores)
        sums_ref[...] = jnp.zeros_like(sums_ref)
        project_sum_ref[...] = jnp.zeros_like(project_sum_ref)

    grad_middle = rows_of(grad_ref)
    tokens, width = grad_middle.shape
    stream = rows_of(stream_ref).astype(jnp.float32)
    shape, inverse = norm_parts(stream)
    rows = pl.ds(pl.multiple_of(step * tokens, tokens), tokens)
    normed = (shape * (1.0 + mod_ref[1:2]) + mod_ref[0:1]).astype(jnp.bfloat16)
    low = (mod_ref[2:3] * grad_middle).astype(jnp.bfloat16)
    left_ref[0, rows, :] = normed
    left_ref[1, rows, :] = low
    add_rows(sums_ref, 0, low.astype(jnp.float32))
    add_rows(sums_ref, 3, grad_middle * rows_of(branch_ref).astype(jnp.float32))
    lower = half_masks(tokens)
    allowed = same_patch(tokens, stride) if stride else None
    scale = HD**-0.5

    @pl.when(step == 0)
    def _():
        for rank in range(ranks):
            wait_loads(weight_ref, semaphores, rank)

    def one_head(chosen, key, value, taken):
        scores = mm(key, chosen.astype(jnp.bfloat16), ((1,), (1,)))
        if stride:
            scores = jnp.where(allowed, scores, BLOCKED)
        probs = softmax_rows(scores, 0)
        grad_probs = mm(value, taken.astype(jnp.bfloat16), ((1,), (1,)))
        inner = jnp.sum(grad_probs * probs, axis=0, keepdims=True)
        return probs.astype(jnp.bfloat16), (probs * (grad_probs - inner)).astype(jnp.bfloat16)

    grad_normed = None
    for rank in range(ranks):
        project = project_ref[rank].reshape(tokens, 5 * PAIR)
        mixed = mixed_ref[rank].reshape(tokens, 2 * PAIR)
        outer_ref[rank, rows, :] = mixed
        grad_mixed = mm(low, weight_ref[rank, :, 4 * PAIR :]).astype(jnp.bfloat16)
        query, key, value = (project[:, n * PAIR : (n + 1) * PAIR] for n in range(3))
        query_wide = query.astype(jnp.float32) * scale
        pair = grad_mixed[:, PAIR:]
        pair_wide = pair.astype(jnp.float32)
        outs = []
        for keep in (lower, ~lower):
            probs, grad_scores = one_head(
                jnp.where(keep, query_wide, 0.0), key, value, jnp.where(keep, pair_wide, 0.0)
            )
            outs.append(
                (mm(grad_scores, key, ((0,), (0,))), mm(grad_scores, query), mm(probs, pair))
            )
        parts = [
            jnp.where(lower, one, two) * factor
            for one, two, factor in zip(outs[0], outs[1], (scale, scale, 1.0))
        ]
        both = project[:, 3 * PAIR : 4 * PAIR].astype(jnp.float32)
        swapped = swap_halves(both).astype(jnp.bfloat16)
        single = swap_halves(grad_mixed[:, :PAIR].astype(jnp.float32))
        probs, grad_scores = one_head(
            jnp.where(lower, both * scale, 0.0),
            swapped,
            project[:, 4 * PAIR :],
            jnp.where(lower, single, 0.0),
        )
        parts.append(
            jnp.where(lower, mm(grad_scores, swapped, ((0,), (0,))), mm(grad_scores, swapped)) * scale
        )
        parts.append(jnp.where(lower, mm(probs, single.astype(jnp.bfloat16)), 0.0))
        whole = jnp.concatenate(parts, axis=1).astype(jnp.bfloat16)
        right_ref[rank, rows, :] = whole
        add_rows(project_sum_ref, rank, whole.astype(jnp.float32))
        term = mm(whole, weight_ref[rank, :, : 5 * PAIR], ((1,), (1,)))
        grad_normed = term if grad_normed is None else grad_normed + term
    add_rows(sums_ref, 1, grad_normed)
    add_rows(sums_ref, 2, grad_normed * shape)
    back = norm_back(grad_normed * (1.0 + mod_ref[1:2]), shape, inverse)
    put(grad_stream_ref, grad_middle + back)

    @pl.when(step == pl.num_programs(0) - 1)
    def _():
        def weights(rank, carry):
            def block(index, inner):
                part = pl.ds(pl.multiple_of(index * BLOCK, BLOCK), BLOCK)
                inside = mm(left_ref[0, :, part], right_ref[rank], ((0,), (0,)))
                outside = mm(left_ref[1, :, part], outer_ref[rank], ((0,), (0,)))
                weight_grad_ref[rank, part, : 4 * PAIR] = inside[:, : 4 * PAIR].astype(jnp.bfloat16)
                weight_grad_ref[rank, part, 4 * PAIR : 5 * PAIR] = (
                    inside[:, 4 * PAIR :] + outside[:, :PAIR]
                ).astype(jnp.bfloat16)
                weight_grad_ref[rank, part, 5 * PAIR :] = outside[:, PAIR:].astype(jnp.bfloat16)
                return inner

            return lax.fori_loop(0, width // BLOCK, block, carry)

        lax.fori_loop(0, ranks, weights, 0)


def fixed(shape):
    return pl.BlockSpec(shape, lambda step: (0,) * len(shape))


def kernel_params():
    return pltpu.CompilerParams(vmem_limit_bytes=VMEM_LIMIT, dimension_semantics=("arbitrary",))


def cost(flops, moved, raised=0):
    return pl.CostEstimate(flops=int(flops), bytes_accessed=int(moved), transcendentals=int(raised))


def group_spec(shape):
    return pl.BlockSpec((shape[0], 1, shape[2], shape[3]), lambda step: (0, step, 0, 0))


def anywhere(sources):
    return [pl.BlockSpec(memory_space=pl.ANY)] * len(sources)


def rank_spec(shape):
    return pl.BlockSpec((shape[0], shape[1], 1) + shape[3:], lambda step: (0, 0, step, 0, 0))


def attention_forward(sources, stream, mod, bias, bias_out, stride):
    shape = stream.shape
    width = shape[-1]
    ranks = bias.shape[0]
    tokens = shape[0] * shape[1] * shape[2]
    spec = group_spec(shape)
    low = jax.ShapeDtypeStruct(shape, jnp.bfloat16)
    wide = jax.ShapeDtypeStruct(shape, jnp.float32)
    project = jax.ShapeDtypeStruct((ranks,) + shape[:3] + (5 * PAIR,), jnp.bfloat16)
    mixed = jax.ShapeDtypeStruct((ranks,) + shape[:3] + (2 * PAIR,), jnp.bfloat16)
    return pl.pallas_call(
        partial(attention_forward_kernel, stride, len(sources)),
        grid=(shape[1],),
        in_specs=anywhere(sources) + [spec, fixed(mod.shape), fixed(bias.shape), fixed(bias_out.shape)],
        out_specs=[rank_spec(project.shape), rank_spec(mixed.shape), spec, spec],
        out_shape=[project, mixed, low, wide],
        scratch_shapes=[
            pltpu.VMEM((ranks, width, 6 * PAIR), jnp.bfloat16),
            pltpu.SemaphoreType.DMA((ranks,)),
        ],
        compiler_params=kernel_params(),
        cost_estimate=cost(8 * tokens * width * width * 1.5, tokens * width * 16),
        name="attention_forward",
    )(*sources, stream, mod, bias, bias_out)


def ffn_weights_scratch(ranks, width, part):
    return [
        pltpu.VMEM((ranks, width, part), jnp.bfloat16),
        pltpu.VMEM((ranks, width, part), jnp.bfloat16),
        pltpu.SemaphoreType.DMA((ranks,)),
        pltpu.SemaphoreType.DMA((ranks,)),
    ]


def ffn_forward(sources, middle, mod, bias_down, bias_up, result_shape, result_type):
    tokens, width = middle.shape
    ranks, _, part = bias_up.shape
    whole = fixed((tokens, width))
    return pl.pallas_call(
        partial(ffn_forward_kernel, SPLIT, len(sources)),
        grid=(ranks,),
        in_specs=anywhere(sources) + [
            whole, fixed(mod.shape), fixed(bias_down.shape),
            pl.BlockSpec((1, 1, part), lambda step: (step, 0, 0)),
        ],
        out_specs=[pl.BlockSpec((1, tokens, part), lambda step: (step, 0, 0)), whole, fixed(result_shape)],
        out_shape=[
            jax.ShapeDtypeStruct((ranks, tokens, part), jnp.bfloat16),
            jax.ShapeDtypeStruct((tokens, width), jnp.bfloat16),
            jax.ShapeDtypeStruct(result_shape, result_type),
        ],
        scratch_shapes=ffn_weights_scratch(ranks, width, part) + [
            pltpu.VMEM((tokens, width), jnp.bfloat16),
            pltpu.VMEM((tokens, width), jnp.float32),
        ],
        compiler_params=kernel_params(),
        cost_estimate=cost(4.8 * tokens * width * ranks * part, tokens * width * 14, tokens * ranks * part),
        name="ffn_forward",
    )(*sources, middle, mod, bias_down, bias_up)


def ffn_backward(sources, grad, middle, branch, hidden, mod):
    tokens, width = middle.shape
    ranks, _, part = hidden.shape
    whole = fixed((tokens, width))
    return pl.pallas_call(
        partial(ffn_backward_kernel, SPLIT, len(sources)),
        grid=(ranks,),
        in_specs=anywhere(sources) + [
            fixed(grad.shape), whole, whole,
            pl.BlockSpec((1, tokens, part), lambda step: (step, 0, 0)),
            fixed(mod.shape),
        ],
        out_specs=[
            whole,
            pl.BlockSpec((2, 1, width, part), lambda step: (0, step, 0, 0)),
            pl.BlockSpec((1, 1, part), lambda step: (step, 0, 0)),
            fixed((4, width)),
        ],
        out_shape=[
            jax.ShapeDtypeStruct((tokens, width), jnp.float32),
            jax.ShapeDtypeStruct((2, ranks, width, part), jnp.bfloat16),
            jax.ShapeDtypeStruct((ranks, 1, part), jnp.float32),
            jax.ShapeDtypeStruct((4, width), jnp.float32),
        ],
        scratch_shapes=ffn_weights_scratch(ranks, width, part) + [
            pltpu.VMEM((tokens, width), jnp.bfloat16),
            pltpu.VMEM((tokens, width), jnp.bfloat16),
            pltpu.VMEM((tokens, part), jnp.bfloat16),
            pltpu.VMEM((tokens, part), jnp.bfloat16),
            pltpu.VMEM((tokens, width), jnp.float32),
        ],
        compiler_params=kernel_params(),
        cost_estimate=cost(9.6 * tokens * width * ranks * part, tokens * width * 20, tokens * ranks * part),
        name="ffn_backward",
    )(*sources, grad, middle, branch, hidden, mod)


def attention_backward(sources, grad, stream, saved, mod, stride, result_type):
    project, mixed, branch = saved
    shape = stream.shape
    width = shape[-1]
    ranks = project.shape[0]
    tokens = shape[0] * shape[1] * shape[2]
    spec = group_spec(shape)
    return pl.pallas_call(
        partial(attention_backward_kernel, stride, len(sources)),
        grid=(shape[1],),
        in_specs=anywhere(sources) + [
            spec, spec, rank_spec(project.shape), rank_spec(mixed.shape), spec, fixed(mod.shape),
        ],
        out_specs=[
            spec, fixed((ranks, width, 6 * PAIR)), fixed((4, width)), fixed((ranks, 5 * PAIR)),
        ],
        out_shape=[
            jax.ShapeDtypeStruct(shape, result_type),
            jax.ShapeDtypeStruct((ranks, width, 6 * PAIR), jnp.bfloat16),
            jax.ShapeDtypeStruct((4, width), jnp.float32),
            jax.ShapeDtypeStruct((ranks, 5 * PAIR), jnp.float32),
        ],
        scratch_shapes=[
            pltpu.VMEM((ranks, width, 6 * PAIR), jnp.bfloat16),
            pltpu.SemaphoreType.DMA((ranks,)),
            pltpu.VMEM((2, tokens, width), jnp.bfloat16),
            pltpu.VMEM((ranks, tokens, 5 * PAIR), jnp.bfloat16),
            pltpu.VMEM((ranks, tokens, 2 * PAIR), jnp.bfloat16),
        ],
        compiler_params=kernel_params(),
        cost_estimate=cost(16 * tokens * width * width * 1.5, tokens * width * 20),
        name="attention_backward",
    )(*sources, grad, stream, project, mixed, branch, mod)


def pack_heads(block):
    query, key, value, outer = block
    return jnp.concatenate(
        [query[:, :PAIR], key[:, :PAIR], value[:, :PAIR], query[:, PAIR:], key[:, PAIR:],
         value[:, PAIR:], outer[:, PAIR:], outer[:, :PAIR]], axis=1
    )


def unpack_heads(packed):
    part = lambda start, size: packed[:, start : start + size]
    join = lambda first, last: jnp.concatenate([part(first, PAIR), part(last, HD)], axis=1)
    return jnp.stack(
        [join(0, 3 * PAIR), join(PAIR, 3 * PAIR + HD), join(2 * PAIR, 4 * PAIR), join(5 * PAIR, 4 * PAIR + HD)]
    )


def pack_bias(query, value, ranks):
    query, value = query.reshape(ranks, -1), value.reshape(ranks, -1)
    none = jnp.zeros((ranks, PAIR), query.dtype)
    return jnp.concatenate(
        [query[:, :PAIR], none, value[:, :PAIR], query[:, PAIR:], none[:, :HD], value[:, PAIR:], none[:, :HD]],
        axis=1,
    )[:, None]


def unpack_bias(sums):
    query = jnp.concatenate([sums[:, :PAIR], sums[:, 3 * PAIR : 3 * PAIR + HD]], axis=1)
    value = jnp.concatenate([sums[:, 2 * PAIR : 3 * PAIR], sums[:, 4 * PAIR : 4 * PAIR + HD]], axis=1)
    return query.reshape(-1), value.reshape(-1)


def place():
    return lax.axis_index("dp"), lax.axis_index("tensor"), lax.axis_size("dp"), lax.axis_size("tensor")


def greet_all():
    device, rank, dp, tp = place()
    me, count = device * tp + rank, dp * tp
    barrier = pltpu.get_barrier_semaphore()

    def greet(index, carry):
        peer = lax.rem(me + index, count)
        pl.semaphore_signal(
            barrier, inc=1, device_id=(peer // tp, lax.rem(peer, tp)), device_id_type=pl.DeviceIdType.MESH
        )
        return carry

    lax.fori_loop(1, count, greet, 0)
    pl.semaphore_wait(barrier, count - 1)


def push(source, target, send, receive, device, rank):
    pltpu.make_async_remote_copy(
        src_ref=source, dst_ref=target, send_sem=send, recv_sem=receive,
        device_id=(device, rank), device_id_type=pl.DeviceIdType.MESH,
    ).start()


def wait_bytes(ref, semaphore):
    pltpu.make_async_copy(ref, ref, semaphore).wait()


def gather_all_kernel(value_ref, out_ref, send, receive):
    device, rank, dp, tp = place()
    me, count = device * tp + rank, dp * tp
    greet_all()

    def one(index, carry):
        peer = lax.rem(me + index, count)
        push(value_ref, out_ref.at[me], send, receive, peer // tp, lax.rem(peer, tp))
        return carry

    lax.fori_loop(1, count, one, 0)
    out_ref[me] = value_ref[...]
    wait_bytes(out_ref.at[pl.ds(0, count - 1)], receive)
    wait_bytes(out_ref.at[pl.ds(0, count - 1)], send)


def gather_all(value, collective_id):
    count = lax.axis_size("dp") * lax.axis_size("tensor")
    return pl.pallas_call(
        gather_all_kernel,
        in_specs=[pl.BlockSpec(memory_space=pltpu.VMEM)],
        out_specs=pl.BlockSpec(memory_space=pltpu.VMEM),
        out_shape=jax.ShapeDtypeStruct((count,) + value.shape, value.dtype),
        scratch_shapes=[pltpu.SemaphoreType.DMA, pltpu.SemaphoreType.DMA],
        compiler_params=pltpu.CompilerParams(collective_id=collective_id, has_side_effects=True),
        name="gather_all",
    )(value)


def reduce_clips_kernel(part_ref, out_ref, land_ref, send, receive, share_send, share_receive):
    device, rank, dp, tp = place()
    me, count = device * tp + rank, dp * tp
    greet_all()

    def one(index, carry):
        peer = lax.rem(me + index, count)
        there, column = peer // tp, lax.rem(peer, tp)
        push(part_ref.at[there, column], land_ref.at[me], send, receive, there, column)
        return carry

    lax.fori_loop(1, count, one, 0)
    land_ref[me] = part_ref[device, rank]
    wait_bytes(land_ref.at[pl.ds(0, count - 1)], receive)
    out_ref[rank] = jnp.sum(land_ref[...], axis=0)
    for step in range(1, tp):
        push(out_ref.at[rank], out_ref.at[rank], share_send, share_receive, device, lax.rem(rank + step, tp))
    wait_bytes(land_ref.at[pl.ds(0, count - 1)], send)
    wait_bytes(out_ref.at[pl.ds(0, tp - 1)], share_receive)
    wait_bytes(out_ref.at[pl.ds(0, tp - 1)], share_send)


def reduce_clips(part, collective_id):
    dp, tp, rows, lanes = part.shape
    return pl.pallas_call(
        reduce_clips_kernel,
        in_specs=[pl.BlockSpec(memory_space=pltpu.VMEM)],
        out_specs=pl.BlockSpec(memory_space=pltpu.VMEM),
        out_shape=jax.ShapeDtypeStruct((tp, rows, lanes), part.dtype),
        scratch_shapes=[pltpu.VMEM((dp * tp, rows, lanes), part.dtype)] + [pltpu.SemaphoreType.DMA] * 4,
        compiler_params=pltpu.CompilerParams(
            collective_id=collective_id, has_side_effects=True, vmem_limit_bytes=VMEM_LIMIT
        ),
        name="reduce_clips",
    )(part)


def sum_ranks_kernel(part_ref, out_ref, land_ref, *semaphores):
    device, rank, dp, tp = place()
    barrier = pltpu.get_barrier_semaphore()
    for step in range(1, tp):
        pl.semaphore_signal(
            barrier, inc=1, device_id=(device, lax.rem(rank + step, tp)), device_id_type=pl.DeviceIdType.MESH
        )

    def greet(step, carry):
        pl.semaphore_signal(
            barrier, inc=1, device_id=(lax.rem(device + step, dp), rank), device_id_type=pl.DeviceIdType.MESH
        )
        return carry

    lax.fori_loop(1, dp, greet, 0)
    pl.semaphore_wait(barrier, tp + dp - 2)
    for step in range(1, tp):
        there = lax.rem(rank + step, tp)
        push(part_ref.at[there], land_ref.at[rank], semaphores[0], semaphores[1], device, there)
    land_ref[rank] = part_ref[rank]
    wait_bytes(land_ref.at[pl.ds(0, tp - 1)], semaphores[1])
    mine = out_ref.at[rank]
    mine[device] = jnp.sum(land_ref[...], axis=0)

    def one(step, carry):
        push(mine.at[device], mine.at[device], semaphores[2], semaphores[3], lax.rem(device + step, dp), rank)
        return carry

    lax.fori_loop(1, dp, one, 0)
    wait_bytes(land_ref.at[pl.ds(0, tp - 1)], semaphores[0])
    wait_bytes(mine.at[pl.ds(0, dp - 1)], semaphores[3])
    for step in range(1, tp):
        push(mine, mine, semaphores[4], semaphores[5], device, lax.rem(rank + step, tp))
    wait_bytes(mine.at[pl.ds(0, dp - 1)], semaphores[2])
    wait_bytes(out_ref.at[pl.ds(0, tp - 1)], semaphores[5])
    wait_bytes(out_ref.at[pl.ds(0, tp - 1)], semaphores[4])


def sum_ranks(part, collective_id):
    tp, rows, lanes = part.shape
    return pl.pallas_call(
        sum_ranks_kernel,
        in_specs=[pl.BlockSpec(memory_space=pltpu.VMEM)],
        out_specs=pl.BlockSpec(memory_space=pltpu.VMEM),
        out_shape=jax.ShapeDtypeStruct((tp, lax.axis_size("dp"), rows, lanes), part.dtype),
        scratch_shapes=[pltpu.VMEM((tp, rows, lanes), part.dtype)] + [pltpu.SemaphoreType.DMA] * 6,
        compiler_params=pltpu.CompilerParams(
            collective_id=collective_id, has_side_effects=True, vmem_limit_bytes=VMEM_LIMIT
        ),
        name="sum_ranks",
    )(part)


def adam_update(weight, first, second, grad, rate, decay):
    first_new = BETA_ONE * first + (1.0 - BETA_ONE) * grad
    second_new = BETA_TWO * second + (1.0 - BETA_TWO) * grad * grad
    corrected = (
        first_new
        / (1.0 - BETA_ONE**STEP)
        / (jnp.sqrt(second_new / (1.0 - BETA_TWO**STEP)) + ADAM_EPS)
    )
    weight_new = weight - rate * (corrected + decay * weight)
    return (weight_new, first_new, second_new, weight_new.astype(jnp.bfloat16))


def dot32(form, left, right):
    return jnp.einsum(form, left, right, preferred_element_type=jnp.float32)


def exchange(blocks):
    return lax.all_to_all(blocks, "tensor", split_axis=0, concat_axis=0, tiled=True)


def flip(value, axis, bit):
    count = lax.axis_size(axis)
    return lax.ppermute(value, axis, [(n, n ^ bit) for n in range(count)])


def far_shift(value, shift):
    far = lax.axis_size("dp") // 2
    return lax.ppermute(
        value, "dp", [(2 * n + side, 2 * ((n + shift) % far) + side) for n in range(far) for side in range(2)]
    )


def add_low(left, right):
    return (left.astype(jnp.float32) + right.astype(jnp.float32)).astype(jnp.bfloat16)


def pick(value, index, axis):
    return lax.dynamic_index_in_dim(value, index, axis, keepdims=False)


def in_pieces(rows):
    return rows % 16 == 0


def gather_weights(shard, after):
    kinds, rows, width = shard.shape
    if not in_pieces(rows):
        whole = lax.all_gather(shard, ("tensor", "dp"), axis=1, tiled=True)
        return (whole.reshape(kinds, -1, lax.axis_size("dp") * rows, width),), after
    if after is not None:
        shard, _ = lax.optimization_barrier((shard, after))
    far = lax.axis_size("dp") // 2
    line = [shard] + [far_shift(shard, shift) for shift in range(1, far)]
    half = far // 2
    mine = jnp.stack(line)
    over_side = flip(mine, "dp", 1)
    over_row = flip(mine, "tensor", 2)
    across = jnp.concatenate([flip(over_side[:half], "tensor", 2), flip(over_row[half:], "dp", 1)])
    own = jnp.stack([jnp.stack([mine, over_side]), jnp.stack([over_row, across])])
    return (own, flip(own, "tensor", 1)), line[-1]


def scatter_weights(grads):
    kinds, ranks, width, cols = grads.shape
    dp = lax.axis_size("dp")
    rows = width // dp
    if not in_pieces(rows):
        flat = grads.reshape(kinds, ranks * width, cols)
        return lax.psum_scatter(flat, ("tensor", "dp"), scatter_dimension=1, tiled=True)
    far, half = dp // 2, dp // 4
    device, rank = lax.axis_index("dp"), lax.axis_index("tensor")
    place, side, row, core = device // 2, device % 2, rank // 2, rank % 2
    grads = grads.reshape(kinds, 2, 2, far, 2, rows, cols)
    grads = add_low(pick(grads, core, 2), flip(pick(grads, 1 - core, 2), "tensor", 1))
    first, last = grads[:, :, :half], grads[:, :, half:]
    first = add_low(pick(first, side, 3), flip(pick(first, 1 - side, 3), "dp", 1))
    last = add_low(pick(last, row, 1), flip(pick(last, 1 - row, 1), "tensor", 2))
    first = add_low(pick(first, row, 1), flip(pick(first, 1 - row, 1), "tensor", 2))
    last = add_low(pick(last, side, 2), flip(pick(last, 1 - side, 2), "dp", 1))
    line = jnp.concatenate([first, last], axis=1)
    total = pick(line, place, 1).astype(jnp.float32)
    for shift in range(1, far):
        total = total + far_shift(pick(line, (place + shift) % far, 1), shift).astype(jnp.float32)
    return total


def per_device(
    clips, cotangent, timesteps, labels, time_table, class_table,
    attention_weights, attention_first, attention_second,
    ffn_weights, ffn_first, ffn_second,
    modulation_weights, modulation_first, modulation_second,
    bias_vectors, bias_first, bias_second,
):
    layers, kinds, rows, cols = attention_weights.shape
    _, frames, patches, width = clips.shape
    mod_rows = modulation_weights.shape[1]
    bias_cols = bias_vectors.shape[1]
    dp, tp = lax.axis_size("dp"), lax.axis_size("tensor")
    position = lax.axis_index("dp") * tp + lax.axis_index("tensor")
    tokens = frames * patches
    strip = patches // (tp * frames)
    blocks = (tp, frames, frames * strip, width)
    pieces = (tp * frames, frames, strip, width)

    embed = time_table[timesteps] + class_table[labels]
    cond_act = jax.nn.silu(embed).astype(jnp.bfloat16)
    low = bias_vectors.astype(jnp.bfloat16).reshape(-1)
    row = jnp.concatenate([cond_act[0], low]).astype(jnp.float32)
    row = jnp.pad(row, (0, -row.shape[0] % 1024)).reshape(-1, 128)
    gathered = gather_all(row, 0).reshape(dp * tp, -1)
    cond_all = gathered[::tp, :width].astype(jnp.bfloat16)
    bias_low = gathered[:, width : width + layers * bias_cols].reshape(dp * tp, layers, bias_cols)
    bias_low = bias_low.transpose(1, 0, 2).reshape(layers, -1)
    cond_rows = lax.dynamic_slice_in_dim(cond_all, position * mod_rows, mod_rows, axis=1)
    modulation_low = modulation_weights.astype(jnp.bfloat16)
    mod_part = dot32("ck,lke->cle", cond_rows, modulation_low)
    mod = reduce_clips(mod_part.reshape(dp, tp, -1, 128), 1).reshape(layers, -1)
    mod_width = mod.shape[-1]
    mod = (mod + bias_low[:, -mod_width:]).reshape(layers, 6, width)
    hidden_width = bias_low.shape[1] - mod_width - 4 * width
    bias_up = bias_low[:, 3 * width : 3 * width + hidden_width].reshape(layers, tp, 1, -1)
    bias_out = bias_low[:, None, 2 * width : 3 * width]
    bias_down = bias_low[:, None, 3 * width + hidden_width : 4 * width + hidden_width]
    bias_project = [
        pack_bias(bias_low[layer, :width], bias_low[layer, width : 2 * width], tp) for layer in range(layers)
    ]

    attention, ffn, after = [], [], None
    for layer in range(layers):
        packed = pack_heads(attention_weights[layer].astype(jnp.bfloat16))[None]
        packed, after = gather_weights(packed, after)
        attention.append(packed)
        wide, after = gather_weights(ffn_weights[layer].astype(jnp.bfloat16), after)
        ffn.append(wide)

    by_patch = lambda v: v.reshape(frames, tp * frames, strip, width).transpose(1, 0, 2, 3)
    cot = exchange(by_patch(cotangent[0]).reshape(blocks))

    def forward(layer, stream, stride, result_shape):
        project, mixed, branch, middle = attention_forward(
            attention[layer], stream, mod[layer], bias_project[layer], bias_out[layer], stride
        )
        middle = middle.reshape(tokens, width)
        hidden, down, result = ffn_forward(
            ffn[layer], middle, mod[layer], bias_down[layer], bias_up[layer], result_shape, jnp.bfloat16
        )
        return result, ((project, mixed, branch), middle, hidden, down)

    def backward(layer, grad, stream, saved, stride, result_type):
        heads, middle, hidden, down = saved
        grad_middle, ffn_grad, up_sum, low_sums = ffn_backward(
            ffn[layer], grad, middle, down, hidden, mod[layer]
        )
        ffn_grad = scatter_weights(ffn_grad)
        grad, attention_grad, sums, project_sum = attention_backward(
            attention[layer], grad_middle.reshape(stream.shape), stream, heads, mod[layer], stride, result_type
        )
        attention_grad = unpack_heads(scatter_weights(attention_grad[None])[0])
        small = jnp.concatenate(
            [*unpack_bias(project_sum), sums[0], up_sum.reshape(-1), low_sums[0],
             sums[1:].reshape(-1), low_sums[1:].reshape(-1)]
        )
        return grad, attention_grad, ffn_grad, small

    first = clips[0].reshape(1, frames, patches, width)
    second, saved_first = forward(0, first, 0, pieces)
    second = exchange(second.reshape(blocks))
    result, saved_second = forward(1, second, strip, (tokens, width))
    result = exchange(result.reshape(blocks)).reshape(pieces)
    output = result.transpose(1, 0, 2, 3).reshape(clips.shape)

    grad, attention_b, ffn_b, small_b = backward(
        1, cot.reshape(tokens, width), second, saved_second, strip, jnp.bfloat16
    )
    grad = exchange(grad).reshape(pieces)
    grad, attention_a, ffn_a, small_a = backward(0, grad, first, saved_first, 0, jnp.float32)
    input_grad = grad.reshape(clips.shape)

    small = jnp.stack([small_a, small_b])
    token_width = small.shape[1] - mod_width
    small = sum_ranks(small.reshape(tp, -1, 128), 2).transpose(1, 0, 2, 3).reshape(dp, layers, -1)
    grad_mod_low = small[..., token_width:].astype(jnp.bfloat16)
    grad_bias_all = jnp.concatenate(
        [small[..., :token_width], grad_mod_low.astype(jnp.float32)], axis=-1
    ).sum(axis=0)
    grad_bias = lax.dynamic_slice_in_dim(grad_bias_all, position * bias_cols, bias_cols, axis=1)
    grad_mod_weight = dot32("ck,cle->lke", cond_rows, grad_mod_low)
    grad_act = dot32("cle,lke->ck", grad_mod_low, modulation_low)
    grad_act = gather_all(jnp.pad(grad_act, ((0, 0), (0, 128 - mod_rows))), 3)[:, :, :mod_rows]
    grad_act = lax.dynamic_index_in_dim(grad_act, lax.axis_index("dp"), axis=1, keepdims=False)
    silu_value, silu_pull = jax.vjp(jax.nn.silu, embed)
    cond_grad = silu_pull(grad_act.reshape(1, width))[0]

    grad_attention = jnp.stack([attention_a, attention_b]).astype(jnp.float32)
    grad_ffn = jnp.stack([ffn_a, ffn_b]).astype(jnp.float32)
    return (output, input_grad, cond_grad) + (
        adam_update(attention_weights, attention_first, attention_second, grad_attention, MATRIX_RATE, MATRIX_DECAY)
        + adam_update(ffn_weights, ffn_first, ffn_second, grad_ffn, MATRIX_RATE, MATRIX_DECAY)
        + adam_update(modulation_weights, modulation_first, modulation_second, grad_mod_weight, MATRIX_RATE, MATRIX_DECAY)
        + adam_update(bias_vectors, bias_first, bias_second, grad_bias, VECTOR_RATE, 0.0)
    )


def solution(mesh):
    tokens = P("dp", "tensor", None, None)
    matrix = P(None, None, "dp", "tensor")
    modulation = P(None, BOTH, None)
    vector = P(None, BOTH)
    return jax.shard_map(
        per_device,
        mesh=mesh,
        in_specs=(tokens, tokens, P("dp"), P("dp"), P(), P())
        + (matrix,) * 6 + (modulation,) * 3 + (vector,) * 3,
        out_specs=(tokens, tokens, P("dp", None)) + (matrix,) * 8 + (modulation,) * 4 + (vector,) * 4,
        check_vma=False,
    )
```

```python
from functools import partial

import jax
import jax.numpy as jnp
from jax import lax
from jax.experimental import pallas as pl
from jax.experimental.pallas import tpu as pltpu
from jax.sharding import PartitionSpec as P

HD = 64
PAIR = 128
BLOCK = 256
SPLIT = 4
STEP = 10
BETA_ONE = 0.9
BETA_TWO = 0.999
ADAM_EPS = 1e-08
MATRIX_RATE = 0.04
VECTOR_RATE = 0.2
MATRIX_DECAY = 0.1
NORM_EPS = 1e-06
GELU_A = (2.0 / 3.141592653589793) ** 0.5
GELU_B = 0.044715
BLOCKED = -1e30
VMEM_LIMIT = 60 * 1024 * 1024
BOTH = ("dp", "tensor")


def mm(left, right, dims=((1,), (0,))):
    return lax.dot_general(left, right, (dims, ((), ())), preferred_element_type=jnp.float32)


def norm_parts(value):
    average = jnp.mean(value, axis=-1, keepdims=True)
    centred = value - average
    spread = jnp.mean(centred * centred, axis=-1, keepdims=True)
    inverse = lax.rsqrt(spread + NORM_EPS)
    return centred * inverse, inverse


def norm_back(grad, shape, inverse):
    first = jnp.mean(grad, axis=-1, keepdims=True)
    second = jnp.mean(grad * shape, axis=-1, keepdims=True)
    return inverse * (grad - first - shape * second)


def rows_of(ref):
    value = ref[...]
    return value.reshape(-1, value.shape[-1])


def put(ref, value):
    ref[...] = value.reshape(ref.shape).astype(ref.dtype)


def add_rows(ref, index, value):
    ref[pl.ds(index, 1), :] += jnp.sum(value, axis=0, keepdims=True)


def half_masks(rows):
    lane = lax.broadcasted_iota(jnp.int32, (rows, PAIR), 1)
    return lane < HD


def same_patch(tokens, stride):
    row = lax.broadcasted_iota(jnp.int32, (tokens, tokens), 0)
    column = lax.broadcasted_iota(jnp.int32, (tokens, tokens), 1)
    return lax.rem(row, stride) == lax.rem(column, stride)


def swap_halves(value):
    return pltpu.roll(value, HD, 1)


def start_loads(sources, kind, target, semaphores):
    if len(sources) == 1:
        for rank in range(target.shape[0]):
            pltpu.make_async_copy(sources[0].at[kind, rank], target.at[rank], semaphores.at[rank]).start()
        return
    far, near, rows = sources[0].shape[2], 2, sources[0].shape[4]
    device, rank = lax.axis_index("dp"), lax.axis_index("tensor")
    for core, source in enumerate(sources):
        for row in range(2):
            for side in range(2):
                for back in range(far):
                    where = lax.rem(device // near + far - back, far) * near + (device % near + side) % near
                    owner = (rank // 2 + row) % 2 * 2 + (rank % 2 + core) % 2
                    pltpu.make_async_copy(
                        source.at[row, side, back, kind],
                        target.at[owner, pl.ds(pl.multiple_of(where * rows, rows), rows)],
                        semaphores.at[owner],
                    ).start()


def wait_loads(target, semaphores, rank):
    pltpu.make_async_copy(target.at[rank], target.at[rank], semaphores.at[rank]).wait()


def softmax_rows(scores, axis):
    raised = jnp.exp(scores - jnp.max(scores, axis=axis, keepdims=True))
    return raised * (1.0 / jnp.sum(raised, axis=axis, keepdims=True))


def attention_forward_kernel(stride, count, *refs):
    sources = refs[:count]
    (stream_ref, mod_ref, bias_ref, bias_out_ref,
     project_ref, mixed_ref, branch_ref, middle_ref, weight_ref, semaphores) = refs[count:]
    ranks = weight_ref.shape[0]

    @pl.when(pl.program_id(0) == 0)
    def _():
        start_loads(sources, 0, weight_ref, semaphores)

    stream = rows_of(stream_ref).astype(jnp.float32)
    tokens, width = stream.shape
    shape, _ = norm_parts(stream)
    normed = (shape * (1.0 + mod_ref[1:2]) + mod_ref[0:1]).astype(jnp.bfloat16)
    lower = half_masks(tokens)
    allowed = same_patch(tokens, stride) if stride else None

    @pl.when(pl.program_id(0) == 0)
    def _():
        for rank in range(ranks):
            wait_loads(weight_ref, semaphores, rank)

    def one_head(chosen, key, value):
        scores = mm(chosen.astype(jnp.bfloat16), key, ((1,), (1,)))
        if stride:
            scores = jnp.where(allowed, scores, BLOCKED)
        return mm(softmax_rows(scores, -1).astype(jnp.bfloat16), value)

    branch = None
    for rank in range(ranks):
        project = (mm(normed, weight_ref[rank, :, : 5 * PAIR]) + bias_ref[rank]).astype(jnp.bfloat16)
        project_ref[rank] = project.reshape(project_ref.shape[1:])
        query = project[:, :PAIR].astype(jnp.float32) * HD**-0.5
        key, value = project[:, PAIR : 2 * PAIR], project[:, 2 * PAIR : 3 * PAIR]
        first = one_head(jnp.where(lower, query, 0.0), key, value)
        second = one_head(jnp.where(lower, 0.0, query), key, value)
        both = project[:, 3 * PAIR : 4 * PAIR].astype(jnp.float32)
        last = one_head(
            jnp.where(lower, both * HD**-0.5, 0.0),
            swap_halves(both).astype(jnp.bfloat16),
            project[:, 4 * PAIR : 5 * PAIR],
        )
        mixed = jnp.concatenate(
            [jnp.where(lower, 0.0, swap_halves(last)), jnp.where(lower, first, second)], axis=1
        ).astype(jnp.bfloat16)
        mixed_ref[rank] = mixed.reshape(mixed_ref.shape[1:])
        term = mm(mixed, weight_ref[rank, :, 4 * PAIR :], ((1,), (1,)))
        branch = term if branch is None else branch + term
    branch = branch + bias_out_ref[...]
    put(branch_ref, branch)
    put(middle_ref, stream + mod_ref[2:3] * branch)


def gelu_parts(value):
    square = value * value
    bent = jnp.tanh(value * (GELU_A + (GELU_A * GELU_B) * square))
    half = 0.5 * (1.0 + bent)
    slope = half + (0.5 * value) * (1.0 - bent * bent) * (GELU_A + (3.0 * GELU_A * GELU_B) * square)
    return value * half, slope


def ffn_forward_kernel(split, count, *refs):
    sources = refs[:count]
    (middle_ref, mod_ref, bias_ref, bias_up_ref,
     hidden_ref, branch_ref, result_ref,
     up_ref, down_ref, up_semaphores, down_semaphores, second_ref, total_ref) = refs[count:]
    step = pl.program_id(0)
    tokens = middle_ref.shape[0]
    chunk = tokens // split

    @pl.when(step == 0)
    def _():
        start_loads(sources, 0, up_ref, up_semaphores)
        start_loads(sources, 1, down_ref, down_semaphores)

        def norm_chunk(index, carry):
            rows = pl.ds(pl.multiple_of(index * chunk, chunk), chunk)
            shape, _ = norm_parts(middle_ref[rows, :])
            second_ref[rows, :] = (shape * (1.0 + mod_ref[4:5]) + mod_ref[3:4]).astype(jnp.bfloat16)
            return carry

        lax.fori_loop(0, split, norm_chunk, 0)

    wait_loads(up_ref, up_semaphores, step)
    wait_loads(down_ref, down_semaphores, step)

    def one(index, carry):
        rows = pl.ds(pl.multiple_of(index * chunk, chunk), chunk)
        hidden = mm(second_ref[rows, :], up_ref[step]) + bias_up_ref[0]
        hidden_ref[0, rows, :] = hidden.astype(jnp.bfloat16)
        active, _ = gelu_parts(hidden)
        part = mm(active.astype(jnp.bfloat16), down_ref[step], ((1,), (1,)))
        total_ref[rows, :] = jnp.where(step == 0, 0.0, total_ref[rows, :]) + part
        return carry

    lax.fori_loop(0, split, one, 0)

    @pl.when(step == pl.num_programs(0) - 1)
    def _():
        for index in range(split):
            rows = slice(index * chunk, (index + 1) * chunk)
            down = total_ref[rows, :] + bias_ref[...]
            branch_ref[rows, :] = down.astype(jnp.bfloat16)
            result = middle_ref[rows, :] + mod_ref[5:6] * down
            store_frame(result_ref, index, chunk, result)


def store_frame(ref, index, chunk, value):
    if len(ref.shape) == 2:
        ref[index * chunk : (index + 1) * chunk, :] = value.astype(ref.dtype)
    else:
        ref[:, index] = value.reshape(ref.shape[0], ref.shape[2], ref.shape[3]).astype(ref.dtype)


def load_frame(ref, index, chunk):
    if len(ref.shape) == 2:
        return ref[index * chunk : (index + 1) * chunk, :].astype(jnp.float32)
    value = ref[:, index]
    return value.reshape(chunk, value.shape[-1]).astype(jnp.float32)


def ffn_backward_kernel(split, count, scattering, steps, *refs):
    sources, chain_source, inputs, outputs, chain_out, scratch, chain_scratch = split_refs(
        refs, scattering, (count, 5, 4, 9)
    )
    grad_ref, middle_ref, branch_ref, hidden_ref, mod_ref = inputs
    grad_middle_ref, weight_grad_ref, up_sum_ref, sums_ref = outputs
    (up_ref, down_ref, up_semaphores, down_semaphores,
     second_ref, low_ref, active_ref, slope_ref, total_ref) = scratch
    step = pl.program_id(0)
    tokens, width = middle_ref.shape
    chunk = tokens // split
    here, chains = make_chains(chain_source, chain_out, chain_scratch)
    run_chains(here, chains, step, steps)

    @pl.when(step == 0)
    def _():
        start_loads(sources, 0, up_ref, up_semaphores)
        start_loads(sources, 1, down_ref, down_semaphores)
        sums_ref[...] = jnp.zeros_like(sums_ref)
        for index in range(split):
            rows = slice(index * chunk, (index + 1) * chunk)
            grad = load_frame(grad_ref, index, chunk)
            low = (mod_ref[5:6] * grad).astype(jnp.bfloat16)
            low_ref[rows, :] = low
            add_rows(sums_ref, 0, low.astype(jnp.float32))
            add_rows(sums_ref, 3, grad * branch_ref[rows, :].astype(jnp.float32))
            shape, _ = norm_parts(middle_ref[rows, :])
            second_ref[rows, :] = (shape * (1.0 + mod_ref[4:5]) + mod_ref[3:4]).astype(jnp.bfloat16)

    up_sum_ref[...] = jnp.zeros_like(up_sum_ref)
    wait_loads(up_ref, up_semaphores, step)
    wait_loads(down_ref, down_semaphores, step)

    def one(index, carry):
        rows = pl.ds(pl.multiple_of(index * chunk, chunk), chunk)
        active, slope = gelu_parts(hidden_ref[0, rows, :].astype(jnp.float32))
        active_ref[rows, :] = active.astype(jnp.bfloat16)
        low = (mm(low_ref[rows, :], down_ref[step]) * slope).astype(jnp.bfloat16)
        slope_ref[rows, :] = low
        up_sum_ref[0] += jnp.sum(low.astype(jnp.float32), axis=0, keepdims=True)
        part = mm(low, up_ref[step], ((1,), (1,)))
        total_ref[rows, :] = jnp.where(step == 0, 0.0, total_ref[rows, :]) + part
        return carry

    lax.fori_loop(0, split, one, 0)

    def weights(index, carry):
        part = pl.ds(pl.multiple_of(index * BLOCK, BLOCK), BLOCK)
        weight_grad_ref[0, 0, part, :] = mm(second_ref[:, part], slope_ref[...], ((0,), (0,))).astype(
            jnp.bfloat16
        )
        weight_grad_ref[1, 0, part, :] = mm(low_ref[:, part], active_ref[...], ((0,), (0,))).astype(
            jnp.bfloat16
        )
        return carry

    lax.fori_loop(0, width // BLOCK, weights, 0)

    @pl.when(step == pl.num_programs(0) - 1)
    def _():
        for index in range(split):
            rows = slice(index * chunk, (index + 1) * chunk)
            shape, inverse = norm_parts(middle_ref[rows, :])
            grad = total_ref[rows, :]
            add_rows(sums_ref, 1, grad)
            add_rows(sums_ref, 2, grad * shape)
            back = norm_back(grad * (1.0 + mod_ref[4:5]), shape, inverse)
            grad_middle_ref[rows, :] = load_frame(grad_ref, index, chunk) + back
        end_chains(chains)


def attention_backward_kernel(stride, count, scattering, steps, *refs):
    sources, chain_source, inputs, outputs, chain_out, scratch, chain_scratch = split_refs(
        refs, scattering, (count, 6, 4, 5)
    )
    grad_ref, stream_ref, project_ref, mixed_ref, branch_ref, mod_ref = inputs
    grad_stream_ref, weight_grad_ref, sums_ref, project_sum_ref = outputs
    weight_ref, semaphores, left_ref, right_ref, outer_ref = scratch
    step = pl.program_id(0)
    ranks = weight_ref.shape[0]
    here, chains = make_chains(chain_source, chain_out, chain_scratch)
    run_chains(here, chains, step, steps)

    @pl.when(step == 0)
    def _():
        start_loads(sources, 0, weight_ref, semaphores)
        sums_ref[...] = jnp.zeros_like(sums_ref)
        project_sum_ref[...] = jnp.zeros_like(project_sum_ref)

    grad_middle = rows_of(grad_ref)
    tokens, width = grad_middle.shape
    stream = rows_of(stream_ref).astype(jnp.float32)
    shape, inverse = norm_parts(stream)
    rows = pl.ds(pl.multiple_of(step * tokens, tokens), tokens)
    normed = (shape * (1.0 + mod_ref[1:2]) + mod_ref[0:1]).astype(jnp.bfloat16)
    low = (mod_ref[2:3] * grad_middle).astype(jnp.bfloat16)
    left_ref[0, rows, :] = normed
    left_ref[1, rows, :] = low
    add_rows(sums_ref, 0, low.astype(jnp.float32))
    add_rows(sums_ref, 3, grad_middle * rows_of(branch_ref).astype(jnp.float32))
    lower = half_masks(tokens)
    allowed = same_patch(tokens, stride) if stride else None
    scale = HD**-0.5

    @pl.when(step == 0)
    def _():
        for rank in range(ranks):
            wait_loads(weight_ref, semaphores, rank)

    def one_head(chosen, key, value, taken):
        scores = mm(key, chosen.astype(jnp.bfloat16), ((1,), (1,)))
        if stride:
            scores = jnp.where(allowed, scores, BLOCKED)
        probs = softmax_rows(scores, 0)
        grad_probs = mm(value, taken.astype(jnp.bfloat16), ((1,), (1,)))
        inner = jnp.sum(grad_probs * probs, axis=0, keepdims=True)
        return probs.astype(jnp.bfloat16), (probs * (grad_probs - inner)).astype(jnp.bfloat16)

    grad_normed = None
    for rank in range(ranks):
        project = project_ref[rank].reshape(tokens, 5 * PAIR)
        mixed = mixed_ref[rank].reshape(tokens, 2 * PAIR)
        outer_ref[rank, rows, :] = mixed
        grad_mixed = mm(low, weight_ref[rank, :, 4 * PAIR :]).astype(jnp.bfloat16)
        query, key, value = (project[:, n * PAIR : (n + 1) * PAIR] for n in range(3))
        query_wide = query.astype(jnp.float32) * scale
        pair = grad_mixed[:, PAIR:]
        pair_wide = pair.astype(jnp.float32)
        outs = []
        for keep in (lower, ~lower):
            probs, grad_scores = one_head(
                jnp.where(keep, query_wide, 0.0), key, value, jnp.where(keep, pair_wide, 0.0)
            )
            outs.append(
                (mm(grad_scores, key, ((0,), (0,))), mm(grad_scores, query), mm(probs, pair))
            )
        parts = [
            jnp.where(lower, one, two) * factor
            for one, two, factor in zip(outs[0], outs[1], (scale, scale, 1.0))
        ]
        both = project[:, 3 * PAIR : 4 * PAIR].astype(jnp.float32)
        swapped = swap_halves(both).astype(jnp.bfloat16)
        single = swap_halves(grad_mixed[:, :PAIR].astype(jnp.float32))
        probs, grad_scores = one_head(
            jnp.where(lower, both * scale, 0.0),
            swapped,
            project[:, 4 * PAIR :],
            jnp.where(lower, single, 0.0),
        )
        parts.append(
            jnp.where(lower, mm(grad_scores, swapped, ((0,), (0,))), mm(grad_scores, swapped)) * scale
        )
        parts.append(jnp.where(lower, mm(probs, single.astype(jnp.bfloat16)), 0.0))
        whole = jnp.concatenate(parts, axis=1).astype(jnp.bfloat16)
        right_ref[rank, rows, :] = whole
        add_rows(project_sum_ref, rank, whole.astype(jnp.float32))
        term = mm(whole, weight_ref[rank, :, : 5 * PAIR], ((1,), (1,)))
        grad_normed = term if grad_normed is None else grad_normed + term
    add_rows(sums_ref, 1, grad_normed)
    add_rows(sums_ref, 2, grad_normed * shape)
    back = norm_back(grad_normed * (1.0 + mod_ref[1:2]), shape, inverse)
    put(grad_stream_ref, grad_middle + back)

    @pl.when(step == pl.num_programs(0) - 1)
    def _():
        def weights(rank, carry):
            def block(index, inner):
                part = pl.ds(pl.multiple_of(index * BLOCK, BLOCK), BLOCK)
                inside = mm(left_ref[0, :, part], right_ref[rank], ((0,), (0,)))
                outside = mm(left_ref[1, :, part], outer_ref[rank], ((0,), (0,)))
                weight_grad_ref[rank, part, : 4 * PAIR] = inside[:, : 4 * PAIR].astype(jnp.bfloat16)
                weight_grad_ref[rank, part, 4 * PAIR : 5 * PAIR] = (
                    inside[:, 4 * PAIR :] + outside[:, :PAIR]
                ).astype(jnp.bfloat16)
                weight_grad_ref[rank, part, 5 * PAIR :] = outside[:, PAIR:].astype(jnp.bfloat16)
                return inner

            return lax.fori_loop(0, width // BLOCK, block, carry)

        lax.fori_loop(0, ranks, weights, 0)
        end_chains(chains)


def fixed(shape):
    return pl.BlockSpec(shape, lambda step: (0,) * len(shape))


def kernel_params(collective_id=None):
    more = {} if collective_id is None else {"collective_id": collective_id, "has_side_effects": True}
    return pltpu.CompilerParams(
        vmem_limit_bytes=VMEM_LIMIT, dimension_semantics=("arbitrary",), **more
    )


def cost(flops, moved, raised=0):
    return pl.CostEstimate(flops=int(flops), bytes_accessed=int(moved), transcendentals=int(raised))


def group_spec(shape):
    return pl.BlockSpec((shape[0], 1, shape[2], shape[3]), lambda step: (0, step, 0, 0))


def anywhere(sources):
    return [pl.BlockSpec(memory_space=pl.ANY)] * len(sources)


def rank_spec(shape):
    return pl.BlockSpec((shape[0], shape[1], 1) + shape[3:], lambda step: (0, 0, step, 0, 0))


def attention_forward(sources, stream, mod, bias, bias_out, stride):
    shape = stream.shape
    width = shape[-1]
    ranks = bias.shape[0]
    tokens = shape[0] * shape[1] * shape[2]
    spec = group_spec(shape)
    low = jax.ShapeDtypeStruct(shape, jnp.bfloat16)
    wide = jax.ShapeDtypeStruct(shape, jnp.float32)
    project = jax.ShapeDtypeStruct((ranks,) + shape[:3] + (5 * PAIR,), jnp.bfloat16)
    mixed = jax.ShapeDtypeStruct((ranks,) + shape[:3] + (2 * PAIR,), jnp.bfloat16)
    return pl.pallas_call(
        partial(attention_forward_kernel, stride, len(sources)),
        grid=(shape[1],),
        in_specs=anywhere(sources) + [spec, fixed(mod.shape), fixed(bias.shape), fixed(bias_out.shape)],
        out_specs=[rank_spec(project.shape), rank_spec(mixed.shape), spec, spec],
        out_shape=[project, mixed, low, wide],
        scratch_shapes=[
            pltpu.VMEM((ranks, width, 6 * PAIR), jnp.bfloat16),
            pltpu.SemaphoreType.DMA((ranks,)),
        ],
        compiler_params=kernel_params(),
        cost_estimate=cost(8 * tokens * width * width * 1.5, tokens * width * 16),
        name="attention_forward",
    )(*sources, stream, mod, bias, bias_out)


def ffn_weights_scratch(ranks, width, part):
    return [
        pltpu.VMEM((ranks, width, part), jnp.bfloat16),
        pltpu.VMEM((ranks, width, part), jnp.bfloat16),
        pltpu.SemaphoreType.DMA((ranks,)),
        pltpu.SemaphoreType.DMA((ranks,)),
    ]


def ffn_forward(sources, middle, mod, bias_down, bias_up, result_shape, result_type):
    tokens, width = middle.shape
    ranks, _, part = bias_up.shape
    whole = fixed((tokens, width))
    return pl.pallas_call(
        partial(ffn_forward_kernel, SPLIT, len(sources)),
        grid=(ranks,),
        in_specs=anywhere(sources) + [
            whole, fixed(mod.shape), fixed(bias_down.shape),
            pl.BlockSpec((1, 1, part), lambda step: (step, 0, 0)),
        ],
        out_specs=[pl.BlockSpec((1, tokens, part), lambda step: (step, 0, 0)), whole, fixed(result_shape)],
        out_shape=[
            jax.ShapeDtypeStruct((ranks, tokens, part), jnp.bfloat16),
            jax.ShapeDtypeStruct((tokens, width), jnp.bfloat16),
            jax.ShapeDtypeStruct(result_shape, result_type),
        ],
        scratch_shapes=ffn_weights_scratch(ranks, width, part) + [
            pltpu.VMEM((tokens, width), jnp.bfloat16),
            pltpu.VMEM((tokens, width), jnp.float32),
        ],
        compiler_params=kernel_params(),
        cost_estimate=cost(4.8 * tokens * width * ranks * part, tokens * width * 14, tokens * ranks * part),
        name="ffn_forward",
    )(*sources, middle, mod, bias_down, bias_up)


def ffn_backward(sources, grad, middle, branch, hidden, mod, scatter=None, collective_id=None):
    tokens, width = middle.shape
    ranks, _, part = hidden.shape
    whole = fixed((tokens, width))
    extra, extra_in, extra_out, extra_shape, extra_scratch = chain_arguments(scatter)
    return pl.pallas_call(
        partial(ffn_backward_kernel, SPLIT, len(sources), len(extra), ranks),
        grid=(ranks,),
        in_specs=anywhere(sources) + extra_in + [
            fixed(grad.shape), whole, whole,
            pl.BlockSpec((1, tokens, part), lambda step: (step, 0, 0)),
            fixed(mod.shape),
        ],
        out_specs=[
            whole,
            pl.BlockSpec((2, 1, width, part), lambda step: (0, step, 0, 0)),
            pl.BlockSpec((1, 1, part), lambda step: (step, 0, 0)),
            fixed((4, width)),
        ] + extra_out,
        out_shape=[
            jax.ShapeDtypeStruct((tokens, width), jnp.float32),
            jax.ShapeDtypeStruct((2, ranks, width, part), jnp.bfloat16),
            jax.ShapeDtypeStruct((ranks, 1, part), jnp.float32),
            jax.ShapeDtypeStruct((4, width), jnp.float32),
        ] + extra_shape,
        scratch_shapes=ffn_weights_scratch(ranks, width, part) + [
            pltpu.VMEM((tokens, width), jnp.bfloat16),
            pltpu.VMEM((tokens, width), jnp.bfloat16),
            pltpu.VMEM((tokens, part), jnp.bfloat16),
            pltpu.VMEM((tokens, part), jnp.bfloat16),
            pltpu.VMEM((tokens, width), jnp.float32),
        ] + extra_scratch,
        compiler_params=kernel_params(collective_id),
        cost_estimate=cost(9.6 * tokens * width * ranks * part, tokens * width * 20, tokens * ranks * part),
        name="ffn_backward",
    )(*sources, *extra, grad, middle, branch, hidden, mod)


def attention_backward(sources, grad, stream, saved, mod, stride, result_type, scatter=None, collective_id=None):
    project, mixed, branch = saved
    shape = stream.shape
    width = shape[-1]
    ranks = project.shape[0]
    tokens = shape[0] * shape[1] * shape[2]
    spec = group_spec(shape)
    extra, extra_in, extra_out, extra_shape, extra_scratch = chain_arguments(scatter)
    return pl.pallas_call(
        partial(attention_backward_kernel, stride, len(sources), len(extra), shape[1]),
        grid=(shape[1],),
        in_specs=anywhere(sources) + extra_in + [
            spec, spec, rank_spec(project.shape), rank_spec(mixed.shape), spec, fixed(mod.shape),
        ],
        out_specs=[
            spec, fixed((ranks, width, 6 * PAIR)), fixed((4, width)), fixed((ranks, 5 * PAIR)),
        ] + extra_out,
        out_shape=[
            jax.ShapeDtypeStruct(shape, result_type),
            jax.ShapeDtypeStruct((ranks, width, 6 * PAIR), jnp.bfloat16),
            jax.ShapeDtypeStruct((4, width), jnp.float32),
            jax.ShapeDtypeStruct((ranks, 5 * PAIR), jnp.float32),
        ] + extra_shape,
        scratch_shapes=[
            pltpu.VMEM((ranks, width, 6 * PAIR), jnp.bfloat16),
            pltpu.SemaphoreType.DMA((ranks,)),
            pltpu.VMEM((2, tokens, width), jnp.bfloat16),
            pltpu.VMEM((ranks, tokens, 5 * PAIR), jnp.bfloat16),
            pltpu.VMEM((ranks, tokens, 2 * PAIR), jnp.bfloat16),
        ] + extra_scratch,
        compiler_params=kernel_params(collective_id),
        cost_estimate=cost(16 * tokens * width * width * 1.5, tokens * width * 20),
        name="attention_backward",
    )(*sources, *extra, grad, stream, project, mixed, branch, mod)


def pack_heads(block):
    query, key, value, outer = block
    return jnp.concatenate(
        [query[:, :PAIR], key[:, :PAIR], value[:, :PAIR], query[:, PAIR:], key[:, PAIR:],
         value[:, PAIR:], outer[:, PAIR:], outer[:, :PAIR]], axis=1
    )


def unpack_heads(packed):
    part = lambda start, size: packed[:, start : start + size]
    join = lambda first, last: jnp.concatenate([part(first, PAIR), part(last, HD)], axis=1)
    return jnp.stack(
        [join(0, 3 * PAIR), join(PAIR, 3 * PAIR + HD), join(2 * PAIR, 4 * PAIR), join(5 * PAIR, 4 * PAIR + HD)]
    )


def pack_bias(query, value, ranks):
    query, value = query.reshape(ranks, -1), value.reshape(ranks, -1)
    none = jnp.zeros((ranks, PAIR), query.dtype)
    return jnp.concatenate(
        [query[:, :PAIR], none, value[:, :PAIR], query[:, PAIR:], none[:, :HD], value[:, PAIR:], none[:, :HD]],
        axis=1,
    )[:, None]


def unpack_bias(sums):
    query = jnp.concatenate([sums[:, :PAIR], sums[:, 3 * PAIR : 3 * PAIR + HD]], axis=1)
    value = jnp.concatenate([sums[:, 2 * PAIR : 3 * PAIR], sums[:, 4 * PAIR : 4 * PAIR + HD]], axis=1)
    return query.reshape(-1), value.reshape(-1)


def place():
    return lax.axis_index("dp"), lax.axis_index("tensor"), lax.axis_size("dp"), lax.axis_size("tensor")


def greet_all():
    device, rank, dp, tp = place()
    me, count = device * tp + rank, dp * tp
    barrier = pltpu.get_barrier_semaphore()

    def greet(index, carry):
        peer = lax.rem(me + index, count)
        pl.semaphore_signal(
            barrier, inc=1, device_id=(peer // tp, lax.rem(peer, tp)), device_id_type=pl.DeviceIdType.MESH
        )
        return carry

    lax.fori_loop(1, count, greet, 0)
    pl.semaphore_wait(barrier, count - 1)


def push(source, target, send, receive, device, rank):
    pltpu.make_async_remote_copy(
        src_ref=source, dst_ref=target, send_sem=send, recv_sem=receive,
        device_id=(device, rank), device_id_type=pl.DeviceIdType.MESH,
    ).start()


def wait_bytes(ref, semaphore):
    pltpu.make_async_copy(ref, ref, semaphore).wait()


def gather_all_kernel(value_ref, out_ref, send, receive):
    device, rank, dp, tp = place()
    me, count = device * tp + rank, dp * tp
    greet_all()

    def one(index, carry):
        peer = lax.rem(me + index, count)
        push(value_ref, out_ref.at[me], send, receive, peer // tp, lax.rem(peer, tp))
        return carry

    lax.fori_loop(1, count, one, 0)
    out_ref[me] = value_ref[...]
    wait_bytes(out_ref.at[pl.ds(0, count - 1)], receive)
    wait_bytes(out_ref.at[pl.ds(0, count - 1)], send)


def gather_all(value, collective_id):
    count = lax.axis_size("dp") * lax.axis_size("tensor")
    return pl.pallas_call(
        gather_all_kernel,
        in_specs=[pl.BlockSpec(memory_space=pltpu.VMEM)],
        out_specs=pl.BlockSpec(memory_space=pltpu.VMEM),
        out_shape=jax.ShapeDtypeStruct((count,) + value.shape, value.dtype),
        scratch_shapes=[pltpu.SemaphoreType.DMA, pltpu.SemaphoreType.DMA],
        compiler_params=pltpu.CompilerParams(collective_id=collective_id, has_side_effects=True),
        name="gather_all",
    )(value)


def reduce_clips_kernel(part_ref, out_ref, land_ref, send, receive, share_send, share_receive):
    device, rank, dp, tp = place()
    me, count = device * tp + rank, dp * tp
    greet_all()

    def one(index, carry):
        peer = lax.rem(me + index, count)
        there, column = peer // tp, lax.rem(peer, tp)
        push(part_ref.at[there, column], land_ref.at[me], send, receive, there, column)
        return carry

    lax.fori_loop(1, count, one, 0)
    land_ref[me] = part_ref[device, rank]
    wait_bytes(land_ref.at[pl.ds(0, count - 1)], receive)
    out_ref[rank] = jnp.sum(land_ref[...], axis=0)
    for step in range(1, tp):
        push(out_ref.at[rank], out_ref.at[rank], share_send, share_receive, device, lax.rem(rank + step, tp))
    wait_bytes(land_ref.at[pl.ds(0, count - 1)], send)
    wait_bytes(out_ref.at[pl.ds(0, tp - 1)], share_receive)
    wait_bytes(out_ref.at[pl.ds(0, tp - 1)], share_send)


def reduce_clips(part, collective_id):
    dp, tp, rows, lanes = part.shape
    return pl.pallas_call(
        reduce_clips_kernel,
        in_specs=[pl.BlockSpec(memory_space=pltpu.VMEM)],
        out_specs=pl.BlockSpec(memory_space=pltpu.VMEM),
        out_shape=jax.ShapeDtypeStruct((tp, rows, lanes), part.dtype),
        scratch_shapes=[pltpu.VMEM((dp * tp, rows, lanes), part.dtype)] + [pltpu.SemaphoreType.DMA] * 4,
        compiler_params=pltpu.CompilerParams(
            collective_id=collective_id, has_side_effects=True, vmem_limit_bytes=VMEM_LIMIT
        ),
        name="reduce_clips",
    )(part)


def sum_ranks_kernel(part_ref, out_ref, land_ref, *semaphores):
    device, rank, dp, tp = place()
    barrier = pltpu.get_barrier_semaphore()
    for step in range(1, tp):
        pl.semaphore_signal(
            barrier, inc=1, device_id=(device, lax.rem(rank + step, tp)), device_id_type=pl.DeviceIdType.MESH
        )

    def greet(step, carry):
        pl.semaphore_signal(
            barrier, inc=1, device_id=(lax.rem(device + step, dp), rank), device_id_type=pl.DeviceIdType.MESH
        )
        return carry

    lax.fori_loop(1, dp, greet, 0)
    pl.semaphore_wait(barrier, tp + dp - 2)
    for step in range(1, tp):
        there = lax.rem(rank + step, tp)
        push(part_ref.at[there], land_ref.at[rank], semaphores[0], semaphores[1], device, there)
    land_ref[rank] = part_ref[rank]
    wait_bytes(land_ref.at[pl.ds(0, tp - 1)], semaphores[1])
    mine = out_ref.at[rank]
    mine[device] = jnp.sum(land_ref[...], axis=0)

    def one(step, carry):
        push(mine.at[device], mine.at[device], semaphores[2], semaphores[3], lax.rem(device + step, dp), rank)
        return carry

    lax.fori_loop(1, dp, one, 0)
    wait_bytes(land_ref.at[pl.ds(0, tp - 1)], semaphores[0])
    wait_bytes(mine.at[pl.ds(0, dp - 1)], semaphores[3])
    for step in range(1, tp):
        push(mine, mine, semaphores[4], semaphores[5], device, lax.rem(rank + step, tp))
    wait_bytes(mine.at[pl.ds(0, dp - 1)], semaphores[2])
    wait_bytes(out_ref.at[pl.ds(0, tp - 1)], semaphores[5])
    wait_bytes(out_ref.at[pl.ds(0, tp - 1)], semaphores[4])


def sum_ranks(part, collective_id):
    tp, rows, lanes = part.shape
    return pl.pallas_call(
        sum_ranks_kernel,
        in_specs=[pl.BlockSpec(memory_space=pltpu.VMEM)],
        out_specs=pl.BlockSpec(memory_space=pltpu.VMEM),
        out_shape=jax.ShapeDtypeStruct((tp, lax.axis_size("dp"), rows, lanes), part.dtype),
        scratch_shapes=[pltpu.VMEM((tp, rows, lanes), part.dtype)] + [pltpu.SemaphoreType.DMA] * 6,
        compiler_params=pltpu.CompilerParams(
            collective_id=collective_id, has_side_effects=True, vmem_limit_bytes=VMEM_LIMIT
        ),
        name="sum_ranks",
    )(part)


CHAIN_SLOTS = 7


class Where:
    def __init__(self):
        device, rank = lax.axis_index("dp"), lax.axis_index("tensor")
        self.count = lax.axis_size("dp") // 2
        self.device, self.rank = device, rank
        self.far, self.side = device // 2, lax.rem(device, 2)
        self.row, self.core = rank // 2, lax.rem(rank, 2)
        self.other_side = self.far * 2 + 1 - self.side
        self.other_row = (1 - self.row) * 2 + self.core
        self.other_core = self.row * 2 + 1 - self.core

    def ahead(self, step):
        return lax.rem(self.far + step, self.count)

    def line(self, step):
        return self.ahead(step) * 2 + self.side


def greet_neighbours(here):
    barrier = pltpu.get_barrier_semaphore()
    peers = [(here.other_side, here.rank), (here.device, here.other_row), (here.device, here.other_core)]
    peers += [(here.line(step), here.rank) for step in range(1, here.count)]
    for peer in peers:
        pl.semaphore_signal(barrier, inc=1, device_id=peer, device_id_type=pl.DeviceIdType.MESH)
    pl.semaphore_wait(barrier, len(peers))


def add_into(target, left, right):
    target[...] = (left[...].astype(jnp.float32) + right[...].astype(jnp.float32)).astype(target.dtype)


class ScatterChain:
    def __init__(self, here, source, out, scratch):
        self.here, self.source, self.out = here, source, out
        (self.keep, self.land_core, self.first_one, self.last_one, self.first_two, self.last_two,
         self.line, self.land_line, self.semaphores) = scratch
        self.rows = self.land_line.shape[1]
        self.half = here.count // 2

    @staticmethod
    def scratch(width, columns, dp):
        rows, far = width // dp, dp // 2
        half = far // 2
        low = lambda *shape: pltpu.VMEM(shape + (columns,), jnp.bfloat16)
        return [
            low(2, width), low(2, width),
            low(2, half, rows), low(2 * half * rows), low(half, rows), low(half, rows),
            low(far, rows), low(far - 1, rows),
            pltpu.SemaphoreType.DMA((CHAIN_SLOTS, 2)),
        ]

    def chunk(self, row, far, side):
        return self.keep.at[row, pl.ds(pl.multiple_of((far * 2 + side) * self.rows, self.rows), self.rows)]

    def send(self, slot, source, target, device, rank):
        push(source, target, self.semaphores.at[slot, 0], self.semaphores.at[slot, 1], device, rank)

    def arrived(self, slot, ref):
        wait_bytes(ref, self.semaphores.at[slot, 1])

    def left(self, slot, ref):
        wait_bytes(ref, self.semaphores.at[slot, 0])

    def stage_core(self):
        here = self.here
        for row in range(2):
            pltpu.make_async_copy(
                self.source.at[row * 2 + here.core], self.keep.at[row], self.semaphores.at[6, 0]
            ).start()
            self.send(0, self.source.at[row * 2 + 1 - here.core], self.land_core.at[row], here.device, here.other_core)

    def stage_one(self):
        here = self.here
        wait_bytes(self.keep, self.semaphores.at[6, 0])
        self.arrived(0, self.land_core)

        def one(index, carry):
            rows = pl.ds(pl.multiple_of(index * self.rows, self.rows), self.rows)
            for row in range(2):
                add_into(self.keep.at[row, rows], self.keep.at[row, rows], self.land_core.at[row, rows])
            return carry

        lax.fori_loop(0, here.count * 2, one, 0)
        start = self.half * 2 * self.rows
        for row in range(2):
            for far in range(self.half):
                self.send(
                    1, self.chunk(row, far, 1 - here.side), self.first_one.at[row, far], here.other_side, here.rank
                )
        self.send(
            2, self.keep.at[1 - here.row, pl.ds(start, start)], self.last_one, here.device, here.other_row
        )

    def stage_two(self):
        here = self.here
        self.arrived(1, self.first_one)
        for row in range(2):
            for far in range(self.half):
                mine = self.chunk(row, far, here.side)
                add_into(mine, mine, self.first_one.at[row, far])
        for far in range(self.half):
            self.send(3, self.chunk(1 - here.row, far, here.side), self.first_two.at[far], here.device, here.other_row)
        self.arrived(2, self.last_one)
        for far in range(self.half):
            for side in range(2):
                mine = self.chunk(here.row, self.half + far, side)
                add_into(mine, mine, self.last_one.at[pl.ds((far * 2 + side) * self.rows, self.rows)])
        for far in range(self.half):
            self.send(
                4, self.chunk(here.row, self.half + far, 1 - here.side), self.last_two.at[far],
                here.other_side, here.rank,
            )

    def stage_line(self):
        here = self.here
        self.arrived(3, self.first_two)
        self.arrived(4, self.last_two)
        for far in range(here.count):
            land = self.first_two.at[far] if far < self.half else self.last_two.at[far - self.half]
            add_into(self.line.at[far], self.chunk(here.row, far, here.side), land)
        for step in range(1, here.count):
            self.send(5, self.line.at[here.ahead(step)], self.land_line.at[step - 1], here.line(step), here.rank)

    def finish(self):
        self.arrived(5, self.land_line)
        total = self.line[self.here.far].astype(jnp.float32)
        for step in range(1, self.here.count):
            total = total + self.land_line[step - 1].astype(jnp.float32)
        self.out[...] = total
        self.left(0, self.land_core)
        self.left(1, self.first_one)
        self.left(2, self.last_one)
        self.left(3, self.first_two)
        self.left(4, self.last_two)
        self.left(5, self.land_line)


def scatter_kernel(source, out, *scratch):
    here = Where()
    greet_neighbours(here)
    chain = ScatterChain(here, source.at[0], out.at[0], scratch)
    chain.stage_core()
    chain.stage_one()
    chain.stage_two()
    chain.stage_line()
    chain.finish()


def scatter_alone(grads, collective_id):
    _, ranks, width, columns = grads.shape
    dp = lax.axis_size("dp")
    return pl.pallas_call(
        scatter_kernel,
        in_specs=[pl.BlockSpec(memory_space=pl.ANY)],
        out_specs=pl.BlockSpec(memory_space=pltpu.VMEM),
        out_shape=jax.ShapeDtypeStruct((1, width // dp, columns), jnp.float32),
        scratch_shapes=ScatterChain.scratch(width, columns, dp),
        compiler_params=pltpu.CompilerParams(
            collective_id=collective_id, has_side_effects=True, vmem_limit_bytes=VMEM_LIMIT
        ),
        name="scatter_alone",
    )(grads)


def chain_stages(chains):
    if not chains:
        return [], []
    if len(chains) == 1:
        only = chains[0]
        return [[only.stage_core], [only.stage_one], [only.stage_two], [only.stage_line]], [only.finish]
    one, two = chains
    return (
        [[one.stage_core, two.stage_core], [one.stage_one], [one.stage_two, two.stage_one],
         [one.stage_line, two.stage_two]],
        [two.stage_line, one.finish, two.finish],
    )


def make_chains(source, out, scratch):
    if source is None:
        return None, []
    here = Where()
    size = len(scratch) // out.shape[0]
    return here, [
        ScatterChain(here, source.at[kind], out.at[kind], scratch[kind * size : (kind + 1) * size])
        for kind in range(out.shape[0])
    ]


def run_chains(here, chains, step, steps):
    stages, _ = chain_stages(chains)
    for index, group in enumerate(stages):

        @pl.when(step == min(index, steps - 1))
        def _():
            if index == 0:
                greet_neighbours(here)
            for stage in group:
                stage()


def end_chains(chains):
    for stage in chain_stages(chains)[1]:
        stage()


def chain_arguments(grads):
    if grads is None:
        return [], [], [], [], []
    kinds, _, width, columns = grads.shape
    dp = lax.axis_size("dp")
    shape = (kinds, width // dp, columns)
    return (
        [grads],
        [pl.BlockSpec(memory_space=pl.ANY)],
        [fixed(shape)],
        [jax.ShapeDtypeStruct(shape, jnp.float32)],
        ScatterChain.scratch(width, columns, dp) * kinds,
    )


def split_refs(refs, scattering, counts):
    sources, inputs, outputs, scratch = counts
    refs = list(refs)
    take = lambda number: [refs.pop(0) for _ in range(number)]
    parts = [take(sources), take(scattering), take(inputs), take(outputs), take(scattering), take(scratch), refs]
    for index in (1, 4):
        parts[index] = parts[index][0] if scattering else None
    return parts


def adam_update(weight, first, second, grad, rate, decay):
    first_new = BETA_ONE * first + (1.0 - BETA_ONE) * grad
    second_new = BETA_TWO * second + (1.0 - BETA_TWO) * grad * grad
    corrected = (
        first_new
        / (1.0 - BETA_ONE**STEP)
        / (jnp.sqrt(second_new / (1.0 - BETA_TWO**STEP)) + ADAM_EPS)
    )
    weight_new = weight - rate * (corrected + decay * weight)
    return (weight_new, first_new, second_new, weight_new.astype(jnp.bfloat16))


def dot32(form, left, right):
    return jnp.einsum(form, left, right, preferred_element_type=jnp.float32)


def exchange(blocks):
    return lax.all_to_all(blocks, "tensor", split_axis=0, concat_axis=0, tiled=True)


def flip(value, axis, bit):
    count = lax.axis_size(axis)
    return lax.ppermute(value, axis, [(n, n ^ bit) for n in range(count)])


def far_shift(value, shift):
    far = lax.axis_size("dp") // 2
    return lax.ppermute(
        value, "dp", [(2 * n + side, 2 * ((n + shift) % far) + side) for n in range(far) for side in range(2)]
    )


def in_pieces(rows):
    return rows % 16 == 0


def gather_weights(shard, after):
    kinds, rows, width = shard.shape
    if not in_pieces(rows):
        whole = lax.all_gather(shard, ("tensor", "dp"), axis=1, tiled=True)
        return (whole.reshape(kinds, -1, lax.axis_size("dp") * rows, width),), after
    if after is not None:
        shard, _ = lax.optimization_barrier((shard, after))
    far = lax.axis_size("dp") // 2
    line = [shard] + [far_shift(shard, shift) for shift in range(1, far)]
    half = far // 2
    mine = jnp.stack(line)
    over_side = flip(mine, "dp", 1)
    over_row = flip(mine, "tensor", 2)
    across = jnp.concatenate([flip(over_side[:half], "tensor", 2), flip(over_row[half:], "dp", 1)])
    own = jnp.stack([jnp.stack([mine, over_side]), jnp.stack([over_row, across])])
    return (own, flip(own, "tensor", 1)), line[-1]


def scatter_plain(grads):
    kinds, ranks, width, cols = grads.shape
    flat = grads.reshape(kinds, ranks * width, cols)
    summed = lax.psum_scatter(flat, ("tensor", "dp"), scatter_dimension=1, tiled=True)
    return summed.astype(jnp.float32)


def per_device(
    clips, cotangent, timesteps, labels, time_table, class_table,
    attention_weights, attention_first, attention_second,
    ffn_weights, ffn_first, ffn_second,
    modulation_weights, modulation_first, modulation_second,
    bias_vectors, bias_first, bias_second,
):
    layers, kinds, rows, cols = attention_weights.shape
    _, frames, patches, width = clips.shape
    mod_rows = modulation_weights.shape[1]
    bias_cols = bias_vectors.shape[1]
    dp, tp = lax.axis_size("dp"), lax.axis_size("tensor")
    position = lax.axis_index("dp") * tp + lax.axis_index("tensor")
    tokens = frames * patches
    strip = patches // (tp * frames)
    blocks = (tp, frames, frames * strip, width)
    pieces = (tp * frames, frames, strip, width)

    embed = time_table[timesteps] + class_table[labels]
    cond_act = jax.nn.silu(embed).astype(jnp.bfloat16)
    low = bias_vectors.astype(jnp.bfloat16).reshape(-1)
    row = jnp.concatenate([cond_act[0], low]).astype(jnp.float32)
    row = jnp.pad(row, (0, -row.shape[0] % 1024)).reshape(-1, 128)
    gathered = gather_all(row, 0).reshape(dp * tp, -1)
    cond_all = gathered[::tp, :width].astype(jnp.bfloat16)
    bias_low = gathered[:, width : width + layers * bias_cols].reshape(dp * tp, layers, bias_cols)
    bias_low = bias_low.transpose(1, 0, 2).reshape(layers, -1)
    cond_rows = lax.dynamic_slice_in_dim(cond_all, position * mod_rows, mod_rows, axis=1)
    modulation_low = modulation_weights.astype(jnp.bfloat16)
    mod_part = dot32("ck,lke->cle", cond_rows, modulation_low)
    mod = reduce_clips(mod_part.reshape(dp, tp, -1, 128), 1).reshape(layers, -1)
    mod_width = mod.shape[-1]
    mod = (mod + bias_low[:, -mod_width:]).reshape(layers, 6, width)
    hidden_width = bias_low.shape[1] - mod_width - 4 * width
    bias_up = bias_low[:, 3 * width : 3 * width + hidden_width].reshape(layers, tp, 1, -1)
    bias_out = bias_low[:, None, 2 * width : 3 * width]
    bias_down = bias_low[:, None, 3 * width + hidden_width : 4 * width + hidden_width]
    bias_project = [
        pack_bias(bias_low[layer, :width], bias_low[layer, width : 2 * width], tp) for layer in range(layers)
    ]

    attention, ffn, after = [], [], None
    for layer in range(layers):
        packed = pack_heads(attention_weights[layer].astype(jnp.bfloat16))[None]
        packed, after = gather_weights(packed, after)
        attention.append(packed)
        wide, after = gather_weights(ffn_weights[layer].astype(jnp.bfloat16), after)
        ffn.append(wide)

    by_patch = lambda v: v.reshape(frames, tp * frames, strip, width).transpose(1, 0, 2, 3)
    cot = exchange(by_patch(cotangent[0]).reshape(blocks))

    def forward(layer, stream, stride, result_shape):
        project, mixed, branch, middle = attention_forward(
            attention[layer], stream, mod[layer], bias_project[layer], bias_out[layer], stride
        )
        middle = middle.reshape(tokens, width)
        hidden, down, result = ffn_forward(
            ffn[layer], middle, mod[layer], bias_down[layer], bias_up[layer], result_shape, jnp.bfloat16
        )
        return result, ((project, mixed, branch), middle, hidden, down)

    fused = in_pieces(rows)

    def backward(layer, grad, stream, saved, stride, result_type, waiting, ids):
        heads, middle, hidden, down = saved
        grad_middle, ffn_grad, up_sum, low_sums, *scattered = ffn_backward(
            ffn[layer], grad, middle, down, hidden, mod[layer], waiting if fused else None, ids[0]
        )
        if waiting is not None and not fused:
            scattered = [scatter_plain(waiting)]
        grad, attention_grad, sums, project_sum, *ffn_done = attention_backward(
            attention[layer], grad_middle.reshape(stream.shape), stream, heads, mod[layer], stride,
            result_type, ffn_grad if fused else None, ids[1],
        )
        if not fused:
            ffn_done = [scatter_plain(ffn_grad)]
        small = jnp.concatenate(
            [*unpack_bias(project_sum), sums[0], up_sum.reshape(-1), low_sums[0],
             sums[1:].reshape(-1), low_sums[1:].reshape(-1)]
        )
        return grad, attention_grad[None], ffn_done[0], small, scattered

    first = clips[0].reshape(1, frames, patches, width)
    second, saved_first = forward(0, first, 0, pieces)
    second = exchange(second.reshape(blocks))
    result, saved_second = forward(1, second, strip, (tokens, width))
    result = exchange(result.reshape(blocks)).reshape(pieces)
    output = result.transpose(1, 0, 2, 3).reshape(clips.shape)

    grad, packed_b, ffn_b, small_b, _ = backward(
        1, cot.reshape(tokens, width), second, saved_second, strip, jnp.bfloat16, None,
        (None, 4 if fused else None),
    )
    grad = exchange(grad).reshape(pieces)
    grad, packed_a, ffn_a, small_a, (packed_b,) = backward(
        0, grad, first, saved_first, 0, jnp.float32, packed_b, (5, 6) if fused else (None, None)
    )
    packed_a = scatter_alone(packed_a, 7) if fused else scatter_plain(packed_a)
    attention_a, attention_b = unpack_heads(packed_a[0]), unpack_heads(packed_b[0])
    input_grad = grad.reshape(clips.shape)

    small = jnp.stack([small_a, small_b])
    token_width = small.shape[1] - mod_width
    small = sum_ranks(small.reshape(tp, -1, 128), 2).transpose(1, 0, 2, 3).reshape(dp, layers, -1)
    grad_mod_low = small[..., token_width:].astype(jnp.bfloat16)
    grad_bias_all = jnp.concatenate(
        [small[..., :token_width], grad_mod_low.astype(jnp.float32)], axis=-1
    ).sum(axis=0)
    grad_bias = lax.dynamic_slice_in_dim(grad_bias_all, position * bias_cols, bias_cols, axis=1)
    grad_mod_weight = dot32("ck,cle->lke", cond_rows, grad_mod_low)
    grad_act = dot32("cle,lke->ck", grad_mod_low, modulation_low)
    grad_act = gather_all(jnp.pad(grad_act, ((0, 0), (0, 128 - mod_rows))), 3)[:, :, :mod_rows]
    grad_act = lax.dynamic_index_in_dim(grad_act, lax.axis_index("dp"), axis=1, keepdims=False)
    silu_value, silu_pull = jax.vjp(jax.nn.silu, embed)
    cond_grad = silu_pull(grad_act.reshape(1, width))[0]

    grad_attention = jnp.stack([attention_a, attention_b])
    grad_ffn = jnp.stack([ffn_a, ffn_b])
    return (output, input_grad, cond_grad) + (
        adam_update(attention_weights, attention_first, attention_second, grad_attention, MATRIX_RATE, MATRIX_DECAY)
        + adam_update(ffn_weights, ffn_first, ffn_second, grad_ffn, MATRIX_RATE, MATRIX_DECAY)
        + adam_update(modulation_weights, modulation_first, modulation_second, grad_mod_weight, MATRIX_RATE, MATRIX_DECAY)
        + adam_update(bias_vectors, bias_first, bias_second, grad_bias, VECTOR_RATE, 0.0)
    )


def solution(mesh):
    tokens = P("dp", "tensor", None, None)
    matrix = P(None, None, "dp", "tensor")
    modulation = P(None, BOTH, None)
    vector = P(None, BOTH)
    return jax.shard_map(
        per_device,
        mesh=mesh,
        in_specs=(tokens, tokens, P("dp"), P("dp"), P(), P())
        + (matrix,) * 6 + (modulation,) * 3 + (vector,) * 3,
        out_specs=(tokens, tokens, P("dp", None)) + (matrix,) * 8 + (modulation,) * 4 + (vector,) * 4,
        check_vma=False,
    )
```

```python
from functools import partial

import jax
import jax.numpy as jnp
from jax import lax
from jax.experimental import pallas as pl
from jax.experimental.pallas import tpu as pltpu
from jax.sharding import PartitionSpec as P

HD = 64
PAIR = 128
BLOCK = 256
SPLIT = 4
STEP = 10
BETA_ONE = 0.9
BETA_TWO = 0.999
ADAM_EPS = 1e-08
MATRIX_RATE = 0.04
VECTOR_RATE = 0.2
MATRIX_DECAY = 0.1
NORM_EPS = 1e-06
GELU_A = (2.0 / 3.141592653589793) ** 0.5
GELU_B = 0.044715
BLOCKED = -1e30
VMEM_LIMIT = 60 * 1024 * 1024
BOTH = ("dp", "tensor")


def mm(left, right, dims=((1,), (0,))):
    return lax.dot_general(left, right, (dims, ((), ())), preferred_element_type=jnp.float32)


def norm_parts(value):
    average = jnp.mean(value, axis=-1, keepdims=True)
    centred = value - average
    spread = jnp.mean(centred * centred, axis=-1, keepdims=True)
    inverse = lax.rsqrt(spread + NORM_EPS)
    return centred * inverse, inverse


def norm_back(grad, shape, inverse):
    first = jnp.mean(grad, axis=-1, keepdims=True)
    second = jnp.mean(grad * shape, axis=-1, keepdims=True)
    return inverse * (grad - first - shape * second)


def rows_of(ref):
    value = ref[...]
    return value.reshape(-1, value.shape[-1])


def put(ref, value):
    ref[...] = value.reshape(ref.shape).astype(ref.dtype)


def add_rows(ref, index, value):
    ref[pl.ds(index, 1), :] += jnp.sum(value, axis=0, keepdims=True)


def half_masks(rows):
    lane = lax.broadcasted_iota(jnp.int32, (rows, PAIR), 1)
    return lane < HD


def same_patch(tokens, stride):
    row = lax.broadcasted_iota(jnp.int32, (tokens, tokens), 0)
    column = lax.broadcasted_iota(jnp.int32, (tokens, tokens), 1)
    return lax.rem(row, stride) == lax.rem(column, stride)


def swap_halves(value):
    return pltpu.roll(value, HD, 1)


def start_loads(source, kind, target, semaphores):
    for rank in range(target.shape[0]):
        pltpu.make_async_copy(source.at[kind, rank], target.at[rank], semaphores.at[rank]).start()


def wait_loads(target, semaphores, rank):
    pltpu.make_async_copy(target.at[rank], target.at[rank], semaphores.at[rank]).wait()


def softmax_rows(scores, axis):
    raised = jnp.exp(scores - jnp.max(scores, axis=axis, keepdims=True))
    return raised * (1.0 / jnp.sum(raised, axis=axis, keepdims=True))


def attention_forward_kernel(
    stride, source, stream_ref, mod_ref, bias_ref, bias_out_ref,
    project_ref, mixed_ref, branch_ref, middle_ref, weight_ref, semaphores,
):
    ranks = weight_ref.shape[0]

    @pl.when(pl.program_id(0) == 0)
    def _():
        start_loads(source, 0, weight_ref, semaphores)

    stream = rows_of(stream_ref).astype(jnp.float32)
    tokens, width = stream.shape
    shape, _ = norm_parts(stream)
    normed = (shape * (1.0 + mod_ref[1:2]) + mod_ref[0:1]).astype(jnp.bfloat16)
    lower = half_masks(tokens)
    allowed = same_patch(tokens, stride) if stride else None

    @pl.when(pl.program_id(0) == 0)
    def _():
        for rank in range(ranks):
            wait_loads(weight_ref, semaphores, rank)

    def one_head(chosen, key, value):
        scores = mm(chosen.astype(jnp.bfloat16), key, ((1,), (1,)))
        if stride:
            scores = jnp.where(allowed, scores, BLOCKED)
        return mm(softmax_rows(scores, -1).astype(jnp.bfloat16), value)

    branch = None
    for rank in range(ranks):
        project = (mm(normed, weight_ref[rank, :, : 5 * PAIR]) + bias_ref[rank]).astype(jnp.bfloat16)
        project_ref[rank] = project.reshape(project_ref.shape[1:])
        query = project[:, :PAIR].astype(jnp.float32) * HD**-0.5
        key, value = project[:, PAIR : 2 * PAIR], project[:, 2 * PAIR : 3 * PAIR]
        first = one_head(jnp.where(lower, query, 0.0), key, value)
        second = one_head(jnp.where(lower, 0.0, query), key, value)
        both = project[:, 3 * PAIR : 4 * PAIR].astype(jnp.float32)
        last = one_head(
            jnp.where(lower, both * HD**-0.5, 0.0),
            swap_halves(both).astype(jnp.bfloat16),
            project[:, 4 * PAIR : 5 * PAIR],
        )
        mixed = jnp.concatenate(
            [jnp.where(lower, 0.0, swap_halves(last)), jnp.where(lower, first, second)], axis=1
        ).astype(jnp.bfloat16)
        mixed_ref[rank] = mixed.reshape(mixed_ref.shape[1:])
        term = mm(mixed, weight_ref[rank, :, 4 * PAIR :], ((1,), (1,)))
        branch = term if branch is None else branch + term
    branch = branch + bias_out_ref[...]
    put(branch_ref, branch)
    put(middle_ref, stream + mod_ref[2:3] * branch)


def gelu_parts(value):
    square = value * value
    bent = jnp.tanh(value * (GELU_A + (GELU_A * GELU_B) * square))
    half = 0.5 * (1.0 + bent)
    slope = half + (0.5 * value) * (1.0 - bent * bent) * (GELU_A + (3.0 * GELU_A * GELU_B) * square)
    return value * half, slope


def ffn_forward_kernel(
    stream, source, middle_ref, mod_ref, bias_ref, bias_up_ref, hidden_ref, branch_ref, *rest
):
    if stream is None:
        result_ref, *rest = rest
    up_ref, down_ref, up_semaphores, down_semaphores = rest
    step = pl.program_id(0)
    ranks = up_ref.shape[0]

    @pl.when(step == 0)
    def _():
        start_loads(source, 0, up_ref, up_semaphores)
        start_loads(source, 1, down_ref, down_semaphores)

    middle = middle_ref[...]
    shape, _ = norm_parts(middle)
    second = (shape * (1.0 + mod_ref[4:5]) + mod_ref[3:4]).astype(jnp.bfloat16)

    @pl.when(step == 0)
    def _():
        for rank in range(ranks):
            wait_loads(up_ref, up_semaphores, rank)
            wait_loads(down_ref, down_semaphores, rank)

    down = None
    for rank in range(ranks):
        hidden = mm(second, up_ref[rank]) + bias_up_ref[rank]
        hidden_ref[rank] = hidden.astype(jnp.bfloat16)
        active, _ = gelu_parts(hidden)
        part = mm(active.astype(jnp.bfloat16), down_ref[rank], ((1,), (1,)))
        down = part if down is None else down + part
    down = down + bias_ref[...]
    branch_ref[...] = down.astype(jnp.bfloat16)
    result = middle + mod_ref[5:6] * down
    if stream is None:
        result_ref[...] = result.astype(result_ref.dtype)
    else:
        stream.put(step, result)


def load_frame(ref, index, chunk):
    if len(ref.shape) == 2:
        return ref[index * chunk : (index + 1) * chunk, :].astype(jnp.float32)
    value = ref[:, index]
    return value.reshape(chunk, value.shape[-1]).astype(jnp.float32)


def ffn_backward_kernel(
    split, source, grad_ref, middle_ref, branch_ref, hidden_ref, mod_ref,
    grad_middle_ref, weight_grad_ref, up_sum_ref, sums_ref,
    up_ref, down_ref, up_semaphores, down_semaphores,
    second_ref, low_ref, active_ref, slope_ref, total_ref,
):
    step = pl.program_id(0)
    tokens, width = middle_ref.shape
    chunk = tokens // split

    @pl.when(step == 0)
    def _():
        start_loads(source, 0, up_ref, up_semaphores)
        start_loads(source, 1, down_ref, down_semaphores)
        sums_ref[...] = jnp.zeros_like(sums_ref)
        for index in range(split):
            rows = slice(index * chunk, (index + 1) * chunk)
            grad = load_frame(grad_ref, index, chunk)
            low = (mod_ref[5:6] * grad).astype(jnp.bfloat16)
            low_ref[rows, :] = low
            add_rows(sums_ref, 0, low.astype(jnp.float32))
            add_rows(sums_ref, 3, grad * branch_ref[rows, :].astype(jnp.float32))
            shape, _ = norm_parts(middle_ref[rows, :])
            second_ref[rows, :] = (shape * (1.0 + mod_ref[4:5]) + mod_ref[3:4]).astype(jnp.bfloat16)

    up_sum_ref[...] = jnp.zeros_like(up_sum_ref)
    wait_loads(up_ref, up_semaphores, step)
    wait_loads(down_ref, down_semaphores, step)

    def one(index, carry):
        rows = pl.ds(pl.multiple_of(index * chunk, chunk), chunk)
        active, slope = gelu_parts(hidden_ref[0, rows, :].astype(jnp.float32))
        active_ref[rows, :] = active.astype(jnp.bfloat16)
        low = (mm(low_ref[rows, :], down_ref[step]) * slope).astype(jnp.bfloat16)
        slope_ref[rows, :] = low
        up_sum_ref[0] += jnp.sum(low.astype(jnp.float32), axis=0, keepdims=True)
        part = mm(low, up_ref[step], ((1,), (1,)))
        total_ref[rows, :] = jnp.where(step == 0, 0.0, total_ref[rows, :]) + part
        return carry

    lax.fori_loop(0, split, one, 0, unroll=True)

    def weights(index, carry):
        part = pl.ds(pl.multiple_of(index * BLOCK, BLOCK), BLOCK)
        weight_grad_ref[0, 0, part, :] = mm(second_ref[:, part], slope_ref[...], ((0,), (0,))).astype(
            jnp.bfloat16
        )
        weight_grad_ref[1, 0, part, :] = mm(low_ref[:, part], active_ref[...], ((0,), (0,))).astype(
            jnp.bfloat16
        )
        return carry

    lax.fori_loop(0, width // BLOCK, weights, 0)

    @pl.when(step == pl.num_programs(0) - 1)
    def _():
        for index in range(split):
            rows = slice(index * chunk, (index + 1) * chunk)
            shape, inverse = norm_parts(middle_ref[rows, :])
            grad = total_ref[rows, :]
            add_rows(sums_ref, 1, grad)
            add_rows(sums_ref, 2, grad * shape)
            back = norm_back(grad * (1.0 + mod_ref[4:5]), shape, inverse)
            grad_middle_ref[rows, :] = load_frame(grad_ref, index, chunk) + back


def attention_backward_kernel(
    stride, swap, source, grad_ref, stream_ref, project_ref, mixed_ref, branch_ref, mod_ref, *refs
):
    if swap is None:
        grad_stream_ref, *refs = refs
    (weight_grad_ref, sums_ref, project_sum_ref,
     weight_ref, semaphores, left_ref, right_ref, outer_ref) = refs
    step = pl.program_id(0)
    ranks = weight_ref.shape[0]

    @pl.when(step == 0)
    def _():
        start_loads(source, 0, weight_ref, semaphores)
        sums_ref[...] = jnp.zeros_like(sums_ref)
        project_sum_ref[...] = jnp.zeros_like(project_sum_ref)

    grad_middle = rows_of(grad_ref)
    tokens, width = grad_middle.shape
    stream = rows_of(stream_ref).astype(jnp.float32)
    shape, inverse = norm_parts(stream)
    rows = pl.ds(pl.multiple_of(step * tokens, tokens), tokens)
    normed = (shape * (1.0 + mod_ref[1:2]) + mod_ref[0:1]).astype(jnp.bfloat16)
    low = (mod_ref[2:3] * grad_middle).astype(jnp.bfloat16)
    left_ref[0, rows, :] = normed
    left_ref[1, rows, :] = low
    add_rows(sums_ref, 0, low.astype(jnp.float32))
    add_rows(sums_ref, 3, grad_middle * rows_of(branch_ref).astype(jnp.float32))
    lower = half_masks(tokens)
    allowed = same_patch(tokens, stride) if stride else None
    scale = HD**-0.5

    @pl.when(step == 0)
    def _():
        for rank in range(ranks):
            wait_loads(weight_ref, semaphores, rank)

    def one_head(chosen, key, value, taken):
        scores = mm(key, chosen.astype(jnp.bfloat16), ((1,), (1,)))
        if stride:
            scores = jnp.where(allowed, scores, BLOCKED)
        probs = softmax_rows(scores, 0)
        grad_probs = mm(value, taken.astype(jnp.bfloat16), ((1,), (1,)))
        inner = jnp.sum(grad_probs * probs, axis=0, keepdims=True)
        return probs.astype(jnp.bfloat16), (probs * (grad_probs - inner)).astype(jnp.bfloat16)

    grad_normed = None
    for rank in range(ranks):
        project = project_ref[rank].reshape(tokens, 5 * PAIR)
        mixed = mixed_ref[rank].reshape(tokens, 2 * PAIR)
        outer_ref[rank, rows, :] = mixed
        grad_mixed = mm(low, weight_ref[rank, :, 4 * PAIR :]).astype(jnp.bfloat16)
        query, key, value = (project[:, n * PAIR : (n + 1) * PAIR] for n in range(3))
        query_wide = query.astype(jnp.float32) * scale
        pair = grad_mixed[:, PAIR:]
        pair_wide = pair.astype(jnp.float32)
        outs = []
        for keep in (lower, ~lower):
            probs, grad_scores = one_head(
                jnp.where(keep, query_wide, 0.0), key, value, jnp.where(keep, pair_wide, 0.0)
            )
            outs.append(
                (mm(grad_scores, key, ((0,), (0,))), mm(grad_scores, query), mm(probs, pair))
            )
        parts = [
            jnp.where(lower, one, two) * factor
            for one, two, factor in zip(outs[0], outs[1], (scale, scale, 1.0))
        ]
        both = project[:, 3 * PAIR : 4 * PAIR].astype(jnp.float32)
        swapped = swap_halves(both).astype(jnp.bfloat16)
        single = swap_halves(grad_mixed[:, :PAIR].astype(jnp.float32))
        probs, grad_scores = one_head(
            jnp.where(lower, both * scale, 0.0),
            swapped,
            project[:, 4 * PAIR :],
            jnp.where(lower, single, 0.0),
        )
        parts.append(
            jnp.where(lower, mm(grad_scores, swapped, ((0,), (0,))), mm(grad_scores, swapped)) * scale
        )
        parts.append(jnp.where(lower, mm(probs, single.astype(jnp.bfloat16)), 0.0))
        whole = jnp.concatenate(parts, axis=1).astype(jnp.bfloat16)
        right_ref[rank, rows, :] = whole
        add_rows(project_sum_ref, rank, whole.astype(jnp.float32))
        term = mm(whole, weight_ref[rank, :, : 5 * PAIR], ((1,), (1,)))
        grad_normed = term if grad_normed is None else grad_normed + term
    add_rows(sums_ref, 1, grad_normed)
    add_rows(sums_ref, 2, grad_normed * shape)
    back = norm_back(grad_normed * (1.0 + mod_ref[1:2]), shape, inverse)
    if swap is None:
        put(grad_stream_ref, grad_middle + back)
    else:
        swap.put(step, grad_middle + back)

    @pl.when(step == pl.num_programs(0) - 1)
    def _():
        def weights(rank, carry):
            def block(index, inner):
                part = pl.ds(pl.multiple_of(index * BLOCK, BLOCK), BLOCK)
                inside = mm(left_ref[0, :, part], right_ref[rank], ((0,), (0,)))
                outside = mm(left_ref[1, :, part], outer_ref[rank], ((0,), (0,)))
                weight_grad_ref[rank, part, : 4 * PAIR] = inside[:, : 4 * PAIR].astype(jnp.bfloat16)
                weight_grad_ref[rank, part, 4 * PAIR : 5 * PAIR] = (
                    inside[:, 4 * PAIR :] + outside[:, :PAIR]
                ).astype(jnp.bfloat16)
                weight_grad_ref[rank, part, 5 * PAIR :] = outside[:, PAIR:].astype(jnp.bfloat16)
                return inner

            return lax.fori_loop(0, width // BLOCK, block, carry)

        lax.fori_loop(0, ranks, weights, 0)


def fixed(shape):
    return pl.BlockSpec(shape, lambda step: (0,) * len(shape))


def cost(flops, moved, raised=0):
    return pl.CostEstimate(flops=int(flops), bytes_accessed=int(moved), transcendentals=int(raised))


def group_spec(shape):
    return pl.BlockSpec((shape[0], 1, shape[2], shape[3]), lambda step: (0, step, 0, 0))


def rank_spec(shape):
    return pl.BlockSpec((shape[0], shape[1], 1) + shape[3:], lambda step: (0, 0, step, 0, 0))


def attention_forward(weight, stream, mod, bias, bias_out, stride, jobs=(), collective_id=None):
    shape = stream.shape
    width = shape[-1]
    ranks = bias.shape[0]
    tokens = shape[0] * shape[1] * shape[2]
    spec = group_spec(shape)
    low = jax.ShapeDtypeStruct(shape, jnp.bfloat16)
    wide = jax.ShapeDtypeStruct(shape, jnp.float32)
    project = jax.ShapeDtypeStruct((ranks,) + shape[:3] + (5 * PAIR,), jnp.bfloat16)
    mixed = jax.ShapeDtypeStruct((ranks,) + shape[:3] + (2 * PAIR,), jnp.bfloat16)
    return call(
        partial(attention_forward_kernel, stride),
        shape[1],
        [weight, stream, mod, bias, bias_out],
        anywhere(1) + [spec, fixed(mod.shape), fixed(bias.shape), fixed(bias_out.shape)],
        [project, mixed, low, wide],
        [rank_spec(project.shape), rank_spec(mixed.shape), spec, spec],
        [pltpu.VMEM((ranks, width, 6 * PAIR), jnp.bfloat16), pltpu.SemaphoreType.DMA((ranks,))],
        jobs,
        collective_id,
        cost(8 * tokens * width * width * 1.5, tokens * width * 16),
        "attention_forward",
    )


def ffn_weights_scratch(ranks, width, part):
    return [
        pltpu.VMEM((ranks, width, part), jnp.bfloat16),
        pltpu.VMEM((ranks, width, part), jnp.bfloat16),
        pltpu.SemaphoreType.DMA((ranks,)),
        pltpu.SemaphoreType.DMA((ranks,)),
    ]


def ffn_forward(weights, middle, mod, bias_down, bias_up, stream=None, jobs=(), collective_id=None):
    tokens, width = middle.shape
    ranks, _, part = bias_up.shape
    chunk = tokens // SPLIT
    block = pl.BlockSpec((chunk, width), lambda step: (step, 0))
    result = [jax.ShapeDtypeStruct((tokens, width), jnp.bfloat16)] if stream is None else []
    return call(
        partial(ffn_forward_kernel, stream),
        SPLIT,
        [weights, middle, mod, bias_down, bias_up],
        anywhere(1) + [block, fixed(mod.shape), fixed(bias_down.shape), fixed(bias_up.shape)],
        [
            jax.ShapeDtypeStruct((ranks, tokens, part), jnp.bfloat16),
            jax.ShapeDtypeStruct((tokens, width), jnp.bfloat16),
        ] + result,
        [pl.BlockSpec((ranks, chunk, part), lambda step: (0, step, 0)), block] + [block] * len(result),
        ffn_weights_scratch(ranks, width, part),
        ([] if stream is None else [stream]) + list(jobs),
        collective_id,
        cost(4.8 * tokens * width * ranks * part, tokens * width * 14, tokens * ranks * part),
        "ffn_forward",
    )


def ffn_backward(weights, grad, middle, branch, hidden, mod, jobs=(), collective_id=None):
    tokens, width = middle.shape
    ranks, _, part = hidden.shape
    whole = fixed((tokens, width))
    return call(
        partial(ffn_backward_kernel, SPLIT),
        ranks,
        [weights, grad, middle, branch, hidden, mod],
        anywhere(1) + [
            fixed(grad.shape), whole, whole,
            pl.BlockSpec((1, tokens, part), lambda step: (step, 0, 0)),
            fixed(mod.shape),
        ],
        [
            jax.ShapeDtypeStruct((tokens, width), jnp.float32),
            jax.ShapeDtypeStruct((2, ranks, width, part), jnp.bfloat16),
            jax.ShapeDtypeStruct((ranks, 1, part), jnp.float32),
            jax.ShapeDtypeStruct((4, width), jnp.float32),
        ],
        [
            whole,
            pl.BlockSpec((2, 1, width, part), lambda step: (0, step, 0, 0)),
            pl.BlockSpec((1, 1, part), lambda step: (step, 0, 0)),
            fixed((4, width)),
        ],
        ffn_weights_scratch(ranks, width, part) + [
            pltpu.VMEM((tokens, width), jnp.bfloat16),
            pltpu.VMEM((tokens, width), jnp.bfloat16),
            pltpu.VMEM((tokens, part), jnp.bfloat16),
            pltpu.VMEM((tokens, part), jnp.bfloat16),
            pltpu.VMEM((tokens, width), jnp.float32),
        ],
        jobs,
        collective_id,
        cost(9.6 * tokens * width * ranks * part, tokens * width * 20, tokens * ranks * part),
        "ffn_backward",
    )


def attention_backward(weight, grad, stream, saved, mod, stride, swap=None, jobs=(), collective_id=None):
    project, mixed, branch = saved
    shape = stream.shape
    width = shape[-1]
    ranks = project.shape[0]
    tokens = shape[0] * shape[1] * shape[2]
    spec = group_spec(shape)
    result = [jax.ShapeDtypeStruct(shape, jnp.float32)] if swap is None else []
    return call(
        partial(attention_backward_kernel, stride, swap),
        shape[1],
        [weight, grad, stream, project, mixed, branch, mod],
        anywhere(1) + [
            spec, spec, rank_spec(project.shape), rank_spec(mixed.shape), spec, fixed(mod.shape),
        ],
        result + [
            jax.ShapeDtypeStruct((ranks, width, 6 * PAIR), jnp.bfloat16),
            jax.ShapeDtypeStruct((4, width), jnp.float32),
            jax.ShapeDtypeStruct((ranks, 5 * PAIR), jnp.float32),
        ],
        [spec] * len(result) + [
            fixed((ranks, width, 6 * PAIR)), fixed((4, width)), fixed((ranks, 5 * PAIR)),
        ],
        [
            pltpu.VMEM((ranks, width, 6 * PAIR), jnp.bfloat16),
            pltpu.SemaphoreType.DMA((ranks,)),
            pltpu.VMEM((2, tokens, width), jnp.bfloat16),
            pltpu.VMEM((ranks, tokens, 5 * PAIR), jnp.bfloat16),
            pltpu.VMEM((ranks, tokens, 2 * PAIR), jnp.bfloat16),
        ],
        ([] if swap is None else [swap]) + list(jobs),
        collective_id,
        cost(16 * tokens * width * width * 1.5, tokens * width * 20),
        "attention_backward",
    )


def pack_heads(block):
    query, key, value, outer = block
    return jnp.concatenate(
        [query[:, :PAIR], key[:, :PAIR], value[:, :PAIR], query[:, PAIR:], key[:, PAIR:],
         value[:, PAIR:], outer[:, PAIR:], outer[:, :PAIR]], axis=1
    )


def unpack_heads(packed):
    part = lambda start, size: packed[:, start : start + size]
    join = lambda first, last: jnp.concatenate([part(first, PAIR), part(last, HD)], axis=1)
    return jnp.stack(
        [join(0, 3 * PAIR), join(PAIR, 3 * PAIR + HD), join(2 * PAIR, 4 * PAIR), join(5 * PAIR, 4 * PAIR + HD)]
    )


def pack_bias(query, value, ranks):
    query, value = query.reshape(ranks, -1), value.reshape(ranks, -1)
    none = jnp.zeros((ranks, PAIR), query.dtype)
    return jnp.concatenate(
        [query[:, :PAIR], none, value[:, :PAIR], query[:, PAIR:], none[:, :HD], value[:, PAIR:], none[:, :HD]],
        axis=1,
    )[:, None]


def unpack_bias(sums):
    query = jnp.concatenate([sums[:, :PAIR], sums[:, 3 * PAIR : 3 * PAIR + HD]], axis=1)
    value = jnp.concatenate([sums[:, 2 * PAIR : 3 * PAIR], sums[:, 4 * PAIR : 4 * PAIR + HD]], axis=1)
    return query.reshape(-1), value.reshape(-1)


def place():
    return lax.axis_index("dp"), lax.axis_index("tensor"), lax.axis_size("dp"), lax.axis_size("tensor")


def greet_all():
    device, rank, dp, tp = place()
    me, count = device * tp + rank, dp * tp
    barrier = pltpu.get_barrier_semaphore()

    def greet(index, carry):
        peer = lax.rem(me + index, count)
        pl.semaphore_signal(
            barrier, inc=1, device_id=(peer // tp, lax.rem(peer, tp)), device_id_type=pl.DeviceIdType.MESH
        )
        return carry

    lax.fori_loop(1, count, greet, 0)
    pl.semaphore_wait(barrier, count - 1)


def push(source, target, send, receive, device, rank):
    pltpu.make_async_remote_copy(
        src_ref=source, dst_ref=target, send_sem=send, recv_sem=receive,
        device_id=(device, rank), device_id_type=pl.DeviceIdType.MESH,
    ).start()


def wait_bytes(ref, semaphore):
    pltpu.make_async_copy(ref, ref, semaphore).wait()


def gather_all_kernel(value_ref, out_ref, send, receive):
    device, rank, dp, tp = place()
    me, count = device * tp + rank, dp * tp
    greet_all()

    def one(index, carry):
        peer = lax.rem(me + index, count)
        push(value_ref, out_ref.at[me], send, receive, peer // tp, lax.rem(peer, tp))
        return carry

    lax.fori_loop(1, count, one, 0)
    out_ref[me] = value_ref[...]
    wait_bytes(out_ref.at[pl.ds(0, count - 1)], receive)
    wait_bytes(out_ref.at[pl.ds(0, count - 1)], send)


def gather_all(value, collective_id):
    count = lax.axis_size("dp") * lax.axis_size("tensor")
    return pl.pallas_call(
        gather_all_kernel,
        in_specs=[pl.BlockSpec(memory_space=pltpu.VMEM)],
        out_specs=pl.BlockSpec(memory_space=pltpu.VMEM),
        out_shape=jax.ShapeDtypeStruct((count,) + value.shape, value.dtype),
        scratch_shapes=[pltpu.SemaphoreType.DMA, pltpu.SemaphoreType.DMA],
        compiler_params=pltpu.CompilerParams(collective_id=collective_id, has_side_effects=True),
        name="gather_all",
    )(value)


def sum_ranks_kernel(part_ref, out_ref, land_ref, *semaphores):
    device, rank, dp, tp = place()
    barrier = pltpu.get_barrier_semaphore()
    for step in range(1, tp):
        pl.semaphore_signal(
            barrier, inc=1, device_id=(device, lax.rem(rank + step, tp)), device_id_type=pl.DeviceIdType.MESH
        )

    def greet(step, carry):
        pl.semaphore_signal(
            barrier, inc=1, device_id=(lax.rem(device + step, dp), rank), device_id_type=pl.DeviceIdType.MESH
        )
        return carry

    lax.fori_loop(1, dp, greet, 0)
    pl.semaphore_wait(barrier, tp + dp - 2)
    for step in range(1, tp):
        there = lax.rem(rank + step, tp)
        push(part_ref.at[there], land_ref.at[rank], semaphores[0], semaphores[1], device, there)
    land_ref[rank] = part_ref[rank]
    wait_bytes(land_ref.at[pl.ds(0, tp - 1)], semaphores[1])
    mine = out_ref.at[rank]
    mine[device] = jnp.sum(land_ref[...], axis=0)

    def one(step, carry):
        push(mine.at[device], mine.at[device], semaphores[2], semaphores[3], lax.rem(device + step, dp), rank)
        return carry

    lax.fori_loop(1, dp, one, 0)
    wait_bytes(land_ref.at[pl.ds(0, tp - 1)], semaphores[0])
    wait_bytes(mine.at[pl.ds(0, dp - 1)], semaphores[3])
    for step in range(1, tp):
        push(mine, mine, semaphores[4], semaphores[5], device, lax.rem(rank + step, tp))
    wait_bytes(mine.at[pl.ds(0, dp - 1)], semaphores[2])
    wait_bytes(out_ref.at[pl.ds(0, tp - 1)], semaphores[5])
    wait_bytes(out_ref.at[pl.ds(0, tp - 1)], semaphores[4])


def sum_ranks(part, collective_id):
    tp, rows, lanes = part.shape
    return pl.pallas_call(
        sum_ranks_kernel,
        in_specs=[pl.BlockSpec(memory_space=pltpu.VMEM)],
        out_specs=pl.BlockSpec(memory_space=pltpu.VMEM),
        out_shape=jax.ShapeDtypeStruct((tp, lax.axis_size("dp"), rows, lanes), part.dtype),
        scratch_shapes=[pltpu.VMEM((tp, rows, lanes), part.dtype)] + [pltpu.SemaphoreType.DMA] * 6,
        compiler_params=pltpu.CompilerParams(
            collective_id=collective_id, has_side_effects=True, vmem_limit_bytes=VMEM_LIMIT
        ),
        name="sum_ranks",
    )(part)


CHAIN_SLOTS = 7


class Where:
    def __init__(self):
        device, rank = lax.axis_index("dp"), lax.axis_index("tensor")
        self.count = lax.axis_size("dp") // 2
        self.device, self.rank = device, rank
        self.far, self.side = device // 2, lax.rem(device, 2)
        self.row, self.core = rank // 2, lax.rem(rank, 2)
        self.other_side = self.far * 2 + 1 - self.side
        self.other_row = (1 - self.row) * 2 + self.core
        self.other_core = self.row * 2 + 1 - self.core

    def ahead(self, step):
        return lax.rem(self.far + step, self.count)

    def line(self, step):
        return self.ahead(step) * 2 + self.side


def greet_neighbours(here):
    barrier = pltpu.get_barrier_semaphore()
    peers = [(here.other_side, here.rank), (here.device, here.other_row), (here.device, here.other_core)]
    peers += [(here.line(step), here.rank) for step in range(1, here.count)]
    for peer in peers:
        pl.semaphore_signal(barrier, inc=1, device_id=peer, device_id_type=pl.DeviceIdType.MESH)
    pl.semaphore_wait(barrier, len(peers))


def add_into(target, left, right):
    target[...] = (left[...].astype(jnp.float32) + right[...].astype(jnp.float32)).astype(target.dtype)


class ScatterChain:
    def __init__(self, here, source, out, scratch):
        self.here, self.source, self.out = here, source, out
        (self.keep, self.land_core, self.first_one, self.last_one, self.first_two, self.last_two,
         self.line, self.land_line, self.semaphores) = scratch
        self.rows = self.land_line.shape[1]
        self.half = here.count // 2

    @staticmethod
    def scratch(width, columns, dp):
        rows, far = width // dp, dp // 2
        half = far // 2
        low = lambda *shape: pltpu.VMEM(shape + (columns,), jnp.bfloat16)
        return [
            low(2, width), low(2, width),
            low(2, half, rows), low(2 * half * rows), low(half, rows), low(half, rows),
            low(far, rows), low(far - 1, rows),
            pltpu.SemaphoreType.DMA((CHAIN_SLOTS, 2)),
        ]

    def chunk(self, row, far, side):
        return self.keep.at[row, pl.ds(pl.multiple_of((far * 2 + side) * self.rows, self.rows), self.rows)]

    def send(self, slot, source, target, device, rank):
        push(source, target, self.semaphores.at[slot, 0], self.semaphores.at[slot, 1], device, rank)

    def arrived(self, slot, ref):
        wait_bytes(ref, self.semaphores.at[slot, 1])

    def left(self, slot, ref):
        wait_bytes(ref, self.semaphores.at[slot, 0])

    def stage_core(self):
        here = self.here
        for row in range(2):
            pltpu.make_async_copy(
                self.source.at[row * 2 + here.core], self.keep.at[row], self.semaphores.at[6, 0]
            ).start()
            self.send(0, self.source.at[row * 2 + 1 - here.core], self.land_core.at[row], here.device, here.other_core)

    def stage_one(self):
        here = self.here
        wait_bytes(self.keep, self.semaphores.at[6, 0])
        self.arrived(0, self.land_core)

        def one(index, carry):
            rows = pl.ds(pl.multiple_of(index * self.rows, self.rows), self.rows)
            for row in range(2):
                add_into(self.keep.at[row, rows], self.keep.at[row, rows], self.land_core.at[row, rows])
            return carry

        lax.fori_loop(0, here.count * 2, one, 0)
        start = self.half * 2 * self.rows
        for row in range(2):
            for far in range(self.half):
                self.send(
                    1, self.chunk(row, far, 1 - here.side), self.first_one.at[row, far], here.other_side, here.rank
                )
        self.send(
            2, self.keep.at[1 - here.row, pl.ds(start, start)], self.last_one, here.device, here.other_row
        )

    def stage_two(self):
        here = self.here
        self.arrived(1, self.first_one)
        for row in range(2):
            for far in range(self.half):
                mine = self.chunk(row, far, here.side)
                add_into(mine, mine, self.first_one.at[row, far])
        for far in range(self.half):
            self.send(3, self.chunk(1 - here.row, far, here.side), self.first_two.at[far], here.device, here.other_row)
        self.arrived(2, self.last_one)
        for far in range(self.half):
            for side in range(2):
                mine = self.chunk(here.row, self.half + far, side)
                add_into(mine, mine, self.last_one.at[pl.ds((far * 2 + side) * self.rows, self.rows)])
        for far in range(self.half):
            self.send(
                4, self.chunk(here.row, self.half + far, 1 - here.side), self.last_two.at[far],
                here.other_side, here.rank,
            )

    def stage_line(self):
        here = self.here
        self.arrived(3, self.first_two)
        self.arrived(4, self.last_two)
        for far in range(here.count):
            land = self.first_two.at[far] if far < self.half else self.last_two.at[far - self.half]
            add_into(self.line.at[far], self.chunk(here.row, far, here.side), land)
        for step in range(1, here.count):
            self.send(5, self.line.at[here.ahead(step)], self.land_line.at[step - 1], here.line(step), here.rank)

    def finish(self):
        self.arrived(5, self.land_line)
        total = self.line[self.here.far].astype(jnp.float32)
        for step in range(1, self.here.count):
            total = total + self.land_line[step - 1].astype(jnp.float32)
        self.out[...] = total
        self.left(0, self.land_core)
        self.left(1, self.first_one)
        self.left(2, self.last_one)
        self.left(3, self.first_two)
        self.left(4, self.last_two)
        self.left(5, self.land_line)


def scatter_kernel(source, out, *scratch):
    here = Where()
    greet_neighbours(here)
    chain = ScatterChain(here, source.at[0], out.at[0], scratch)
    chain.stage_core()
    chain.stage_one()
    chain.stage_two()
    chain.stage_line()
    chain.finish()


def scatter_alone(grads, collective_id):
    _, ranks, width, columns = grads.shape
    dp = lax.axis_size("dp")
    return pl.pallas_call(
        scatter_kernel,
        in_specs=[pl.BlockSpec(memory_space=pl.ANY)],
        out_specs=pl.BlockSpec(memory_space=pltpu.VMEM),
        out_shape=jax.ShapeDtypeStruct((1, width // dp, columns), jnp.float32),
        scratch_shapes=ScatterChain.scratch(width, columns, dp),
        compiler_params=pltpu.CompilerParams(
            collective_id=collective_id, has_side_effects=True, vmem_limit_bytes=VMEM_LIMIT
        ),
        name="scatter_alone",
    )(grads)


class GatherChain:
    def __init__(self, here, source, out, semaphores):
        self.here, self.source, self.out, self.semaphores = here, source, out, semaphores
        self.rows = out.shape[1] // (2 * here.count)
        self.half = here.count // 2

    @staticmethod
    def scratch():
        return [pltpu.SemaphoreType.DMA((9, 2))]

    def piece(self, rank, far, side):
        rows = pl.ds(pl.multiple_of((far * 2 + side) * self.rows, self.rows), self.rows)
        return self.out.at[rank, rows]

    def send(self, slot, source, target, device, rank):
        push(source, target, self.semaphores.at[slot, 0], self.semaphores.at[slot, 1], device, rank)

    def wait(self, slot, way, pieces):
        wait_bytes(self.out.at[0, pl.ds(0, pieces * self.rows)], self.semaphores.at[slot, way])

    def stage_line(self):
        here = self.here
        mine = self.piece(here.rank, here.far, here.side)
        pltpu.make_async_copy(self.source, mine, self.semaphores.at[8, 0]).start()
        for step in range(1, here.count):
            self.send(0, self.source, mine, here.line(step), here.rank)

    def line_arrived(self):
        self.wait(8, 0, 1)
        self.wait(0, 1, self.here.count - 1)

    def line_left(self):
        self.wait(0, 0, self.here.count - 1)

    def stage_near(self):
        here = self.here
        for far in range(here.count):
            mine = self.piece(here.rank, far, here.side)
            self.send(1, mine, mine, here.other_side, here.rank)
            self.send(2, mine, mine, here.device, here.other_row)
        for far in range(here.count):
            mine = self.piece(here.rank, far, here.side)
            self.send(3, mine, mine, here.device, here.other_core)

    def stage_across(self):
        here, count = self.here, self.here.count
        self.wait(1, 1, count)
        for far in range(self.half):
            other = self.piece(here.rank, far, 1 - here.side)
            self.send(4, other, other, here.device, here.other_row)
        self.wait(2, 1, count)
        for far in range(self.half, count):
            other = self.piece(here.other_row, far, here.side)
            self.send(5, other, other, here.other_side, here.rank)
        for far in range(count):
            for other in (self.piece(here.rank, far, 1 - here.side), self.piece(here.other_row, far, here.side)):
                self.send(6, other, other, here.device, here.other_core)

    def stage_core(self):
        here, count = self.here, self.here.count
        self.wait(4, 1, self.half)
        self.wait(5, 1, count - self.half)
        for far in range(count):
            other = self.piece(here.other_row, far, 1 - here.side)
            self.send(7, other, other, here.device, here.other_core)

    def finish(self):
        count, half = self.here.count, self.half
        self.wait(3, 1, count)
        self.wait(6, 1, 2 * count)
        self.wait(7, 1, count)
        for slot, pieces in ((1, count), (2, count), (3, count), (4, half), (5, count - half), (6, 2 * count), (7, count)):
            self.wait(slot, 0, pieces)


class Job:
    operands, shapes, specs, aliases, space = (), (), (), {}, ()
    stages, last = (), ()


def anywhere(count):
    return [pl.BlockSpec(memory_space=pl.ANY)] * count


class ScatterJob(Job):
    def __init__(self, grads):
        kinds, _, width, columns = grads.shape
        dp = lax.axis_size("dp")
        shape = (kinds, width // dp, columns)
        self.operands = [grads]
        self.shapes, self.specs = [jax.ShapeDtypeStruct(shape, jnp.float32)], [fixed(shape)]
        self.space = ScatterChain.scratch(width, columns, dp) * kinds

    def bind(self, here, inputs, outputs, space):
        size = len(space) // outputs[0].shape[0]
        chains = [
            ScatterChain(here, inputs[0].at[kind], outputs[0].at[kind], space[kind * size : (kind + 1) * size])
            for kind in range(outputs[0].shape[0])
        ]
        one = chains[0]
        if len(chains) == 1:
            self.stages = [[one.stage_core], [one.stage_one], [one.stage_two], [one.stage_line]]
            self.last = [one.finish]
            return
        two = chains[1]
        self.stages = [
            [one.stage_core, two.stage_core], [one.stage_one], [one.stage_two, two.stage_one],
            [one.stage_line, two.stage_two],
        ]
        self.last = [two.stage_line, one.finish, two.finish]


class SpreadJob(Job):
    def __init__(self, buffer):
        self.operands = [buffer]
        self.shapes, self.specs = [jax.ShapeDtypeStruct(buffer.shape, buffer.dtype)], anywhere(1)
        self.aliases = {0: 0}
        self.space = GatherChain.scratch() * 2

    def bind(self, here, inputs, outputs, space):
        one, two = (GatherChain(here, None, outputs[0].at[kind], space[kind]) for kind in range(2))
        self.stages = [
            [one.stage_near], [one.stage_across, two.stage_near], [one.stage_core, two.stage_across], [],
        ]
        self.last = [two.stage_core, one.finish, two.finish]


class GatherJob(Job):
    def __init__(self, whole, begun):
        dp, tp = lax.axis_size("dp"), lax.axis_size("tensor")
        self.operands = [whole, begun]
        self.shapes = [
            jax.ShapeDtypeStruct((v.shape[0], tp, dp * v.shape[1], v.shape[2]), v.dtype) for v in (whole, begun)
        ]
        self.specs = anywhere(2)
        self.space = GatherChain.scratch() * 3

    def chains(self, here, inputs, outputs, space):
        whole = GatherChain(here, inputs[0].at[0], outputs[0].at[0], space[0])
        begun = [
            GatherChain(here, inputs[1].at[kind], outputs[1].at[kind], space[1 + kind]) for kind in range(2)
        ]
        return whole, *begun

    def bind(self, here, inputs, outputs, space):
        whole, one, two = self.chains(here, inputs, outputs, space)
        self.stages = [
            [whole.stage_line], [whole.line_arrived, whole.stage_near, one.stage_line],
            [whole.stage_across, two.stage_line], [whole.stage_core],
        ]
        self.last = [
            whole.finish, whole.line_left, one.line_arrived, one.line_left, two.line_arrived, two.line_left
        ]


class SwapJob(Job):
    def __init__(self, blocks):
        self.operands = [blocks]
        self.shapes, self.specs = [jax.ShapeDtypeStruct(blocks.shape, blocks.dtype)], anywhere(1)
        self.space = [pltpu.SemaphoreType.DMA((3,))]

    def bind(self, here, inputs, outputs, space):
        source, out, semaphores = inputs[0], outputs[0], space[0]
        ranks = out.shape[0]

        def start():
            pltpu.make_async_copy(source.at[here.rank], out.at[here.rank], semaphores.at[2]).start()
            for step in range(1, ranks):
                there = lax.rem(here.rank + step, ranks)
                push(source.at[there], out.at[here.rank], semaphores.at[0], semaphores.at[1], here.device, there)

        def finish():
            wait_bytes(out.at[0], semaphores.at[2])
            wait_bytes(out.at[pl.ds(0, ranks - 1)], semaphores.at[1])
            wait_bytes(out.at[pl.ds(0, ranks - 1)], semaphores.at[0])

        self.stages, self.last = [[start]], [finish]


class StreamJob(Job):
    def __init__(self, shape, frames):
        self.shape, self.frames = shape, frames
        self.shapes, self.specs = [jax.ShapeDtypeStruct(shape, jnp.bfloat16)], anywhere(1)
        ranks, groups, rows, width = shape
        block = (groups, ranks, rows, width)
        if frames:
            block = (frames, ranks, groups, rows // frames, width)
        self.space = [pltpu.VMEM(block, jnp.bfloat16), pltpu.SemaphoreType.DMA((3,))]

    def bind(self, here, inputs, outputs, space):
        self.here, self.out = here, outputs[0]
        self.buffer, self.semaphores = space
        ranks = self.shape[0]

        def finish():
            wait_bytes(self.out.at[0], self.semaphores.at[2])
            wait_bytes(self.out.at[pl.ds(0, ranks - 1)], self.semaphores.at[1])
            wait_bytes(self.out.at[pl.ds(0, ranks - 1)], self.semaphores.at[0])

        self.stages, self.last = [[]], [finish]

    def put(self, step, value):
        here, ranks = self.here, self.shape[0]
        self.buffer[step] = value.reshape(self.buffer.shape[1:]).astype(jnp.bfloat16)
        if self.frames:
            strip = self.buffer.shape[3]
            target = self.out.at[here.rank, :, pl.ds(pl.multiple_of(step * strip, strip), strip)]
        else:
            target = self.out.at[here.rank, step]
        pltpu.make_async_copy(self.buffer.at[step, here.rank], target, self.semaphores.at[2]).start()
        for ahead in range(1, ranks):
            there = lax.rem(here.rank + ahead, ranks)
            push(
                self.buffer.at[step, there], target, self.semaphores.at[0], self.semaphores.at[1],
                here.device, there,
            )


def greet_jobs(here):
    barrier = pltpu.get_barrier_semaphore()
    ranks = lax.axis_size("tensor")
    peers = [(here.other_side, here.rank)]
    peers += [(here.line(step), here.rank) for step in range(1, here.count)]
    peers += [(here.device, lax.rem(here.rank + step, ranks)) for step in range(1, ranks)]
    for peer in peers:
        pl.semaphore_signal(barrier, inc=1, device_id=peer, device_id_type=pl.DeviceIdType.MESH)
    pl.semaphore_wait(barrier, len(peers))


def call(body, steps, arguments, in_specs, out_shape, out_specs, scratch, jobs, collective_id, estimate, name):
    operands = [v for job in jobs for v in job.operands]
    shapes = [v for job in jobs for v in job.shapes]
    specs = [v for job in jobs for v in job.specs]
    space = [v for job in jobs for v in job.space]
    aliases, before, after = {}, len(arguments), len(out_shape)
    for job in jobs:
        for source, target in job.aliases.items():
            aliases[before + source] = after + target
        before, after = before + len(job.operands), after + len(job.shapes)

    def kernel(*refs):
        refs = list(refs)
        take = lambda number: [refs.pop(0) for _ in range(number)]
        inputs, job_inputs = take(len(arguments)), take(len(operands))
        outputs, job_outputs = take(len(out_shape)), take(len(shapes))
        own, job_space = take(len(scratch)), refs
        step = pl.program_id(0)
        if jobs:
            here = Where()
            for job in jobs:
                pick = lambda pool, number: [pool.pop(0) for _ in range(number)]
                job.bind(
                    here, pick(job_inputs, len(job.operands)), pick(job_outputs, len(job.shapes)),
                    pick(job_space, len(job.space)),
                )
            for index in range(steps):
                todo = [stage for job in jobs if index < len(job.stages) for stage in job.stages[index]]
                if not todo and index:
                    continue

                @pl.when(step == index)
                def _():
                    if index == 0:
                        greet_jobs(here)
                    for stage in todo:
                        stage()

        body(*inputs, *outputs, *own)
        if jobs:

            @pl.when(step == steps - 1)
            def _():
                for job in jobs:
                    for stage in job.last:
                        stage()

    more = {"collective_id": collective_id, "has_side_effects": True} if jobs else {}
    return pl.pallas_call(
        kernel,
        grid=(steps,),
        in_specs=list(in_specs) + anywhere(len(operands)),
        out_specs=list(out_specs) + specs,
        out_shape=list(out_shape) + shapes,
        scratch_shapes=list(scratch) + space,
        input_output_aliases=aliases,
        compiler_params=pltpu.CompilerParams(
            vmem_limit_bytes=VMEM_LIMIT, dimension_semantics=("arbitrary",), **more
        ),
        cost_estimate=estimate,
        name=name,
    )(*arguments, *operands)


def entry_kernel(
    per_device, row_ref, modulation_ref, *refs
):
    gather = len(refs) > 8
    refs = list(refs)
    sources = [refs.pop(0), refs.pop(0)] if gather else []
    gathered_ref, mod_ref = refs.pop(0), refs.pop(0)
    targets = [refs.pop(0), refs.pop(0)] if gather else []
    part_ref, land_ref, semaphores, *space = refs
    device, rank, dp, tp = place()
    me, count = device * tp + rank, dp * tp
    quarter = land_ref.shape[2]
    if gather:
        whole, one, two = GatherJob.chains(None, Where(), sources, targets, space)
    greet_all()

    def tell(index, carry):
        peer = lax.rem(me + index, count)
        push(
            row_ref, gathered_ref.at[me], semaphores.at[0], semaphores.at[1], peer // tp, lax.rem(peer, tp)
        )
        return carry

    lax.fori_loop(1, count, tell, 0)
    gathered_ref[me] = row_ref[...]
    if gather:
        whole.stage_line()
    wait_bytes(gathered_ref.at[pl.ds(0, count - 1)], semaphores.at[1])
    padded = modulation_ref.shape[1]
    width = dp * tp * per_device
    chosen = jnp.zeros((count, padded), jnp.float32)
    row = lax.broadcasted_iota(jnp.int32, (PAIR, padded), 0)
    column = lax.broadcasted_iota(jnp.int32, (PAIR, padded), 1)
    for index in range(width // PAIR):
        match = (row + index * PAIR == column + me * per_device) & (column < per_device)
        chosen += mm(
            gathered_ref[:, index, :].astype(jnp.bfloat16), jnp.where(match, 1.0, 0.0).astype(jnp.bfloat16)
        )
    clip = lax.broadcasted_iota(jnp.int32, (dp, count), 0)
    member = lax.broadcasted_iota(jnp.int32, (dp, count), 1)
    leaders = jnp.where(member == clip * tp, 1.0, 0.0).astype(jnp.bfloat16)
    rows = mm(leaders, chosen.astype(jnp.bfloat16)).astype(jnp.bfloat16)
    for layer in range(modulation_ref.shape[0]):
        part = mm(rows, modulation_ref[layer])
        size = part.shape[1]
        for index in range(dp):
            part_ref[index, :, layer * size : (layer + 1) * size] = part[index : index + 1]

    def share(index, carry):
        peer = lax.rem(me + index, count)
        there, lane = peer // tp, lax.rem(peer, tp)
        source = part_ref.at[there, :, pl.ds(pl.multiple_of(lane * quarter, PAIR), quarter)]
        push(source, land_ref.at[me], semaphores.at[2], semaphores.at[3], there, lane)
        return carry

    lax.fori_loop(1, count, share, 0)
    mine = pl.ds(pl.multiple_of(rank * quarter, PAIR), quarter)
    land_ref[me] = part_ref[device, :, mine]
    if gather:
        whole.line_arrived()
        whole.stage_near()
        one.stage_line()
    wait_bytes(land_ref.at[pl.ds(0, count - 1)], semaphores.at[3])
    mod_ref[:, mine] = jnp.sum(land_ref[...], axis=0)
    for step in range(1, tp):
        push(
            mod_ref.at[:, mine], mod_ref.at[:, mine], semaphores.at[4], semaphores.at[5],
            device, lax.rem(rank + step, tp),
        )
    if gather:
        whole.stage_across()
        two.stage_line()
        whole.stage_core()
    wait_bytes(gathered_ref.at[pl.ds(0, count - 1)], semaphores.at[0])
    wait_bytes(land_ref.at[pl.ds(0, count - 1)], semaphores.at[2])
    wait_bytes(mod_ref.at[:, pl.ds(0, (tp - 1) * quarter)], semaphores.at[5])
    wait_bytes(mod_ref.at[:, pl.ds(0, (tp - 1) * quarter)], semaphores.at[4])
    if gather:
        for chain in (one, two):
            chain.line_arrived()
        whole.finish()
        for chain in (whole, one, two):
            chain.line_left()


def enter(row, modulation, per_device, weights, collective_id):
    dp, tp = lax.axis_size("dp"), lax.axis_size("tensor")
    count = dp * tp
    whole = modulation.shape[0] * modulation.shape[2]
    inside = pl.BlockSpec(memory_space=pltpu.VMEM)
    job = GatherJob(*weights) if weights else Job()
    return pl.pallas_call(
        partial(entry_kernel, per_device),
        in_specs=[inside, inside] + anywhere(len(job.operands)),
        out_specs=[inside, inside] + list(job.specs),
        out_shape=[
            jax.ShapeDtypeStruct((count,) + row.shape, jnp.float32),
            jax.ShapeDtypeStruct((1, whole), jnp.float32),
        ] + list(job.shapes),
        scratch_shapes=[
            pltpu.VMEM((dp, 1, whole), jnp.float32),
            pltpu.VMEM((count, 1, whole // tp), jnp.float32),
            pltpu.SemaphoreType.DMA((6,)),
        ] + list(job.space),
        compiler_params=pltpu.CompilerParams(
            collective_id=collective_id, has_side_effects=True, vmem_limit_bytes=VMEM_LIMIT
        ),
        name="enter",
    )(row, modulation, *job.operands)


def adam_update(weight, first, second, grad, rate, decay):
    first_new = BETA_ONE * first + (1.0 - BETA_ONE) * grad
    second_new = BETA_TWO * second + (1.0 - BETA_TWO) * grad * grad
    corrected = (
        first_new
        / (1.0 - BETA_ONE**STEP)
        / (jnp.sqrt(second_new / (1.0 - BETA_TWO**STEP)) + ADAM_EPS)
    )
    weight_new = weight - rate * (corrected + decay * weight)
    return (weight_new, first_new, second_new, weight_new.astype(jnp.bfloat16))


def dot32(form, left, right):
    return jnp.einsum(form, left, right, preferred_element_type=jnp.float32)


def exchange(blocks):
    return lax.all_to_all(blocks, "tensor", split_axis=0, concat_axis=0, tiled=True)


def gather_plain(shard):
    kinds, rows, width = shard.shape
    whole = lax.all_gather(shard, ("tensor", "dp"), axis=1, tiled=True)
    return whole.reshape(kinds, -1, lax.axis_size("dp") * rows, width)


def scatter_plain(grads):
    kinds, ranks, width, cols = grads.shape
    flat = grads.reshape(kinds, ranks * width, cols)
    summed = lax.psum_scatter(flat, ("tensor", "dp"), scatter_dimension=1, tiled=True)
    return summed.astype(jnp.float32)


def per_device(
    clips, cotangent, timesteps, labels, time_table, class_table,
    attention_weights, attention_first, attention_second,
    ffn_weights, ffn_first, ffn_second,
    modulation_weights, modulation_first, modulation_second,
    bias_vectors, bias_first, bias_second,
):
    layers, kinds, rows, cols = attention_weights.shape
    _, frames, patches, width = clips.shape
    mod_rows = modulation_weights.shape[1]
    bias_cols = bias_vectors.shape[1]
    dp, tp = lax.axis_size("dp"), lax.axis_size("tensor")
    position = lax.axis_index("dp") * tp + lax.axis_index("tensor")
    tokens = frames * patches
    strip = patches // (tp * frames)
    blocks = (tp, frames, frames * strip, width)
    pieces = (tp * frames, frames, strip, width)

    embed = time_table[timesteps] + class_table[labels]
    cond_act = jax.nn.silu(embed).astype(jnp.bfloat16)
    fused = rows % 16 == 0
    shards = [
        (
            pack_heads(attention_weights[layer].astype(jnp.bfloat16))[None],
            ffn_weights[layer].astype(jnp.bfloat16),
        )
        for layer in range(layers)
    ]
    low = bias_vectors.astype(jnp.bfloat16).reshape(-1)
    row = jnp.concatenate([cond_act[0], low]).astype(jnp.float32)
    row = jnp.pad(row, (0, -row.shape[0] % 1024)).reshape(-1, 128)
    modulation_low = modulation_weights.astype(jnp.bfloat16)
    modulation_low = jnp.pad(modulation_low, ((0, 0), (0, -mod_rows % 32), (0, 0)))
    gathered, mod, *begun = enter(row, modulation_low, mod_rows, shards[0] if fused else None, 0)
    gathered = gathered.reshape(dp * tp, -1)
    cond_all = gathered[::tp, :width].astype(jnp.bfloat16)
    bias_low = gathered[:, width : width + layers * bias_cols].reshape(dp * tp, layers, bias_cols)
    bias_low = bias_low.transpose(1, 0, 2).reshape(layers, -1)
    cond_rows = lax.dynamic_slice_in_dim(cond_all, position * mod_rows, mod_rows, axis=1)
    cond_rows = jnp.pad(cond_rows, ((0, 0), (0, -mod_rows % 32)))
    mod = mod.reshape(layers, -1)
    mod_width = mod.shape[-1]
    mod = (mod + bias_low[:, -mod_width:]).reshape(layers, 6, width)
    hidden_width = bias_low.shape[1] - mod_width - 4 * width
    bias_up = bias_low[:, 3 * width : 3 * width + hidden_width].reshape(layers, tp, 1, -1)
    bias_out = bias_low[:, None, 2 * width : 3 * width]
    bias_down = bias_low[:, None, 3 * width + hidden_width : 4 * width + hidden_width]
    bias_project = [
        pack_bias(bias_low[layer, :width], bias_low[layer, width : 2 * width], tp) for layer in range(layers)
    ]

    by_patch = lambda v: v.reshape(frames, tp * frames, strip, width).transpose(1, 0, 2, 3)
    cot = by_patch(cotangent[0]).reshape(blocks)
    first = clips[0].reshape(1, frames, patches, width)

    attend = lambda layer, weight, stream, stride, *more: attention_forward(
        weight, stream, mod[layer], bias_project[layer], bias_out[layer], stride, *more
    )
    expand = lambda layer, weights, middle, *more: ffn_forward(
        weights, middle.reshape(tokens, width), mod[layer], bias_down[layer], bias_up[layer], *more
    )
    if fused:
        attention_a, ffn_a = begun
        *heads_a, middle_a, ffn_a = attend(0, attention_a, first, 0, [SpreadJob(ffn_a)], 1)
        hidden_a, down_a, second, attention_b, ffn_b = expand(
            0, ffn_a, middle_a, StreamJob(blocks, frames), [GatherJob(*shards[1])], 2
        )
        *heads_b, middle_b, ffn_b = attend(1, attention_b, second, strip, [SpreadJob(ffn_b)], 3)
        hidden_b, down_b, result, cot = expand(1, ffn_b, middle_b, None, [SwapJob(cot)], 4)
    else:
        (attention_a, ffn_a), (attention_b, ffn_b) = [[gather_plain(v) for v in pair] for pair in shards]
        *heads_a, middle_a = attend(0, attention_a, first, 0)
        hidden_a, down_a, second = expand(0, ffn_a, middle_a)
        second = exchange(by_patch(second).reshape(blocks))
        *heads_b, middle_b = attend(1, attention_b, second, strip)
        hidden_b, down_b, result = expand(1, ffn_b, middle_b)
        cot = exchange(cot)
    middle_a, middle_b = middle_a.reshape(tokens, width), middle_b.reshape(tokens, width)
    result = result.reshape(blocks)
    cot = cot.reshape(tokens, width)

    if fused:
        grad, ffn_grad, *sums_b, result = ffn_backward(
            ffn_b, cot, middle_b, down_b, hidden_b, mod[1], [SwapJob(result)], 5
        )
        packed_b, *more_b, grad, done_ffn_b = attention_backward(
            attention_b, grad.reshape(blocks), second, heads_b, mod[1], strip,
            StreamJob(blocks, 0), [ScatterJob(ffn_grad)], 6,
        )
        grad, ffn_grad, *sums_a, done_b = ffn_backward(
            ffn_a, grad.reshape(pieces), middle_a, down_a, hidden_a, mod[0], [ScatterJob(packed_b[None])], 7
        )
        grad, packed_a, *more_a, done_ffn_a = attention_backward(
            attention_a, grad.reshape(first.shape), first, heads_a, mod[0], 0, None, [ScatterJob(ffn_grad)], 8
        )
        done_a = scatter_alone(packed_a[None], 9)
    else:
        result = exchange(result)
        grad, ffn_grad, *sums_b = ffn_backward(ffn_b, cot, middle_b, down_b, hidden_b, mod[1])
        done_ffn_b = scatter_plain(ffn_grad)
        grad, packed_b, *more_b = attention_backward(
            attention_b, grad.reshape(blocks), second, heads_b, mod[1], strip
        )
        done_b = scatter_plain(packed_b[None])
        grad = exchange(grad.astype(jnp.bfloat16))
        grad, ffn_grad, *sums_a = ffn_backward(ffn_a, grad.reshape(pieces), middle_a, down_a, hidden_a, mod[0])
        done_ffn_a = scatter_plain(ffn_grad)
        grad, packed_a, *more_a = attention_backward(attention_a, grad.reshape(first.shape), first, heads_a, mod[0], 0)
        done_a = scatter_plain(packed_a[None])
    output = result.reshape(pieces).transpose(1, 0, 2, 3).reshape(clips.shape)
    input_grad = grad.reshape(clips.shape)
    grad_attention = jnp.stack([unpack_heads(done_a[0]), unpack_heads(done_b[0])])
    grad_ffn = jnp.stack([done_ffn_a, done_ffn_b])

    def gather_small(more, sums):
        attention_sums, project_sum = more
        up_sum, low_sums = sums
        return jnp.concatenate(
            [*unpack_bias(project_sum), attention_sums[0], up_sum.reshape(-1), low_sums[0],
             attention_sums[1:].reshape(-1), low_sums[1:].reshape(-1)]
        )

    small_a, small_b = gather_small(more_a, sums_a), gather_small(more_b, sums_b)
    small = jnp.stack([small_a, small_b])
    token_width = small.shape[1] - mod_width
    small = sum_ranks(small.reshape(tp, -1, 128), 10).transpose(1, 0, 2, 3).reshape(dp, layers, -1)
    grad_mod_low = small[..., token_width:].astype(jnp.bfloat16)
    grad_bias_all = jnp.concatenate(
        [small[..., :token_width], grad_mod_low.astype(jnp.float32)], axis=-1
    ).sum(axis=0)
    grad_bias = lax.dynamic_slice_in_dim(grad_bias_all, position * bias_cols, bias_cols, axis=1)
    grad_mod_weight = dot32("ck,cle->lke", cond_rows, grad_mod_low)[:, :mod_rows]
    grad_act = dot32("cle,lke->ck", grad_mod_low, modulation_low)
    grad_act = gather_all(jnp.pad(grad_act, ((0, 0), (0, 128 - grad_act.shape[1]))), 11)[:, :, :mod_rows]
    grad_act = lax.dynamic_index_in_dim(grad_act, lax.axis_index("dp"), axis=1, keepdims=False)
    silu_value, silu_pull = jax.vjp(jax.nn.silu, embed)
    cond_grad = silu_pull(grad_act.reshape(1, width))[0]

    return (output, input_grad, cond_grad) + (
        adam_update(attention_weights, attention_first, attention_second, grad_attention, MATRIX_RATE, MATRIX_DECAY)
        + adam_update(ffn_weights, ffn_first, ffn_second, grad_ffn, MATRIX_RATE, MATRIX_DECAY)
        + adam_update(modulation_weights, modulation_first, modulation_second, grad_mod_weight, MATRIX_RATE, MATRIX_DECAY)
        + adam_update(bias_vectors, bias_first, bias_second, grad_bias, VECTOR_RATE, 0.0)
    )


def solution(mesh):
    tokens = P("dp", "tensor", None, None)
    matrix = P(None, None, "dp", "tensor")
    modulation = P(None, BOTH, None)
    vector = P(None, BOTH)
    return jax.shard_map(
        per_device,
        mesh=mesh,
        in_specs=(tokens, tokens, P("dp"), P("dp"), P(), P())
        + (matrix,) * 6 + (modulation,) * 3 + (vector,) * 3,
        out_specs=(tokens, tokens, P("dp", None)) + (matrix,) * 8 + (modulation,) * 4 + (vector,) * 4,
        check_vma=False,
    )
```

```python
from functools import partial

import jax
import jax.numpy as jnp
from jax import lax
from jax.experimental import pallas as pl
from jax.experimental.pallas import tpu as pltpu
from jax.sharding import PartitionSpec as P

HD = 64
PAIR = 128
BLOCK = 256
SPLIT = 4
STEP = 10
BETA_ONE = 0.9
BETA_TWO = 0.999
ADAM_EPS = 1e-08
MATRIX_RATE = 0.04
VECTOR_RATE = 0.2
MATRIX_DECAY = 0.1
NORM_EPS = 1e-06
GELU_A = (2.0 / 3.141592653589793) ** 0.5
GELU_B = 0.044715
BLOCKED = -1e30
VMEM_LIMIT = 60 * 1024 * 1024
BOTH = ("dp", "tensor")


def mm(left, right, dims=((1,), (0,))):
    return lax.dot_general(left, right, (dims, ((), ())), preferred_element_type=jnp.float32)


def norm_parts(value):
    average = jnp.mean(value, axis=-1, keepdims=True)
    centred = value - average
    spread = jnp.mean(centred * centred, axis=-1, keepdims=True)
    inverse = lax.rsqrt(spread + NORM_EPS)
    return centred * inverse, inverse


def norm_back(grad, shape, inverse):
    first = jnp.mean(grad, axis=-1, keepdims=True)
    second = jnp.mean(grad * shape, axis=-1, keepdims=True)
    return inverse * (grad - first - shape * second)


def rows_of(ref):
    value = ref[...]
    return value.reshape(-1, value.shape[-1])


def put(ref, value):
    ref[...] = value.reshape(ref.shape).astype(ref.dtype)


def add_rows(ref, index, value):
    ref[pl.ds(index, 1), :] += jnp.sum(value, axis=0, keepdims=True)


def half_masks(rows):
    lane = lax.broadcasted_iota(jnp.int32, (rows, PAIR), 1)
    return lane < HD


def same_patch(tokens, stride):
    row = lax.broadcasted_iota(jnp.int32, (tokens, tokens), 0)
    column = lax.broadcasted_iota(jnp.int32, (tokens, tokens), 1)
    return lax.rem(row, stride) == lax.rem(column, stride)


def swap_halves(value):
    return pltpu.roll(value, HD, 1)


def start_loads(source, target, semaphores):
    for rank in range(target.shape[0]):
        pltpu.make_async_copy(source.at[rank], target.at[rank], semaphores.at[rank]).start()


def wait_loads(target, semaphores, rank):
    pltpu.make_async_copy(target.at[rank], target.at[rank], semaphores.at[rank]).wait()


def softmax_rows(scores, axis):
    raised = jnp.exp(scores - jnp.max(scores, axis=axis, keepdims=True))
    return raised * (1.0 / jnp.sum(raised, axis=axis, keepdims=True))


def attention_forward_kernel(
    stride, hook, source, stream_ref, mod_ref, bias_ref, bias_out_ref,
    project_ref, mixed_ref, branch_ref, middle_ref, weight_ref, semaphores,
):
    ranks = weight_ref.shape[0]

    @pl.when(pl.program_id(0) == 0)
    def _():
        start_loads(source, weight_ref, semaphores)

    stream = rows_of(stream_ref).astype(jnp.float32)
    tokens, width = stream.shape
    shape, _ = norm_parts(stream)
    normed = (shape * (1.0 + mod_ref[1:2]) + mod_ref[0:1]).astype(jnp.bfloat16)
    lower = half_masks(tokens)
    allowed = same_patch(tokens, stride) if stride else None

    @pl.when(pl.program_id(0) == 0)
    def _():
        for rank in range(ranks):
            wait_loads(weight_ref, semaphores, rank)

    def one_head(chosen, key, value):
        scores = mm(chosen.astype(jnp.bfloat16), key, ((1,), (1,)))
        if stride:
            scores = jnp.where(allowed, scores, BLOCKED)
        return mm(softmax_rows(scores, -1).astype(jnp.bfloat16), value)

    branch = None
    for rank in range(ranks):
        hook(rank)
        project = (mm(normed, weight_ref[rank, :, : 5 * PAIR]) + bias_ref[rank]).astype(jnp.bfloat16)
        project_ref[rank] = project.reshape(project_ref.shape[1:])
        query = project[:, :PAIR].astype(jnp.float32) * HD**-0.5
        key, value = project[:, PAIR : 2 * PAIR], project[:, 2 * PAIR : 3 * PAIR]
        first = one_head(jnp.where(lower, query, 0.0), key, value)
        second = one_head(jnp.where(lower, 0.0, query), key, value)
        both = project[:, 3 * PAIR : 4 * PAIR].astype(jnp.float32)
        last = one_head(
            jnp.where(lower, both * HD**-0.5, 0.0),
            swap_halves(both).astype(jnp.bfloat16),
            project[:, 4 * PAIR : 5 * PAIR],
        )
        mixed = jnp.concatenate(
            [jnp.where(lower, 0.0, swap_halves(last)), jnp.where(lower, first, second)], axis=1
        ).astype(jnp.bfloat16)
        mixed_ref[rank] = mixed.reshape(mixed_ref.shape[1:])
        term = mm(mixed, weight_ref[rank, :, 4 * PAIR :], ((1,), (1,)))
        branch = term if branch is None else branch + term
    branch = branch + bias_out_ref[...]
    put(branch_ref, branch)
    put(middle_ref, stream + mod_ref[2:3] * branch)


def gelu_parts(value):
    square = value * value
    bent = jnp.tanh(value * (GELU_A + (GELU_A * GELU_B) * square))
    half = 0.5 * (1.0 + bent)
    slope = half + (0.5 * value) * (1.0 - bent * bent) * (GELU_A + (3.0 * GELU_A * GELU_B) * square)
    return value * half, slope


def ffn_forward_kernel(
    stream, hook, up_source, down_source, middle_ref, mod_ref, bias_ref, bias_up_ref, hidden_ref, branch_ref, *rest
):
    if stream is None:
        result_ref, *rest = rest
    up_ref, down_ref, up_semaphores, down_semaphores = rest
    step = pl.program_id(0)
    ranks = up_ref.shape[0]

    @pl.when(step == 0)
    def _():
        start_loads(up_source, up_ref, up_semaphores)
        start_loads(down_source, down_ref, down_semaphores)

    middle = middle_ref[...]
    shape, _ = norm_parts(middle)
    second = (shape * (1.0 + mod_ref[4:5]) + mod_ref[3:4]).astype(jnp.bfloat16)

    @pl.when(step == 0)
    def _():
        for rank in range(ranks):
            wait_loads(up_ref, up_semaphores, rank)
            wait_loads(down_ref, down_semaphores, rank)

    down = None
    for rank in range(ranks):
        hook(rank)
        hidden = mm(second, up_ref[rank]) + bias_up_ref[rank]
        hidden_ref[rank] = hidden.astype(jnp.bfloat16)
        active, _ = gelu_parts(hidden)
        part = mm(active.astype(jnp.bfloat16), down_ref[rank], ((1,), (1,)))
        down = part if down is None else down + part
    down = down + bias_ref[...]
    branch_ref[...] = down.astype(jnp.bfloat16)
    result = middle + mod_ref[5:6] * down
    if stream is None:
        result_ref[...] = result.astype(result_ref.dtype)
    else:
        stream.put(step, result)


def load_frame(ref, index, chunk):
    if len(ref.shape) == 2:
        return ref[index * chunk : (index + 1) * chunk, :].astype(jnp.float32)
    value = ref[:, index]
    return value.reshape(chunk, value.shape[-1]).astype(jnp.float32)


def ffn_backward_kernel(
    split, hook, up_source, down_source, grad_ref, middle_ref, branch_ref, hidden_ref, mod_ref,
    grad_middle_ref, weight_grad_ref, up_sum_ref, sums_ref,
    up_ref, down_ref, up_semaphores, down_semaphores,
    second_ref, low_ref, active_ref, slope_ref, total_ref,
):
    step = pl.program_id(0)
    tokens, width = middle_ref.shape
    chunk = tokens // split

    @pl.when(step == 0)
    def _():
        start_loads(up_source, up_ref, up_semaphores)
        start_loads(down_source, down_ref, down_semaphores)
        sums_ref[...] = jnp.zeros_like(sums_ref)
        for index in range(split):
            rows = slice(index * chunk, (index + 1) * chunk)
            grad = load_frame(grad_ref, index, chunk)
            low = (mod_ref[5:6] * grad).astype(jnp.bfloat16)
            low_ref[rows, :] = low
            add_rows(sums_ref, 0, low.astype(jnp.float32))
            add_rows(sums_ref, 3, grad * branch_ref[rows, :].astype(jnp.float32))
            shape, _ = norm_parts(middle_ref[rows, :])
            second_ref[rows, :] = (shape * (1.0 + mod_ref[4:5]) + mod_ref[3:4]).astype(jnp.bfloat16)

    up_sum_ref[...] = jnp.zeros_like(up_sum_ref)
    wait_loads(up_ref, up_semaphores, step)
    wait_loads(down_ref, down_semaphores, step)

    for index in range(split):
        hook(index)
        rows = slice(index * chunk, (index + 1) * chunk)
        active, slope = gelu_parts(hidden_ref[0, rows, :].astype(jnp.float32))
        active_ref[rows, :] = active.astype(jnp.bfloat16)
        low = (mm(low_ref[rows, :], down_ref[step]) * slope).astype(jnp.bfloat16)
        slope_ref[rows, :] = low
        up_sum_ref[0] += jnp.sum(low.astype(jnp.float32), axis=0, keepdims=True)
        part = mm(low, up_ref[step], ((1,), (1,)))
        total_ref[rows, :] = jnp.where(step == 0, 0.0, total_ref[rows, :]) + part

    def weights(index, carry):
        part = pl.ds(pl.multiple_of(index * BLOCK, BLOCK), BLOCK)
        weight_grad_ref[0, 0, part, :] = mm(second_ref[:, part], slope_ref[...], ((0,), (0,))).astype(
            jnp.bfloat16
        )
        weight_grad_ref[1, 0, part, :] = mm(low_ref[:, part], active_ref[...], ((0,), (0,))).astype(
            jnp.bfloat16
        )
        return carry

    lax.fori_loop(0, width // BLOCK, weights, 0)

    @pl.when(step == pl.num_programs(0) - 1)
    def _():
        for index in range(split):
            rows = slice(index * chunk, (index + 1) * chunk)
            shape, inverse = norm_parts(middle_ref[rows, :])
            grad = total_ref[rows, :]
            add_rows(sums_ref, 1, grad)
            add_rows(sums_ref, 2, grad * shape)
            back = norm_back(grad * (1.0 + mod_ref[4:5]), shape, inverse)
            grad_middle_ref[rows, :] = load_frame(grad_ref, index, chunk) + back


def attention_backward_kernel(
    stride, swap, hook, source, grad_ref, stream_ref, project_ref, mixed_ref, branch_ref, mod_ref, *refs
):
    if swap is None:
        grad_stream_ref, *refs = refs
    (weight_grad_ref, sums_ref, project_sum_ref,
     weight_ref, semaphores, left_ref, right_ref, outer_ref) = refs
    step = pl.program_id(0)
    ranks = weight_ref.shape[0]

    @pl.when(step == 0)
    def _():
        start_loads(source, weight_ref, semaphores)
        sums_ref[...] = jnp.zeros_like(sums_ref)
        project_sum_ref[...] = jnp.zeros_like(project_sum_ref)

    grad_middle = rows_of(grad_ref)
    tokens, width = grad_middle.shape
    stream = rows_of(stream_ref).astype(jnp.float32)
    shape, inverse = norm_parts(stream)
    rows = pl.ds(pl.multiple_of(step * tokens, tokens), tokens)
    normed = (shape * (1.0 + mod_ref[1:2]) + mod_ref[0:1]).astype(jnp.bfloat16)
    low = (mod_ref[2:3] * grad_middle).astype(jnp.bfloat16)
    left_ref[0, rows, :] = normed
    left_ref[1, rows, :] = low
    add_rows(sums_ref, 0, low.astype(jnp.float32))
    add_rows(sums_ref, 3, grad_middle * rows_of(branch_ref).astype(jnp.float32))
    lower = half_masks(tokens)
    allowed = same_patch(tokens, stride) if stride else None
    scale = HD**-0.5

    @pl.when(step == 0)
    def _():
        for rank in range(ranks):
            wait_loads(weight_ref, semaphores, rank)

    def one_head(chosen, key, value, taken):
        scores = mm(key, chosen.astype(jnp.bfloat16), ((1,), (1,)))
        if stride:
            scores = jnp.where(allowed, scores, BLOCKED)
        probs = softmax_rows(scores, 0)
        grad_probs = mm(value, taken.astype(jnp.bfloat16), ((1,), (1,)))
        inner = jnp.sum(grad_probs * probs, axis=0, keepdims=True)
        return probs.astype(jnp.bfloat16), (probs * (grad_probs - inner)).astype(jnp.bfloat16)

    grad_normed = None
    for rank in range(ranks):
        hook(rank)
        project = project_ref[rank].reshape(tokens, 5 * PAIR)
        mixed = mixed_ref[rank].reshape(tokens, 2 * PAIR)
        outer_ref[rank, rows, :] = mixed
        grad_mixed = mm(low, weight_ref[rank, :, 4 * PAIR :]).astype(jnp.bfloat16)
        query, key, value = (project[:, n * PAIR : (n + 1) * PAIR] for n in range(3))
        query_wide = query.astype(jnp.float32) * scale
        pair = grad_mixed[:, PAIR:]
        pair_wide = pair.astype(jnp.float32)
        outs = []
        for keep in (lower, ~lower):
            probs, grad_scores = one_head(
                jnp.where(keep, query_wide, 0.0), key, value, jnp.where(keep, pair_wide, 0.0)
            )
            outs.append(
                (mm(grad_scores, key, ((0,), (0,))), mm(grad_scores, query), mm(probs, pair))
            )
        parts = [
            jnp.where(lower, one, two) * factor
            for one, two, factor in zip(outs[0], outs[1], (scale, scale, 1.0))
        ]
        both = project[:, 3 * PAIR : 4 * PAIR].astype(jnp.float32)
        swapped = swap_halves(both).astype(jnp.bfloat16)
        single = swap_halves(grad_mixed[:, :PAIR].astype(jnp.float32))
        probs, grad_scores = one_head(
            jnp.where(lower, both * scale, 0.0),
            swapped,
            project[:, 4 * PAIR :],
            jnp.where(lower, single, 0.0),
        )
        parts.append(
            jnp.where(lower, mm(grad_scores, swapped, ((0,), (0,))), mm(grad_scores, swapped)) * scale
        )
        parts.append(jnp.where(lower, mm(probs, single.astype(jnp.bfloat16)), 0.0))
        whole = jnp.concatenate(parts, axis=1).astype(jnp.bfloat16)
        right_ref[rank, rows, :] = whole
        add_rows(project_sum_ref, rank, whole.astype(jnp.float32))
        term = mm(whole, weight_ref[rank, :, : 5 * PAIR], ((1,), (1,)))
        grad_normed = term if grad_normed is None else grad_normed + term
    add_rows(sums_ref, 1, grad_normed)
    add_rows(sums_ref, 2, grad_normed * shape)
    back = norm_back(grad_normed * (1.0 + mod_ref[1:2]), shape, inverse)
    if swap is None:
        put(grad_stream_ref, grad_middle + back)
    else:
        swap.put(step, grad_middle + back)

    @pl.when(step == pl.num_programs(0) - 1)
    def _():
        def weights(rank, carry):
            def block(index, inner):
                part = pl.ds(pl.multiple_of(index * BLOCK, BLOCK), BLOCK)
                inside = mm(left_ref[0, :, part], right_ref[rank], ((0,), (0,)))
                outside = mm(left_ref[1, :, part], outer_ref[rank], ((0,), (0,)))
                weight_grad_ref[rank, part, : 4 * PAIR] = inside[:, : 4 * PAIR].astype(jnp.bfloat16)
                weight_grad_ref[rank, part, 4 * PAIR : 5 * PAIR] = (
                    inside[:, 4 * PAIR :] + outside[:, :PAIR]
                ).astype(jnp.bfloat16)
                weight_grad_ref[rank, part, 5 * PAIR :] = outside[:, PAIR:].astype(jnp.bfloat16)
                return inner

            return lax.fori_loop(0, width // BLOCK, block, carry)

        lax.fori_loop(0, ranks, weights, 0)


def fixed(shape):
    return pl.BlockSpec(shape, lambda step: (0,) * len(shape))


def cost(flops, moved, raised=0):
    return pl.CostEstimate(flops=int(flops), bytes_accessed=int(moved), transcendentals=int(raised))


def group_spec(shape):
    return pl.BlockSpec((shape[0], 1, shape[2], shape[3]), lambda step: (0, step, 0, 0))


def rank_spec(shape):
    return pl.BlockSpec((shape[0], shape[1], 1) + shape[3:], lambda step: (0, 0, step, 0, 0))


def attention_forward(weight, stream, mod, bias, bias_out, stride, jobs=(), collective_id=None):
    shape = stream.shape
    width = shape[-1]
    ranks = bias.shape[0]
    tokens = shape[0] * shape[1] * shape[2]
    spec = group_spec(shape)
    low = jax.ShapeDtypeStruct(shape, jnp.bfloat16)
    wide = jax.ShapeDtypeStruct(shape, jnp.float32)
    project = jax.ShapeDtypeStruct((ranks,) + shape[:3] + (5 * PAIR,), jnp.bfloat16)
    mixed = jax.ShapeDtypeStruct((ranks,) + shape[:3] + (2 * PAIR,), jnp.bfloat16)
    return call(
        partial(attention_forward_kernel, stride),
        shape[1],
        [weight, stream, mod, bias, bias_out],
        anywhere(1) + [spec, fixed(mod.shape), fixed(bias.shape), fixed(bias_out.shape)],
        [project, mixed, low, wide],
        [rank_spec(project.shape), rank_spec(mixed.shape), spec, spec],
        [pltpu.VMEM((ranks, width, 6 * PAIR), jnp.bfloat16), pltpu.SemaphoreType.DMA((ranks,))],
        jobs,
        collective_id,
        cost(8 * tokens * width * width * 1.5, tokens * width * 16),
        "attention_forward",
    )


def ffn_weights_scratch(ranks, width, part):
    return [
        pltpu.VMEM((ranks, width, part), jnp.bfloat16),
        pltpu.VMEM((ranks, width, part), jnp.bfloat16),
        pltpu.SemaphoreType.DMA((ranks,)),
        pltpu.SemaphoreType.DMA((ranks,)),
    ]


def ffn_forward(up, down, middle, mod, bias_down, bias_up, stream=None, jobs=(), collective_id=None):
    tokens, width = middle.shape
    ranks, _, part = bias_up.shape
    chunk = tokens // SPLIT
    block = pl.BlockSpec((chunk, width), lambda step: (step, 0))
    result = [jax.ShapeDtypeStruct((tokens, width), jnp.bfloat16)] if stream is None else []
    return call(
        partial(ffn_forward_kernel, stream),
        SPLIT,
        [up, down, middle, mod, bias_down, bias_up],
        anywhere(2) + [block, fixed(mod.shape), fixed(bias_down.shape), fixed(bias_up.shape)],
        [
            jax.ShapeDtypeStruct((ranks, tokens, part), jnp.bfloat16),
            jax.ShapeDtypeStruct((tokens, width), jnp.bfloat16),
        ] + result,
        [pl.BlockSpec((ranks, chunk, part), lambda step: (0, step, 0)), block] + [block] * len(result),
        ffn_weights_scratch(ranks, width, part),
        ([] if stream is None else [stream]) + list(jobs),
        collective_id,
        cost(4.8 * tokens * width * ranks * part, tokens * width * 14, tokens * ranks * part),
        "ffn_forward",
    )


def ffn_backward(up, down, grad, middle, branch, hidden, mod, jobs=(), collective_id=None):
    tokens, width = middle.shape
    ranks, _, part = hidden.shape
    whole = fixed((tokens, width))
    return call(
        partial(ffn_backward_kernel, SPLIT),
        ranks,
        [up, down, grad, middle, branch, hidden, mod],
        anywhere(2) + [
            fixed(grad.shape), whole, whole,
            pl.BlockSpec((1, tokens, part), lambda step: (step, 0, 0)),
            fixed(mod.shape),
        ],
        [
            jax.ShapeDtypeStruct((tokens, width), jnp.float32),
            jax.ShapeDtypeStruct((2, ranks, width, part), jnp.bfloat16),
            jax.ShapeDtypeStruct((ranks, 1, part), jnp.float32),
            jax.ShapeDtypeStruct((4, width), jnp.float32),
        ],
        [
            whole,
            pl.BlockSpec((2, 1, width, part), lambda step: (0, step, 0, 0)),
            pl.BlockSpec((1, 1, part), lambda step: (step, 0, 0)),
            fixed((4, width)),
        ],
        ffn_weights_scratch(ranks, width, part) + [
            pltpu.VMEM((tokens, width), jnp.bfloat16),
            pltpu.VMEM((tokens, width), jnp.bfloat16),
            pltpu.VMEM((tokens, part), jnp.bfloat16),
            pltpu.VMEM((tokens, part), jnp.bfloat16),
            pltpu.VMEM((tokens, width), jnp.float32),
        ],
        jobs,
        collective_id,
        cost(9.6 * tokens * width * ranks * part, tokens * width * 20, tokens * ranks * part),
        "ffn_backward",
    )


def attention_backward(weight, grad, stream, saved, mod, stride, swap=None, jobs=(), collective_id=None):
    project, mixed, branch = saved
    shape = stream.shape
    width = shape[-1]
    ranks = project.shape[0]
    tokens = shape[0] * shape[1] * shape[2]
    spec = group_spec(shape)
    result = [jax.ShapeDtypeStruct(shape, jnp.float32)] if swap is None else []
    return call(
        partial(attention_backward_kernel, stride, swap),
        shape[1],
        [weight, grad, stream, project, mixed, branch, mod],
        anywhere(1) + [
            spec, spec, rank_spec(project.shape), rank_spec(mixed.shape), spec, fixed(mod.shape),
        ],
        result + [
            jax.ShapeDtypeStruct((ranks, width, 6 * PAIR), jnp.bfloat16),
            jax.ShapeDtypeStruct((4, width), jnp.float32),
            jax.ShapeDtypeStruct((ranks, 5 * PAIR), jnp.float32),
        ],
        [spec] * len(result) + [
            fixed((ranks, width, 6 * PAIR)), fixed((4, width)), fixed((ranks, 5 * PAIR)),
        ],
        [
            pltpu.VMEM((ranks, width, 6 * PAIR), jnp.bfloat16),
            pltpu.SemaphoreType.DMA((ranks,)),
            pltpu.VMEM((2, tokens, width), jnp.bfloat16),
            pltpu.VMEM((ranks, tokens, 5 * PAIR), jnp.bfloat16),
            pltpu.VMEM((ranks, tokens, 2 * PAIR), jnp.bfloat16),
        ],
        ([] if swap is None else [swap]) + list(jobs),
        collective_id,
        cost(16 * tokens * width * width * 1.5, tokens * width * 20),
        "attention_backward",
    )


def pack_heads(block):
    query, key, value, outer = block
    return jnp.concatenate(
        [query[:, :PAIR], key[:, :PAIR], value[:, :PAIR], query[:, PAIR:], key[:, PAIR:],
         value[:, PAIR:], outer[:, PAIR:], outer[:, :PAIR]], axis=1
    )


def unpack_heads(packed):
    part = lambda start, size: packed[:, start : start + size]
    join = lambda first, last: jnp.concatenate([part(first, PAIR), part(last, HD)], axis=1)
    return jnp.stack(
        [join(0, 3 * PAIR), join(PAIR, 3 * PAIR + HD), join(2 * PAIR, 4 * PAIR), join(5 * PAIR, 4 * PAIR + HD)]
    )


def pack_bias(query, value, ranks):
    query, value = query.reshape(ranks, -1), value.reshape(ranks, -1)
    none = jnp.zeros((ranks, PAIR), query.dtype)
    return jnp.concatenate(
        [query[:, :PAIR], none, value[:, :PAIR], query[:, PAIR:], none[:, :HD], value[:, PAIR:], none[:, :HD]],
        axis=1,
    )[:, None]


def unpack_bias(sums):
    query = jnp.concatenate([sums[:, :PAIR], sums[:, 3 * PAIR : 3 * PAIR + HD]], axis=1)
    value = jnp.concatenate([sums[:, 2 * PAIR : 3 * PAIR], sums[:, 4 * PAIR : 4 * PAIR + HD]], axis=1)
    return query.reshape(-1), value.reshape(-1)


def place():
    return lax.axis_index("dp"), lax.axis_index("tensor"), lax.axis_size("dp"), lax.axis_size("tensor")


def greet_all():
    device, rank, dp, tp = place()
    me, count = device * tp + rank, dp * tp
    barrier = pltpu.get_barrier_semaphore()

    def greet(index, carry):
        peer = lax.rem(me + index, count)
        pl.semaphore_signal(
            barrier, inc=1, device_id=(peer // tp, lax.rem(peer, tp)), device_id_type=pl.DeviceIdType.MESH
        )
        return carry

    lax.fori_loop(1, count, greet, 0)
    pl.semaphore_wait(barrier, count - 1)


def push(source, target, send, receive, device, rank):
    pltpu.make_async_remote_copy(
        src_ref=source, dst_ref=target, send_sem=send, recv_sem=receive,
        device_id=(device, rank), device_id_type=pl.DeviceIdType.MESH,
    ).start()


def wait_bytes(ref, semaphore):
    pltpu.make_async_copy(ref, ref, semaphore).wait()


CHAIN_SLOTS = 7


class Where:
    def __init__(self):
        device, rank = lax.axis_index("dp"), lax.axis_index("tensor")
        self.count = lax.axis_size("dp") // 2
        self.device, self.rank = device, rank
        self.far, self.side = device // 2, lax.rem(device, 2)
        self.row, self.core = rank // 2, lax.rem(rank, 2)
        self.other_side = self.far * 2 + 1 - self.side
        self.other_row = (1 - self.row) * 2 + self.core
        self.other_core = self.row * 2 + 1 - self.core

    def ahead(self, step):
        return lax.rem(self.far + step, self.count)

    def line(self, step):
        return self.ahead(step) * 2 + self.side


def greet_neighbours(here):
    barrier = pltpu.get_barrier_semaphore()
    peers = [(here.other_side, here.rank), (here.device, here.other_row), (here.device, here.other_core)]
    peers += [(here.line(step), here.rank) for step in range(1, here.count)]
    for peer in peers:
        pl.semaphore_signal(barrier, inc=1, device_id=peer, device_id_type=pl.DeviceIdType.MESH)
    pl.semaphore_wait(barrier, len(peers))


def add_into(target, left, right):
    target[...] = (left[...].astype(jnp.float32) + right[...].astype(jnp.float32)).astype(target.dtype)


class ScatterChain:
    def __init__(self, here, source, out, scratch):
        self.here, self.source, self.out = here, source, out
        (self.keep, self.land_core, self.first_one, self.last_one, self.first_two, self.last_two,
         self.line, self.land_line, self.semaphores) = scratch
        self.rows = self.land_line.shape[1]
        self.half = here.count // 2

    @staticmethod
    def scratch(width, columns, dp):
        rows, far = width // dp, dp // 2
        half = far // 2
        low = lambda *shape: pltpu.VMEM(shape + (columns,), jnp.bfloat16)
        return [
            low(2, width), low(2, width),
            low(2, half, rows), low(2 * half * rows), low(half, rows), low(half, rows),
            low(far, rows), low(far - 1, rows),
            pltpu.SemaphoreType.DMA((CHAIN_SLOTS, 2)),
        ]

    def chunk(self, row, far, side):
        return self.keep.at[row, pl.ds(pl.multiple_of((far * 2 + side) * self.rows, self.rows), self.rows)]

    def send(self, slot, source, target, device, rank):
        push(source, target, self.semaphores.at[slot, 0], self.semaphores.at[slot, 1], device, rank)

    def arrived(self, slot, ref):
        wait_bytes(ref, self.semaphores.at[slot, 1])

    def left(self, slot, ref):
        wait_bytes(ref, self.semaphores.at[slot, 0])

    def stage_core(self):
        here = self.here
        for row in range(2):
            pltpu.make_async_copy(
                self.source.at[row * 2 + here.core], self.keep.at[row], self.semaphores.at[6, 0]
            ).start()
            self.send(0, self.source.at[row * 2 + 1 - here.core], self.land_core.at[row], here.device, here.other_core)

    def stage_one(self):
        here = self.here
        wait_bytes(self.keep, self.semaphores.at[6, 0])
        self.arrived(0, self.land_core)

        def one(index, carry):
            rows = pl.ds(pl.multiple_of(index * self.rows, self.rows), self.rows)
            for row in range(2):
                add_into(self.keep.at[row, rows], self.keep.at[row, rows], self.land_core.at[row, rows])
            return carry

        lax.fori_loop(0, here.count * 2, one, 0)
        start = self.half * 2 * self.rows
        for row in range(2):
            for far in range(self.half):
                self.send(
                    1, self.chunk(row, far, 1 - here.side), self.first_one.at[row, far], here.other_side, here.rank
                )
        self.send(
            2, self.keep.at[1 - here.row, pl.ds(start, start)], self.last_one, here.device, here.other_row
        )

    def stage_two(self):
        here = self.here
        self.arrived(1, self.first_one)
        for row in range(2):
            for far in range(self.half):
                mine = self.chunk(row, far, here.side)
                add_into(mine, mine, self.first_one.at[row, far])
        for far in range(self.half):
            self.send(3, self.chunk(1 - here.row, far, here.side), self.first_two.at[far], here.device, here.other_row)
        self.arrived(2, self.last_one)
        for far in range(self.half):
            for side in range(2):
                mine = self.chunk(here.row, self.half + far, side)
                add_into(mine, mine, self.last_one.at[pl.ds((far * 2 + side) * self.rows, self.rows)])
        for far in range(self.half):
            self.send(
                4, self.chunk(here.row, self.half + far, 1 - here.side), self.last_two.at[far],
                here.other_side, here.rank,
            )

    def stage_line(self):
        here = self.here
        self.arrived(3, self.first_two)
        self.arrived(4, self.last_two)
        for far in range(here.count):
            land = self.first_two.at[far] if far < self.half else self.last_two.at[far - self.half]
            add_into(self.line.at[far], self.chunk(here.row, far, here.side), land)
        for step in range(1, here.count):
            self.send(5, self.line.at[here.ahead(step)], self.land_line.at[step - 1], here.line(step), here.rank)

    def finish(self):
        self.arrived(5, self.land_line)
        total = self.line[self.here.far].astype(jnp.float32)
        for step in range(1, self.here.count):
            total = total + self.land_line[step - 1].astype(jnp.float32)
        self.out[...] = total
        self.left(0, self.land_core)
        self.left(1, self.first_one)
        self.left(2, self.last_one)
        self.left(3, self.first_two)
        self.left(4, self.last_two)
        self.left(5, self.land_line)


def leave_kernel(mod_start, *refs):
    refs = list(refs)
    scattering = len(refs) > 10
    source = refs.pop(0) if scattering else None
    small_ref, modulation_ref, *refs = refs
    out = refs.pop(0) if scattering else None
    sum_ref, act_ref, land_ref, acting_ref, semaphores, *space = refs
    device, rank, dp, tp = place()
    me, count = device * tp + rank, dp * tp
    greet_all()
    if scattering:
        chain = ScatterChain(Where(), source, out, space)
        chain.stage_core()
    for step in range(1, tp):
        there = lax.rem(rank + step, tp)
        push(small_ref.at[there], land_ref.at[rank], semaphores.at[0], semaphores.at[1], device, there)
    land_ref[rank] = small_ref[rank]
    wait_bytes(land_ref.at[pl.ds(0, tp - 1)], semaphores.at[1])
    mine = sum_ref.at[rank]
    mine[device] = jnp.sum(land_ref[...], axis=0)

    def one(step, carry):
        push(mine.at[device], mine.at[device], semaphores.at[2], semaphores.at[3], lax.rem(device + step, dp), rank)
        return carry

    lax.fori_loop(1, dp, one, 0)
    if scattering:
        chain.stage_one()
    wait_bytes(mine.at[pl.ds(0, dp - 1)], semaphores.at[3])
    for step in range(1, tp):
        push(mine, mine, semaphores.at[4], semaphores.at[5], device, lax.rem(rank + step, tp))
    wait_bytes(sum_ref.at[pl.ds(0, tp - 1)], semaphores.at[5])
    layers, padded, columns = modulation_ref.shape
    lines = sum_ref.shape[2]
    total = jnp.zeros((dp, padded), jnp.float32)
    for layer in range(layers):
        for index in range(columns // PAIR):
            line = layer * (tp * lines // layers) + mod_start // PAIR + index
            low = sum_ref[line // lines, :, line % lines, :].astype(jnp.bfloat16)
            total += mm(low, modulation_ref[layer, :, index * PAIR : (index + 1) * PAIR], ((1,), (1,)))
    acting_ref[...] = jnp.concatenate([total, jnp.zeros((dp, PAIR - padded), jnp.float32)], axis=1)
    act_ref[me] = acting_ref[...]

    def tell(index, carry):
        peer = lax.rem(me + index, count)
        push(acting_ref, act_ref.at[me], semaphores.at[6], semaphores.at[7], peer // tp, lax.rem(peer, tp))
        return carry

    lax.fori_loop(1, count, tell, 0)
    if scattering:
        chain.stage_two()
        chain.stage_line()
    wait_bytes(act_ref.at[pl.ds(0, count - 1)], semaphores.at[7])
    wait_bytes(act_ref.at[pl.ds(0, count - 1)], semaphores.at[6])
    wait_bytes(land_ref.at[pl.ds(0, tp - 1)], semaphores.at[0])
    wait_bytes(mine.at[pl.ds(0, dp - 1)], semaphores.at[2])
    wait_bytes(sum_ref.at[pl.ds(0, tp - 1)], semaphores.at[4])
    if scattering:
        chain.finish()


def leave(small, modulation, mod_start, grads, collective_id):
    tp, lines, lanes = small.shape
    dp = lax.axis_size("dp")
    inside = pl.BlockSpec(memory_space=pltpu.VMEM)
    shapes, space = [], []
    if grads is not None:
        _, width, columns = grads.shape
        shapes = [jax.ShapeDtypeStruct((width // dp, columns), jnp.float32)]
        space = ScatterChain.scratch(width, columns, dp)
    return pl.pallas_call(
        partial(leave_kernel, mod_start),
        in_specs=[pl.BlockSpec(memory_space=pl.ANY)] * len(shapes) + [inside, inside],
        out_specs=[inside] * (len(shapes) + 2),
        out_shape=shapes + [
            jax.ShapeDtypeStruct((tp, dp, lines, lanes), jnp.float32),
            jax.ShapeDtypeStruct((dp * tp, dp, lanes), jnp.float32),
        ],
        scratch_shapes=[
            pltpu.VMEM((tp, lines, lanes), jnp.float32),
            pltpu.VMEM((dp, lanes), jnp.float32),
            pltpu.SemaphoreType.DMA((8,)),
        ] + space,
        compiler_params=pltpu.CompilerParams(
            collective_id=collective_id, has_side_effects=True, vmem_limit_bytes=VMEM_LIMIT
        ),
        name="leave",
    )(*([] if grads is None else [grads]), small, modulation)


class GatherChain:
    def __init__(self, here, source, out, semaphores):
        self.here, self.source, self.out, self.semaphores = here, source, out, semaphores
        self.rows = out.shape[1] // (2 * here.count)
        self.half = here.count // 2

    @staticmethod
    def scratch():
        return [pltpu.SemaphoreType.DMA((9, 2))]

    def piece(self, rank, far, side):
        rows = pl.ds(pl.multiple_of((far * 2 + side) * self.rows, self.rows), self.rows)
        return self.out.at[rank, rows]

    def send(self, slot, source, target, device, rank):
        push(source, target, self.semaphores.at[slot, 0], self.semaphores.at[slot, 1], device, rank)

    def wait(self, slot, way, pieces):
        wait_bytes(self.out.at[0, pl.ds(0, pieces * self.rows)], self.semaphores.at[slot, way])

    def stage_line(self):
        here = self.here
        mine = self.piece(here.rank, here.far, here.side)
        pltpu.make_async_copy(self.source, mine, self.semaphores.at[8, 0]).start()
        for step in range(1, here.count):
            self.send(0, self.source, mine, here.line(step), here.rank)

    def line_arrived(self):
        self.wait(8, 0, 1)
        self.wait(0, 1, self.here.count - 1)

    def line_left(self):
        self.wait(0, 0, self.here.count - 1)

    def stage_near(self):
        here = self.here
        for far in range(here.count):
            mine = self.piece(here.rank, far, here.side)
            self.send(1, mine, mine, here.other_side, here.rank)
            self.send(2, mine, mine, here.device, here.other_row)
        for far in range(here.count):
            mine = self.piece(here.rank, far, here.side)
            self.send(3, mine, mine, here.device, here.other_core)

    def stage_across(self):
        here, count = self.here, self.here.count
        self.wait(1, 1, count)
        for far in range(self.half):
            other = self.piece(here.rank, far, 1 - here.side)
            self.send(4, other, other, here.device, here.other_row)
        self.wait(2, 1, count)
        for far in range(self.half, count):
            other = self.piece(here.other_row, far, here.side)
            self.send(5, other, other, here.other_side, here.rank)
        for far in range(count):
            for other in (self.piece(here.rank, far, 1 - here.side), self.piece(here.other_row, far, here.side)):
                self.send(6, other, other, here.device, here.other_core)

    def stage_core(self):
        here, count = self.here, self.here.count
        self.wait(4, 1, self.half)
        self.wait(5, 1, count - self.half)
        for far in range(count):
            other = self.piece(here.other_row, far, 1 - here.side)
            self.send(7, other, other, here.device, here.other_core)

    def finish(self):
        count, half = self.here.count, self.half
        self.wait(3, 1, count)
        self.wait(6, 1, 2 * count)
        self.wait(7, 1, count)
        for slot, pieces in ((1, count), (2, count), (3, count), (4, half), (5, count - half), (6, 2 * count), (7, count)):
            self.wait(slot, 0, pieces)


class Job:
    operands, shapes, specs, aliases, space = (), (), (), {}, ()
    stages, last = {}, ()


def anywhere(count):
    return [pl.BlockSpec(memory_space=pl.ANY)] * count


class ScatterJob(Job):
    def __init__(self, grads):
        kinds, _, width, columns = grads.shape
        dp = lax.axis_size("dp")
        shape = (kinds, width // dp, columns)
        self.operands = [grads]
        self.shapes, self.specs = [jax.ShapeDtypeStruct(shape, jnp.float32)], [fixed(shape)]
        self.space = ScatterChain.scratch(width, columns, dp) * kinds

    def bind(self, here, inputs, outputs, space):
        size = len(space) // outputs[0].shape[0]
        chains = [
            ScatterChain(here, inputs[0].at[kind], outputs[0].at[kind], space[kind * size : (kind + 1) * size])
            for kind in range(outputs[0].shape[0])
        ]
        one = chains[0]
        if len(chains) == 1:
            self.stages = {
                (0, 0): [one.stage_core], (0, 3): [one.stage_one], (2, 0): [one.stage_two], (3, 0): [one.stage_line],
            }
            self.last = [one.finish]
            return
        two = chains[1]
        self.stages = {
            (0, 0): [one.stage_core, two.stage_core], (0, 2): [one.stage_one], (0, 3): [two.stage_one],
            (1, 3): [one.stage_two], (2, 3): [two.stage_two], (3, 1): [one.stage_line], (3, 3): [two.stage_line],
        }
        self.last = [one.finish, two.finish]


class FlowJob(Job):
    def __init__(self, spread, lines):
        dp, tp = lax.axis_size("dp"), lax.axis_size("tensor")
        self.spread = len(spread)
        self.operands = list(spread) + list(lines)
        self.shapes = [jax.ShapeDtypeStruct(v.shape, v.dtype) for v in spread]
        self.shapes += [jax.ShapeDtypeStruct((tp, dp * v.shape[0], v.shape[1]), v.dtype) for v in lines]
        self.specs = anywhere(len(self.shapes))
        self.aliases = {index: index for index in range(len(spread))}
        self.space = GatherChain.scratch() * len(self.shapes)

    def bind(self, here, inputs, outputs, space):
        chains = [GatherChain(here, *refs) for refs in zip(inputs, outputs, space)]
        spread, lines = chains[: self.spread], chains[self.spread :]
        self.stages = {(0, 0): [], (1, 0): [], (2, 0): [], (3, 0): []}
        self.last = []
        if lines:
            self.stages[0, 0].append(lines[0].stage_line)
        if len(lines) > 1:
            self.stages[1, 0].append(lines[1].stage_line)
        if spread:
            self.stages[0, 0].insert(0, spread[0].stage_near)
            self.stages[1, 0].insert(0, spread[0].stage_across)
            self.stages[2, 0].append(spread[0].stage_core)
        if len(spread) > 1:
            self.stages[1, 0].insert(1, spread[1].stage_near)
            self.stages[2, 0].append(spread[1].stage_across)
            self.last.append(spread[1].stage_core)
        self.last += [chain.finish for chain in spread]
        for chain in lines:
            self.last += [chain.line_arrived, chain.line_left]


class SwapJob(Job):
    def __init__(self, blocks):
        self.operands = [blocks]
        self.shapes, self.specs = [jax.ShapeDtypeStruct(blocks.shape, blocks.dtype)], anywhere(1)
        self.space = [pltpu.SemaphoreType.DMA((3,))]

    def bind(self, here, inputs, outputs, space):
        source, out, semaphores = inputs[0], outputs[0], space[0]
        ranks = out.shape[0]

        def start():
            pltpu.make_async_copy(source.at[here.rank], out.at[here.rank], semaphores.at[2]).start()
            for step in range(1, ranks):
                there = lax.rem(here.rank + step, ranks)
                push(source.at[there], out.at[here.rank], semaphores.at[0], semaphores.at[1], here.device, there)

        def finish():
            wait_bytes(out.at[0], semaphores.at[2])
            wait_bytes(out.at[pl.ds(0, ranks - 1)], semaphores.at[1])
            wait_bytes(out.at[pl.ds(0, ranks - 1)], semaphores.at[0])

        self.stages, self.last = {(0, 0): [start]}, [finish]


class StreamJob(Job):
    def __init__(self, shape, frames):
        self.shape, self.frames = shape, frames
        self.shapes, self.specs = [jax.ShapeDtypeStruct(shape, jnp.bfloat16)], anywhere(1)
        ranks, groups, rows, width = shape
        block = (groups, ranks, rows, width)
        if frames:
            block = (frames, ranks, groups, rows // frames, width)
        self.space = [pltpu.VMEM(block, jnp.bfloat16), pltpu.SemaphoreType.DMA((3,))]

    def bind(self, here, inputs, outputs, space):
        self.here, self.out = here, outputs[0]
        self.buffer, self.semaphores = space
        ranks = self.shape[0]

        def finish():
            wait_bytes(self.out.at[0], self.semaphores.at[2])
            wait_bytes(self.out.at[pl.ds(0, ranks - 1)], self.semaphores.at[1])
            wait_bytes(self.out.at[pl.ds(0, ranks - 1)], self.semaphores.at[0])

        self.stages, self.last = {}, [finish]

    def put(self, step, value):
        here, ranks = self.here, self.shape[0]
        self.buffer[step] = value.reshape(self.buffer.shape[1:]).astype(jnp.bfloat16)
        if self.frames:
            strip = self.buffer.shape[3]
            target = self.out.at[here.rank, :, pl.ds(pl.multiple_of(step * strip, strip), strip)]
        else:
            target = self.out.at[here.rank, step]
        pltpu.make_async_copy(self.buffer.at[step, here.rank], target, self.semaphores.at[2]).start()
        for ahead in range(1, ranks):
            there = lax.rem(here.rank + ahead, ranks)
            push(
                self.buffer.at[step, there], target, self.semaphores.at[0], self.semaphores.at[1],
                here.device, there,
            )


def greet_jobs(here):
    barrier = pltpu.get_barrier_semaphore()
    ranks = lax.axis_size("tensor")
    peers = [(here.other_side, here.rank)]
    peers += [(here.line(step), here.rank) for step in range(1, here.count)]
    peers += [(here.device, lax.rem(here.rank + step, ranks)) for step in range(1, ranks)]
    for peer in peers:
        pl.semaphore_signal(barrier, inc=1, device_id=peer, device_id_type=pl.DeviceIdType.MESH)
    pl.semaphore_wait(barrier, len(peers))


def call(body, steps, arguments, in_specs, out_shape, out_specs, scratch, jobs, collective_id, estimate, name):
    operands = [v for job in jobs for v in job.operands]
    shapes = [v for job in jobs for v in job.shapes]
    specs = [v for job in jobs for v in job.specs]
    space = [v for job in jobs for v in job.space]
    aliases, before, after = {}, len(arguments), len(out_shape)
    for job in jobs:
        for source, target in job.aliases.items():
            aliases[before + source] = after + target
        before, after = before + len(job.operands), after + len(job.shapes)

    def kernel(*refs):
        refs = list(refs)
        take = lambda number: [refs.pop(0) for _ in range(number)]
        inputs, job_inputs = take(len(arguments)), take(len(operands))
        outputs, job_outputs = take(len(out_shape)), take(len(shapes))
        own, job_space = take(len(scratch)), refs
        step = pl.program_id(0)
        if jobs:
            here = Where()
            for job in jobs:
                pick = lambda pool, number: [pool.pop(0) for _ in range(number)]
                job.bind(
                    here, pick(job_inputs, len(job.operands)), pick(job_outputs, len(job.shapes)),
                    pick(job_space, len(job.space)),
                )

        def hook(spot):
            for index in range(steps):
                todo = [stage for job in jobs for stage in job.stages.get((index, spot), ())]
                if todo or (jobs and spot == 0 and index == 0):

                    @pl.when(step == index)
                    def _():
                        if index == 0 and spot == 0:
                            greet_jobs(here)
                        for stage in todo:
                            stage()

        hook(0)
        body(lambda spot: hook(spot) if spot else None, *inputs, *outputs, *own)
        if jobs:

            @pl.when(step == steps - 1)
            def _():
                for job in jobs:
                    for stage in job.last:
                        stage()

    more = {"collective_id": collective_id, "has_side_effects": True} if jobs else {}
    return pl.pallas_call(
        kernel,
        grid=(steps,),
        in_specs=list(in_specs) + anywhere(len(operands)),
        out_specs=list(out_specs) + specs,
        out_shape=list(out_shape) + shapes,
        scratch_shapes=list(scratch) + space,
        input_output_aliases=aliases,
        compiler_params=pltpu.CompilerParams(
            vmem_limit_bytes=VMEM_LIMIT, dimension_semantics=("arbitrary",), **more
        ),
        cost_estimate=estimate,
        name=name,
    )(*arguments, *operands)


def entry_kernel(
    per_device, row_ref, modulation_ref, *refs
):
    gather = (len(refs) - 5) // 3
    refs = list(refs)
    sources = [refs.pop(0) for _ in range(gather)]
    gathered_ref, mod_ref = refs.pop(0), refs.pop(0)
    targets = [refs.pop(0) for _ in range(gather)]
    part_ref, land_ref, semaphores, *space = refs
    device, rank, dp, tp = place()
    me, count = device * tp + rank, dp * tp
    quarter = land_ref.shape[2]
    if gather:
        here = Where()
        whole, one, two = (GatherChain(here, *group) for group in zip(sources, targets, space))
    greet_all()

    def tell(index, carry):
        peer = lax.rem(me + index, count)
        push(
            row_ref, gathered_ref.at[me], semaphores.at[0], semaphores.at[1], peer // tp, lax.rem(peer, tp)
        )
        return carry

    lax.fori_loop(1, count, tell, 0)
    gathered_ref[me] = row_ref[...]
    if gather:
        whole.stage_line()
    wait_bytes(gathered_ref.at[pl.ds(0, count - 1)], semaphores.at[1])
    padded = modulation_ref.shape[1]
    width = dp * tp * per_device
    chosen = jnp.zeros((count, padded), jnp.float32)
    row = lax.broadcasted_iota(jnp.int32, (PAIR, padded), 0)
    column = lax.broadcasted_iota(jnp.int32, (PAIR, padded), 1)
    for index in range(width // PAIR):
        match = (row + index * PAIR == column + me * per_device) & (column < per_device)
        chosen += mm(
            gathered_ref[:, index, :].astype(jnp.bfloat16), jnp.where(match, 1.0, 0.0).astype(jnp.bfloat16)
        )
    clip = lax.broadcasted_iota(jnp.int32, (dp, count), 0)
    member = lax.broadcasted_iota(jnp.int32, (dp, count), 1)
    leaders = jnp.where(member == clip * tp, 1.0, 0.0).astype(jnp.bfloat16)
    rows = mm(leaders, chosen.astype(jnp.bfloat16)).astype(jnp.bfloat16)
    for layer in range(modulation_ref.shape[0]):
        part = mm(rows, modulation_ref[layer])
        size = part.shape[1]
        for index in range(dp):
            part_ref[index, :, layer * size : (layer + 1) * size] = part[index : index + 1]

    def share(index, carry):
        peer = lax.rem(me + index, count)
        there, lane = peer // tp, lax.rem(peer, tp)
        source = part_ref.at[there, :, pl.ds(pl.multiple_of(lane * quarter, PAIR), quarter)]
        push(source, land_ref.at[me], semaphores.at[2], semaphores.at[3], there, lane)
        return carry

    lax.fori_loop(1, count, share, 0)
    mine = pl.ds(pl.multiple_of(rank * quarter, PAIR), quarter)
    land_ref[me] = part_ref[device, :, mine]
    if gather:
        whole.line_arrived()
        whole.stage_near()
        one.stage_line()
    wait_bytes(land_ref.at[pl.ds(0, count - 1)], semaphores.at[3])
    mod_ref[:, mine] = jnp.sum(land_ref[...], axis=0)
    for step in range(1, tp):
        push(
            mod_ref.at[:, mine], mod_ref.at[:, mine], semaphores.at[4], semaphores.at[5],
            device, lax.rem(rank + step, tp),
        )
    if gather:
        whole.stage_across()
        two.stage_line()
        whole.stage_core()
    wait_bytes(gathered_ref.at[pl.ds(0, count - 1)], semaphores.at[0])
    wait_bytes(land_ref.at[pl.ds(0, count - 1)], semaphores.at[2])
    wait_bytes(mod_ref.at[:, pl.ds(0, (tp - 1) * quarter)], semaphores.at[5])
    wait_bytes(mod_ref.at[:, pl.ds(0, (tp - 1) * quarter)], semaphores.at[4])
    if gather:
        for chain in (one, two):
            chain.line_arrived()
        whole.finish()
        for chain in (whole, one, two):
            chain.line_left()


def enter(row, modulation, per_device, weights, collective_id):
    dp, tp = lax.axis_size("dp"), lax.axis_size("tensor")
    count = dp * tp
    whole = modulation.shape[0] * modulation.shape[2]
    inside = pl.BlockSpec(memory_space=pltpu.VMEM)
    job = FlowJob((), weights) if weights else Job()
    return pl.pallas_call(
        partial(entry_kernel, per_device),
        in_specs=[inside, inside] + anywhere(len(job.operands)),
        out_specs=[inside, inside] + list(job.specs),
        out_shape=[
            jax.ShapeDtypeStruct((count,) + row.shape, jnp.float32),
            jax.ShapeDtypeStruct((1, whole), jnp.float32),
        ] + list(job.shapes),
        scratch_shapes=[
            pltpu.VMEM((dp, 1, whole), jnp.float32),
            pltpu.VMEM((count, 1, whole // tp), jnp.float32),
            pltpu.SemaphoreType.DMA((6,)),
        ] + list(job.space),
        compiler_params=pltpu.CompilerParams(
            collective_id=collective_id, has_side_effects=True, vmem_limit_bytes=VMEM_LIMIT
        ),
        name="enter",
    )(row, modulation, *job.operands)


def adam_update(weight, first, second, grad, rate, decay):
    first_new = BETA_ONE * first + (1.0 - BETA_ONE) * grad
    second_new = BETA_TWO * second + (1.0 - BETA_TWO) * grad * grad
    corrected = (
        first_new
        / (1.0 - BETA_ONE**STEP)
        / (jnp.sqrt(second_new / (1.0 - BETA_TWO**STEP)) + ADAM_EPS)
    )
    weight_new = weight - rate * (corrected + decay * weight)
    return (weight_new, first_new, second_new, weight_new.astype(jnp.bfloat16))


def dot32(form, left, right):
    return jnp.einsum(form, left, right, preferred_element_type=jnp.float32)


def exchange(blocks):
    return lax.all_to_all(blocks, "tensor", split_axis=0, concat_axis=0, tiled=True)


def gather_plain(shard):
    rows, width = shard.shape
    whole = lax.all_gather(shard, ("tensor", "dp"), axis=0, tiled=True)
    return whole.reshape(-1, lax.axis_size("dp") * rows, width)


def scatter_plain(grads):
    kinds, ranks, width, cols = grads.shape
    flat = grads.reshape(kinds, ranks * width, cols)
    summed = lax.psum_scatter(flat, ("tensor", "dp"), scatter_dimension=1, tiled=True)
    return summed.astype(jnp.float32)


def per_device(
    clips, cotangent, timesteps, labels, time_table, class_table,
    attention_weights, attention_first, attention_second,
    ffn_weights, ffn_first, ffn_second,
    modulation_weights, modulation_first, modulation_second,
    bias_vectors, bias_first, bias_second,
):
    layers, kinds, rows, cols = attention_weights.shape
    _, frames, patches, width = clips.shape
    mod_rows = modulation_weights.shape[1]
    bias_cols = bias_vectors.shape[1]
    dp, tp = lax.axis_size("dp"), lax.axis_size("tensor")
    position = lax.axis_index("dp") * tp + lax.axis_index("tensor")
    tokens = frames * patches
    strip = patches // (tp * frames)
    blocks = (tp, frames, frames * strip, width)
    pieces = (tp * frames, frames, strip, width)

    embed = time_table[timesteps] + class_table[labels]
    cond_act = jax.nn.silu(embed).astype(jnp.bfloat16)
    fused = rows % 16 == 0
    shards = [
        (
            pack_heads(attention_weights[layer].astype(jnp.bfloat16)),
            ffn_weights[layer, 0].astype(jnp.bfloat16),
            ffn_weights[layer, 1].astype(jnp.bfloat16),
        )
        for layer in range(layers)
    ]
    low = bias_vectors.astype(jnp.bfloat16).reshape(-1)
    row = jnp.concatenate([cond_act[0], low]).astype(jnp.float32)
    row = jnp.pad(row, (0, -row.shape[0] % 1024)).reshape(-1, 128)
    modulation_low = modulation_weights.astype(jnp.bfloat16)
    modulation_low = jnp.pad(modulation_low, ((0, 0), (0, -mod_rows % 32), (0, 0)))
    gathered, mod, *begun = enter(row, modulation_low, mod_rows, shards[0] if fused else None, 0)
    gathered = gathered.reshape(dp * tp, -1)
    cond_all = gathered[::tp, :width].astype(jnp.bfloat16)
    bias_low = gathered[:, width : width + layers * bias_cols].reshape(dp * tp, layers, bias_cols)
    bias_low = bias_low.transpose(1, 0, 2).reshape(layers, -1)
    cond_rows = lax.dynamic_slice_in_dim(cond_all, position * mod_rows, mod_rows, axis=1)
    cond_rows = jnp.pad(cond_rows, ((0, 0), (0, -mod_rows % 32)))
    mod = mod.reshape(layers, -1)
    mod_width = mod.shape[-1]
    mod = (mod + bias_low[:, -mod_width:]).reshape(layers, 6, width)
    hidden_width = bias_low.shape[1] - mod_width - 4 * width
    bias_up = bias_low[:, 3 * width : 3 * width + hidden_width].reshape(layers, tp, 1, -1)
    bias_out = bias_low[:, None, 2 * width : 3 * width]
    bias_down = bias_low[:, None, 3 * width + hidden_width : 4 * width + hidden_width]
    bias_project = [
        pack_bias(bias_low[layer, :width], bias_low[layer, width : 2 * width], tp) for layer in range(layers)
    ]

    by_patch = lambda v: v.reshape(frames, tp * frames, strip, width).transpose(1, 0, 2, 3)
    cot = by_patch(cotangent[0]).reshape(blocks)
    first = clips[0].reshape(1, frames, patches, width)

    attend = lambda layer, weight, stream, stride, *more: attention_forward(
        weight, stream, mod[layer], bias_project[layer], bias_out[layer], stride, *more
    )
    expand = lambda layer, up, down, middle, *more: ffn_forward(
        up, down, middle.reshape(tokens, width), mod[layer], bias_down[layer], bias_up[layer], *more
    )
    if fused:
        packed_b, up_b, down_b = shards[1]
        attention_a, up_a, down_a = begun
        *heads_a, middle_a, up_a, down_a, attention_b, up_b = attend(
            0, attention_a, first, 0, [FlowJob([up_a, down_a], [packed_b, up_b])], 1
        )
        hidden_a, pushed_a, second, attention_b, up_b, down_b = expand(
            0, up_a, down_a, middle_a, StreamJob(blocks, frames), [FlowJob([attention_b, up_b], [down_b])], 2
        )
        *heads_b, middle_b, down_b = attend(1, attention_b, second, strip, [FlowJob([down_b], [])], 3)
        hidden_b, pushed_b, result, cot = expand(1, up_b, down_b, middle_b, None, [SwapJob(cot)], 4)
    else:
        (attention_a, up_a, down_a), (attention_b, up_b, down_b) = [[gather_plain(v) for v in group] for group in shards]
        *heads_a, middle_a = attend(0, attention_a, first, 0)
        hidden_a, pushed_a, second = expand(0, up_a, down_a, middle_a)
        second = exchange(by_patch(second).reshape(blocks))
        *heads_b, middle_b = attend(1, attention_b, second, strip)
        hidden_b, pushed_b, result = expand(1, up_b, down_b, middle_b)
        cot = exchange(cot)
    middle_a, middle_b = middle_a.reshape(tokens, width), middle_b.reshape(tokens, width)
    result = result.reshape(blocks)
    cot = cot.reshape(tokens, width)

    if fused:
        grad, ffn_grad, *sums_b, result = ffn_backward(
            up_b, down_b, cot, middle_b, pushed_b, hidden_b, mod[1], [SwapJob(result)], 5
        )
        packed_b, *more_b, grad, done_ffn_b = attention_backward(
            attention_b, grad.reshape(blocks), second, heads_b, mod[1], strip,
            StreamJob(blocks, 0), [ScatterJob(ffn_grad)], 6,
        )
        grad, ffn_grad, *sums_a, done_b = ffn_backward(
            up_a, down_a, grad.reshape(pieces), middle_a, pushed_a, hidden_a, mod[0], [ScatterJob(packed_b[None])], 7
        )
        grad, packed_a, *more_a, done_ffn_a = attention_backward(
            attention_a, grad.reshape(first.shape), first, heads_a, mod[0], 0, None, [ScatterJob(ffn_grad)], 8
        )
    else:
        result = exchange(result)
        grad, ffn_grad, *sums_b = ffn_backward(up_b, down_b, cot, middle_b, pushed_b, hidden_b, mod[1])
        done_ffn_b = scatter_plain(ffn_grad)
        grad, packed_b, *more_b = attention_backward(
            attention_b, grad.reshape(blocks), second, heads_b, mod[1], strip
        )
        done_b = scatter_plain(packed_b[None])
        grad = exchange(grad.astype(jnp.bfloat16))
        grad, ffn_grad, *sums_a = ffn_backward(up_a, down_a, grad.reshape(pieces), middle_a, pushed_a, hidden_a, mod[0])
        done_ffn_a = scatter_plain(ffn_grad)
        grad, packed_a, *more_a = attention_backward(attention_a, grad.reshape(first.shape), first, heads_a, mod[0], 0)
        done_a = scatter_plain(packed_a[None])
    output = result.reshape(pieces).transpose(1, 0, 2, 3).reshape(clips.shape)
    input_grad = grad.reshape(clips.shape)

    def gather_small(more, sums):
        attention_sums, project_sum = more
        up_sum, low_sums = sums
        return jnp.concatenate(
            [*unpack_bias(project_sum), attention_sums[0], up_sum.reshape(-1), low_sums[0],
             attention_sums[1:].reshape(-1), low_sums[1:].reshape(-1)]
        )

    small = jnp.stack([gather_small(more_a, sums_a), gather_small(more_b, sums_b)])
    token_width = small.shape[1] - mod_width
    *done, small, grad_act = leave(
        small.reshape(tp, -1, 128), modulation_low, token_width, packed_a if fused else None, 9
    )
    if fused:
        done_a = done[0][None]
    small = small.transpose(1, 0, 2, 3).reshape(dp, layers, -1)
    grad_mod_low = small[..., token_width:].astype(jnp.bfloat16)
    grad_bias_all = jnp.concatenate(
        [small[..., :token_width], grad_mod_low.astype(jnp.float32)], axis=-1
    ).sum(axis=0)
    grad_bias = lax.dynamic_slice_in_dim(grad_bias_all, position * bias_cols, bias_cols, axis=1)
    grad_mod_weight = dot32("ck,cle->lke", cond_rows, grad_mod_low)[:, :mod_rows]
    grad_act = lax.dynamic_index_in_dim(
        grad_act[:, :, :mod_rows], lax.axis_index("dp"), axis=1, keepdims=False
    )
    grad_attention = jnp.stack([unpack_heads(done_a[0]), unpack_heads(done_b[0])])
    grad_ffn = jnp.stack([done_ffn_a, done_ffn_b])
    silu_value, silu_pull = jax.vjp(jax.nn.silu, embed)
    cond_grad = silu_pull(grad_act.reshape(1, width))[0]

    return (output, input_grad, cond_grad) + (
        adam_update(attention_weights, attention_first, attention_second, grad_attention, MATRIX_RATE, MATRIX_DECAY)
        + adam_update(ffn_weights, ffn_first, ffn_second, grad_ffn, MATRIX_RATE, MATRIX_DECAY)
        + adam_update(modulation_weights, modulation_first, modulation_second, grad_mod_weight, MATRIX_RATE, MATRIX_DECAY)
        + adam_update(bias_vectors, bias_first, bias_second, grad_bias, VECTOR_RATE, 0.0)
    )


def solution(mesh):
    tokens = P("dp", "tensor", None, None)
    matrix = P(None, None, "dp", "tensor")
    modulation = P(None, BOTH, None)
    vector = P(None, BOTH)
    return jax.shard_map(
        per_device,
        mesh=mesh,
        in_specs=(tokens, tokens, P("dp"), P("dp"), P(), P())
        + (matrix,) * 6 + (modulation,) * 3 + (vector,) * 3,
        out_specs=(tokens, tokens, P("dp", None)) + (matrix,) * 8 + (modulation,) * 4 + (vector,) * 4,
        check_vma=False,
    )
```

```python
from functools import partial

import jax
import jax.numpy as jnp
from jax import lax
from jax.experimental import pallas as pl
from jax.experimental.pallas import tpu as pltpu
from jax.sharding import PartitionSpec as P

HD = 64
PAIR = 128
BLOCK = 256
SPLIT = 4
PARTS = 3
STEP = 10
BETA_ONE = 0.9
BETA_TWO = 0.999
ADAM_EPS = 1e-08
MATRIX_RATE = 0.04
VECTOR_RATE = 0.2
MATRIX_DECAY = 0.1
NORM_EPS = 1e-06
GELU_A = (2.0 / 3.141592653589793) ** 0.5
GELU_B = 0.044715
BLOCKED = -1e30
VMEM_LIMIT = 60 * 1024 * 1024
BOTH = ("dp", "tensor")


def mm(left, right, dims=((1,), (0,))):
    return lax.dot_general(left, right, (dims, ((), ())), preferred_element_type=jnp.float32)


def norm_parts(value):
    average = jnp.mean(value, axis=-1, keepdims=True)
    centred = value - average
    spread = jnp.mean(centred * centred, axis=-1, keepdims=True)
    inverse = lax.rsqrt(spread + NORM_EPS)
    return centred * inverse, inverse


def norm_back(grad, shape, inverse):
    first = jnp.mean(grad, axis=-1, keepdims=True)
    second = jnp.mean(grad * shape, axis=-1, keepdims=True)
    return inverse * (grad - first - shape * second)


def rows_of(ref):
    value = ref[...]
    return value.reshape(-1, value.shape[-1])


def put(ref, value):
    ref[...] = value.reshape(ref.shape).astype(ref.dtype)


def add_rows(ref, index, value):
    ref[pl.ds(index, 1), :] += jnp.sum(value, axis=0, keepdims=True)


def half_masks(rows):
    lane = lax.broadcasted_iota(jnp.int32, (rows, PAIR), 1)
    return lane < HD


def same_patch(tokens, stride):
    row = lax.broadcasted_iota(jnp.int32, (tokens, tokens), 0)
    column = lax.broadcasted_iota(jnp.int32, (tokens, tokens), 1)
    return lax.rem(row, stride) == lax.rem(column, stride)


def swap_halves(value):
    return pltpu.roll(value, HD, 1)


def start_loads(source, target, semaphores):
    for rank in range(target.shape[0]):
        pltpu.make_async_copy(source.at[rank], target.at[rank], semaphores.at[rank]).start()


def wait_loads(target, semaphores, rank):
    pltpu.make_async_copy(target.at[rank], target.at[rank], semaphores.at[rank]).wait()


def softmax_rows(scores, axis):
    raised = jnp.exp(scores - jnp.max(scores, axis=axis, keepdims=True))
    return raised * (1.0 / jnp.sum(raised, axis=axis, keepdims=True))


def attention_forward_kernel(
    stride, hook, source, stream_ref, mod_ref, bias_ref, bias_out_ref,
    project_ref, mixed_ref, branch_ref, middle_ref, weight_ref, semaphores,
):
    ranks = weight_ref.shape[0]

    @pl.when(pl.program_id(0) == 0)
    def _():
        start_loads(source, weight_ref, semaphores)

    stream = rows_of(stream_ref).astype(jnp.float32)
    tokens, width = stream.shape
    shape, _ = norm_parts(stream)
    normed = (shape * (1.0 + mod_ref[1:2]) + mod_ref[0:1]).astype(jnp.bfloat16)
    lower = half_masks(tokens)
    allowed = same_patch(tokens, stride) if stride else None

    @pl.when(pl.program_id(0) == 0)
    def _():
        for rank in range(ranks):
            wait_loads(weight_ref, semaphores, rank)

    def one_head(chosen, key, value):
        scores = mm(chosen.astype(jnp.bfloat16), key, ((1,), (1,)))
        if stride:
            scores = jnp.where(allowed, scores, BLOCKED)
        return mm(softmax_rows(scores, -1).astype(jnp.bfloat16), value)

    branch = None
    for rank in range(ranks):
        hook(rank)
        project = (mm(normed, weight_ref[rank, :, : 5 * PAIR]) + bias_ref[rank]).astype(jnp.bfloat16)
        project_ref[rank] = project.reshape(project_ref.shape[1:])
        query = project[:, :PAIR].astype(jnp.float32) * HD**-0.5
        key, value = project[:, PAIR : 2 * PAIR], project[:, 2 * PAIR : 3 * PAIR]
        first = one_head(jnp.where(lower, query, 0.0), key, value)
        second = one_head(jnp.where(lower, 0.0, query), key, value)
        both = project[:, 3 * PAIR : 4 * PAIR].astype(jnp.float32)
        last = one_head(
            jnp.where(lower, both * HD**-0.5, 0.0),
            swap_halves(both).astype(jnp.bfloat16),
            project[:, 4 * PAIR : 5 * PAIR],
        )
        mixed = jnp.concatenate(
            [jnp.where(lower, 0.0, swap_halves(last)), jnp.where(lower, first, second)], axis=1
        ).astype(jnp.bfloat16)
        mixed_ref[rank] = mixed.reshape(mixed_ref.shape[1:])
        term = mm(mixed, weight_ref[rank, :, 4 * PAIR :], ((1,), (1,)))
        branch = term if branch is None else branch + term
    branch = branch + bias_out_ref[...]
    put(branch_ref, branch)
    put(middle_ref, stream + mod_ref[2:3] * branch)


def gelu_parts(value):
    square = value * value
    bent = jnp.tanh(value * (GELU_A + (GELU_A * GELU_B) * square))
    half = 0.5 * (1.0 + bent)
    slope = half + (0.5 * value) * (1.0 - bent * bent) * (GELU_A + (3.0 * GELU_A * GELU_B) * square)
    return value * half, slope


def ffn_forward_kernel(
    stream, hook, up_source, down_source, middle_ref, mod_ref, bias_ref, bias_up_ref, hidden_ref, branch_ref, *rest
):
    if stream is None:
        result_ref, *rest = rest
    up_ref, down_ref, up_semaphores, down_semaphores = rest
    step = pl.program_id(0)
    ranks = up_ref.shape[0]

    @pl.when(step == 0)
    def _():
        start_loads(up_source, up_ref, up_semaphores)
        start_loads(down_source, down_ref, down_semaphores)

    middle = middle_ref[...]
    shape, _ = norm_parts(middle)
    second = (shape * (1.0 + mod_ref[4:5]) + mod_ref[3:4]).astype(jnp.bfloat16)

    @pl.when(step == 0)
    def _():
        for rank in range(ranks):
            wait_loads(up_ref, up_semaphores, rank)
            wait_loads(down_ref, down_semaphores, rank)

    down = None
    for rank in range(ranks):
        hook(rank)
        hidden = mm(second, up_ref[rank]) + bias_up_ref[rank]
        hidden_ref[rank] = hidden.astype(jnp.bfloat16)
        active, _ = gelu_parts(hidden)
        part = mm(active.astype(jnp.bfloat16), down_ref[rank], ((1,), (1,)))
        down = part if down is None else down + part
    down = down + bias_ref[...]
    branch_ref[...] = down.astype(jnp.bfloat16)
    result = middle + mod_ref[5:6] * down
    if stream is None:
        result_ref[...] = result.astype(result_ref.dtype)
    else:
        stream.put(step, result)


def load_frame(ref, index, chunk):
    if len(ref.shape) == 2:
        return ref[index * chunk : (index + 1) * chunk, :].astype(jnp.float32)
    value = ref[:, index]
    return value.reshape(chunk, value.shape[-1]).astype(jnp.float32)


def ffn_backward_kernel(
    split, hook, up_source, down_source, grad_ref, middle_ref, branch_ref, hidden_ref, mod_ref,
    grad_middle_ref, weight_grad_ref, up_sum_ref, sums_ref,
    up_ref, down_ref, up_semaphores, down_semaphores,
    second_ref, low_ref, active_ref, slope_ref, total_ref,
):
    step = pl.program_id(0)
    tokens, width = middle_ref.shape
    chunk = tokens // split

    @pl.when(step == 0)
    def _():
        start_loads(up_source, up_ref, up_semaphores)
        start_loads(down_source, down_ref, down_semaphores)
        sums_ref[...] = jnp.zeros_like(sums_ref)
        for index in range(split):
            rows = slice(index * chunk, (index + 1) * chunk)
            grad = load_frame(grad_ref, index, chunk)
            low = (mod_ref[5:6] * grad).astype(jnp.bfloat16)
            low_ref[rows, :] = low
            add_rows(sums_ref, 0, low.astype(jnp.float32))
            add_rows(sums_ref, 3, grad * branch_ref[rows, :].astype(jnp.float32))
            shape, _ = norm_parts(middle_ref[rows, :])
            second_ref[rows, :] = (shape * (1.0 + mod_ref[4:5]) + mod_ref[3:4]).astype(jnp.bfloat16)

    up_sum_ref[...] = jnp.zeros_like(up_sum_ref)
    wait_loads(up_ref, up_semaphores, step)
    wait_loads(down_ref, down_semaphores, step)

    for index in range(split):
        hook(index)
        rows = slice(index * chunk, (index + 1) * chunk)
        active, slope = gelu_parts(hidden_ref[0, rows, :].astype(jnp.float32))
        active_ref[rows, :] = active.astype(jnp.bfloat16)
        low = (mm(low_ref[rows, :], down_ref[step]) * slope).astype(jnp.bfloat16)
        slope_ref[rows, :] = low
        up_sum_ref[0] += jnp.sum(low.astype(jnp.float32), axis=0, keepdims=True)
        part = mm(low, up_ref[step], ((1,), (1,)))
        total_ref[rows, :] = jnp.where(step == 0, 0.0, total_ref[rows, :]) + part

    def weights(index, carry):
        part = pl.ds(pl.multiple_of(index * BLOCK, BLOCK), BLOCK)
        weight_grad_ref[0, 0, part, :] = mm(second_ref[:, part], slope_ref[...], ((0,), (0,))).astype(
            jnp.bfloat16
        )
        weight_grad_ref[1, 0, part, :] = mm(low_ref[:, part], active_ref[...], ((0,), (0,))).astype(
            jnp.bfloat16
        )
        return carry

    lax.fori_loop(0, width // BLOCK, weights, 0)

    @pl.when(step == pl.num_programs(0) - 1)
    def _():
        for index in range(split):
            rows = slice(index * chunk, (index + 1) * chunk)
            shape, inverse = norm_parts(middle_ref[rows, :])
            grad = total_ref[rows, :]
            add_rows(sums_ref, 1, grad)
            add_rows(sums_ref, 2, grad * shape)
            back = norm_back(grad * (1.0 + mod_ref[4:5]), shape, inverse)
            grad_middle_ref[rows, :] = load_frame(grad_ref, index, chunk) + back


def attention_backward_kernel(
    stride, swap, hook, source, grad_ref, stream_ref, project_ref, mixed_ref, branch_ref, mod_ref, *refs
):
    if swap is None:
        grad_stream_ref, *refs = refs
    (weight_grad_ref, sums_ref, project_sum_ref,
     weight_ref, semaphores, left_ref, right_ref, outer_ref) = refs
    step = pl.program_id(0)
    ranks = weight_ref.shape[0]

    @pl.when(step == 0)
    def _():
        start_loads(source, weight_ref, semaphores)
        sums_ref[...] = jnp.zeros_like(sums_ref)
        project_sum_ref[...] = jnp.zeros_like(project_sum_ref)

    grad_middle = rows_of(grad_ref)
    tokens, width = grad_middle.shape
    stream = rows_of(stream_ref).astype(jnp.float32)
    shape, inverse = norm_parts(stream)
    rows = pl.ds(pl.multiple_of(step * tokens, tokens), tokens)
    normed = (shape * (1.0 + mod_ref[1:2]) + mod_ref[0:1]).astype(jnp.bfloat16)
    low = (mod_ref[2:3] * grad_middle).astype(jnp.bfloat16)
    left_ref[0, rows, :] = normed
    left_ref[1, rows, :] = low
    add_rows(sums_ref, 0, low.astype(jnp.float32))
    add_rows(sums_ref, 3, grad_middle * rows_of(branch_ref).astype(jnp.float32))
    lower = half_masks(tokens)
    allowed = same_patch(tokens, stride) if stride else None
    scale = HD**-0.5

    @pl.when(step == 0)
    def _():
        for rank in range(ranks):
            wait_loads(weight_ref, semaphores, rank)

    def one_head(chosen, key, value, taken):
        scores = mm(key, chosen.astype(jnp.bfloat16), ((1,), (1,)))
        if stride:
            scores = jnp.where(allowed, scores, BLOCKED)
        probs = softmax_rows(scores, 0)
        grad_probs = mm(value, taken.astype(jnp.bfloat16), ((1,), (1,)))
        inner = jnp.sum(grad_probs * probs, axis=0, keepdims=True)
        return probs.astype(jnp.bfloat16), (probs * (grad_probs - inner)).astype(jnp.bfloat16)

    grad_normed = None
    for rank in range(ranks):
        hook(rank)
        project = project_ref[rank].reshape(tokens, 5 * PAIR)
        mixed = mixed_ref[rank].reshape(tokens, 2 * PAIR)
        outer_ref[rank, rows, :] = mixed
        grad_mixed = mm(low, weight_ref[rank, :, 4 * PAIR :]).astype(jnp.bfloat16)
        query, key, value = (project[:, n * PAIR : (n + 1) * PAIR] for n in range(3))
        query_wide = query.astype(jnp.float32) * scale
        pair = grad_mixed[:, PAIR:]
        pair_wide = pair.astype(jnp.float32)
        outs = []
        for keep in (lower, ~lower):
            probs, grad_scores = one_head(
                jnp.where(keep, query_wide, 0.0), key, value, jnp.where(keep, pair_wide, 0.0)
            )
            outs.append(
                (mm(grad_scores, key, ((0,), (0,))), mm(grad_scores, query), mm(probs, pair))
            )
        parts = [
            jnp.where(lower, one, two) * factor
            for one, two, factor in zip(outs[0], outs[1], (scale, scale, 1.0))
        ]
        both = project[:, 3 * PAIR : 4 * PAIR].astype(jnp.float32)
        swapped = swap_halves(both).astype(jnp.bfloat16)
        single = swap_halves(grad_mixed[:, :PAIR].astype(jnp.float32))
        probs, grad_scores = one_head(
            jnp.where(lower, both * scale, 0.0),
            swapped,
            project[:, 4 * PAIR :],
            jnp.where(lower, single, 0.0),
        )
        parts.append(
            jnp.where(lower, mm(grad_scores, swapped, ((0,), (0,))), mm(grad_scores, swapped)) * scale
        )
        parts.append(jnp.where(lower, mm(probs, single.astype(jnp.bfloat16)), 0.0))
        whole = jnp.concatenate(parts, axis=1).astype(jnp.bfloat16)
        right_ref[rank, rows, :] = whole
        add_rows(project_sum_ref, rank, whole.astype(jnp.float32))
        term = mm(whole, weight_ref[rank, :, : 5 * PAIR], ((1,), (1,)))
        grad_normed = term if grad_normed is None else grad_normed + term
    add_rows(sums_ref, 1, grad_normed)
    add_rows(sums_ref, 2, grad_normed * shape)
    back = norm_back(grad_normed * (1.0 + mod_ref[1:2]), shape, inverse)
    if swap is None:
        put(grad_stream_ref, grad_middle + back)
    else:
        swap.put(step, grad_middle + back)

    @pl.when(step == pl.num_programs(0) - 1)
    def _():
        def weights(rank, carry):
            def block(index, inner):
                part = pl.ds(pl.multiple_of(index * BLOCK, BLOCK), BLOCK)
                inside = mm(left_ref[0, :, part], right_ref[rank], ((0,), (0,)))
                outside = mm(left_ref[1, :, part], outer_ref[rank], ((0,), (0,)))
                weight_grad_ref[rank, part, : 4 * PAIR] = inside[:, : 4 * PAIR].astype(jnp.bfloat16)
                weight_grad_ref[rank, part, 4 * PAIR : 5 * PAIR] = (
                    inside[:, 4 * PAIR :] + outside[:, :PAIR]
                ).astype(jnp.bfloat16)
                weight_grad_ref[rank, part, 5 * PAIR :] = outside[:, PAIR:].astype(jnp.bfloat16)
                return inner

            return lax.fori_loop(0, width // BLOCK, block, carry)

        lax.fori_loop(0, ranks, weights, 0)


def fixed(shape):
    return pl.BlockSpec(shape, lambda step: (0,) * len(shape))


def cost(flops, moved, raised=0):
    return pl.CostEstimate(flops=int(flops), bytes_accessed=int(moved), transcendentals=int(raised))


def group_spec(shape):
    return pl.BlockSpec((shape[0], 1, shape[2], shape[3]), lambda step: (0, step, 0, 0))


def rank_spec(shape):
    return pl.BlockSpec((shape[0], shape[1], 1) + shape[3:], lambda step: (0, 0, step, 0, 0))


def attention_forward(weight, stream, mod, bias, bias_out, stride, jobs=(), collective_id=None):
    shape = stream.shape
    width = shape[-1]
    ranks = bias.shape[0]
    tokens = shape[0] * shape[1] * shape[2]
    spec = group_spec(shape)
    low = jax.ShapeDtypeStruct(shape, jnp.bfloat16)
    wide = jax.ShapeDtypeStruct(shape, jnp.float32)
    project = jax.ShapeDtypeStruct((ranks,) + shape[:3] + (5 * PAIR,), jnp.bfloat16)
    mixed = jax.ShapeDtypeStruct((ranks,) + shape[:3] + (2 * PAIR,), jnp.bfloat16)
    return call(
        partial(attention_forward_kernel, stride),
        shape[1],
        [weight, stream, mod, bias, bias_out],
        anywhere(1) + [spec, fixed(mod.shape), fixed(bias.shape), fixed(bias_out.shape)],
        [project, mixed, low, wide],
        [rank_spec(project.shape), rank_spec(mixed.shape), spec, spec],
        [pltpu.VMEM((ranks, width, 6 * PAIR), jnp.bfloat16), pltpu.SemaphoreType.DMA((ranks,))],
        jobs,
        collective_id,
        cost(8 * tokens * width * width * 1.5, tokens * width * 16),
        "attention_forward",
    )


def ffn_weights_scratch(ranks, width, part):
    return [
        pltpu.VMEM((ranks, width, part), jnp.bfloat16),
        pltpu.VMEM((ranks, width, part), jnp.bfloat16),
        pltpu.SemaphoreType.DMA((ranks,)),
        pltpu.SemaphoreType.DMA((ranks,)),
    ]


def ffn_forward(up, down, middle, mod, bias_down, bias_up, stream=None, jobs=(), collective_id=None):
    tokens, width = middle.shape
    ranks, _, part = bias_up.shape
    chunk = tokens // SPLIT
    block = pl.BlockSpec((chunk, width), lambda step: (step, 0))
    result = [jax.ShapeDtypeStruct((tokens, width), jnp.bfloat16)] if stream is None else []
    return call(
        partial(ffn_forward_kernel, stream),
        SPLIT,
        [up, down, middle, mod, bias_down, bias_up],
        anywhere(2) + [block, fixed(mod.shape), fixed(bias_down.shape), fixed(bias_up.shape)],
        [
            jax.ShapeDtypeStruct((ranks, tokens, part), jnp.bfloat16),
            jax.ShapeDtypeStruct((tokens, width), jnp.bfloat16),
        ] + result,
        [pl.BlockSpec((ranks, chunk, part), lambda step: (0, step, 0)), block] + [block] * len(result),
        ffn_weights_scratch(ranks, width, part),
        ([] if stream is None else [stream]) + list(jobs),
        collective_id,
        cost(4.8 * tokens * width * ranks * part, tokens * width * 14, tokens * ranks * part),
        "ffn_forward",
    )


def ffn_backward(up, down, grad, middle, branch, hidden, mod, jobs=(), collective_id=None):
    tokens, width = middle.shape
    ranks, _, part = hidden.shape
    whole = fixed((tokens, width))
    return call(
        partial(ffn_backward_kernel, SPLIT),
        ranks,
        [up, down, grad, middle, branch, hidden, mod],
        anywhere(2) + [
            fixed(grad.shape), whole, whole,
            pl.BlockSpec((1, tokens, part), lambda step: (step, 0, 0)),
            fixed(mod.shape),
        ],
        [
            jax.ShapeDtypeStruct((tokens, width), jnp.float32),
            jax.ShapeDtypeStruct((2, ranks, width, part), jnp.bfloat16),
            jax.ShapeDtypeStruct((ranks, 1, part), jnp.float32),
            jax.ShapeDtypeStruct((4, width), jnp.float32),
        ],
        [
            whole,
            pl.BlockSpec((2, 1, width, part), lambda step: (0, step, 0, 0)),
            pl.BlockSpec((1, 1, part), lambda step: (step, 0, 0)),
            fixed((4, width)),
        ],
        ffn_weights_scratch(ranks, width, part) + [
            pltpu.VMEM((tokens, width), jnp.bfloat16),
            pltpu.VMEM((tokens, width), jnp.bfloat16),
            pltpu.VMEM((tokens, part), jnp.bfloat16),
            pltpu.VMEM((tokens, part), jnp.bfloat16),
            pltpu.VMEM((tokens, width), jnp.float32),
        ],
        jobs,
        collective_id,
        cost(9.6 * tokens * width * ranks * part, tokens * width * 20, tokens * ranks * part),
        "ffn_backward",
    )


def attention_backward(weight, grad, stream, saved, mod, stride, swap=None, jobs=(), collective_id=None):
    project, mixed, branch = saved
    shape = stream.shape
    width = shape[-1]
    ranks = project.shape[0]
    tokens = shape[0] * shape[1] * shape[2]
    spec = group_spec(shape)
    result = [jax.ShapeDtypeStruct(shape, jnp.float32)] if swap is None else []
    return call(
        partial(attention_backward_kernel, stride, swap),
        shape[1],
        [weight, grad, stream, project, mixed, branch, mod],
        anywhere(1) + [
            spec, spec, rank_spec(project.shape), rank_spec(mixed.shape), spec, fixed(mod.shape),
        ],
        result + [
            jax.ShapeDtypeStruct((ranks, width, 6 * PAIR), jnp.bfloat16),
            jax.ShapeDtypeStruct((4, width), jnp.float32),
            jax.ShapeDtypeStruct((ranks, 5 * PAIR), jnp.float32),
        ],
        [spec] * len(result) + [
            fixed((ranks, width, 6 * PAIR)), fixed((4, width)), fixed((ranks, 5 * PAIR)),
        ],
        [
            pltpu.VMEM((ranks, width, 6 * PAIR), jnp.bfloat16),
            pltpu.SemaphoreType.DMA((ranks,)),
            pltpu.VMEM((2, tokens, width), jnp.bfloat16),
            pltpu.VMEM((ranks, tokens, 5 * PAIR), jnp.bfloat16),
            pltpu.VMEM((ranks, tokens, 2 * PAIR), jnp.bfloat16),
        ],
        ([] if swap is None else [swap]) + list(jobs),
        collective_id,
        cost(16 * tokens * width * width * 1.5, tokens * width * 20),
        "attention_backward",
    )


def pack_heads(block):
    query, key, value, outer = block
    return jnp.concatenate(
        [query[:, :PAIR], key[:, :PAIR], value[:, :PAIR], query[:, PAIR:], key[:, PAIR:],
         value[:, PAIR:], outer[:, PAIR:], outer[:, :PAIR]], axis=1
    )


def unpack_heads(packed):
    part = lambda start, size: packed[:, start : start + size]
    join = lambda first, last: jnp.concatenate([part(first, PAIR), part(last, HD)], axis=1)
    return jnp.stack(
        [join(0, 3 * PAIR), join(PAIR, 3 * PAIR + HD), join(2 * PAIR, 4 * PAIR), join(5 * PAIR, 4 * PAIR + HD)]
    )


def pack_bias(query, value, ranks):
    query, value = query.reshape(ranks, -1), value.reshape(ranks, -1)
    none = jnp.zeros((ranks, PAIR), query.dtype)
    return jnp.concatenate(
        [query[:, :PAIR], none, value[:, :PAIR], query[:, PAIR:], none[:, :HD], value[:, PAIR:], none[:, :HD]],
        axis=1,
    )[:, None]


def unpack_bias(sums):
    query = jnp.concatenate([sums[:, :PAIR], sums[:, 3 * PAIR : 3 * PAIR + HD]], axis=1)
    value = jnp.concatenate([sums[:, 2 * PAIR : 3 * PAIR], sums[:, 4 * PAIR : 4 * PAIR + HD]], axis=1)
    return query.reshape(-1), value.reshape(-1)


def place():
    return lax.axis_index("dp"), lax.axis_index("tensor"), lax.axis_size("dp"), lax.axis_size("tensor")


def greet_all():
    device, rank, dp, tp = place()
    me, count = device * tp + rank, dp * tp
    barrier = pltpu.get_barrier_semaphore()

    def greet(index, carry):
        peer = lax.rem(me + index, count)
        pl.semaphore_signal(
            barrier, inc=1, device_id=(peer // tp, lax.rem(peer, tp)), device_id_type=pl.DeviceIdType.MESH
        )
        return carry

    lax.fori_loop(1, count, greet, 0)
    pl.semaphore_wait(barrier, count - 1)


def push(source, target, send, receive, device, rank):
    pltpu.make_async_remote_copy(
        src_ref=source, dst_ref=target, send_sem=send, recv_sem=receive,
        device_id=(device, rank), device_id_type=pl.DeviceIdType.MESH,
    ).start()


def wait_bytes(ref, semaphore):
    pltpu.make_async_copy(ref, ref, semaphore).wait()


class Where:
    def __init__(self):
        device, rank = lax.axis_index("dp"), lax.axis_index("tensor")
        self.count = lax.axis_size("dp") // 2
        self.device, self.rank = device, rank
        self.far, self.side = device // 2, lax.rem(device, 2)
        self.row, self.core = rank // 2, lax.rem(rank, 2)
        self.other_side = self.far * 2 + 1 - self.side
        self.other_row = (1 - self.row) * 2 + self.core
        self.other_core = self.row * 2 + 1 - self.core

    def ahead(self, step):
        return lax.rem(self.far + step, self.count)

    def line(self, step):
        return self.ahead(step) * 2 + self.side


def greet_neighbours(here):
    barrier = pltpu.get_barrier_semaphore()
    peers = [(here.other_side, here.rank), (here.device, here.other_row), (here.device, here.other_core)]
    peers += [(here.line(step), here.rank) for step in range(1, here.count)]
    for peer in peers:
        pl.semaphore_signal(barrier, inc=1, device_id=peer, device_id_type=pl.DeviceIdType.MESH)
    pl.semaphore_wait(barrier, len(peers))


def add_into(target, left, right):
    target[...] = (left[...].astype(jnp.float32) + right[...].astype(jnp.float32)).astype(target.dtype)


class ScatterChain:
    def __init__(self, here, source, line, lead, scratch):
        self.here, self.source, self.line, self.lead = here, source, line, lead
        self.keep, self.land_core, self.first_one, self.last_one, self.first_two, self.last_two, self.semaphores = scratch
        self.rows = line.shape[1]

    @staticmethod
    def scratch(width, columns, dp, lead):
        rows, far = width // dp, dp // 2
        low = lambda *shape: pltpu.VMEM(shape + (columns,), jnp.bfloat16)
        return [
            low(2, width), low(2, width),
            low(2, lead, rows), low(2 * (far - lead) * rows), low(lead, rows), low(far - lead, rows),
            pltpu.SemaphoreType.DMA((6, 2)),
        ]

    def chunk(self, row, far, side):
        return self.keep.at[row, pl.ds(pl.multiple_of((far * 2 + side) * self.rows, self.rows), self.rows)]

    def send(self, slot, source, target, device, rank):
        push(source, target, self.semaphores.at[slot, 0], self.semaphores.at[slot, 1], device, rank)

    def arrived(self, slot, ref):
        wait_bytes(ref, self.semaphores.at[slot, 1])

    def left(self, slot, ref):
        wait_bytes(ref, self.semaphores.at[slot, 0])

    def stage_core(self):
        here = self.here
        for row in range(2):
            pltpu.make_async_copy(
                self.source.at[row * 2 + here.core], self.keep.at[row], self.semaphores.at[5, 0]
            ).start()
            self.send(0, self.source.at[row * 2 + 1 - here.core], self.land_core.at[row], here.device, here.other_core)

    def stage_one(self):
        here = self.here
        wait_bytes(self.keep, self.semaphores.at[5, 0])
        self.arrived(0, self.land_core)

        def one(index, carry):
            rows = pl.ds(pl.multiple_of(index * self.rows, self.rows), self.rows)
            for row in range(2):
                add_into(self.keep.at[row, rows], self.keep.at[row, rows], self.land_core.at[row, rows])
            return carry

        lax.fori_loop(0, here.count * 2, one, 0)
        for row in range(2):
            for far in range(self.lead):
                self.send(
                    1, self.chunk(row, far, 1 - here.side), self.first_one.at[row, far], here.other_side, here.rank
                )
        start, size = self.lead * 2 * self.rows, (here.count - self.lead) * 2 * self.rows
        self.send(2, self.keep.at[1 - here.row, pl.ds(start, size)], self.last_one, here.device, here.other_row)

    def stage_two(self):
        here, lead = self.here, self.lead
        self.arrived(1, self.first_one)
        for row in range(2):
            for far in range(lead):
                mine = self.chunk(row, far, here.side)
                add_into(mine, mine, self.first_one.at[row, far])
        for far in range(lead):
            self.send(3, self.chunk(1 - here.row, far, here.side), self.first_two.at[far], here.device, here.other_row)
        self.arrived(2, self.last_one)
        for far in range(lead, here.count):
            for side in range(2):
                mine = self.chunk(here.row, far, side)
                add_into(mine, mine, self.last_one.at[pl.ds(((far - lead) * 2 + side) * self.rows, self.rows)])
        for far in range(lead, here.count):
            self.send(
                4, self.chunk(here.row, far, 1 - here.side), self.last_two.at[far - lead], here.other_side, here.rank
            )

    def merge(self):
        here = self.here
        self.arrived(3, self.first_two)
        self.arrived(4, self.last_two)
        for far in range(here.count):
            land = self.first_two.at[far] if far < self.lead else self.last_two.at[far - self.lead]
            add_into(self.line.at[far], self.chunk(here.row, far, here.side), land)

    def finish(self):
        self.left(0, self.land_core)
        self.left(1, self.first_one)
        self.left(2, self.last_one)
        self.left(3, self.first_two)
        self.left(4, self.last_two)


class LineChain:
    def __init__(self, here, line, out, land, semaphores):
        self.here, self.line, self.out, self.land, self.semaphores = here, line, out, land, semaphores

    @staticmethod
    def scratch(far, rows, columns):
        return [pltpu.VMEM((far - 1, rows, columns), jnp.bfloat16), pltpu.SemaphoreType.DMA((2,))]

    def start(self):
        here = self.here
        for step in range(1, here.count):
            push(
                self.line.at[here.ahead(step)], self.land.at[step - 1], self.semaphores.at[0],
                self.semaphores.at[1], here.line(step), here.rank,
            )

    def finish(self):
        wait_bytes(self.land, self.semaphores.at[1])
        total = self.line[self.here.far].astype(jnp.float32)
        for step in range(1, self.here.count):
            total = total + self.land[step - 1].astype(jnp.float32)
        self.out[...] = total
        wait_bytes(self.land, self.semaphores.at[0])


def leave_kernel(mod_start, *refs):
    refs = list(refs)
    scattering = len(refs) > 10
    source, begun = (refs.pop(0), refs.pop(0)) if scattering else (None, None)
    small_ref, modulation_ref, *refs = refs
    out, begun_out = (refs.pop(0), refs.pop(0)) if scattering else (None, None)
    sum_ref, act_ref, land_ref, acting_ref, semaphores, *space = refs
    device, rank, dp, tp = place()
    me, count = device * tp + rank, dp * tp
    greet_all()
    if scattering:
        here = Where()
        line_ref, *space = space
        pick = lambda number: [space.pop(0) for _ in range(number)]
        chains, trails = [], []
        for index in range(PARTS):
            size = out.shape[1] // PARTS
            part = pl.ds(index * size, size)
            line = line_ref.at[index]
            chains.append(ScatterChain(here, source.at[:, :, part], line, here.count // 2, pick(7)))
            trails.append(LineChain(here, line, out.at[:, part], *pick(2)))
        others = [LineChain(here, begun.at[kind], begun_out.at[kind], *pick(2)) for kind in range(begun.shape[0])]
        for chain in chains:
            chain.stage_core()
        for chain in others:
            chain.start()
    for step in range(1, tp):
        there = lax.rem(rank + step, tp)
        push(small_ref.at[there], land_ref.at[rank], semaphores.at[0], semaphores.at[1], device, there)
    land_ref[rank] = small_ref[rank]
    wait_bytes(land_ref.at[pl.ds(0, tp - 1)], semaphores.at[1])
    mine = sum_ref.at[rank]
    mine[device] = jnp.sum(land_ref[...], axis=0)

    def one(step, carry):
        push(mine.at[device], mine.at[device], semaphores.at[2], semaphores.at[3], lax.rem(device + step, dp), rank)
        return carry

    lax.fori_loop(1, dp, one, 0)
    if scattering:
        for chain in chains:
            chain.stage_one()
    wait_bytes(mine.at[pl.ds(0, dp - 1)], semaphores.at[3])
    for step in range(1, tp):
        push(mine, mine, semaphores.at[4], semaphores.at[5], device, lax.rem(rank + step, tp))
    wait_bytes(sum_ref.at[pl.ds(0, tp - 1)], semaphores.at[5])
    layers, padded, columns = modulation_ref.shape
    lines = sum_ref.shape[2]
    total = jnp.zeros((dp, padded), jnp.float32)
    for layer in range(layers):
        for index in range(columns // PAIR):
            line = layer * (tp * lines // layers) + mod_start // PAIR + index
            low = sum_ref[line // lines, :, line % lines, :].astype(jnp.bfloat16)
            total += mm(low, modulation_ref[layer, :, index * PAIR : (index + 1) * PAIR], ((1,), (1,)))
    acting_ref[...] = jnp.concatenate([total, jnp.zeros((dp, PAIR - padded), jnp.float32)], axis=1)
    act_ref[me] = acting_ref[...]

    def tell(index, carry):
        peer = lax.rem(me + index, count)
        push(acting_ref, act_ref.at[me], semaphores.at[6], semaphores.at[7], peer // tp, lax.rem(peer, tp))
        return carry

    lax.fori_loop(1, count, tell, 0)
    if scattering:
        for chain in chains:
            chain.stage_two()
        for chain, line in zip(chains, trails):
            chain.merge()
            line.start()
        for chain in others:
            chain.finish()
    wait_bytes(act_ref.at[pl.ds(0, count - 1)], semaphores.at[7])
    wait_bytes(act_ref.at[pl.ds(0, count - 1)], semaphores.at[6])
    wait_bytes(land_ref.at[pl.ds(0, tp - 1)], semaphores.at[0])
    wait_bytes(mine.at[pl.ds(0, dp - 1)], semaphores.at[2])
    wait_bytes(sum_ref.at[pl.ds(0, tp - 1)], semaphores.at[4])
    if scattering:
        for chain in chains + trails:
            chain.finish()


def leave(small, modulation, mod_start, grads, begun, collective_id):
    tp, lines, lanes = small.shape
    dp = lax.axis_size("dp")
    inside = pl.BlockSpec(memory_space=pltpu.VMEM)
    shapes, space, extra = [], [], []
    if grads is not None:
        _, width, columns = grads.shape
        rows, far, part = width // dp, dp // 2, columns // PARTS
        kinds = begun.shape[0]
        extra = [grads, begun]
        shapes = [
            jax.ShapeDtypeStruct((rows, columns), jnp.float32),
            jax.ShapeDtypeStruct((kinds, rows, columns), jnp.float32),
        ]
        space = [pltpu.VMEM((PARTS, far, rows, part), jnp.bfloat16)]
        for _ in range(PARTS):
            space += ScatterChain.scratch(width, part, dp, far // 2) + LineChain.scratch(far, rows, part)
        space += LineChain.scratch(far, rows, columns) * kinds
    return pl.pallas_call(
        partial(leave_kernel, mod_start),
        in_specs=[pl.BlockSpec(memory_space=pl.ANY), inside][: len(extra)] + [inside, inside],
        out_specs=[inside] * (len(shapes) + 2),
        out_shape=shapes + [
            jax.ShapeDtypeStruct((tp, dp, lines, lanes), jnp.float32),
            jax.ShapeDtypeStruct((dp * tp, dp, lanes), jnp.float32),
        ],
        scratch_shapes=[
            pltpu.VMEM((tp, lines, lanes), jnp.float32),
            pltpu.VMEM((dp, lanes), jnp.float32),
            pltpu.SemaphoreType.DMA((8,)),
        ] + space,
        compiler_params=pltpu.CompilerParams(
            collective_id=collective_id, has_side_effects=True, vmem_limit_bytes=VMEM_LIMIT
        ),
        name="leave",
    )(*extra, small, modulation)


class GatherChain:
    def __init__(self, here, source, out, semaphores, half=None):
        self.here, self.source, self.out, self.semaphores = here, source, out, semaphores
        self.rows = out.shape[1] // (2 * here.count)
        self.half = here.count // 2 if half is None else half

    @staticmethod
    def scratch():
        return [pltpu.SemaphoreType.DMA((9, 2))]

    def piece(self, rank, far, side):
        rows = pl.ds(pl.multiple_of((far * 2 + side) * self.rows, self.rows), self.rows)
        return self.out.at[rank, rows]

    def send(self, slot, source, target, device, rank):
        push(source, target, self.semaphores.at[slot, 0], self.semaphores.at[slot, 1], device, rank)

    def wait(self, slot, way, pieces):
        wait_bytes(self.out.at[0, pl.ds(0, pieces * self.rows)], self.semaphores.at[slot, way])

    def stage_line(self):
        here = self.here
        mine = self.piece(here.rank, here.far, here.side)
        pltpu.make_async_copy(self.source, mine, self.semaphores.at[8, 0]).start()
        for step in range(1, here.count):
            self.send(0, self.source, mine, here.line(step), here.rank)

    def line_arrived(self):
        self.wait(8, 0, 1)
        self.wait(0, 1, self.here.count - 1)

    def line_left(self):
        self.wait(0, 0, self.here.count - 1)

    def stage_near(self):
        here = self.here
        for far in range(here.count):
            mine = self.piece(here.rank, far, here.side)
            self.send(1, mine, mine, here.other_side, here.rank)
            self.send(2, mine, mine, here.device, here.other_row)
        for far in range(here.count):
            mine = self.piece(here.rank, far, here.side)
            self.send(3, mine, mine, here.device, here.other_core)

    def stage_across(self):
        here, count = self.here, self.here.count
        self.wait(1, 1, count)
        for far in range(self.half):
            other = self.piece(here.rank, far, 1 - here.side)
            self.send(4, other, other, here.device, here.other_row)
        self.wait(2, 1, count)
        for far in range(self.half, count):
            other = self.piece(here.other_row, far, here.side)
            self.send(5, other, other, here.other_side, here.rank)
        for far in range(count):
            for other in (self.piece(here.rank, far, 1 - here.side), self.piece(here.other_row, far, here.side)):
                self.send(6, other, other, here.device, here.other_core)

    def stage_core(self):
        here, count = self.here, self.here.count
        self.wait(4, 1, self.half)
        self.wait(5, 1, count - self.half)
        for far in range(count):
            other = self.piece(here.other_row, far, 1 - here.side)
            self.send(7, other, other, here.device, here.other_core)

    def finish(self):
        count, half = self.here.count, self.half
        self.wait(3, 1, count)
        self.wait(6, 1, 2 * count)
        self.wait(7, 1, count)
        for slot, pieces in ((1, count), (2, count), (3, count), (4, half), (5, count - half), (6, 2 * count), (7, count)):
            self.wait(slot, 0, pieces)


class Job:
    operands, sources, shapes, specs, aliases, space = (), None, (), (), {}, ()
    stages, last = {}, ()


def anywhere(count):
    return [pl.BlockSpec(memory_space=pl.ANY)] * count


class ScatterJob(Job):
    def __init__(self, grads, lead):
        kinds, _, width, columns = grads.shape
        dp = lax.axis_size("dp")
        self.lead = lead
        shape = (kinds, dp // 2, width // dp, columns)
        self.operands = [grads]
        self.shapes, self.specs = [jax.ShapeDtypeStruct(shape, jnp.bfloat16)], [fixed(shape)]
        self.space = ScatterChain.scratch(width, columns, dp, lead) * kinds

    def bind(self, here, inputs, outputs, space):
        kinds = outputs[0].shape[0]
        size = len(space) // kinds
        chains = [
            ScatterChain(
                here, inputs[0].at[kind], outputs[0].at[kind], self.lead, space[kind * size : (kind + 1) * size]
            )
            for kind in range(kinds)
        ]
        one = chains[0]
        if kinds == 1:
            self.stages = {(0, 0): [one.stage_core], (0, 3): [one.stage_one], (2, 1): [one.stage_two]}
            self.last = [one.merge, one.finish]
            return
        two = chains[1]
        self.stages = {
            (0, 0): [one.stage_core, two.stage_core], (0, 2): [one.stage_one], (0, 3): [two.stage_one],
            (2, 1): [one.stage_two], (3, 1): [two.stage_two],
        }
        self.last = [one.merge, two.merge, one.finish, two.finish]


class LineJob(Job):
    def __init__(self, line):
        kinds, far, rows, columns = line.shape
        shape = (kinds, rows, columns)
        self.operands, self.sources = [line], [fixed(line.shape)]
        self.shapes, self.specs = [jax.ShapeDtypeStruct(shape, jnp.float32)], [fixed(shape)]
        self.space = LineChain.scratch(far, rows, columns) * kinds

    def bind(self, here, inputs, outputs, space):
        chains = [
            LineChain(here, inputs[0].at[kind], outputs[0].at[kind], *space[2 * kind : 2 * kind + 2])
            for kind in range(outputs[0].shape[0])
        ]
        self.stages = {(0, 0): [chain.start for chain in chains]}
        self.last = [chain.finish for chain in chains]


class FlowJob(Job):
    def __init__(self, spread, lines, half=None):
        dp, tp = lax.axis_size("dp"), lax.axis_size("tensor")
        self.spread, self.half = len(spread), half
        self.operands = list(spread) + list(lines)
        self.shapes = [jax.ShapeDtypeStruct(v.shape, v.dtype) for v in spread]
        self.shapes += [jax.ShapeDtypeStruct((tp, dp * v.shape[0], v.shape[1]), v.dtype) for v in lines]
        self.specs = anywhere(len(self.shapes))
        self.aliases = {index: index for index in range(len(spread))}
        self.space = GatherChain.scratch() * len(self.shapes)

    def bind(self, here, inputs, outputs, space):
        chains = [GatherChain(here, *refs, self.half) for refs in zip(inputs, outputs, space)]
        spread, lines = chains[: self.spread], chains[self.spread :]
        self.stages = {
            (0, 0): [chain.stage_near for chain in spread] + [chain.stage_line for chain in lines[:1]],
            (1, 0): [chain.stage_line for chain in lines[1:]],
            (3, 0): [chain.stage_across for chain in spread[:1]],
        }
        self.last = [chain.stage_across for chain in spread[1:]]
        self.last += [chain.stage_core for chain in spread]
        self.last += [chain.finish for chain in spread]
        for chain in lines:
            self.last += [chain.line_arrived, chain.line_left]


class SwapJob(Job):
    def __init__(self, blocks):
        self.operands = [blocks]
        self.shapes, self.specs = [jax.ShapeDtypeStruct(blocks.shape, blocks.dtype)], anywhere(1)
        self.space = [pltpu.SemaphoreType.DMA((3,))]

    def bind(self, here, inputs, outputs, space):
        source, out, semaphores = inputs[0], outputs[0], space[0]
        ranks = out.shape[0]

        def start():
            pltpu.make_async_copy(source.at[here.rank], out.at[here.rank], semaphores.at[2]).start()
            for step in range(1, ranks):
                there = lax.rem(here.rank + step, ranks)
                push(source.at[there], out.at[here.rank], semaphores.at[0], semaphores.at[1], here.device, there)

        def finish():
            wait_bytes(out.at[0], semaphores.at[2])
            wait_bytes(out.at[pl.ds(0, ranks - 1)], semaphores.at[1])
            wait_bytes(out.at[pl.ds(0, ranks - 1)], semaphores.at[0])

        self.stages, self.last = {(0, 0): [start]}, [finish]


class StreamJob(Job):
    def __init__(self, shape, frames):
        self.shape, self.frames = shape, frames
        self.shapes, self.specs = [jax.ShapeDtypeStruct(shape, jnp.bfloat16)], anywhere(1)
        ranks, groups, rows, width = shape
        block = (groups, ranks, rows, width)
        if frames:
            block = (frames, ranks, groups, rows // frames, width)
        self.space = [pltpu.VMEM(block, jnp.bfloat16), pltpu.SemaphoreType.DMA((3,))]

    def bind(self, here, inputs, outputs, space):
        self.here, self.out = here, outputs[0]
        self.buffer, self.semaphores = space
        ranks = self.shape[0]

        def finish():
            wait_bytes(self.out.at[0], self.semaphores.at[2])
            wait_bytes(self.out.at[pl.ds(0, ranks - 1)], self.semaphores.at[1])
            wait_bytes(self.out.at[pl.ds(0, ranks - 1)], self.semaphores.at[0])

        self.stages, self.last = {}, [finish]

    def put(self, step, value):
        here, ranks = self.here, self.shape[0]
        self.buffer[step] = value.reshape(self.buffer.shape[1:]).astype(jnp.bfloat16)
        if self.frames:
            strip = self.buffer.shape[3]
            target = self.out.at[here.rank, :, pl.ds(pl.multiple_of(step * strip, strip), strip)]
        else:
            target = self.out.at[here.rank, step]
        pltpu.make_async_copy(self.buffer.at[step, here.rank], target, self.semaphores.at[2]).start()
        for ahead in range(1, ranks):
            there = lax.rem(here.rank + ahead, ranks)
            push(
                self.buffer.at[step, there], target, self.semaphores.at[0], self.semaphores.at[1],
                here.device, there,
            )


def greet_jobs(here):
    barrier = pltpu.get_barrier_semaphore()
    ranks = lax.axis_size("tensor")
    peers = [(here.other_side, here.rank)]
    peers += [(here.line(step), here.rank) for step in range(1, here.count)]
    peers += [(here.device, lax.rem(here.rank + step, ranks)) for step in range(1, ranks)]
    for peer in peers:
        pl.semaphore_signal(barrier, inc=1, device_id=peer, device_id_type=pl.DeviceIdType.MESH)
    pl.semaphore_wait(barrier, len(peers))


def call(body, steps, arguments, in_specs, out_shape, out_specs, scratch, jobs, collective_id, estimate, name):
    operands = [v for job in jobs for v in job.operands]
    sources = [v for job in jobs for v in (job.sources or anywhere(len(job.operands)))]
    shapes = [v for job in jobs for v in job.shapes]
    specs = [v for job in jobs for v in job.specs]
    space = [v for job in jobs for v in job.space]
    aliases, before, after = {}, len(arguments), len(out_shape)
    for job in jobs:
        for source, target in job.aliases.items():
            aliases[before + source] = after + target
        before, after = before + len(job.operands), after + len(job.shapes)

    def kernel(*refs):
        refs = list(refs)
        take = lambda number: [refs.pop(0) for _ in range(number)]
        inputs, job_inputs = take(len(arguments)), take(len(operands))
        outputs, job_outputs = take(len(out_shape)), take(len(shapes))
        own, job_space = take(len(scratch)), refs
        step = pl.program_id(0)
        if jobs:
            here = Where()
            for job in jobs:
                pick = lambda pool, number: [pool.pop(0) for _ in range(number)]
                job.bind(
                    here, pick(job_inputs, len(job.operands)), pick(job_outputs, len(job.shapes)),
                    pick(job_space, len(job.space)),
                )

        def hook(spot):
            for index in range(steps):
                todo = [stage for job in jobs for stage in job.stages.get((index, spot), ())]
                if todo or (jobs and spot == 0 and index == 0):

                    @pl.when(step == index)
                    def _():
                        if index == 0 and spot == 0:
                            greet_jobs(here)
                        for stage in todo:
                            stage()

        hook(0)
        body(lambda spot: hook(spot) if spot else None, *inputs, *outputs, *own)
        if jobs:

            @pl.when(step == steps - 1)
            def _():
                for job in jobs:
                    for stage in job.last:
                        stage()

    more = {"collective_id": collective_id, "has_side_effects": True} if jobs else {}
    return pl.pallas_call(
        kernel,
        grid=(steps,),
        in_specs=list(in_specs) + sources,
        out_specs=list(out_specs) + specs,
        out_shape=list(out_shape) + shapes,
        scratch_shapes=list(scratch) + space,
        input_output_aliases=aliases,
        compiler_params=pltpu.CompilerParams(
            vmem_limit_bytes=VMEM_LIMIT, dimension_semantics=("arbitrary",), **more
        ),
        cost_estimate=estimate,
        name=name,
    )(*arguments, *operands)


def entry_kernel(
    per_device, row_ref, modulation_ref, *refs
):
    gather = 3 if len(refs) > 5 else 0
    refs = list(refs)
    sources = [refs.pop(0) for _ in range(gather)]
    gathered_ref, mod_ref = refs.pop(0), refs.pop(0)
    targets = [refs.pop(0) for _ in range(gather)]
    part_ref, land_ref, semaphores, *space = refs
    device, rank, dp, tp = place()
    me, count = device * tp + rank, dp * tp
    quarter = land_ref.shape[2]
    if gather:
        here = Where()
        size = sources[0].shape[1] // PARTS
        parts = []
        for index in range(PARTS):
            part = pl.ds(index * size, size)
            parts.append(GatherChain(here, sources[0].at[:, part], targets[0].at[:, :, part], space.pop(0)))
        one, two = (GatherChain(here, *group) for group in zip(sources[1:], targets[1:], space))
    greet_all()

    def tell(index, carry):
        peer = lax.rem(me + index, count)
        push(
            row_ref, gathered_ref.at[me], semaphores.at[0], semaphores.at[1], peer // tp, lax.rem(peer, tp)
        )
        return carry

    lax.fori_loop(1, count, tell, 0)
    gathered_ref[me] = row_ref[...]
    if gather:
        for chain in parts:
            chain.stage_line()
    wait_bytes(gathered_ref.at[pl.ds(0, count - 1)], semaphores.at[1])
    padded = modulation_ref.shape[1]
    width = dp * tp * per_device
    chosen = jnp.zeros((count, padded), jnp.float32)
    row = lax.broadcasted_iota(jnp.int32, (PAIR, padded), 0)
    column = lax.broadcasted_iota(jnp.int32, (PAIR, padded), 1)
    for index in range(width // PAIR):
        match = (row + index * PAIR == column + me * per_device) & (column < per_device)
        chosen += mm(
            gathered_ref[:, index, :].astype(jnp.bfloat16), jnp.where(match, 1.0, 0.0).astype(jnp.bfloat16)
        )
    clip = lax.broadcasted_iota(jnp.int32, (dp, count), 0)
    member = lax.broadcasted_iota(jnp.int32, (dp, count), 1)
    leaders = jnp.where(member == clip * tp, 1.0, 0.0).astype(jnp.bfloat16)
    rows = mm(leaders, chosen.astype(jnp.bfloat16)).astype(jnp.bfloat16)
    for layer in range(modulation_ref.shape[0]):
        part = mm(rows, modulation_ref[layer])
        size = part.shape[1]
        for index in range(dp):
            part_ref[index, :, layer * size : (layer + 1) * size] = part[index : index + 1]

    def share(index, carry):
        peer = lax.rem(me + index, count)
        there, lane = peer // tp, lax.rem(peer, tp)
        source = part_ref.at[there, :, pl.ds(pl.multiple_of(lane * quarter, PAIR), quarter)]
        push(source, land_ref.at[me], semaphores.at[2], semaphores.at[3], there, lane)
        return carry

    lax.fori_loop(1, count, share, 0)
    mine = pl.ds(pl.multiple_of(rank * quarter, PAIR), quarter)
    land_ref[me] = part_ref[device, :, mine]
    if gather:
        for chain in parts:
            chain.line_arrived()
            chain.stage_near()
        one.stage_line()
    wait_bytes(land_ref.at[pl.ds(0, count - 1)], semaphores.at[3])
    mod_ref[:, mine] = jnp.sum(land_ref[...], axis=0)
    for step in range(1, tp):
        push(
            mod_ref.at[:, mine], mod_ref.at[:, mine], semaphores.at[4], semaphores.at[5],
            device, lax.rem(rank + step, tp),
        )
    if gather:
        for chain in parts:
            chain.stage_across()
        two.stage_line()
        for chain in parts:
            chain.stage_core()
    wait_bytes(gathered_ref.at[pl.ds(0, count - 1)], semaphores.at[0])
    wait_bytes(land_ref.at[pl.ds(0, count - 1)], semaphores.at[2])
    wait_bytes(mod_ref.at[:, pl.ds(0, (tp - 1) * quarter)], semaphores.at[5])
    wait_bytes(mod_ref.at[:, pl.ds(0, (tp - 1) * quarter)], semaphores.at[4])
    if gather:
        for chain in (one, two):
            chain.line_arrived()
        for chain in parts:
            chain.finish()
        for chain in (*parts, one, two):
            chain.line_left()


def enter(row, modulation, per_device, weights, collective_id):
    dp, tp = lax.axis_size("dp"), lax.axis_size("tensor")
    count = dp * tp
    whole = modulation.shape[0] * modulation.shape[2]
    inside = pl.BlockSpec(memory_space=pltpu.VMEM)
    job = FlowJob((), weights) if weights else Job()
    return pl.pallas_call(
        partial(entry_kernel, per_device),
        in_specs=[inside, inside] + anywhere(len(job.operands)),
        out_specs=[inside, inside] + list(job.specs),
        out_shape=[
            jax.ShapeDtypeStruct((count,) + row.shape, jnp.float32),
            jax.ShapeDtypeStruct((1, whole), jnp.float32),
        ] + list(job.shapes),
        scratch_shapes=[
            pltpu.VMEM((dp, 1, whole), jnp.float32),
            pltpu.VMEM((count, 1, whole // tp), jnp.float32),
            pltpu.SemaphoreType.DMA((6,)),
        ] + (GatherChain.scratch() * (PARTS + 2) if weights else []),
        compiler_params=pltpu.CompilerParams(
            collective_id=collective_id, has_side_effects=True, vmem_limit_bytes=VMEM_LIMIT
        ),
        name="enter",
    )(row, modulation, *job.operands)


def adam_update(weight, first, second, grad, rate, decay):
    first_new = BETA_ONE * first + (1.0 - BETA_ONE) * grad
    second_new = BETA_TWO * second + (1.0 - BETA_TWO) * grad * grad
    corrected = (
        first_new
        / (1.0 - BETA_ONE**STEP)
        / (jnp.sqrt(second_new / (1.0 - BETA_TWO**STEP)) + ADAM_EPS)
    )
    weight_new = weight - rate * (corrected + decay * weight)
    return (weight_new, first_new, second_new, weight_new.astype(jnp.bfloat16))


def dot32(form, left, right):
    return jnp.einsum(form, left, right, preferred_element_type=jnp.float32)


def exchange(blocks):
    return lax.all_to_all(blocks, "tensor", split_axis=0, concat_axis=0, tiled=True)


def gather_plain(shard):
    rows, width = shard.shape
    whole = lax.all_gather(shard, ("tensor", "dp"), axis=0, tiled=True)
    return whole.reshape(-1, lax.axis_size("dp") * rows, width)


def scatter_plain(grads):
    kinds, ranks, width, cols = grads.shape
    flat = grads.reshape(kinds, ranks * width, cols)
    summed = lax.psum_scatter(flat, ("tensor", "dp"), scatter_dimension=1, tiled=True)
    return summed.astype(jnp.float32)


def per_device(
    clips, cotangent, timesteps, labels, time_table, class_table,
    attention_weights, attention_first, attention_second,
    ffn_weights, ffn_first, ffn_second,
    modulation_weights, modulation_first, modulation_second,
    bias_vectors, bias_first, bias_second,
):
    layers, kinds, rows, cols = attention_weights.shape
    _, frames, patches, width = clips.shape
    mod_rows = modulation_weights.shape[1]
    bias_cols = bias_vectors.shape[1]
    dp, tp = lax.axis_size("dp"), lax.axis_size("tensor")
    position = lax.axis_index("dp") * tp + lax.axis_index("tensor")
    tokens = frames * patches
    strip = patches // (tp * frames)
    blocks = (tp, frames, frames * strip, width)
    pieces = (tp * frames, frames, strip, width)

    embed = time_table[timesteps] + class_table[labels]
    cond_act = jax.nn.silu(embed).astype(jnp.bfloat16)
    fused = rows % 16 == 0
    shards = [
        (
            pack_heads(attention_weights[layer].astype(jnp.bfloat16)),
            ffn_weights[layer, 0].astype(jnp.bfloat16),
            ffn_weights[layer, 1].astype(jnp.bfloat16),
        )
        for layer in range(layers)
    ]
    low = bias_vectors.astype(jnp.bfloat16).reshape(-1)
    row = jnp.concatenate([cond_act[0], low]).astype(jnp.float32)
    row = jnp.pad(row, (0, -row.shape[0] % 1024)).reshape(-1, 128)
    modulation_low = modulation_weights.astype(jnp.bfloat16)
    modulation_low = jnp.pad(modulation_low, ((0, 0), (0, -mod_rows % 32), (0, 0)))
    gathered, mod, *begun = enter(row, modulation_low, mod_rows, shards[0] if fused else None, 0)
    gathered = gathered.reshape(dp * tp, -1)
    cond_all = gathered[::tp, :width].astype(jnp.bfloat16)
    bias_low = gathered[:, width : width + layers * bias_cols].reshape(dp * tp, layers, bias_cols)
    bias_low = bias_low.transpose(1, 0, 2).reshape(layers, -1)
    cond_rows = lax.dynamic_slice_in_dim(cond_all, position * mod_rows, mod_rows, axis=1)
    cond_rows = jnp.pad(cond_rows, ((0, 0), (0, -mod_rows % 32)))
    mod = mod.reshape(layers, -1)
    mod_width = mod.shape[-1]
    mod = (mod + bias_low[:, -mod_width:]).reshape(layers, 6, width)
    hidden_width = bias_low.shape[1] - mod_width - 4 * width
    bias_up = bias_low[:, 3 * width : 3 * width + hidden_width].reshape(layers, tp, 1, -1)
    bias_out = bias_low[:, None, 2 * width : 3 * width]
    bias_down = bias_low[:, None, 3 * width + hidden_width : 4 * width + hidden_width]
    bias_project = [
        pack_bias(bias_low[layer, :width], bias_low[layer, width : 2 * width], tp) for layer in range(layers)
    ]

    by_patch = lambda v: v.reshape(frames, tp * frames, strip, width).transpose(1, 0, 2, 3)
    cot = by_patch(cotangent[0]).reshape(blocks)
    first = clips[0].reshape(1, frames, patches, width)

    attend = lambda layer, weight, stream, stride, *more: attention_forward(
        weight, stream, mod[layer], bias_project[layer], bias_out[layer], stride, *more
    )
    expand = lambda layer, up, down, middle, *more: ffn_forward(
        up, down, middle.reshape(tokens, width), mod[layer], bias_down[layer], bias_up[layer], *more
    )
    if fused:
        packed_b, up_b, down_b = shards[1]
        attention_a, up_a, down_a = begun
        *heads_a, middle_a, up_a, down_a, attention_b, up_b = attend(
            0, attention_a, first, 0, [FlowJob([up_a, down_a], [packed_b, up_b])], 1
        )
        hidden_a, pushed_a, second, attention_b, up_b, down_b = expand(
            0, up_a, down_a, middle_a, StreamJob(blocks, frames), [FlowJob([attention_b, up_b], [down_b], dp // 8)], 2
        )
        *heads_b, middle_b, down_b = attend(1, attention_b, second, strip, [FlowJob([down_b], [])], 3)
        hidden_b, pushed_b, result, cot = expand(1, up_b, down_b, middle_b, None, [SwapJob(cot)], 4)
    else:
        (attention_a, up_a, down_a), (attention_b, up_b, down_b) = [[gather_plain(v) for v in group] for group in shards]
        *heads_a, middle_a = attend(0, attention_a, first, 0)
        hidden_a, pushed_a, second = expand(0, up_a, down_a, middle_a)
        second = exchange(by_patch(second).reshape(blocks))
        *heads_b, middle_b = attend(1, attention_b, second, strip)
        hidden_b, pushed_b, result = expand(1, up_b, down_b, middle_b)
        cot = exchange(cot)
    middle_a, middle_b = middle_a.reshape(tokens, width), middle_b.reshape(tokens, width)
    result = result.reshape(blocks)
    cot = cot.reshape(tokens, width)

    if fused:
        grad, ffn_grad, *sums_b, result = ffn_backward(
            up_b, down_b, cot, middle_b, pushed_b, hidden_b, mod[1], [SwapJob(result)], 5
        )
        packed_b, *more_b, grad, line_ffn_b = attention_backward(
            attention_b, grad.reshape(blocks), second, heads_b, mod[1], strip,
            StreamJob(blocks, 0), [ScatterJob(ffn_grad, 3 * dp // 8)], 6,
        )
        grad, ffn_grad, *sums_a, done_ffn_b, line_b = ffn_backward(
            up_a, down_a, grad.reshape(pieces), middle_a, pushed_a, hidden_a, mod[0],
            [LineJob(line_ffn_b), ScatterJob(packed_b[None], dp // 4)], 7,
        )
        grad, packed_a, *more_a, done_b, line_ffn_a = attention_backward(
            attention_a, grad.reshape(first.shape), first, heads_a, mod[0], 0, None,
            [LineJob(line_b), ScatterJob(ffn_grad, dp // 4)], 8,
        )
    else:
        result = exchange(result)
        grad, ffn_grad, *sums_b = ffn_backward(up_b, down_b, cot, middle_b, pushed_b, hidden_b, mod[1])
        done_ffn_b = scatter_plain(ffn_grad)
        grad, packed_b, *more_b = attention_backward(
            attention_b, grad.reshape(blocks), second, heads_b, mod[1], strip
        )
        done_b = scatter_plain(packed_b[None])
        grad = exchange(grad.astype(jnp.bfloat16))
        grad, ffn_grad, *sums_a = ffn_backward(up_a, down_a, grad.reshape(pieces), middle_a, pushed_a, hidden_a, mod[0])
        done_ffn_a = scatter_plain(ffn_grad)
        grad, packed_a, *more_a = attention_backward(attention_a, grad.reshape(first.shape), first, heads_a, mod[0], 0)
        done_a = scatter_plain(packed_a[None])
    output = result.reshape(pieces).transpose(1, 0, 2, 3).reshape(clips.shape)
    input_grad = grad.reshape(clips.shape)

    def gather_small(more, sums):
        attention_sums, project_sum = more
        up_sum, low_sums = sums
        return jnp.concatenate(
            [*unpack_bias(project_sum), attention_sums[0], up_sum.reshape(-1), low_sums[0],
             attention_sums[1:].reshape(-1), low_sums[1:].reshape(-1)]
        )

    small = jnp.stack([gather_small(more_a, sums_a), gather_small(more_b, sums_b)])
    token_width = small.shape[1] - mod_width
    *done, small, grad_act = leave(
        small.reshape(tp, -1, 128), modulation_low, token_width,
        *((packed_a, line_ffn_a) if fused else (None, None)), 9,
    )
    if fused:
        done_a, done_ffn_a = done[0][None], done[1]
    small = small.transpose(1, 0, 2, 3).reshape(dp, layers, -1)
    grad_mod_low = small[..., token_width:].astype(jnp.bfloat16)
    grad_bias_all = jnp.concatenate(
        [small[..., :token_width], grad_mod_low.astype(jnp.float32)], axis=-1
    ).sum(axis=0)
    grad_bias = lax.dynamic_slice_in_dim(grad_bias_all, position * bias_cols, bias_cols, axis=1)
    grad_mod_weight = dot32("ck,cle->lke", cond_rows, grad_mod_low)[:, :mod_rows]
    grad_act = lax.dynamic_index_in_dim(
        grad_act[:, :, :mod_rows], lax.axis_index("dp"), axis=1, keepdims=False
    )
    grad_attention = jnp.stack([unpack_heads(done_a[0]), unpack_heads(done_b[0])])
    grad_ffn = jnp.stack([done_ffn_a, done_ffn_b])
    silu_value, silu_pull = jax.vjp(jax.nn.silu, embed)
    cond_grad = silu_pull(grad_act.reshape(1, width))[0]

    return (output, input_grad, cond_grad) + (
        adam_update(attention_weights, attention_first, attention_second, grad_attention, MATRIX_RATE, MATRIX_DECAY)
        + adam_update(ffn_weights, ffn_first, ffn_second, grad_ffn, MATRIX_RATE, MATRIX_DECAY)
        + adam_update(modulation_weights, modulation_first, modulation_second, grad_mod_weight, MATRIX_RATE, MATRIX_DECAY)
        + adam_update(bias_vectors, bias_first, bias_second, grad_bias, VECTOR_RATE, 0.0)
    )


def solution(mesh):
    tokens = P("dp", "tensor", None, None)
    matrix = P(None, None, "dp", "tensor")
    modulation = P(None, BOTH, None)
    vector = P(None, BOTH)
    return jax.shard_map(
        per_device,
        mesh=mesh,
        in_specs=(tokens, tokens, P("dp"), P("dp"), P(), P())
        + (matrix,) * 6 + (modulation,) * 3 + (vector,) * 3,
        out_specs=(tokens, tokens, P("dp", None)) + (matrix,) * 8 + (modulation,) * 4 + (vector,) * 4,
        check_vma=False,
    )
```

```python
from functools import partial

import jax
import jax.numpy as jnp
from jax import lax
from jax.experimental import pallas as pl
from jax.experimental.pallas import tpu as pltpu
from jax.sharding import PartitionSpec as P

HD = 64
PAIR = 128
BLOCK = 256
SPLIT = 4
PARTS = 3
STEP = 10
BETA_ONE = 0.9
BETA_TWO = 0.999
ADAM_EPS = 1e-08
MATRIX_RATE = 0.04
VECTOR_RATE = 0.2
MATRIX_DECAY = 0.1
NORM_EPS = 1e-06
GELU_A = (2.0 / 3.141592653589793) ** 0.5
GELU_B = 0.044715
BLOCKED = -1e30
VMEM_LIMIT = 60 * 1024 * 1024
BOTH = ("dp", "tensor")


def mm(left, right, dims=((1,), (0,))):
    return lax.dot_general(left, right, (dims, ((), ())), preferred_element_type=jnp.float32)


def norm_parts(value):
    average = jnp.mean(value, axis=-1, keepdims=True)
    centred = value - average
    spread = jnp.mean(centred * centred, axis=-1, keepdims=True)
    inverse = lax.rsqrt(spread + NORM_EPS)
    return centred * inverse, inverse


def norm_back(grad, shape, inverse):
    first = jnp.mean(grad, axis=-1, keepdims=True)
    second = jnp.mean(grad * shape, axis=-1, keepdims=True)
    return inverse * (grad - first - shape * second)


def rows_of(ref):
    value = ref[...]
    return value.reshape(-1, value.shape[-1])


def put(ref, value):
    ref[...] = value.reshape(ref.shape).astype(ref.dtype)


def add_rows(ref, index, value):
    ref[pl.ds(index, 1), :] += jnp.sum(value, axis=0, keepdims=True)


def half_masks(rows):
    lane = lax.broadcasted_iota(jnp.int32, (rows, PAIR), 1)
    return lane < HD


def same_patch(tokens, stride):
    row = lax.broadcasted_iota(jnp.int32, (tokens, tokens), 0)
    column = lax.broadcasted_iota(jnp.int32, (tokens, tokens), 1)
    return lax.rem(row, stride) == lax.rem(column, stride)


def swap_halves(value):
    return pltpu.roll(value, HD, 1)


def start_loads(source, target, semaphores):
    for rank in range(target.shape[0]):
        pltpu.make_async_copy(source.at[rank], target.at[rank], semaphores.at[rank]).start()


def wait_loads(target, semaphores, rank):
    pltpu.make_async_copy(target.at[rank], target.at[rank], semaphores.at[rank]).wait()


def softmax_rows(scores, axis):
    raised = jnp.exp(scores - jnp.max(scores, axis=axis, keepdims=True))
    return raised * (1.0 / jnp.sum(raised, axis=axis, keepdims=True))


def attention_forward_kernel(
    stride, hook, source, stream_ref, mod_ref, bias_ref, bias_out_ref,
    project_ref, mixed_ref, branch_ref, middle_ref, weight_ref, semaphores,
):
    ranks = weight_ref.shape[0]

    @pl.when(pl.program_id(0) == 0)
    def _():
        start_loads(source, weight_ref, semaphores)

    stream = rows_of(stream_ref).astype(jnp.float32)
    tokens, width = stream.shape
    shape, _ = norm_parts(stream)
    normed = (shape * (1.0 + mod_ref[1:2]) + mod_ref[0:1]).astype(jnp.bfloat16)
    lower = half_masks(tokens)
    allowed = same_patch(tokens, stride) if stride else None

    @pl.when(pl.program_id(0) == 0)
    def _():
        for rank in range(ranks):
            wait_loads(weight_ref, semaphores, rank)

    def one_head(chosen, key, value):
        scores = mm(chosen.astype(jnp.bfloat16), key, ((1,), (1,)))
        if stride:
            scores = jnp.where(allowed, scores, BLOCKED)
        return mm(softmax_rows(scores, -1).astype(jnp.bfloat16), value)

    branch = None
    for rank in range(ranks):
        hook(rank)
        project = (mm(normed, weight_ref[rank, :, : 5 * PAIR]) + bias_ref[rank]).astype(jnp.bfloat16)
        project_ref[rank] = project.reshape(project_ref.shape[1:])
        query = project[:, :PAIR].astype(jnp.float32) * HD**-0.5
        key, value = project[:, PAIR : 2 * PAIR], project[:, 2 * PAIR : 3 * PAIR]
        first = one_head(jnp.where(lower, query, 0.0), key, value)
        second = one_head(jnp.where(lower, 0.0, query), key, value)
        both = project[:, 3 * PAIR : 4 * PAIR].astype(jnp.float32)
        last = one_head(
            jnp.where(lower, both * HD**-0.5, 0.0),
            swap_halves(both).astype(jnp.bfloat16),
            project[:, 4 * PAIR : 5 * PAIR],
        )
        mixed = jnp.concatenate(
            [jnp.where(lower, 0.0, swap_halves(last)), jnp.where(lower, first, second)], axis=1
        ).astype(jnp.bfloat16)
        mixed_ref[rank] = mixed.reshape(mixed_ref.shape[1:])
        term = mm(mixed, weight_ref[rank, :, 4 * PAIR :], ((1,), (1,)))
        branch = term if branch is None else branch + term
    branch = branch + bias_out_ref[...]
    put(branch_ref, branch)
    put(middle_ref, stream + mod_ref[2:3] * branch)


def gelu_parts(value):
    square = value * value
    bent = jnp.tanh(value * (GELU_A + (GELU_A * GELU_B) * square))
    half = 0.5 * (1.0 + bent)
    slope = half + (0.5 * value) * (1.0 - bent * bent) * (GELU_A + (3.0 * GELU_A * GELU_B) * square)
    return value * half, slope


def ffn_forward_kernel(
    stream, hook, up_source, down_source, middle_ref, mod_ref, bias_ref, bias_up_ref, hidden_ref, branch_ref, *rest
):
    if stream is None:
        result_ref, *rest = rest
    up_ref, down_ref, up_semaphores, down_semaphores = rest
    step = pl.program_id(0)
    ranks = up_ref.shape[0]

    @pl.when(step == 0)
    def _():
        start_loads(up_source, up_ref, up_semaphores)
        start_loads(down_source, down_ref, down_semaphores)

    middle = middle_ref[...]
    shape, _ = norm_parts(middle)
    second = (shape * (1.0 + mod_ref[4:5]) + mod_ref[3:4]).astype(jnp.bfloat16)

    @pl.when(step == 0)
    def _():
        for rank in range(ranks):
            wait_loads(up_ref, up_semaphores, rank)
            wait_loads(down_ref, down_semaphores, rank)

    down = None
    for rank in range(ranks):
        hook(rank)
        hidden = mm(second, up_ref[rank]) + bias_up_ref[rank]
        hidden_ref[rank] = hidden.astype(jnp.bfloat16)
        active, _ = gelu_parts(hidden)
        part = mm(active.astype(jnp.bfloat16), down_ref[rank], ((1,), (1,)))
        down = part if down is None else down + part
    down = down + bias_ref[...]
    branch_ref[...] = down.astype(jnp.bfloat16)
    result = middle + mod_ref[5:6] * down
    if stream is None:
        result_ref[...] = result.astype(result_ref.dtype)
    else:
        stream.put(step, result)


def load_frame(ref, index, chunk):
    if len(ref.shape) == 2:
        return ref[index * chunk : (index + 1) * chunk, :].astype(jnp.float32)
    value = ref[:, index]
    return value.reshape(chunk, value.shape[-1]).astype(jnp.float32)


def ffn_backward_kernel(
    split, hook, up_source, down_source, grad_ref, middle_ref, branch_ref, hidden_ref, mod_ref,
    grad_middle_ref, weight_grad_ref, up_sum_ref, sums_ref,
    up_ref, down_ref, up_semaphores, down_semaphores,
    second_ref, low_ref, low_across_ref, active_ref, slope_ref, total_ref,
):
    step = pl.program_id(0)
    tokens, width = middle_ref.shape
    chunk = tokens // split

    @pl.when(step == 0)
    def _():
        start_loads(up_source, up_ref, up_semaphores)
        start_loads(down_source, down_ref, down_semaphores)
        sums_ref[...] = jnp.zeros_like(sums_ref)
        for index in range(split):
            rows = slice(index * chunk, (index + 1) * chunk)
            grad = load_frame(grad_ref, index, chunk)
            low = (mod_ref[5:6] * grad).astype(jnp.bfloat16)
            low_ref[rows, :] = low
            low_across_ref[:, rows] = low.T
            add_rows(sums_ref, 0, low.astype(jnp.float32))
            add_rows(sums_ref, 3, grad * branch_ref[rows, :].astype(jnp.float32))
            shape, _ = norm_parts(middle_ref[rows, :])
            second = (shape * (1.0 + mod_ref[4:5]) + mod_ref[3:4]).astype(jnp.bfloat16)
            second_ref[:, rows] = second.T

    up_sum_ref[...] = jnp.zeros_like(up_sum_ref)
    wait_loads(up_ref, up_semaphores, step)
    wait_loads(down_ref, down_semaphores, step)

    for index in range(split):
        hook(index)
        rows = slice(index * chunk, (index + 1) * chunk)
        active, slope = gelu_parts(hidden_ref[0, rows, :].astype(jnp.float32))
        active_ref[rows, :] = active.astype(jnp.bfloat16)
        low = (mm(low_ref[rows, :], down_ref[step]) * slope).astype(jnp.bfloat16)
        slope_ref[rows, :] = low
        up_sum_ref[0] += jnp.sum(low.astype(jnp.float32), axis=0, keepdims=True)
        part = mm(low, up_ref[step], ((1,), (1,)))
        total_ref[rows, :] = jnp.where(step == 0, 0.0, total_ref[rows, :]) + part

    def weights(index, carry):
        part = pl.ds(pl.multiple_of(index * BLOCK, BLOCK), BLOCK)
        weight_grad_ref[0, 0, part, :] = mm(second_ref[part, :], slope_ref[...]).astype(
            jnp.bfloat16
        )
        weight_grad_ref[1, 0, part, :] = mm(low_across_ref[part, :], active_ref[...]).astype(
            jnp.bfloat16
        )
        return carry

    lax.fori_loop(0, width // BLOCK, weights, 0)

    @pl.when(step == pl.num_programs(0) - 1)
    def _():
        for index in range(split):
            rows = slice(index * chunk, (index + 1) * chunk)
            shape, inverse = norm_parts(middle_ref[rows, :])
            grad = total_ref[rows, :]
            add_rows(sums_ref, 1, grad)
            add_rows(sums_ref, 2, grad * shape)
            back = norm_back(grad * (1.0 + mod_ref[4:5]), shape, inverse)
            grad_middle_ref[rows, :] = load_frame(grad_ref, index, chunk) + back


def attention_backward_kernel(
    stride, swap, hook, source, grad_ref, stream_ref, project_ref, mixed_ref, branch_ref, mod_ref, *refs
):
    if swap is None:
        grad_stream_ref, *refs = refs
    (weight_grad_ref, sums_ref, project_sum_ref,
     weight_ref, semaphores, left_ref, right_ref, outer_ref) = refs
    step = pl.program_id(0)
    ranks = weight_ref.shape[0]

    @pl.when(step == 0)
    def _():
        start_loads(source, weight_ref, semaphores)
        sums_ref[...] = jnp.zeros_like(sums_ref)
        project_sum_ref[...] = jnp.zeros_like(project_sum_ref)

    grad_middle = rows_of(grad_ref)
    tokens, width = grad_middle.shape
    stream = rows_of(stream_ref).astype(jnp.float32)
    shape, inverse = norm_parts(stream)
    rows = pl.ds(pl.multiple_of(step * tokens, tokens), tokens)
    normed = (shape * (1.0 + mod_ref[1:2]) + mod_ref[0:1]).astype(jnp.bfloat16)
    low = (mod_ref[2:3] * grad_middle).astype(jnp.bfloat16)
    left_ref[0, :, rows] = normed.T
    left_ref[1, :, rows] = low.T
    add_rows(sums_ref, 0, low.astype(jnp.float32))
    add_rows(sums_ref, 3, grad_middle * rows_of(branch_ref).astype(jnp.float32))
    lower = half_masks(tokens)
    allowed = same_patch(tokens, stride) if stride else None
    scale = HD**-0.5

    @pl.when(step == 0)
    def _():
        for rank in range(ranks):
            wait_loads(weight_ref, semaphores, rank)

    def one_head(chosen, key, value, taken):
        scores = mm(key, chosen.astype(jnp.bfloat16), ((1,), (1,)))
        if stride:
            scores = jnp.where(allowed, scores, BLOCKED)
        probs = softmax_rows(scores, 0)
        grad_probs = mm(value, taken.astype(jnp.bfloat16), ((1,), (1,)))
        inner = jnp.sum(grad_probs * probs, axis=0, keepdims=True)
        return probs.astype(jnp.bfloat16), (probs * (grad_probs - inner)).astype(jnp.bfloat16)

    grad_normed = None
    for rank in range(ranks):
        hook(rank)
        project = project_ref[rank].reshape(tokens, 5 * PAIR)
        mixed = mixed_ref[rank].reshape(tokens, 2 * PAIR)
        outer_ref[rank, rows, :] = mixed
        grad_mixed = mm(low, weight_ref[rank, :, 4 * PAIR :]).astype(jnp.bfloat16)
        query, key, value = (project[:, n * PAIR : (n + 1) * PAIR] for n in range(3))
        query_wide = query.astype(jnp.float32) * scale
        pair = grad_mixed[:, PAIR:]
        pair_wide = pair.astype(jnp.float32)
        outs = []
        for keep in (lower, ~lower):
            probs, grad_scores = one_head(
                jnp.where(keep, query_wide, 0.0), key, value, jnp.where(keep, pair_wide, 0.0)
            )
            outs.append(
                (mm(grad_scores, key, ((0,), (0,))), mm(grad_scores, query), mm(probs, pair))
            )
        parts = [
            jnp.where(lower, one, two) * factor
            for one, two, factor in zip(outs[0], outs[1], (scale, scale, 1.0))
        ]
        both = project[:, 3 * PAIR : 4 * PAIR].astype(jnp.float32)
        swapped = swap_halves(both).astype(jnp.bfloat16)
        single = swap_halves(grad_mixed[:, :PAIR].astype(jnp.float32))
        probs, grad_scores = one_head(
            jnp.where(lower, both * scale, 0.0),
            swapped,
            project[:, 4 * PAIR :],
            jnp.where(lower, single, 0.0),
        )
        parts.append(
            jnp.where(lower, mm(grad_scores, swapped, ((0,), (0,))), mm(grad_scores, swapped)) * scale
        )
        parts.append(jnp.where(lower, mm(probs, single.astype(jnp.bfloat16)), 0.0))
        whole = jnp.concatenate(parts, axis=1).astype(jnp.bfloat16)
        right_ref[rank, rows, :] = whole
        add_rows(project_sum_ref, rank, whole.astype(jnp.float32))
        term = mm(whole, weight_ref[rank, :, : 5 * PAIR], ((1,), (1,)))
        grad_normed = term if grad_normed is None else grad_normed + term
    add_rows(sums_ref, 1, grad_normed)
    add_rows(sums_ref, 2, grad_normed * shape)
    back = norm_back(grad_normed * (1.0 + mod_ref[1:2]), shape, inverse)
    if swap is None:
        put(grad_stream_ref, grad_middle + back)
    else:
        swap.put(step, grad_middle + back)

    @pl.when(step == pl.num_programs(0) - 1)
    def _():
        def weights(rank, carry):
            def block(index, inner):
                part = pl.ds(pl.multiple_of(index * BLOCK, BLOCK), BLOCK)
                inside = mm(left_ref[0, part, :], right_ref[rank])
                outside = mm(left_ref[1, part, :], outer_ref[rank])
                weight_grad_ref[rank, part, : 4 * PAIR] = inside[:, : 4 * PAIR].astype(jnp.bfloat16)
                weight_grad_ref[rank, part, 4 * PAIR : 5 * PAIR] = (
                    inside[:, 4 * PAIR :] + outside[:, :PAIR]
                ).astype(jnp.bfloat16)
                weight_grad_ref[rank, part, 5 * PAIR :] = outside[:, PAIR:].astype(jnp.bfloat16)
                return inner

            return lax.fori_loop(0, width // BLOCK, block, carry)

        lax.fori_loop(0, ranks, weights, 0)


def fixed(shape):
    return pl.BlockSpec(shape, lambda step: (0,) * len(shape), pipeline_mode=pl.Buffered(1))


def cost(flops, moved, raised=0):
    return pl.CostEstimate(flops=int(flops), bytes_accessed=int(moved), transcendentals=int(raised))


def group_spec(shape):
    return pl.BlockSpec((shape[0], 1, shape[2], shape[3]), lambda step: (0, step, 0, 0))


def rank_spec(shape):
    return pl.BlockSpec((shape[0], shape[1], 1) + shape[3:], lambda step: (0, 0, step, 0, 0))


def attention_forward(weight, stream, mod, bias, bias_out, stride, jobs=(), collective_id=None):
    shape = stream.shape
    width = shape[-1]
    ranks = bias.shape[0]
    tokens = shape[0] * shape[1] * shape[2]
    spec = group_spec(shape)
    low = jax.ShapeDtypeStruct(shape, jnp.bfloat16)
    wide = jax.ShapeDtypeStruct(shape, jnp.float32)
    project = jax.ShapeDtypeStruct((ranks,) + shape[:3] + (5 * PAIR,), jnp.bfloat16)
    mixed = jax.ShapeDtypeStruct((ranks,) + shape[:3] + (2 * PAIR,), jnp.bfloat16)
    return call(
        partial(attention_forward_kernel, stride),
        shape[1],
        [weight, stream, mod, bias, bias_out],
        anywhere(1) + [spec, fixed(mod.shape), fixed(bias.shape), fixed(bias_out.shape)],
        [project, mixed, low, wide],
        [rank_spec(project.shape), rank_spec(mixed.shape), spec, spec],
        [pltpu.VMEM((ranks, width, 6 * PAIR), jnp.bfloat16), pltpu.SemaphoreType.DMA((ranks,))],
        jobs,
        collective_id,
        cost(8 * tokens * width * width * 1.5, tokens * width * 16),
        "attention_forward",
    )


def ffn_weights_scratch(ranks, width, part):
    return [
        pltpu.VMEM((ranks, width, part), jnp.bfloat16),
        pltpu.VMEM((ranks, width, part), jnp.bfloat16),
        pltpu.SemaphoreType.DMA((ranks,)),
        pltpu.SemaphoreType.DMA((ranks,)),
    ]


def ffn_forward(up, down, middle, mod, bias_down, bias_up, stream=None, jobs=(), collective_id=None):
    tokens, width = middle.shape
    ranks, _, part = bias_up.shape
    chunk = tokens // SPLIT
    block = pl.BlockSpec((chunk, width), lambda step: (step, 0))
    result = [jax.ShapeDtypeStruct((tokens, width), jnp.bfloat16)] if stream is None else []
    return call(
        partial(ffn_forward_kernel, stream),
        SPLIT,
        [up, down, middle, mod, bias_down, bias_up],
        anywhere(2) + [block, fixed(mod.shape), fixed(bias_down.shape), fixed(bias_up.shape)],
        [
            jax.ShapeDtypeStruct((ranks, tokens, part), jnp.bfloat16),
            jax.ShapeDtypeStruct((tokens, width), jnp.bfloat16),
        ] + result,
        [pl.BlockSpec((ranks, chunk, part), lambda step: (0, step, 0)), block] + [block] * len(result),
        ffn_weights_scratch(ranks, width, part),
        ([] if stream is None else [stream]) + list(jobs),
        collective_id,
        cost(4.8 * tokens * width * ranks * part, tokens * width * 14, tokens * ranks * part),
        "ffn_forward",
    )


def ffn_backward(up, down, grad, middle, branch, hidden, mod, jobs=(), collective_id=None):
    tokens, width = middle.shape
    ranks, _, part = hidden.shape
    whole = fixed((tokens, width))
    return call(
        partial(ffn_backward_kernel, SPLIT),
        ranks,
        [up, down, grad, middle, branch, hidden, mod],
        anywhere(2) + [
            fixed(grad.shape), whole, whole,
            pl.BlockSpec((1, tokens, part), lambda step: (step, 0, 0)),
            fixed(mod.shape),
        ],
        [
            jax.ShapeDtypeStruct((tokens, width), jnp.float32),
            jax.ShapeDtypeStruct((2, ranks, width, part), jnp.bfloat16),
            jax.ShapeDtypeStruct((ranks, 1, part), jnp.float32),
            jax.ShapeDtypeStruct((4, width), jnp.float32),
        ],
        [
            whole,
            pl.BlockSpec((2, 1, width, part), lambda step: (0, step, 0, 0)),
            pl.BlockSpec((1, 1, part), lambda step: (step, 0, 0)),
            fixed((4, width)),
        ],
        ffn_weights_scratch(ranks, width, part) + [
            pltpu.VMEM((width, tokens), jnp.bfloat16),
            pltpu.VMEM((tokens, width), jnp.bfloat16),
            pltpu.VMEM((width, tokens), jnp.bfloat16),
            pltpu.VMEM((tokens, part), jnp.bfloat16),
            pltpu.VMEM((tokens, part), jnp.bfloat16),
            pltpu.VMEM((tokens, width), jnp.float32),
        ],
        jobs,
        collective_id,
        cost(9.6 * tokens * width * ranks * part, tokens * width * 20, tokens * ranks * part),
        "ffn_backward",
    )


def attention_backward(weight, grad, stream, saved, mod, stride, swap=None, jobs=(), collective_id=None):
    project, mixed, branch = saved
    shape = stream.shape
    width = shape[-1]
    ranks = project.shape[0]
    tokens = shape[0] * shape[1] * shape[2]
    spec = group_spec(shape)
    result = [jax.ShapeDtypeStruct(shape, jnp.float32)] if swap is None else []
    return call(
        partial(attention_backward_kernel, stride, swap),
        shape[1],
        [weight, grad, stream, project, mixed, branch, mod],
        anywhere(1) + [
            spec, spec, rank_spec(project.shape), rank_spec(mixed.shape), spec, fixed(mod.shape),
        ],
        result + [
            jax.ShapeDtypeStruct((ranks, width, 6 * PAIR), jnp.bfloat16),
            jax.ShapeDtypeStruct((4, width), jnp.float32),
            jax.ShapeDtypeStruct((ranks, 5 * PAIR), jnp.float32),
        ],
        [spec] * len(result) + [
            fixed((ranks, width, 6 * PAIR)), fixed((4, width)), fixed((ranks, 5 * PAIR)),
        ],
        [
            pltpu.VMEM((ranks, width, 6 * PAIR), jnp.bfloat16),
            pltpu.SemaphoreType.DMA((ranks,)),
            pltpu.VMEM((2, width, tokens), jnp.bfloat16),
            pltpu.VMEM((ranks, tokens, 5 * PAIR), jnp.bfloat16),
            pltpu.VMEM((ranks, tokens, 2 * PAIR), jnp.bfloat16),
        ],
        ([] if swap is None else [swap]) + list(jobs),
        collective_id,
        cost(16 * tokens * width * width * 1.5, tokens * width * 20),
        "attention_backward",
    )


def pack_heads(block):
    query, key, value, outer = block
    return jnp.concatenate(
        [query[:, :PAIR], key[:, :PAIR], value[:, :PAIR], query[:, PAIR:], key[:, PAIR:],
         value[:, PAIR:], outer[:, PAIR:], outer[:, :PAIR]], axis=1
    )


def unpack_heads(packed):
    part = lambda start, size: packed[:, start : start + size]
    join = lambda first, last: jnp.concatenate([part(first, PAIR), part(last, HD)], axis=1)
    return jnp.stack(
        [join(0, 3 * PAIR), join(PAIR, 3 * PAIR + HD), join(2 * PAIR, 4 * PAIR), join(5 * PAIR, 4 * PAIR + HD)]
    )


def pack_bias(query, value, ranks):
    query, value = query.reshape(ranks, -1), value.reshape(ranks, -1)
    none = jnp.zeros((ranks, PAIR), query.dtype)
    return jnp.concatenate(
        [query[:, :PAIR], none, value[:, :PAIR], query[:, PAIR:], none[:, :HD], value[:, PAIR:], none[:, :HD]],
        axis=1,
    )[:, None]


def unpack_bias(sums):
    query = jnp.concatenate([sums[:, :PAIR], sums[:, 3 * PAIR : 3 * PAIR + HD]], axis=1)
    value = jnp.concatenate([sums[:, 2 * PAIR : 3 * PAIR], sums[:, 4 * PAIR : 4 * PAIR + HD]], axis=1)
    return query.reshape(-1), value.reshape(-1)


def place():
    return lax.axis_index("dp"), lax.axis_index("tensor"), lax.axis_size("dp"), lax.axis_size("tensor")


def greet_all():
    device, rank, dp, tp = place()
    me, count = device * tp + rank, dp * tp
    barrier = pltpu.get_barrier_semaphore()

    def greet(index, carry):
        peer = lax.rem(me + index, count)
        pl.semaphore_signal(
            barrier, inc=1, device_id=(peer // tp, lax.rem(peer, tp)), device_id_type=pl.DeviceIdType.MESH
        )
        return carry

    lax.fori_loop(1, count, greet, 0)
    pl.semaphore_wait(barrier, count - 1)


def push(source, target, send, receive, device, rank):
    pltpu.make_async_remote_copy(
        src_ref=source, dst_ref=target, send_sem=send, recv_sem=receive,
        device_id=(device, rank), device_id_type=pl.DeviceIdType.MESH,
    ).start()


def wait_bytes(ref, semaphore):
    pltpu.make_async_copy(ref, ref, semaphore).wait()


class Where:
    def __init__(self):
        device, rank = lax.axis_index("dp"), lax.axis_index("tensor")
        self.count = lax.axis_size("dp") // 2
        self.device, self.rank = device, rank
        self.far, self.side = device // 2, lax.rem(device, 2)
        self.row, self.core = rank // 2, lax.rem(rank, 2)
        self.other_side = self.far * 2 + 1 - self.side
        self.other_row = (1 - self.row) * 2 + self.core
        self.other_core = self.row * 2 + 1 - self.core

    def ahead(self, step):
        return lax.rem(self.far + step, self.count)

    def line(self, step):
        return self.ahead(step) * 2 + self.side


def greet_neighbours(here):
    barrier = pltpu.get_barrier_semaphore()
    peers = [(here.other_side, here.rank), (here.device, here.other_row), (here.device, here.other_core)]
    peers += [(here.line(step), here.rank) for step in range(1, here.count)]
    for peer in peers:
        pl.semaphore_signal(barrier, inc=1, device_id=peer, device_id_type=pl.DeviceIdType.MESH)
    pl.semaphore_wait(barrier, len(peers))


def add_into(target, left, right):
    target[...] = (left[...].astype(jnp.float32) + right[...].astype(jnp.float32)).astype(target.dtype)


class ScatterChain:
    def __init__(self, here, source, line, lead, scratch):
        self.here, self.source, self.line, self.lead = here, source, line, lead
        self.keep, self.land_core, self.first_one, self.last_one, self.first_two, self.last_two, self.semaphores = scratch
        self.rows = line.shape[1]

    @staticmethod
    def scratch(width, columns, dp, lead):
        rows, far = width // dp, dp // 2
        low = lambda *shape: pltpu.VMEM(shape + (columns,), jnp.bfloat16)
        return [
            low(2, width), low(2, width),
            low(2, lead, rows), low(2 * (far - lead) * rows), low(lead, rows), low(far - lead, rows),
            pltpu.SemaphoreType.DMA((6, 2)),
        ]

    def chunk(self, row, far, side):
        return self.keep.at[row, pl.ds(pl.multiple_of((far * 2 + side) * self.rows, self.rows), self.rows)]

    def send(self, slot, source, target, device, rank):
        push(source, target, self.semaphores.at[slot, 0], self.semaphores.at[slot, 1], device, rank)

    def arrived(self, slot, ref):
        wait_bytes(ref, self.semaphores.at[slot, 1])

    def left(self, slot, ref):
        wait_bytes(ref, self.semaphores.at[slot, 0])

    def stage_core(self):
        here = self.here
        for row in range(2):
            pltpu.make_async_copy(
                self.source.at[row * 2 + here.core], self.keep.at[row], self.semaphores.at[5, 0]
            ).start()
            self.send(0, self.source.at[row * 2 + 1 - here.core], self.land_core.at[row], here.device, here.other_core)

    def stage_one(self):
        here = self.here
        wait_bytes(self.keep, self.semaphores.at[5, 0])
        self.arrived(0, self.land_core)

        def one(index, carry):
            rows = pl.ds(pl.multiple_of(index * self.rows, self.rows), self.rows)
            for row in range(2):
                add_into(self.keep.at[row, rows], self.keep.at[row, rows], self.land_core.at[row, rows])
            return carry

        lax.fori_loop(0, here.count * 2, one, 0)
        for row in range(2):
            for far in range(self.lead):
                self.send(
                    1, self.chunk(row, far, 1 - here.side), self.first_one.at[row, far], here.other_side, here.rank
                )
        start, size = self.lead * 2 * self.rows, (here.count - self.lead) * 2 * self.rows
        self.send(2, self.keep.at[1 - here.row, pl.ds(start, size)], self.last_one, here.device, here.other_row)

    def stage_two(self):
        here, lead = self.here, self.lead
        self.arrived(1, self.first_one)
        for row in range(2):
            for far in range(lead):
                mine = self.chunk(row, far, here.side)
                add_into(mine, mine, self.first_one.at[row, far])
        for far in range(lead):
            self.send(3, self.chunk(1 - here.row, far, here.side), self.first_two.at[far], here.device, here.other_row)
        self.arrived(2, self.last_one)
        for far in range(lead, here.count):
            for side in range(2):
                mine = self.chunk(here.row, far, side)
                add_into(mine, mine, self.last_one.at[pl.ds(((far - lead) * 2 + side) * self.rows, self.rows)])
        for far in range(lead, here.count):
            self.send(
                4, self.chunk(here.row, far, 1 - here.side), self.last_two.at[far - lead], here.other_side, here.rank
            )

    def merge(self):
        here = self.here
        self.arrived(3, self.first_two)
        self.arrived(4, self.last_two)
        for far in range(here.count):
            land = self.first_two.at[far] if far < self.lead else self.last_two.at[far - self.lead]
            add_into(self.line.at[far], self.chunk(here.row, far, here.side), land)

    def finish(self):
        self.left(0, self.land_core)
        self.left(1, self.first_one)
        self.left(2, self.last_one)
        self.left(3, self.first_two)
        self.left(4, self.last_two)


class LineChain:
    def __init__(self, here, line, out, land, semaphores):
        self.here, self.line, self.out, self.land, self.semaphores = here, line, out, land, semaphores

    @staticmethod
    def scratch(far, rows, columns):
        return [pltpu.VMEM((far - 1, rows, columns), jnp.bfloat16), pltpu.SemaphoreType.DMA((2,))]

    def start(self):
        here = self.here
        for step in range(1, here.count):
            push(
                self.line.at[here.ahead(step)], self.land.at[step - 1], self.semaphores.at[0],
                self.semaphores.at[1], here.line(step), here.rank,
            )

    def finish(self):
        wait_bytes(self.land, self.semaphores.at[1])
        total = self.line[self.here.far].astype(jnp.float32)
        for step in range(1, self.here.count):
            total = total + self.land[step - 1].astype(jnp.float32)
        self.out[...] = total
        wait_bytes(self.land, self.semaphores.at[0])


def leave_kernel(mod_start, *refs):
    refs = list(refs)
    scattering = len(refs) > 10
    source, begun = (refs.pop(0), refs.pop(0)) if scattering else (None, None)
    small_ref, modulation_ref, *refs = refs
    out, begun_out = (refs.pop(0), refs.pop(0)) if scattering else (None, None)
    sum_ref, act_ref, land_ref, acting_ref, semaphores, *space = refs
    device, rank, dp, tp = place()
    me, count = device * tp + rank, dp * tp
    greet_all()
    if scattering:
        here = Where()
        line_ref, *space = space
        pick = lambda number: [space.pop(0) for _ in range(number)]
        chains, trails = [], []
        for index in range(PARTS):
            size = out.shape[1] // PARTS
            part = pl.ds(index * size, size)
            line = line_ref.at[index]
            chains.append(ScatterChain(here, source.at[:, :, part], line, here.count // 2, pick(7)))
            trails.append(LineChain(here, line, out.at[:, part], *pick(2)))
        others = [LineChain(here, begun.at[kind], begun_out.at[kind], *pick(2)) for kind in range(begun.shape[0])]
        for chain in chains:
            chain.stage_core()
    for step in range(1, tp):
        there = lax.rem(rank + step, tp)
        push(small_ref.at[there], land_ref.at[rank], semaphores.at[0], semaphores.at[1], device, there)
    land_ref[rank] = small_ref[rank]
    wait_bytes(land_ref.at[pl.ds(0, tp - 1)], semaphores.at[1])
    mine = sum_ref.at[rank]
    mine[device] = jnp.sum(land_ref[...], axis=0)

    def one(step, carry):
        push(mine.at[device], mine.at[device], semaphores.at[2], semaphores.at[3], lax.rem(device + step, dp), rank)
        return carry

    lax.fori_loop(1, dp, one, 0)
    if scattering:
        for chain in others:
            chain.start()
    wait_bytes(mine.at[pl.ds(0, dp - 1)], semaphores.at[3])
    for step in range(1, tp):
        push(mine, mine, semaphores.at[4], semaphores.at[5], device, lax.rem(rank + step, tp))
    if scattering:
        for chain in chains:
            chain.stage_one()
    wait_bytes(sum_ref.at[pl.ds(0, tp - 1)], semaphores.at[5])
    layers, padded, columns = modulation_ref.shape
    lines = sum_ref.shape[2]
    total = jnp.zeros((dp, padded), jnp.float32)
    for layer in range(layers):
        for index in range(columns // PAIR):
            line = layer * (tp * lines // layers) + mod_start // PAIR + index
            low = sum_ref[line // lines, :, line % lines, :].astype(jnp.bfloat16)
            total += mm(low, modulation_ref[layer, :, index * PAIR : (index + 1) * PAIR], ((1,), (1,)))
    acting_ref[...] = jnp.concatenate([total, jnp.zeros((dp, PAIR - padded), jnp.float32)], axis=1)
    act_ref[me] = acting_ref[...]

    def tell(index, carry):
        peer = lax.rem(me + index, count)
        push(acting_ref, act_ref.at[me], semaphores.at[6], semaphores.at[7], peer // tp, lax.rem(peer, tp))
        return carry

    lax.fori_loop(1, count, tell, 0)
    if scattering:
        for chain in chains:
            chain.stage_two()
        for chain, line in zip(chains, trails):
            chain.merge()
            line.start()
        for chain in others:
            chain.finish()
    wait_bytes(act_ref.at[pl.ds(0, count - 1)], semaphores.at[7])
    wait_bytes(act_ref.at[pl.ds(0, count - 1)], semaphores.at[6])
    wait_bytes(land_ref.at[pl.ds(0, tp - 1)], semaphores.at[0])
    wait_bytes(mine.at[pl.ds(0, dp - 1)], semaphores.at[2])
    wait_bytes(sum_ref.at[pl.ds(0, tp - 1)], semaphores.at[4])
    if scattering:
        for chain in chains + trails:
            chain.finish()


def leave(small, modulation, mod_start, grads, begun, collective_id):
    tp, lines, lanes = small.shape
    dp = lax.axis_size("dp")
    inside = pl.BlockSpec(memory_space=pltpu.VMEM)
    shapes, space, extra = [], [], []
    if grads is not None:
        _, width, columns = grads.shape
        rows, far, part = width // dp, dp // 2, columns // PARTS
        kinds = begun.shape[0]
        extra = [grads, begun]
        shapes = [
            jax.ShapeDtypeStruct((rows, columns), jnp.float32),
            jax.ShapeDtypeStruct((kinds, rows, columns), jnp.float32),
        ]
        space = [pltpu.VMEM((PARTS, far, rows, part), jnp.bfloat16)]
        for _ in range(PARTS):
            space += ScatterChain.scratch(width, part, dp, far // 2) + LineChain.scratch(far, rows, part)
        space += LineChain.scratch(far, rows, columns) * kinds
    return pl.pallas_call(
        partial(leave_kernel, mod_start),
        in_specs=[pl.BlockSpec(memory_space=pl.ANY), inside][: len(extra)] + [inside, inside],
        out_specs=[inside] * (len(shapes) + 2),
        out_shape=shapes + [
            jax.ShapeDtypeStruct((tp, dp, lines, lanes), jnp.float32),
            jax.ShapeDtypeStruct((dp * tp, dp, lanes), jnp.float32),
        ],
        scratch_shapes=[
            pltpu.VMEM((tp, lines, lanes), jnp.float32),
            pltpu.VMEM((dp, lanes), jnp.float32),
            pltpu.SemaphoreType.DMA((8,)),
        ] + space,
        compiler_params=pltpu.CompilerParams(
            collective_id=collective_id, has_side_effects=True, vmem_limit_bytes=VMEM_LIMIT
        ),
        name="leave",
    )(*extra, small, modulation)


class GatherChain:
    def __init__(self, here, source, out, semaphores, half=None):
        self.here, self.source, self.out, self.semaphores = here, source, out, semaphores
        self.rows = out.shape[1] // (2 * here.count)
        self.half = here.count // 2 if half is None else half

    @staticmethod
    def scratch():
        return [pltpu.SemaphoreType.DMA((9, 2))]

    def piece(self, rank, far, side):
        rows = pl.ds(pl.multiple_of((far * 2 + side) * self.rows, self.rows), self.rows)
        return self.out.at[rank, rows]

    def send(self, slot, source, target, device, rank):
        push(source, target, self.semaphores.at[slot, 0], self.semaphores.at[slot, 1], device, rank)

    def wait(self, slot, way, pieces):
        wait_bytes(self.out.at[0, pl.ds(0, pieces * self.rows)], self.semaphores.at[slot, way])

    def stage_line(self):
        here = self.here
        mine = self.piece(here.rank, here.far, here.side)
        pltpu.make_async_copy(self.source, mine, self.semaphores.at[8, 0]).start()
        for step in range(1, here.count):
            self.send(0, self.source, mine, here.line(step), here.rank)

    def line_arrived(self):
        self.wait(8, 0, 1)
        self.wait(0, 1, self.here.count - 1)

    def line_left(self):
        self.wait(0, 0, self.here.count - 1)

    def stage_near(self):
        here = self.here
        for far in range(here.count):
            mine = self.piece(here.rank, far, here.side)
            self.send(1, mine, mine, here.other_side, here.rank)
            self.send(2, mine, mine, here.device, here.other_row)
        for far in range(here.count):
            mine = self.piece(here.rank, far, here.side)
            self.send(3, mine, mine, here.device, here.other_core)

    def stage_across(self):
        here, count = self.here, self.here.count
        self.wait(1, 1, count)
        for far in range(self.half):
            other = self.piece(here.rank, far, 1 - here.side)
            self.send(4, other, other, here.device, here.other_row)
        self.wait(2, 1, count)
        for far in range(self.half, count):
            other = self.piece(here.other_row, far, here.side)
            self.send(5, other, other, here.other_side, here.rank)
        for far in range(count):
            for other in (self.piece(here.rank, far, 1 - here.side), self.piece(here.other_row, far, here.side)):
                self.send(6, other, other, here.device, here.other_core)

    def stage_core(self):
        here, count = self.here, self.here.count
        self.wait(4, 1, self.half)
        self.wait(5, 1, count - self.half)
        for far in range(count):
            other = self.piece(here.other_row, far, 1 - here.side)
            self.send(7, other, other, here.device, here.other_core)

    def finish(self):
        count, half = self.here.count, self.half
        self.wait(3, 1, count)
        self.wait(6, 1, 2 * count)
        self.wait(7, 1, count)
        for slot, pieces in ((1, count), (2, count), (3, count), (4, half), (5, count - half), (6, 2 * count), (7, count)):
            self.wait(slot, 0, pieces)


class Job:
    operands, sources, shapes, specs, aliases, space = (), None, (), (), {}, ()
    stages, last = {}, ()


def anywhere(count):
    return [pl.BlockSpec(memory_space=pl.ANY)] * count


class ScatterJob(Job):
    def __init__(self, grads, lead):
        _, _, width, columns = grads[0][0].shape
        dp = lax.axis_size("dp")
        self.lead, self.kinds = lead, [kind for _, kind in grads]
        shape = (len(grads), dp // 2, width // dp, columns)
        self.operands = [array for array, _ in grads]
        self.shapes, self.specs = [jax.ShapeDtypeStruct(shape, jnp.bfloat16)], [fixed(shape)]
        self.space = ScatterChain.scratch(width, columns, dp, lead) * len(grads)

    def bind(self, here, inputs, outputs, space):
        size = len(space) // len(inputs)
        chains = [
            ScatterChain(
                here, source.at[kind], outputs[0].at[index], self.lead, space[index * size : (index + 1) * size]
            )
            for index, (source, kind) in enumerate(zip(inputs, self.kinds))
        ]
        one = chains[0]
        if len(chains) == 1:
            self.stages = {(0, 0): [one.stage_core], (0, 3): [one.stage_one], (2, 1): [one.stage_two]}
            self.last = [one.merge, one.finish]
            return
        two = chains[1]
        self.stages = {
            (0, 0): [one.stage_core, two.stage_core], (0, 2): [one.stage_one], (0, 3): [two.stage_one],
            (2, 1): [one.stage_two], (3, 1): [two.stage_two],
        }
        self.last = [one.merge, two.merge, one.finish, two.finish]


class LineJob(Job):
    def __init__(self, line):
        kinds, far, rows, columns = line.shape
        shape = (kinds, rows, columns)
        self.operands, self.sources = [line], [fixed(line.shape)]
        self.shapes, self.specs = [jax.ShapeDtypeStruct(shape, jnp.float32)], [fixed(shape)]
        self.space = LineChain.scratch(far, rows, columns) * kinds

    def bind(self, here, inputs, outputs, space):
        chains = [
            LineChain(here, inputs[0].at[kind], outputs[0].at[kind], *space[2 * kind : 2 * kind + 2])
            for kind in range(outputs[0].shape[0])
        ]
        self.stages = {(0, 0): [chain.start for chain in chains]}
        self.last = [chain.finish for chain in chains]


class FlowJob(Job):
    def __init__(self, spread, lines, half=None, late=()):
        dp, tp = lax.axis_size("dp"), lax.axis_size("tensor")
        self.counts, self.half = (len(spread), len(late)), half
        shards = list(late) + list(lines)
        self.operands = list(spread) + shards
        self.shapes = [jax.ShapeDtypeStruct(v.shape, v.dtype) for v in spread]
        self.shapes += [jax.ShapeDtypeStruct((tp, dp * v.shape[0], v.shape[1]), v.dtype) for v in shards]
        self.specs = anywhere(len(self.shapes))
        self.aliases = {index: index for index in range(len(spread))}
        self.space = GatherChain.scratch() * len(self.shapes)

    def bind(self, here, inputs, outputs, space):
        chains = [GatherChain(here, *refs, self.half) for refs in zip(inputs, outputs, space)]
        first, late = self.counts
        spread, late, lines = chains[:first], chains[first : first + late], chains[first + late :]
        self.stages = {
            (0, 0): [chain.stage_near for chain in spread] + [chain.stage_line for chain in late + lines],
            (3, 0): [chain.stage_across for chain in spread],
        }
        for chain in late:
            self.stages[3, 0] += [chain.line_arrived, chain.stage_near]
        self.last = [chain.stage_across for chain in late]
        self.last += [chain.stage_core for chain in spread + late]
        self.last += [chain.finish for chain in spread + late]
        self.last += [chain.line_arrived for chain in lines]
        self.last += [chain.line_left for chain in late + lines]


class SwapJob(Job):
    def __init__(self, blocks):
        self.operands = [blocks]
        self.shapes, self.specs = [jax.ShapeDtypeStruct(blocks.shape, blocks.dtype)], anywhere(1)
        self.space = [pltpu.SemaphoreType.DMA((3,))]

    def bind(self, here, inputs, outputs, space):
        source, out, semaphores = inputs[0], outputs[0], space[0]
        ranks = out.shape[0]

        def start():
            pltpu.make_async_copy(source.at[here.rank], out.at[here.rank], semaphores.at[2]).start()
            for step in range(1, ranks):
                there = lax.rem(here.rank + step, ranks)
                push(source.at[there], out.at[here.rank], semaphores.at[0], semaphores.at[1], here.device, there)

        def finish():
            wait_bytes(out.at[0], semaphores.at[2])
            wait_bytes(out.at[pl.ds(0, ranks - 1)], semaphores.at[1])
            wait_bytes(out.at[pl.ds(0, ranks - 1)], semaphores.at[0])

        self.stages, self.last = {(0, 0): [start]}, [finish]


class StreamJob(Job):
    def __init__(self, shape, frames):
        self.shape, self.frames = shape, frames
        self.shapes, self.specs = [jax.ShapeDtypeStruct(shape, jnp.bfloat16)], anywhere(1)
        ranks, groups, rows, width = shape
        block = (groups, ranks, rows, width)
        if frames:
            block = (frames, ranks, groups, rows // frames, width)
        self.space = [pltpu.VMEM(block, jnp.bfloat16), pltpu.SemaphoreType.DMA((3,))]

    def bind(self, here, inputs, outputs, space):
        self.here, self.out = here, outputs[0]
        self.buffer, self.semaphores = space
        ranks = self.shape[0]

        def finish():
            wait_bytes(self.out.at[0], self.semaphores.at[2])
            wait_bytes(self.out.at[pl.ds(0, ranks - 1)], self.semaphores.at[1])
            wait_bytes(self.out.at[pl.ds(0, ranks - 1)], self.semaphores.at[0])

        self.stages, self.last = {}, [finish]

    def put(self, step, value):
        here, ranks = self.here, self.shape[0]
        self.buffer[step] = value.reshape(self.buffer.shape[1:]).astype(jnp.bfloat16)
        if self.frames:
            strip = self.buffer.shape[3]
            target = self.out.at[here.rank, :, pl.ds(pl.multiple_of(step * strip, strip), strip)]
        else:
            target = self.out.at[here.rank, step]
        pltpu.make_async_copy(self.buffer.at[step, here.rank], target, self.semaphores.at[2]).start()
        for ahead in range(1, ranks):
            there = lax.rem(here.rank + ahead, ranks)
            push(
                self.buffer.at[step, there], target, self.semaphores.at[0], self.semaphores.at[1],
                here.device, there,
            )


def greet_jobs(here):
    barrier = pltpu.get_barrier_semaphore()
    ranks = lax.axis_size("tensor")
    peers = [(here.other_side, here.rank)]
    peers += [(here.line(step), here.rank) for step in range(1, here.count)]
    peers += [(here.device, lax.rem(here.rank + step, ranks)) for step in range(1, ranks)]
    for peer in peers:
        pl.semaphore_signal(barrier, inc=1, device_id=peer, device_id_type=pl.DeviceIdType.MESH)
    pl.semaphore_wait(barrier, len(peers))


def call(body, steps, arguments, in_specs, out_shape, out_specs, scratch, jobs, collective_id, estimate, name):
    operands = [v for job in jobs for v in job.operands]
    sources = [v for job in jobs for v in (job.sources or anywhere(len(job.operands)))]
    shapes = [v for job in jobs for v in job.shapes]
    specs = [v for job in jobs for v in job.specs]
    space = [v for job in jobs for v in job.space]
    aliases, before, after = {}, len(arguments), len(out_shape)
    for job in jobs:
        for source, target in job.aliases.items():
            aliases[before + source] = after + target
        before, after = before + len(job.operands), after + len(job.shapes)

    def kernel(*refs):
        refs = list(refs)
        take = lambda number: [refs.pop(0) for _ in range(number)]
        inputs, job_inputs = take(len(arguments)), take(len(operands))
        outputs, job_outputs = take(len(out_shape)), take(len(shapes))
        own, job_space = take(len(scratch)), refs
        step = pl.program_id(0)
        if jobs:
            here = Where()
            for job in jobs:
                pick = lambda pool, number: [pool.pop(0) for _ in range(number)]
                job.bind(
                    here, pick(job_inputs, len(job.operands)), pick(job_outputs, len(job.shapes)),
                    pick(job_space, len(job.space)),
                )

        def hook(spot):
            for index in range(steps):
                todo = [stage for job in jobs for stage in job.stages.get((index, spot), ())]
                if todo or (jobs and spot == 0 and index == 0):

                    @pl.when(step == index)
                    def _():
                        if index == 0 and spot == 0:
                            greet_jobs(here)
                        for stage in todo:
                            stage()

        hook(0)
        body(lambda spot: hook(spot) if spot else None, *inputs, *outputs, *own)
        if jobs:

            @pl.when(step == steps - 1)
            def _():
                for job in jobs:
                    for stage in job.last:
                        stage()

    more = {"collective_id": collective_id, "has_side_effects": True} if jobs else {}
    return pl.pallas_call(
        kernel,
        grid=(steps,),
        in_specs=list(in_specs) + sources,
        out_specs=list(out_specs) + specs,
        out_shape=list(out_shape) + shapes,
        scratch_shapes=list(scratch) + space,
        input_output_aliases=aliases,
        compiler_params=pltpu.CompilerParams(
            vmem_limit_bytes=VMEM_LIMIT, dimension_semantics=("arbitrary",), **more
        ),
        cost_estimate=estimate,
        name=name,
    )(*arguments, *operands)


def entry_kernel(
    per_device, row_ref, modulation_ref, *refs
):
    gather = 2 if len(refs) > 5 else 0
    refs = list(refs)
    sources = [refs.pop(0) for _ in range(gather)]
    gathered_ref, mod_ref = refs.pop(0), refs.pop(0)
    targets = [refs.pop(0) for _ in range(gather)]
    part_ref, land_ref, semaphores, *space = refs
    device, rank, dp, tp = place()
    me, count = device * tp + rank, dp * tp
    quarter = land_ref.shape[2]
    if gather:
        here = Where()
        size = sources[0].shape[1] // PARTS
        parts = []
        for index in range(PARTS):
            part = pl.ds(index * size, size)
            parts.append(GatherChain(here, sources[0].at[:, part], targets[0].at[:, :, part], space.pop(0)))
        following = GatherChain(here, sources[1], targets[1], space[0])
    greet_all()

    def tell(index, carry):
        peer = lax.rem(me + index, count)
        push(
            row_ref, gathered_ref.at[me], semaphores.at[0], semaphores.at[1], peer // tp, lax.rem(peer, tp)
        )
        return carry

    lax.fori_loop(1, count, tell, 0)
    gathered_ref[me] = row_ref[...]
    if gather:
        for chain in parts:
            chain.stage_line()
    wait_bytes(gathered_ref.at[pl.ds(0, count - 1)], semaphores.at[1])
    padded = modulation_ref.shape[1]
    width = dp * tp * per_device
    chosen = jnp.zeros((count, padded), jnp.float32)
    row = lax.broadcasted_iota(jnp.int32, (PAIR, padded), 0)
    column = lax.broadcasted_iota(jnp.int32, (PAIR, padded), 1)
    for index in range(width // PAIR):
        match = (row + index * PAIR == column + me * per_device) & (column < per_device)
        chosen += mm(
            gathered_ref[:, index, :].astype(jnp.bfloat16), jnp.where(match, 1.0, 0.0).astype(jnp.bfloat16)
        )
    clip = lax.broadcasted_iota(jnp.int32, (dp, count), 0)
    member = lax.broadcasted_iota(jnp.int32, (dp, count), 1)
    leaders = jnp.where(member == clip * tp, 1.0, 0.0).astype(jnp.bfloat16)
    rows = mm(leaders, chosen.astype(jnp.bfloat16)).astype(jnp.bfloat16)
    for layer in range(modulation_ref.shape[0]):
        part = mm(rows, modulation_ref[layer])
        size = part.shape[1]
        for index in range(dp):
            part_ref[index, :, layer * size : (layer + 1) * size] = part[index : index + 1]

    def share(index, carry):
        peer = lax.rem(me + index, count)
        there, lane = peer // tp, lax.rem(peer, tp)
        source = part_ref.at[there, :, pl.ds(pl.multiple_of(lane * quarter, PAIR), quarter)]
        push(source, land_ref.at[me], semaphores.at[2], semaphores.at[3], there, lane)
        return carry

    lax.fori_loop(1, count, share, 0)
    mine = pl.ds(pl.multiple_of(rank * quarter, PAIR), quarter)
    land_ref[me] = part_ref[device, :, mine]
    if gather:
        for chain in parts:
            chain.line_arrived()
            chain.stage_near()
        following.stage_line()
    wait_bytes(land_ref.at[pl.ds(0, count - 1)], semaphores.at[3])
    mod_ref[:, mine] = jnp.sum(land_ref[...], axis=0)
    for step in range(1, tp):
        push(
            mod_ref.at[:, mine], mod_ref.at[:, mine], semaphores.at[4], semaphores.at[5],
            device, lax.rem(rank + step, tp),
        )
    if gather:
        for chain in parts:
            chain.stage_across()
        for chain in parts:
            chain.stage_core()
    wait_bytes(gathered_ref.at[pl.ds(0, count - 1)], semaphores.at[0])
    wait_bytes(land_ref.at[pl.ds(0, count - 1)], semaphores.at[2])
    wait_bytes(mod_ref.at[:, pl.ds(0, (tp - 1) * quarter)], semaphores.at[5])
    wait_bytes(mod_ref.at[:, pl.ds(0, (tp - 1) * quarter)], semaphores.at[4])
    if gather:
        following.line_arrived()
        for chain in parts:
            chain.finish()
        for chain in (*parts, following):
            chain.line_left()


def enter(row, modulation, per_device, weights, collective_id):
    dp, tp = lax.axis_size("dp"), lax.axis_size("tensor")
    count = dp * tp
    whole = modulation.shape[0] * modulation.shape[2]
    inside = pl.BlockSpec(memory_space=pltpu.VMEM)
    job = FlowJob((), weights) if weights else Job()
    return pl.pallas_call(
        partial(entry_kernel, per_device),
        in_specs=[inside, inside] + anywhere(len(job.operands)),
        out_specs=[inside, inside] + list(job.specs),
        out_shape=[
            jax.ShapeDtypeStruct((count,) + row.shape, jnp.float32),
            jax.ShapeDtypeStruct((1, whole), jnp.float32),
        ] + list(job.shapes),
        scratch_shapes=[
            pltpu.VMEM((dp, 1, whole), jnp.float32),
            pltpu.VMEM((count, 1, whole // tp), jnp.float32),
            pltpu.SemaphoreType.DMA((6,)),
        ] + (GatherChain.scratch() * (PARTS + 1) if weights else []),
        compiler_params=pltpu.CompilerParams(
            collective_id=collective_id, has_side_effects=True, vmem_limit_bytes=VMEM_LIMIT
        ),
        name="enter",
    )(row, modulation, *job.operands)


def adam_update(weight, first, second, grad, rate, decay):
    first_new = BETA_ONE * first + (1.0 - BETA_ONE) * grad
    second_new = BETA_TWO * second + (1.0 - BETA_TWO) * grad * grad
    corrected = (
        first_new
        / (1.0 - BETA_ONE**STEP)
        / (jnp.sqrt(second_new / (1.0 - BETA_TWO**STEP)) + ADAM_EPS)
    )
    weight_new = weight - rate * (corrected + decay * weight)
    return (weight_new, first_new, second_new, weight_new.astype(jnp.bfloat16))


def dot32(form, left, right):
    return jnp.einsum(form, left, right, preferred_element_type=jnp.float32)


def exchange(blocks):
    return lax.all_to_all(blocks, "tensor", split_axis=0, concat_axis=0, tiled=True)


def gather_plain(shard):
    rows, width = shard.shape
    whole = lax.all_gather(shard, ("tensor", "dp"), axis=0, tiled=True)
    return whole.reshape(-1, lax.axis_size("dp") * rows, width)


def scatter_plain(grads):
    kinds, ranks, width, cols = grads.shape
    flat = grads.reshape(kinds, ranks * width, cols)
    summed = lax.psum_scatter(flat, ("tensor", "dp"), scatter_dimension=1, tiled=True)
    return summed.astype(jnp.float32)


def per_device(
    clips, cotangent, timesteps, labels, time_table, class_table,
    attention_weights, attention_first, attention_second,
    ffn_weights, ffn_first, ffn_second,
    modulation_weights, modulation_first, modulation_second,
    bias_vectors, bias_first, bias_second,
):
    layers, kinds, rows, cols = attention_weights.shape
    _, frames, patches, width = clips.shape
    mod_rows = modulation_weights.shape[1]
    bias_cols = bias_vectors.shape[1]
    dp, tp = lax.axis_size("dp"), lax.axis_size("tensor")
    position = lax.axis_index("dp") * tp + lax.axis_index("tensor")
    tokens = frames * patches
    strip = patches // (tp * frames)
    blocks = (tp, frames, frames * strip, width)
    pieces = (tp * frames, frames, strip, width)

    embed = time_table[timesteps] + class_table[labels]
    cond_act = jax.nn.silu(embed).astype(jnp.bfloat16)
    fused = rows % 16 == 0
    shards = [
        (
            pack_heads(attention_weights[layer].astype(jnp.bfloat16)),
            ffn_weights[layer, 0].astype(jnp.bfloat16),
            ffn_weights[layer, 1].astype(jnp.bfloat16),
        )
        for layer in range(layers)
    ]
    low = bias_vectors.astype(jnp.bfloat16).reshape(-1)
    row = jnp.concatenate([cond_act[0], low]).astype(jnp.float32)
    row = jnp.pad(row, (0, -row.shape[0] % 1024)).reshape(-1, 128)
    modulation_low = modulation_weights.astype(jnp.bfloat16)
    modulation_low = jnp.pad(modulation_low, ((0, 0), (0, -mod_rows % 32), (0, 0)))
    gathered, mod, *begun = enter(row, modulation_low, mod_rows, shards[0][:2] if fused else None, 0)
    gathered = gathered.reshape(dp * tp, -1)
    cond_all = gathered[::tp, :width].astype(jnp.bfloat16)
    bias_low = gathered[:, width : width + layers * bias_cols].reshape(dp * tp, layers, bias_cols)
    bias_low = bias_low.transpose(1, 0, 2).reshape(layers, -1)
    cond_rows = lax.dynamic_slice_in_dim(cond_all, position * mod_rows, mod_rows, axis=1)
    cond_rows = jnp.pad(cond_rows, ((0, 0), (0, -mod_rows % 32)))
    mod = mod.reshape(layers, -1)
    mod_width = mod.shape[-1]
    mod = (mod + bias_low[:, -mod_width:]).reshape(layers, 6, width)
    hidden_width = bias_low.shape[1] - mod_width - 4 * width
    bias_up = bias_low[:, 3 * width : 3 * width + hidden_width].reshape(layers, tp, 1, -1)
    bias_out = bias_low[:, None, 2 * width : 3 * width]
    bias_down = bias_low[:, None, 3 * width + hidden_width : 4 * width + hidden_width]
    bias_project = [
        pack_bias(bias_low[layer, :width], bias_low[layer, width : 2 * width], tp) for layer in range(layers)
    ]

    by_patch = lambda v: v.reshape(frames, tp * frames, strip, width).transpose(1, 0, 2, 3)
    cot = by_patch(cotangent[0]).reshape(blocks)
    first = clips[0].reshape(1, frames, patches, width)

    attend = lambda layer, weight, stream, stride, *more: attention_forward(
        weight, stream, mod[layer], bias_project[layer], bias_out[layer], stride, *more
    )
    expand = lambda layer, up, down, middle, *more: ffn_forward(
        up, down, middle.reshape(tokens, width), mod[layer], bias_down[layer], bias_up[layer], *more
    )
    if fused:
        attention_a, up_a = begun
        *heads_a, middle_a, up_a, down_a, attention_b = attend(
            0, attention_a, first, 0, [FlowJob([up_a], [shards[1][0]], None, [shards[0][2]])], 1
        )
        hidden_a, pushed_a, second, attention_b, up_b, down_b = expand(
            0, up_a, down_a, middle_a, StreamJob(blocks, frames),
            [FlowJob([attention_b], [shards[1][2]], dp // 8, [shards[1][1]])], 2,
        )
        *heads_b, middle_b, down_b = attend(1, attention_b, second, strip, [FlowJob([down_b], [])], 3)
        hidden_b, pushed_b, result, cot = expand(1, up_b, down_b, middle_b, None, [SwapJob(cot)], 4)
    else:
        (attention_a, up_a, down_a), (attention_b, up_b, down_b) = [[gather_plain(v) for v in group] for group in shards]
        *heads_a, middle_a = attend(0, attention_a, first, 0)
        hidden_a, pushed_a, second = expand(0, up_a, down_a, middle_a)
        second = exchange(by_patch(second).reshape(blocks))
        *heads_b, middle_b = attend(1, attention_b, second, strip)
        hidden_b, pushed_b, result = expand(1, up_b, down_b, middle_b)
        cot = exchange(cot)
    middle_a, middle_b = middle_a.reshape(tokens, width), middle_b.reshape(tokens, width)
    result = result.reshape(blocks)
    cot = cot.reshape(tokens, width)

    if fused:
        grad, ffn_grad, *sums_b, result = ffn_backward(
            up_b, down_b, cot, middle_b, pushed_b, hidden_b, mod[1], [SwapJob(result)], 5
        )
        packed_b, *more_b, grad, line_up = attention_backward(
            attention_b, grad.reshape(blocks), second, heads_b, mod[1], strip,
            StreamJob(blocks, 0), [ScatterJob([(ffn_grad, 0)], 3 * dp // 8)], 6,
        )
        waiting = [(ffn_grad, 1), (packed_b[None], 0)]
        grad, ffn_grad, *sums_a, done_up, line_b = ffn_backward(
            up_a, down_a, grad.reshape(pieces), middle_a, pushed_a, hidden_a, mod[0],
            [LineJob(line_up), ScatterJob(waiting, dp // 4)], 7,
        )
        grad, packed_a, *more_a, done_b, line_ffn_a = attention_backward(
            attention_a, grad.reshape(first.shape), first, heads_a, mod[0], 0, None,
            [LineJob(line_b), ScatterJob([(ffn_grad, 0), (ffn_grad, 1)], dp // 4)], 8,
        )
        done_ffn_b, done_b = jnp.concatenate([done_up, done_b[:1]]), done_b[1:]
    else:
        result = exchange(result)
        grad, ffn_grad, *sums_b = ffn_backward(up_b, down_b, cot, middle_b, pushed_b, hidden_b, mod[1])
        done_ffn_b = scatter_plain(ffn_grad)
        grad, packed_b, *more_b = attention_backward(
            attention_b, grad.reshape(blocks), second, heads_b, mod[1], strip
        )
        done_b = scatter_plain(packed_b[None])
        grad = exchange(grad.astype(jnp.bfloat16))
        grad, ffn_grad, *sums_a = ffn_backward(up_a, down_a, grad.reshape(pieces), middle_a, pushed_a, hidden_a, mod[0])
        done_ffn_a = scatter_plain(ffn_grad)
        grad, packed_a, *more_a = attention_backward(attention_a, grad.reshape(first.shape), first, heads_a, mod[0], 0)
        done_a = scatter_plain(packed_a[None])
    output = result.reshape(pieces).transpose(1, 0, 2, 3).reshape(clips.shape)
    input_grad = grad.reshape(clips.shape)

    def gather_small(more, sums):
        attention_sums, project_sum = more
        up_sum, low_sums = sums
        return jnp.concatenate(
            [*unpack_bias(project_sum), attention_sums[0], up_sum.reshape(-1), low_sums[0],
             attention_sums[1:].reshape(-1), low_sums[1:].reshape(-1)]
        )

    small = jnp.stack([gather_small(more_a, sums_a), gather_small(more_b, sums_b)])
    token_width = small.shape[1] - mod_width
    *done, small, grad_act = leave(
        small.reshape(tp, -1, 128), modulation_low, token_width,
        *((packed_a, line_ffn_a) if fused else (None, None)), 9,
    )
    if fused:
        done_a, done_ffn_a = done[0][None], done[1]
    small = small.transpose(1, 0, 2, 3).reshape(dp, layers, -1)
    grad_mod_low = small[..., token_width:].astype(jnp.bfloat16)
    grad_bias_all = jnp.concatenate(
        [small[..., :token_width], grad_mod_low.astype(jnp.float32)], axis=-1
    ).sum(axis=0)
    grad_bias = lax.dynamic_slice_in_dim(grad_bias_all, position * bias_cols, bias_cols, axis=1)
    grad_mod_weight = dot32("ck,cle->lke", cond_rows, grad_mod_low)[:, :mod_rows]
    grad_act = lax.dynamic_index_in_dim(
        grad_act[:, :, :mod_rows], lax.axis_index("dp"), axis=1, keepdims=False
    )
    grad_attention = jnp.stack([unpack_heads(done_a[0]), unpack_heads(done_b[0])])
    grad_ffn = jnp.stack([done_ffn_a, done_ffn_b])
    silu_value, silu_pull = jax.vjp(jax.nn.silu, embed)
    cond_grad = silu_pull(grad_act.reshape(1, width))[0]

    return (output, input_grad, cond_grad) + (
        adam_update(attention_weights, attention_first, attention_second, grad_attention, MATRIX_RATE, MATRIX_DECAY)
        + adam_update(ffn_weights, ffn_first, ffn_second, grad_ffn, MATRIX_RATE, MATRIX_DECAY)
        + adam_update(modulation_weights, modulation_first, modulation_second, grad_mod_weight, MATRIX_RATE, MATRIX_DECAY)
        + adam_update(bias_vectors, bias_first, bias_second, grad_bias, VECTOR_RATE, 0.0)
    )


def solution(mesh):
    tokens = P("dp", "tensor", None, None)
    matrix = P(None, None, "dp", "tensor")
    modulation = P(None, BOTH, None)
    vector = P(None, BOTH)
    return jax.shard_map(
        per_device,
        mesh=mesh,
        in_specs=(tokens, tokens, P("dp"), P("dp"), P(), P())
        + (matrix,) * 6 + (modulation,) * 3 + (vector,) * 3,
        out_specs=(tokens, tokens, P("dp", None)) + (matrix,) * 8 + (modulation,) * 4 + (vector,) * 4,
        check_vma=False,
    )
```

```python
from functools import partial

import jax
import jax.numpy as jnp
from jax import lax
from jax.experimental import pallas as pl
from jax.experimental.pallas import tpu as pltpu
from jax.sharding import PartitionSpec as P

HD = 64
PAIR = 128
PARTS = 3
STEP = 10
BETA_ONE = 0.9
BETA_TWO = 0.999
ADAM_EPS = 1e-08
MATRIX_RATE = 0.04
VECTOR_RATE = 0.2
MATRIX_DECAY = 0.1
NORM_EPS = 1e-06
GELU_A = (2.0 / 3.141592653589793) ** 0.5
GELU_B = 0.044715
BLOCKED = -1e30
VMEM_LIMIT = 60 * 1024 * 1024
BOTH = ("dp", "tensor")


def mm(left, right, dims=((1,), (0,))):
    return lax.dot_general(left, right, (dims, ((), ())), preferred_element_type=jnp.float32)


def norm_parts(value):
    average = jnp.mean(value, axis=-1, keepdims=True)
    centred = value - average
    spread = jnp.mean(centred * centred, axis=-1, keepdims=True)
    inverse = lax.rsqrt(spread + NORM_EPS)
    return centred * inverse, inverse


def norm_back(grad, shape, inverse):
    first = jnp.mean(grad, axis=-1, keepdims=True)
    second = jnp.mean(grad * shape, axis=-1, keepdims=True)
    return inverse * (grad - first - shape * second)


def rows_of(ref):
    value = ref[...]
    return value.reshape(-1, value.shape[-1])


def put(ref, value):
    ref[...] = value.reshape(ref.shape).astype(ref.dtype)


def add_rows(ref, index, value):
    ref[pl.ds(index, 1), :] += jnp.sum(value, axis=0, keepdims=True)


def half_masks(rows):
    lane = lax.broadcasted_iota(jnp.int32, (rows, PAIR), 1)
    return lane < HD


def same_patch(tokens, stride):
    row = lax.broadcasted_iota(jnp.int32, (tokens, tokens), 0)
    column = lax.broadcasted_iota(jnp.int32, (tokens, tokens), 1)
    return lax.rem(row, stride) == lax.rem(column, stride)


def swap_halves(value):
    return pltpu.roll(value, HD, 1)


def start_loads(source, target, semaphores):
    for rank in range(target.shape[0]):
        pltpu.make_async_copy(source.at[rank], target.at[rank], semaphores.at[rank]).start()


def wait_loads(target, semaphores, rank):
    pltpu.make_async_copy(target.at[rank], target.at[rank], semaphores.at[rank]).wait()


def softmax_rows(scores, axis):
    raised = jnp.exp(scores - jnp.max(scores, axis=axis, keepdims=True))
    return raised * (1.0 / jnp.sum(raised, axis=axis, keepdims=True))


def attention_forward_kernel(
    stride, hook, source, stream_ref, mod_ref, bias_ref, bias_out_ref,
    project_ref, mixed_ref, branch_ref, middle_ref, weight_ref, semaphores,
):
    ranks = weight_ref.shape[0]

    @pl.when(pl.program_id(0) == 0)
    def _():
        start_loads(source, weight_ref, semaphores)

    stream = rows_of(stream_ref).astype(jnp.float32)
    tokens, width = stream.shape
    shape, _ = norm_parts(stream)
    normed = (shape * (1.0 + mod_ref[1:2]) + mod_ref[0:1]).astype(jnp.bfloat16)
    lower = half_masks(tokens)
    allowed = same_patch(tokens, stride) if stride else None

    @pl.when(pl.program_id(0) == 0)
    def _():
        for rank in range(ranks):
            wait_loads(weight_ref, semaphores, rank)

    def one_head(chosen, key, value):
        scores = mm(chosen.astype(jnp.bfloat16), key, ((1,), (1,)))
        if stride:
            scores = jnp.where(allowed, scores, BLOCKED)
        return mm(softmax_rows(scores, -1).astype(jnp.bfloat16), value)

    branch = None
    for rank in range(ranks):
        hook(rank)
        project = (mm(normed, weight_ref[rank, :, : 5 * PAIR]) + bias_ref[rank]).astype(jnp.bfloat16)
        project_ref[rank] = project.reshape(project_ref.shape[1:])
        query = project[:, :PAIR].astype(jnp.float32) * HD**-0.5
        key, value = project[:, PAIR : 2 * PAIR], project[:, 2 * PAIR : 3 * PAIR]
        first = one_head(jnp.where(lower, query, 0.0), key, value)
        second = one_head(jnp.where(lower, 0.0, query), key, value)
        both = project[:, 3 * PAIR : 4 * PAIR].astype(jnp.float32)
        last = one_head(
            jnp.where(lower, both * HD**-0.5, 0.0),
            swap_halves(both).astype(jnp.bfloat16),
            project[:, 4 * PAIR : 5 * PAIR],
        )
        mixed = jnp.concatenate(
            [jnp.where(lower, 0.0, swap_halves(last)), jnp.where(lower, first, second)], axis=1
        ).astype(jnp.bfloat16)
        mixed_ref[rank] = mixed.reshape(mixed_ref.shape[1:])
        term = mm(mixed, weight_ref[rank, :, 4 * PAIR :], ((1,), (1,)))
        branch = term if branch is None else branch + term
    branch = branch + bias_out_ref[...]
    put(branch_ref, branch)
    put(middle_ref, stream + mod_ref[2:3] * branch)


def gelu_parts(value):
    square = value * value
    bent = jnp.tanh(value * (GELU_A + (GELU_A * GELU_B) * square))
    half = 0.5 * (1.0 + bent)
    slope = half + (0.5 * value) * (1.0 - bent * bent) * (GELU_A + (3.0 * GELU_A * GELU_B) * square)
    return value * half, slope


def ffn_forward_kernel(
    stream, hook, up_source, down_source, middle_ref, mod_ref, bias_ref, bias_up_ref, hidden_ref, branch_ref, *rest
):
    if stream is None:
        result_ref, *rest = rest
    up_ref, down_ref, up_semaphores, down_semaphores = rest
    step = pl.program_id(0)
    ranks = up_ref.shape[0]

    @pl.when(step == 0)
    def _():
        start_loads(up_source, up_ref, up_semaphores)
        start_loads(down_source, down_ref, down_semaphores)

    middle = middle_ref[...]
    shape, _ = norm_parts(middle)
    second = (shape * (1.0 + mod_ref[4:5]) + mod_ref[3:4]).astype(jnp.bfloat16)

    @pl.when(step == 0)
    def _():
        for rank in range(ranks):
            wait_loads(up_ref, up_semaphores, rank)
            wait_loads(down_ref, down_semaphores, rank)

    down = None
    for rank in range(ranks):
        hook(rank)
        hidden = mm(second, up_ref[rank]) + bias_up_ref[rank]
        hidden_ref[rank] = hidden.astype(jnp.bfloat16)
        active, _ = gelu_parts(hidden)
        part = mm(active.astype(jnp.bfloat16), down_ref[rank], ((1,), (1,)))
        down = part if down is None else down + part
    down = down + bias_ref[...]
    branch_ref[...] = down.astype(jnp.bfloat16)
    result = middle + mod_ref[5:6] * down
    if stream is None:
        result_ref[...] = result.astype(result_ref.dtype)
    else:
        stream.put(step, result)


def load_rows(ref, index, chunk):
    if len(ref.shape) == 2:
        return ref[index * chunk : (index + 1) * chunk, :].astype(jnp.float32)
    blocks, _, strip, width = ref.shape
    frames = chunk // (blocks * strip)
    parts = [ref[:, index * frames + frame].reshape(blocks * strip, width) for frame in range(frames)]
    return jnp.concatenate(parts, axis=0).astype(jnp.float32)


def ffn_backward_kernel(
    split, hook, up_source, down_source, grad_ref, middle_ref, branch_ref, hidden_ref, mod_ref,
    grad_middle_ref, weight_grad_ref, up_sum_ref, sums_ref,
    up_ref, down_ref, up_semaphores, down_semaphores,
    second_ref, low_ref, low_across_ref, active_ref, slope_ref, total_ref,
):
    step = pl.program_id(0)
    tokens, width = middle_ref.shape
    chunk = tokens // split

    @pl.when(step == 0)
    def _():
        start_loads(up_source, up_ref, up_semaphores)
        start_loads(down_source, down_ref, down_semaphores)
        sums_ref[...] = jnp.zeros_like(sums_ref)
        for index in range(split):
            rows = slice(index * chunk, (index + 1) * chunk)
            grad = load_rows(grad_ref, index, chunk)
            low = (mod_ref[5:6] * grad).astype(jnp.bfloat16)
            low_ref[rows, :] = low
            low_across_ref[:, rows] = low.T
            add_rows(sums_ref, 0, low.astype(jnp.float32))
            add_rows(sums_ref, 3, grad * branch_ref[rows, :].astype(jnp.float32))
            shape, _ = norm_parts(middle_ref[rows, :])
            second = (shape * (1.0 + mod_ref[4:5]) + mod_ref[3:4]).astype(jnp.bfloat16)
            second_ref[:, rows] = second.T

    up_sum_ref[...] = jnp.zeros_like(up_sum_ref)
    wait_loads(up_ref, up_semaphores, step)
    wait_loads(down_ref, down_semaphores, step)

    for index in range(split):
        hook(index)
        rows = slice(index * chunk, (index + 1) * chunk)
        active, slope = gelu_parts(hidden_ref[0, rows, :].astype(jnp.float32))
        active_ref[rows, :] = active.astype(jnp.bfloat16)
        low = (mm(low_ref[rows, :], down_ref[step]) * slope).astype(jnp.bfloat16)
        slope_ref[rows, :] = low
        up_sum_ref[0] += jnp.sum(low.astype(jnp.float32), axis=0, keepdims=True)
        part = mm(low, up_ref[step], ((1,), (1,)))
        total_ref[rows, :] = jnp.where(step == 0, 0.0, total_ref[rows, :]) + part

    hook(2)
    weight_grad_ref[0, 0] = mm(second_ref[...], slope_ref[...]).astype(jnp.bfloat16)
    hook(3)
    weight_grad_ref[1, 0] = mm(low_across_ref[...], active_ref[...]).astype(jnp.bfloat16)

    @pl.when(step == pl.num_programs(0) - 1)
    def _():
        for index in range(split):
            rows = slice(index * chunk, (index + 1) * chunk)
            shape, inverse = norm_parts(middle_ref[rows, :])
            grad = total_ref[rows, :]
            add_rows(sums_ref, 1, grad)
            add_rows(sums_ref, 2, grad * shape)
            back = norm_back(grad * (1.0 + mod_ref[4:5]), shape, inverse)
            grad_middle_ref[rows, :] = load_rows(grad_ref, index, chunk) + back


def attention_backward_kernel(
    stride, swap, hook, source, grad_ref, stream_ref, project_ref, mixed_ref, branch_ref, mod_ref, *refs
):
    if swap is None:
        grad_stream_ref, *refs = refs
    (weight_grad_ref, sums_ref, project_sum_ref,
     weight_ref, semaphores, left_ref, right_ref, outer_ref) = refs
    step = pl.program_id(0)
    ranks = weight_ref.shape[0]

    @pl.when(step == 0)
    def _():
        start_loads(source, weight_ref, semaphores)
        sums_ref[...] = jnp.zeros_like(sums_ref)
        project_sum_ref[...] = jnp.zeros_like(project_sum_ref)

    grad_middle = rows_of(grad_ref)
    tokens, width = grad_middle.shape
    stream = rows_of(stream_ref).astype(jnp.float32)
    shape, inverse = norm_parts(stream)
    rows = pl.ds(pl.multiple_of(step * tokens, tokens), tokens)
    normed = (shape * (1.0 + mod_ref[1:2]) + mod_ref[0:1]).astype(jnp.bfloat16)
    low = (mod_ref[2:3] * grad_middle).astype(jnp.bfloat16)
    left_ref[0, :, rows] = normed.T
    left_ref[1, :, rows] = low.T
    add_rows(sums_ref, 0, low.astype(jnp.float32))
    add_rows(sums_ref, 3, grad_middle * rows_of(branch_ref).astype(jnp.float32))
    lower = half_masks(tokens)
    allowed = same_patch(tokens, stride) if stride else None
    scale = HD**-0.5

    @pl.when(step == 0)
    def _():
        for rank in range(ranks):
            wait_loads(weight_ref, semaphores, rank)

    def one_head(chosen, key, value, taken):
        scores = mm(key, chosen.astype(jnp.bfloat16), ((1,), (1,)))
        if stride:
            scores = jnp.where(allowed, scores, BLOCKED)
        probs = softmax_rows(scores, 0)
        grad_probs = mm(value, taken.astype(jnp.bfloat16), ((1,), (1,)))
        inner = jnp.sum(grad_probs * probs, axis=0, keepdims=True)
        return probs.astype(jnp.bfloat16), (probs * (grad_probs - inner)).astype(jnp.bfloat16)

    grad_normed = None
    for rank in range(ranks):
        hook(rank)
        project = project_ref[rank].reshape(tokens, 5 * PAIR)
        mixed = mixed_ref[rank].reshape(tokens, 2 * PAIR)
        outer_ref[rank, rows, :] = mixed
        grad_mixed = mm(low, weight_ref[rank, :, 4 * PAIR :]).astype(jnp.bfloat16)
        query, key, value = (project[:, n * PAIR : (n + 1) * PAIR] for n in range(3))
        query_wide = query.astype(jnp.float32) * scale
        pair = grad_mixed[:, PAIR:]
        pair_wide = pair.astype(jnp.float32)
        outs = []
        for keep in (lower, ~lower):
            probs, grad_scores = one_head(
                jnp.where(keep, query_wide, 0.0), key, value, jnp.where(keep, pair_wide, 0.0)
            )
            outs.append(
                (mm(grad_scores, key, ((0,), (0,))), mm(grad_scores, query), mm(probs, pair))
            )
        parts = [
            jnp.where(lower, one, two) * factor
            for one, two, factor in zip(outs[0], outs[1], (scale, scale, 1.0))
        ]
        both = project[:, 3 * PAIR : 4 * PAIR].astype(jnp.float32)
        swapped = swap_halves(both).astype(jnp.bfloat16)
        single = swap_halves(grad_mixed[:, :PAIR].astype(jnp.float32))
        probs, grad_scores = one_head(
            jnp.where(lower, both * scale, 0.0),
            swapped,
            project[:, 4 * PAIR :],
            jnp.where(lower, single, 0.0),
        )
        parts.append(
            jnp.where(lower, mm(grad_scores, swapped, ((0,), (0,))), mm(grad_scores, swapped)) * scale
        )
        parts.append(jnp.where(lower, mm(probs, single.astype(jnp.bfloat16)), 0.0))
        whole = jnp.concatenate(parts, axis=1).astype(jnp.bfloat16)
        right_ref[rank, rows, :] = whole
        add_rows(project_sum_ref, rank, whole.astype(jnp.float32))
        term = mm(whole, weight_ref[rank, :, : 5 * PAIR], ((1,), (1,)))
        grad_normed = term if grad_normed is None else grad_normed + term
    add_rows(sums_ref, 1, grad_normed)
    add_rows(sums_ref, 2, grad_normed * shape)
    back = norm_back(grad_normed * (1.0 + mod_ref[1:2]), shape, inverse)
    if swap is None:
        put(grad_stream_ref, grad_middle + back)
    else:
        swap.put(step, grad_middle + back)

    @pl.when(step == pl.num_programs(0) - 1)
    def _():
        def weights(rank, carry):
            inside = mm(left_ref[0], right_ref[rank])
            outside = mm(left_ref[1], outer_ref[rank])
            weight_grad_ref[rank, :, : 4 * PAIR] = inside[:, : 4 * PAIR].astype(jnp.bfloat16)
            weight_grad_ref[rank, :, 4 * PAIR : 5 * PAIR] = (
                inside[:, 4 * PAIR :] + outside[:, :PAIR]
            ).astype(jnp.bfloat16)
            weight_grad_ref[rank, :, 5 * PAIR :] = outside[:, PAIR:].astype(jnp.bfloat16)
            return carry

        lax.fori_loop(0, ranks, weights, 0)


def fixed(shape):
    return pl.BlockSpec(shape, lambda step: (0,) * len(shape), pipeline_mode=pl.Buffered(1))


def cost(flops, moved, raised=0):
    return pl.CostEstimate(flops=int(flops), bytes_accessed=int(moved), transcendentals=int(raised))


def group_spec(shape):
    return pl.BlockSpec((shape[0], 1, shape[2], shape[3]), lambda step: (0, step, 0, 0))


def rank_spec(shape):
    return pl.BlockSpec((shape[0], shape[1], 1) + shape[3:], lambda step: (0, 0, step, 0, 0))


def attention_forward(weight, stream, mod, bias, bias_out, stride, jobs=(), collective_id=None):
    shape = stream.shape
    width = shape[-1]
    ranks = bias.shape[0]
    tokens = shape[0] * shape[1] * shape[2]
    spec = group_spec(shape)
    low = jax.ShapeDtypeStruct(shape, jnp.bfloat16)
    wide = jax.ShapeDtypeStruct(shape, jnp.float32)
    project = jax.ShapeDtypeStruct((ranks,) + shape[:3] + (5 * PAIR,), jnp.bfloat16)
    mixed = jax.ShapeDtypeStruct((ranks,) + shape[:3] + (2 * PAIR,), jnp.bfloat16)
    return call(
        partial(attention_forward_kernel, stride),
        shape[1],
        [weight, stream, mod, bias, bias_out],
        anywhere(1) + [spec, fixed(mod.shape), fixed(bias.shape), fixed(bias_out.shape)],
        [project, mixed, low, wide],
        [rank_spec(project.shape), rank_spec(mixed.shape), spec, spec],
        [pltpu.VMEM((ranks, width, 6 * PAIR), jnp.bfloat16), pltpu.SemaphoreType.DMA((ranks,))],
        jobs,
        collective_id,
        cost(8 * tokens * width * width * 1.5, tokens * width * 16),
        "attention_forward",
    )


def ffn_weights_scratch(ranks, width, part):
    return [
        pltpu.VMEM((ranks, width, part), jnp.bfloat16),
        pltpu.VMEM((ranks, width, part), jnp.bfloat16),
        pltpu.SemaphoreType.DMA((ranks,)),
        pltpu.SemaphoreType.DMA((ranks,)),
    ]


def ffn_forward(up, down, middle, mod, bias_down, bias_up, stream=None, jobs=(), collective_id=None):
    tokens, width = middle.shape
    ranks, _, part = bias_up.shape
    steps = 2
    chunk = tokens // steps
    block = pl.BlockSpec((chunk, width), lambda step: (step, 0))
    result = [jax.ShapeDtypeStruct((tokens, width), jnp.bfloat16)] if stream is None else []
    return call(
        partial(ffn_forward_kernel, stream),
        steps,
        [up, down, middle, mod, bias_down, bias_up],
        anywhere(2) + [block, fixed(mod.shape), fixed(bias_down.shape), fixed(bias_up.shape)],
        [
            jax.ShapeDtypeStruct((ranks, tokens, part), jnp.bfloat16),
            jax.ShapeDtypeStruct((tokens, width), jnp.bfloat16),
        ] + result,
        [pl.BlockSpec((ranks, chunk, part), lambda step: (0, step, 0)), block] + [block] * len(result),
        ffn_weights_scratch(ranks, width, part),
        ([] if stream is None else [stream]) + list(jobs),
        collective_id,
        cost(4.8 * tokens * width * ranks * part, tokens * width * 14, tokens * ranks * part),
        "ffn_forward",
    )


def ffn_backward(up, down, grad, middle, branch, hidden, mod, jobs=(), collective_id=None):
    tokens, width = middle.shape
    ranks, _, part = hidden.shape
    whole = fixed((tokens, width))
    return call(
        partial(ffn_backward_kernel, 2),
        ranks,
        [up, down, grad, middle, branch, hidden, mod],
        anywhere(2) + [
            fixed(grad.shape), whole, whole,
            pl.BlockSpec((1, tokens, part), lambda step: (step, 0, 0)),
            fixed(mod.shape),
        ],
        [
            jax.ShapeDtypeStruct((tokens, width), jnp.float32),
            jax.ShapeDtypeStruct((2, ranks, width, part), jnp.bfloat16),
            jax.ShapeDtypeStruct((ranks, 1, part), jnp.float32),
            jax.ShapeDtypeStruct((4, width), jnp.float32),
        ],
        [
            whole,
            pl.BlockSpec((2, 1, width, part), lambda step: (0, step, 0, 0)),
            pl.BlockSpec((1, 1, part), lambda step: (step, 0, 0)),
            fixed((4, width)),
        ],
        ffn_weights_scratch(ranks, width, part) + [
            pltpu.VMEM((width, tokens), jnp.bfloat16),
            pltpu.VMEM((tokens, width), jnp.bfloat16),
            pltpu.VMEM((width, tokens), jnp.bfloat16),
            pltpu.VMEM((tokens, part), jnp.bfloat16),
            pltpu.VMEM((tokens, part), jnp.bfloat16),
            pltpu.VMEM((tokens, width), jnp.float32),
        ],
        jobs,
        collective_id,
        cost(9.6 * tokens * width * ranks * part, tokens * width * 20, tokens * ranks * part),
        "ffn_backward",
    )


def attention_backward(weight, grad, stream, saved, mod, stride, swap=None, jobs=(), collective_id=None):
    project, mixed, branch = saved
    shape = stream.shape
    width = shape[-1]
    ranks = project.shape[0]
    tokens = shape[0] * shape[1] * shape[2]
    spec = group_spec(shape)
    result = [jax.ShapeDtypeStruct(shape, jnp.float32)] if swap is None else []
    return call(
        partial(attention_backward_kernel, stride, swap),
        shape[1],
        [weight, grad, stream, project, mixed, branch, mod],
        anywhere(1) + [
            spec, spec, rank_spec(project.shape), rank_spec(mixed.shape), spec, fixed(mod.shape),
        ],
        result + [
            jax.ShapeDtypeStruct((ranks, width, 6 * PAIR), jnp.bfloat16),
            jax.ShapeDtypeStruct((4, width), jnp.float32),
            jax.ShapeDtypeStruct((ranks, 5 * PAIR), jnp.float32),
        ],
        [spec] * len(result) + [
            fixed((ranks, width, 6 * PAIR)), fixed((4, width)), fixed((ranks, 5 * PAIR)),
        ],
        [
            pltpu.VMEM((ranks, width, 6 * PAIR), jnp.bfloat16),
            pltpu.SemaphoreType.DMA((ranks,)),
            pltpu.VMEM((2, width, tokens), jnp.bfloat16),
            pltpu.VMEM((ranks, tokens, 5 * PAIR), jnp.bfloat16),
            pltpu.VMEM((ranks, tokens, 2 * PAIR), jnp.bfloat16),
        ],
        ([] if swap is None else [swap]) + list(jobs),
        collective_id,
        cost(16 * tokens * width * width * 1.5, tokens * width * 20),
        "attention_backward",
    )


def pack_heads(block):
    query, key, value, outer = block
    return jnp.concatenate(
        [query[:, :PAIR], key[:, :PAIR], value[:, :PAIR], query[:, PAIR:], key[:, PAIR:],
         value[:, PAIR:], outer[:, PAIR:], outer[:, :PAIR]], axis=1
    )


def unpack_heads(packed):
    part = lambda start, size: packed[:, start : start + size]
    join = lambda first, last: jnp.concatenate([part(first, PAIR), part(last, HD)], axis=1)
    return jnp.stack(
        [join(0, 3 * PAIR), join(PAIR, 3 * PAIR + HD), join(2 * PAIR, 4 * PAIR), join(5 * PAIR, 4 * PAIR + HD)]
    )


def pack_bias(query, value, ranks):
    query, value = query.reshape(ranks, -1), value.reshape(ranks, -1)
    none = jnp.zeros((ranks, PAIR), query.dtype)
    return jnp.concatenate(
        [query[:, :PAIR], none, value[:, :PAIR], query[:, PAIR:], none[:, :HD], value[:, PAIR:], none[:, :HD]],
        axis=1,
    )[:, None]


def unpack_bias(sums):
    query = jnp.concatenate([sums[:, :PAIR], sums[:, 3 * PAIR : 3 * PAIR + HD]], axis=1)
    value = jnp.concatenate([sums[:, 2 * PAIR : 3 * PAIR], sums[:, 4 * PAIR : 4 * PAIR + HD]], axis=1)
    return query.reshape(-1), value.reshape(-1)


def place():
    return lax.axis_index("dp"), lax.axis_index("tensor"), lax.axis_size("dp"), lax.axis_size("tensor")


def greet_all():
    device, rank, dp, tp = place()
    me, count = device * tp + rank, dp * tp
    barrier = pltpu.get_barrier_semaphore()

    def greet(index, carry):
        peer = lax.rem(me + index, count)
        pl.semaphore_signal(
            barrier, inc=1, device_id=(peer // tp, lax.rem(peer, tp)), device_id_type=pl.DeviceIdType.MESH
        )
        return carry

    lax.fori_loop(1, count, greet, 0)
    pl.semaphore_wait(barrier, count - 1)


def push(source, target, send, receive, device, rank):
    pltpu.make_async_remote_copy(
        src_ref=source, dst_ref=target, send_sem=send, recv_sem=receive,
        device_id=(device, rank), device_id_type=pl.DeviceIdType.MESH,
    ).start()


def wait_bytes(ref, semaphore):
    pltpu.make_async_copy(ref, ref, semaphore).wait()


class Where:
    def __init__(self):
        device, rank = lax.axis_index("dp"), lax.axis_index("tensor")
        self.count = lax.axis_size("dp") // 2
        self.device, self.rank = device, rank
        self.far, self.side = device // 2, lax.rem(device, 2)
        self.row, self.core = rank // 2, lax.rem(rank, 2)
        self.other_side = self.far * 2 + 1 - self.side
        self.other_row = (1 - self.row) * 2 + self.core
        self.other_core = self.row * 2 + 1 - self.core

    def ahead(self, step):
        return lax.rem(self.far + step, self.count)

    def line(self, step):
        return self.ahead(step) * 2 + self.side


def greet_neighbours(here):
    barrier = pltpu.get_barrier_semaphore()
    peers = [(here.other_side, here.rank), (here.device, here.other_row), (here.device, here.other_core)]
    peers += [(here.line(step), here.rank) for step in range(1, here.count)]
    for peer in peers:
        pl.semaphore_signal(barrier, inc=1, device_id=peer, device_id_type=pl.DeviceIdType.MESH)
    pl.semaphore_wait(barrier, len(peers))


def add_into(target, left, right):
    target[...] = (left[...].astype(jnp.float32) + right[...].astype(jnp.float32)).astype(target.dtype)


class ScatterChain:
    def __init__(self, here, source, line, lead, scratch):
        self.here, self.source, self.line, self.lead = here, source, line, lead
        self.keep, self.land_core, self.first_one, self.last_one, self.first_two, self.last_two, self.semaphores = scratch
        self.rows = line.shape[1]

    @staticmethod
    def scratch(width, columns, dp, lead):
        rows, far = width // dp, dp // 2
        low = lambda *shape: pltpu.VMEM(shape + (columns,), jnp.bfloat16)
        return [
            low(2, width), low(2, width),
            low(2, lead, rows), low(2 * (far - lead) * rows), low(lead, rows), low(far - lead, rows),
            pltpu.SemaphoreType.DMA((6, 2)),
        ]

    def chunk(self, row, far, side):
        return self.keep.at[row, pl.ds(pl.multiple_of((far * 2 + side) * self.rows, self.rows), self.rows)]

    def send(self, slot, source, target, device, rank):
        push(source, target, self.semaphores.at[slot, 0], self.semaphores.at[slot, 1], device, rank)

    def arrived(self, slot, ref):
        wait_bytes(ref, self.semaphores.at[slot, 1])

    def left(self, slot, ref):
        wait_bytes(ref, self.semaphores.at[slot, 0])

    def stage_core(self):
        here = self.here
        for row in range(2):
            pltpu.make_async_copy(
                self.source.at[row * 2 + here.core], self.keep.at[row], self.semaphores.at[5, 0]
            ).start()
            self.send(0, self.source.at[row * 2 + 1 - here.core], self.land_core.at[row], here.device, here.other_core)

    def stage_one(self):
        here = self.here
        wait_bytes(self.keep, self.semaphores.at[5, 0])
        self.arrived(0, self.land_core)

        def one(index, carry):
            rows = pl.ds(pl.multiple_of(index * self.rows, self.rows), self.rows)
            for row in range(2):
                add_into(self.keep.at[row, rows], self.keep.at[row, rows], self.land_core.at[row, rows])
            return carry

        lax.fori_loop(0, here.count * 2, one, 0)
        for row in range(2):
            for far in range(self.lead):
                self.send(
                    1, self.chunk(row, far, 1 - here.side), self.first_one.at[row, far], here.other_side, here.rank
                )
        start, size = self.lead * 2 * self.rows, (here.count - self.lead) * 2 * self.rows
        self.send(2, self.keep.at[1 - here.row, pl.ds(start, size)], self.last_one, here.device, here.other_row)

    def stage_two(self):
        here, lead = self.here, self.lead
        self.arrived(1, self.first_one)
        for row in range(2):
            for far in range(lead):
                mine = self.chunk(row, far, here.side)
                add_into(mine, mine, self.first_one.at[row, far])
        for far in range(lead):
            self.send(3, self.chunk(1 - here.row, far, here.side), self.first_two.at[far], here.device, here.other_row)
        self.arrived(2, self.last_one)
        for far in range(lead, here.count):
            for side in range(2):
                mine = self.chunk(here.row, far, side)
                add_into(mine, mine, self.last_one.at[pl.ds(((far - lead) * 2 + side) * self.rows, self.rows)])
        for far in range(lead, here.count):
            self.send(
                4, self.chunk(here.row, far, 1 - here.side), self.last_two.at[far - lead], here.other_side, here.rank
            )

    def merge(self):
        here = self.here
        self.arrived(3, self.first_two)
        self.arrived(4, self.last_two)
        for far in range(here.count):
            land = self.first_two.at[far] if far < self.lead else self.last_two.at[far - self.lead]
            add_into(self.line.at[far], self.chunk(here.row, far, here.side), land)

    def finish(self):
        self.left(0, self.land_core)
        self.left(1, self.first_one)
        self.left(2, self.last_one)
        self.left(3, self.first_two)
        self.left(4, self.last_two)


class LineChain:
    def __init__(self, here, line, out, land, semaphores):
        self.here, self.line, self.out, self.land, self.semaphores = here, line, out, land, semaphores

    @staticmethod
    def scratch(far, rows, columns):
        return [pltpu.VMEM((far - 1, rows, columns), jnp.bfloat16), pltpu.SemaphoreType.DMA((2,))]

    def start(self):
        here = self.here
        for step in range(1, here.count):
            push(
                self.line.at[here.ahead(step)], self.land.at[step - 1], self.semaphores.at[0],
                self.semaphores.at[1], here.line(step), here.rank,
            )

    def finish(self):
        wait_bytes(self.land, self.semaphores.at[1])
        total = self.line[self.here.far].astype(jnp.float32)
        for step in range(1, self.here.count):
            total = total + self.land[step - 1].astype(jnp.float32)
        self.out[...] = total
        wait_bytes(self.land, self.semaphores.at[0])


def leave_kernel(mod_start, *refs):
    refs = list(refs)
    scattering = len(refs) > 10
    source, begun = (refs.pop(0), refs.pop(0)) if scattering else (None, None)
    small_ref, modulation_ref, *refs = refs
    out, begun_out = (refs.pop(0), refs.pop(0)) if scattering else (None, None)
    sum_ref, act_ref, land_ref, acting_ref, semaphores, *space = refs
    device, rank, dp, tp = place()
    me, count = device * tp + rank, dp * tp
    greet_all()
    if scattering:
        here = Where()
        line_ref, *space = space
        pick = lambda number: [space.pop(0) for _ in range(number)]
        chains, trails = [], []
        for index in range(PARTS):
            size = out.shape[1] // PARTS
            part = pl.ds(index * size, size)
            line = line_ref.at[index]
            chains.append(ScatterChain(here, source.at[:, :, part], line, here.count // 2, pick(7)))
            trails.append(LineChain(here, line, out.at[:, part], *pick(2)))
        others = [LineChain(here, begun.at[kind], begun_out.at[kind], *pick(2)) for kind in range(begun.shape[0])]
        for chain in chains:
            chain.stage_core()
    for step in range(1, tp):
        there = lax.rem(rank + step, tp)
        push(small_ref.at[there], land_ref.at[rank], semaphores.at[0], semaphores.at[1], device, there)
    land_ref[rank] = small_ref[rank]
    wait_bytes(land_ref.at[pl.ds(0, tp - 1)], semaphores.at[1])
    mine = sum_ref.at[rank]
    mine[device] = jnp.sum(land_ref[...], axis=0)

    def one(step, carry):
        push(mine.at[device], mine.at[device], semaphores.at[2], semaphores.at[3], lax.rem(device + step, dp), rank)
        return carry

    lax.fori_loop(1, dp, one, 0)
    if scattering:
        for chain in others:
            chain.start()
    wait_bytes(mine.at[pl.ds(0, dp - 1)], semaphores.at[3])
    for step in range(1, tp):
        push(mine, mine, semaphores.at[4], semaphores.at[5], device, lax.rem(rank + step, tp))
    if scattering:
        for chain in chains:
            chain.stage_one()
    wait_bytes(sum_ref.at[pl.ds(0, tp - 1)], semaphores.at[5])
    layers, padded, columns = modulation_ref.shape
    lines = sum_ref.shape[2]
    total = jnp.zeros((dp, padded), jnp.float32)
    for layer in range(layers):
        for index in range(columns // PAIR):
            line = layer * (tp * lines // layers) + mod_start // PAIR + index
            low = sum_ref[line // lines, :, line % lines, :].astype(jnp.bfloat16)
            total += mm(low, modulation_ref[layer, :, index * PAIR : (index + 1) * PAIR], ((1,), (1,)))
    acting_ref[...] = jnp.concatenate([total, jnp.zeros((dp, PAIR - padded), jnp.float32)], axis=1)
    act_ref[me] = acting_ref[...]

    def tell(index, carry):
        peer = lax.rem(me + index, count)
        push(acting_ref, act_ref.at[me], semaphores.at[6], semaphores.at[7], peer // tp, lax.rem(peer, tp))
        return carry

    lax.fori_loop(1, count, tell, 0)
    if scattering:
        for chain in chains:
            chain.stage_two()
        for chain, line in zip(chains, trails):
            chain.merge()
            line.start()
        for chain in others:
            chain.finish()
    wait_bytes(act_ref.at[pl.ds(0, count - 1)], semaphores.at[7])
    wait_bytes(act_ref.at[pl.ds(0, count - 1)], semaphores.at[6])
    wait_bytes(land_ref.at[pl.ds(0, tp - 1)], semaphores.at[0])
    wait_bytes(mine.at[pl.ds(0, dp - 1)], semaphores.at[2])
    wait_bytes(sum_ref.at[pl.ds(0, tp - 1)], semaphores.at[4])
    if scattering:
        for chain in chains + trails:
            chain.finish()


def leave(small, modulation, mod_start, grads, begun, collective_id):
    tp, lines, lanes = small.shape
    dp = lax.axis_size("dp")
    inside = pl.BlockSpec(memory_space=pltpu.VMEM)
    shapes, space, extra = [], [], []
    if grads is not None:
        _, width, columns = grads.shape
        rows, far, part = width // dp, dp // 2, columns // PARTS
        kinds = begun.shape[0]
        extra = [grads, begun]
        shapes = [
            jax.ShapeDtypeStruct((rows, columns), jnp.float32),
            jax.ShapeDtypeStruct((kinds, rows, columns), jnp.float32),
        ]
        space = [pltpu.VMEM((PARTS, far, rows, part), jnp.bfloat16)]
        for _ in range(PARTS):
            space += ScatterChain.scratch(width, part, dp, far // 2) + LineChain.scratch(far, rows, part)
        space += LineChain.scratch(far, rows, columns) * kinds
    return pl.pallas_call(
        partial(leave_kernel, mod_start),
        in_specs=[pl.BlockSpec(memory_space=pl.ANY), inside][: len(extra)] + [inside, inside],
        out_specs=[inside] * (len(shapes) + 2),
        out_shape=shapes + [
            jax.ShapeDtypeStruct((tp, dp, lines, lanes), jnp.float32),
            jax.ShapeDtypeStruct((dp * tp, dp, lanes), jnp.float32),
        ],
        scratch_shapes=[
            pltpu.VMEM((tp, lines, lanes), jnp.float32),
            pltpu.VMEM((dp, lanes), jnp.float32),
            pltpu.SemaphoreType.DMA((8,)),
        ] + space,
        compiler_params=pltpu.CompilerParams(
            collective_id=collective_id, has_side_effects=True, vmem_limit_bytes=VMEM_LIMIT
        ),
        name="leave",
    )(*extra, small, modulation)


class GatherChain:
    def __init__(self, here, source, out, semaphores, half=None):
        self.here, self.source, self.out, self.semaphores = here, source, out, semaphores
        self.rows = out.shape[1] // (2 * here.count)
        self.half = here.count // 2 if half is None else half

    @staticmethod
    def scratch():
        return [pltpu.SemaphoreType.DMA((9, 2))]

    def piece(self, rank, far, side):
        rows = pl.ds(pl.multiple_of((far * 2 + side) * self.rows, self.rows), self.rows)
        return self.out.at[rank, rows]

    def send(self, slot, source, target, device, rank):
        push(source, target, self.semaphores.at[slot, 0], self.semaphores.at[slot, 1], device, rank)

    def wait(self, slot, way, pieces):
        wait_bytes(self.out.at[0, pl.ds(0, pieces * self.rows)], self.semaphores.at[slot, way])

    def stage_line(self):
        here = self.here
        mine = self.piece(here.rank, here.far, here.side)
        pltpu.make_async_copy(self.source, mine, self.semaphores.at[8, 0]).start()
        for step in range(1, here.count):
            self.send(0, self.source, mine, here.line(step), here.rank)

    def line_arrived(self):
        self.wait(8, 0, 1)
        self.wait(0, 1, self.here.count - 1)

    def line_left(self):
        self.wait(0, 0, self.here.count - 1)

    def stage_near(self):
        here = self.here
        for turn in range(2):
            over_row = lax.rem(here.core + turn, 2) == 1
            device = jnp.where(over_row, here.device, here.other_side)
            rank = jnp.where(over_row, here.other_row, here.rank)
            for far in range(here.count):
                mine = self.piece(here.rank, far, here.side)
                self.send(1 + lax.rem(here.core + turn, 2), mine, mine, device, rank)
        for far in range(here.count):
            mine = self.piece(here.rank, far, here.side)
            self.send(3, mine, mine, here.device, here.other_core)

    def stage_across(self):
        here, count = self.here, self.here.count
        self.wait(1, 1, count)
        for far in range(self.half):
            other = self.piece(here.rank, far, 1 - here.side)
            self.send(4, other, other, here.device, here.other_row)
        self.wait(2, 1, count)
        for far in range(self.half, count):
            other = self.piece(here.other_row, far, here.side)
            self.send(5, other, other, here.other_side, here.rank)
        for far in range(count):
            for other in (self.piece(here.rank, far, 1 - here.side), self.piece(here.other_row, far, here.side)):
                self.send(6, other, other, here.device, here.other_core)

    def stage_core(self):
        here, count = self.here, self.here.count
        self.wait(4, 1, self.half)
        self.wait(5, 1, count - self.half)
        for far in range(count):
            other = self.piece(here.other_row, far, 1 - here.side)
            self.send(7, other, other, here.device, here.other_core)

    def finish(self):
        count, half = self.here.count, self.half
        self.wait(3, 1, count)
        self.wait(6, 1, 2 * count)
        self.wait(7, 1, count)
        for slot, pieces in ((1, count), (2, count), (3, count), (4, half), (5, count - half), (6, 2 * count), (7, count)):
            self.wait(slot, 0, pieces)


class Job:
    operands, sources, shapes, specs, aliases, space = (), None, (), (), {}, ()
    stages, last = {}, ()


def anywhere(count):
    return [pl.BlockSpec(memory_space=pl.ANY)] * count


class ScatterJob(Job):
    def __init__(self, grads, lead, close=False):
        _, _, width, columns = grads[0][0].shape
        dp = lax.axis_size("dp")
        far, rows = dp // 2, width // dp
        self.lead, self.close, self.kinds = lead, close, [kind for _, kind in grads]
        self.operands = [array for array, _ in grads]
        shape = (len(grads) - close, far, rows, columns)
        self.shapes, self.specs = [jax.ShapeDtypeStruct(shape, jnp.bfloat16)], [fixed(shape)]
        self.space = ScatterChain.scratch(width, columns, dp, lead) * len(grads)
        if close:
            self.shapes.append(jax.ShapeDtypeStruct((1, rows, columns), jnp.float32))
            self.specs.append(fixed((1, rows, columns)))
            self.space = [pltpu.VMEM((far, rows, columns), jnp.bfloat16)] + LineChain.scratch(
                far, rows, columns
            ) + self.space

    def bind(self, here, inputs, outputs, space):
        lines = [outputs[0].at[index] for index in range(outputs[0].shape[0])]
        if self.close:
            own, land, semaphores, *space = space
            lines.insert(0, own)
            line = LineChain(here, own, outputs[1].at[0], land, semaphores)
        size = len(space) // len(inputs)
        chains = [
            ScatterChain(
                here, source.at[kind], lines[index], self.lead, space[index * size : (index + 1) * size]
            )
            for index, (source, kind) in enumerate(zip(inputs, self.kinds))
        ]
        one = chains[0]
        if len(chains) == 1:
            self.stages = {(0, 0): [one.stage_core], (0, 3): [one.stage_one], (2, 1): [one.stage_two]}
            self.last = [one.merge, one.finish]
            return
        two = chains[1]
        if self.close:
            self.stages = {
                (0, 0): [one.stage_core, two.stage_core], (0, 2): [one.stage_one], (2, 0): [one.stage_two, two.stage_one],
                (2, 3): [one.merge, line.start],
            }
            self.last = [two.stage_two, line.finish, two.merge, one.finish, two.finish]
            return
        self.stages = {
            (0, 0): [one.stage_core, two.stage_core], (0, 2): [one.stage_one], (0, 3): [two.stage_one],
            (2, 1): [one.stage_two], (3, 1): [two.stage_two],
        }
        self.last = [one.merge, two.merge, one.finish, two.finish]


class LineJob(Job):
    def __init__(self, line):
        kinds, far, rows, columns = line.shape
        shape = (kinds, rows, columns)
        self.operands, self.sources = [line], [fixed(line.shape)]
        self.shapes, self.specs = [jax.ShapeDtypeStruct(shape, jnp.float32)], [fixed(shape)]
        self.space = LineChain.scratch(far, rows, columns) * kinds

    def bind(self, here, inputs, outputs, space):
        chains = [
            LineChain(here, inputs[0].at[kind], outputs[0].at[kind], *space[2 * kind : 2 * kind + 2])
            for kind in range(outputs[0].shape[0])
        ]
        self.stages = {(0, 0): [chain.start for chain in chains]}
        self.last = [chain.finish for chain in chains]


class FlowJob(Job):
    def __init__(self, spread, lines, half=None, late=()):
        dp, tp = lax.axis_size("dp"), lax.axis_size("tensor")
        self.counts, self.half = (len(spread), len(late)), half
        shards = list(late) + list(lines)
        self.operands = list(spread) + shards
        self.shapes = [jax.ShapeDtypeStruct(v.shape, v.dtype) for v in spread]
        self.shapes += [jax.ShapeDtypeStruct((tp, dp * v.shape[0], v.shape[1]), v.dtype) for v in shards]
        self.specs = anywhere(len(self.shapes))
        self.aliases = {index: index for index in range(len(spread))}
        self.space = GatherChain.scratch() * len(self.shapes)

    def bind(self, here, inputs, outputs, space):
        chains = [GatherChain(here, *refs, self.half) for refs in zip(inputs, outputs, space)]
        first, late = self.counts
        spread, late, lines = chains[:first], chains[first : first + late], chains[first + late :]
        self.stages = {
            (0, 0): [chain.stage_near for chain in spread] + [chain.stage_line for chain in late + lines],
            (3, 0): [chain.stage_across for chain in spread],
        }
        for chain in late:
            self.stages[3, 0] += [chain.line_arrived, chain.stage_near]
        self.last = [chain.stage_across for chain in late]
        self.last += [chain.stage_core for chain in spread + late]
        self.last += [chain.finish for chain in spread + late]
        self.last += [chain.line_arrived for chain in lines]
        self.last += [chain.line_left for chain in late + lines]


class SwapJob(Job):
    def __init__(self, blocks):
        self.operands = [blocks]
        self.shapes, self.specs = [jax.ShapeDtypeStruct(blocks.shape, blocks.dtype)], anywhere(1)
        self.space = [pltpu.SemaphoreType.DMA((3,))]

    def bind(self, here, inputs, outputs, space):
        source, out, semaphores = inputs[0], outputs[0], space[0]
        ranks = out.shape[0]

        def start():
            pltpu.make_async_copy(source.at[here.rank], out.at[here.rank], semaphores.at[2]).start()
            for step in range(1, ranks):
                there = lax.rem(here.rank + step, ranks)
                push(source.at[there], out.at[here.rank], semaphores.at[0], semaphores.at[1], here.device, there)

        def finish():
            wait_bytes(out.at[0], semaphores.at[2])
            wait_bytes(out.at[pl.ds(0, ranks - 1)], semaphores.at[1])
            wait_bytes(out.at[pl.ds(0, ranks - 1)], semaphores.at[0])

        self.stages, self.last = {(0, 0): [start]}, [finish]


class StreamJob(Job):
    def __init__(self, shape, frames):
        self.shape, self.frames = shape, frames
        self.shapes, self.specs = [jax.ShapeDtypeStruct(shape, jnp.bfloat16)], anywhere(1)
        ranks, groups, rows, width = shape
        block = (groups, ranks, rows, width)
        if frames:
            block = (frames, ranks, groups, rows // frames, width)
        self.space = [pltpu.VMEM(block, jnp.bfloat16), pltpu.SemaphoreType.DMA((3,))]

    def bind(self, here, inputs, outputs, space):
        self.here, self.out = here, outputs[0]
        self.buffer, self.semaphores = space
        ranks = self.shape[0]

        def finish():
            wait_bytes(self.out.at[0], self.semaphores.at[2])
            wait_bytes(self.out.at[pl.ds(0, ranks - 1)], self.semaphores.at[1])
            wait_bytes(self.out.at[pl.ds(0, ranks - 1)], self.semaphores.at[0])

        self.stages, self.last = {}, [finish]

    def put(self, step, value):
        here, ranks = self.here, self.shape[0]
        size = self.buffer.size // self.buffer.shape[0] // value.shape[1]
        if value.shape[0] > size:
            count = value.shape[0] // size
            for index in range(count):
                self.put(step * count + index, value[index * size : (index + 1) * size])
            return
        self.buffer[step] = value.reshape(self.buffer.shape[1:]).astype(jnp.bfloat16)
        if self.frames:
            strip = self.buffer.shape[3]
            target = self.out.at[here.rank, :, pl.ds(pl.multiple_of(step * strip, strip), strip)]
        else:
            target = self.out.at[here.rank, step]
        pltpu.make_async_copy(self.buffer.at[step, here.rank], target, self.semaphores.at[2]).start()
        for ahead in range(1, ranks):
            there = lax.rem(here.rank + ahead, ranks)
            push(
                self.buffer.at[step, there], target, self.semaphores.at[0], self.semaphores.at[1],
                here.device, there,
            )


def greet_jobs(here):
    barrier = pltpu.get_barrier_semaphore()
    ranks = lax.axis_size("tensor")
    peers = [(here.other_side, here.rank)]
    peers += [(here.line(step), here.rank) for step in range(1, here.count)]
    peers += [(here.device, lax.rem(here.rank + step, ranks)) for step in range(1, ranks)]
    for peer in peers:
        pl.semaphore_signal(barrier, inc=1, device_id=peer, device_id_type=pl.DeviceIdType.MESH)
    pl.semaphore_wait(barrier, len(peers))


def call(body, steps, arguments, in_specs, out_shape, out_specs, scratch, jobs, collective_id, estimate, name):
    operands = [v for job in jobs for v in job.operands]
    sources = [v for job in jobs for v in (job.sources or anywhere(len(job.operands)))]
    shapes = [v for job in jobs for v in job.shapes]
    specs = [v for job in jobs for v in job.specs]
    space = [v for job in jobs for v in job.space]
    aliases, before, after = {}, len(arguments), len(out_shape)
    for job in jobs:
        for source, target in job.aliases.items():
            aliases[before + source] = after + target
        before, after = before + len(job.operands), after + len(job.shapes)

    def kernel(*refs):
        refs = list(refs)
        take = lambda number: [refs.pop(0) for _ in range(number)]
        inputs, job_inputs = take(len(arguments)), take(len(operands))
        outputs, job_outputs = take(len(out_shape)), take(len(shapes))
        own, job_space = take(len(scratch)), refs
        step = pl.program_id(0)
        if jobs:
            here = Where()
            for job in jobs:
                pick = lambda pool, number: [pool.pop(0) for _ in range(number)]
                job.bind(
                    here, pick(job_inputs, len(job.operands)), pick(job_outputs, len(job.shapes)),
                    pick(job_space, len(job.space)),
                )

        def hook(spot):
            for index in range(steps):
                todo = [
                    stage
                    for job in jobs
                    for (late, place), stages in sorted(job.stages.items())
                    if (late * 4 + place) * steps // 4 == index * 4 + spot
                    for stage in stages
                ]
                if todo or (jobs and spot == 0 and index == 0):

                    @pl.when(step == index)
                    def _():
                        if index == 0 and spot == 0:
                            greet_jobs(here)
                        for stage in todo:
                            stage()

        hook(0)
        body(lambda spot: hook(spot) if spot else None, *inputs, *outputs, *own)
        if jobs:

            @pl.when(step == steps - 1)
            def _():
                for job in jobs:
                    for stage in job.last:
                        stage()

    more = {"collective_id": collective_id, "has_side_effects": True} if jobs else {}
    return pl.pallas_call(
        kernel,
        grid=(steps,),
        in_specs=list(in_specs) + sources,
        out_specs=list(out_specs) + specs,
        out_shape=list(out_shape) + shapes,
        scratch_shapes=list(scratch) + space,
        input_output_aliases=aliases,
        compiler_params=pltpu.CompilerParams(
            vmem_limit_bytes=VMEM_LIMIT, dimension_semantics=("arbitrary",), **more
        ),
        cost_estimate=estimate,
        name=name,
    )(*arguments, *operands)


def entry_kernel(
    per_device, row_ref, modulation_ref, *refs
):
    gather = 2 if len(refs) > 5 else 0
    refs = list(refs)
    sources = [refs.pop(0) for _ in range(gather)]
    gathered_ref, mod_ref = refs.pop(0), refs.pop(0)
    targets = [refs.pop(0) for _ in range(gather)]
    part_ref, land_ref, semaphores, *space = refs
    device, rank, dp, tp = place()
    me, count = device * tp + rank, dp * tp
    quarter = land_ref.shape[2]
    if gather:
        here = Where()
        size = sources[0].shape[1] // PARTS
        parts = []
        for index in range(PARTS):
            part = pl.ds(index * size, size)
            parts.append(GatherChain(here, sources[0].at[:, part], targets[0].at[:, :, part], space.pop(0)))
        following = GatherChain(here, sources[1], targets[1], space[0])
    greet_all()

    def tell(index, carry):
        peer = lax.rem(me + index, count)
        push(
            row_ref, gathered_ref.at[me], semaphores.at[0], semaphores.at[1], peer // tp, lax.rem(peer, tp)
        )
        return carry

    lax.fori_loop(1, count, tell, 0)
    gathered_ref[me] = row_ref[...]
    if gather:
        for chain in parts:
            chain.stage_line()
    wait_bytes(gathered_ref.at[pl.ds(0, count - 1)], semaphores.at[1])
    padded = modulation_ref.shape[1]
    width = dp * tp * per_device
    chosen = jnp.zeros((count, padded), jnp.float32)
    row = lax.broadcasted_iota(jnp.int32, (PAIR, padded), 0)
    column = lax.broadcasted_iota(jnp.int32, (PAIR, padded), 1)
    for index in range(width // PAIR):
        match = (row + index * PAIR == column + me * per_device) & (column < per_device)
        chosen += mm(
            gathered_ref[:, index, :].astype(jnp.bfloat16), jnp.where(match, 1.0, 0.0).astype(jnp.bfloat16)
        )
    clip = lax.broadcasted_iota(jnp.int32, (dp, count), 0)
    member = lax.broadcasted_iota(jnp.int32, (dp, count), 1)
    leaders = jnp.where(member == clip * tp, 1.0, 0.0).astype(jnp.bfloat16)
    rows = mm(leaders, chosen.astype(jnp.bfloat16)).astype(jnp.bfloat16)
    for layer in range(modulation_ref.shape[0]):
        part = mm(rows, modulation_ref[layer])
        size = part.shape[1]
        for index in range(dp):
            part_ref[index, :, layer * size : (layer + 1) * size] = part[index : index + 1]

    def share(index, carry):
        peer = lax.rem(me + index, count)
        there, lane = peer // tp, lax.rem(peer, tp)
        source = part_ref.at[there, :, pl.ds(pl.multiple_of(lane * quarter, PAIR), quarter)]
        push(source, land_ref.at[me], semaphores.at[2], semaphores.at[3], there, lane)
        return carry

    lax.fori_loop(1, count, share, 0)
    mine = pl.ds(pl.multiple_of(rank * quarter, PAIR), quarter)
    land_ref[me] = part_ref[device, :, mine]
    if gather:
        for chain in parts:
            chain.line_arrived()
            chain.stage_near()
        following.stage_line()
    wait_bytes(land_ref.at[pl.ds(0, count - 1)], semaphores.at[3])
    mod_ref[:, mine] = jnp.sum(land_ref[...], axis=0)
    for step in range(1, tp):
        push(
            mod_ref.at[:, mine], mod_ref.at[:, mine], semaphores.at[4], semaphores.at[5],
            device, lax.rem(rank + step, tp),
        )
    if gather:
        for chain in parts:
            chain.stage_across()
        for chain in parts:
            chain.stage_core()
    wait_bytes(gathered_ref.at[pl.ds(0, count - 1)], semaphores.at[0])
    wait_bytes(land_ref.at[pl.ds(0, count - 1)], semaphores.at[2])
    wait_bytes(mod_ref.at[:, pl.ds(0, (tp - 1) * quarter)], semaphores.at[5])
    wait_bytes(mod_ref.at[:, pl.ds(0, (tp - 1) * quarter)], semaphores.at[4])
    if gather:
        following.line_arrived()
        for chain in parts:
            chain.finish()
        for chain in (*parts, following):
            chain.line_left()


def enter(row, modulation, per_device, weights, collective_id):
    dp, tp = lax.axis_size("dp"), lax.axis_size("tensor")
    count = dp * tp
    whole = modulation.shape[0] * modulation.shape[2]
    inside = pl.BlockSpec(memory_space=pltpu.VMEM)
    job = FlowJob((), weights) if weights else Job()
    return pl.pallas_call(
        partial(entry_kernel, per_device),
        in_specs=[inside, inside] + anywhere(len(job.operands)),
        out_specs=[inside, inside] + list(job.specs),
        out_shape=[
            jax.ShapeDtypeStruct((count,) + row.shape, jnp.float32),
            jax.ShapeDtypeStruct((1, whole), jnp.float32),
        ] + list(job.shapes),
        scratch_shapes=[
            pltpu.VMEM((dp, 1, whole), jnp.float32),
            pltpu.VMEM((count, 1, whole // tp), jnp.float32),
            pltpu.SemaphoreType.DMA((6,)),
        ] + (GatherChain.scratch() * (PARTS + 1) if weights else []),
        compiler_params=pltpu.CompilerParams(
            collective_id=collective_id, has_side_effects=True, vmem_limit_bytes=VMEM_LIMIT
        ),
        name="enter",
    )(row, modulation, *job.operands)


def adam_update(weight, first, second, grad, rate, decay):
    first_new = BETA_ONE * first + (1.0 - BETA_ONE) * grad
    second_new = BETA_TWO * second + (1.0 - BETA_TWO) * grad * grad
    corrected = (
        first_new
        / (1.0 - BETA_ONE**STEP)
        / (jnp.sqrt(second_new / (1.0 - BETA_TWO**STEP)) + ADAM_EPS)
    )
    weight_new = weight - rate * (corrected + decay * weight)
    return (weight_new, first_new, second_new, weight_new.astype(jnp.bfloat16))


def dot32(form, left, right):
    return jnp.einsum(form, left, right, preferred_element_type=jnp.float32)


def exchange(blocks):
    return lax.all_to_all(blocks, "tensor", split_axis=0, concat_axis=0, tiled=True)


def gather_plain(shard):
    rows, width = shard.shape
    whole = lax.all_gather(shard, ("tensor", "dp"), axis=0, tiled=True)
    return whole.reshape(-1, lax.axis_size("dp") * rows, width)


def scatter_plain(grads):
    kinds, ranks, width, cols = grads.shape
    flat = grads.reshape(kinds, ranks * width, cols)
    summed = lax.psum_scatter(flat, ("tensor", "dp"), scatter_dimension=1, tiled=True)
    return summed.astype(jnp.float32)


def per_device(
    clips, cotangent, timesteps, labels, time_table, class_table,
    attention_weights, attention_first, attention_second,
    ffn_weights, ffn_first, ffn_second,
    modulation_weights, modulation_first, modulation_second,
    bias_vectors, bias_first, bias_second,
):
    layers, kinds, rows, cols = attention_weights.shape
    _, frames, patches, width = clips.shape
    mod_rows = modulation_weights.shape[1]
    bias_cols = bias_vectors.shape[1]
    dp, tp = lax.axis_size("dp"), lax.axis_size("tensor")
    position = lax.axis_index("dp") * tp + lax.axis_index("tensor")
    tokens = frames * patches
    strip = patches // (tp * frames)
    blocks = (tp, frames, frames * strip, width)
    pieces = (tp * frames, frames, strip, width)

    embed = time_table[timesteps] + class_table[labels]
    cond_act = jax.nn.silu(embed).astype(jnp.bfloat16)
    fused = rows % 16 == 0
    shards = [
        (
            pack_heads(attention_weights[layer].astype(jnp.bfloat16)),
            ffn_weights[layer, 0].astype(jnp.bfloat16),
            ffn_weights[layer, 1].astype(jnp.bfloat16),
        )
        for layer in range(layers)
    ]
    low = bias_vectors.astype(jnp.bfloat16).reshape(-1)
    row = jnp.concatenate([cond_act[0], low]).astype(jnp.float32)
    row = jnp.pad(row, (0, -row.shape[0] % 1024)).reshape(-1, 128)
    modulation_low = modulation_weights.astype(jnp.bfloat16)
    modulation_low = jnp.pad(modulation_low, ((0, 0), (0, -mod_rows % 32), (0, 0)))
    gathered, mod, *begun = enter(row, modulation_low, mod_rows, shards[0][:2] if fused else None, 0)
    gathered = gathered.reshape(dp * tp, -1)
    cond_all = gathered[::tp, :width].astype(jnp.bfloat16)
    bias_low = gathered[:, width : width + layers * bias_cols].reshape(dp * tp, layers, bias_cols)
    bias_low = bias_low.transpose(1, 0, 2).reshape(layers, -1)
    cond_rows = lax.dynamic_slice_in_dim(cond_all, position * mod_rows, mod_rows, axis=1)
    cond_rows = jnp.pad(cond_rows, ((0, 0), (0, -mod_rows % 32)))
    mod = mod.reshape(layers, -1)
    mod_width = mod.shape[-1]
    mod = (mod + bias_low[:, -mod_width:]).reshape(layers, 6, width)
    hidden_width = bias_low.shape[1] - mod_width - 4 * width
    bias_up = bias_low[:, 3 * width : 3 * width + hidden_width].reshape(layers, tp, 1, -1)
    bias_out = bias_low[:, None, 2 * width : 3 * width]
    bias_down = bias_low[:, None, 3 * width + hidden_width : 4 * width + hidden_width]
    bias_project = [
        pack_bias(bias_low[layer, :width], bias_low[layer, width : 2 * width], tp) for layer in range(layers)
    ]

    by_patch = lambda v: v.reshape(frames, tp * frames, strip, width).transpose(1, 0, 2, 3)
    cot = by_patch(cotangent[0]).reshape(blocks)
    first = clips[0].reshape(1, frames, patches, width)

    attend = lambda layer, weight, stream, stride, *more: attention_forward(
        weight, stream, mod[layer], bias_project[layer], bias_out[layer], stride, *more
    )
    expand = lambda layer, up, down, middle, *more: ffn_forward(
        up, down, middle.reshape(tokens, width), mod[layer], bias_down[layer], bias_up[layer], *more
    )
    if fused:
        attention_a, up_a = begun
        *heads_a, middle_a, up_a, down_a, attention_b = attend(
            0, attention_a, first, 0, [FlowJob([up_a], [shards[1][0]], None, [shards[0][2]])], 1
        )
        hidden_a, pushed_a, second, attention_b, up_b, down_b = expand(
            0, up_a, down_a, middle_a, StreamJob(blocks, frames),
            [FlowJob([attention_b], [shards[1][2]], dp // 8, [shards[1][1]])], 2,
        )
        *heads_b, middle_b, down_b = attend(1, attention_b, second, strip, [FlowJob([down_b], [])], 3)
        hidden_b, pushed_b, result, cot = expand(1, up_b, down_b, middle_b, None, [SwapJob(cot)], 4)
    else:
        (attention_a, up_a, down_a), (attention_b, up_b, down_b) = [[gather_plain(v) for v in group] for group in shards]
        *heads_a, middle_a = attend(0, attention_a, first, 0)
        hidden_a, pushed_a, second = expand(0, up_a, down_a, middle_a)
        second = exchange(by_patch(second).reshape(blocks))
        *heads_b, middle_b = attend(1, attention_b, second, strip)
        hidden_b, pushed_b, result = expand(1, up_b, down_b, middle_b)
        cot = exchange(cot)
    middle_a, middle_b = middle_a.reshape(tokens, width), middle_b.reshape(tokens, width)
    result = result.reshape(blocks)
    cot = cot.reshape(tokens, width)

    if fused:
        grad, ffn_grad, *sums_b, result = ffn_backward(
            up_b, down_b, cot, middle_b, pushed_b, hidden_b, mod[1], [SwapJob(result)], 5
        )
        packed_b, *more_b, grad, line_up = attention_backward(
            attention_b, grad.reshape(blocks), second, heads_b, mod[1], strip,
            StreamJob(blocks, 0), [ScatterJob([(ffn_grad, 0)], 3 * dp // 8)], 6,
        )
        waiting = [(ffn_grad, 1), (packed_b[None], 0)]
        grad, ffn_grad, *sums_a, done_up, line_b = ffn_backward(
            up_a, down_a, grad.reshape(pieces), middle_a, pushed_a, hidden_a, mod[0],
            [LineJob(line_up), ScatterJob(waiting, dp // 4)], 7,
        )
        grad, packed_a, *more_a, done_b, line_ffn_a, done_up_a = attention_backward(
            attention_a, grad.reshape(first.shape), first, heads_a, mod[0], 0, None,
            [LineJob(line_b), ScatterJob([(ffn_grad, 0), (ffn_grad, 1)], dp // 4, True)], 8,
        )
        done_ffn_b, done_b = jnp.concatenate([done_up, done_b[:1]]), done_b[1:]
    else:
        result = exchange(result)
        grad, ffn_grad, *sums_b = ffn_backward(up_b, down_b, cot, middle_b, pushed_b, hidden_b, mod[1])
        done_ffn_b = scatter_plain(ffn_grad)
        grad, packed_b, *more_b = attention_backward(
            attention_b, grad.reshape(blocks), second, heads_b, mod[1], strip
        )
        done_b = scatter_plain(packed_b[None])
        grad = exchange(grad.astype(jnp.bfloat16))
        grad, ffn_grad, *sums_a = ffn_backward(up_a, down_a, grad.reshape(pieces), middle_a, pushed_a, hidden_a, mod[0])
        done_ffn_a = scatter_plain(ffn_grad)
        grad, packed_a, *more_a = attention_backward(attention_a, grad.reshape(first.shape), first, heads_a, mod[0], 0)
        done_a = scatter_plain(packed_a[None])
    output = result.reshape(pieces).transpose(1, 0, 2, 3).reshape(clips.shape)
    input_grad = grad.reshape(clips.shape)

    def gather_small(more, sums):
        attention_sums, project_sum = more
        up_sum, low_sums = sums
        return jnp.concatenate(
            [*unpack_bias(project_sum), attention_sums[0], up_sum.reshape(-1), low_sums[0],
             attention_sums[1:].reshape(-1), low_sums[1:].reshape(-1)]
        )

    small = jnp.stack([gather_small(more_a, sums_a), gather_small(more_b, sums_b)])
    token_width = small.shape[1] - mod_width
    *done, small, grad_act = leave(
        small.reshape(tp, -1, 128), modulation_low, token_width,
        *((packed_a, line_ffn_a) if fused else (None, None)), 9,
    )
    if fused:
        done_a, done_ffn_a = done[0][None], jnp.concatenate([done_up_a, done[1]])
    small = small.transpose(1, 0, 2, 3).reshape(dp, layers, -1)
    grad_mod_low = small[..., token_width:].astype(jnp.bfloat16)
    grad_bias_all = jnp.concatenate(
        [small[..., :token_width], grad_mod_low.astype(jnp.float32)], axis=-1
    ).sum(axis=0)
    grad_bias = lax.dynamic_slice_in_dim(grad_bias_all, position * bias_cols, bias_cols, axis=1)
    grad_mod_weight = dot32("ck,cle->lke", cond_rows, grad_mod_low)[:, :mod_rows]
    grad_act = lax.dynamic_index_in_dim(
        grad_act[:, :, :mod_rows], lax.axis_index("dp"), axis=1, keepdims=False
    )
    grad_attention = jnp.stack([unpack_heads(done_a[0]), unpack_heads(done_b[0])])
    grad_ffn = jnp.stack([done_ffn_a, done_ffn_b])
    silu_value, silu_pull = jax.vjp(jax.nn.silu, embed)
    cond_grad = silu_pull(grad_act.reshape(1, width))[0]

    return (output, input_grad, cond_grad) + (
        adam_update(attention_weights, attention_first, attention_second, grad_attention, MATRIX_RATE, MATRIX_DECAY)
        + adam_update(ffn_weights, ffn_first, ffn_second, grad_ffn, MATRIX_RATE, MATRIX_DECAY)
        + adam_update(modulation_weights, modulation_first, modulation_second, grad_mod_weight, MATRIX_RATE, MATRIX_DECAY)
        + adam_update(bias_vectors, bias_first, bias_second, grad_bias, VECTOR_RATE, 0.0)
    )


def solution(mesh):
    tokens = P("dp", "tensor", None, None)
    matrix = P(None, None, "dp", "tensor")
    modulation = P(None, BOTH, None)
    vector = P(None, BOTH)
    return jax.shard_map(
        per_device,
        mesh=mesh,
        in_specs=(tokens, tokens, P("dp"), P("dp"), P(), P())
        + (matrix,) * 6 + (modulation,) * 3 + (vector,) * 3,
        out_specs=(tokens, tokens, P("dp", None)) + (matrix,) * 8 + (modulation,) * 4 + (vector,) * 4,
        check_vma=False,
    )
```

```python
from functools import partial

import jax
import jax.numpy as jnp
from jax import lax
from jax.experimental import pallas as pl
from jax.experimental.pallas import tpu as pltpu
from jax.sharding import PartitionSpec as P

HD = 64
PAIR = 128
BLOCK = 256
PARTS = 3
STEP = 10
BETA_ONE = 0.9
BETA_TWO = 0.999
ADAM_EPS = 1e-08
MATRIX_RATE = 0.04
VECTOR_RATE = 0.2
MATRIX_DECAY = 0.1
NORM_EPS = 1e-06
GELU_A = (2.0 / 3.141592653589793) ** 0.5
GELU_B = 0.044715
BLOCKED = -1e30
VMEM_LIMIT = 60 * 1024 * 1024
BOTH = ("dp", "tensor")


def mm(left, right, dims=((1,), (0,))):
    return lax.dot_general(left, right, (dims, ((), ())), preferred_element_type=jnp.float32)


def norm_parts(value):
    average = jnp.mean(value, axis=-1, keepdims=True)
    centred = value - average
    spread = jnp.mean(centred * centred, axis=-1, keepdims=True)
    inverse = lax.rsqrt(spread + NORM_EPS)
    return centred * inverse, inverse


def norm_back(grad, shape, inverse):
    first = jnp.mean(grad, axis=-1, keepdims=True)
    second = jnp.mean(grad * shape, axis=-1, keepdims=True)
    return inverse * (grad - first - shape * second)


def rows_of(ref):
    value = ref[...]
    return value.reshape(-1, value.shape[-1])


def put(ref, value):
    ref[...] = value.reshape(ref.shape).astype(ref.dtype)


def add_rows(ref, index, value):
    ref[pl.ds(index, 1), :] += jnp.sum(value, axis=0, keepdims=True)


def half_masks(rows):
    lane = lax.broadcasted_iota(jnp.int32, (rows, PAIR), 1)
    return lane < HD


def same_patch(tokens, stride):
    row = lax.broadcasted_iota(jnp.int32, (tokens, tokens), 0)
    column = lax.broadcasted_iota(jnp.int32, (tokens, tokens), 1)
    return lax.rem(row, stride) == lax.rem(column, stride)


def by_halves(value):
    rows, width = value.shape
    return value.reshape(-1, 2, 8, width).transpose(1, 0, 2, 3).reshape(rows, width)


def from_halves(value):
    rows, width = value.shape
    return value.reshape(2, -1, 8, width).transpose(1, 0, 2, 3).reshape(rows, width)


def swap_halves(value):
    return pltpu.roll(value, HD, 1)


def start_loads(source, target, semaphores):
    for rank in range(target.shape[0]):
        pltpu.make_async_copy(source.at[rank], target.at[rank], semaphores.at[rank]).start()


def start_columns(source, target, semaphores):
    part = source.shape[2]
    for rank in range(source.shape[0]):
        columns = pl.ds(rank * part, part)
        pltpu.make_async_copy(source.at[rank], target.at[:, columns], semaphores.at[rank]).start()


def wait_columns(target, semaphores, rank, part):
    columns = target.at[:, pl.ds(0, part)]
    pltpu.make_async_copy(columns, columns, semaphores.at[rank]).wait()


def wait_loads(target, semaphores, rank):
    pltpu.make_async_copy(target.at[rank], target.at[rank], semaphores.at[rank]).wait()


def softmax_rows(scores, axis):
    raised = jnp.exp(scores - jnp.max(scores, axis=axis, keepdims=True))
    return raised * (1.0 / jnp.sum(raised, axis=axis, keepdims=True))


def attention_forward_kernel(
    stride, hook, source, stream_ref, mod_ref, bias_ref, bias_out_ref,
    project_ref, mixed_ref, branch_ref, middle_ref, weight_ref, semaphores,
):
    ranks = weight_ref.shape[0]

    @pl.when(pl.program_id(0) == 0)
    def _():
        start_loads(source, weight_ref, semaphores)

    stream = rows_of(stream_ref).astype(jnp.float32)
    if stride:
        stream = by_halves(stream)
    tokens, width = stream.shape
    size = tokens // 2 if stride else tokens
    spans = [slice(start, start + size) for start in range(0, tokens, size)]
    shape, _ = norm_parts(stream)
    normed = (shape * (1.0 + mod_ref[1:2]) + mod_ref[0:1]).astype(jnp.bfloat16)
    lower = half_masks(tokens)
    allowed = same_patch(size, stride // 2) if stride else None

    @pl.when(pl.program_id(0) == 0)
    def _():
        for rank in range(ranks):
            wait_loads(weight_ref, semaphores, rank)

    def one_head(chosen, key, value):
        chosen, outs = chosen.astype(jnp.bfloat16), []
        for span in spans:
            scores = mm(chosen[span], key[span], ((1,), (1,)))
            if stride:
                scores = jnp.where(allowed, scores, BLOCKED)
            outs.append(mm(softmax_rows(scores, -1).astype(jnp.bfloat16), value[span]))
        return jnp.concatenate(outs, axis=0)

    branch = None
    for rank in range(ranks):
        hook(rank)
        project = (mm(normed, weight_ref[rank, :, : 5 * PAIR]) + bias_ref[rank]).astype(jnp.bfloat16)
        project_ref[rank] = project.reshape(project_ref.shape[1:])
        query = project[:, :PAIR].astype(jnp.float32) * HD**-0.5
        key, value = project[:, PAIR : 2 * PAIR], project[:, 2 * PAIR : 3 * PAIR]
        first = one_head(jnp.where(lower, query, 0.0), key, value)
        second = one_head(jnp.where(lower, 0.0, query), key, value)
        both = project[:, 3 * PAIR : 4 * PAIR].astype(jnp.float32)
        last = one_head(
            jnp.where(lower, both * HD**-0.5, 0.0),
            swap_halves(both).astype(jnp.bfloat16),
            project[:, 4 * PAIR : 5 * PAIR],
        )
        mixed = jnp.concatenate(
            [jnp.where(lower, 0.0, swap_halves(last)), jnp.where(lower, first, second)], axis=1
        ).astype(jnp.bfloat16)
        mixed_ref[rank] = mixed.reshape(mixed_ref.shape[1:])
        term = mm(mixed, weight_ref[rank, :, 4 * PAIR :], ((1,), (1,)))
        branch = term if branch is None else branch + term
    branch = branch + bias_out_ref[...]
    middle = stream + mod_ref[2:3] * branch
    if stride:
        branch, middle = from_halves(branch), from_halves(middle)
    put(branch_ref, branch)
    put(middle_ref, middle)


def gelu_parts(value):
    square = value * value
    bent = jnp.tanh(value * (GELU_A + (GELU_A * GELU_B) * square))
    half = 0.5 * (1.0 + bent)
    slope = half + (0.5 * value) * (1.0 - bent * bent) * (GELU_A + (3.0 * GELU_A * GELU_B) * square)
    return value * half, slope


def ffn_forward_kernel(
    stream, hook, up_source, down_source, middle_ref, mod_ref, bias_ref, bias_up_ref, hidden_ref, branch_ref, *rest
):
    if stream is None:
        result_ref, *rest = rest
    up_ref, down_ref, up_semaphores, down_semaphores, active_ref = rest
    step = pl.program_id(0)
    ranks, _, part = hidden_ref.shape

    @pl.when(step == 0)
    def _():
        start_columns(up_source, up_ref, up_semaphores)
        start_columns(down_source, down_ref, down_semaphores)

    middle = middle_ref[...]
    shape, _ = norm_parts(middle)
    second = (shape * (1.0 + mod_ref[4:5]) + mod_ref[3:4]).astype(jnp.bfloat16)

    @pl.when(step == 0)
    def _():
        for rank in range(ranks):
            wait_columns(up_ref, up_semaphores, rank, part)
            wait_columns(down_ref, down_semaphores, rank, part)

    for rank in range(ranks):
        hook(rank)
        for start in range(0, part, BLOCK):
            inside = slice(start, start + BLOCK)
            columns = slice(rank * part + start, rank * part + start + BLOCK)
            hidden = mm(second, up_ref[:, columns]) + bias_up_ref[rank, :, inside]
            hidden_ref[rank, :, inside] = hidden.astype(jnp.bfloat16)
            active, _ = gelu_parts(hidden)
            active_ref[:, columns] = active.astype(jnp.bfloat16)
    down = mm(active_ref[...], down_ref[...], ((1,), (1,))) + bias_ref[...]
    branch_ref[...] = down.astype(jnp.bfloat16)
    result = middle + mod_ref[5:6] * down
    if stream is None:
        result_ref[...] = result.astype(result_ref.dtype)
    else:
        stream.put(step, result)


def load_rows(ref, index, chunk):
    if len(ref.shape) == 2:
        return ref[index * chunk : (index + 1) * chunk, :].astype(jnp.float32)
    blocks, _, strip, width = ref.shape
    frames = chunk // (blocks * strip)
    parts = [ref[:, index * frames + frame].reshape(blocks * strip, width) for frame in range(frames)]
    return jnp.concatenate(parts, axis=0).astype(jnp.float32)


def ffn_backward_kernel(
    split, hook, up_source, down_source, grad_ref, middle_ref, branch_ref, hidden_ref, mod_ref,
    grad_middle_ref, weight_grad_ref, up_sum_ref, sums_ref,
    up_ref, down_ref, up_semaphores, down_semaphores,
    second_ref, low_ref, low_across_ref, active_ref, slope_ref,
):
    step = pl.program_id(0)
    tokens, width = middle_ref.shape
    part = hidden_ref.shape[2]
    chunk = tokens // split

    @pl.when(step == 0)
    def _():
        start_columns(down_source, down_ref, down_semaphores)
        start_columns(up_source, up_ref, up_semaphores)
        sums_ref[...] = jnp.zeros_like(sums_ref)
        for index in range(split):
            rows = slice(index * chunk, (index + 1) * chunk)
            grad = load_rows(grad_ref, index, chunk)
            low = (mod_ref[5:6] * grad).astype(jnp.bfloat16)
            low_ref[rows, :] = low
            low_across_ref[:, rows] = low.T
            add_rows(sums_ref, 0, low.astype(jnp.float32))
            add_rows(sums_ref, 3, grad * branch_ref[rows, :].astype(jnp.float32))
            shape, _ = norm_parts(middle_ref[rows, :])
            second = (shape * (1.0 + mod_ref[4:5]) + mod_ref[3:4]).astype(jnp.bfloat16)
            second_ref[:, rows] = second.T

    up_sum_ref[...] = jnp.zeros_like(up_sum_ref)
    wait_columns(down_ref, down_semaphores, step, part)
    for index in range(split):
        if index == split // 2:
            hook(1)
        rows = slice(index * chunk, (index + 1) * chunk)
        for start in range(0, part, BLOCK):
            inside = slice(start, start + BLOCK)
            columns = pl.ds(pl.multiple_of(step * part + start, BLOCK), BLOCK)
            active, slope = gelu_parts(hidden_ref[0, rows, inside].astype(jnp.float32))
            active_ref[rows, inside] = active.astype(jnp.bfloat16)
            low = (mm(low_ref[rows, :], down_ref[:, columns]) * slope).astype(jnp.bfloat16)
            slope_ref[rows, columns] = low
            up_sum_ref[0, :, inside] += jnp.sum(low.astype(jnp.float32), axis=0, keepdims=True)
    hook(2)
    whole = pl.ds(pl.multiple_of(step * part, BLOCK), part)
    weight_grad_ref[0, 0] = mm(second_ref[...], slope_ref[:, whole]).astype(jnp.bfloat16)
    hook(3)
    weight_grad_ref[1, 0] = mm(low_across_ref[...], active_ref[...]).astype(jnp.bfloat16)

    @pl.when(step == pl.num_programs(0) - 1)
    def _():
        for rank in range(up_source.shape[0]):
            wait_columns(up_ref, up_semaphores, rank, part)
        for index in range(split):
            rows = slice(index * chunk, (index + 1) * chunk)
            shape, inverse = norm_parts(middle_ref[rows, :])
            grad = mm(slope_ref[rows, :], up_ref[...], ((1,), (1,)))
            add_rows(sums_ref, 1, grad)
            add_rows(sums_ref, 2, grad * shape)
            back = norm_back(grad * (1.0 + mod_ref[4:5]), shape, inverse)
            grad_middle_ref[rows, :] = load_rows(grad_ref, index, chunk) + back


def attention_backward_kernel(
    stride, swap, hook, source, grad_ref, stream_ref, project_ref, mixed_ref, branch_ref, mod_ref, *refs
):
    if swap is None:
        grad_stream_ref, *refs = refs
    (weight_grad_ref, sums_ref, project_sum_ref,
     weight_ref, semaphores, left_ref, right_ref, outer_ref) = refs
    step = pl.program_id(0)
    ranks = weight_ref.shape[0]

    @pl.when(step == 0)
    def _():
        start_loads(source, weight_ref, semaphores)
        sums_ref[...] = jnp.zeros_like(sums_ref)
        project_sum_ref[...] = jnp.zeros_like(project_sum_ref)

    grad_middle = rows_of(grad_ref)
    tokens, width = grad_middle.shape
    stream = rows_of(stream_ref).astype(jnp.float32)
    branch = rows_of(branch_ref).astype(jnp.float32)
    if stride:
        grad_middle, stream, branch = by_halves(grad_middle), by_halves(stream), by_halves(branch)
    size = tokens // 2 if stride else tokens
    spans = [slice(start, start + size) for start in range(0, tokens, size)]
    shape, inverse = norm_parts(stream)
    rows = pl.ds(pl.multiple_of(step * tokens, tokens), tokens)
    normed = (shape * (1.0 + mod_ref[1:2]) + mod_ref[0:1]).astype(jnp.bfloat16)
    low = (mod_ref[2:3] * grad_middle).astype(jnp.bfloat16)
    left_ref[0, :, rows] = normed.T
    left_ref[1, :, rows] = low.T
    add_rows(sums_ref, 0, low.astype(jnp.float32))
    add_rows(sums_ref, 3, grad_middle * branch)
    lower = half_masks(tokens)
    allowed = same_patch(size, stride // 2) if stride else None
    scale = HD**-0.5

    @pl.when(step == 0)
    def _():
        for rank in range(ranks):
            wait_loads(weight_ref, semaphores, rank)

    def one_head(chosen, key, value, taken):
        chosen, taken, outs = chosen.astype(jnp.bfloat16), taken.astype(jnp.bfloat16), []
        for span in spans:
            scores = mm(key[span], chosen[span], ((1,), (1,)))
            if stride:
                scores = jnp.where(allowed, scores, BLOCKED)
            probs = softmax_rows(scores, 0)
            grad_probs = mm(value[span], taken[span], ((1,), (1,)))
            inner = jnp.sum(grad_probs * probs, axis=0, keepdims=True)
            outs.append((probs.astype(jnp.bfloat16), (probs * (grad_probs - inner)).astype(jnp.bfloat16)))
        return outs

    def times(lefts, right, dims=((1,), (0,))):
        parts = [mm(left, right[span], dims) for left, span in zip(lefts, spans)]
        return jnp.concatenate(parts, axis=0)

    grad_normed = None
    for rank in range(ranks):
        hook(rank)
        project = project_ref[rank].reshape(tokens, 5 * PAIR)
        mixed = mixed_ref[rank].reshape(tokens, 2 * PAIR)
        outer_ref[rank, rows, :] = mixed
        grad_mixed = mm(low, weight_ref[rank, :, 4 * PAIR :]).astype(jnp.bfloat16)
        query, key, value = (project[:, n * PAIR : (n + 1) * PAIR] for n in range(3))
        query_wide = query.astype(jnp.float32) * scale
        pair = grad_mixed[:, PAIR:]
        pair_wide = pair.astype(jnp.float32)
        outs = []
        for keep in (lower, ~lower):
            probs, grad_scores = zip(
                *one_head(jnp.where(keep, query_wide, 0.0), key, value, jnp.where(keep, pair_wide, 0.0))
            )
            outs.append(
                (times(grad_scores, key, ((0,), (0,))), times(grad_scores, query), times(probs, pair))
            )
        parts = [
            jnp.where(lower, one, two) * factor
            for one, two, factor in zip(outs[0], outs[1], (scale, scale, 1.0))
        ]
        both = project[:, 3 * PAIR : 4 * PAIR].astype(jnp.float32)
        swapped = swap_halves(both).astype(jnp.bfloat16)
        single = swap_halves(grad_mixed[:, :PAIR].astype(jnp.float32))
        probs, grad_scores = zip(
            *one_head(
                jnp.where(lower, both * scale, 0.0),
                swapped,
                project[:, 4 * PAIR :],
                jnp.where(lower, single, 0.0),
            )
        )
        parts.append(
            jnp.where(lower, times(grad_scores, swapped, ((0,), (0,))), times(grad_scores, swapped)) * scale
        )
        parts.append(jnp.where(lower, times(probs, single.astype(jnp.bfloat16)), 0.0))
        whole = jnp.concatenate(parts, axis=1).astype(jnp.bfloat16)
        right_ref[rank, rows, :] = whole
        add_rows(project_sum_ref, rank, whole.astype(jnp.float32))
        term = mm(whole, weight_ref[rank, :, : 5 * PAIR], ((1,), (1,)))
        grad_normed = term if grad_normed is None else grad_normed + term
    add_rows(sums_ref, 1, grad_normed)
    add_rows(sums_ref, 2, grad_normed * shape)
    back = norm_back(grad_normed * (1.0 + mod_ref[1:2]), shape, inverse)
    result = grad_middle + back
    if stride:
        result = from_halves(result)
    if swap is None:
        put(grad_stream_ref, result)
    else:
        swap.put(step, result)

    @pl.when(step == pl.num_programs(0) - 1)
    def _():
        def weights(rank, carry):
            inside = mm(left_ref[0], right_ref[rank])
            outside = mm(left_ref[1], outer_ref[rank])
            weight_grad_ref[rank, :, : 4 * PAIR] = inside[:, : 4 * PAIR].astype(jnp.bfloat16)
            weight_grad_ref[rank, :, 4 * PAIR : 5 * PAIR] = (
                inside[:, 4 * PAIR :] + outside[:, :PAIR]
            ).astype(jnp.bfloat16)
            weight_grad_ref[rank, :, 5 * PAIR :] = outside[:, PAIR:].astype(jnp.bfloat16)
            return carry

        lax.fori_loop(0, ranks, weights, 0)


def fixed(shape):
    return pl.BlockSpec(shape, lambda step: (0,) * len(shape), pipeline_mode=pl.Buffered(1))


def cost(flops, moved, raised=0):
    return pl.CostEstimate(flops=int(flops), bytes_accessed=int(moved), transcendentals=int(raised))


def group_spec(shape):
    return pl.BlockSpec((shape[0], 1, shape[2], shape[3]), lambda step: (0, step, 0, 0))


def rank_spec(shape):
    return pl.BlockSpec((shape[0], shape[1], 1) + shape[3:], lambda step: (0, 0, step, 0, 0))


def attention_forward(weight, stream, mod, bias, bias_out, stride, jobs=(), collective_id=None):
    shape = stream.shape
    width = shape[-1]
    ranks = bias.shape[0]
    tokens = shape[0] * shape[1] * shape[2]
    spec = group_spec(shape)
    low = jax.ShapeDtypeStruct(shape, jnp.bfloat16)
    wide = jax.ShapeDtypeStruct(shape, jnp.float32)
    project = jax.ShapeDtypeStruct((ranks,) + shape[:3] + (5 * PAIR,), jnp.bfloat16)
    mixed = jax.ShapeDtypeStruct((ranks,) + shape[:3] + (2 * PAIR,), jnp.bfloat16)
    return call(
        partial(attention_forward_kernel, stride),
        shape[1],
        [weight, stream, mod, bias, bias_out],
        anywhere(1) + [spec, fixed(mod.shape), fixed(bias.shape), fixed(bias_out.shape)],
        [project, mixed, low, wide],
        [rank_spec(project.shape), rank_spec(mixed.shape), spec, spec],
        [pltpu.VMEM((ranks, width, 6 * PAIR), jnp.bfloat16), pltpu.SemaphoreType.DMA((ranks,))],
        jobs,
        collective_id,
        cost(8 * tokens * width * width * 1.5, tokens * width * 16),
        "attention_forward",
    )


def ffn_weights_scratch(ranks, width, part):
    return [
        pltpu.VMEM((width, ranks * part), jnp.bfloat16),
        pltpu.VMEM((width, ranks * part), jnp.bfloat16),
        pltpu.SemaphoreType.DMA((ranks,)),
        pltpu.SemaphoreType.DMA((ranks,)),
    ]


def ffn_forward(up, down, middle, mod, bias_down, bias_up, stream=None, jobs=(), collective_id=None):
    tokens, width = middle.shape
    ranks, _, part = bias_up.shape
    steps = 4
    chunk = tokens // steps
    block = pl.BlockSpec((chunk, width), lambda step: (step, 0))
    result = [jax.ShapeDtypeStruct((tokens, width), jnp.bfloat16)] if stream is None else []
    return call(
        partial(ffn_forward_kernel, stream),
        steps,
        [up, down, middle, mod, bias_down, bias_up],
        anywhere(2) + [block, fixed(mod.shape), fixed(bias_down.shape), fixed(bias_up.shape)],
        [
            jax.ShapeDtypeStruct((ranks, tokens, part), jnp.bfloat16),
            jax.ShapeDtypeStruct((tokens, width), jnp.bfloat16),
        ] + result,
        [pl.BlockSpec((ranks, chunk, part), lambda step: (0, step, 0)), block] + [block] * len(result),
        ffn_weights_scratch(ranks, width, part) + [pltpu.VMEM((chunk, ranks * part), jnp.bfloat16)],
        ([] if stream is None else [stream]) + list(jobs),
        collective_id,
        cost(4.8 * tokens * width * ranks * part, tokens * width * 14, tokens * ranks * part),
        "ffn_forward",
    )


def ffn_backward(up, down, grad, middle, branch, hidden, mod, jobs=(), collective_id=None):
    tokens, width = middle.shape
    ranks, _, part = hidden.shape
    whole = fixed((tokens, width))
    return call(
        partial(ffn_backward_kernel, 4),
        ranks,
        [up, down, grad, middle, branch, hidden, mod],
        anywhere(2) + [
            fixed(grad.shape), whole, whole,
            pl.BlockSpec((1, tokens, part), lambda step: (step, 0, 0)),
            fixed(mod.shape),
        ],
        [
            jax.ShapeDtypeStruct((tokens, width), jnp.float32),
            jax.ShapeDtypeStruct((2, ranks, width, part), jnp.bfloat16),
            jax.ShapeDtypeStruct((ranks, 1, part), jnp.float32),
            jax.ShapeDtypeStruct((4, width), jnp.float32),
        ],
        [
            whole,
            pl.BlockSpec((2, 1, width, part), lambda step: (0, step, 0, 0)),
            pl.BlockSpec((1, 1, part), lambda step: (step, 0, 0)),
            fixed((4, width)),
        ],
        ffn_weights_scratch(ranks, width, part) + [
            pltpu.VMEM((width, tokens), jnp.bfloat16),
            pltpu.VMEM((tokens, width), jnp.bfloat16),
            pltpu.VMEM((width, tokens), jnp.bfloat16),
            pltpu.VMEM((tokens, part), jnp.bfloat16),
            pltpu.VMEM((tokens, ranks * part), jnp.bfloat16),
        ],
        jobs,
        collective_id,
        cost(9.6 * tokens * width * ranks * part, tokens * width * 20, tokens * ranks * part),
        "ffn_backward",
    )


def attention_backward(weight, grad, stream, saved, mod, stride, swap=None, jobs=(), collective_id=None):
    project, mixed, branch = saved
    shape = stream.shape
    width = shape[-1]
    ranks = project.shape[0]
    tokens = shape[0] * shape[1] * shape[2]
    spec = group_spec(shape)
    result = [jax.ShapeDtypeStruct(shape, jnp.float32)] if swap is None else []
    return call(
        partial(attention_backward_kernel, stride, swap),
        shape[1],
        [weight, grad, stream, project, mixed, branch, mod],
        anywhere(1) + [
            spec, spec, rank_spec(project.shape), rank_spec(mixed.shape), spec, fixed(mod.shape),
        ],
        result + [
            jax.ShapeDtypeStruct((ranks, width, 6 * PAIR), jnp.bfloat16),
            jax.ShapeDtypeStruct((4, width), jnp.float32),
            jax.ShapeDtypeStruct((ranks, 5 * PAIR), jnp.float32),
        ],
        [spec] * len(result) + [
            fixed((ranks, width, 6 * PAIR)), fixed((4, width)), fixed((ranks, 5 * PAIR)),
        ],
        [
            pltpu.VMEM((ranks, width, 6 * PAIR), jnp.bfloat16),
            pltpu.SemaphoreType.DMA((ranks,)),
            pltpu.VMEM((2, width, tokens), jnp.bfloat16),
            pltpu.VMEM((ranks, tokens, 5 * PAIR), jnp.bfloat16),
            pltpu.VMEM((ranks, tokens, 2 * PAIR), jnp.bfloat16),
        ],
        ([] if swap is None else [swap]) + list(jobs),
        collective_id,
        cost(16 * tokens * width * width * 1.5, tokens * width * 20),
        "attention_backward",
    )


def pack_heads(block):
    query, key, value, outer = block
    return jnp.concatenate(
        [query[:, :PAIR], key[:, :PAIR], value[:, :PAIR], query[:, PAIR:], key[:, PAIR:],
         value[:, PAIR:], outer[:, PAIR:], outer[:, :PAIR]], axis=1
    )


def unpack_heads(packed):
    part = lambda start, size: packed[:, start : start + size]
    join = lambda first, last: jnp.concatenate([part(first, PAIR), part(last, HD)], axis=1)
    return jnp.stack(
        [join(0, 3 * PAIR), join(PAIR, 3 * PAIR + HD), join(2 * PAIR, 4 * PAIR), join(5 * PAIR, 4 * PAIR + HD)]
    )


def pack_bias(query, value, ranks):
    query, value = query.reshape(ranks, -1), value.reshape(ranks, -1)
    none = jnp.zeros((ranks, PAIR), query.dtype)
    return jnp.concatenate(
        [query[:, :PAIR], none, value[:, :PAIR], query[:, PAIR:], none[:, :HD], value[:, PAIR:], none[:, :HD]],
        axis=1,
    )[:, None]


def unpack_bias(sums):
    query = jnp.concatenate([sums[:, :PAIR], sums[:, 3 * PAIR : 3 * PAIR + HD]], axis=1)
    value = jnp.concatenate([sums[:, 2 * PAIR : 3 * PAIR], sums[:, 4 * PAIR : 4 * PAIR + HD]], axis=1)
    return query.reshape(-1), value.reshape(-1)


def place():
    return lax.axis_index("dp"), lax.axis_index("tensor"), lax.axis_size("dp"), lax.axis_size("tensor")


def greet_all():
    device, rank, dp, tp = place()
    me, count = device * tp + rank, dp * tp
    barrier = pltpu.get_barrier_semaphore()

    def greet(index, carry):
        peer = lax.rem(me + index, count)
        pl.semaphore_signal(
            barrier, inc=1, device_id=(peer // tp, lax.rem(peer, tp)), device_id_type=pl.DeviceIdType.MESH
        )
        return carry

    lax.fori_loop(1, count, greet, 0)
    pl.semaphore_wait(barrier, count - 1)


def push(source, target, send, receive, device, rank):
    pltpu.make_async_remote_copy(
        src_ref=source, dst_ref=target, send_sem=send, recv_sem=receive,
        device_id=(device, rank), device_id_type=pl.DeviceIdType.MESH,
    ).start()


def wait_bytes(ref, semaphore):
    pltpu.make_async_copy(ref, ref, semaphore).wait()


class Where:
    def __init__(self):
        device, rank = lax.axis_index("dp"), lax.axis_index("tensor")
        self.count = lax.axis_size("dp") // 2
        self.device, self.rank = device, rank
        self.far, self.side = device // 2, lax.rem(device, 2)
        self.row, self.core = rank // 2, lax.rem(rank, 2)
        self.other_side = self.far * 2 + 1 - self.side
        self.other_row = (1 - self.row) * 2 + self.core
        self.other_core = self.row * 2 + 1 - self.core

    def ahead(self, step):
        return lax.rem(self.far + step, self.count)

    def line(self, step):
        return self.ahead(step) * 2 + self.side


def greet_neighbours(here):
    barrier = pltpu.get_barrier_semaphore()
    peers = [(here.other_side, here.rank), (here.device, here.other_row), (here.device, here.other_core)]
    peers += [(here.line(step), here.rank) for step in range(1, here.count)]
    for peer in peers:
        pl.semaphore_signal(barrier, inc=1, device_id=peer, device_id_type=pl.DeviceIdType.MESH)
    pl.semaphore_wait(barrier, len(peers))


def add_into(target, left, right):
    target[...] = (left[...].astype(jnp.float32) + right[...].astype(jnp.float32)).astype(target.dtype)


class ScatterChain:
    def __init__(self, here, source, line, lead, scratch):
        self.here, self.source, self.line, self.lead = here, source, line, lead
        self.keep, self.land_core, self.first_one, self.last_one, self.first_two, self.last_two, self.semaphores = scratch
        self.rows = line.shape[1]

    @staticmethod
    def scratch(width, columns, dp, lead):
        rows, far = width // dp, dp // 2
        low = lambda *shape: pltpu.VMEM(shape + (columns,), jnp.bfloat16)
        return [
            low(2, width), low(2, width),
            low(2, lead, rows), low(2 * (far - lead) * rows), low(lead, rows), low(far - lead, rows),
            pltpu.SemaphoreType.DMA((6, 2)),
        ]

    def chunk(self, row, far, side):
        return self.keep.at[row, pl.ds(pl.multiple_of((far * 2 + side) * self.rows, self.rows), self.rows)]

    def send(self, slot, source, target, device, rank):
        push(source, target, self.semaphores.at[slot, 0], self.semaphores.at[slot, 1], device, rank)

    def arrived(self, slot, ref):
        wait_bytes(ref, self.semaphores.at[slot, 1])

    def left(self, slot, ref):
        wait_bytes(ref, self.semaphores.at[slot, 0])

    def stage_core(self):
        here = self.here
        for row in range(2):
            pltpu.make_async_copy(
                self.source.at[row * 2 + here.core], self.keep.at[row], self.semaphores.at[5, 0]
            ).start()
            self.send(0, self.source.at[row * 2 + 1 - here.core], self.land_core.at[row], here.device, here.other_core)

    def stage_one(self):
        here = self.here
        wait_bytes(self.keep, self.semaphores.at[5, 0])
        self.arrived(0, self.land_core)

        def one(index, carry):
            rows = pl.ds(pl.multiple_of(index * self.rows, self.rows), self.rows)
            for row in range(2):
                add_into(self.keep.at[row, rows], self.keep.at[row, rows], self.land_core.at[row, rows])
            return carry

        lax.fori_loop(0, here.count * 2, one, 0)
        for row in range(2):
            for far in range(self.lead):
                self.send(
                    1, self.chunk(row, far, 1 - here.side), self.first_one.at[row, far], here.other_side, here.rank
                )
        start, size = self.lead * 2 * self.rows, (here.count - self.lead) * 2 * self.rows
        self.send(2, self.keep.at[1 - here.row, pl.ds(start, size)], self.last_one, here.device, here.other_row)

    def stage_two(self):
        here, lead = self.here, self.lead
        self.arrived(1, self.first_one)
        for row in range(2):
            for far in range(lead):
                mine = self.chunk(row, far, here.side)
                add_into(mine, mine, self.first_one.at[row, far])
        for far in range(lead):
            self.send(3, self.chunk(1 - here.row, far, here.side), self.first_two.at[far], here.device, here.other_row)
        self.arrived(2, self.last_one)
        for far in range(lead, here.count):
            for side in range(2):
                mine = self.chunk(here.row, far, side)
                add_into(mine, mine, self.last_one.at[pl.ds(((far - lead) * 2 + side) * self.rows, self.rows)])
        for far in range(lead, here.count):
            self.send(
                4, self.chunk(here.row, far, 1 - here.side), self.last_two.at[far - lead], here.other_side, here.rank
            )

    def merge(self):
        here = self.here
        self.arrived(3, self.first_two)
        self.arrived(4, self.last_two)
        for far in range(here.count):
            land = self.first_two.at[far] if far < self.lead else self.last_two.at[far - self.lead]
            add_into(self.line.at[far], self.chunk(here.row, far, here.side), land)

    def finish(self):
        self.left(0, self.land_core)
        self.left(1, self.first_one)
        self.left(2, self.last_one)
        self.left(3, self.first_two)
        self.left(4, self.last_two)


class LineChain:
    def __init__(self, here, line, out, land, semaphores):
        self.here, self.line, self.out, self.land, self.semaphores = here, line, out, land, semaphores

    @staticmethod
    def scratch(far, rows, columns):
        return [pltpu.VMEM((far - 1, rows, columns), jnp.bfloat16), pltpu.SemaphoreType.DMA((2,))]

    def start(self):
        here = self.here
        for step in range(1, here.count):
            push(
                self.line.at[here.ahead(step)], self.land.at[step - 1], self.semaphores.at[0],
                self.semaphores.at[1], here.line(step), here.rank,
            )

    def finish(self):
        wait_bytes(self.land, self.semaphores.at[1])
        total = self.line[self.here.far].astype(jnp.float32)
        for step in range(1, self.here.count):
            total = total + self.land[step - 1].astype(jnp.float32)
        self.out[...] = total
        wait_bytes(self.land, self.semaphores.at[0])


def leave_kernel(mod_start, *refs):
    refs = list(refs)
    scattering = len(refs) > 10
    source, begun = (refs.pop(0), refs.pop(0)) if scattering else (None, None)
    small_ref, modulation_ref, *refs = refs
    out, begun_out = (refs.pop(0), refs.pop(0)) if scattering else (None, None)
    sum_ref, act_ref, land_ref, acting_ref, semaphores, *space = refs
    device, rank, dp, tp = place()
    me, count = device * tp + rank, dp * tp
    greet_all()
    if scattering:
        here = Where()
        line_ref, *space = space
        pick = lambda number: [space.pop(0) for _ in range(number)]
        chains, trails = [], []
        for index in range(PARTS):
            size = out.shape[1] // PARTS
            part = pl.ds(index * size, size)
            line = line_ref.at[index]
            chains.append(ScatterChain(here, source.at[:, :, part], line, here.count // 2, pick(7)))
            trails.append(LineChain(here, line, out.at[:, part], *pick(2)))
        others = [LineChain(here, begun.at[kind], begun_out.at[kind], *pick(2)) for kind in range(begun.shape[0])]
        for chain in chains:
            chain.stage_core()
    for step in range(1, tp):
        there = lax.rem(rank + step, tp)
        push(small_ref.at[there], land_ref.at[rank], semaphores.at[0], semaphores.at[1], device, there)
    land_ref[rank] = small_ref[rank]
    wait_bytes(land_ref.at[pl.ds(0, tp - 1)], semaphores.at[1])
    mine = sum_ref.at[rank]
    mine[device] = jnp.sum(land_ref[...], axis=0)

    def one(step, carry):
        push(mine.at[device], mine.at[device], semaphores.at[2], semaphores.at[3], lax.rem(device + step, dp), rank)
        return carry

    lax.fori_loop(1, dp, one, 0)
    if scattering:
        for chain in others:
            chain.start()
    wait_bytes(mine.at[pl.ds(0, dp - 1)], semaphores.at[3])
    for step in range(1, tp):
        push(mine, mine, semaphores.at[4], semaphores.at[5], device, lax.rem(rank + step, tp))
    if scattering:
        for chain in chains:
            chain.stage_one()
        chains[0].stage_two()
    wait_bytes(sum_ref.at[pl.ds(0, tp - 1)], semaphores.at[5])
    layers, padded, columns = modulation_ref.shape
    lines = sum_ref.shape[2]
    total = jnp.zeros((dp, padded), jnp.float32)
    for layer in range(layers):
        for index in range(columns // PAIR):
            line = layer * (tp * lines // layers) + mod_start // PAIR + index
            low = sum_ref[line // lines, :, line % lines, :].astype(jnp.bfloat16)
            total += mm(low, modulation_ref[layer, :, index * PAIR : (index + 1) * PAIR], ((1,), (1,)))
    acting_ref[...] = jnp.concatenate([total, jnp.zeros((dp, PAIR - padded), jnp.float32)], axis=1)
    act_ref[me] = acting_ref[...]

    def tell(index, carry):
        peer = lax.rem(me + index, count)
        push(acting_ref, act_ref.at[me], semaphores.at[6], semaphores.at[7], peer // tp, lax.rem(peer, tp))
        return carry

    lax.fori_loop(1, count, tell, 0)
    if scattering:
        for chain in chains[1:]:
            chain.stage_two()
        for chain, line in zip(chains, trails):
            chain.merge()
            line.start()
        for chain in others:
            chain.finish()
    wait_bytes(act_ref.at[pl.ds(0, count - 1)], semaphores.at[7])
    wait_bytes(act_ref.at[pl.ds(0, count - 1)], semaphores.at[6])
    wait_bytes(land_ref.at[pl.ds(0, tp - 1)], semaphores.at[0])
    wait_bytes(mine.at[pl.ds(0, dp - 1)], semaphores.at[2])
    wait_bytes(sum_ref.at[pl.ds(0, tp - 1)], semaphores.at[4])
    if scattering:
        for chain in chains + trails:
            chain.finish()


def leave(small, modulation, mod_start, grads, begun, collective_id):
    tp, lines, lanes = small.shape
    dp = lax.axis_size("dp")
    inside = pl.BlockSpec(memory_space=pltpu.VMEM)
    shapes, space, extra = [], [], []
    if grads is not None:
        _, width, columns = grads.shape
        rows, far, part = width // dp, dp // 2, columns // PARTS
        kinds = begun.shape[0]
        extra = [grads, begun]
        shapes = [
            jax.ShapeDtypeStruct((rows, columns), jnp.float32),
            jax.ShapeDtypeStruct((kinds, rows, columns), jnp.float32),
        ]
        space = [pltpu.VMEM((PARTS, far, rows, part), jnp.bfloat16)]
        for _ in range(PARTS):
            space += ScatterChain.scratch(width, part, dp, far // 2) + LineChain.scratch(far, rows, part)
        space += LineChain.scratch(far, rows, columns) * kinds
    return pl.pallas_call(
        partial(leave_kernel, mod_start),
        in_specs=[pl.BlockSpec(memory_space=pl.ANY), inside][: len(extra)] + [inside, inside],
        out_specs=[inside] * (len(shapes) + 2),
        out_shape=shapes + [
            jax.ShapeDtypeStruct((tp, dp, lines, lanes), jnp.float32),
            jax.ShapeDtypeStruct((dp * tp, dp, lanes), jnp.float32),
        ],
        scratch_shapes=[
            pltpu.VMEM((tp, lines, lanes), jnp.float32),
            pltpu.VMEM((dp, lanes), jnp.float32),
            pltpu.SemaphoreType.DMA((8,)),
        ] + space,
        compiler_params=pltpu.CompilerParams(
            collective_id=collective_id, has_side_effects=True, vmem_limit_bytes=VMEM_LIMIT
        ),
        name="leave",
    )(*extra, small, modulation)


class GatherChain:
    def __init__(self, here, source, out, semaphores, half=None):
        self.here, self.source, self.out, self.semaphores = here, source, out, semaphores
        self.rows = out.shape[1] // (2 * here.count)
        self.half = here.count // 2 if half is None else half

    @staticmethod
    def scratch():
        return [pltpu.SemaphoreType.DMA((9, 2))]

    def piece(self, rank, far, side):
        rows = pl.ds(pl.multiple_of((far * 2 + side) * self.rows, self.rows), self.rows)
        return self.out.at[rank, rows]

    def send(self, slot, source, target, device, rank):
        push(source, target, self.semaphores.at[slot, 0], self.semaphores.at[slot, 1], device, rank)

    def wait(self, slot, way, pieces):
        wait_bytes(self.out.at[0, pl.ds(0, pieces * self.rows)], self.semaphores.at[slot, way])

    def stage_line(self):
        here = self.here
        mine = self.piece(here.rank, here.far, here.side)
        pltpu.make_async_copy(self.source, mine, self.semaphores.at[8, 0]).start()
        for step in range(1, here.count):
            self.send(0, self.source, mine, here.line(step), here.rank)

    def line_arrived(self):
        self.wait(8, 0, 1)
        self.wait(0, 1, self.here.count - 1)

    def line_left(self):
        self.wait(0, 0, self.here.count - 1)

    def stage_near(self):
        here = self.here
        for turn in range(2):
            over_row = lax.rem(here.core + turn, 2) == 1
            device = jnp.where(over_row, here.device, here.other_side)
            rank = jnp.where(over_row, here.other_row, here.rank)
            for far in range(here.count):
                mine = self.piece(here.rank, far, here.side)
                self.send(1 + lax.rem(here.core + turn, 2), mine, mine, device, rank)
        for far in range(here.count):
            mine = self.piece(here.rank, far, here.side)
            self.send(3, mine, mine, here.device, here.other_core)

    def stage_across(self):
        here, count = self.here, self.here.count
        self.wait(1, 1, count)
        for far in range(self.half):
            other = self.piece(here.rank, far, 1 - here.side)
            self.send(4, other, other, here.device, here.other_row)
        self.wait(2, 1, count)
        for far in range(self.half, count):
            other = self.piece(here.other_row, far, here.side)
            self.send(5, other, other, here.other_side, here.rank)
        for far in range(count):
            for other in (self.piece(here.rank, far, 1 - here.side), self.piece(here.other_row, far, here.side)):
                self.send(6, other, other, here.device, here.other_core)

    def stage_core(self):
        here, count = self.here, self.here.count
        self.wait(4, 1, self.half)
        self.wait(5, 1, count - self.half)
        for far in range(count):
            other = self.piece(here.other_row, far, 1 - here.side)
            self.send(7, other, other, here.device, here.other_core)

    def finish(self):
        count, half = self.here.count, self.half
        self.wait(3, 1, count)
        self.wait(6, 1, 2 * count)
        self.wait(7, 1, count)
        for slot, pieces in ((1, count), (2, count), (3, count), (4, half), (5, count - half), (6, 2 * count), (7, count)):
            self.wait(slot, 0, pieces)


class Job:
    operands, sources, shapes, specs, aliases, space = (), None, (), (), {}, ()
    stages, last = {}, ()


def anywhere(count):
    return [pl.BlockSpec(memory_space=pl.ANY)] * count


class ScatterJob(Job):
    def __init__(self, grads, lead, close=False):
        _, _, width, columns = grads[0][0].shape
        dp = lax.axis_size("dp")
        far, rows = dp // 2, width // dp
        self.lead, self.close, self.kinds = lead, close, [kind for _, kind in grads]
        self.operands = [array for array, _ in grads]
        shape = (len(grads) - close, far, rows, columns)
        self.shapes, self.specs = [jax.ShapeDtypeStruct(shape, jnp.bfloat16)], [fixed(shape)]
        self.space = ScatterChain.scratch(width, columns, dp, lead) * len(grads)
        if close:
            self.shapes.append(jax.ShapeDtypeStruct((1, rows, columns), jnp.float32))
            self.specs.append(fixed((1, rows, columns)))
            self.space = [pltpu.VMEM((far, rows, columns), jnp.bfloat16)] + LineChain.scratch(
                far, rows, columns
            ) + self.space

    def bind(self, here, inputs, outputs, space):
        lines = [outputs[0].at[index] for index in range(outputs[0].shape[0])]
        if self.close:
            own, land, semaphores, *space = space
            lines.insert(0, own)
            line = LineChain(here, own, outputs[1].at[0], land, semaphores)
        size = len(space) // len(inputs)
        chains = [
            ScatterChain(
                here, source.at[kind], lines[index], self.lead, space[index * size : (index + 1) * size]
            )
            for index, (source, kind) in enumerate(zip(inputs, self.kinds))
        ]
        one = chains[0]
        if len(chains) == 1:
            self.stages = {(0, 0): [one.stage_core], (0, 3): [one.stage_one], (2, 1): [one.stage_two]}
            self.last = [one.merge, one.finish]
            return
        two = chains[1]
        if self.close:
            self.stages = {
                (0, 0): [one.stage_core, two.stage_core], (0, 2): [one.stage_one], (2, 0): [one.stage_two, two.stage_one],
                (2, 3): [one.merge, line.start],
            }
            self.last = [two.stage_two, line.finish, two.merge, one.finish, two.finish]
            return
        self.stages = {
            (0, 0): [one.stage_core, two.stage_core], (0, 2): [one.stage_one], (0, 3): [two.stage_one],
            (2, 1): [one.stage_two], (3, 1): [two.stage_two],
        }
        self.last = [one.merge, two.merge, one.finish, two.finish]


class LineJob(Job):
    def __init__(self, line):
        kinds, far, rows, columns = line.shape
        shape = (kinds, rows, columns)
        self.operands, self.sources = [line], [fixed(line.shape)]
        self.shapes, self.specs = [jax.ShapeDtypeStruct(shape, jnp.float32)], [fixed(shape)]
        self.space = LineChain.scratch(far, rows, columns) * kinds

    def bind(self, here, inputs, outputs, space):
        chains = [
            LineChain(here, inputs[0].at[kind], outputs[0].at[kind], *space[2 * kind : 2 * kind + 2])
            for kind in range(outputs[0].shape[0])
        ]
        self.stages = {(0, 0): [chain.start for chain in chains]}
        self.last = [chain.finish for chain in chains]


class FlowJob(Job):
    def __init__(self, spread, lines, half=None, late=()):
        dp, tp = lax.axis_size("dp"), lax.axis_size("tensor")
        self.counts, self.half = (len(spread), len(late)), half
        shards = list(late) + list(lines)
        self.operands = list(spread) + shards
        self.shapes = [jax.ShapeDtypeStruct(v.shape, v.dtype) for v in spread]
        self.shapes += [jax.ShapeDtypeStruct((tp, dp * v.shape[0], v.shape[1]), v.dtype) for v in shards]
        self.specs = anywhere(len(self.shapes))
        self.aliases = {index: index for index in range(len(spread))}
        self.space = GatherChain.scratch() * len(self.shapes)

    def bind(self, here, inputs, outputs, space):
        chains = [GatherChain(here, *refs, self.half) for refs in zip(inputs, outputs, space)]
        first, late = self.counts
        spread, late, lines = chains[:first], chains[first : first + late], chains[first + late :]
        self.stages = {
            (0, 0): [chain.stage_near for chain in spread] + [chain.stage_line for chain in late + lines],
            (3, 0): [chain.stage_across for chain in spread],
        }
        for chain in late:
            self.stages[3, 0] += [chain.line_arrived, chain.stage_near]
        self.last = [chain.stage_across for chain in late]
        self.last += [chain.stage_core for chain in spread + late]
        self.last += [chain.finish for chain in spread + late]
        self.last += [chain.line_arrived for chain in lines]
        self.last += [chain.line_left for chain in late + lines]


class SwapJob(Job):
    def __init__(self, blocks):
        self.operands = [blocks]
        self.shapes, self.specs = [jax.ShapeDtypeStruct(blocks.shape, blocks.dtype)], anywhere(1)
        self.space = [pltpu.SemaphoreType.DMA((3,))]

    def bind(self, here, inputs, outputs, space):
        source, out, semaphores = inputs[0], outputs[0], space[0]
        ranks = out.shape[0]

        def start():
            pltpu.make_async_copy(source.at[here.rank], out.at[here.rank], semaphores.at[2]).start()
            for step in range(1, ranks):
                there = lax.rem(here.rank + step, ranks)
                push(source.at[there], out.at[here.rank], semaphores.at[0], semaphores.at[1], here.device, there)

        def finish():
            wait_bytes(out.at[0], semaphores.at[2])
            wait_bytes(out.at[pl.ds(0, ranks - 1)], semaphores.at[1])
            wait_bytes(out.at[pl.ds(0, ranks - 1)], semaphores.at[0])

        self.stages, self.last = {(0, 0): [start]}, [finish]


class StreamJob(Job):
    def __init__(self, shape, frames):
        self.shape, self.frames = shape, frames
        self.shapes, self.specs = [jax.ShapeDtypeStruct(shape, jnp.bfloat16)], anywhere(1)
        ranks, groups, rows, width = shape
        block = (groups, ranks, rows, width)
        if frames:
            block = (frames, ranks, groups, rows // frames, width)
        self.space = [pltpu.VMEM(block, jnp.bfloat16), pltpu.SemaphoreType.DMA((3,))]

    def bind(self, here, inputs, outputs, space):
        self.here, self.out = here, outputs[0]
        self.buffer, self.semaphores = space
        ranks = self.shape[0]

        def finish():
            wait_bytes(self.out.at[0], self.semaphores.at[2])
            wait_bytes(self.out.at[pl.ds(0, ranks - 1)], self.semaphores.at[1])
            wait_bytes(self.out.at[pl.ds(0, ranks - 1)], self.semaphores.at[0])

        self.stages, self.last = {}, [finish]

    def put(self, step, value):
        here, ranks = self.here, self.shape[0]
        size = self.buffer.size // self.buffer.shape[0] // value.shape[1]
        if value.shape[0] > size:
            count = value.shape[0] // size
            for index in range(count):
                self.put(step * count + index, value[index * size : (index + 1) * size])
            return
        self.buffer[step] = value.reshape(self.buffer.shape[1:]).astype(jnp.bfloat16)
        if self.frames:
            strip = self.buffer.shape[3]
            target = self.out.at[here.rank, :, pl.ds(pl.multiple_of(step * strip, strip), strip)]
        else:
            target = self.out.at[here.rank, step]
        pltpu.make_async_copy(self.buffer.at[step, here.rank], target, self.semaphores.at[2]).start()
        for ahead in range(1, ranks):
            there = lax.rem(here.rank + ahead, ranks)
            push(
                self.buffer.at[step, there], target, self.semaphores.at[0], self.semaphores.at[1],
                here.device, there,
            )


def greet_jobs(here):
    barrier = pltpu.get_barrier_semaphore()
    ranks = lax.axis_size("tensor")
    peers = [(here.other_side, here.rank)]
    peers += [(here.line(step), here.rank) for step in range(1, here.count)]
    peers += [(here.device, lax.rem(here.rank + step, ranks)) for step in range(1, ranks)]
    for peer in peers:
        pl.semaphore_signal(barrier, inc=1, device_id=peer, device_id_type=pl.DeviceIdType.MESH)
    pl.semaphore_wait(barrier, len(peers))


def call(body, steps, arguments, in_specs, out_shape, out_specs, scratch, jobs, collective_id, estimate, name):
    operands = [v for job in jobs for v in job.operands]
    sources = [v for job in jobs for v in (job.sources or anywhere(len(job.operands)))]
    shapes = [v for job in jobs for v in job.shapes]
    specs = [v for job in jobs for v in job.specs]
    space = [v for job in jobs for v in job.space]
    aliases, before, after = {}, len(arguments), len(out_shape)
    for job in jobs:
        for source, target in job.aliases.items():
            aliases[before + source] = after + target
        before, after = before + len(job.operands), after + len(job.shapes)

    def kernel(*refs):
        refs = list(refs)
        take = lambda number: [refs.pop(0) for _ in range(number)]
        inputs, job_inputs = take(len(arguments)), take(len(operands))
        outputs, job_outputs = take(len(out_shape)), take(len(shapes))
        own, job_space = take(len(scratch)), refs
        step = pl.program_id(0)
        if jobs:
            here = Where()
            for job in jobs:
                pick = lambda pool, number: [pool.pop(0) for _ in range(number)]
                job.bind(
                    here, pick(job_inputs, len(job.operands)), pick(job_outputs, len(job.shapes)),
                    pick(job_space, len(job.space)),
                )

        def hook(spot):
            for index in range(steps):
                todo = [
                    stage
                    for job in jobs
                    for (late, place), stages in sorted(job.stages.items())
                    if (late * 4 + place) * steps // 4 == index * 4 + spot
                    for stage in stages
                ]
                if todo or (jobs and spot == 0 and index == 0):

                    @pl.when(step == index)
                    def _():
                        if index == 0 and spot == 0:
                            greet_jobs(here)
                        for stage in todo:
                            stage()

        hook(0)
        body(lambda spot: hook(spot) if spot else None, *inputs, *outputs, *own)
        if jobs:

            @pl.when(step == steps - 1)
            def _():
                for job in jobs:
                    for stage in job.last:
                        stage()

    more = {"collective_id": collective_id, "has_side_effects": True} if jobs else {}
    return pl.pallas_call(
        kernel,
        grid=(steps,),
        in_specs=list(in_specs) + sources,
        out_specs=list(out_specs) + specs,
        out_shape=list(out_shape) + shapes,
        scratch_shapes=list(scratch) + space,
        input_output_aliases=aliases,
        compiler_params=pltpu.CompilerParams(
            vmem_limit_bytes=VMEM_LIMIT, dimension_semantics=("arbitrary",), **more
        ),
        cost_estimate=estimate,
        name=name,
    )(*arguments, *operands)


def entry_kernel(
    per_device, row_ref, modulation_ref, *refs
):
    gather = 2 if len(refs) > 5 else 0
    refs = list(refs)
    sources = [refs.pop(0) for _ in range(gather)]
    gathered_ref, mod_ref = refs.pop(0), refs.pop(0)
    targets = [refs.pop(0) for _ in range(gather)]
    part_ref, land_ref, semaphores, *space = refs
    device, rank, dp, tp = place()
    me, count = device * tp + rank, dp * tp
    quarter = land_ref.shape[2]
    if gather:
        here = Where()
        size = sources[0].shape[1] // PARTS
        parts = []
        for index in range(PARTS):
            part = pl.ds(index * size, size)
            parts.append(GatherChain(here, sources[0].at[:, part], targets[0].at[:, :, part], space.pop(0)))
        following = GatherChain(here, sources[1], targets[1], space[0])
    greet_all()

    def tell(index, carry):
        peer = lax.rem(me + index, count)
        push(
            row_ref, gathered_ref.at[me], semaphores.at[0], semaphores.at[1], peer // tp, lax.rem(peer, tp)
        )
        return carry

    lax.fori_loop(1, count, tell, 0)
    gathered_ref[me] = row_ref[...]
    if gather:
        for chain in parts:
            chain.stage_line()
    wait_bytes(gathered_ref.at[pl.ds(0, count - 1)], semaphores.at[1])
    padded = modulation_ref.shape[1]
    width = dp * tp * per_device
    chosen = jnp.zeros((count, padded), jnp.float32)
    row = lax.broadcasted_iota(jnp.int32, (PAIR, padded), 0)
    column = lax.broadcasted_iota(jnp.int32, (PAIR, padded), 1)
    for index in range(width // PAIR):
        match = (row + index * PAIR == column + me * per_device) & (column < per_device)
        chosen += mm(
            gathered_ref[:, index, :].astype(jnp.bfloat16), jnp.where(match, 1.0, 0.0).astype(jnp.bfloat16)
        )
    clip = lax.broadcasted_iota(jnp.int32, (dp, count), 0)
    member = lax.broadcasted_iota(jnp.int32, (dp, count), 1)
    leaders = jnp.where(member == clip * tp, 1.0, 0.0).astype(jnp.bfloat16)
    rows = mm(leaders, chosen.astype(jnp.bfloat16)).astype(jnp.bfloat16)
    for layer in range(modulation_ref.shape[0]):
        part = mm(rows, modulation_ref[layer])
        size = part.shape[1]
        for index in range(dp):
            part_ref[index, :, layer * size : (layer + 1) * size] = part[index : index + 1]

    def share(index, carry):
        peer = lax.rem(me + index, count)
        there, lane = peer // tp, lax.rem(peer, tp)
        source = part_ref.at[there, :, pl.ds(pl.multiple_of(lane * quarter, PAIR), quarter)]
        push(source, land_ref.at[me], semaphores.at[2], semaphores.at[3], there, lane)
        return carry

    lax.fori_loop(1, count, share, 0)
    mine = pl.ds(pl.multiple_of(rank * quarter, PAIR), quarter)
    land_ref[me] = part_ref[device, :, mine]
    if gather:
        for chain in parts:
            chain.line_arrived()
            chain.stage_near()
        following.stage_line()
    wait_bytes(land_ref.at[pl.ds(0, count - 1)], semaphores.at[3])
    mod_ref[:, mine] = jnp.sum(land_ref[...], axis=0)
    for step in range(1, tp):
        push(
            mod_ref.at[:, mine], mod_ref.at[:, mine], semaphores.at[4], semaphores.at[5],
            device, lax.rem(rank + step, tp),
        )
    if gather:
        for chain in parts:
            chain.stage_across()
        for chain in parts:
            chain.stage_core()
    wait_bytes(gathered_ref.at[pl.ds(0, count - 1)], semaphores.at[0])
    wait_bytes(land_ref.at[pl.ds(0, count - 1)], semaphores.at[2])
    wait_bytes(mod_ref.at[:, pl.ds(0, (tp - 1) * quarter)], semaphores.at[5])
    wait_bytes(mod_ref.at[:, pl.ds(0, (tp - 1) * quarter)], semaphores.at[4])
    if gather:
        following.line_arrived()
        for chain in parts:
            chain.finish()
        for chain in (*parts, following):
            chain.line_left()


def enter(row, modulation, per_device, weights, collective_id):
    dp, tp = lax.axis_size("dp"), lax.axis_size("tensor")
    count = dp * tp
    whole = modulation.shape[0] * modulation.shape[2]
    inside = pl.BlockSpec(memory_space=pltpu.VMEM)
    job = FlowJob((), weights) if weights else Job()
    return pl.pallas_call(
        partial(entry_kernel, per_device),
        in_specs=[inside, inside] + anywhere(len(job.operands)),
        out_specs=[inside, inside] + list(job.specs),
        out_shape=[
            jax.ShapeDtypeStruct((count,) + row.shape, jnp.float32),
            jax.ShapeDtypeStruct((1, whole), jnp.float32),
        ] + list(job.shapes),
        scratch_shapes=[
            pltpu.VMEM((dp, 1, whole), jnp.float32),
            pltpu.VMEM((count, 1, whole // tp), jnp.float32),
            pltpu.SemaphoreType.DMA((6,)),
        ] + (GatherChain.scratch() * (PARTS + 1) if weights else []),
        compiler_params=pltpu.CompilerParams(
            collective_id=collective_id, has_side_effects=True, vmem_limit_bytes=VMEM_LIMIT
        ),
        name="enter",
    )(row, modulation, *job.operands)


def adam_update(weight, first, second, grad, rate, decay):
    first_new = BETA_ONE * first + (1.0 - BETA_ONE) * grad
    second_new = BETA_TWO * second + (1.0 - BETA_TWO) * grad * grad
    corrected = (
        first_new
        / (1.0 - BETA_ONE**STEP)
        / (jnp.sqrt(second_new / (1.0 - BETA_TWO**STEP)) + ADAM_EPS)
    )
    weight_new = weight - rate * (corrected + decay * weight)
    return (weight_new, first_new, second_new, weight_new.astype(jnp.bfloat16))


def dot32(form, left, right):
    return jnp.einsum(form, left, right, preferred_element_type=jnp.float32)


def exchange(blocks):
    return lax.all_to_all(blocks, "tensor", split_axis=0, concat_axis=0, tiled=True)


def gather_plain(shard):
    rows, width = shard.shape
    whole = lax.all_gather(shard, ("tensor", "dp"), axis=0, tiled=True)
    return whole.reshape(-1, lax.axis_size("dp") * rows, width)


def scatter_plain(grads):
    kinds, ranks, width, cols = grads.shape
    flat = grads.reshape(kinds, ranks * width, cols)
    summed = lax.psum_scatter(flat, ("tensor", "dp"), scatter_dimension=1, tiled=True)
    return summed.astype(jnp.float32)


def per_device(
    clips, cotangent, timesteps, labels, time_table, class_table,
    attention_weights, attention_first, attention_second,
    ffn_weights, ffn_first, ffn_second,
    modulation_weights, modulation_first, modulation_second,
    bias_vectors, bias_first, bias_second,
):
    layers, kinds, rows, cols = attention_weights.shape
    _, frames, patches, width = clips.shape
    mod_rows = modulation_weights.shape[1]
    bias_cols = bias_vectors.shape[1]
    dp, tp = lax.axis_size("dp"), lax.axis_size("tensor")
    position = lax.axis_index("dp") * tp + lax.axis_index("tensor")
    tokens = frames * patches
    strip = patches // (tp * frames)
    blocks = (tp, frames, frames * strip, width)
    pieces = (tp * frames, frames, strip, width)

    embed = time_table[timesteps] + class_table[labels]
    cond_act = jax.nn.silu(embed).astype(jnp.bfloat16)
    fused = rows % 16 == 0
    shards = [
        (
            pack_heads(attention_weights[layer].astype(jnp.bfloat16)),
            ffn_weights[layer, 0].astype(jnp.bfloat16),
            ffn_weights[layer, 1].astype(jnp.bfloat16),
        )
        for layer in range(layers)
    ]
    low = bias_vectors.astype(jnp.bfloat16).reshape(-1)
    row = jnp.concatenate([cond_act[0], low]).astype(jnp.float32)
    row = jnp.pad(row, (0, -row.shape[0] % 1024)).reshape(-1, 128)
    modulation_low = modulation_weights.astype(jnp.bfloat16)
    modulation_low = jnp.pad(modulation_low, ((0, 0), (0, -mod_rows % 32), (0, 0)))
    gathered, mod, *begun = enter(row, modulation_low, mod_rows, shards[0][:2] if fused else None, 0)
    gathered = gathered.reshape(dp * tp, -1)
    cond_all = gathered[::tp, :width].astype(jnp.bfloat16)
    bias_low = gathered[:, width : width + layers * bias_cols].reshape(dp * tp, layers, bias_cols)
    bias_low = bias_low.transpose(1, 0, 2).reshape(layers, -1)
    cond_rows = lax.dynamic_slice_in_dim(cond_all, position * mod_rows, mod_rows, axis=1)
    cond_rows = jnp.pad(cond_rows, ((0, 0), (0, -mod_rows % 32)))
    mod = mod.reshape(layers, -1)
    mod_width = mod.shape[-1]
    mod = (mod + bias_low[:, -mod_width:]).reshape(layers, 6, width)
    hidden_width = bias_low.shape[1] - mod_width - 4 * width
    bias_up = bias_low[:, 3 * width : 3 * width + hidden_width].reshape(layers, tp, 1, -1)
    bias_out = bias_low[:, None, 2 * width : 3 * width]
    bias_down = bias_low[:, None, 3 * width + hidden_width : 4 * width + hidden_width]
    bias_project = [
        pack_bias(bias_low[layer, :width], bias_low[layer, width : 2 * width], tp) for layer in range(layers)
    ]

    by_patch = lambda v: v.reshape(frames, tp * frames, strip, width).transpose(1, 0, 2, 3)
    cot = by_patch(cotangent[0]).reshape(blocks)
    first = clips[0].reshape(1, frames, patches, width)

    attend = lambda layer, weight, stream, stride, *more: attention_forward(
        weight, stream, mod[layer], bias_project[layer], bias_out[layer], stride, *more
    )
    expand = lambda layer, up, down, middle, *more: ffn_forward(
        up, down, middle.reshape(tokens, width), mod[layer], bias_down[layer], bias_up[layer], *more
    )
    if fused:
        attention_a, up_a = begun
        *heads_a, middle_a, up_a, down_a, attention_b = attend(
            0, attention_a, first, 0, [FlowJob([up_a], [shards[1][0]], None, [shards[0][2]])], 1
        )
        hidden_a, pushed_a, second, attention_b, up_b, down_b = expand(
            0, up_a, down_a, middle_a, StreamJob(blocks, frames),
            [FlowJob([attention_b], [shards[1][2]], dp // 8, [shards[1][1]])], 2,
        )
        *heads_b, middle_b, down_b = attend(1, attention_b, second, strip, [FlowJob([down_b], [])], 3)
        hidden_b, pushed_b, result, cot = expand(1, up_b, down_b, middle_b, None, [SwapJob(cot)], 4)
    else:
        (attention_a, up_a, down_a), (attention_b, up_b, down_b) = [[gather_plain(v) for v in group] for group in shards]
        *heads_a, middle_a = attend(0, attention_a, first, 0)
        hidden_a, pushed_a, second = expand(0, up_a, down_a, middle_a)
        second = exchange(by_patch(second).reshape(blocks))
        *heads_b, middle_b = attend(1, attention_b, second, strip)
        hidden_b, pushed_b, result = expand(1, up_b, down_b, middle_b)
        cot = exchange(cot)
    middle_a, middle_b = middle_a.reshape(tokens, width), middle_b.reshape(tokens, width)
    result = result.reshape(blocks)
    cot = cot.reshape(tokens, width)

    if fused:
        grad, ffn_grad, *sums_b, result = ffn_backward(
            up_b, down_b, cot, middle_b, pushed_b, hidden_b, mod[1], [SwapJob(result)], 5
        )
        packed_b, *more_b, grad, line_up = attention_backward(
            attention_b, grad.reshape(blocks), second, heads_b, mod[1], strip,
            StreamJob(blocks, 0), [ScatterJob([(ffn_grad, 0)], 3 * dp // 8)], 6,
        )
        waiting = [(ffn_grad, 1), (packed_b[None], 0)]
        grad, ffn_grad, *sums_a, done_up, line_b = ffn_backward(
            up_a, down_a, grad.reshape(pieces), middle_a, pushed_a, hidden_a, mod[0],
            [LineJob(line_up), ScatterJob(waiting, dp // 4)], 7,
        )
        grad, packed_a, *more_a, done_b, line_ffn_a, done_up_a = attention_backward(
            attention_a, grad.reshape(first.shape), first, heads_a, mod[0], 0, None,
            [LineJob(line_b), ScatterJob([(ffn_grad, 0), (ffn_grad, 1)], dp // 4, True)], 8,
        )
        done_ffn_b, done_b = jnp.concatenate([done_up, done_b[:1]]), done_b[1:]
    else:
        result = exchange(result)
        grad, ffn_grad, *sums_b = ffn_backward(up_b, down_b, cot, middle_b, pushed_b, hidden_b, mod[1])
        done_ffn_b = scatter_plain(ffn_grad)
        grad, packed_b, *more_b = attention_backward(
            attention_b, grad.reshape(blocks), second, heads_b, mod[1], strip
        )
        done_b = scatter_plain(packed_b[None])
        grad = exchange(grad.astype(jnp.bfloat16))
        grad, ffn_grad, *sums_a = ffn_backward(up_a, down_a, grad.reshape(pieces), middle_a, pushed_a, hidden_a, mod[0])
        done_ffn_a = scatter_plain(ffn_grad)
        grad, packed_a, *more_a = attention_backward(attention_a, grad.reshape(first.shape), first, heads_a, mod[0], 0)
        done_a = scatter_plain(packed_a[None])
    output = result.reshape(pieces).transpose(1, 0, 2, 3).reshape(clips.shape)
    input_grad = grad.reshape(clips.shape)

    def gather_small(more, sums):
        attention_sums, project_sum = more
        up_sum, low_sums = sums
        return jnp.concatenate(
            [*unpack_bias(project_sum), attention_sums[0], up_sum.reshape(-1), low_sums[0],
             attention_sums[1:].reshape(-1), low_sums[1:].reshape(-1)]
        )

    small = jnp.stack([gather_small(more_a, sums_a), gather_small(more_b, sums_b)])
    token_width = small.shape[1] - mod_width
    *done, small, grad_act = leave(
        small.reshape(tp, -1, 128), modulation_low, token_width,
        *((packed_a, line_ffn_a) if fused else (None, None)), 9,
    )
    if fused:
        done_a, done_ffn_a = done[0][None], jnp.concatenate([done_up_a, done[1]])
    small = small.transpose(1, 0, 2, 3).reshape(dp, layers, -1)
    grad_mod_low = small[..., token_width:].astype(jnp.bfloat16)
    grad_bias_all = jnp.concatenate(
        [small[..., :token_width], grad_mod_low.astype(jnp.float32)], axis=-1
    ).sum(axis=0)
    grad_bias = lax.dynamic_slice_in_dim(grad_bias_all, position * bias_cols, bias_cols, axis=1)
    grad_mod_weight = dot32("ck,cle->lke", cond_rows, grad_mod_low)[:, :mod_rows]
    grad_act = lax.dynamic_index_in_dim(
        grad_act[:, :, :mod_rows], lax.axis_index("dp"), axis=1, keepdims=False
    )
    grad_attention = jnp.stack([unpack_heads(done_a[0]), unpack_heads(done_b[0])])
    grad_ffn = jnp.stack([done_ffn_a, done_ffn_b])
    silu_value, silu_pull = jax.vjp(jax.nn.silu, embed)
    cond_grad = silu_pull(grad_act.reshape(1, width))[0]

    return (output, input_grad, cond_grad) + (
        adam_update(attention_weights, attention_first, attention_second, grad_attention, MATRIX_RATE, MATRIX_DECAY)
        + adam_update(ffn_weights, ffn_first, ffn_second, grad_ffn, MATRIX_RATE, MATRIX_DECAY)
        + adam_update(modulation_weights, modulation_first, modulation_second, grad_mod_weight, MATRIX_RATE, MATRIX_DECAY)
        + adam_update(bias_vectors, bias_first, bias_second, grad_bias, VECTOR_RATE, 0.0)
    )


def solution(mesh):
    tokens = P("dp", "tensor", None, None)
    matrix = P(None, None, "dp", "tensor")
    modulation = P(None, BOTH, None)
    vector = P(None, BOTH)
    return jax.shard_map(
        per_device,
        mesh=mesh,
        in_specs=(tokens, tokens, P("dp"), P("dp"), P(), P())
        + (matrix,) * 6 + (modulation,) * 3 + (vector,) * 3,
        out_specs=(tokens, tokens, P("dp", None)) + (matrix,) * 8 + (modulation,) * 4 + (vector,) * 4,
        check_vma=False,
    )
```

```python
from functools import partial

import jax
import jax.numpy as jnp
from jax import lax
from jax.experimental import pallas as pl
from jax.experimental.pallas import tpu as pltpu
from jax.sharding import PartitionSpec as P

HD = 64
PAIR = 128
PARTS = 3
STEP = 10
BETA_ONE = 0.9
BETA_TWO = 0.999
ADAM_EPS = 1e-08
MATRIX_RATE = 0.04
VECTOR_RATE = 0.2
MATRIX_DECAY = 0.1
NORM_EPS = 1e-06
GELU_A = (2.0 / 3.141592653589793) ** 0.5
GELU_B = 0.044715
BLOCKED = -1e30
VMEM_LIMIT = 60 * 1024 * 1024
BOTH = ("dp", "tensor")


def mm(left, right, dims=((1,), (0,))):
    return lax.dot_general(left, right, (dims, ((), ())), preferred_element_type=jnp.float32)


def norm_parts(value):
    average = jnp.mean(value, axis=-1, keepdims=True)
    centred = value - average
    spread = jnp.mean(centred * centred, axis=-1, keepdims=True)
    inverse = lax.rsqrt(spread + NORM_EPS)
    return centred * inverse, inverse


def norm_back(grad, shape, inverse):
    first = jnp.mean(grad, axis=-1, keepdims=True)
    second = jnp.mean(grad * shape, axis=-1, keepdims=True)
    return inverse * (grad - first - shape * second)


def rows_of(ref):
    value = ref[...]
    return value.reshape(-1, value.shape[-1])


def put(ref, value):
    ref[...] = value.reshape(ref.shape).astype(ref.dtype)


def add_rows(ref, index, value):
    ref[pl.ds(index, 1), :] += jnp.sum(value, axis=0, keepdims=True)


def half_masks(rows):
    lane = lax.broadcasted_iota(jnp.int32, (rows, PAIR), 1)
    return lane < HD


def same_patch(tokens, stride):
    row = lax.broadcasted_iota(jnp.int32, (tokens, tokens), 0)
    column = lax.broadcasted_iota(jnp.int32, (tokens, tokens), 1)
    return lax.rem(row, stride) == lax.rem(column, stride)


def swap_halves(value):
    return pltpu.roll(value, HD, 1)


def start_loads(source, target, semaphores):
    for rank in range(target.shape[0]):
        pltpu.make_async_copy(source.at[rank], target.at[rank], semaphores.at[rank]).start()


def wait_loads(target, semaphores, rank):
    pltpu.make_async_copy(target.at[rank], target.at[rank], semaphores.at[rank]).wait()


def softmax_rows(scores, axis):
    raised = jnp.exp(scores - jnp.max(scores, axis=axis, keepdims=True))
    return raised * (1.0 / jnp.sum(raised, axis=axis, keepdims=True))


def attention_forward_kernel(
    stride, hook, source, stream_ref, mod_ref, bias_ref, bias_out_ref,
    project_ref, mixed_ref, branch_ref, middle_ref, weight_ref, semaphores,
):
    ranks = weight_ref.shape[0]

    @pl.when(pl.program_id(0) == 0)
    def _():
        start_loads(source, weight_ref, semaphores)

    stream = rows_of(stream_ref).astype(jnp.float32)
    tokens, width = stream.shape
    shape, _ = norm_parts(stream)
    normed = (shape * (1.0 + mod_ref[1:2]) + mod_ref[0:1]).astype(jnp.bfloat16)
    lower = half_masks(tokens)
    allowed = same_patch(tokens, stride) if stride else None

    @pl.when(pl.program_id(0) == 0)
    def _():
        for rank in range(ranks):
            wait_loads(weight_ref, semaphores, rank)

    def mix(heads):
        scores = [mm(chosen.astype(jnp.bfloat16), key, ((1,), (1,))) for chosen, key, _ in heads]
        outs = []
        for score, (_, _, value) in zip(scores, heads):
            if stride:
                score = jnp.where(allowed, score, BLOCKED)
            outs.append(mm(softmax_rows(score, -1).astype(jnp.bfloat16), value))
        return outs

    branch = None
    for rank in range(ranks):
        hook(rank)
        project = (mm(normed, weight_ref[rank, :, : 5 * PAIR]) + bias_ref[rank]).astype(jnp.bfloat16)
        project_ref[rank] = project.reshape(project_ref.shape[1:])
        query = project[:, :PAIR].astype(jnp.float32) * HD**-0.5
        key, value = project[:, PAIR : 2 * PAIR], project[:, 2 * PAIR : 3 * PAIR]
        both = project[:, 3 * PAIR : 4 * PAIR].astype(jnp.float32)
        first, second, last = mix(
            [
                (jnp.where(lower, query, 0.0), key, value),
                (jnp.where(lower, 0.0, query), key, value),
                (
                    jnp.where(lower, both * HD**-0.5, 0.0),
                    swap_halves(both).astype(jnp.bfloat16),
                    project[:, 4 * PAIR : 5 * PAIR],
                ),
            ]
        )
        mixed = jnp.concatenate(
            [jnp.where(lower, 0.0, swap_halves(last)), jnp.where(lower, first, second)], axis=1
        ).astype(jnp.bfloat16)
        mixed_ref[rank] = mixed.reshape(mixed_ref.shape[1:])
        term = mm(mixed, weight_ref[rank, :, 4 * PAIR :], ((1,), (1,)))
        branch = term if branch is None else branch + term
    branch = branch + bias_out_ref[...]
    put(branch_ref, branch)
    put(middle_ref, stream + mod_ref[2:3] * branch)


def gelu_parts(value):
    square = value * value
    bent = jnp.tanh(value * (GELU_A + (GELU_A * GELU_B) * square))
    half = 0.5 * (1.0 + bent)
    slope = half + (0.5 * value) * (1.0 - bent * bent) * (GELU_A + (3.0 * GELU_A * GELU_B) * square)
    return value * half, slope


def ffn_forward_kernel(
    stream, hook, up_source, down_source, middle_ref, mod_ref, bias_ref, bias_up_ref, hidden_ref, branch_ref, *rest
):
    if stream is None:
        result_ref, *rest = rest
    up_ref, down_ref, up_semaphores, down_semaphores = rest
    step = pl.program_id(0)
    ranks = up_ref.shape[0]

    @pl.when(step == 0)
    def _():
        start_loads(up_source, up_ref, up_semaphores)
        start_loads(down_source, down_ref, down_semaphores)

    middle = middle_ref[...]
    shape, _ = norm_parts(middle)
    second = (shape * (1.0 + mod_ref[4:5]) + mod_ref[3:4]).astype(jnp.bfloat16)

    @pl.when(step == 0)
    def _():
        for rank in range(ranks):
            wait_loads(up_ref, up_semaphores, rank)
            wait_loads(down_ref, down_semaphores, rank)

    down = None
    for rank in range(ranks):
        hook(rank)
        hidden = mm(second, up_ref[rank]) + bias_up_ref[rank]
        hidden_ref[rank] = hidden.astype(jnp.bfloat16)
        active, _ = gelu_parts(hidden)
        part = mm(active.astype(jnp.bfloat16), down_ref[rank], ((1,), (1,)))
        down = part if down is None else down + part
    down = down + bias_ref[...]
    branch_ref[...] = down.astype(jnp.bfloat16)
    result = middle + mod_ref[5:6] * down
    if stream is None:
        result_ref[...] = result.astype(result_ref.dtype)
    else:
        stream.put(step, result)


def load_rows(ref, index, chunk):
    if len(ref.shape) == 2:
        return ref[index * chunk : (index + 1) * chunk, :].astype(jnp.float32)
    blocks, _, strip, width = ref.shape
    frames = chunk // (blocks * strip)
    parts = [ref[:, index * frames + frame].reshape(blocks * strip, width) for frame in range(frames)]
    return jnp.concatenate(parts, axis=0).astype(jnp.float32)


def ffn_backward_kernel(
    split, cores, hook, up_source, down_source, grad_ref, middle_ref, branch_ref, hidden_ref, mod_ref,
    grad_middle_ref, up_sum_ref, sums_ref, *refs
):
    if cores is None:
        weight_grad_ref, *refs = refs
    (up_ref, down_ref, up_semaphores, down_semaphores,
     second_ref, low_ref, low_across_ref, active_ref, slope_ref, total_ref) = refs
    step = pl.program_id(0)
    tokens, width = middle_ref.shape
    chunk = tokens // split

    @pl.when(step == 0)
    def _():
        start_loads(up_source, up_ref, up_semaphores)
        start_loads(down_source, down_ref, down_semaphores)
        sums_ref[...] = jnp.zeros_like(sums_ref)
        for index in range(split):
            rows = slice(index * chunk, (index + 1) * chunk)
            grad = load_rows(grad_ref, index, chunk)
            low = (mod_ref[5:6] * grad).astype(jnp.bfloat16)
            low_ref[rows, :] = low
            low_across_ref[:, rows] = low.T
            add_rows(sums_ref, 0, low.astype(jnp.float32))
            add_rows(sums_ref, 3, grad * branch_ref[rows, :].astype(jnp.float32))
            shape, _ = norm_parts(middle_ref[rows, :])
            second = (shape * (1.0 + mod_ref[4:5]) + mod_ref[3:4]).astype(jnp.bfloat16)
            second_ref[:, rows] = second.T

    up_sum_ref[...] = jnp.zeros_like(up_sum_ref)
    wait_loads(up_ref, up_semaphores, step)
    wait_loads(down_ref, down_semaphores, step)

    for index in range(split):
        hook(index)
        rows = slice(index * chunk, (index + 1) * chunk)
        active, slope = gelu_parts(hidden_ref[0, rows, :].astype(jnp.float32))
        active_ref[rows, :] = active.astype(jnp.bfloat16)
        low = (mm(low_ref[rows, :], down_ref[step]) * slope).astype(jnp.bfloat16)
        slope_ref[rows, :] = low
        up_sum_ref[0] += jnp.sum(low.astype(jnp.float32), axis=0, keepdims=True)
        part = mm(low, up_ref[step], ((1,), (1,)))
        total_ref[rows, :] = jnp.where(step == 0, 0.0, total_ref[rows, :]) + part

    hook(2)
    made = weight_grad_ref.at[:, 0] if cores is None else cores.slot(step)
    made[0] = mm(second_ref[...], slope_ref[...]).astype(jnp.bfloat16)
    hook(3)
    made[1] = mm(low_across_ref[...], active_ref[...]).astype(jnp.bfloat16)
    if cores is not None:
        cores.send(step)

    @pl.when(step == pl.num_programs(0) - 1)
    def _():
        for index in range(split):
            rows = slice(index * chunk, (index + 1) * chunk)
            shape, inverse = norm_parts(middle_ref[rows, :])
            grad = total_ref[rows, :]
            add_rows(sums_ref, 1, grad)
            add_rows(sums_ref, 2, grad * shape)
            back = norm_back(grad * (1.0 + mod_ref[4:5]), shape, inverse)
            grad_middle_ref[rows, :] = load_rows(grad_ref, index, chunk) + back


def attention_backward_kernel(
    stride, swap, cores, hook, source, grad_ref, stream_ref, project_ref, mixed_ref, branch_ref, mod_ref, *refs
):
    if swap is None:
        grad_stream_ref, *refs = refs
    if cores is None:
        weight_grad_ref, *refs = refs
    (sums_ref, project_sum_ref,
     weight_ref, semaphores, left_ref, right_ref, outer_ref) = refs
    step = pl.program_id(0)
    ranks = weight_ref.shape[0]

    @pl.when(step == 0)
    def _():
        start_loads(source, weight_ref, semaphores)
        sums_ref[...] = jnp.zeros_like(sums_ref)
        project_sum_ref[...] = jnp.zeros_like(project_sum_ref)

    grad_middle = rows_of(grad_ref)
    tokens, width = grad_middle.shape
    stream = rows_of(stream_ref).astype(jnp.float32)
    shape, inverse = norm_parts(stream)
    rows = pl.ds(pl.multiple_of(step * tokens, tokens), tokens)
    normed = (shape * (1.0 + mod_ref[1:2]) + mod_ref[0:1]).astype(jnp.bfloat16)
    low = (mod_ref[2:3] * grad_middle).astype(jnp.bfloat16)
    left_ref[0, :, rows] = normed.T
    left_ref[1, :, rows] = low.T
    add_rows(sums_ref, 0, low.astype(jnp.float32))
    add_rows(sums_ref, 3, grad_middle * rows_of(branch_ref).astype(jnp.float32))
    lower = half_masks(tokens)
    allowed = same_patch(tokens, stride) if stride else None
    scale = HD**-0.5

    @pl.when(step == 0)
    def _():
        for rank in range(ranks):
            wait_loads(weight_ref, semaphores, rank)

    def score_grads(heads):
        scores = [mm(key, chosen.astype(jnp.bfloat16), ((1,), (1,))) for chosen, key, _, _ in heads]
        grad_probs = [mm(value, taken.astype(jnp.bfloat16), ((1,), (1,))) for _, _, value, taken in heads]
        outs = []
        for score, grad_prob in zip(scores, grad_probs):
            if stride:
                score = jnp.where(allowed, score, BLOCKED)
            probs = softmax_rows(score, 0)
            inner = jnp.sum(grad_prob * probs, axis=0, keepdims=True)
            outs.append((probs.astype(jnp.bfloat16), (probs * (grad_prob - inner)).astype(jnp.bfloat16)))
        return outs

    grad_normed = None
    for rank in range(ranks):
        hook(rank)
        project = project_ref[rank].reshape(tokens, 5 * PAIR)
        mixed = mixed_ref[rank].reshape(tokens, 2 * PAIR)
        outer_ref[rank, rows, :] = mixed
        grad_mixed = mm(low, weight_ref[rank, :, 4 * PAIR :]).astype(jnp.bfloat16)
        query, key, value = (project[:, n * PAIR : (n + 1) * PAIR] for n in range(3))
        query_wide = query.astype(jnp.float32) * scale
        pair = grad_mixed[:, PAIR:]
        pair_wide = pair.astype(jnp.float32)
        both = project[:, 3 * PAIR : 4 * PAIR].astype(jnp.float32)
        swapped = swap_halves(both).astype(jnp.bfloat16)
        single = swap_halves(grad_mixed[:, :PAIR].astype(jnp.float32))
        heads = [
            (jnp.where(keep, query_wide, 0.0), key, value, jnp.where(keep, pair_wide, 0.0)) for keep in (lower, ~lower)
        ]
        heads.append(
            (jnp.where(lower, both * scale, 0.0), swapped, project[:, 4 * PAIR :], jnp.where(lower, single, 0.0))
        )
        solved = score_grads(heads)
        outs = [
            (mm(grad_scores, key, ((0,), (0,))), mm(grad_scores, query), mm(probs, pair))
            for probs, grad_scores in solved[:2]
        ]
        parts = [
            jnp.where(lower, one, two) * factor
            for one, two, factor in zip(outs[0], outs[1], (scale, scale, 1.0))
        ]
        probs, grad_scores = solved[2]
        parts.append(
            jnp.where(lower, mm(grad_scores, swapped, ((0,), (0,))), mm(grad_scores, swapped)) * scale
        )
        parts.append(jnp.where(lower, mm(probs, single.astype(jnp.bfloat16)), 0.0))
        whole = jnp.concatenate(parts, axis=1).astype(jnp.bfloat16)
        right_ref[rank, rows, :] = whole
        add_rows(project_sum_ref, rank, whole.astype(jnp.float32))
        term = mm(whole, weight_ref[rank, :, : 5 * PAIR], ((1,), (1,)))
        grad_normed = term if grad_normed is None else grad_normed + term
    add_rows(sums_ref, 1, grad_normed)
    add_rows(sums_ref, 2, grad_normed * shape)
    back = norm_back(grad_normed * (1.0 + mod_ref[1:2]), shape, inverse)
    if swap is None:
        put(grad_stream_ref, grad_middle + back)
    else:
        swap.put(step, grad_middle + back)

    @pl.when(step == pl.num_programs(0) - 1)
    def _():
        def weights(rank, carry):
            inside = mm(left_ref[0], right_ref[rank])
            outside = mm(left_ref[1], outer_ref[rank])
            made = weight_grad_ref.at[rank] if cores is None else cores.slot(rank).at[0]
            made[:, : 4 * PAIR] = inside[:, : 4 * PAIR].astype(jnp.bfloat16)
            made[:, 4 * PAIR : 5 * PAIR] = (inside[:, 4 * PAIR :] + outside[:, :PAIR]).astype(jnp.bfloat16)
            made[:, 5 * PAIR :] = outside[:, PAIR:].astype(jnp.bfloat16)
            if cores is not None:
                cores.send(rank)
            return carry

        lax.fori_loop(0, ranks, weights, 0)


def fixed(shape):
    return pl.BlockSpec(shape, lambda step: (0,) * len(shape), pipeline_mode=pl.Buffered(1))


def cost(flops, moved, raised=0):
    return pl.CostEstimate(flops=int(flops), bytes_accessed=int(moved), transcendentals=int(raised))


def group_spec(shape):
    return pl.BlockSpec((shape[0], 1, shape[2], shape[3]), lambda step: (0, step, 0, 0))


def rank_spec(shape):
    return pl.BlockSpec((shape[0], shape[1], 1) + shape[3:], lambda step: (0, 0, step, 0, 0))


def attention_forward(weight, stream, mod, bias, bias_out, stride, jobs=(), collective_id=None):
    shape = stream.shape
    width = shape[-1]
    ranks = bias.shape[0]
    tokens = shape[0] * shape[1] * shape[2]
    spec = group_spec(shape)
    low = jax.ShapeDtypeStruct(shape, jnp.bfloat16)
    wide = jax.ShapeDtypeStruct(shape, jnp.float32)
    project = jax.ShapeDtypeStruct((ranks,) + shape[:3] + (5 * PAIR,), jnp.bfloat16)
    mixed = jax.ShapeDtypeStruct((ranks,) + shape[:3] + (2 * PAIR,), jnp.bfloat16)
    return call(
        partial(attention_forward_kernel, stride),
        shape[1],
        [weight, stream, mod, bias, bias_out],
        anywhere(1) + [spec, fixed(mod.shape), fixed(bias.shape), fixed(bias_out.shape)],
        [project, mixed, low, wide],
        [rank_spec(project.shape), rank_spec(mixed.shape), spec, spec],
        [pltpu.VMEM((ranks, width, 6 * PAIR), jnp.bfloat16), pltpu.SemaphoreType.DMA((ranks,))],
        jobs,
        collective_id,
        cost(8 * tokens * width * width * 1.5, tokens * width * 16),
        "attention_forward",
    )


def ffn_weights_scratch(ranks, width, part):
    return [
        pltpu.VMEM((ranks, width, part), jnp.bfloat16),
        pltpu.VMEM((ranks, width, part), jnp.bfloat16),
        pltpu.SemaphoreType.DMA((ranks,)),
        pltpu.SemaphoreType.DMA((ranks,)),
    ]


def ffn_forward(up, down, middle, mod, bias_down, bias_up, stream=None, jobs=(), collective_id=None):
    tokens, width = middle.shape
    ranks, _, part = bias_up.shape
    steps = 4
    chunk = tokens // steps
    block = pl.BlockSpec((chunk, width), lambda step: (step, 0))
    result = [jax.ShapeDtypeStruct((tokens, width), jnp.bfloat16)] if stream is None else []
    return call(
        partial(ffn_forward_kernel, stream),
        steps,
        [up, down, middle, mod, bias_down, bias_up],
        anywhere(2) + [block, fixed(mod.shape), fixed(bias_down.shape), fixed(bias_up.shape)],
        [
            jax.ShapeDtypeStruct((ranks, tokens, part), jnp.bfloat16),
            jax.ShapeDtypeStruct((tokens, width), jnp.bfloat16),
        ] + result,
        [pl.BlockSpec((ranks, chunk, part), lambda step: (0, step, 0)), block] + [block] * len(result),
        ffn_weights_scratch(ranks, width, part),
        ([] if stream is None else [stream]) + list(jobs),
        collective_id,
        cost(4.8 * tokens * width * ranks * part, tokens * width * 14, tokens * ranks * part),
        "ffn_forward",
    )


def ffn_backward(up, down, grad, middle, branch, hidden, mod, cores=None, jobs=(), collective_id=None):
    tokens, width = middle.shape
    ranks, _, part = hidden.shape
    whole = fixed((tokens, width))
    made = [jax.ShapeDtypeStruct((2, ranks, width, part), jnp.bfloat16)] if cores is None else []
    return call(
        partial(ffn_backward_kernel, 2, cores),
        ranks,
        [up, down, grad, middle, branch, hidden, mod],
        anywhere(2) + [
            fixed(grad.shape), whole, whole,
            pl.BlockSpec((1, tokens, part), lambda step: (step, 0, 0)),
            fixed(mod.shape),
        ],
        [
            jax.ShapeDtypeStruct((tokens, width), jnp.float32),
            jax.ShapeDtypeStruct((ranks, 1, part), jnp.float32),
            jax.ShapeDtypeStruct((4, width), jnp.float32),
        ] + made,
        [
            whole,
            pl.BlockSpec((1, 1, part), lambda step: (step, 0, 0)),
            fixed((4, width)),
        ] + [pl.BlockSpec((2, 1, width, part), lambda step: (0, step, 0, 0))] * len(made),
        ffn_weights_scratch(ranks, width, part) + [
            pltpu.VMEM((width, tokens), jnp.bfloat16),
            pltpu.VMEM((tokens, width), jnp.bfloat16),
            pltpu.VMEM((width, tokens), jnp.bfloat16),
            pltpu.VMEM((tokens, part), jnp.bfloat16),
            pltpu.VMEM((tokens, part), jnp.bfloat16),
            pltpu.VMEM((tokens, width), jnp.float32),
        ],
        ([] if cores is None else [cores]) + list(jobs),
        collective_id,
        cost(9.6 * tokens * width * ranks * part, tokens * width * 20, tokens * ranks * part),
        "ffn_backward",
    )


def attention_backward(weight, grad, stream, saved, mod, stride, swap=None, cores=None, jobs=(), collective_id=None):
    project, mixed, branch = saved
    shape = stream.shape
    width = shape[-1]
    ranks = project.shape[0]
    tokens = shape[0] * shape[1] * shape[2]
    spec = group_spec(shape)
    result = [jax.ShapeDtypeStruct(shape, jnp.float32)] if swap is None else []
    made = [jax.ShapeDtypeStruct((ranks, width, 6 * PAIR), jnp.bfloat16)] if cores is None else []
    return call(
        partial(attention_backward_kernel, stride, swap, cores),
        shape[1],
        [weight, grad, stream, project, mixed, branch, mod],
        anywhere(1) + [
            spec, spec, rank_spec(project.shape), rank_spec(mixed.shape), spec, fixed(mod.shape),
        ],
        result + made + [
            jax.ShapeDtypeStruct((4, width), jnp.float32),
            jax.ShapeDtypeStruct((ranks, 5 * PAIR), jnp.float32),
        ],
        [spec] * len(result) + [fixed((ranks, width, 6 * PAIR))] * len(made) + [
            fixed((4, width)), fixed((ranks, 5 * PAIR)),
        ],
        [
            pltpu.VMEM((ranks, width, 6 * PAIR), jnp.bfloat16),
            pltpu.SemaphoreType.DMA((ranks,)),
            pltpu.VMEM((2, width, tokens), jnp.bfloat16),
            pltpu.VMEM((ranks, tokens, 5 * PAIR), jnp.bfloat16),
            pltpu.VMEM((ranks, tokens, 2 * PAIR), jnp.bfloat16),
        ],
        [job for job in (swap, cores) if job is not None] + list(jobs),
        collective_id,
        cost(16 * tokens * width * width * 1.5, tokens * width * 20),
        "attention_backward",
    )


def pack_heads(block):
    query, key, value, outer = block
    return jnp.concatenate(
        [query[:, :PAIR], key[:, :PAIR], value[:, :PAIR], query[:, PAIR:], key[:, PAIR:],
         value[:, PAIR:], outer[:, PAIR:], outer[:, :PAIR]], axis=1
    )


def unpack_heads(packed):
    part = lambda start, size: packed[:, start : start + size]
    join = lambda first, last: jnp.concatenate([part(first, PAIR), part(last, HD)], axis=1)
    return jnp.stack(
        [join(0, 3 * PAIR), join(PAIR, 3 * PAIR + HD), join(2 * PAIR, 4 * PAIR), join(5 * PAIR, 4 * PAIR + HD)]
    )


def pack_bias(query, value, ranks):
    query, value = query.reshape(ranks, -1), value.reshape(ranks, -1)
    none = jnp.zeros((ranks, PAIR), query.dtype)
    return jnp.concatenate(
        [query[:, :PAIR], none, value[:, :PAIR], query[:, PAIR:], none[:, :HD], value[:, PAIR:], none[:, :HD]],
        axis=1,
    )[:, None]


def unpack_bias(sums):
    query = jnp.concatenate([sums[:, :PAIR], sums[:, 3 * PAIR : 3 * PAIR + HD]], axis=1)
    value = jnp.concatenate([sums[:, 2 * PAIR : 3 * PAIR], sums[:, 4 * PAIR : 4 * PAIR + HD]], axis=1)
    return query.reshape(-1), value.reshape(-1)


def place():
    return lax.axis_index("dp"), lax.axis_index("tensor"), lax.axis_size("dp"), lax.axis_size("tensor")


def greet_all():
    device, rank, dp, tp = place()
    me, count = device * tp + rank, dp * tp
    barrier = pltpu.get_barrier_semaphore()

    def greet(index, carry):
        peer = lax.rem(me + index, count)
        pl.semaphore_signal(
            barrier, inc=1, device_id=(peer // tp, lax.rem(peer, tp)), device_id_type=pl.DeviceIdType.MESH
        )
        return carry

    lax.fori_loop(1, count, greet, 0)
    pl.semaphore_wait(barrier, count - 1)


def push(source, target, send, receive, device, rank):
    pltpu.make_async_remote_copy(
        src_ref=source, dst_ref=target, send_sem=send, recv_sem=receive,
        device_id=(device, rank), device_id_type=pl.DeviceIdType.MESH,
    ).start()


def wait_bytes(ref, semaphore):
    pltpu.make_async_copy(ref, ref, semaphore).wait()


class Where:
    def __init__(self):
        device, rank = lax.axis_index("dp"), lax.axis_index("tensor")
        self.count = lax.axis_size("dp") // 2
        self.device, self.rank = device, rank
        self.far, self.side = device // 2, lax.rem(device, 2)
        self.row, self.core = rank // 2, lax.rem(rank, 2)
        self.other_side = self.far * 2 + 1 - self.side
        self.other_row = (1 - self.row) * 2 + self.core
        self.other_core = self.row * 2 + 1 - self.core

    def ahead(self, step):
        return lax.rem(self.far + step, self.count)

    def line(self, step):
        return self.ahead(step) * 2 + self.side


def greet_neighbours(here):
    barrier = pltpu.get_barrier_semaphore()
    peers = [(here.other_side, here.rank), (here.device, here.other_row), (here.device, here.other_core)]
    peers += [(here.line(step), here.rank) for step in range(1, here.count)]
    for peer in peers:
        pl.semaphore_signal(barrier, inc=1, device_id=peer, device_id_type=pl.DeviceIdType.MESH)
    pl.semaphore_wait(barrier, len(peers))


def add_into(target, left, right):
    target[...] = (left[...].astype(jnp.float32) + right[...].astype(jnp.float32)).astype(target.dtype)


class ScatterChain:
    def __init__(self, here, kept, given, line, lead, scratch):
        self.here, self.kept, self.given, self.line, self.lead = here, kept, given, line, lead
        self.keep, self.land_core, self.first_one, self.last_one, self.first_two, self.last_two, self.semaphores = scratch
        self.rows = line.shape[1]

    @staticmethod
    def scratch(width, columns, dp, lead):
        rows, far = width // dp, dp // 2
        low = lambda *shape: pltpu.VMEM(shape + (columns,), jnp.bfloat16)
        return [
            low(2, width), low(2, width),
            low(2, lead, rows), low(2 * (far - lead) * rows), low(lead, rows), low(far - lead, rows),
            pltpu.SemaphoreType.DMA((6, 2)),
        ]

    def chunk(self, row, far, side):
        return self.keep.at[row, pl.ds(pl.multiple_of((far * 2 + side) * self.rows, self.rows), self.rows)]

    def send(self, slot, source, target, device, rank):
        push(source, target, self.semaphores.at[slot, 0], self.semaphores.at[slot, 1], device, rank)

    def arrived(self, slot, ref):
        wait_bytes(ref, self.semaphores.at[slot, 1])

    def left(self, slot, ref):
        wait_bytes(ref, self.semaphores.at[slot, 0])

    def stage_load(self):
        pltpu.make_async_copy(self.kept, self.keep, self.semaphores.at[5, 0]).start()
        pltpu.make_async_copy(self.given, self.land_core, self.semaphores.at[5, 1]).start()

    def stage_one(self):
        here = self.here
        wait_bytes(self.keep, self.semaphores.at[5, 0])
        wait_bytes(self.land_core, self.semaphores.at[5, 1])

        def one(index, carry):
            rows = pl.ds(pl.multiple_of(index * self.rows, self.rows), self.rows)
            for row in range(2):
                add_into(self.keep.at[row, rows], self.keep.at[row, rows], self.land_core.at[row, rows])
            return carry

        lax.fori_loop(0, here.count * 2, one, 0)
        for row in range(2):
            for far in range(self.lead):
                self.send(
                    1, self.chunk(row, far, 1 - here.side), self.first_one.at[row, far], here.other_side, here.rank
                )
        start, size = self.lead * 2 * self.rows, (here.count - self.lead) * 2 * self.rows
        self.send(2, self.keep.at[1 - here.row, pl.ds(start, size)], self.last_one, here.device, here.other_row)

    def stage_two(self):
        here, lead = self.here, self.lead
        self.arrived(1, self.first_one)
        for row in range(2):
            for far in range(lead):
                mine = self.chunk(row, far, here.side)
                add_into(mine, mine, self.first_one.at[row, far])
        for far in range(lead):
            self.send(3, self.chunk(1 - here.row, far, here.side), self.first_two.at[far], here.device, here.other_row)
        self.arrived(2, self.last_one)
        for far in range(lead, here.count):
            for side in range(2):
                mine = self.chunk(here.row, far, side)
                add_into(mine, mine, self.last_one.at[pl.ds(((far - lead) * 2 + side) * self.rows, self.rows)])
        for far in range(lead, here.count):
            self.send(
                4, self.chunk(here.row, far, 1 - here.side), self.last_two.at[far - lead], here.other_side, here.rank
            )

    def merge(self):
        here = self.here
        self.arrived(3, self.first_two)
        self.arrived(4, self.last_two)
        for far in range(here.count):
            land = self.first_two.at[far] if far < self.lead else self.last_two.at[far - self.lead]
            add_into(self.line.at[far], self.chunk(here.row, far, here.side), land)

    def finish(self):
        self.left(1, self.first_one)
        self.left(2, self.last_one)
        self.left(3, self.first_two)
        self.left(4, self.last_two)


class LineChain:
    def __init__(self, here, line, out, land, semaphores):
        self.here, self.line, self.out, self.land, self.semaphores = here, line, out, land, semaphores

    @staticmethod
    def scratch(far, rows, columns):
        return [pltpu.VMEM((far - 1, rows, columns), jnp.bfloat16), pltpu.SemaphoreType.DMA((2,))]

    def start(self):
        here = self.here
        for step in range(1, here.count):
            push(
                self.line.at[here.ahead(step)], self.land.at[step - 1], self.semaphores.at[0],
                self.semaphores.at[1], here.line(step), here.rank,
            )

    def finish(self):
        wait_bytes(self.land, self.semaphores.at[1])
        total = self.line[self.here.far].astype(jnp.float32)
        for step in range(1, self.here.count):
            total = total + self.land[step - 1].astype(jnp.float32)
        self.out[...] = total
        wait_bytes(self.land, self.semaphores.at[0])


def leave_kernel(mod_start, *refs):
    refs = list(refs)
    scattering = len(refs) > 10
    kept, given, begun = (refs.pop(0), refs.pop(0), refs.pop(0)) if scattering else (None, None, None)
    small_ref, modulation_ref, *refs = refs
    out, begun_out = (refs.pop(0), refs.pop(0)) if scattering else (None, None)
    sum_ref, act_ref, land_ref, acting_ref, semaphores, *space = refs
    device, rank, dp, tp = place()
    me, count = device * tp + rank, dp * tp
    greet_all()
    if scattering:
        here = Where()
        line_ref, *space = space
        pick = lambda number: [space.pop(0) for _ in range(number)]
        chains, trails = [], []
        for index in range(PARTS):
            size = out.shape[1] // PARTS
            part = pl.ds(index * size, size)
            line = line_ref.at[index]
            chains.append(
                ScatterChain(here, kept.at[0, :, :, part], given.at[0, :, :, part], line, here.count // 2, pick(7))
            )
            trails.append(LineChain(here, line, out.at[:, part], *pick(2)))
        others = [LineChain(here, begun.at[kind], begun_out.at[kind], *pick(2)) for kind in range(begun.shape[0])]
        for chain in chains:
            chain.stage_load()
    for step in range(1, tp):
        there = lax.rem(rank + step, tp)
        push(small_ref.at[there], land_ref.at[rank], semaphores.at[0], semaphores.at[1], device, there)
    land_ref[rank] = small_ref[rank]
    wait_bytes(land_ref.at[pl.ds(0, tp - 1)], semaphores.at[1])
    mine = sum_ref.at[rank]
    mine[device] = jnp.sum(land_ref[...], axis=0)

    def one(step, carry):
        push(mine.at[device], mine.at[device], semaphores.at[2], semaphores.at[3], lax.rem(device + step, dp), rank)
        return carry

    lax.fori_loop(1, dp, one, 0)
    if scattering:
        for chain in others:
            chain.start()
    wait_bytes(mine.at[pl.ds(0, dp - 1)], semaphores.at[3])
    for step in range(1, tp):
        push(mine, mine, semaphores.at[4], semaphores.at[5], device, lax.rem(rank + step, tp))
    if scattering:
        for chain in chains:
            chain.stage_one()
        chains[0].stage_two()
    wait_bytes(sum_ref.at[pl.ds(0, tp - 1)], semaphores.at[5])
    layers, padded, columns = modulation_ref.shape
    lines = sum_ref.shape[2]
    total = jnp.zeros((dp, padded), jnp.float32)
    for layer in range(layers):
        for index in range(columns // PAIR):
            line = layer * (tp * lines // layers) + mod_start // PAIR + index
            low = sum_ref[line // lines, :, line % lines, :].astype(jnp.bfloat16)
            total += mm(low, modulation_ref[layer, :, index * PAIR : (index + 1) * PAIR], ((1,), (1,)))
    acting_ref[...] = jnp.concatenate([total, jnp.zeros((dp, PAIR - padded), jnp.float32)], axis=1)
    act_ref[me] = acting_ref[...]

    def tell(index, carry):
        peer = lax.rem(me + index, count)
        push(acting_ref, act_ref.at[me], semaphores.at[6], semaphores.at[7], peer // tp, lax.rem(peer, tp))
        return carry

    lax.fori_loop(1, count, tell, 0)
    if scattering:
        for chain in chains[1:]:
            chain.stage_two()
        for chain, line in zip(chains, trails):
            chain.merge()
            line.start()
        for chain in others:
            chain.finish()
    wait_bytes(act_ref.at[pl.ds(0, count - 1)], semaphores.at[7])
    wait_bytes(act_ref.at[pl.ds(0, count - 1)], semaphores.at[6])
    wait_bytes(land_ref.at[pl.ds(0, tp - 1)], semaphores.at[0])
    wait_bytes(mine.at[pl.ds(0, dp - 1)], semaphores.at[2])
    wait_bytes(sum_ref.at[pl.ds(0, tp - 1)], semaphores.at[4])
    if scattering:
        for chain in chains + trails:
            chain.finish()


def leave(small, modulation, mod_start, halves, begun, collective_id):
    tp, lines, lanes = small.shape
    dp = lax.axis_size("dp")
    inside = pl.BlockSpec(memory_space=pltpu.VMEM)
    shapes, space, extra = [], [], []
    if halves is not None:
        _, _, width, columns = halves[0].shape
        rows, far, part = width // dp, dp // 2, columns // PARTS
        kinds = begun.shape[0]
        extra = [*halves, begun]
        shapes = [
            jax.ShapeDtypeStruct((rows, columns), jnp.float32),
            jax.ShapeDtypeStruct((kinds, rows, columns), jnp.float32),
        ]
        space = [pltpu.VMEM((PARTS, far, rows, part), jnp.bfloat16)]
        for _ in range(PARTS):
            space += ScatterChain.scratch(width, part, dp, far // 2) + LineChain.scratch(far, rows, part)
        space += LineChain.scratch(far, rows, columns) * kinds
    return pl.pallas_call(
        partial(leave_kernel, mod_start),
        in_specs=([pl.BlockSpec(memory_space=pl.ANY)] * 2 + [inside])[: len(extra)] + [inside, inside],
        out_specs=[inside] * (len(shapes) + 2),
        out_shape=shapes + [
            jax.ShapeDtypeStruct((tp, dp, lines, lanes), jnp.float32),
            jax.ShapeDtypeStruct((dp * tp, dp, lanes), jnp.float32),
        ],
        scratch_shapes=[
            pltpu.VMEM((tp, lines, lanes), jnp.float32),
            pltpu.VMEM((dp, lanes), jnp.float32),
            pltpu.SemaphoreType.DMA((8,)),
        ] + space,
        compiler_params=pltpu.CompilerParams(
            collective_id=collective_id, has_side_effects=True, vmem_limit_bytes=VMEM_LIMIT
        ),
        name="leave",
    )(*extra, small, modulation)


class GatherChain:
    def __init__(self, here, source, out, semaphores, half=None):
        self.here, self.source, self.out, self.semaphores = here, source, out, semaphores
        self.rows = out.shape[1] // (2 * here.count)
        self.half = here.count // 2 if half is None else half

    @staticmethod
    def scratch():
        return [pltpu.SemaphoreType.DMA((9, 2))]

    def piece(self, rank, far, side):
        rows = pl.ds(pl.multiple_of((far * 2 + side) * self.rows, self.rows), self.rows)
        return self.out.at[rank, rows]

    def send(self, slot, source, target, device, rank):
        push(source, target, self.semaphores.at[slot, 0], self.semaphores.at[slot, 1], device, rank)

    def wait(self, slot, way, pieces):
        wait_bytes(self.out.at[0, pl.ds(0, pieces * self.rows)], self.semaphores.at[slot, way])

    def stage_line(self):
        here = self.here
        mine = self.piece(here.rank, here.far, here.side)
        pltpu.make_async_copy(self.source, mine, self.semaphores.at[8, 0]).start()
        for step in range(1, here.count):
            self.send(0, self.source, mine, here.line(step), here.rank)

    def line_arrived(self):
        self.wait(8, 0, 1)
        self.wait(0, 1, self.here.count - 1)

    def line_left(self):
        self.wait(0, 0, self.here.count - 1)

    def stage_near(self):
        here = self.here
        for turn in range(2):
            over_row = lax.rem(here.core + turn, 2) == 1
            device = jnp.where(over_row, here.device, here.other_side)
            rank = jnp.where(over_row, here.other_row, here.rank)
            for far in range(here.count):
                mine = self.piece(here.rank, far, here.side)
                self.send(1 + lax.rem(here.core + turn, 2), mine, mine, device, rank)
        for far in range(here.count):
            mine = self.piece(here.rank, far, here.side)
            self.send(3, mine, mine, here.device, here.other_core)

    def stage_across(self):
        here, count = self.here, self.here.count
        self.wait(1, 1, count)
        for far in range(self.half):
            other = self.piece(here.rank, far, 1 - here.side)
            self.send(4, other, other, here.device, here.other_row)
        self.wait(2, 1, count)
        for far in range(self.half, count):
            other = self.piece(here.other_row, far, here.side)
            self.send(5, other, other, here.other_side, here.rank)
        for far in range(count):
            for other in (self.piece(here.rank, far, 1 - here.side), self.piece(here.other_row, far, here.side)):
                self.send(6, other, other, here.device, here.other_core)

    def stage_core(self):
        here, count = self.here, self.here.count
        self.wait(4, 1, self.half)
        self.wait(5, 1, count - self.half)
        for far in range(count):
            other = self.piece(here.other_row, far, 1 - here.side)
            self.send(7, other, other, here.device, here.other_core)

    def finish(self):
        count, half = self.here.count, self.half
        self.wait(3, 1, count)
        self.wait(6, 1, 2 * count)
        self.wait(7, 1, count)
        for slot, pieces in ((1, count), (2, count), (3, count), (4, half), (5, count - half), (6, 2 * count), (7, count)):
            self.wait(slot, 0, pieces)


class Job:
    operands, sources, shapes, specs, aliases, space = (), None, (), (), {}, ()
    stages, last = {}, ()


def anywhere(count):
    return [pl.BlockSpec(memory_space=pl.ANY)] * count


class CoreJob(Job):
    def __init__(self, kinds, width, columns):
        shape = (kinds, 2, width, columns)
        self.shapes, self.specs = [jax.ShapeDtypeStruct(shape, jnp.bfloat16)] * 2, anywhere(2)
        self.space = [pltpu.VMEM((2, kinds, width, columns), jnp.bfloat16), pltpu.SemaphoreType.DMA((3,))]

    def bind(self, here, inputs, outputs, space):
        self.here, (self.kept, self.given), (self.buffer, self.semaphores) = here, outputs, space
        self.stages = {}
        self.last = [lambda: self.sent(0), lambda: self.sent(1), lambda: wait_bytes(self.given, self.semaphores.at[2])]

    def sent(self, core):
        wait_bytes(self.buffer.at[core], self.semaphores.at[core])

    def slot(self, rank):
        core = lax.rem(rank, 2)

        @pl.when(rank >= 2)
        def _():
            self.sent(core)

        return self.buffer.at[core]

    def send(self, rank):
        here, row, core = self.here, rank // 2, lax.rem(rank, 2)

        @pl.when(core == here.core)
        def _():
            pltpu.make_async_copy(self.buffer.at[core], self.kept.at[:, row], self.semaphores.at[core]).start()

        @pl.when(core != here.core)
        def _():
            push(
                self.buffer.at[core], self.given.at[:, row], self.semaphores.at[core], self.semaphores.at[2],
                here.device, here.other_core,
            )


class ScatterJob(Job):
    def __init__(self, grads, lead, close=False):
        _, _, width, columns = grads[0][0][0].shape
        dp = lax.axis_size("dp")
        far, rows = dp // 2, width // dp
        self.lead, self.close, self.kinds = lead, close, [kind for _, kind in grads]
        self.operands = [array for sides, _ in grads for array in sides]
        shape = (len(grads) - close, far, rows, columns)
        self.shapes, self.specs = [jax.ShapeDtypeStruct(shape, jnp.bfloat16)], [fixed(shape)]
        self.space = ScatterChain.scratch(width, columns, dp, lead) * len(grads)
        if close:
            self.shapes.append(jax.ShapeDtypeStruct((1, rows, columns), jnp.float32))
            self.specs.append(fixed((1, rows, columns)))
            self.space = [pltpu.VMEM((far, rows, columns), jnp.bfloat16)] + LineChain.scratch(
                far, rows, columns
            ) + self.space

    def bind(self, here, inputs, outputs, space):
        lines = [outputs[0].at[index] for index in range(outputs[0].shape[0])]
        if self.close:
            own, land, semaphores, *space = space
            lines.insert(0, own)
            line = LineChain(here, own, outputs[1].at[0], land, semaphores)
        size = 2 * len(space) // len(inputs)
        chains = [
            ScatterChain(
                here, inputs[2 * index].at[kind], inputs[2 * index + 1].at[kind], lines[index], self.lead,
                space[index * size : (index + 1) * size],
            )
            for index, kind in enumerate(self.kinds)
        ]
        one = chains[0]
        if len(chains) == 1:
            self.stages = {(0, 0): [one.stage_load], (0, 1): [one.stage_one], (2, 0): [one.stage_two]}
            self.last = [one.merge, one.finish]
            return
        two = chains[1]
        if self.close:
            self.stages = {
                (0, 0): [one.stage_load, two.stage_load], (0, 1): [one.stage_one],
                (1, 2): [one.stage_two, two.stage_one], (2, 1): [one.merge, line.start], (3, 2): [two.stage_two],
            }
            self.last = [line.finish, two.merge, one.finish, two.finish]
            return
        self.stages = {
            (0, 0): [one.stage_load, two.stage_load], (0, 1): [one.stage_one], (0, 3): [two.stage_one],
            (2, 0): [one.stage_two], (3, 2): [two.stage_two],
        }
        self.last = [one.merge, two.merge, one.finish, two.finish]


class LineJob(Job):
    def __init__(self, line):
        kinds, far, rows, columns = line.shape
        shape = (kinds, rows, columns)
        self.operands, self.sources = [line], [fixed(line.shape)]
        self.shapes, self.specs = [jax.ShapeDtypeStruct(shape, jnp.float32)], [fixed(shape)]
        self.space = LineChain.scratch(far, rows, columns) * kinds

    def bind(self, here, inputs, outputs, space):
        chains = [
            LineChain(here, inputs[0].at[kind], outputs[0].at[kind], *space[2 * kind : 2 * kind + 2])
            for kind in range(outputs[0].shape[0])
        ]
        self.stages = {(0, 0): [chain.start for chain in chains]}
        self.last = [chain.finish for chain in chains]


class FlowJob(Job):
    def __init__(self, spread, lines, half=None, late=()):
        dp, tp = lax.axis_size("dp"), lax.axis_size("tensor")
        self.counts, self.half = (len(spread), len(late)), half
        shards = list(late) + list(lines)
        self.operands = list(spread) + shards
        self.shapes = [jax.ShapeDtypeStruct(v.shape, v.dtype) for v in spread]
        self.shapes += [jax.ShapeDtypeStruct((tp, dp * v.shape[0], v.shape[1]), v.dtype) for v in shards]
        self.specs = anywhere(len(self.shapes))
        self.aliases = {index: index for index in range(len(spread))}
        self.space = GatherChain.scratch() * len(self.shapes)

    def bind(self, here, inputs, outputs, space):
        chains = [GatherChain(here, *refs, self.half) for refs in zip(inputs, outputs, space)]
        first, late = self.counts
        spread, late, lines = chains[:first], chains[first : first + late], chains[first + late :]
        self.stages = {
            (0, 0): [chain.stage_near for chain in spread] + [chain.stage_line for chain in late + lines],
            (3, 0): [chain.stage_across for chain in spread],
        }
        for chain in late:
            self.stages[3, 0] += [chain.line_arrived, chain.stage_near]
        self.last = [chain.stage_across for chain in late]
        self.last += [chain.stage_core for chain in spread + late]
        self.last += [chain.finish for chain in spread + late]
        self.last += [chain.line_arrived for chain in lines]
        self.last += [chain.line_left for chain in late + lines]


class SwapJob(Job):
    def __init__(self, blocks):
        self.operands = [blocks]
        self.shapes, self.specs = [jax.ShapeDtypeStruct(blocks.shape, blocks.dtype)], anywhere(1)
        self.space = [pltpu.SemaphoreType.DMA((3,))]

    def bind(self, here, inputs, outputs, space):
        source, out, semaphores = inputs[0], outputs[0], space[0]
        ranks = out.shape[0]

        def start():
            pltpu.make_async_copy(source.at[here.rank], out.at[here.rank], semaphores.at[2]).start()
            for step in range(1, ranks):
                there = lax.rem(here.rank + step, ranks)
                push(source.at[there], out.at[here.rank], semaphores.at[0], semaphores.at[1], here.device, there)

        def finish():
            wait_bytes(out.at[0], semaphores.at[2])
            wait_bytes(out.at[pl.ds(0, ranks - 1)], semaphores.at[1])
            wait_bytes(out.at[pl.ds(0, ranks - 1)], semaphores.at[0])

        self.stages, self.last = {(0, 0): [start]}, [finish]


class StreamJob(Job):
    def __init__(self, shape, frames):
        self.shape, self.frames = shape, frames
        self.shapes, self.specs = [jax.ShapeDtypeStruct(shape, jnp.bfloat16)], anywhere(1)
        ranks, groups, rows, width = shape
        block = (groups, ranks, rows, width)
        if frames:
            block = (frames, ranks, groups, rows // frames, width)
        self.space = [pltpu.VMEM(block, jnp.bfloat16), pltpu.SemaphoreType.DMA((3,))]

    def bind(self, here, inputs, outputs, space):
        self.here, self.out = here, outputs[0]
        self.buffer, self.semaphores = space
        ranks = self.shape[0]

        def finish():
            wait_bytes(self.out.at[0], self.semaphores.at[2])
            wait_bytes(self.out.at[pl.ds(0, ranks - 1)], self.semaphores.at[1])
            wait_bytes(self.out.at[pl.ds(0, ranks - 1)], self.semaphores.at[0])

        self.stages, self.last = {}, [finish]

    def put(self, step, value):
        here, ranks = self.here, self.shape[0]
        size = self.buffer.size // self.buffer.shape[0] // value.shape[1]
        if value.shape[0] > size:
            count = value.shape[0] // size
            for index in range(count):
                self.put(step * count + index, value[index * size : (index + 1) * size])
            return
        self.buffer[step] = value.reshape(self.buffer.shape[1:]).astype(jnp.bfloat16)
        if self.frames:
            strip = self.buffer.shape[3]
            target = self.out.at[here.rank, :, pl.ds(pl.multiple_of(step * strip, strip), strip)]
        else:
            target = self.out.at[here.rank, step]
        pltpu.make_async_copy(self.buffer.at[step, here.rank], target, self.semaphores.at[2]).start()
        for ahead in range(1, ranks):
            there = lax.rem(here.rank + ahead, ranks)
            push(
                self.buffer.at[step, there], target, self.semaphores.at[0], self.semaphores.at[1],
                here.device, there,
            )


def greet_jobs(here):
    barrier = pltpu.get_barrier_semaphore()
    ranks = lax.axis_size("tensor")
    peers = [(here.other_side, here.rank)]
    peers += [(here.line(step), here.rank) for step in range(1, here.count)]
    peers += [(here.device, lax.rem(here.rank + step, ranks)) for step in range(1, ranks)]
    for peer in peers:
        pl.semaphore_signal(barrier, inc=1, device_id=peer, device_id_type=pl.DeviceIdType.MESH)
    pl.semaphore_wait(barrier, len(peers))


def call(body, steps, arguments, in_specs, out_shape, out_specs, scratch, jobs, collective_id, estimate, name):
    operands = [v for job in jobs for v in job.operands]
    sources = [v for job in jobs for v in (job.sources or anywhere(len(job.operands)))]
    shapes = [v for job in jobs for v in job.shapes]
    specs = [v for job in jobs for v in job.specs]
    space = [v for job in jobs for v in job.space]
    aliases, before, after = {}, len(arguments), len(out_shape)
    for job in jobs:
        for source, target in job.aliases.items():
            aliases[before + source] = after + target
        before, after = before + len(job.operands), after + len(job.shapes)

    def kernel(*refs):
        refs = list(refs)
        take = lambda number: [refs.pop(0) for _ in range(number)]
        inputs, job_inputs = take(len(arguments)), take(len(operands))
        outputs, job_outputs = take(len(out_shape)), take(len(shapes))
        own, job_space = take(len(scratch)), refs
        step = pl.program_id(0)
        if jobs:
            here = Where()
            for job in jobs:
                pick = lambda pool, number: [pool.pop(0) for _ in range(number)]
                job.bind(
                    here, pick(job_inputs, len(job.operands)), pick(job_outputs, len(job.shapes)),
                    pick(job_space, len(job.space)),
                )

        def hook(spot):
            for index in range(steps):
                todo = [
                    stage
                    for job in jobs
                    for (late, place), stages in sorted(job.stages.items())
                    if (late * 4 + place) * steps // 4 == index * 4 + spot
                    for stage in stages
                ]
                if todo or (jobs and spot == 0 and index == 0):

                    @pl.when(step == index)
                    def _():
                        if index == 0 and spot == 0:
                            greet_jobs(here)
                        for stage in todo:
                            stage()

        hook(0)
        body(lambda spot: hook(spot) if spot else None, *inputs, *outputs, *own)
        if jobs:

            @pl.when(step == steps - 1)
            def _():
                for job in jobs:
                    for stage in job.last:
                        stage()

    more = {"collective_id": collective_id, "has_side_effects": True} if jobs else {}
    return pl.pallas_call(
        kernel,
        grid=(steps,),
        in_specs=list(in_specs) + sources,
        out_specs=list(out_specs) + specs,
        out_shape=list(out_shape) + shapes,
        scratch_shapes=list(scratch) + space,
        input_output_aliases=aliases,
        compiler_params=pltpu.CompilerParams(
            vmem_limit_bytes=VMEM_LIMIT, dimension_semantics=("arbitrary",), **more
        ),
        cost_estimate=estimate,
        name=name,
    )(*arguments, *operands)


def entry_kernel(
    per_device, row_ref, modulation_ref, *refs
):
    gather = 2 if len(refs) > 5 else 0
    refs = list(refs)
    sources = [refs.pop(0) for _ in range(gather)]
    gathered_ref, mod_ref = refs.pop(0), refs.pop(0)
    targets = [refs.pop(0) for _ in range(gather)]
    part_ref, land_ref, semaphores, *space = refs
    device, rank, dp, tp = place()
    me, count = device * tp + rank, dp * tp
    quarter = land_ref.shape[2]
    if gather:
        here = Where()
        size = sources[0].shape[1] // PARTS
        parts = []
        for index in range(PARTS):
            part = pl.ds(index * size, size)
            parts.append(GatherChain(here, sources[0].at[:, part], targets[0].at[:, :, part], space.pop(0)))
        following = GatherChain(here, sources[1], targets[1], space[0])
    greet_all()

    def tell(index, carry):
        peer = lax.rem(me + index, count)
        push(
            row_ref, gathered_ref.at[me], semaphores.at[0], semaphores.at[1], peer // tp, lax.rem(peer, tp)
        )
        return carry

    lax.fori_loop(1, count, tell, 0)
    gathered_ref[me] = row_ref[...]
    if gather:
        for chain in parts:
            chain.stage_line()
    wait_bytes(gathered_ref.at[pl.ds(0, count - 1)], semaphores.at[1])
    padded = modulation_ref.shape[1]
    width = dp * tp * per_device
    chosen = jnp.zeros((count, padded), jnp.float32)
    row = lax.broadcasted_iota(jnp.int32, (PAIR, padded), 0)
    column = lax.broadcasted_iota(jnp.int32, (PAIR, padded), 1)
    for index in range(width // PAIR):
        match = (row + index * PAIR == column + me * per_device) & (column < per_device)
        chosen += mm(
            gathered_ref[:, index, :].astype(jnp.bfloat16), jnp.where(match, 1.0, 0.0).astype(jnp.bfloat16)
        )
    clip = lax.broadcasted_iota(jnp.int32, (dp, count), 0)
    member = lax.broadcasted_iota(jnp.int32, (dp, count), 1)
    leaders = jnp.where(member == clip * tp, 1.0, 0.0).astype(jnp.bfloat16)
    rows = mm(leaders, chosen.astype(jnp.bfloat16)).astype(jnp.bfloat16)
    for layer in range(modulation_ref.shape[0]):
        part = mm(rows, modulation_ref[layer])
        size = part.shape[1]
        for index in range(dp):
            part_ref[index, :, layer * size : (layer + 1) * size] = part[index : index + 1]

    def share(index, carry):
        peer = lax.rem(me + index, count)
        there, lane = peer // tp, lax.rem(peer, tp)
        source = part_ref.at[there, :, pl.ds(pl.multiple_of(lane * quarter, PAIR), quarter)]
        push(source, land_ref.at[me], semaphores.at[2], semaphores.at[3], there, lane)
        return carry

    lax.fori_loop(1, count, share, 0)
    mine = pl.ds(pl.multiple_of(rank * quarter, PAIR), quarter)
    land_ref[me] = part_ref[device, :, mine]
    if gather:
        for chain in parts:
            chain.line_arrived()
            chain.stage_near()
        following.stage_line()
    wait_bytes(land_ref.at[pl.ds(0, count - 1)], semaphores.at[3])
    mod_ref[:, mine] = jnp.sum(land_ref[...], axis=0)
    for step in range(1, tp):
        push(
            mod_ref.at[:, mine], mod_ref.at[:, mine], semaphores.at[4], semaphores.at[5],
            device, lax.rem(rank + step, tp),
        )
    if gather:
        for chain in parts:
            chain.stage_across()
        for chain in parts:
            chain.stage_core()
    wait_bytes(gathered_ref.at[pl.ds(0, count - 1)], semaphores.at[0])
    wait_bytes(land_ref.at[pl.ds(0, count - 1)], semaphores.at[2])
    wait_bytes(mod_ref.at[:, pl.ds(0, (tp - 1) * quarter)], semaphores.at[5])
    wait_bytes(mod_ref.at[:, pl.ds(0, (tp - 1) * quarter)], semaphores.at[4])
    if gather:
        following.line_arrived()
        for chain in parts:
            chain.finish()
        for chain in (*parts, following):
            chain.line_left()


def enter(row, modulation, per_device, weights, collective_id):
    dp, tp = lax.axis_size("dp"), lax.axis_size("tensor")
    count = dp * tp
    whole = modulation.shape[0] * modulation.shape[2]
    inside = pl.BlockSpec(memory_space=pltpu.VMEM)
    job = FlowJob((), weights) if weights else Job()
    return pl.pallas_call(
        partial(entry_kernel, per_device),
        in_specs=[inside, inside] + anywhere(len(job.operands)),
        out_specs=[inside, inside] + list(job.specs),
        out_shape=[
            jax.ShapeDtypeStruct((count,) + row.shape, jnp.float32),
            jax.ShapeDtypeStruct((1, whole), jnp.float32),
        ] + list(job.shapes),
        scratch_shapes=[
            pltpu.VMEM((dp, 1, whole), jnp.float32),
            pltpu.VMEM((count, 1, whole // tp), jnp.float32),
            pltpu.SemaphoreType.DMA((6,)),
        ] + (GatherChain.scratch() * (PARTS + 1) if weights else []),
        compiler_params=pltpu.CompilerParams(
            collective_id=collective_id, has_side_effects=True, vmem_limit_bytes=VMEM_LIMIT
        ),
        name="enter",
    )(row, modulation, *job.operands)


def adam_update(weight, first, second, grad, rate, decay):
    first_new = BETA_ONE * first + (1.0 - BETA_ONE) * grad
    second_new = BETA_TWO * second + (1.0 - BETA_TWO) * grad * grad
    corrected = (
        first_new
        / (1.0 - BETA_ONE**STEP)
        / (jnp.sqrt(second_new / (1.0 - BETA_TWO**STEP)) + ADAM_EPS)
    )
    weight_new = weight - rate * (corrected + decay * weight)
    return (weight_new, first_new, second_new, weight_new.astype(jnp.bfloat16))


def dot32(form, left, right):
    return jnp.einsum(form, left, right, preferred_element_type=jnp.float32)


def exchange(blocks):
    return lax.all_to_all(blocks, "tensor", split_axis=0, concat_axis=0, tiled=True)


def gather_plain(shard):
    rows, width = shard.shape
    whole = lax.all_gather(shard, ("tensor", "dp"), axis=0, tiled=True)
    return whole.reshape(-1, lax.axis_size("dp") * rows, width)


def scatter_plain(grads):
    kinds, ranks, width, cols = grads.shape
    flat = grads.reshape(kinds, ranks * width, cols)
    summed = lax.psum_scatter(flat, ("tensor", "dp"), scatter_dimension=1, tiled=True)
    return summed.astype(jnp.float32)


def per_device(
    clips, cotangent, timesteps, labels, time_table, class_table,
    attention_weights, attention_first, attention_second,
    ffn_weights, ffn_first, ffn_second,
    modulation_weights, modulation_first, modulation_second,
    bias_vectors, bias_first, bias_second,
):
    layers, kinds, rows, cols = attention_weights.shape
    _, frames, patches, width = clips.shape
    mod_rows = modulation_weights.shape[1]
    bias_cols = bias_vectors.shape[1]
    dp, tp = lax.axis_size("dp"), lax.axis_size("tensor")
    position = lax.axis_index("dp") * tp + lax.axis_index("tensor")
    tokens = frames * patches
    strip = patches // (tp * frames)
    blocks = (tp, frames, frames * strip, width)
    pieces = (tp * frames, frames, strip, width)

    embed = time_table[timesteps] + class_table[labels]
    cond_act = jax.nn.silu(embed).astype(jnp.bfloat16)
    fused = rows % 16 == 0
    shards = [
        (
            pack_heads(attention_weights[layer].astype(jnp.bfloat16)),
            ffn_weights[layer, 0].astype(jnp.bfloat16),
            ffn_weights[layer, 1].astype(jnp.bfloat16),
        )
        for layer in range(layers)
    ]
    low = bias_vectors.astype(jnp.bfloat16).reshape(-1)
    row = jnp.concatenate([cond_act[0], low]).astype(jnp.float32)
    row = jnp.pad(row, (0, -row.shape[0] % 1024)).reshape(-1, 128)
    modulation_low = modulation_weights.astype(jnp.bfloat16)
    modulation_low = jnp.pad(modulation_low, ((0, 0), (0, -mod_rows % 32), (0, 0)))
    gathered, mod, *begun = enter(row, modulation_low, mod_rows, shards[0][:2] if fused else None, 0)
    gathered = gathered.reshape(dp * tp, -1)
    cond_all = gathered[::tp, :width].astype(jnp.bfloat16)
    bias_low = gathered[:, width : width + layers * bias_cols].reshape(dp * tp, layers, bias_cols)
    bias_low = bias_low.transpose(1, 0, 2).reshape(layers, -1)
    cond_rows = lax.dynamic_slice_in_dim(cond_all, position * mod_rows, mod_rows, axis=1)
    cond_rows = jnp.pad(cond_rows, ((0, 0), (0, -mod_rows % 32)))
    mod = mod.reshape(layers, -1)
    mod_width = mod.shape[-1]
    mod = (mod + bias_low[:, -mod_width:]).reshape(layers, 6, width)
    hidden_width = bias_low.shape[1] - mod_width - 4 * width
    bias_up = bias_low[:, 3 * width : 3 * width + hidden_width].reshape(layers, tp, 1, -1)
    bias_out = bias_low[:, None, 2 * width : 3 * width]
    bias_down = bias_low[:, None, 3 * width + hidden_width : 4 * width + hidden_width]
    bias_project = [
        pack_bias(bias_low[layer, :width], bias_low[layer, width : 2 * width], tp) for layer in range(layers)
    ]

    by_patch = lambda v: v.reshape(frames, tp * frames, strip, width).transpose(1, 0, 2, 3)
    cot = by_patch(cotangent[0]).reshape(blocks)
    first = clips[0].reshape(1, frames, patches, width)

    attend = lambda layer, weight, stream, stride, *more: attention_forward(
        weight, stream, mod[layer], bias_project[layer], bias_out[layer], stride, *more
    )
    expand = lambda layer, up, down, middle, *more: ffn_forward(
        up, down, middle.reshape(tokens, width), mod[layer], bias_down[layer], bias_up[layer], *more
    )
    if fused:
        attention_a, up_a = begun
        *heads_a, middle_a, up_a, down_a, attention_b = attend(
            0, attention_a, first, 0, [FlowJob([up_a], [shards[1][0]], None, [shards[0][2]])], 1
        )
        hidden_a, pushed_a, second, attention_b, up_b, down_b = expand(
            0, up_a, down_a, middle_a, StreamJob(blocks, frames),
            [FlowJob([attention_b], [shards[1][2]], dp // 8, [shards[1][1]])], 2,
        )
        *heads_b, middle_b, down_b = attend(1, attention_b, second, strip, [FlowJob([down_b], [])], 3)
        hidden_b, pushed_b, result, cot = expand(1, up_b, down_b, middle_b, None, [SwapJob(cot)], 4)
    else:
        (attention_a, up_a, down_a), (attention_b, up_b, down_b) = [[gather_plain(v) for v in group] for group in shards]
        *heads_a, middle_a = attend(0, attention_a, first, 0)
        hidden_a, pushed_a, second = expand(0, up_a, down_a, middle_a)
        second = exchange(by_patch(second).reshape(blocks))
        *heads_b, middle_b = attend(1, attention_b, second, strip)
        hidden_b, pushed_b, result = expand(1, up_b, down_b, middle_b)
        cot = exchange(cot)
    middle_a, middle_b = middle_a.reshape(tokens, width), middle_b.reshape(tokens, width)
    result = result.reshape(blocks)
    cot = cot.reshape(tokens, width)

    if fused:
        ffn_cores = lambda: CoreJob(2, width, ffn_weights.shape[-1])
        head_cores = lambda: CoreJob(1, width, kinds * cols)
        grad, *sums_b, kept, given, result = ffn_backward(
            up_b, down_b, cot, middle_b, pushed_b, hidden_b, mod[1], ffn_cores(), [SwapJob(result)], 5
        )
        ffn_grad = (kept, given)
        *more_b, grad, kept, given, line_up = attention_backward(
            attention_b, grad.reshape(blocks), second, heads_b, mod[1], strip,
            StreamJob(blocks, 0), head_cores(), [ScatterJob([(ffn_grad, 0)], 3 * dp // 8)], 6,
        )
        waiting = [(ffn_grad, 1), ((kept, given), 0)]
        grad, *sums_a, kept, given, done_up, line_b = ffn_backward(
            up_a, down_a, grad.reshape(pieces), middle_a, pushed_a, hidden_a, mod[0], ffn_cores(),
            [LineJob(line_up), ScatterJob(waiting, dp // 4)], 7,
        )
        ffn_grad = (kept, given)
        grad, *more_a, kept, given, done_b, line_ffn_a, done_up_a = attention_backward(
            attention_a, grad.reshape(first.shape), first, heads_a, mod[0], 0, None, head_cores(),
            [LineJob(line_b), ScatterJob([(ffn_grad, 0), (ffn_grad, 1)], dp // 4, True)], 8,
        )
        packed_a = (kept, given)
        done_ffn_b, done_b = jnp.concatenate([done_up, done_b[:1]]), done_b[1:]
    else:
        result = exchange(result)
        grad, *sums_b, ffn_grad = ffn_backward(up_b, down_b, cot, middle_b, pushed_b, hidden_b, mod[1])
        done_ffn_b = scatter_plain(ffn_grad)
        grad, packed_b, *more_b = attention_backward(
            attention_b, grad.reshape(blocks), second, heads_b, mod[1], strip
        )
        done_b = scatter_plain(packed_b[None])
        grad = exchange(grad.astype(jnp.bfloat16))
        grad, *sums_a, ffn_grad = ffn_backward(up_a, down_a, grad.reshape(pieces), middle_a, pushed_a, hidden_a, mod[0])
        done_ffn_a = scatter_plain(ffn_grad)
        grad, packed_a, *more_a = attention_backward(attention_a, grad.reshape(first.shape), first, heads_a, mod[0], 0)
        done_a = scatter_plain(packed_a[None])
    output = result.reshape(pieces).transpose(1, 0, 2, 3).reshape(clips.shape)
    input_grad = grad.reshape(clips.shape)

    def gather_small(more, sums):
        attention_sums, project_sum = more
        up_sum, low_sums = sums
        return jnp.concatenate(
            [*unpack_bias(project_sum), attention_sums[0], up_sum.reshape(-1), low_sums[0],
             attention_sums[1:].reshape(-1), low_sums[1:].reshape(-1)]
        )

    small = jnp.stack([gather_small(more_a, sums_a), gather_small(more_b, sums_b)])
    token_width = small.shape[1] - mod_width
    *done, small, grad_act = leave(
        small.reshape(tp, -1, 128), modulation_low, token_width,
        *((packed_a, line_ffn_a) if fused else (None, None)), 9,
    )
    if fused:
        done_a, done_ffn_a = done[0][None], jnp.concatenate([done_up_a, done[1]])
    small = small.transpose(1, 0, 2, 3).reshape(dp, layers, -1)
    grad_mod_low = small[..., token_width:].astype(jnp.bfloat16)
    grad_bias_all = jnp.concatenate(
        [small[..., :token_width], grad_mod_low.astype(jnp.float32)], axis=-1
    ).sum(axis=0)
    grad_bias = lax.dynamic_slice_in_dim(grad_bias_all, position * bias_cols, bias_cols, axis=1)
    grad_mod_weight = dot32("ck,cle->lke", cond_rows, grad_mod_low)[:, :mod_rows]
    grad_act = lax.dynamic_index_in_dim(
        grad_act[:, :, :mod_rows], lax.axis_index("dp"), axis=1, keepdims=False
    )
    grad_attention = jnp.stack([unpack_heads(done_a[0]), unpack_heads(done_b[0])])
    grad_ffn = jnp.stack([done_ffn_a, done_ffn_b])
    silu_value, silu_pull = jax.vjp(jax.nn.silu, embed)
    cond_grad = silu_pull(grad_act.reshape(1, width))[0]

    return (output, input_grad, cond_grad) + (
        adam_update(attention_weights, attention_first, attention_second, grad_attention, MATRIX_RATE, MATRIX_DECAY)
        + adam_update(ffn_weights, ffn_first, ffn_second, grad_ffn, MATRIX_RATE, MATRIX_DECAY)
        + adam_update(modulation_weights, modulation_first, modulation_second, grad_mod_weight, MATRIX_RATE, MATRIX_DECAY)
        + adam_update(bias_vectors, bias_first, bias_second, grad_bias, VECTOR_RATE, 0.0)
    )


def solution(mesh):
    tokens = P("dp", "tensor", None, None)
    matrix = P(None, None, "dp", "tensor")
    modulation = P(None, BOTH, None)
    vector = P(None, BOTH)
    return jax.shard_map(
        per_device,
        mesh=mesh,
        in_specs=(tokens, tokens, P("dp"), P("dp"), P(), P())
        + (matrix,) * 6 + (modulation,) * 3 + (vector,) * 3,
        out_specs=(tokens, tokens, P("dp", None)) + (matrix,) * 8 + (modulation,) * 4 + (vector,) * 4,
        check_vma=False,
    )
```

```python
from functools import partial

import jax
import jax.numpy as jnp
from jax import lax
from jax.experimental import pallas as pl
from jax.experimental.pallas import tpu as pltpu
from jax.sharding import PartitionSpec as P

HD = 64
PAIR = 128
PARTS = 3
STEP = 10
BETA_ONE = 0.9
BETA_TWO = 0.999
ADAM_EPS = 1e-08
MATRIX_RATE = 0.04
VECTOR_RATE = 0.2
MATRIX_DECAY = 0.1
NORM_EPS = 1e-06
GELU_A = (2.0 / 3.141592653589793) ** 0.5
GELU_B = 0.044715
BLOCKED = -1e30
VMEM_LIMIT = 60 * 1024 * 1024
BOTH = ("dp", "tensor")


def mm(left, right, dims=((1,), (0,))):
    return lax.dot_general(left, right, (dims, ((), ())), preferred_element_type=jnp.float32)


def norm_parts(value):
    average = jnp.mean(value, axis=-1, keepdims=True)
    centred = value - average
    spread = jnp.mean(centred * centred, axis=-1, keepdims=True)
    inverse = lax.rsqrt(spread + NORM_EPS)
    return centred * inverse, inverse


def norm_back(grad, shape, inverse):
    first = jnp.mean(grad, axis=-1, keepdims=True)
    second = jnp.mean(grad * shape, axis=-1, keepdims=True)
    return inverse * (grad - first - shape * second)


def rows_of(ref):
    value = ref[...]
    return value.reshape(-1, value.shape[-1])


def put(ref, value):
    ref[...] = value.reshape(ref.shape).astype(ref.dtype)


def add_rows(ref, index, value):
    ref[pl.ds(index, 1), :] += jnp.sum(value, axis=0, keepdims=True)


def half_masks(rows):
    lane = lax.broadcasted_iota(jnp.int32, (rows, PAIR), 1)
    return lane < HD


def same_patch(tokens, stride):
    row = lax.broadcasted_iota(jnp.int32, (tokens, tokens), 0)
    column = lax.broadcasted_iota(jnp.int32, (tokens, tokens), 1)
    return lax.rem(row, stride) == lax.rem(column, stride)


def swap_halves(value):
    return pltpu.roll(value, HD, 1)


def start_loads(source, target, semaphores):
    for rank in range(target.shape[0]):
        pltpu.make_async_copy(source.at[rank], target.at[rank], semaphores.at[rank]).start()


def wait_loads(target, semaphores, rank):
    pltpu.make_async_copy(target.at[rank], target.at[rank], semaphores.at[rank]).wait()


def softmax_rows(scores, axis):
    raised = jnp.exp(scores - jnp.max(scores, axis=axis, keepdims=True))
    return raised * (1.0 / jnp.sum(raised, axis=axis, keepdims=True))


def attention_forward_kernel(
    stride, hook, source, stream_ref, mod_ref, bias_ref, bias_out_ref,
    project_ref, mixed_ref, branch_ref, middle_ref, weight_ref, semaphores,
):
    ranks = weight_ref.shape[0]

    @pl.when(pl.program_id(0) == 0)
    def _():
        start_loads(source, weight_ref, semaphores)

    stream = rows_of(stream_ref).astype(jnp.float32)
    tokens, width = stream.shape
    shape, _ = norm_parts(stream)
    normed = (shape * (1.0 + mod_ref[1:2]) + mod_ref[0:1]).astype(jnp.bfloat16)
    lower = half_masks(tokens)
    allowed = same_patch(tokens, stride) if stride else None

    @pl.when(pl.program_id(0) == 0)
    def _():
        for rank in range(ranks):
            wait_loads(weight_ref, semaphores, rank)

    def mix(heads):
        scores = [mm(chosen.astype(jnp.bfloat16), key, ((1,), (1,))) for chosen, key, _ in heads]
        outs = []
        for score, (_, _, value) in zip(scores, heads):
            if stride:
                score = jnp.where(allowed, score, BLOCKED)
            outs.append(mm(softmax_rows(score, -1).astype(jnp.bfloat16), value))
        return outs

    branch = None
    for rank in range(ranks):
        hook(rank)
        project = (mm(normed, weight_ref[rank, :, : 5 * PAIR]) + bias_ref[rank]).astype(jnp.bfloat16)
        project_ref[rank] = project.reshape(project_ref.shape[1:])
        query = project[:, :PAIR].astype(jnp.float32) * HD**-0.5
        key, value = project[:, PAIR : 2 * PAIR], project[:, 2 * PAIR : 3 * PAIR]
        both = project[:, 3 * PAIR : 4 * PAIR].astype(jnp.float32)
        first, second, last = mix(
            [
                (jnp.where(lower, query, 0.0), key, value),
                (jnp.where(lower, 0.0, query), key, value),
                (
                    jnp.where(lower, both * HD**-0.5, 0.0),
                    swap_halves(both).astype(jnp.bfloat16),
                    project[:, 4 * PAIR : 5 * PAIR],
                ),
            ]
        )
        mixed = jnp.concatenate(
            [jnp.where(lower, 0.0, swap_halves(last)), jnp.where(lower, first, second)], axis=1
        ).astype(jnp.bfloat16)
        mixed_ref[rank] = mixed.reshape(mixed_ref.shape[1:])
        term = mm(mixed, weight_ref[rank, :, 4 * PAIR :], ((1,), (1,)))
        branch = term if branch is None else branch + term
    branch = branch + bias_out_ref[...]
    put(branch_ref, branch)
    put(middle_ref, stream + mod_ref[2:3] * branch)


def gelu_parts(value):
    square = value * value
    bent = jnp.tanh(value * (GELU_A + (GELU_A * GELU_B) * square))
    half = 0.5 * (1.0 + bent)
    slope = half + (0.5 * value) * (1.0 - bent * bent) * (GELU_A + (3.0 * GELU_A * GELU_B) * square)
    return value * half, slope


def ffn_forward_kernel(
    stream, hook, up_source, down_source, middle_ref, mod_ref, bias_ref, bias_up_ref, hidden_ref, branch_ref, *rest
):
    if stream is None:
        result_ref, *rest = rest
    up_ref, down_ref, up_semaphores, down_semaphores = rest
    step = pl.program_id(0)
    ranks = up_ref.shape[0]

    @pl.when(step == 0)
    def _():
        start_loads(up_source, up_ref, up_semaphores)
        start_loads(down_source, down_ref, down_semaphores)

    middle = middle_ref[...]
    shape, _ = norm_parts(middle)
    second = (shape * (1.0 + mod_ref[4:5]) + mod_ref[3:4]).astype(jnp.bfloat16)

    @pl.when(step == 0)
    def _():
        for rank in range(ranks):
            wait_loads(up_ref, up_semaphores, rank)
            wait_loads(down_ref, down_semaphores, rank)

    down = None
    for rank in range(ranks):
        hook(rank)
        hidden = mm(second, up_ref[rank]) + bias_up_ref[rank]
        hidden_ref[rank] = hidden.astype(jnp.bfloat16)
        active, _ = gelu_parts(hidden)
        part = mm(active.astype(jnp.bfloat16), down_ref[rank], ((1,), (1,)))
        down = part if down is None else down + part
    down = down + bias_ref[...]
    branch_ref[...] = down.astype(jnp.bfloat16)
    result = middle + mod_ref[5:6] * down
    if stream is None:
        result_ref[...] = result.astype(result_ref.dtype)
    else:
        stream.put(step, result)


def load_rows(ref, index, chunk):
    if len(ref.shape) == 2:
        return ref[index * chunk : (index + 1) * chunk, :].astype(jnp.float32)
    blocks, _, strip, width = ref.shape
    frames = chunk // (blocks * strip)
    parts = [ref[:, index * frames + frame].reshape(blocks * strip, width) for frame in range(frames)]
    return jnp.concatenate(parts, axis=0).astype(jnp.float32)


def ffn_backward_kernel(
    split, cores, hook, up_source, down_source, grad_ref, middle_ref, branch_ref, hidden_ref, mod_ref,
    grad_middle_ref, up_sum_ref, sums_ref, *refs
):
    if cores is None:
        weight_grad_ref, *refs = refs
    (up_ref, down_ref, up_semaphores, down_semaphores,
     second_ref, low_ref, low_across_ref, active_ref, slope_ref, total_ref) = refs
    step = pl.program_id(0)
    rank = step if cores is None else cores.rank(step)
    tokens, width = middle_ref.shape
    chunk = tokens // split

    @pl.when(step == 0)
    def _():
        start_loads(up_source, up_ref, up_semaphores)
        start_loads(down_source, down_ref, down_semaphores)
        sums_ref[...] = jnp.zeros_like(sums_ref)
        up_sum_ref[...] = jnp.zeros_like(up_sum_ref)
        for index in range(split):
            rows = slice(index * chunk, (index + 1) * chunk)
            grad = load_rows(grad_ref, index, chunk)
            low = (mod_ref[5:6] * grad).astype(jnp.bfloat16)
            low_ref[rows, :] = low
            low_across_ref[:, rows] = low.T
            add_rows(sums_ref, 0, low.astype(jnp.float32))
            add_rows(sums_ref, 3, grad * branch_ref[rows, :].astype(jnp.float32))
            shape, _ = norm_parts(middle_ref[rows, :])
            second = (shape * (1.0 + mod_ref[4:5]) + mod_ref[3:4]).astype(jnp.bfloat16)
            second_ref[:, rows] = second.T

    wait_loads(up_ref, up_semaphores, rank)
    wait_loads(down_ref, down_semaphores, rank)

    for index in range(split):
        hook(index)
        rows = slice(index * chunk, (index + 1) * chunk)
        active, slope = gelu_parts(hidden_ref[rank, rows, :].astype(jnp.float32))
        active_ref[rows, :] = active.astype(jnp.bfloat16)
        low = (mm(low_ref[rows, :], down_ref[rank]) * slope).astype(jnp.bfloat16)
        slope_ref[rows, :] = low
        up_sum_ref[rank] += jnp.sum(low.astype(jnp.float32), axis=0, keepdims=True)
        part = mm(low, up_ref[rank], ((1,), (1,)))
        total_ref[rows, :] = jnp.where(step == 0, 0.0, total_ref[rows, :]) + part
    hook(2)
    up_made = mm(second_ref[...], slope_ref[...])
    if cores is None:
        weight_grad_ref[0, 0] = up_made.astype(jnp.bfloat16)
    else:
        cores.put(step, 0, up_made)
    hook(3)
    down_made = mm(low_across_ref[...], active_ref[...])
    if cores is None:
        weight_grad_ref[1, 0] = down_made.astype(jnp.bfloat16)
    else:
        cores.put(step, 1, down_made)
        cores.send(step)

    @pl.when(step == pl.num_programs(0) - 1)
    def _():
        for index in range(split):
            rows = slice(index * chunk, (index + 1) * chunk)
            shape, inverse = norm_parts(middle_ref[rows, :])
            grad = total_ref[rows, :]
            add_rows(sums_ref, 1, grad)
            add_rows(sums_ref, 2, grad * shape)
            back = norm_back(grad * (1.0 + mod_ref[4:5]), shape, inverse)
            grad_middle_ref[rows, :] = load_rows(grad_ref, index, chunk) + back


def attention_backward_kernel(
    stride, swap, cores, hook, source, grad_ref, stream_ref, project_ref, mixed_ref, branch_ref, mod_ref, *refs
):
    if swap is None:
        grad_stream_ref, *refs = refs
    if cores is None:
        weight_grad_ref, *refs = refs
    (sums_ref, project_sum_ref,
     weight_ref, semaphores, left_ref, right_ref, outer_ref) = refs
    step = pl.program_id(0)
    ranks = weight_ref.shape[0]

    @pl.when(step == 0)
    def _():
        start_loads(source, weight_ref, semaphores)
        sums_ref[...] = jnp.zeros_like(sums_ref)
        project_sum_ref[...] = jnp.zeros_like(project_sum_ref)

    grad_middle = rows_of(grad_ref)
    tokens, width = grad_middle.shape
    stream = rows_of(stream_ref).astype(jnp.float32)
    shape, inverse = norm_parts(stream)
    rows = pl.ds(pl.multiple_of(step * tokens, tokens), tokens)
    normed = (shape * (1.0 + mod_ref[1:2]) + mod_ref[0:1]).astype(jnp.bfloat16)
    low = (mod_ref[2:3] * grad_middle).astype(jnp.bfloat16)
    left_ref[0, :, rows] = normed.T
    left_ref[1, :, rows] = low.T
    add_rows(sums_ref, 0, low.astype(jnp.float32))
    add_rows(sums_ref, 3, grad_middle * rows_of(branch_ref).astype(jnp.float32))
    lower = half_masks(tokens)
    allowed = same_patch(tokens, stride) if stride else None
    scale = HD**-0.5

    @pl.when(step == 0)
    def _():
        for rank in range(ranks):
            wait_loads(weight_ref, semaphores, rank)

    def score_grads(heads):
        scores = [mm(key, chosen.astype(jnp.bfloat16), ((1,), (1,))) for chosen, key, _, _ in heads]
        grad_probs = [mm(value, taken.astype(jnp.bfloat16), ((1,), (1,))) for _, _, value, taken in heads]
        outs = []
        for score, grad_prob in zip(scores, grad_probs):
            if stride:
                score = jnp.where(allowed, score, BLOCKED)
            probs = softmax_rows(score, 0)
            inner = jnp.sum(grad_prob * probs, axis=0, keepdims=True)
            outs.append((probs.astype(jnp.bfloat16), (probs * (grad_prob - inner)).astype(jnp.bfloat16)))
        return outs

    grad_normed = None
    for rank in range(ranks):
        hook(rank)
        project = project_ref[rank].reshape(tokens, 5 * PAIR)
        mixed = mixed_ref[rank].reshape(tokens, 2 * PAIR)
        outer_ref[rank, rows, :] = mixed
        grad_mixed = mm(low, weight_ref[rank, :, 4 * PAIR :]).astype(jnp.bfloat16)
        query, key, value = (project[:, n * PAIR : (n + 1) * PAIR] for n in range(3))
        query_wide = query.astype(jnp.float32) * scale
        pair = grad_mixed[:, PAIR:]
        pair_wide = pair.astype(jnp.float32)
        both = project[:, 3 * PAIR : 4 * PAIR].astype(jnp.float32)
        swapped = swap_halves(both).astype(jnp.bfloat16)
        single = swap_halves(grad_mixed[:, :PAIR].astype(jnp.float32))
        heads = [
            (jnp.where(keep, query_wide, 0.0), key, value, jnp.where(keep, pair_wide, 0.0)) for keep in (lower, ~lower)
        ]
        heads.append(
            (jnp.where(lower, both * scale, 0.0), swapped, project[:, 4 * PAIR :], jnp.where(lower, single, 0.0))
        )
        solved = score_grads(heads)
        outs = [
            (mm(grad_scores, key, ((0,), (0,))), mm(grad_scores, query), mm(probs, pair))
            for probs, grad_scores in solved[:2]
        ]
        parts = [
            jnp.where(lower, one, two) * factor
            for one, two, factor in zip(outs[0], outs[1], (scale, scale, 1.0))
        ]
        probs, grad_scores = solved[2]
        parts.append(
            jnp.where(lower, mm(grad_scores, swapped, ((0,), (0,))), mm(grad_scores, swapped)) * scale
        )
        parts.append(jnp.where(lower, mm(probs, single.astype(jnp.bfloat16)), 0.0))
        whole = jnp.concatenate(parts, axis=1).astype(jnp.bfloat16)
        right_ref[rank, rows, :] = whole
        add_rows(project_sum_ref, rank, whole.astype(jnp.float32))
        term = mm(whole, weight_ref[rank, :, : 5 * PAIR], ((1,), (1,)))
        grad_normed = term if grad_normed is None else grad_normed + term
    add_rows(sums_ref, 1, grad_normed)
    add_rows(sums_ref, 2, grad_normed * shape)
    back = norm_back(grad_normed * (1.0 + mod_ref[1:2]), shape, inverse)
    if swap is None:
        put(grad_stream_ref, grad_middle + back)
    else:
        swap.put(step, grad_middle + back)

    @pl.when(step == pl.num_programs(0) - 1)
    def _():
        def weights(turn, carry):
            rank = turn if cores is None else cores.rank(turn)
            inside = mm(left_ref[0], right_ref[rank])
            outside = mm(left_ref[1], outer_ref[rank])
            made = jnp.concatenate(
                [inside[:, : 4 * PAIR], inside[:, 4 * PAIR :] + outside[:, :PAIR], outside[:, PAIR:]], axis=1
            )
            if cores is None:
                weight_grad_ref[rank] = made.astype(jnp.bfloat16)
            else:
                cores.put(turn, 0, made)
                cores.send(turn)
            return carry

        lax.fori_loop(0, ranks, weights, 0)


def fixed(shape):
    return pl.BlockSpec(shape, lambda step: (0,) * len(shape), pipeline_mode=pl.Buffered(1))


def cost(flops, moved, raised=0):
    return pl.CostEstimate(flops=int(flops), bytes_accessed=int(moved), transcendentals=int(raised))


def group_spec(shape):
    return pl.BlockSpec((shape[0], 1, shape[2], shape[3]), lambda step: (0, step, 0, 0))


def rank_spec(shape):
    return pl.BlockSpec((shape[0], shape[1], 1) + shape[3:], lambda step: (0, 0, step, 0, 0))


def attention_forward(weight, stream, mod, bias, bias_out, stride, jobs=(), collective_id=None):
    shape = stream.shape
    width = shape[-1]
    ranks = bias.shape[0]
    tokens = shape[0] * shape[1] * shape[2]
    spec = group_spec(shape)
    low = jax.ShapeDtypeStruct(shape, jnp.bfloat16)
    wide = jax.ShapeDtypeStruct(shape, jnp.float32)
    project = jax.ShapeDtypeStruct((ranks,) + shape[:3] + (5 * PAIR,), jnp.bfloat16)
    mixed = jax.ShapeDtypeStruct((ranks,) + shape[:3] + (2 * PAIR,), jnp.bfloat16)
    return call(
        partial(attention_forward_kernel, stride),
        shape[1],
        [weight, stream, mod, bias, bias_out],
        anywhere(1) + [spec, fixed(mod.shape), fixed(bias.shape), fixed(bias_out.shape)],
        [project, mixed, low, wide],
        [rank_spec(project.shape), rank_spec(mixed.shape), spec, spec],
        [pltpu.VMEM((ranks, width, 6 * PAIR), jnp.bfloat16), pltpu.SemaphoreType.DMA((ranks,))],
        jobs,
        collective_id,
        cost(8 * tokens * width * width * 1.5, tokens * width * 16),
        "attention_forward",
    )


def ffn_weights_scratch(ranks, width, part):
    return [
        pltpu.VMEM((ranks, width, part), jnp.bfloat16),
        pltpu.VMEM((ranks, width, part), jnp.bfloat16),
        pltpu.SemaphoreType.DMA((ranks,)),
        pltpu.SemaphoreType.DMA((ranks,)),
    ]


def ffn_forward(up, down, middle, mod, bias_down, bias_up, stream=None, jobs=(), collective_id=None):
    tokens, width = middle.shape
    ranks, _, part = bias_up.shape
    steps = 4
    chunk = tokens // steps
    block = pl.BlockSpec((chunk, width), lambda step: (step, 0))
    result = [jax.ShapeDtypeStruct((tokens, width), jnp.bfloat16)] if stream is None else []
    return call(
        partial(ffn_forward_kernel, stream),
        steps,
        [up, down, middle, mod, bias_down, bias_up],
        anywhere(2) + [block, fixed(mod.shape), fixed(bias_down.shape), fixed(bias_up.shape)],
        [
            jax.ShapeDtypeStruct((ranks, tokens, part), jnp.bfloat16),
            jax.ShapeDtypeStruct((tokens, width), jnp.bfloat16),
        ] + result,
        [pl.BlockSpec((ranks, chunk, part), lambda step: (0, step, 0)), block] + [block] * len(result),
        ffn_weights_scratch(ranks, width, part),
        ([] if stream is None else [stream]) + list(jobs),
        collective_id,
        cost(4.8 * tokens * width * ranks * part, tokens * width * 14, tokens * ranks * part),
        "ffn_forward",
    )


def ffn_backward(up, down, grad, middle, branch, hidden, mod, cores=None, jobs=(), collective_id=None):
    tokens, width = middle.shape
    ranks, _, part = hidden.shape
    whole = fixed((tokens, width))
    made = [jax.ShapeDtypeStruct((2, ranks, width, part), jnp.bfloat16)] if cores is None else []
    return call(
        partial(ffn_backward_kernel, 2, cores),
        ranks,
        [up, down, grad, middle, branch, hidden, mod],
        anywhere(2) + [
            fixed(grad.shape), whole, whole, fixed(hidden.shape), fixed(mod.shape),
        ],
        [
            jax.ShapeDtypeStruct((tokens, width), jnp.float32),
            jax.ShapeDtypeStruct((ranks, 1, part), jnp.float32),
            jax.ShapeDtypeStruct((4, width), jnp.float32),
        ] + made,
        [
            whole,
            fixed((ranks, 1, part)),
            fixed((4, width)),
        ] + [pl.BlockSpec((2, 1, width, part), lambda step: (0, step, 0, 0))] * len(made),
        ffn_weights_scratch(ranks, width, part) + [
            pltpu.VMEM((width, tokens), jnp.bfloat16),
            pltpu.VMEM((tokens, width), jnp.bfloat16),
            pltpu.VMEM((width, tokens), jnp.bfloat16),
            pltpu.VMEM((tokens, part), jnp.bfloat16),
            pltpu.VMEM((tokens, part), jnp.bfloat16),
            pltpu.VMEM((tokens, width), jnp.float32),
        ],
        ([] if cores is None else [cores]) + list(jobs),
        collective_id,
        cost(9.6 * tokens * width * ranks * part, tokens * width * 20, tokens * ranks * part),
        "ffn_backward",
    )


def attention_backward(weight, grad, stream, saved, mod, stride, swap=None, cores=None, jobs=(), collective_id=None):
    project, mixed, branch = saved
    shape = stream.shape
    width = shape[-1]
    ranks = project.shape[0]
    tokens = shape[0] * shape[1] * shape[2]
    spec = group_spec(shape)
    result = [jax.ShapeDtypeStruct(shape, jnp.float32)] if swap is None else []
    made = [jax.ShapeDtypeStruct((ranks, width, 6 * PAIR), jnp.bfloat16)] if cores is None else []
    return call(
        partial(attention_backward_kernel, stride, swap, cores),
        shape[1],
        [weight, grad, stream, project, mixed, branch, mod],
        anywhere(1) + [
            spec, spec, rank_spec(project.shape), rank_spec(mixed.shape), spec, fixed(mod.shape),
        ],
        result + made + [
            jax.ShapeDtypeStruct((4, width), jnp.float32),
            jax.ShapeDtypeStruct((ranks, 5 * PAIR), jnp.float32),
        ],
        [spec] * len(result) + [fixed((ranks, width, 6 * PAIR))] * len(made) + [
            fixed((4, width)), fixed((ranks, 5 * PAIR)),
        ],
        [
            pltpu.VMEM((ranks, width, 6 * PAIR), jnp.bfloat16),
            pltpu.SemaphoreType.DMA((ranks,)),
            pltpu.VMEM((2, width, tokens), jnp.bfloat16),
            pltpu.VMEM((ranks, tokens, 5 * PAIR), jnp.bfloat16),
            pltpu.VMEM((ranks, tokens, 2 * PAIR), jnp.bfloat16),
        ],
        [job for job in (swap, cores) if job is not None] + list(jobs),
        collective_id,
        cost(16 * tokens * width * width * 1.5, tokens * width * 20),
        "attention_backward",
    )


def pack_heads(block):
    query, key, value, outer = block
    return jnp.concatenate(
        [query[:, :PAIR], key[:, :PAIR], value[:, :PAIR], query[:, PAIR:], key[:, PAIR:],
         value[:, PAIR:], outer[:, PAIR:], outer[:, :PAIR]], axis=1
    )


def unpack_heads(packed):
    part = lambda start, size: packed[:, start : start + size]
    join = lambda first, last: jnp.concatenate([part(first, PAIR), part(last, HD)], axis=1)
    return jnp.stack(
        [join(0, 3 * PAIR), join(PAIR, 3 * PAIR + HD), join(2 * PAIR, 4 * PAIR), join(5 * PAIR, 4 * PAIR + HD)]
    )


def pack_bias(query, value, ranks):
    query, value = query.reshape(ranks, -1), value.reshape(ranks, -1)
    none = jnp.zeros((ranks, PAIR), query.dtype)
    return jnp.concatenate(
        [query[:, :PAIR], none, value[:, :PAIR], query[:, PAIR:], none[:, :HD], value[:, PAIR:], none[:, :HD]],
        axis=1,
    )[:, None]


def unpack_bias(sums):
    query = jnp.concatenate([sums[:, :PAIR], sums[:, 3 * PAIR : 3 * PAIR + HD]], axis=1)
    value = jnp.concatenate([sums[:, 2 * PAIR : 3 * PAIR], sums[:, 4 * PAIR : 4 * PAIR + HD]], axis=1)
    return query.reshape(-1), value.reshape(-1)


def place():
    return lax.axis_index("dp"), lax.axis_index("tensor"), lax.axis_size("dp"), lax.axis_size("tensor")


def greet_all():
    device, rank, dp, tp = place()
    me, count = device * tp + rank, dp * tp
    barrier = pltpu.get_barrier_semaphore()

    def greet(index, carry):
        peer = lax.rem(me + index, count)
        pl.semaphore_signal(
            barrier, inc=1, device_id=(peer // tp, lax.rem(peer, tp)), device_id_type=pl.DeviceIdType.MESH
        )
        return carry

    lax.fori_loop(1, count, greet, 0)
    pl.semaphore_wait(barrier, count - 1)


def push(source, target, send, receive, device, rank):
    pltpu.make_async_remote_copy(
        src_ref=source, dst_ref=target, send_sem=send, recv_sem=receive,
        device_id=(device, rank), device_id_type=pl.DeviceIdType.MESH,
    ).start()


def wait_bytes(ref, semaphore):
    pltpu.make_async_copy(ref, ref, semaphore).wait()


class Where:
    def __init__(self):
        device, rank = lax.axis_index("dp"), lax.axis_index("tensor")
        self.count = lax.axis_size("dp") // 2
        self.device, self.rank = device, rank
        self.far, self.side = device // 2, lax.rem(device, 2)
        self.row, self.core = rank // 2, lax.rem(rank, 2)
        self.other_side = self.far * 2 + 1 - self.side
        self.other_row = (1 - self.row) * 2 + self.core
        self.other_core = self.row * 2 + 1 - self.core

    def ahead(self, step):
        return lax.rem(self.far + step, self.count)

    def line(self, step):
        return self.ahead(step) * 2 + self.side


def greet_neighbours(here):
    barrier = pltpu.get_barrier_semaphore()
    peers = [(here.other_side, here.rank), (here.device, here.other_row), (here.device, here.other_core)]
    peers += [(here.line(step), here.rank) for step in range(1, here.count)]
    for peer in peers:
        pl.semaphore_signal(barrier, inc=1, device_id=peer, device_id_type=pl.DeviceIdType.MESH)
    pl.semaphore_wait(barrier, len(peers))


def add_into(target, left, right):
    target[...] = left[...] + right[...]


class ScatterChain:
    def __init__(self, here, kept, line, lead, scratch):
        self.here, self.kept, self.line, self.lead = here, kept, line, lead
        self.keep, self.first_one, self.last_one, self.first_two, self.last_two, self.semaphores = scratch
        self.rows = line.shape[1]

    @staticmethod
    def scratch(width, columns, dp, lead):
        rows, far = width // dp, dp // 2
        low = lambda *shape: pltpu.VMEM(shape + (columns,), jnp.bfloat16)
        return [
            low(2, width),
            low(2, lead, rows), low(2 * (far - lead) * rows), low(lead, rows), low(far - lead, rows),
            pltpu.SemaphoreType.DMA((6, 2)),
        ]

    def chunk(self, row, far, side):
        return self.keep.at[row, pl.ds(pl.multiple_of((far * 2 + side) * self.rows, self.rows), self.rows)]

    def send(self, slot, source, target, device, rank):
        push(source, target, self.semaphores.at[slot, 0], self.semaphores.at[slot, 1], device, rank)

    def arrived(self, slot, ref):
        wait_bytes(ref, self.semaphores.at[slot, 1])

    def left(self, slot, ref):
        wait_bytes(ref, self.semaphores.at[slot, 0])

    def stage_load(self):
        pltpu.make_async_copy(self.kept, self.keep, self.semaphores.at[5, 0]).start()

    def stage_one(self):
        here = self.here
        wait_bytes(self.keep, self.semaphores.at[5, 0])
        for row in range(2):
            for far in range(self.lead):
                self.send(
                    1, self.chunk(row, far, 1 - here.side), self.first_one.at[row, far], here.other_side, here.rank
                )
        start, size = self.lead * 2 * self.rows, (here.count - self.lead) * 2 * self.rows
        self.send(2, self.keep.at[1 - here.row, pl.ds(start, size)], self.last_one, here.device, here.other_row)

    def stage_two(self):
        here, lead = self.here, self.lead
        self.arrived(1, self.first_one)
        for row in range(2):
            for far in range(lead):
                mine = self.chunk(row, far, here.side)
                add_into(mine, mine, self.first_one.at[row, far])
        for far in range(lead):
            self.send(3, self.chunk(1 - here.row, far, here.side), self.first_two.at[far], here.device, here.other_row)
        self.arrived(2, self.last_one)
        for far in range(lead, here.count):
            for side in range(2):
                mine = self.chunk(here.row, far, side)
                add_into(mine, mine, self.last_one.at[pl.ds(((far - lead) * 2 + side) * self.rows, self.rows)])
        for far in range(lead, here.count):
            self.send(
                4, self.chunk(here.row, far, 1 - here.side), self.last_two.at[far - lead], here.other_side, here.rank
            )

    def merge(self):
        here = self.here
        self.arrived(3, self.first_two)
        self.arrived(4, self.last_two)
        for far in range(here.count):
            land = self.first_two.at[far] if far < self.lead else self.last_two.at[far - self.lead]
            add_into(self.line.at[far], self.chunk(here.row, far, here.side), land)

    def finish(self):
        self.left(1, self.first_one)
        self.left(2, self.last_one)
        self.left(3, self.first_two)
        self.left(4, self.last_two)


class LineChain:
    def __init__(self, here, line, out, land, semaphores):
        self.here, self.line, self.out, self.land, self.semaphores = here, line, out, land, semaphores

    @staticmethod
    def scratch(far, rows, columns):
        return [pltpu.VMEM((far - 1, rows, columns), jnp.bfloat16), pltpu.SemaphoreType.DMA((2,))]

    def start(self):
        here = self.here
        for step in range(1, here.count):
            push(
                self.line.at[here.ahead(step)], self.land.at[step - 1], self.semaphores.at[0],
                self.semaphores.at[1], here.line(step), here.rank,
            )

    def finish(self):
        wait_bytes(self.land, self.semaphores.at[1])
        total = self.line[self.here.far].astype(jnp.float32)
        for step in range(1, self.here.count):
            total = total + self.land[step - 1].astype(jnp.float32)
        self.out[...] = total
        wait_bytes(self.land, self.semaphores.at[0])


def leave_kernel(mod_start, *refs):
    refs = list(refs)
    scattering = len(refs) > 10
    kept, begun = (refs.pop(0), refs.pop(0)) if scattering else (None, None)
    small_ref, modulation_ref, *refs = refs
    out, begun_out = (refs.pop(0), refs.pop(0)) if scattering else (None, None)
    sum_ref, act_ref, land_ref, acting_ref, semaphores, *space = refs
    device, rank, dp, tp = place()
    me, count = device * tp + rank, dp * tp
    greet_all()
    if scattering:
        here = Where()
        line_ref, *space = space
        pick = lambda number: [space.pop(0) for _ in range(number)]
        chains, trails = [], []
        for index in range(PARTS):
            size = out.shape[1] // PARTS
            part = pl.ds(index * size, size)
            line = line_ref.at[index]
            chains.append(ScatterChain(here, kept.at[0, :, :, part], line, here.count // 2, pick(6)))
            trails.append(LineChain(here, line, out.at[:, part], *pick(2)))
        others = [LineChain(here, begun.at[kind], begun_out.at[kind], *pick(2)) for kind in range(begun.shape[0])]
        for chain in chains:
            chain.stage_load()
    for step in range(1, tp):
        there = lax.rem(rank + step, tp)
        push(small_ref.at[there], land_ref.at[rank], semaphores.at[0], semaphores.at[1], device, there)
    land_ref[rank] = small_ref[rank]
    wait_bytes(land_ref.at[pl.ds(0, tp - 1)], semaphores.at[1])
    mine = sum_ref.at[rank]
    mine[device] = jnp.sum(land_ref[...], axis=0)

    def one(step, carry):
        push(mine.at[device], mine.at[device], semaphores.at[2], semaphores.at[3], lax.rem(device + step, dp), rank)
        return carry

    lax.fori_loop(1, dp, one, 0)
    if scattering:
        for chain in others:
            chain.start()
    wait_bytes(mine.at[pl.ds(0, dp - 1)], semaphores.at[3])
    for step in range(1, tp):
        push(mine, mine, semaphores.at[4], semaphores.at[5], device, lax.rem(rank + step, tp))
    if scattering:
        for chain in chains:
            chain.stage_one()
        chains[0].stage_two()
    wait_bytes(sum_ref.at[pl.ds(0, tp - 1)], semaphores.at[5])
    layers, padded, columns = modulation_ref.shape
    lines = sum_ref.shape[2]
    total = jnp.zeros((dp, padded), jnp.float32)
    for layer in range(layers):
        for index in range(columns // PAIR):
            line = layer * (tp * lines // layers) + mod_start // PAIR + index
            low = sum_ref[line // lines, :, line % lines, :].astype(jnp.bfloat16)
            total += mm(low, modulation_ref[layer, :, index * PAIR : (index + 1) * PAIR], ((1,), (1,)))
    acting_ref[...] = jnp.concatenate([total, jnp.zeros((dp, PAIR - padded), jnp.float32)], axis=1)
    act_ref[me] = acting_ref[...]

    def tell(index, carry):
        peer = lax.rem(me + index, count)
        push(acting_ref, act_ref.at[me], semaphores.at[6], semaphores.at[7], peer // tp, lax.rem(peer, tp))
        return carry

    lax.fori_loop(1, count, tell, 0)
    if scattering:
        for chain in chains[1:]:
            chain.stage_two()
        for chain, line in zip(chains, trails):
            chain.merge()
            line.start()
        for chain in others:
            chain.finish()
    wait_bytes(act_ref.at[pl.ds(0, count - 1)], semaphores.at[7])
    wait_bytes(act_ref.at[pl.ds(0, count - 1)], semaphores.at[6])
    wait_bytes(land_ref.at[pl.ds(0, tp - 1)], semaphores.at[0])
    wait_bytes(mine.at[pl.ds(0, dp - 1)], semaphores.at[2])
    wait_bytes(sum_ref.at[pl.ds(0, tp - 1)], semaphores.at[4])
    if scattering:
        for chain in chains + trails:
            chain.finish()


def leave(small, modulation, mod_start, kept, begun, collective_id):
    tp, lines, lanes = small.shape
    dp = lax.axis_size("dp")
    inside = pl.BlockSpec(memory_space=pltpu.VMEM)
    shapes, space, extra = [], [], []
    if kept is not None:
        _, _, width, columns = kept.shape
        rows, far, part = width // dp, dp // 2, columns // PARTS
        kinds = begun.shape[0]
        extra = [kept, begun]
        shapes = [
            jax.ShapeDtypeStruct((rows, columns), jnp.float32),
            jax.ShapeDtypeStruct((kinds, rows, columns), jnp.float32),
        ]
        space = [pltpu.VMEM((PARTS, far, rows, part), jnp.bfloat16)]
        for _ in range(PARTS):
            space += ScatterChain.scratch(width, part, dp, far // 2) + LineChain.scratch(far, rows, part)
        space += LineChain.scratch(far, rows, columns) * kinds
    return pl.pallas_call(
        partial(leave_kernel, mod_start),
        in_specs=[pl.BlockSpec(memory_space=pl.ANY), inside][: len(extra)] + [inside, inside],
        out_specs=[inside] * (len(shapes) + 2),
        out_shape=shapes + [
            jax.ShapeDtypeStruct((tp, dp, lines, lanes), jnp.float32),
            jax.ShapeDtypeStruct((dp * tp, dp, lanes), jnp.float32),
        ],
        scratch_shapes=[
            pltpu.VMEM((tp, lines, lanes), jnp.float32),
            pltpu.VMEM((dp, lanes), jnp.float32),
            pltpu.SemaphoreType.DMA((8,)),
        ] + space,
        compiler_params=pltpu.CompilerParams(
            collective_id=collective_id, has_side_effects=True, vmem_limit_bytes=VMEM_LIMIT
        ),
        name="leave",
    )(*extra, small, modulation)


class GatherChain:
    def __init__(self, here, source, out, semaphores, half=None):
        self.here, self.source, self.out, self.semaphores = here, source, out, semaphores
        self.half = here.count // 2 if half is None else half

    @staticmethod
    def scratch():
        return [pltpu.SemaphoreType.DMA((9, 2))]

    def pieces(self, rank, side, first=0, last=None):
        last = self.here.count if last is None else last
        return self.out.at[rank, pl.ds(first, last - first), side]

    def send(self, slot, pieces, device, rank):
        push(pieces, pieces, self.semaphores.at[slot, 0], self.semaphores.at[slot, 1], device, rank)

    def wait(self, slot, way, pieces):
        wait_bytes(self.pieces(0, 0, 0, pieces), self.semaphores.at[slot, way])

    def stage_line(self):
        here = self.here
        mine = self.out.at[here.rank, here.far, here.side]
        pltpu.make_async_copy(self.source, mine, self.semaphores.at[8, 0]).start()
        for step in range(1, here.count):
            push(
                self.source, mine, self.semaphores.at[0, 0], self.semaphores.at[0, 1], here.line(step), here.rank
            )

    def line_arrived(self):
        self.wait(8, 0, 1)
        self.wait(0, 1, self.here.count - 1)

    def line_left(self):
        self.wait(0, 0, self.here.count - 1)

    def stage_near(self):
        here = self.here
        mine = self.pieces(here.rank, here.side)
        self.send(1, mine, here.other_side, here.rank)
        self.send(2, mine, here.device, here.other_row)
        self.send(3, mine, here.device, here.other_core)

    def stage_across(self):
        here, count = self.here, self.here.count
        self.wait(1, 1, count)
        self.send(4, self.pieces(here.rank, 1 - here.side, 0, self.half), here.device, here.other_row)
        self.wait(2, 1, count)
        self.send(5, self.pieces(here.other_row, here.side, self.half, count), here.other_side, here.rank)
        self.send(6, self.pieces(here.rank, 1 - here.side), here.device, here.other_core)
        self.send(7, self.pieces(here.other_row, here.side), here.device, here.other_core)

    def stage_core(self):
        here, count = self.here, self.here.count
        self.wait(4, 1, self.half)
        self.wait(5, 1, count - self.half)
        self.send(8, self.pieces(here.other_row, 1 - here.side), here.device, here.other_core)

    def finish(self):
        count, half = self.here.count, self.half
        for slot in (3, 6, 7, 8):
            self.wait(slot, 1, count)
        for slot, pieces in ((1, count), (2, count), (3, count), (4, half), (5, count - half), (6, count), (7, count)):
            self.wait(slot, 0, pieces)
        self.wait(8, 0, count)


def column_parts(here, source, out, semaphores, half=None):
    size = out.shape[4] // PARTS
    chains = []
    for index, semaphore in enumerate(semaphores):
        part = pl.ds(index * size, size)
        shard = None if source is None else source.at[:, part]
        chains.append(GatherChain(here, shard, out.at[:, :, :, :, part], semaphore, half))
    return chains


class Job:
    operands, sources, shapes, specs, aliases, space = (), None, (), (), {}, ()
    stages, last = {}, ()


def anywhere(count):
    return [pl.BlockSpec(memory_space=pl.ANY)] * count


class CoreJob(Job):
    def __init__(self, kinds, width, columns):
        block = (kinds, width, columns)
        self.shapes, self.specs = [jax.ShapeDtypeStruct((kinds, 2, width, columns), jnp.bfloat16)], anywhere(1)
        self.space = [
            pltpu.VMEM((2,) + block, jnp.bfloat16),
            pltpu.VMEM((2,) + block, jnp.bfloat16),
            pltpu.SemaphoreType.DMA((4,)),
        ]

    def bind(self, here, inputs, outputs, space):
        self.here, self.kept, (self.buffer, self.land, self.semaphores) = here, outputs[0], space
        self.stages = {}
        self.last = [lambda: self.sent(0), lambda: self.sent(1)]

    def sent(self, own):
        wait_bytes(self.buffer.at[own], self.semaphores.at[own])

    def rank(self, turn):
        return turn + (1 - self.here.core) * (1 - 2 * lax.rem(turn, 2))

    def put(self, turn, kind, value):
        row, own = turn // 2, lax.rem(turn, 2)
        if kind == 0:

            @pl.when(turn >= 2)
            def _():
                self.sent(own)

        @pl.when(own == 0)
        def _():
            self.buffer[0, kind] = value.astype(jnp.bfloat16)

        @pl.when(own == 1)
        def _():
            if kind == 0:
                wait_bytes(self.land.at[row], self.semaphores.at[2 + row])
            self.buffer[1, kind] = (value + self.land[row, kind].astype(jnp.float32)).astype(jnp.bfloat16)

    def send(self, turn):
        here, row, own = self.here, turn // 2, lax.rem(turn, 2)

        @pl.when(own == 0)
        def _():
            push(
                self.buffer.at[0], self.land.at[row], self.semaphores.at[0], self.semaphores.at[2 + row],
                here.device, here.other_core,
            )

        @pl.when(own == 1)
        def _():
            pltpu.make_async_copy(self.buffer.at[1], self.kept.at[:, row], self.semaphores.at[1]).start()


class ScatterJob(Job):
    def __init__(self, grads, lead, close=False):
        _, _, width, columns = grads[0][0].shape
        dp = lax.axis_size("dp")
        far, rows = dp // 2, width // dp
        self.lead, self.close, self.kinds = lead, close, [kind for _, kind in grads]
        self.operands = [array for array, _ in grads]
        shape = (len(grads) - close, far, rows, columns)
        self.shapes, self.specs = [jax.ShapeDtypeStruct(shape, jnp.bfloat16)], [fixed(shape)]
        self.space = ScatterChain.scratch(width, columns, dp, lead) * len(grads)
        if close:
            self.shapes.append(jax.ShapeDtypeStruct((1, rows, columns), jnp.float32))
            self.specs.append(fixed((1, rows, columns)))
            self.space = [pltpu.VMEM((far, rows, columns), jnp.bfloat16)] + LineChain.scratch(
                far, rows, columns
            ) + self.space

    def bind(self, here, inputs, outputs, space):
        lines = [outputs[0].at[index] for index in range(outputs[0].shape[0])]
        if self.close:
            own, land, semaphores, *space = space
            lines.insert(0, own)
            line = LineChain(here, own, outputs[1].at[0], land, semaphores)
        size = len(space) // len(inputs)
        chains = [
            ScatterChain(
                here, inputs[index].at[kind], lines[index], self.lead, space[index * size : (index + 1) * size]
            )
            for index, kind in enumerate(self.kinds)
        ]
        one = chains[0]
        if len(chains) == 1:
            self.stages = {(0, 0): [one.stage_load], (0, 1): [one.stage_one], (2, 0): [one.stage_two]}
            self.last = [one.merge, one.finish]
            return
        two = chains[1]
        if self.close:
            self.stages = {
                (0, 0): [one.stage_load, two.stage_load], (0, 1): [one.stage_one],
                (1, 2): [one.stage_two, two.stage_one], (2, 1): [one.merge, line.start], (3, 2): [two.stage_two],
            }
            self.last = [line.finish, two.merge, one.finish, two.finish]
            return
        self.stages = {
            (0, 0): [one.stage_load, two.stage_load], (0, 1): [one.stage_one], (0, 3): [two.stage_one],
            (2, 0): [one.stage_two], (3, 2): [two.stage_two],
        }
        self.last = [one.merge, two.merge, one.finish, two.finish]


class LineJob(Job):
    def __init__(self, line):
        kinds, far, rows, columns = line.shape
        shape = (kinds, rows, columns)
        self.operands, self.sources = [line], [fixed(line.shape)]
        self.shapes, self.specs = [jax.ShapeDtypeStruct(shape, jnp.float32)], [fixed(shape)]
        self.space = LineChain.scratch(far, rows, columns) * kinds

    def bind(self, here, inputs, outputs, space):
        chains = [
            LineChain(here, inputs[0].at[kind], outputs[0].at[kind], *space[2 * kind : 2 * kind + 2])
            for kind in range(outputs[0].shape[0])
        ]
        self.stages = {(0, 0): [chain.start for chain in chains]}
        self.last = [chain.finish for chain in chains]


class FlowJob(Job):
    def __init__(self, spread, lines, half=None, late=()):
        dp, tp = lax.axis_size("dp"), lax.axis_size("tensor")
        self.counts, self.half = (len(spread), len(late)), half
        shards = list(late) + list(lines)
        self.operands = list(spread) + shards
        self.shapes = [jax.ShapeDtypeStruct(v.shape, v.dtype) for v in spread]
        self.shapes += [jax.ShapeDtypeStruct((tp, dp // 2, 2) + v.shape, v.dtype) for v in shards]
        self.specs = anywhere(len(self.shapes))
        self.aliases = {index: index for index in range(len(spread))}
        self.space = GatherChain.scratch() * (PARTS * len(self.shapes))

    def bind(self, here, inputs, outputs, space):
        first, late = self.counts
        chains = [
            column_parts(
                here, inputs[index] if index >= first else None, outputs[index],
                space[index * PARTS : (index + 1) * PARTS], self.half,
            )
            for index in range(len(inputs))
        ]
        spread, late, lines = (
            [chain for group in chosen for chain in group]
            for chosen in (chains[:first], chains[first : first + late], chains[first + late :])
        )
        self.stages = {(0, 0): [chain.stage_near for chain in spread]}
        self.stages[0, 0] += [chain.stage_line for chain in late + lines]
        for index, spot in zip(range(PARTS), ((1, 1), (2, 0), (3, 0))):
            self.stages[spot] = [chain.stage_across for chain in spread[index::PARTS]]
            for chain in late[index::PARTS]:
                self.stages[spot] += [chain.line_arrived, chain.stage_near]
        self.last = [chain.stage_across for chain in late]
        self.last += [chain.stage_core for chain in spread + late]
        self.last += [chain.finish for chain in spread + late]
        self.last += [chain.line_arrived for chain in lines]
        self.last += [chain.line_left for chain in late + lines]


class SwapJob(Job):
    def __init__(self, blocks):
        self.operands = [blocks]
        self.shapes, self.specs = [jax.ShapeDtypeStruct(blocks.shape, blocks.dtype)], anywhere(1)
        self.space = [pltpu.SemaphoreType.DMA((3,))]

    def bind(self, here, inputs, outputs, space):
        source, out, semaphores = inputs[0], outputs[0], space[0]
        ranks = out.shape[0]

        def start():
            pltpu.make_async_copy(source.at[here.rank], out.at[here.rank], semaphores.at[2]).start()
            for step in range(1, ranks):
                there = lax.rem(here.rank + step, ranks)
                push(source.at[there], out.at[here.rank], semaphores.at[0], semaphores.at[1], here.device, there)

        def finish():
            wait_bytes(out.at[0], semaphores.at[2])
            wait_bytes(out.at[pl.ds(0, ranks - 1)], semaphores.at[1])
            wait_bytes(out.at[pl.ds(0, ranks - 1)], semaphores.at[0])

        self.stages, self.last = {(0, 0): [start]}, [finish]


class StreamJob(Job):
    def __init__(self, shape, frames):
        self.shape, self.frames = shape, frames
        self.shapes, self.specs = [jax.ShapeDtypeStruct(shape, jnp.bfloat16)], anywhere(1)
        ranks, groups, rows, width = shape
        block = (groups, ranks, rows, width)
        if frames:
            block = (frames, ranks, groups, rows // frames, width)
        self.space = [pltpu.VMEM(block, jnp.bfloat16), pltpu.SemaphoreType.DMA((3,))]

    def bind(self, here, inputs, outputs, space):
        self.here, self.out = here, outputs[0]
        self.buffer, self.semaphores = space
        ranks = self.shape[0]

        def finish():
            wait_bytes(self.out.at[0], self.semaphores.at[2])
            wait_bytes(self.out.at[pl.ds(0, ranks - 1)], self.semaphores.at[1])
            wait_bytes(self.out.at[pl.ds(0, ranks - 1)], self.semaphores.at[0])

        self.stages, self.last = {}, [finish]

    def put(self, step, value):
        here, ranks = self.here, self.shape[0]
        size = self.buffer.size // self.buffer.shape[0] // value.shape[1]
        if value.shape[0] > size:
            count = value.shape[0] // size
            for index in range(count):
                self.put(step * count + index, value[index * size : (index + 1) * size])
            return
        self.buffer[step] = value.reshape(self.buffer.shape[1:]).astype(jnp.bfloat16)
        if self.frames:
            strip = self.buffer.shape[3]
            target = self.out.at[here.rank, :, pl.ds(pl.multiple_of(step * strip, strip), strip)]
        else:
            target = self.out.at[here.rank, step]
        pltpu.make_async_copy(self.buffer.at[step, here.rank], target, self.semaphores.at[2]).start()
        for ahead in range(1, ranks):
            there = lax.rem(here.rank + ahead, ranks)
            push(
                self.buffer.at[step, there], target, self.semaphores.at[0], self.semaphores.at[1],
                here.device, there,
            )


def greet_jobs(here):
    barrier = pltpu.get_barrier_semaphore()
    ranks = lax.axis_size("tensor")
    peers = [(here.other_side, here.rank)]
    peers += [(here.line(step), here.rank) for step in range(1, here.count)]
    peers += [(here.device, lax.rem(here.rank + step, ranks)) for step in range(1, ranks)]
    for peer in peers:
        pl.semaphore_signal(barrier, inc=1, device_id=peer, device_id_type=pl.DeviceIdType.MESH)
    pl.semaphore_wait(barrier, len(peers))


def call(body, steps, arguments, in_specs, out_shape, out_specs, scratch, jobs, collective_id, estimate, name):
    operands = [v for job in jobs for v in job.operands]
    sources = [v for job in jobs for v in (job.sources or anywhere(len(job.operands)))]
    shapes = [v for job in jobs for v in job.shapes]
    specs = [v for job in jobs for v in job.specs]
    space = [v for job in jobs for v in job.space]
    aliases, before, after = {}, len(arguments), len(out_shape)
    for job in jobs:
        for source, target in job.aliases.items():
            aliases[before + source] = after + target
        before, after = before + len(job.operands), after + len(job.shapes)

    def kernel(*refs):
        refs = list(refs)
        take = lambda number: [refs.pop(0) for _ in range(number)]
        inputs, job_inputs = take(len(arguments)), take(len(operands))
        outputs, job_outputs = take(len(out_shape)), take(len(shapes))
        own, job_space = take(len(scratch)), refs
        step = pl.program_id(0)
        if jobs:
            here = Where()
            for job in jobs:
                pick = lambda pool, number: [pool.pop(0) for _ in range(number)]
                job.bind(
                    here, pick(job_inputs, len(job.operands)), pick(job_outputs, len(job.shapes)),
                    pick(job_space, len(job.space)),
                )

        def hook(spot):
            for index in range(steps):
                todo = [
                    stage
                    for job in jobs
                    for (late, place), stages in sorted(job.stages.items())
                    if (late * 4 + place) * steps // 4 == index * 4 + spot
                    for stage in stages
                ]
                if todo or (jobs and spot == 0 and index == 0):

                    @pl.when(step == index)
                    def _():
                        if index == 0 and spot == 0:
                            greet_jobs(here)
                        for stage in todo:
                            stage()

        hook(0)
        body(lambda spot: hook(spot) if spot else None, *inputs, *outputs, *own)
        if jobs:

            @pl.when(step == steps - 1)
            def _():
                for job in jobs:
                    for stage in job.last:
                        stage()

    more = {"collective_id": collective_id, "has_side_effects": True} if jobs else {}
    return pl.pallas_call(
        kernel,
        grid=(steps,),
        in_specs=list(in_specs) + sources,
        out_specs=list(out_specs) + specs,
        out_shape=list(out_shape) + shapes,
        scratch_shapes=list(scratch) + space,
        input_output_aliases=aliases,
        compiler_params=pltpu.CompilerParams(
            vmem_limit_bytes=VMEM_LIMIT, dimension_semantics=("arbitrary",), **more
        ),
        cost_estimate=estimate,
        name=name,
    )(*arguments, *operands)


def entry_kernel(
    per_device, row_ref, modulation_ref, *refs
):
    gather = 2 if len(refs) > 5 else 0
    refs = list(refs)
    sources = [refs.pop(0) for _ in range(gather)]
    gathered_ref, mod_ref = refs.pop(0), refs.pop(0)
    targets = [refs.pop(0) for _ in range(gather)]
    part_ref, land_ref, semaphores, *space = refs
    device, rank, dp, tp = place()
    me, count = device * tp + rank, dp * tp
    quarter = land_ref.shape[2]
    if gather:
        here = Where()
        parts = column_parts(here, sources[0], targets[0], space[:PARTS])
        following = GatherChain(here, sources[1], targets[1], space[PARTS])
    greet_all()

    def tell(index, carry):
        peer = lax.rem(me + index, count)
        push(
            row_ref, gathered_ref.at[me], semaphores.at[0], semaphores.at[1], peer // tp, lax.rem(peer, tp)
        )
        return carry

    lax.fori_loop(1, count, tell, 0)
    gathered_ref[me] = row_ref[...]
    if gather:
        for chain in parts:
            chain.stage_line()
    wait_bytes(gathered_ref.at[pl.ds(0, count - 1)], semaphores.at[1])
    padded = modulation_ref.shape[1]
    width = dp * tp * per_device
    chosen = jnp.zeros((count, padded), jnp.float32)
    row = lax.broadcasted_iota(jnp.int32, (PAIR, padded), 0)
    column = lax.broadcasted_iota(jnp.int32, (PAIR, padded), 1)
    for index in range(width // PAIR):
        match = (row + index * PAIR == column + me * per_device) & (column < per_device)
        chosen += mm(
            gathered_ref[:, index, :].astype(jnp.bfloat16), jnp.where(match, 1.0, 0.0).astype(jnp.bfloat16)
        )
    clip = lax.broadcasted_iota(jnp.int32, (dp, count), 0)
    member = lax.broadcasted_iota(jnp.int32, (dp, count), 1)
    leaders = jnp.where(member == clip * tp, 1.0, 0.0).astype(jnp.bfloat16)
    rows = mm(leaders, chosen.astype(jnp.bfloat16)).astype(jnp.bfloat16)
    for layer in range(modulation_ref.shape[0]):
        part = mm(rows, modulation_ref[layer])
        size = part.shape[1]
        for index in range(dp):
            part_ref[index, :, layer * size : (layer + 1) * size] = part[index : index + 1]

    def share(index, carry):
        peer = lax.rem(me + index, count)
        there, lane = peer // tp, lax.rem(peer, tp)
        source = part_ref.at[there, :, pl.ds(pl.multiple_of(lane * quarter, PAIR), quarter)]
        push(source, land_ref.at[me], semaphores.at[2], semaphores.at[3], there, lane)
        return carry

    lax.fori_loop(1, count, share, 0)
    mine = pl.ds(pl.multiple_of(rank * quarter, PAIR), quarter)
    land_ref[me] = part_ref[device, :, mine]
    if gather:
        for chain in parts:
            chain.line_arrived()
            chain.stage_near()
        following.stage_line()
    wait_bytes(land_ref.at[pl.ds(0, count - 1)], semaphores.at[3])
    mod_ref[:, mine] = jnp.sum(land_ref[...], axis=0)
    for step in range(1, tp):
        push(
            mod_ref.at[:, mine], mod_ref.at[:, mine], semaphores.at[4], semaphores.at[5],
            device, lax.rem(rank + step, tp),
        )
    if gather:
        for chain in parts:
            chain.stage_across()
        for chain in parts:
            chain.stage_core()
    wait_bytes(gathered_ref.at[pl.ds(0, count - 1)], semaphores.at[0])
    wait_bytes(land_ref.at[pl.ds(0, count - 1)], semaphores.at[2])
    wait_bytes(mod_ref.at[:, pl.ds(0, (tp - 1) * quarter)], semaphores.at[5])
    wait_bytes(mod_ref.at[:, pl.ds(0, (tp - 1) * quarter)], semaphores.at[4])
    if gather:
        following.line_arrived()
        for chain in parts:
            chain.finish()
        for chain in (*parts, following):
            chain.line_left()


def enter(row, modulation, per_device, weights, collective_id):
    dp, tp = lax.axis_size("dp"), lax.axis_size("tensor")
    count = dp * tp
    whole = modulation.shape[0] * modulation.shape[2]
    inside = pl.BlockSpec(memory_space=pltpu.VMEM)
    job = FlowJob((), weights) if weights else Job()
    return pl.pallas_call(
        partial(entry_kernel, per_device),
        in_specs=[inside, inside] + anywhere(len(job.operands)),
        out_specs=[inside, inside] + list(job.specs),
        out_shape=[
            jax.ShapeDtypeStruct((count,) + row.shape, jnp.float32),
            jax.ShapeDtypeStruct((1, whole), jnp.float32),
        ] + list(job.shapes),
        scratch_shapes=[
            pltpu.VMEM((dp, 1, whole), jnp.float32),
            pltpu.VMEM((count, 1, whole // tp), jnp.float32),
            pltpu.SemaphoreType.DMA((6,)),
        ] + (GatherChain.scratch() * (PARTS + 1) if weights else []),
        compiler_params=pltpu.CompilerParams(
            collective_id=collective_id, has_side_effects=True, vmem_limit_bytes=VMEM_LIMIT
        ),
        name="enter",
    )(row, modulation, *job.operands)


def adam_update(weight, first, second, grad, rate, decay):
    first_new = BETA_ONE * first + (1.0 - BETA_ONE) * grad
    second_new = BETA_TWO * second + (1.0 - BETA_TWO) * grad * grad
    corrected = (
        first_new
        / (1.0 - BETA_ONE**STEP)
        / (jnp.sqrt(second_new / (1.0 - BETA_TWO**STEP)) + ADAM_EPS)
    )
    weight_new = weight - rate * (corrected + decay * weight)
    return (weight_new, first_new, second_new, weight_new.astype(jnp.bfloat16))


def dot32(form, left, right):
    return jnp.einsum(form, left, right, preferred_element_type=jnp.float32)


def exchange(blocks):
    return lax.all_to_all(blocks, "tensor", split_axis=0, concat_axis=0, tiled=True)


def gather_plain(shard):
    rows, width = shard.shape
    whole = lax.all_gather(shard, ("tensor", "dp"), axis=0, tiled=True)
    return whole.reshape(-1, lax.axis_size("dp") * rows, width)


def scatter_plain(grads):
    kinds, ranks, width, cols = grads.shape
    flat = grads.reshape(kinds, ranks * width, cols)
    summed = lax.psum_scatter(flat, ("tensor", "dp"), scatter_dimension=1, tiled=True)
    return summed.astype(jnp.float32)


def per_device(
    clips, cotangent, timesteps, labels, time_table, class_table,
    attention_weights, attention_first, attention_second,
    ffn_weights, ffn_first, ffn_second,
    modulation_weights, modulation_first, modulation_second,
    bias_vectors, bias_first, bias_second,
):
    layers, kinds, rows, cols = attention_weights.shape
    _, frames, patches, width = clips.shape
    mod_rows = modulation_weights.shape[1]
    bias_cols = bias_vectors.shape[1]
    dp, tp = lax.axis_size("dp"), lax.axis_size("tensor")
    position = lax.axis_index("dp") * tp + lax.axis_index("tensor")
    tokens = frames * patches
    strip = patches // (tp * frames)
    blocks = (tp, frames, frames * strip, width)
    pieces = (tp * frames, frames, strip, width)

    embed = time_table[timesteps] + class_table[labels]
    cond_act = jax.nn.silu(embed).astype(jnp.bfloat16)
    fused = rows % 16 == 0
    shards = [
        (
            pack_heads(attention_weights[layer].astype(jnp.bfloat16)),
            ffn_weights[layer, 0].astype(jnp.bfloat16),
            ffn_weights[layer, 1].astype(jnp.bfloat16),
        )
        for layer in range(layers)
    ]
    low = bias_vectors.astype(jnp.bfloat16).reshape(-1)
    row = jnp.concatenate([cond_act[0], low]).astype(jnp.float32)
    row = jnp.pad(row, (0, -row.shape[0] % 1024)).reshape(-1, 128)
    modulation_low = modulation_weights.astype(jnp.bfloat16)
    modulation_low = jnp.pad(modulation_low, ((0, 0), (0, -mod_rows % 32), (0, 0)))
    gathered, mod, *begun = enter(row, modulation_low, mod_rows, shards[0][:2] if fused else None, 0)
    gathered = gathered.reshape(dp * tp, -1)
    cond_all = gathered[::tp, :width].astype(jnp.bfloat16)
    bias_low = gathered[:, width : width + layers * bias_cols].reshape(dp * tp, layers, bias_cols)
    bias_low = bias_low.transpose(1, 0, 2).reshape(layers, -1)
    cond_rows = lax.dynamic_slice_in_dim(cond_all, position * mod_rows, mod_rows, axis=1)
    cond_rows = jnp.pad(cond_rows, ((0, 0), (0, -mod_rows % 32)))
    mod = mod.reshape(layers, -1)
    mod_width = mod.shape[-1]
    mod = (mod + bias_low[:, -mod_width:]).reshape(layers, 6, width)
    hidden_width = bias_low.shape[1] - mod_width - 4 * width
    bias_up = bias_low[:, 3 * width : 3 * width + hidden_width].reshape(layers, tp, 1, -1)
    bias_out = bias_low[:, None, 2 * width : 3 * width]
    bias_down = bias_low[:, None, 3 * width + hidden_width : 4 * width + hidden_width]
    bias_project = [
        pack_bias(bias_low[layer, :width], bias_low[layer, width : 2 * width], tp) for layer in range(layers)
    ]

    by_patch = lambda v: v.reshape(frames, tp * frames, strip, width).transpose(1, 0, 2, 3)
    cot = by_patch(cotangent[0]).reshape(blocks)
    first = clips[0].reshape(1, frames, patches, width)

    whole = lambda weight: weight.reshape(tp, width, -1)
    attend = lambda layer, weight, stream, stride, *more: attention_forward(
        whole(weight), stream, mod[layer], bias_project[layer], bias_out[layer], stride, *more
    )
    expand = lambda layer, up, down, middle, *more: ffn_forward(
        whole(up), whole(down), middle.reshape(tokens, width), mod[layer], bias_down[layer], bias_up[layer], *more
    )
    if fused:
        attention_a, up_a = begun
        *heads_a, middle_a, up_a, down_a, attention_b = attend(
            0, attention_a, first, 0, [FlowJob([up_a], [shards[1][0]], None, [shards[0][2]])], 1
        )
        hidden_a, pushed_a, second, attention_b, up_b, down_b = expand(
            0, up_a, down_a, middle_a, StreamJob(blocks, frames),
            [FlowJob([attention_b], [shards[1][2]], dp // 8, [shards[1][1]])], 2,
        )
        *heads_b, middle_b, down_b = attend(1, attention_b, second, strip, [FlowJob([down_b], [])], 3)
        hidden_b, pushed_b, result, cot = expand(1, up_b, down_b, middle_b, None, [SwapJob(cot)], 4)
        attention_a, up_a, down_a = whole(attention_a), whole(up_a), whole(down_a)
        attention_b, up_b, down_b = whole(attention_b), whole(up_b), whole(down_b)
    else:
        (attention_a, up_a, down_a), (attention_b, up_b, down_b) = [[gather_plain(v) for v in group] for group in shards]
        *heads_a, middle_a = attend(0, attention_a, first, 0)
        hidden_a, pushed_a, second = expand(0, up_a, down_a, middle_a)
        second = exchange(by_patch(second).reshape(blocks))
        *heads_b, middle_b = attend(1, attention_b, second, strip)
        hidden_b, pushed_b, result = expand(1, up_b, down_b, middle_b)
        cot = exchange(cot)
    middle_a, middle_b = middle_a.reshape(tokens, width), middle_b.reshape(tokens, width)
    result = result.reshape(blocks)
    cot = cot.reshape(tokens, width)

    if fused:
        ffn_cores = lambda: CoreJob(2, width, ffn_weights.shape[-1])
        head_cores = lambda: CoreJob(1, width, kinds * cols)
        grad, *sums_b, kept, result = ffn_backward(
            up_b, down_b, cot, middle_b, pushed_b, hidden_b, mod[1], ffn_cores(), [SwapJob(result)], 5
        )
        ffn_grad = kept
        *more_b, grad, kept, line_up = attention_backward(
            attention_b, grad.reshape(blocks), second, heads_b, mod[1], strip,
            StreamJob(blocks, 0), head_cores(), [ScatterJob([(ffn_grad, 0)], 3 * dp // 8)], 6,
        )
        waiting = [(ffn_grad, 1), (kept, 0)]
        grad, *sums_a, kept, done_up, line_b = ffn_backward(
            up_a, down_a, grad.reshape(pieces), middle_a, pushed_a, hidden_a, mod[0], ffn_cores(),
            [LineJob(line_up), ScatterJob(waiting, dp // 4)], 7,
        )
        ffn_grad = kept
        grad, *more_a, kept, done_b, line_ffn_a, done_up_a = attention_backward(
            attention_a, grad.reshape(first.shape), first, heads_a, mod[0], 0, None, head_cores(),
            [LineJob(line_b), ScatterJob([(ffn_grad, 0), (ffn_grad, 1)], dp // 4, True)], 8,
        )
        packed_a = kept
        done_ffn_b, done_b = jnp.concatenate([done_up, done_b[:1]]), done_b[1:]
    else:
        result = exchange(result)
        grad, *sums_b, ffn_grad = ffn_backward(up_b, down_b, cot, middle_b, pushed_b, hidden_b, mod[1])
        done_ffn_b = scatter_plain(ffn_grad)
        grad, packed_b, *more_b = attention_backward(
            attention_b, grad.reshape(blocks), second, heads_b, mod[1], strip
        )
        done_b = scatter_plain(packed_b[None])
        grad = exchange(grad.astype(jnp.bfloat16))
        grad, *sums_a, ffn_grad = ffn_backward(up_a, down_a, grad.reshape(pieces), middle_a, pushed_a, hidden_a, mod[0])
        done_ffn_a = scatter_plain(ffn_grad)
        grad, packed_a, *more_a = attention_backward(attention_a, grad.reshape(first.shape), first, heads_a, mod[0], 0)
        done_a = scatter_plain(packed_a[None])
    output = result.reshape(pieces).transpose(1, 0, 2, 3).reshape(clips.shape)
    input_grad = grad.reshape(clips.shape)

    def gather_small(more, sums):
        attention_sums, project_sum = more
        up_sum, low_sums = sums
        return jnp.concatenate(
            [*unpack_bias(project_sum), attention_sums[0], up_sum.reshape(-1), low_sums[0],
             attention_sums[1:].reshape(-1), low_sums[1:].reshape(-1)]
        )

    small = jnp.stack([gather_small(more_a, sums_a), gather_small(more_b, sums_b)])
    token_width = small.shape[1] - mod_width
    *done, small, grad_act = leave(
        small.reshape(tp, -1, 128), modulation_low, token_width,
        *((packed_a, line_ffn_a) if fused else (None, None)), 9,
    )
    if fused:
        done_a, done_ffn_a = done[0][None], jnp.concatenate([done_up_a, done[1]])
    small = small.transpose(1, 0, 2, 3).reshape(dp, layers, -1)
    grad_mod_low = small[..., token_width:].astype(jnp.bfloat16)
    grad_bias_all = jnp.concatenate(
        [small[..., :token_width], grad_mod_low.astype(jnp.float32)], axis=-1
    ).sum(axis=0)
    grad_bias = lax.dynamic_slice_in_dim(grad_bias_all, position * bias_cols, bias_cols, axis=1)
    grad_mod_weight = dot32("ck,cle->lke", cond_rows, grad_mod_low)[:, :mod_rows]
    grad_act = lax.dynamic_index_in_dim(
        grad_act[:, :, :mod_rows], lax.axis_index("dp"), axis=1, keepdims=False
    )
    grad_attention = jnp.stack([unpack_heads(done_a[0]), unpack_heads(done_b[0])])
    grad_ffn = jnp.stack([done_ffn_a, done_ffn_b])
    silu_value, silu_pull = jax.vjp(jax.nn.silu, embed)
    cond_grad = silu_pull(grad_act.reshape(1, width))[0]

    return (output, input_grad, cond_grad) + (
        adam_update(attention_weights, attention_first, attention_second, grad_attention, MATRIX_RATE, MATRIX_DECAY)
        + adam_update(ffn_weights, ffn_first, ffn_second, grad_ffn, MATRIX_RATE, MATRIX_DECAY)
        + adam_update(modulation_weights, modulation_first, modulation_second, grad_mod_weight, MATRIX_RATE, MATRIX_DECAY)
        + adam_update(bias_vectors, bias_first, bias_second, grad_bias, VECTOR_RATE, 0.0)
    )


def solution(mesh):
    tokens = P("dp", "tensor", None, None)
    matrix = P(None, None, "dp", "tensor")
    modulation = P(None, BOTH, None)
    vector = P(None, BOTH)
    return jax.shard_map(
        per_device,
        mesh=mesh,
        in_specs=(tokens, tokens, P("dp"), P("dp"), P(), P())
        + (matrix,) * 6 + (modulation,) * 3 + (vector,) * 3,
        out_specs=(tokens, tokens, P("dp", None)) + (matrix,) * 8 + (modulation,) * 4 + (vector,) * 4,
        check_vma=False,
    )
```

```python
from functools import partial

import jax
import jax.numpy as jnp
from jax import lax
from jax.experimental import pallas as pl
from jax.experimental.pallas import tpu as pltpu
from jax.sharding import PartitionSpec as P

HD = 64
PAIR = 128
PARTS = 3
STEP = 10
BETA_ONE = 0.9
BETA_TWO = 0.999
ADAM_EPS = 1e-08
MATRIX_RATE = 0.04
VECTOR_RATE = 0.2
MATRIX_DECAY = 0.1
NORM_EPS = 1e-06
GELU_A = (2.0 / 3.141592653589793) ** 0.5
GELU_B = 0.044715
BLOCKED = -1e30
VMEM_LIMIT = 60 * 1024 * 1024
BOTH = ("dp", "tensor")


def mm(left, right, dims=((1,), (0,))):
    return lax.dot_general(left, right, (dims, ((), ())), preferred_element_type=jnp.float32)


def norm_parts(value):
    average = jnp.mean(value, axis=-1, keepdims=True)
    centred = value - average
    spread = jnp.mean(centred * centred, axis=-1, keepdims=True)
    inverse = lax.rsqrt(spread + NORM_EPS)
    return centred * inverse, inverse


def norm_back(grad, shape, inverse):
    first = jnp.mean(grad, axis=-1, keepdims=True)
    second = jnp.mean(grad * shape, axis=-1, keepdims=True)
    return inverse * (grad - first - shape * second)


def rows_of(ref):
    value = ref[...]
    return value.reshape(-1, value.shape[-1])


def put(ref, value):
    ref[...] = value.reshape(ref.shape).astype(ref.dtype)


def add_rows(ref, index, value):
    ref[pl.ds(index, 1), :] += jnp.sum(value, axis=0, keepdims=True)


def half_masks(rows):
    lane = lax.broadcasted_iota(jnp.int32, (rows, PAIR), 1)
    return lane < HD


def same_patch(tokens, stride):
    row = lax.broadcasted_iota(jnp.int32, (tokens, tokens), 0)
    column = lax.broadcasted_iota(jnp.int32, (tokens, tokens), 1)
    return lax.rem(row, stride) == lax.rem(column, stride)


def swap_halves(value):
    return pltpu.roll(value, HD, 1)


def start_loads(source, target, semaphores):
    for rank in range(target.shape[0]):
        pltpu.make_async_copy(source.at[rank], target.at[rank], semaphores.at[rank]).start()


def wait_loads(target, semaphores, rank):
    pltpu.make_async_copy(target.at[rank], target.at[rank], semaphores.at[rank]).wait()


def softmax_rows(scores, axis):
    raised = jnp.exp(scores - jnp.max(scores, axis=axis, keepdims=True))
    return raised * (1.0 / jnp.sum(raised, axis=axis, keepdims=True))


def attention_forward_kernel(
    stride, hook, source, stream_ref, mod_ref, bias_ref, bias_out_ref,
    project_ref, mixed_ref, branch_ref, middle_ref, weight_ref, semaphores,
):
    ranks = weight_ref.shape[0]

    @pl.when(pl.program_id(0) == 0)
    def _():
        start_loads(source, weight_ref, semaphores)

    stream = rows_of(stream_ref).astype(jnp.float32)
    tokens, width = stream.shape
    shape, _ = norm_parts(stream)
    normed = (shape * (1.0 + mod_ref[1:2]) + mod_ref[0:1]).astype(jnp.bfloat16)
    lower = half_masks(tokens)
    allowed = same_patch(tokens, stride) if stride else None

    @pl.when(pl.program_id(0) == 0)
    def _():
        for rank in range(ranks):
            wait_loads(weight_ref, semaphores, rank)

    def mix(heads):
        scores = [mm(chosen.astype(jnp.bfloat16), key, ((1,), (1,))) for chosen, key, _ in heads]
        outs = []
        for score, (_, _, value) in zip(scores, heads):
            if stride:
                score = jnp.where(allowed, score, BLOCKED)
            outs.append(mm(softmax_rows(score, -1).astype(jnp.bfloat16), value))
        return outs

    branch = None
    for rank in range(ranks):
        hook(rank)
        project = (mm(normed, weight_ref[rank, :, : 5 * PAIR]) + bias_ref[rank]).astype(jnp.bfloat16)
        project_ref[rank] = project.reshape(project_ref.shape[1:])
        query = project[:, :PAIR].astype(jnp.float32) * HD**-0.5
        key, value = project[:, PAIR : 2 * PAIR], project[:, 2 * PAIR : 3 * PAIR]
        both = project[:, 3 * PAIR : 4 * PAIR].astype(jnp.float32)
        first, second, last = mix(
            [
                (jnp.where(lower, query, 0.0), key, value),
                (jnp.where(lower, 0.0, query), key, value),
                (
                    jnp.where(lower, both * HD**-0.5, 0.0),
                    swap_halves(both).astype(jnp.bfloat16),
                    project[:, 4 * PAIR : 5 * PAIR],
                ),
            ]
        )
        mixed = jnp.concatenate(
            [jnp.where(lower, 0.0, swap_halves(last)), jnp.where(lower, first, second)], axis=1
        ).astype(jnp.bfloat16)
        mixed_ref[rank] = mixed.reshape(mixed_ref.shape[1:])
        term = mm(mixed, weight_ref[rank, :, 4 * PAIR :], ((1,), (1,)))
        branch = term if branch is None else branch + term
    branch = branch + bias_out_ref[...]
    put(branch_ref, branch)
    put(middle_ref, stream + mod_ref[2:3] * branch)


def gelu_parts(value):
    square = value * value
    bent = jnp.tanh(value * (GELU_A + (GELU_A * GELU_B) * square))
    half = 0.5 * (1.0 + bent)
    slope = half + (0.5 * value) * (1.0 - bent * bent) * (GELU_A + (3.0 * GELU_A * GELU_B) * square)
    return value * half, slope


def turn_of(rank):
    core = lax.rem(lax.axis_index("tensor"), 2)
    return rank + (1 - core) * (1 - 2 * (rank % 2))


def ffn_forward_kernel(
    stream, turned, hook, up_source, down_source, middle_ref, mod_ref, bias_ref, bias_up_ref, hidden_ref, branch_ref, *rest
):
    if stream is None:
        result_ref, *rest = rest
    up_ref, down_ref, up_semaphores, down_semaphores = rest
    step = pl.program_id(0)
    ranks = up_ref.shape[0]

    @pl.when(step == 0)
    def _():
        start_loads(up_source, up_ref, up_semaphores)
        start_loads(down_source, down_ref, down_semaphores)

    middle = middle_ref[...]
    shape, _ = norm_parts(middle)
    second = (shape * (1.0 + mod_ref[4:5]) + mod_ref[3:4]).astype(jnp.bfloat16)

    @pl.when(step == 0)
    def _():
        for rank in range(ranks):
            wait_loads(up_ref, up_semaphores, rank)
            wait_loads(down_ref, down_semaphores, rank)

    down = None
    for rank in range(ranks):
        hook(rank)
        hidden = mm(second, up_ref[rank]) + bias_up_ref[rank]
        hidden_ref[turn_of(rank) if turned else rank] = hidden.astype(jnp.bfloat16)
        active, _ = gelu_parts(hidden)
        part = mm(active.astype(jnp.bfloat16), down_ref[rank], ((1,), (1,)))
        down = part if down is None else down + part
    down = down + bias_ref[...]
    branch_ref[...] = down.astype(jnp.bfloat16)
    result = middle + mod_ref[5:6] * down
    if stream is None:
        result_ref[...] = result.astype(result_ref.dtype)
    else:
        stream.put(step, result)


def load_rows(ref, index, chunk):
    if len(ref.shape) == 2:
        return ref[index * chunk : (index + 1) * chunk, :].astype(jnp.float32)
    blocks, _, strip, width = ref.shape
    frames = chunk // (blocks * strip)
    parts = [ref[:, index * frames + frame].reshape(blocks * strip, width) for frame in range(frames)]
    return jnp.concatenate(parts, axis=0).astype(jnp.float32)


def ffn_backward_kernel(
    split, cores, hook, up_source, down_source, grad_ref, middle_ref, branch_ref, hidden_ref, mod_ref,
    grad_middle_ref, up_sum_ref, sums_ref, *refs
):
    if cores is None:
        weight_grad_ref, *refs = refs
    (up_ref, down_ref, up_semaphores, down_semaphores,
     second_ref, low_ref, low_across_ref, active_ref, slope_ref, total_ref) = refs
    step = pl.program_id(0)
    rank = step if cores is None else cores.rank(step)
    tokens, width = middle_ref.shape
    chunk = tokens // split

    @pl.when(step == 0)
    def _():
        start_loads(up_source, up_ref, up_semaphores)
        start_loads(down_source, down_ref, down_semaphores)
        sums_ref[...] = jnp.zeros_like(sums_ref)
        up_sum_ref[...] = jnp.zeros_like(up_sum_ref)
        for index in range(split):
            rows = slice(index * chunk, (index + 1) * chunk)
            grad = load_rows(grad_ref, index, chunk)
            low = (mod_ref[5:6] * grad).astype(jnp.bfloat16)
            low_ref[rows, :] = low
            low_across_ref[:, rows] = low.T
            add_rows(sums_ref, 0, low.astype(jnp.float32))
            add_rows(sums_ref, 3, grad * branch_ref[rows, :].astype(jnp.float32))
            shape, _ = norm_parts(middle_ref[rows, :])
            second = (shape * (1.0 + mod_ref[4:5]) + mod_ref[3:4]).astype(jnp.bfloat16)
            second_ref[:, rows] = second.T

    wait_loads(up_ref, up_semaphores, rank)
    wait_loads(down_ref, down_semaphores, rank)

    for index in range(split):
        hook(index)
        rows = slice(index * chunk, (index + 1) * chunk)
        active, slope = gelu_parts(hidden_ref[0, rows, :].astype(jnp.float32))
        active_ref[rows, :] = active.astype(jnp.bfloat16)
        low = (mm(low_ref[rows, :], down_ref[rank]) * slope).astype(jnp.bfloat16)
        slope_ref[rows, :] = low
        up_sum_ref[rank] += jnp.sum(low.astype(jnp.float32), axis=0, keepdims=True)
        part = mm(low, up_ref[rank], ((1,), (1,)))
        total_ref[rows, :] = jnp.where(step == 0, 0.0, total_ref[rows, :]) + part
    hook(2)
    up_made = mm(second_ref[...], slope_ref[...])
    if cores is None:
        weight_grad_ref[0, 0] = up_made.astype(jnp.bfloat16)
    else:
        cores.put(step, 0, up_made)
        cores.send(step, 0)
    hook(3)
    down_made = mm(low_across_ref[...], active_ref[...])
    if cores is None:
        weight_grad_ref[1, 0] = down_made.astype(jnp.bfloat16)
    else:
        cores.put(step, 1, down_made)
        cores.send(step, 1)

    @pl.when(step == pl.num_programs(0) - 1)
    def _():
        for index in range(split):
            rows = slice(index * chunk, (index + 1) * chunk)
            shape, inverse = norm_parts(middle_ref[rows, :])
            grad = total_ref[rows, :]
            add_rows(sums_ref, 1, grad)
            add_rows(sums_ref, 2, grad * shape)
            back = norm_back(grad * (1.0 + mod_ref[4:5]), shape, inverse)
            grad_middle_ref[rows, :] = load_rows(grad_ref, index, chunk) + back


def attention_backward_kernel(
    stride, swap, cores, hook, source, grad_ref, stream_ref, project_ref, mixed_ref, branch_ref, mod_ref, *refs
):
    if swap is None:
        grad_stream_ref, *refs = refs
    if cores is None:
        weight_grad_ref, *refs = refs
    (sums_ref, project_sum_ref,
     weight_ref, semaphores, left_ref, right_ref, outer_ref) = refs
    step = pl.program_id(0)
    ranks = weight_ref.shape[0]

    @pl.when(step == 0)
    def _():
        start_loads(source, weight_ref, semaphores)
        sums_ref[...] = jnp.zeros_like(sums_ref)
        project_sum_ref[...] = jnp.zeros_like(project_sum_ref)

    grad_middle = rows_of(grad_ref)
    tokens, width = grad_middle.shape
    stream = rows_of(stream_ref).astype(jnp.float32)
    shape, inverse = norm_parts(stream)
    rows = pl.ds(pl.multiple_of(step * tokens, tokens), tokens)
    normed = (shape * (1.0 + mod_ref[1:2]) + mod_ref[0:1]).astype(jnp.bfloat16)
    low = (mod_ref[2:3] * grad_middle).astype(jnp.bfloat16)
    left_ref[0, :, rows] = normed.T
    left_ref[1, :, rows] = low.T
    add_rows(sums_ref, 0, low.astype(jnp.float32))
    add_rows(sums_ref, 3, grad_middle * rows_of(branch_ref).astype(jnp.float32))
    lower = half_masks(tokens)
    allowed = same_patch(tokens, stride) if stride else None
    scale = HD**-0.5

    @pl.when(step == 0)
    def _():
        for rank in range(ranks):
            wait_loads(weight_ref, semaphores, rank)

    def score_grads(heads):
        scores = [mm(key, chosen.astype(jnp.bfloat16), ((1,), (1,))) for chosen, key, _, _ in heads]
        grad_probs = [mm(value, taken.astype(jnp.bfloat16), ((1,), (1,))) for _, _, value, taken in heads]
        outs = []
        for score, grad_prob in zip(scores, grad_probs):
            if stride:
                score = jnp.where(allowed, score, BLOCKED)
            probs = softmax_rows(score, 0)
            inner = jnp.sum(grad_prob * probs, axis=0, keepdims=True)
            outs.append((probs.astype(jnp.bfloat16), (probs * (grad_prob - inner)).astype(jnp.bfloat16)))
        return outs

    grad_normed = None
    for rank in range(ranks):
        hook(rank)
        project = project_ref[rank].reshape(tokens, 5 * PAIR)
        mixed = mixed_ref[rank].reshape(tokens, 2 * PAIR)
        outer_ref[rank, rows, :] = mixed
        grad_mixed = mm(low, weight_ref[rank, :, 4 * PAIR :]).astype(jnp.bfloat16)
        query, key, value = (project[:, n * PAIR : (n + 1) * PAIR] for n in range(3))
        query_wide = query.astype(jnp.float32) * scale
        pair = grad_mixed[:, PAIR:]
        pair_wide = pair.astype(jnp.float32)
        both = project[:, 3 * PAIR : 4 * PAIR].astype(jnp.float32)
        swapped = swap_halves(both).astype(jnp.bfloat16)
        single = swap_halves(grad_mixed[:, :PAIR].astype(jnp.float32))
        heads = [
            (jnp.where(keep, query_wide, 0.0), key, value, jnp.where(keep, pair_wide, 0.0)) for keep in (lower, ~lower)
        ]
        heads.append(
            (jnp.where(lower, both * scale, 0.0), swapped, project[:, 4 * PAIR :], jnp.where(lower, single, 0.0))
        )
        solved = score_grads(heads)
        outs = [
            (mm(grad_scores, key, ((0,), (0,))), mm(grad_scores, query), mm(probs, pair))
            for probs, grad_scores in solved[:2]
        ]
        parts = [
            jnp.where(lower, one, two) * factor
            for one, two, factor in zip(outs[0], outs[1], (scale, scale, 1.0))
        ]
        probs, grad_scores = solved[2]
        parts.append(
            jnp.where(lower, mm(grad_scores, swapped, ((0,), (0,))), mm(grad_scores, swapped)) * scale
        )
        parts.append(jnp.where(lower, mm(probs, single.astype(jnp.bfloat16)), 0.0))
        whole = jnp.concatenate(parts, axis=1).astype(jnp.bfloat16)
        right_ref[rank, rows, :] = whole
        add_rows(project_sum_ref, rank, whole.astype(jnp.float32))
        term = mm(whole, weight_ref[rank, :, : 5 * PAIR], ((1,), (1,)))
        grad_normed = term if grad_normed is None else grad_normed + term
    add_rows(sums_ref, 1, grad_normed)
    add_rows(sums_ref, 2, grad_normed * shape)
    back = norm_back(grad_normed * (1.0 + mod_ref[1:2]), shape, inverse)
    if swap is None:
        put(grad_stream_ref, grad_middle + back)
    else:
        swap.put(step, grad_middle + back)

    @pl.when(step == pl.num_programs(0) - 1)
    def _():
        def weights(turn, carry):
            rank = turn if cores is None else cores.rank(turn)
            inside = mm(left_ref[0], right_ref[rank])
            outside = mm(left_ref[1], outer_ref[rank])
            made = jnp.concatenate(
                [inside[:, : 4 * PAIR], inside[:, 4 * PAIR :] + outside[:, :PAIR], outside[:, PAIR:]], axis=1
            )
            if cores is None:
                weight_grad_ref[rank] = made.astype(jnp.bfloat16)
            else:
                cores.put(turn, 0, made)
                cores.send(turn, 0)
            return carry

        lax.fori_loop(0, ranks, weights, 0)


def fixed(shape):
    return pl.BlockSpec(shape, lambda step: (0,) * len(shape), pipeline_mode=pl.Buffered(1))


def cost(flops, moved, raised=0):
    return pl.CostEstimate(flops=int(flops), bytes_accessed=int(moved), transcendentals=int(raised))


def group_spec(shape):
    return pl.BlockSpec((shape[0], 1, shape[2], shape[3]), lambda step: (0, step, 0, 0))


def rank_spec(shape):
    return pl.BlockSpec((shape[0], shape[1], 1) + shape[3:], lambda step: (0, 0, step, 0, 0))


def attention_forward(weight, stream, mod, bias, bias_out, stride, jobs=(), collective_id=None):
    shape = stream.shape
    width = shape[-1]
    ranks = bias.shape[0]
    tokens = shape[0] * shape[1] * shape[2]
    spec = group_spec(shape)
    low = jax.ShapeDtypeStruct(shape, jnp.bfloat16)
    wide = jax.ShapeDtypeStruct(shape, jnp.float32)
    project = jax.ShapeDtypeStruct((ranks,) + shape[:3] + (5 * PAIR,), jnp.bfloat16)
    mixed = jax.ShapeDtypeStruct((ranks,) + shape[:3] + (2 * PAIR,), jnp.bfloat16)
    return call(
        partial(attention_forward_kernel, stride),
        shape[1],
        [weight, stream, mod, bias, bias_out],
        anywhere(1) + [spec, fixed(mod.shape), fixed(bias.shape), fixed(bias_out.shape)],
        [project, mixed, low, wide],
        [rank_spec(project.shape), rank_spec(mixed.shape), spec, spec],
        [pltpu.VMEM((ranks, width, 6 * PAIR), jnp.bfloat16), pltpu.SemaphoreType.DMA((ranks,))],
        jobs,
        collective_id,
        cost(8 * tokens * width * width * 1.5, tokens * width * 16),
        "attention_forward",
    )


def ffn_weights_scratch(ranks, width, part):
    return [
        pltpu.VMEM((ranks, width, part), jnp.bfloat16),
        pltpu.VMEM((ranks, width, part), jnp.bfloat16),
        pltpu.SemaphoreType.DMA((ranks,)),
        pltpu.SemaphoreType.DMA((ranks,)),
    ]


def ffn_forward(up, down, middle, mod, bias_down, bias_up, stream=None, jobs=(), collective_id=None, turned=False):
    tokens, width = middle.shape
    ranks, _, part = bias_up.shape
    steps = 4
    chunk = tokens // steps
    block = pl.BlockSpec((chunk, width), lambda step: (step, 0))
    result = [jax.ShapeDtypeStruct((tokens, width), jnp.bfloat16)] if stream is None else []
    return call(
        partial(ffn_forward_kernel, stream, turned),
        steps,
        [up, down, middle, mod, bias_down, bias_up],
        anywhere(2) + [block, fixed(mod.shape), fixed(bias_down.shape), fixed(bias_up.shape)],
        [
            jax.ShapeDtypeStruct((ranks, tokens, part), jnp.bfloat16),
            jax.ShapeDtypeStruct((tokens, width), jnp.bfloat16),
        ] + result,
        [pl.BlockSpec((ranks, chunk, part), lambda step: (0, step, 0)), block] + [block] * len(result),
        ffn_weights_scratch(ranks, width, part),
        ([] if stream is None else [stream]) + list(jobs),
        collective_id,
        cost(4.8 * tokens * width * ranks * part, tokens * width * 14, tokens * ranks * part),
        "ffn_forward",
    )


def ffn_backward(up, down, grad, middle, branch, hidden, mod, cores=None, jobs=(), collective_id=None):
    tokens, width = middle.shape
    ranks, _, part = hidden.shape
    whole = fixed((tokens, width))
    made = [jax.ShapeDtypeStruct((2, ranks, width, part), jnp.bfloat16)] if cores is None else []
    return call(
        partial(ffn_backward_kernel, 2, cores),
        ranks,
        [up, down, grad, middle, branch, hidden, mod],
        anywhere(2) + [
            fixed(grad.shape), whole, whole,
            pl.BlockSpec((1, tokens, part), lambda step: (step, 0, 0)),
            fixed(mod.shape),
        ],
        [
            jax.ShapeDtypeStruct((tokens, width), jnp.float32),
            jax.ShapeDtypeStruct((ranks, 1, part), jnp.float32),
            jax.ShapeDtypeStruct((4, width), jnp.float32),
        ] + made,
        [
            whole,
            fixed((ranks, 1, part)),
            fixed((4, width)),
        ] + [pl.BlockSpec((2, 1, width, part), lambda step: (0, step, 0, 0))] * len(made),
        ffn_weights_scratch(ranks, width, part) + [
            pltpu.VMEM((width, tokens), jnp.bfloat16),
            pltpu.VMEM((tokens, width), jnp.bfloat16),
            pltpu.VMEM((width, tokens), jnp.bfloat16),
            pltpu.VMEM((tokens, part), jnp.bfloat16),
            pltpu.VMEM((tokens, part), jnp.bfloat16),
            pltpu.VMEM((tokens, width), jnp.float32),
        ],
        ([] if cores is None else [cores]) + list(jobs),
        collective_id,
        cost(9.6 * tokens * width * ranks * part, tokens * width * 20, tokens * ranks * part),
        "ffn_backward",
    )


def attention_backward(weight, grad, stream, saved, mod, stride, swap=None, cores=None, jobs=(), collective_id=None):
    project, mixed, branch = saved
    shape = stream.shape
    width = shape[-1]
    ranks = project.shape[0]
    tokens = shape[0] * shape[1] * shape[2]
    spec = group_spec(shape)
    result = [jax.ShapeDtypeStruct(shape, jnp.float32)] if swap is None else []
    made = [jax.ShapeDtypeStruct((ranks, width, 6 * PAIR), jnp.bfloat16)] if cores is None else []
    return call(
        partial(attention_backward_kernel, stride, swap, cores),
        shape[1],
        [weight, grad, stream, project, mixed, branch, mod],
        anywhere(1) + [
            spec, spec, rank_spec(project.shape), rank_spec(mixed.shape), spec, fixed(mod.shape),
        ],
        result + made + [
            jax.ShapeDtypeStruct((4, width), jnp.float32),
            jax.ShapeDtypeStruct((ranks, 5 * PAIR), jnp.float32),
        ],
        [spec] * len(result) + [fixed((ranks, width, 6 * PAIR))] * len(made) + [
            fixed((4, width)), fixed((ranks, 5 * PAIR)),
        ],
        [
            pltpu.VMEM((ranks, width, 6 * PAIR), jnp.bfloat16),
            pltpu.SemaphoreType.DMA((ranks,)),
            pltpu.VMEM((2, width, tokens), jnp.bfloat16),
            pltpu.VMEM((ranks, tokens, 5 * PAIR), jnp.bfloat16),
            pltpu.VMEM((ranks, tokens, 2 * PAIR), jnp.bfloat16),
        ],
        [job for job in (swap, cores) if job is not None] + list(jobs),
        collective_id,
        cost(16 * tokens * width * width * 1.5, tokens * width * 20),
        "attention_backward",
    )


def pack_heads(block):
    query, key, value, outer = block
    return jnp.concatenate(
        [query[:, :PAIR], key[:, :PAIR], value[:, :PAIR], query[:, PAIR:], key[:, PAIR:],
         value[:, PAIR:], outer[:, PAIR:], outer[:, :PAIR]], axis=1
    )


def unpack_heads(packed):
    part = lambda start, size: packed[:, start : start + size]
    join = lambda first, last: jnp.concatenate([part(first, PAIR), part(last, HD)], axis=1)
    return [join(0, 3 * PAIR), join(PAIR, 3 * PAIR + HD), join(2 * PAIR, 4 * PAIR), join(5 * PAIR, 4 * PAIR + HD)]


def pack_bias(query, value, ranks):
    query, value = query.reshape(ranks, -1), value.reshape(ranks, -1)
    none = jnp.zeros((ranks, PAIR), query.dtype)
    return jnp.concatenate(
        [query[:, :PAIR], none, value[:, :PAIR], query[:, PAIR:], none[:, :HD], value[:, PAIR:], none[:, :HD]],
        axis=1,
    )[:, None]


def unpack_bias(sums):
    query = jnp.concatenate([sums[:, :PAIR], sums[:, 3 * PAIR : 3 * PAIR + HD]], axis=1)
    value = jnp.concatenate([sums[:, 2 * PAIR : 3 * PAIR], sums[:, 4 * PAIR : 4 * PAIR + HD]], axis=1)
    return query.reshape(-1), value.reshape(-1)


def place():
    return lax.axis_index("dp"), lax.axis_index("tensor"), lax.axis_size("dp"), lax.axis_size("tensor")


def greet_all():
    device, rank, dp, tp = place()
    me, count = device * tp + rank, dp * tp
    barrier = pltpu.get_barrier_semaphore()

    def greet(index, carry):
        peer = lax.rem(me + index, count)
        pl.semaphore_signal(
            barrier, inc=1, device_id=(peer // tp, lax.rem(peer, tp)), device_id_type=pl.DeviceIdType.MESH
        )
        return carry

    lax.fori_loop(1, count, greet, 0)
    pl.semaphore_wait(barrier, count - 1)


def push(source, target, send, receive, device, rank):
    pltpu.make_async_remote_copy(
        src_ref=source, dst_ref=target, send_sem=send, recv_sem=receive,
        device_id=(device, rank), device_id_type=pl.DeviceIdType.MESH,
    ).start()


def wait_bytes(ref, semaphore):
    pltpu.make_async_copy(ref, ref, semaphore).wait()


class Where:
    def __init__(self):
        device, rank = lax.axis_index("dp"), lax.axis_index("tensor")
        self.count = lax.axis_size("dp") // 2
        self.device, self.rank = device, rank
        self.far, self.side = device // 2, lax.rem(device, 2)
        self.row, self.core = rank // 2, lax.rem(rank, 2)
        self.other_side = self.far * 2 + 1 - self.side
        self.other_row = (1 - self.row) * 2 + self.core
        self.other_core = self.row * 2 + 1 - self.core

    def ahead(self, step):
        return lax.rem(self.far + step, self.count)

    def line(self, step):
        return self.ahead(step) * 2 + self.side


def greet_neighbours(here):
    barrier = pltpu.get_barrier_semaphore()
    peers = [(here.other_side, here.rank), (here.device, here.other_row), (here.device, here.other_core)]
    peers += [(here.line(step), here.rank) for step in range(1, here.count)]
    for peer in peers:
        pl.semaphore_signal(barrier, inc=1, device_id=peer, device_id_type=pl.DeviceIdType.MESH)
    pl.semaphore_wait(barrier, len(peers))


def add_into(target, left, right):
    target[...] = left[...] + right[...]


class ScatterChain:
    def __init__(self, here, kept, line, lead, scratch):
        self.here, self.kept, self.line, self.lead = here, kept, line, lead
        self.keep, self.first_one, self.last_one, self.first_two, self.last_two, self.semaphores = scratch
        self.rows = line.shape[1]

    @staticmethod
    def scratch(width, columns, dp, lead):
        rows, far = width // dp, dp // 2
        low = lambda *shape: pltpu.VMEM(shape + (columns,), jnp.bfloat16)
        return [
            low(2, width),
            low(2, lead, rows), low(2 * (far - lead) * rows), low(lead, rows), low(far - lead, rows),
            pltpu.SemaphoreType.DMA((6, 2)),
        ]

    def chunk(self, row, far, side):
        return self.keep.at[row, pl.ds(pl.multiple_of((far * 2 + side) * self.rows, self.rows), self.rows)]

    def send(self, slot, source, target, device, rank):
        push(source, target, self.semaphores.at[slot, 0], self.semaphores.at[slot, 1], device, rank)

    def arrived(self, slot, ref):
        wait_bytes(ref, self.semaphores.at[slot, 1])

    def left(self, slot, ref):
        wait_bytes(ref, self.semaphores.at[slot, 0])

    def stage_one(self):
        here, lead = self.here, self.lead
        pltpu.make_async_copy(self.kept, self.keep, self.semaphores.at[5, 0]).start()
        for row in range(2):
            for far in range(lead):
                rows = pl.ds(pl.multiple_of((far * 2 + 1 - here.side) * self.rows, self.rows), self.rows)
                self.send(1, self.kept.at[row, rows], self.first_one.at[row, far], here.other_side, here.rank)
        start, size = lead * 2 * self.rows, (here.count - lead) * 2 * self.rows
        self.send(2, self.kept.at[1 - here.row, pl.ds(start, size)], self.last_one, here.device, here.other_row)

    def stage_two(self):
        here, lead = self.here, self.lead
        wait_bytes(self.keep, self.semaphores.at[5, 0])
        self.arrived(1, self.first_one)
        for row in range(2):
            for far in range(lead):
                mine = self.chunk(row, far, here.side)
                add_into(mine, mine, self.first_one.at[row, far])
        for far in range(lead):
            self.send(3, self.chunk(1 - here.row, far, here.side), self.first_two.at[far], here.device, here.other_row)
        self.arrived(2, self.last_one)
        for far in range(lead, here.count):
            for side in range(2):
                mine = self.chunk(here.row, far, side)
                add_into(mine, mine, self.last_one.at[pl.ds(((far - lead) * 2 + side) * self.rows, self.rows)])
        for far in range(lead, here.count):
            self.send(
                4, self.chunk(here.row, far, 1 - here.side), self.last_two.at[far - lead], here.other_side, here.rank
            )

    def merge(self):
        here = self.here
        self.arrived(3, self.first_two)
        self.arrived(4, self.last_two)
        for far in range(here.count):
            land = self.first_two.at[far] if far < self.lead else self.last_two.at[far - self.lead]
            add_into(self.line.at[far], self.chunk(here.row, far, here.side), land)

    def finish(self):
        self.left(1, self.first_one)
        self.left(2, self.last_one)
        self.left(3, self.first_two)
        self.left(4, self.last_two)


class LineChain:
    def __init__(self, here, line, out, land, semaphores):
        self.here, self.line, self.out, self.land, self.semaphores = here, line, out, land, semaphores

    @staticmethod
    def scratch(far, rows, columns):
        return [pltpu.VMEM((far - 1, rows, columns), jnp.bfloat16), pltpu.SemaphoreType.DMA((2,))]

    def start(self):
        here = self.here
        for step in range(1, here.count):
            push(
                self.line.at[here.ahead(step)], self.land.at[step - 1], self.semaphores.at[0],
                self.semaphores.at[1], here.line(step), here.rank,
            )

    def finish(self):
        wait_bytes(self.land, self.semaphores.at[1])
        total = self.line[self.here.far].astype(jnp.float32)
        for step in range(1, self.here.count):
            total = total + self.land[step - 1].astype(jnp.float32)
        self.out[...] = total
        wait_bytes(self.land, self.semaphores.at[0])


def leave_kernel(mod_start, *refs):
    refs = list(refs)
    scattering = len(refs) > 10
    kept, begun, *done = [refs.pop(0) for _ in range(6 if scattering else 2)]
    if not scattering:
        refs = [kept, begun] + refs
    small_ref, modulation_ref, *refs = refs
    heads_out, wide_out = (refs.pop(0), refs.pop(0)) if scattering else (None, None)
    sum_ref, act_ref, land_ref, acting_ref, semaphores, *space = refs
    device, rank, dp, tp = place()
    me, count = device * tp + rank, dp * tp
    greet_all()
    if scattering:
        here = Where()
        line_ref, out, *space = space
        pick = lambda number: [space.pop(0) for _ in range(number)]
        chains, trails = [], []
        for index in range(PARTS):
            size = out.shape[1] // PARTS
            part = pl.ds(index * size, size)
            line = line_ref.at[index]
            chains.append(ScatterChain(here, kept.at[0, :, :, part], line, here.count // 2, pick(6)))
            trails.append(LineChain(here, line, out.at[:, part], *pick(2)))
        others = [LineChain(here, begun.at[0], wide_out.at[0, 1], *pick(2))]
        for chain in chains:
            chain.stage_one()
    for step in range(1, tp):
        there = lax.rem(rank + step, tp)
        push(small_ref.at[there], land_ref.at[rank], semaphores.at[0], semaphores.at[1], device, there)
    land_ref[rank] = small_ref[rank]
    wait_bytes(land_ref.at[pl.ds(0, tp - 1)], semaphores.at[1])
    mine = sum_ref.at[rank]
    mine[device] = jnp.sum(land_ref[...], axis=0)

    def one(step, carry):
        push(mine.at[device], mine.at[device], semaphores.at[2], semaphores.at[3], lax.rem(device + step, dp), rank)
        return carry

    lax.fori_loop(1, dp, one, 0)
    if scattering:
        for chain in others:
            chain.start()
    wait_bytes(mine.at[pl.ds(0, dp - 1)], semaphores.at[3])
    for step in range(1, tp):
        push(mine, mine, semaphores.at[4], semaphores.at[5], device, lax.rem(rank + step, tp))
    if scattering:
        chains[0].stage_two()
    wait_bytes(sum_ref.at[pl.ds(0, tp - 1)], semaphores.at[5])
    layers, padded, columns = modulation_ref.shape
    lines = sum_ref.shape[2]
    total = jnp.zeros((dp, padded), jnp.float32)
    for layer in range(layers):
        for index in range(columns // PAIR):
            line = layer * (tp * lines // layers) + mod_start // PAIR + index
            low = sum_ref[line // lines, :, line % lines, :].astype(jnp.bfloat16)
            total += mm(low, modulation_ref[layer, :, index * PAIR : (index + 1) * PAIR], ((1,), (1,)))
    acting_ref[...] = jnp.concatenate([total, jnp.zeros((dp, PAIR - padded), jnp.float32)], axis=1)
    act_ref[me] = acting_ref[...]

    def tell(index, carry):
        peer = lax.rem(me + index, count)
        push(acting_ref, act_ref.at[me], semaphores.at[6], semaphores.at[7], peer // tp, lax.rem(peer, tp))
        return carry

    lax.fori_loop(1, count, tell, 0)
    if scattering:
        for chain in chains[1:]:
            chain.stage_two()
        for chain, line in zip(chains, trails):
            chain.merge()
            line.start()
        for chain in others:
            chain.finish()
    wait_bytes(act_ref.at[pl.ds(0, count - 1)], semaphores.at[7])
    wait_bytes(act_ref.at[pl.ds(0, count - 1)], semaphores.at[6])
    wait_bytes(land_ref.at[pl.ds(0, tp - 1)], semaphores.at[0])
    wait_bytes(mine.at[pl.ds(0, dp - 1)], semaphores.at[2])
    wait_bytes(sum_ref.at[pl.ds(0, tp - 1)], semaphores.at[4])
    if scattering:
        for chain in chains + trails:
            chain.finish()
        up_first, up_last, down_last, heads_last = done
        wide_out[0, 0], wide_out[1, 0], wide_out[1, 1] = up_first[0], up_last[0], down_last[0]
        for layer, packed in enumerate((out[...], heads_last[0])):
            parts = unpack_heads(packed)
            for kind in range(4):
                heads_out[layer, kind] = parts[kind]


def leave(small, modulation, mod_start, kept, begun, done, collective_id):
    tp, lines, lanes = small.shape
    dp = lax.axis_size("dp")
    inside = pl.BlockSpec(memory_space=pltpu.VMEM)
    shapes, space, extra = [], [], []
    if kept is not None:
        _, _, width, columns = kept.shape
        rows, far, part = width // dp, dp // 2, columns // PARTS
        extra = [kept, begun, *done]
        shapes = [
            jax.ShapeDtypeStruct((2, 4, rows, columns // 4), jnp.float32),
            jax.ShapeDtypeStruct((2, 2, rows, columns), jnp.float32),
        ]
        space = [pltpu.VMEM((PARTS, far, rows, part), jnp.bfloat16), pltpu.VMEM((rows, columns), jnp.float32)]
        for _ in range(PARTS):
            space += ScatterChain.scratch(width, part, dp, far // 2) + LineChain.scratch(far, rows, part)
        space += LineChain.scratch(far, rows, columns)
    return pl.pallas_call(
        partial(leave_kernel, mod_start),
        in_specs=([pl.BlockSpec(memory_space=pl.ANY)] + [inside] * 5)[: len(extra)] + [inside, inside],
        out_specs=[inside] * (len(shapes) + 2),
        out_shape=shapes + [
            jax.ShapeDtypeStruct((tp, dp, lines, lanes), jnp.float32),
            jax.ShapeDtypeStruct((dp * tp, dp, lanes), jnp.float32),
        ],
        scratch_shapes=[
            pltpu.VMEM((tp, lines, lanes), jnp.float32),
            pltpu.VMEM((dp, lanes), jnp.float32),
            pltpu.SemaphoreType.DMA((8,)),
        ] + space,
        compiler_params=pltpu.CompilerParams(
            collective_id=collective_id, has_side_effects=True, vmem_limit_bytes=VMEM_LIMIT
        ),
        name="leave",
    )(*extra, small, modulation)


class GatherChain:
    def __init__(self, here, source, out, semaphores, half=None):
        self.here, self.source, self.out, self.semaphores = here, source, out, semaphores
        self.half = here.count // 2 if half is None else half

    @staticmethod
    def scratch():
        return [pltpu.SemaphoreType.DMA((9, 2))]

    def pieces(self, rank, side, first=0, last=None):
        last = self.here.count if last is None else last
        return self.out.at[rank, pl.ds(first, last - first), side]

    def send(self, slot, pieces, device, rank):
        push(pieces, pieces, self.semaphores.at[slot, 0], self.semaphores.at[slot, 1], device, rank)

    def wait(self, slot, way, pieces):
        wait_bytes(self.pieces(0, 0, 0, pieces), self.semaphores.at[slot, way])

    def stage_line(self):
        here = self.here
        mine = self.out.at[here.rank, here.far, here.side]
        pltpu.make_async_copy(self.source, mine, self.semaphores.at[8, 0]).start()
        for step in range(1, here.count):
            push(
                self.source, mine, self.semaphores.at[0, 0], self.semaphores.at[0, 1], here.line(step), here.rank
            )

    def line_arrived(self):
        self.wait(8, 0, 1)
        self.wait(0, 1, self.here.count - 1)

    def line_left(self):
        self.wait(0, 0, self.here.count - 1)

    def stage_near(self):
        here = self.here
        mine = self.pieces(here.rank, here.side)
        self.send(1, mine, here.other_side, here.rank)
        self.send(2, mine, here.device, here.other_row)
        self.send(3, mine, here.device, here.other_core)

    def stage_across(self):
        here, count = self.here, self.here.count
        self.wait(1, 1, count)
        self.send(4, self.pieces(here.rank, 1 - here.side, 0, self.half), here.device, here.other_row)
        self.wait(2, 1, count)
        self.send(5, self.pieces(here.other_row, here.side, self.half, count), here.other_side, here.rank)
        self.send(6, self.pieces(here.rank, 1 - here.side), here.device, here.other_core)
        self.send(7, self.pieces(here.other_row, here.side), here.device, here.other_core)

    def stage_core(self):
        here, count = self.here, self.here.count
        self.wait(4, 1, self.half)
        self.wait(5, 1, count - self.half)
        self.send(8, self.pieces(here.other_row, 1 - here.side), here.device, here.other_core)

    def finish(self):
        count, half = self.here.count, self.half
        for slot in (3, 6, 7, 8):
            self.wait(slot, 1, count)
        for slot, pieces in ((1, count), (2, count), (3, count), (4, half), (5, count - half), (6, count), (7, count)):
            self.wait(slot, 0, pieces)
        self.wait(8, 0, count)


def column_parts(here, source, out, semaphores, half=None):
    size = out.shape[4] // PARTS
    chains = []
    for index, semaphore in enumerate(semaphores):
        part = pl.ds(index * size, size)
        shard = None if source is None else source.at[:, part]
        chains.append(GatherChain(here, shard, out.at[:, :, :, :, part], semaphore, half))
    return chains


class Job:
    operands, sources, shapes, specs, aliases, space = (), None, (), (), {}, ()
    stages, last = {}, ()


def anywhere(count):
    return [pl.BlockSpec(memory_space=pl.ANY)] * count


class CoreJob(Job):
    def __init__(self, kinds, width, columns):
        block = (kinds, width, columns)
        self.shapes, self.specs = [jax.ShapeDtypeStruct((kinds, 2, width, columns), jnp.bfloat16)], anywhere(1)
        self.space = [
            pltpu.VMEM((2,) + block, jnp.bfloat16),
            pltpu.VMEM((2,) + block, jnp.bfloat16),
            pltpu.SemaphoreType.DMA((4, kinds)),
        ]

    def bind(self, here, inputs, outputs, space):
        self.here, self.kept, (self.buffer, self.land, self.semaphores) = here, outputs[0], space
        self.stages = {}
        self.last = [
            partial(self.sent, own, kind) for own in range(2) for kind in range(self.buffer.shape[1])
        ]

    def sent(self, own, kind):
        wait_bytes(self.buffer.at[own, kind], self.semaphores.at[own, kind])

    def rank(self, turn):
        return turn_of(turn)

    def put(self, turn, kind, value):
        row, own = turn // 2, lax.rem(turn, 2)

        @pl.when(turn >= 2)
        def _():
            self.sent(own, kind)

        @pl.when(own == 0)
        def _():
            self.buffer[0, kind] = value.astype(jnp.bfloat16)

        @pl.when(own == 1)
        def _():
            wait_bytes(self.land.at[row, kind], self.semaphores.at[2 + row, kind])
            self.buffer[1, kind] = (value + self.land[row, kind].astype(jnp.float32)).astype(jnp.bfloat16)

    def send(self, turn, kind):
        here, row, own = self.here, turn // 2, lax.rem(turn, 2)

        @pl.when(own == 0)
        def _():
            push(
                self.buffer.at[0, kind], self.land.at[row, kind], self.semaphores.at[0, kind],
                self.semaphores.at[2 + row, kind], here.device, here.other_core,
            )

        @pl.when(own == 1)
        def _():
            pltpu.make_async_copy(
                self.buffer.at[1, kind], self.kept.at[kind, row], self.semaphores.at[1, kind]
            ).start()


class ScatterJob(Job):
    def __init__(self, grads, lead, close=False):
        _, _, width, columns = grads[0][0].shape
        dp = lax.axis_size("dp")
        far, rows = dp // 2, width // dp
        self.lead, self.close, self.kinds = lead, close, [kind for _, kind in grads]
        self.operands = [array for array, _ in grads]
        shape = (len(grads) - close, far, rows, columns)
        self.shapes, self.specs = [jax.ShapeDtypeStruct(shape, jnp.bfloat16)], [fixed(shape)]
        self.space = ScatterChain.scratch(width, columns, dp, lead) * len(grads)
        if close:
            self.shapes.append(jax.ShapeDtypeStruct((1, rows, columns), jnp.float32))
            self.specs.append(fixed((1, rows, columns)))
            self.space = [pltpu.VMEM((far, rows, columns), jnp.bfloat16)] + LineChain.scratch(
                far, rows, columns
            ) + self.space

    def bind(self, here, inputs, outputs, space):
        lines = [outputs[0].at[index] for index in range(outputs[0].shape[0])]
        if self.close:
            own, land, semaphores, *space = space
            lines.insert(0, own)
            line = LineChain(here, own, outputs[1].at[0], land, semaphores)
        size = len(space) // len(inputs)
        chains = [
            ScatterChain(
                here, inputs[index].at[kind], lines[index], self.lead, space[index * size : (index + 1) * size]
            )
            for index, kind in enumerate(self.kinds)
        ]
        one = chains[0]
        if len(chains) == 1:
            self.stages = {(0, 0): [one.stage_one], (2, 0): [one.stage_two]}
            self.last = [one.merge, one.finish]
            return
        two = chains[1]
        if self.close:
            self.stages = {
                (0, 0): [one.stage_one], (1, 2): [one.stage_two], (2, 0): [one.merge, line.start, two.stage_one],
                (3, 2): [two.stage_two],
            }
            self.last = [line.finish, two.merge, one.finish, two.finish]
            return
        self.stages = {
            (0, 0): [one.stage_one, two.stage_one], (1, 3): [one.stage_two], (3, 1): [two.stage_two],
        }
        self.last = [one.merge, two.merge, one.finish, two.finish]


class LineJob(Job):
    def __init__(self, line):
        kinds, far, rows, columns = line.shape
        shape = (kinds, rows, columns)
        self.operands, self.sources = [line], [fixed(line.shape)]
        self.shapes, self.specs = [jax.ShapeDtypeStruct(shape, jnp.float32)], [fixed(shape)]
        self.space = LineChain.scratch(far, rows, columns) * kinds

    def bind(self, here, inputs, outputs, space):
        chains = [
            LineChain(here, inputs[0].at[kind], outputs[0].at[kind], *space[2 * kind : 2 * kind + 2])
            for kind in range(outputs[0].shape[0])
        ]
        self.stages = {(0, 0): [chain.start for chain in chains]}
        self.last = [chain.finish for chain in chains]


class FlowJob(Job):
    def __init__(self, spread, lines, half=None, late=()):
        dp, tp = lax.axis_size("dp"), lax.axis_size("tensor")
        self.counts, self.half = (len(spread), len(late)), half
        shards = list(late) + list(lines)
        self.operands = list(spread) + shards
        self.shapes = [jax.ShapeDtypeStruct(v.shape, v.dtype) for v in spread]
        self.shapes += [jax.ShapeDtypeStruct((tp, dp // 2, 2) + v.shape, v.dtype) for v in shards]
        self.specs = anywhere(len(self.shapes))
        self.aliases = {index: index for index in range(len(spread))}
        self.space = GatherChain.scratch() * (PARTS * len(self.shapes))

    def bind(self, here, inputs, outputs, space):
        first, late = self.counts
        chains = [
            column_parts(
                here, inputs[index] if index >= first else None, outputs[index],
                space[index * PARTS : (index + 1) * PARTS], self.half,
            )
            for index in range(len(inputs))
        ]
        spread, late, lines = (
            [chain for group in chosen for chain in group]
            for chosen in (chains[:first], chains[first : first + late], chains[first + late :])
        )
        self.stages = {(0, 0): [chain.stage_near for chain in spread]}
        self.stages[0, 0] += [chain.stage_line for chain in late + lines]
        for index, spot in zip(range(PARTS), ((1, 1), (2, 0), (3, 0))):
            self.stages[spot] = [chain.stage_across for chain in spread[index::PARTS]]
            for chain in late[index::PARTS]:
                self.stages[spot] += [chain.line_arrived, chain.stage_near]
        self.last = [chain.stage_across for chain in late]
        self.last += [chain.stage_core for chain in spread + late]
        self.last += [chain.finish for chain in spread + late]
        self.last += [chain.line_arrived for chain in lines]
        self.last += [chain.line_left for chain in late + lines]


class SwapJob(Job):
    def __init__(self, tokens, to_frames):
        self.to_frames = to_frames
        self.operands = [tokens]
        shape = tokens.shape
        shape = (shape[2], shape[0], shape[1]) + shape[3:] if to_frames else (shape[1], shape[2], shape[0]) + shape[3:]
        self.shapes, self.specs = [jax.ShapeDtypeStruct(shape, tokens.dtype)], anywhere(1)
        self.space = [pltpu.SemaphoreType.DMA((3,))]

    def bind(self, here, inputs, outputs, space):
        source, out, semaphores = inputs[0], outputs[0], space[0]
        frames, ranks = out.shape[:2] if self.to_frames else (out.shape[2], out.shape[0])
        few = pl.ds(0, ranks - 1)
        most, mine = (out.at[:, few], out.at[:, 0]) if self.to_frames else (out.at[few], out.at[0])

        def ends(frame, there):
            if self.to_frames:
                return source.at[there, :, frame], out.at[frame, here.rank]
            return source.at[frame, there], out.at[here.rank, :, frame]

        def start():
            for frame in range(frames):
                pltpu.make_async_copy(*ends(frame, here.rank), semaphores.at[2]).start()
            for step in range(1, ranks):
                there = lax.rem(here.rank + step, ranks)
                for frame in range(frames):
                    push(*ends(frame, there), semaphores.at[0], semaphores.at[1], here.device, there)

        def finish():
            wait_bytes(mine, semaphores.at[2])
            wait_bytes(most, semaphores.at[1])
            wait_bytes(most, semaphores.at[0])

        self.stages, self.last = {(0, 0): [start]}, [finish]


class StreamJob(Job):
    def __init__(self, shape, frames):
        self.shape, self.frames = shape, frames
        self.shapes, self.specs = [jax.ShapeDtypeStruct(shape, jnp.bfloat16)], anywhere(1)
        ranks, groups, rows, width = shape
        block = (groups, ranks, rows, width)
        if frames:
            block = (frames, ranks, groups, rows // frames, width)
        self.space = [pltpu.VMEM(block, jnp.bfloat16), pltpu.SemaphoreType.DMA((3,))]

    def bind(self, here, inputs, outputs, space):
        self.here, self.out = here, outputs[0]
        self.buffer, self.semaphores = space
        ranks = self.shape[0]

        def finish():
            wait_bytes(self.out.at[0], self.semaphores.at[2])
            wait_bytes(self.out.at[pl.ds(0, ranks - 1)], self.semaphores.at[1])
            wait_bytes(self.out.at[pl.ds(0, ranks - 1)], self.semaphores.at[0])

        self.stages, self.last = {}, [finish]

    def put(self, step, value):
        here, ranks = self.here, self.shape[0]
        size = self.buffer.size // self.buffer.shape[0] // value.shape[1]
        if value.shape[0] > size:
            count = value.shape[0] // size
            for index in range(count):
                self.put(step * count + index, value[index * size : (index + 1) * size])
            return
        self.buffer[step] = value.reshape(self.buffer.shape[1:]).astype(jnp.bfloat16)
        if self.frames:
            strip = self.buffer.shape[3]
            target = self.out.at[here.rank, :, pl.ds(pl.multiple_of(step * strip, strip), strip)]
        else:
            target = self.out.at[here.rank, step]
        pltpu.make_async_copy(self.buffer.at[step, here.rank], target, self.semaphores.at[2]).start()
        for ahead in range(1, ranks):
            there = lax.rem(here.rank + ahead, ranks)
            push(
                self.buffer.at[step, there], target, self.semaphores.at[0], self.semaphores.at[1],
                here.device, there,
            )


def greet_jobs(here):
    barrier = pltpu.get_barrier_semaphore()
    ranks = lax.axis_size("tensor")
    peers = [(here.other_side, here.rank)]
    peers += [(here.line(step), here.rank) for step in range(1, here.count)]
    peers += [(here.device, lax.rem(here.rank + step, ranks)) for step in range(1, ranks)]
    for peer in peers:
        pl.semaphore_signal(barrier, inc=1, device_id=peer, device_id_type=pl.DeviceIdType.MESH)
    pl.semaphore_wait(barrier, len(peers))


def call(body, steps, arguments, in_specs, out_shape, out_specs, scratch, jobs, collective_id, estimate, name):
    operands = [v for job in jobs for v in job.operands]
    sources = [v for job in jobs for v in (job.sources or anywhere(len(job.operands)))]
    shapes = [v for job in jobs for v in job.shapes]
    specs = [v for job in jobs for v in job.specs]
    space = [v for job in jobs for v in job.space]
    aliases, before, after = {}, len(arguments), len(out_shape)
    for job in jobs:
        for source, target in job.aliases.items():
            aliases[before + source] = after + target
        before, after = before + len(job.operands), after + len(job.shapes)

    def kernel(*refs):
        refs = list(refs)
        take = lambda number: [refs.pop(0) for _ in range(number)]
        inputs, job_inputs = take(len(arguments)), take(len(operands))
        outputs, job_outputs = take(len(out_shape)), take(len(shapes))
        own, job_space = take(len(scratch)), refs
        step = pl.program_id(0)
        if jobs:
            here = Where()
            for job in jobs:
                pick = lambda pool, number: [pool.pop(0) for _ in range(number)]
                job.bind(
                    here, pick(job_inputs, len(job.operands)), pick(job_outputs, len(job.shapes)),
                    pick(job_space, len(job.space)),
                )

        def hook(spot):
            for index in range(steps):
                todo = [
                    stage
                    for job in jobs
                    for (late, place), stages in sorted(job.stages.items())
                    if (late * 4 + place) * steps // 4 == index * 4 + spot
                    for stage in stages
                ]
                if todo or (jobs and spot == 0 and index == 0):

                    @pl.when(step == index)
                    def _():
                        if index == 0 and spot == 0:
                            greet_jobs(here)
                        for stage in todo:
                            stage()

        hook(0)
        body(lambda spot: hook(spot) if spot else None, *inputs, *outputs, *own)
        if jobs:

            @pl.when(step == steps - 1)
            def _():
                for job in jobs:
                    for stage in job.last:
                        stage()

    more = {"collective_id": collective_id, "has_side_effects": True} if jobs else {}
    return pl.pallas_call(
        kernel,
        grid=(steps,),
        in_specs=list(in_specs) + sources,
        out_specs=list(out_specs) + specs,
        out_shape=list(out_shape) + shapes,
        scratch_shapes=list(scratch) + space,
        input_output_aliases=aliases,
        compiler_params=pltpu.CompilerParams(
            vmem_limit_bytes=VMEM_LIMIT, dimension_semantics=("arbitrary",), **more
        ),
        cost_estimate=estimate,
        name=name,
    )(*arguments, *operands)


def entry_kernel(
    per_device, row_ref, modulation_ref, *refs
):
    gather = 2 if len(refs) > 5 else 0
    refs = list(refs)
    sources = [refs.pop(0) for _ in range(gather)]
    gathered_ref, mod_ref = refs.pop(0), refs.pop(0)
    targets = [refs.pop(0) for _ in range(gather)]
    part_ref, land_ref, semaphores, *space = refs
    device, rank, dp, tp = place()
    me, count = device * tp + rank, dp * tp
    quarter = land_ref.shape[2]
    if gather:
        here = Where()
        parts = column_parts(here, sources[0], targets[0], space[:PARTS])
        following = GatherChain(here, sources[1], targets[1], space[PARTS])
    greet_all()

    def tell(index, carry):
        peer = lax.rem(me + index, count)
        push(
            row_ref, gathered_ref.at[me], semaphores.at[0], semaphores.at[1], peer // tp, lax.rem(peer, tp)
        )
        return carry

    lax.fori_loop(1, count, tell, 0)
    gathered_ref[me] = row_ref[...]
    if gather:
        for chain in parts:
            chain.stage_line()
    wait_bytes(gathered_ref.at[pl.ds(0, count - 1)], semaphores.at[1])
    padded = modulation_ref.shape[1]
    width = dp * tp * per_device
    chosen = jnp.zeros((count, padded), jnp.float32)
    row = lax.broadcasted_iota(jnp.int32, (PAIR, padded), 0)
    column = lax.broadcasted_iota(jnp.int32, (PAIR, padded), 1)
    for index in range(width // PAIR):
        match = (row + index * PAIR == column + me * per_device) & (column < per_device)
        chosen += mm(
            gathered_ref[:, index, :].astype(jnp.bfloat16), jnp.where(match, 1.0, 0.0).astype(jnp.bfloat16)
        )
    clip = lax.broadcasted_iota(jnp.int32, (dp, count), 0)
    member = lax.broadcasted_iota(jnp.int32, (dp, count), 1)
    leaders = jnp.where(member == clip * tp, 1.0, 0.0).astype(jnp.bfloat16)
    rows = mm(leaders, chosen.astype(jnp.bfloat16)).astype(jnp.bfloat16)
    for layer in range(modulation_ref.shape[0]):
        part = mm(rows, modulation_ref[layer])
        size = part.shape[1]
        for index in range(dp):
            part_ref[index, :, layer * size : (layer + 1) * size] = part[index : index + 1]

    def share(index, carry):
        peer = lax.rem(me + index, count)
        there, lane = peer // tp, lax.rem(peer, tp)
        source = part_ref.at[there, :, pl.ds(pl.multiple_of(lane * quarter, PAIR), quarter)]
        push(source, land_ref.at[me], semaphores.at[2], semaphores.at[3], there, lane)
        return carry

    lax.fori_loop(1, count, share, 0)
    mine = pl.ds(pl.multiple_of(rank * quarter, PAIR), quarter)
    land_ref[me] = part_ref[device, :, mine]
    if gather:
        for chain in parts:
            chain.line_arrived()
            chain.stage_near()
        following.stage_line()
    wait_bytes(land_ref.at[pl.ds(0, count - 1)], semaphores.at[3])
    mod_ref[:, mine] = jnp.sum(land_ref[...], axis=0)
    for step in range(1, tp):
        push(
            mod_ref.at[:, mine], mod_ref.at[:, mine], semaphores.at[4], semaphores.at[5],
            device, lax.rem(rank + step, tp),
        )
    if gather:
        for chain in parts:
            chain.stage_across()
        for chain in parts:
            chain.stage_core()
    wait_bytes(gathered_ref.at[pl.ds(0, count - 1)], semaphores.at[0])
    wait_bytes(land_ref.at[pl.ds(0, count - 1)], semaphores.at[2])
    wait_bytes(mod_ref.at[:, pl.ds(0, (tp - 1) * quarter)], semaphores.at[5])
    wait_bytes(mod_ref.at[:, pl.ds(0, (tp - 1) * quarter)], semaphores.at[4])
    if gather:
        following.line_arrived()
        for chain in parts:
            chain.finish()
        for chain in (*parts, following):
            chain.line_left()


def enter(row, modulation, per_device, weights, collective_id):
    dp, tp = lax.axis_size("dp"), lax.axis_size("tensor")
    count = dp * tp
    whole = modulation.shape[0] * modulation.shape[2]
    inside = pl.BlockSpec(memory_space=pltpu.VMEM)
    job = FlowJob((), weights) if weights else Job()
    return pl.pallas_call(
        partial(entry_kernel, per_device),
        in_specs=[inside, inside] + anywhere(len(job.operands)),
        out_specs=[inside, inside] + list(job.specs),
        out_shape=[
            jax.ShapeDtypeStruct((count,) + row.shape, jnp.float32),
            jax.ShapeDtypeStruct((1, whole), jnp.float32),
        ] + list(job.shapes),
        scratch_shapes=[
            pltpu.VMEM((dp, 1, whole), jnp.float32),
            pltpu.VMEM((count, 1, whole // tp), jnp.float32),
            pltpu.SemaphoreType.DMA((6,)),
        ] + (GatherChain.scratch() * (PARTS + 1) if weights else []),
        compiler_params=pltpu.CompilerParams(
            collective_id=collective_id, has_side_effects=True, vmem_limit_bytes=VMEM_LIMIT
        ),
        name="enter",
    )(row, modulation, *job.operands)


def adam_update(weight, first, second, grad, rate, decay):
    first_new = BETA_ONE * first + (1.0 - BETA_ONE) * grad
    second_new = BETA_TWO * second + (1.0 - BETA_TWO) * grad * grad
    corrected = (
        first_new
        / (1.0 - BETA_ONE**STEP)
        / (jnp.sqrt(second_new / (1.0 - BETA_TWO**STEP)) + ADAM_EPS)
    )
    weight_new = weight - rate * (corrected + decay * weight)
    return (weight_new, first_new, second_new, weight_new.astype(jnp.bfloat16))


def dot32(form, left, right):
    return jnp.einsum(form, left, right, preferred_element_type=jnp.float32)


def exchange(blocks):
    return lax.all_to_all(blocks, "tensor", split_axis=0, concat_axis=0, tiled=True)


def gather_plain(shard):
    rows, width = shard.shape
    whole = lax.all_gather(shard, ("tensor", "dp"), axis=0, tiled=True)
    return whole.reshape(-1, lax.axis_size("dp") * rows, width)


def scatter_plain(grads):
    kinds, ranks, width, cols = grads.shape
    flat = grads.reshape(kinds, ranks * width, cols)
    summed = lax.psum_scatter(flat, ("tensor", "dp"), scatter_dimension=1, tiled=True)
    return summed.astype(jnp.float32)


def per_device(
    clips, cotangent, timesteps, labels, time_table, class_table,
    attention_weights, attention_first, attention_second,
    ffn_weights, ffn_first, ffn_second,
    modulation_weights, modulation_first, modulation_second,
    bias_vectors, bias_first, bias_second,
):
    layers, kinds, rows, cols = attention_weights.shape
    _, frames, patches, width = clips.shape
    mod_rows = modulation_weights.shape[1]
    bias_cols = bias_vectors.shape[1]
    dp, tp = lax.axis_size("dp"), lax.axis_size("tensor")
    position = lax.axis_index("dp") * tp + lax.axis_index("tensor")
    tokens = frames * patches
    strip = patches // (tp * frames)
    blocks = (tp, frames, frames * strip, width)
    pieces = (tp * frames, frames, strip, width)

    embed = time_table[timesteps] + class_table[labels]
    cond_act = jax.nn.silu(embed).astype(jnp.bfloat16)
    fused = rows % 16 == 0
    shards = [
        (
            pack_heads(attention_weights[layer].astype(jnp.bfloat16)),
            ffn_weights[layer, 0].astype(jnp.bfloat16),
            ffn_weights[layer, 1].astype(jnp.bfloat16),
        )
        for layer in range(layers)
    ]
    low = bias_vectors.astype(jnp.bfloat16).reshape(-1)
    row = jnp.concatenate([cond_act[0], low]).astype(jnp.float32)
    row = jnp.pad(row, (0, -row.shape[0] % 1024)).reshape(-1, 128)
    modulation_low = modulation_weights.astype(jnp.bfloat16)
    modulation_low = jnp.pad(modulation_low, ((0, 0), (0, -mod_rows % 32), (0, 0)))
    gathered, mod, *begun = enter(row, modulation_low, mod_rows, shards[0][:2] if fused else None, 0)
    gathered = gathered.reshape(dp * tp, -1)
    cond_all = gathered[::tp, :width].astype(jnp.bfloat16)
    bias_low = gathered[:, width : width + layers * bias_cols].reshape(dp * tp, layers, bias_cols)
    bias_low = bias_low.transpose(1, 0, 2).reshape(layers, -1)
    cond_rows = lax.dynamic_slice_in_dim(cond_all, position * mod_rows, mod_rows, axis=1)
    cond_rows = jnp.pad(cond_rows, ((0, 0), (0, -mod_rows % 32)))
    mod = mod.reshape(layers, -1)
    mod_width = mod.shape[-1]
    mod = (mod + bias_low[:, -mod_width:]).reshape(layers, 6, width)
    hidden_width = bias_low.shape[1] - mod_width - 4 * width
    bias_up = bias_low[:, 3 * width : 3 * width + hidden_width].reshape(layers, tp, 1, -1)
    bias_out = bias_low[:, None, 2 * width : 3 * width]
    bias_down = bias_low[:, None, 3 * width + hidden_width : 4 * width + hidden_width]
    bias_project = [
        pack_bias(bias_low[layer, :width], bias_low[layer, width : 2 * width], tp) for layer in range(layers)
    ]

    by_patch = lambda v: v.reshape(frames, tp * frames, strip, width).transpose(1, 0, 2, 3)
    first = clips[0].reshape(1, frames, patches, width)

    whole = lambda weight: weight.reshape(tp, width, -1)
    attend = lambda layer, weight, stream, stride, *more: attention_forward(
        whole(weight), stream, mod[layer], bias_project[layer], bias_out[layer], stride, *more
    )
    expand = lambda layer, up, down, middle, *more: ffn_forward(
        whole(up), whole(down), middle.reshape(tokens, width), mod[layer], bias_down[layer], bias_up[layer], *more
    )
    if fused:
        attention_a, up_a = begun
        *heads_a, middle_a, up_a, down_a, attention_b = attend(
            0, attention_a, first, 0, [FlowJob([up_a], [shards[1][0]], None, [shards[0][2]])], 1
        )
        hidden_a, pushed_a, second, attention_b, up_b, down_b = expand(
            0, up_a, down_a, middle_a, StreamJob(blocks, frames),
            [FlowJob([attention_b], [shards[1][2]], dp // 8, [shards[1][1]])], 2, True,
        )
        *heads_b, middle_b, down_b = attend(1, attention_b, second, strip, [FlowJob([down_b], [])], 3)
        cot = cotangent.reshape(frames, tp, frames, strip, width)
        hidden_b, pushed_b, result, cot = expand(
            1, up_b, down_b, middle_b, None, [SwapJob(cot, False)], 4, True
        )
        attention_a, up_a, down_a = whole(attention_a), whole(up_a), whole(down_a)
        attention_b, up_b, down_b = whole(attention_b), whole(up_b), whole(down_b)
    else:
        (attention_a, up_a, down_a), (attention_b, up_b, down_b) = [[gather_plain(v) for v in group] for group in shards]
        *heads_a, middle_a = attend(0, attention_a, first, 0)
        hidden_a, pushed_a, second = expand(0, up_a, down_a, middle_a)
        second = exchange(by_patch(second).reshape(blocks))
        *heads_b, middle_b = attend(1, attention_b, second, strip)
        hidden_b, pushed_b, result = expand(1, up_b, down_b, middle_b)
        cot = exchange(by_patch(cotangent[0]).reshape(blocks))
    middle_a, middle_b = middle_a.reshape(tokens, width), middle_b.reshape(tokens, width)
    cot = cot.reshape(tokens, width)

    if fused:
        ffn_cores = lambda: CoreJob(2, width, ffn_weights.shape[-1])
        head_cores = lambda: CoreJob(1, width, kinds * cols)
        grad, *sums_b, kept, result = ffn_backward(
            up_b, down_b, cot, middle_b, pushed_b, hidden_b, mod[1], ffn_cores(),
            [SwapJob(result.reshape(tp, frames, frames, strip, width), True)], 5,
        )
        output = result.reshape(clips.shape)
        ffn_grad = kept
        *more_b, grad, kept, line_up = attention_backward(
            attention_b, grad.reshape(blocks), second, heads_b, mod[1], strip,
            StreamJob(blocks, 0), head_cores(), [ScatterJob([(ffn_grad, 0)], 3 * dp // 8)], 6,
        )
        waiting = [(ffn_grad, 1), (kept, 0)]
        grad, *sums_a, kept, done_up, line_b = ffn_backward(
            up_a, down_a, grad.reshape(pieces), middle_a, pushed_a, hidden_a, mod[0], ffn_cores(),
            [LineJob(line_up), ScatterJob(waiting, dp // 4)], 7,
        )
        ffn_grad = kept
        grad, *more_a, kept, done_b, line_ffn_a, done_up_a = attention_backward(
            attention_a, grad.reshape(first.shape), first, heads_a, mod[0], 0, None, head_cores(),
            [LineJob(line_b), ScatterJob([(ffn_grad, 0), (ffn_grad, 1)], dp // 4, True)], 8,
        )
        packed_a = kept
        done = (done_up_a, done_up, done_b[:1], done_b[1:])
    else:
        result = exchange(result.reshape(blocks)).reshape(pieces)
        output = result.transpose(1, 0, 2, 3).reshape(clips.shape)
        grad, *sums_b, ffn_grad = ffn_backward(up_b, down_b, cot, middle_b, pushed_b, hidden_b, mod[1])
        done_ffn_b = scatter_plain(ffn_grad)
        grad, packed_b, *more_b = attention_backward(
            attention_b, grad.reshape(blocks), second, heads_b, mod[1], strip
        )
        done_b = scatter_plain(packed_b[None])
        grad = exchange(grad.astype(jnp.bfloat16))
        grad, *sums_a, ffn_grad = ffn_backward(up_a, down_a, grad.reshape(pieces), middle_a, pushed_a, hidden_a, mod[0])
        done_ffn_a = scatter_plain(ffn_grad)
        grad, packed_a, *more_a = attention_backward(attention_a, grad.reshape(first.shape), first, heads_a, mod[0], 0)
        done_a = scatter_plain(packed_a[None])
    input_grad = grad.reshape(clips.shape)

    def gather_small(more, sums):
        attention_sums, project_sum = more
        up_sum, low_sums = sums
        return jnp.concatenate(
            [*unpack_bias(project_sum), attention_sums[0], up_sum.reshape(-1), low_sums[0],
             attention_sums[1:].reshape(-1), low_sums[1:].reshape(-1)]
        )

    small = jnp.stack([gather_small(more_a, sums_a), gather_small(more_b, sums_b)])
    token_width = small.shape[1] - mod_width
    *summed, small, grad_act = leave(
        small.reshape(tp, -1, 128), modulation_low, token_width,
        *((packed_a, line_ffn_a, done) if fused else (None, None, None)), 9,
    )
    small = small.transpose(1, 0, 2, 3).reshape(dp, layers, -1)
    grad_mod_low = small[..., token_width:].astype(jnp.bfloat16)
    grad_bias_all = jnp.concatenate(
        [small[..., :token_width], grad_mod_low.astype(jnp.float32)], axis=-1
    ).sum(axis=0)
    grad_bias = lax.dynamic_slice_in_dim(grad_bias_all, position * bias_cols, bias_cols, axis=1)
    grad_mod_weight = dot32("ck,cle->lke", cond_rows, grad_mod_low)[:, :mod_rows]
    grad_act = lax.dynamic_index_in_dim(
        grad_act[:, :, :mod_rows], lax.axis_index("dp"), axis=1, keepdims=False
    )
    if fused:
        grad_attention, grad_ffn = summed
    else:
        grad_attention = jnp.stack([jnp.stack(unpack_heads(done[0])) for done in (done_a, done_b)])
        grad_ffn = jnp.stack([done_ffn_a, done_ffn_b])
    silu_value, silu_pull = jax.vjp(jax.nn.silu, embed)
    cond_grad = silu_pull(grad_act.reshape(1, width))[0]

    return (output, input_grad, cond_grad) + (
        adam_update(attention_weights, attention_first, attention_second, grad_attention, MATRIX_RATE, MATRIX_DECAY)
        + adam_update(ffn_weights, ffn_first, ffn_second, grad_ffn, MATRIX_RATE, MATRIX_DECAY)
        + adam_update(modulation_weights, modulation_first, modulation_second, grad_mod_weight, MATRIX_RATE, MATRIX_DECAY)
        + adam_update(bias_vectors, bias_first, bias_second, grad_bias, VECTOR_RATE, 0.0)
    )


def solution(mesh):
    tokens = P("dp", "tensor", None, None)
    matrix = P(None, None, "dp", "tensor")
    modulation = P(None, BOTH, None)
    vector = P(None, BOTH)
    return jax.shard_map(
        per_device,
        mesh=mesh,
        in_specs=(tokens, tokens, P("dp"), P("dp"), P(), P())
        + (matrix,) * 6 + (modulation,) * 3 + (vector,) * 3,
        out_specs=(tokens, tokens, P("dp", None)) + (matrix,) * 8 + (modulation,) * 4 + (vector,) * 4,
        check_vma=False,
    )
```

```python
from functools import partial

import jax
import jax.numpy as jnp
from jax import lax
from jax.experimental import pallas as pl
from jax.experimental.pallas import tpu as pltpu
from jax.sharding import PartitionSpec as P

HD = 64
PAIR = 128
PARTS = 3
STEP = 10
BETA_ONE = 0.9
BETA_TWO = 0.999
ADAM_EPS = 1e-08
MATRIX_RATE = 0.04
VECTOR_RATE = 0.2
MATRIX_DECAY = 0.1
NORM_EPS = 1e-06
GELU_A = (2.0 / 3.141592653589793) ** 0.5
GELU_B = 0.044715
BLOCKED = -1e30
VMEM_LIMIT = 60 * 1024 * 1024
BOTH = ("dp", "tensor")


def mm(left, right, dims=((1,), (0,))):
    return lax.dot_general(left, right, (dims, ((), ())), preferred_element_type=jnp.float32)


def norm_parts(value):
    average = jnp.mean(value, axis=-1, keepdims=True)
    centred = value - average
    spread = jnp.mean(centred * centred, axis=-1, keepdims=True)
    inverse = lax.rsqrt(spread + NORM_EPS)
    return centred * inverse, inverse


def norm_back(grad, shape, inverse):
    first = jnp.mean(grad, axis=-1, keepdims=True)
    second = jnp.mean(grad * shape, axis=-1, keepdims=True)
    return inverse * (grad - first - shape * second)


def rows_of(ref):
    value = ref[...]
    return value.reshape(-1, value.shape[-1])


def put(ref, value):
    ref[...] = value.reshape(ref.shape).astype(ref.dtype)


def add_rows(ref, index, value):
    ref[pl.ds(index, 1), :] += jnp.sum(value, axis=0, keepdims=True)


def half_masks(rows):
    lane = lax.broadcasted_iota(jnp.int32, (rows, PAIR), 1)
    return lane < HD


def same_patch(tokens, stride):
    row = lax.broadcasted_iota(jnp.int32, (tokens, tokens), 0)
    column = lax.broadcasted_iota(jnp.int32, (tokens, tokens), 1)
    return lax.rem(row, stride) == lax.rem(column, stride)


def swap_halves(value):
    return pltpu.roll(value, HD, 1)


def start_loads(source, target, semaphores):
    for rank in range(target.shape[0]):
        pltpu.make_async_copy(source.at[rank], target.at[rank], semaphores.at[rank]).start()


def wait_loads(target, semaphores, rank):
    pltpu.make_async_copy(target.at[rank], target.at[rank], semaphores.at[rank]).wait()


def softmax_rows(scores, axis):
    raised = jnp.exp(scores - jnp.max(scores, axis=axis, keepdims=True))
    return raised * (1.0 / jnp.sum(raised, axis=axis, keepdims=True))


def attention_forward_kernel(
    stride, hook, source, stream_ref, mod_ref, bias_ref, bias_out_ref,
    project_ref, mixed_ref, branch_ref, middle_ref, weight_ref, semaphores,
):
    ranks = weight_ref.shape[0]

    @pl.when(pl.program_id(0) == 0)
    def _():
        start_loads(source, weight_ref, semaphores)

    stream = rows_of(stream_ref).astype(jnp.float32)
    tokens, width = stream.shape
    shape, _ = norm_parts(stream)
    normed = (shape * (1.0 + mod_ref[1:2]) + mod_ref[0:1]).astype(jnp.bfloat16)
    lower = half_masks(tokens)
    allowed = same_patch(tokens, stride) if stride else None

    @pl.when(pl.program_id(0) == 0)
    def _():
        for rank in range(ranks):
            wait_loads(weight_ref, semaphores, rank)

    def mix(heads):
        scores = [mm(chosen.astype(jnp.bfloat16), key, ((1,), (1,))) for chosen, key, _ in heads]
        outs = []
        for score, (_, _, value) in zip(scores, heads):
            if stride:
                score = jnp.where(allowed, score, BLOCKED)
            outs.append(mm(softmax_rows(score, -1).astype(jnp.bfloat16), value))
        return outs

    branch = None
    for rank in range(ranks):
        hook(rank)
        project = (mm(normed, weight_ref[rank, :, : 5 * PAIR]) + bias_ref[rank]).astype(jnp.bfloat16)
        project_ref[rank] = project.reshape(project_ref.shape[1:])
        query = project[:, :PAIR].astype(jnp.float32) * HD**-0.5
        key, value = project[:, PAIR : 2 * PAIR], project[:, 2 * PAIR : 3 * PAIR]
        both = project[:, 3 * PAIR : 4 * PAIR].astype(jnp.float32)
        first, second, last = mix(
            [
                (jnp.where(lower, query, 0.0), key, value),
                (jnp.where(lower, 0.0, query), key, value),
                (
                    jnp.where(lower, both * HD**-0.5, 0.0),
                    swap_halves(both).astype(jnp.bfloat16),
                    project[:, 4 * PAIR : 5 * PAIR],
                ),
            ]
        )
        mixed = jnp.concatenate(
            [jnp.where(lower, 0.0, swap_halves(last)), jnp.where(lower, first, second)], axis=1
        ).astype(jnp.bfloat16)
        mixed_ref[rank] = mixed.reshape(mixed_ref.shape[1:])
        term = mm(mixed, weight_ref[rank, :, 4 * PAIR :], ((1,), (1,)))
        branch = term if branch is None else branch + term
    branch = branch + bias_out_ref[...]
    put(branch_ref, branch)
    put(middle_ref, stream + mod_ref[2:3] * branch)


def gelu_parts(value):
    square = value * value
    bent = jnp.tanh(value * (GELU_A + (GELU_A * GELU_B) * square))
    half = 0.5 * (1.0 + bent)
    slope = half + (0.5 * value) * (1.0 - bent * bent) * (GELU_A + (3.0 * GELU_A * GELU_B) * square)
    return value * half, slope


def turn_of(rank):
    core = lax.rem(lax.axis_index("tensor"), 2)
    return rank + (1 - core) * (1 - 2 * (rank % 2))


def ffn_forward_kernel(
    stream, turned, hook, up_source, down_source, middle_ref, mod_ref, bias_ref, bias_up_ref, hidden_ref, branch_ref, *rest
):
    if stream is None:
        result_ref, *rest = rest
    up_ref, down_ref, up_semaphores, down_semaphores = rest
    step = pl.program_id(0)
    ranks = up_ref.shape[0]

    @pl.when(step == 0)
    def _():
        start_loads(up_source, up_ref, up_semaphores)
        start_loads(down_source, down_ref, down_semaphores)

    middle = middle_ref[...]
    shape, _ = norm_parts(middle)
    second = (shape * (1.0 + mod_ref[4:5]) + mod_ref[3:4]).astype(jnp.bfloat16)

    @pl.when(step == 0)
    def _():
        for rank in range(ranks):
            wait_loads(up_ref, up_semaphores, rank)
            wait_loads(down_ref, down_semaphores, rank)

    down = None
    for rank in range(ranks):
        hook(rank)
        hidden = mm(second, up_ref[rank]) + bias_up_ref[rank]
        hidden_ref[turn_of(rank) if turned else rank] = hidden.astype(jnp.bfloat16)
        active, _ = gelu_parts(hidden)
        part = mm(active.astype(jnp.bfloat16), down_ref[rank], ((1,), (1,)))
        down = part if down is None else down + part
    down = down + bias_ref[...]
    branch_ref[...] = down.astype(jnp.bfloat16)
    result = middle + mod_ref[5:6] * down
    if stream is None:
        result_ref[...] = result.astype(result_ref.dtype)
    else:
        stream.put(step, result)


def load_rows(ref, index, chunk):
    if len(ref.shape) == 2:
        return ref[index * chunk : (index + 1) * chunk, :].astype(jnp.float32)
    blocks, _, strip, width = ref.shape
    frames = chunk // (blocks * strip)
    parts = [ref[:, index * frames + frame].reshape(blocks * strip, width) for frame in range(frames)]
    return jnp.concatenate(parts, axis=0).astype(jnp.float32)


def ffn_backward_kernel(
    split, cores, hook, up_source, down_source, grad_ref, middle_ref, branch_ref, hidden_ref, mod_ref,
    grad_middle_ref, up_sum_ref, sums_ref, *refs
):
    if cores is None:
        weight_grad_ref, *refs = refs
    (up_ref, down_ref, up_semaphores, down_semaphores,
     second_ref, low_ref, low_across_ref, active_ref, slope_ref, total_ref) = refs
    step = pl.program_id(0)
    rank = step if cores is None else cores.rank(step)
    tokens, width = middle_ref.shape
    chunk = tokens // split

    @pl.when(step == 0)
    def _():
        start_loads(up_source, up_ref, up_semaphores)
        start_loads(down_source, down_ref, down_semaphores)
        sums_ref[...] = jnp.zeros_like(sums_ref)
        up_sum_ref[...] = jnp.zeros_like(up_sum_ref)
        for index in range(split):
            rows = slice(index * chunk, (index + 1) * chunk)
            grad = load_rows(grad_ref, index, chunk)
            low = (mod_ref[5:6] * grad).astype(jnp.bfloat16)
            low_ref[rows, :] = low
            low_across_ref[:, rows] = low.T
            add_rows(sums_ref, 0, low.astype(jnp.float32))
            add_rows(sums_ref, 3, grad * branch_ref[rows, :].astype(jnp.float32))
            shape, _ = norm_parts(middle_ref[rows, :])
            second = (shape * (1.0 + mod_ref[4:5]) + mod_ref[3:4]).astype(jnp.bfloat16)
            second_ref[:, rows] = second.T

    wait_loads(up_ref, up_semaphores, rank)
    wait_loads(down_ref, down_semaphores, rank)

    for index in range(split):
        hook(index)
        rows = slice(index * chunk, (index + 1) * chunk)
        active, slope = gelu_parts(hidden_ref[0, rows, :].astype(jnp.float32))
        active_ref[rows, :] = active.astype(jnp.bfloat16)
        low = (mm(low_ref[rows, :], down_ref[rank]) * slope).astype(jnp.bfloat16)
        slope_ref[rows, :] = low
        up_sum_ref[rank] += jnp.sum(low.astype(jnp.float32), axis=0, keepdims=True)
        part = mm(low, up_ref[rank], ((1,), (1,)))
        total_ref[rows, :] = jnp.where(step == 0, 0.0, total_ref[rows, :]) + part
    hook(2)
    make_up = lambda: mm(second_ref[...], slope_ref[...])
    if cores is None:
        weight_grad_ref[0, 0] = make_up().astype(jnp.bfloat16)
    else:
        cores.put(step, 0, make_up)
        cores.send(step, 0)
    hook(3)
    make_down = lambda: mm(low_across_ref[...], active_ref[...])
    if cores is None:
        weight_grad_ref[1, 0] = make_down().astype(jnp.bfloat16)
    else:
        cores.put(step, 1, make_down)
        cores.send(step, 1)

    @pl.when(step == pl.num_programs(0) - 1)
    def _():
        for index in range(split):
            rows = slice(index * chunk, (index + 1) * chunk)
            shape, inverse = norm_parts(middle_ref[rows, :])
            grad = total_ref[rows, :]
            add_rows(sums_ref, 1, grad)
            add_rows(sums_ref, 2, grad * shape)
            back = norm_back(grad * (1.0 + mod_ref[4:5]), shape, inverse)
            grad_middle_ref[rows, :] = load_rows(grad_ref, index, chunk) + back


def attention_backward_kernel(
    stride, swap, cores, hook, source, grad_ref, stream_ref, project_ref, mixed_ref, branch_ref, mod_ref, *refs
):
    if swap is None:
        grad_stream_ref, *refs = refs
    if cores is None:
        weight_grad_ref, *refs = refs
    (sums_ref, project_sum_ref,
     weight_ref, semaphores, left_ref, right_ref, outer_ref) = refs
    step = pl.program_id(0)
    ranks = weight_ref.shape[0]

    @pl.when(step == 0)
    def _():
        start_loads(source, weight_ref, semaphores)
        sums_ref[...] = jnp.zeros_like(sums_ref)
        project_sum_ref[...] = jnp.zeros_like(project_sum_ref)

    grad_middle = rows_of(grad_ref)
    tokens, width = grad_middle.shape
    stream = rows_of(stream_ref).astype(jnp.float32)
    shape, inverse = norm_parts(stream)
    rows = pl.ds(pl.multiple_of(step * tokens, tokens), tokens)
    normed = (shape * (1.0 + mod_ref[1:2]) + mod_ref[0:1]).astype(jnp.bfloat16)
    low = (mod_ref[2:3] * grad_middle).astype(jnp.bfloat16)
    left_ref[0, :, rows] = normed.T
    left_ref[1, :, rows] = low.T
    add_rows(sums_ref, 0, low.astype(jnp.float32))
    add_rows(sums_ref, 3, grad_middle * rows_of(branch_ref).astype(jnp.float32))
    lower = half_masks(tokens)
    allowed = same_patch(tokens, stride) if stride else None
    scale = HD**-0.5

    @pl.when(step == 0)
    def _():
        for rank in range(ranks):
            wait_loads(weight_ref, semaphores, rank)

    def score_grads(heads):
        scores = [mm(key, chosen.astype(jnp.bfloat16), ((1,), (1,))) for chosen, key, _, _ in heads]
        grad_probs = [mm(value, taken.astype(jnp.bfloat16), ((1,), (1,))) for _, _, value, taken in heads]
        outs = []
        for score, grad_prob in zip(scores, grad_probs):
            if stride:
                score = jnp.where(allowed, score, BLOCKED)
            probs = softmax_rows(score, 0)
            inner = jnp.sum(grad_prob * probs, axis=0, keepdims=True)
            outs.append((probs.astype(jnp.bfloat16), (probs * (grad_prob - inner)).astype(jnp.bfloat16)))
        return outs

    grad_normed = None
    for rank in range(ranks):
        hook(rank)
        project = project_ref[rank].reshape(tokens, 5 * PAIR)
        mixed = mixed_ref[rank].reshape(tokens, 2 * PAIR)
        outer_ref[rank, rows, :] = mixed
        grad_mixed = mm(low, weight_ref[rank, :, 4 * PAIR :]).astype(jnp.bfloat16)
        query, key, value = (project[:, n * PAIR : (n + 1) * PAIR] for n in range(3))
        query_wide = query.astype(jnp.float32) * scale
        pair = grad_mixed[:, PAIR:]
        pair_wide = pair.astype(jnp.float32)
        both = project[:, 3 * PAIR : 4 * PAIR].astype(jnp.float32)
        swapped = swap_halves(both).astype(jnp.bfloat16)
        single = swap_halves(grad_mixed[:, :PAIR].astype(jnp.float32))
        heads = [
            (jnp.where(keep, query_wide, 0.0), key, value, jnp.where(keep, pair_wide, 0.0)) for keep in (lower, ~lower)
        ]
        heads.append(
            (jnp.where(lower, both * scale, 0.0), swapped, project[:, 4 * PAIR :], jnp.where(lower, single, 0.0))
        )
        solved = score_grads(heads)
        outs = [
            (mm(grad_scores, key, ((0,), (0,))), mm(grad_scores, query), mm(probs, pair))
            for probs, grad_scores in solved[:2]
        ]
        parts = [
            jnp.where(lower, one, two) * factor
            for one, two, factor in zip(outs[0], outs[1], (scale, scale, 1.0))
        ]
        probs, grad_scores = solved[2]
        parts.append(
            jnp.where(lower, mm(grad_scores, swapped, ((0,), (0,))), mm(grad_scores, swapped)) * scale
        )
        parts.append(jnp.where(lower, mm(probs, single.astype(jnp.bfloat16)), 0.0))
        whole = jnp.concatenate(parts, axis=1).astype(jnp.bfloat16)
        right_ref[rank, rows, :] = whole
        add_rows(project_sum_ref, rank, whole.astype(jnp.float32))
        term = mm(whole, weight_ref[rank, :, : 5 * PAIR], ((1,), (1,)))
        grad_normed = term if grad_normed is None else grad_normed + term
    add_rows(sums_ref, 1, grad_normed)
    add_rows(sums_ref, 2, grad_normed * shape)
    back = norm_back(grad_normed * (1.0 + mod_ref[1:2]), shape, inverse)
    if swap is None:
        put(grad_stream_ref, grad_middle + back)
    else:
        swap.put(step, grad_middle + back)

    @pl.when(step == pl.num_programs(0) - 1)
    def _():
        def weights(turn, carry):
            rank = turn if cores is None else cores.rank(turn)

            def make():
                inside = mm(left_ref[0], right_ref[rank])
                outside = mm(left_ref[1], outer_ref[rank])
                return jnp.concatenate(
                    [inside[:, : 4 * PAIR], inside[:, 4 * PAIR :] + outside[:, :PAIR], outside[:, PAIR:]], axis=1
                )

            if cores is None:
                weight_grad_ref[rank] = make().astype(jnp.bfloat16)
            else:
                cores.put(turn, 0, make)
                cores.send(turn, 0)
            return carry

        lax.fori_loop(0, ranks, weights, 0)


def fixed(shape):
    return pl.BlockSpec(shape, lambda step: (0,) * len(shape), pipeline_mode=pl.Buffered(1))


def cost(flops, moved, raised=0):
    return pl.CostEstimate(flops=int(flops), bytes_accessed=int(moved), transcendentals=int(raised))


def group_spec(shape):
    return pl.BlockSpec((shape[0], 1, shape[2], shape[3]), lambda step: (0, step, 0, 0))


def rank_spec(shape):
    return pl.BlockSpec((shape[0], shape[1], 1) + shape[3:], lambda step: (0, 0, step, 0, 0))


def attention_forward(weight, stream, mod, bias, bias_out, stride, jobs=(), collective_id=None):
    shape = stream.shape
    width = shape[-1]
    ranks = bias.shape[0]
    tokens = shape[0] * shape[1] * shape[2]
    spec = group_spec(shape)
    low = jax.ShapeDtypeStruct(shape, jnp.bfloat16)
    wide = jax.ShapeDtypeStruct(shape, jnp.float32)
    project = jax.ShapeDtypeStruct((ranks,) + shape[:3] + (5 * PAIR,), jnp.bfloat16)
    mixed = jax.ShapeDtypeStruct((ranks,) + shape[:3] + (2 * PAIR,), jnp.bfloat16)
    return call(
        partial(attention_forward_kernel, stride),
        shape[1],
        [weight, stream, mod, bias, bias_out],
        anywhere(1) + [spec, fixed(mod.shape), fixed(bias.shape), fixed(bias_out.shape)],
        [project, mixed, low, wide],
        [rank_spec(project.shape), rank_spec(mixed.shape), spec, spec],
        [pltpu.VMEM((ranks, width, 6 * PAIR), jnp.bfloat16), pltpu.SemaphoreType.DMA((ranks,))],
        jobs,
        collective_id,
        cost(8 * tokens * width * width * 1.5, tokens * width * 16),
        "attention_forward",
    )


def ffn_weights_scratch(ranks, width, part):
    return [
        pltpu.VMEM((ranks, width, part), jnp.bfloat16),
        pltpu.VMEM((ranks, width, part), jnp.bfloat16),
        pltpu.SemaphoreType.DMA((ranks,)),
        pltpu.SemaphoreType.DMA((ranks,)),
    ]


def ffn_forward(up, down, middle, mod, bias_down, bias_up, stream=None, jobs=(), collective_id=None, turned=False):
    tokens, width = middle.shape
    ranks, _, part = bias_up.shape
    steps = 4
    chunk = tokens // steps
    block = pl.BlockSpec((chunk, width), lambda step: (step, 0))
    result = [jax.ShapeDtypeStruct((tokens, width), jnp.bfloat16)] if stream is None else []
    return call(
        partial(ffn_forward_kernel, stream, turned),
        steps,
        [up, down, middle, mod, bias_down, bias_up],
        anywhere(2) + [block, fixed(mod.shape), fixed(bias_down.shape), fixed(bias_up.shape)],
        [
            jax.ShapeDtypeStruct((ranks, tokens, part), jnp.bfloat16),
            jax.ShapeDtypeStruct((tokens, width), jnp.bfloat16),
        ] + result,
        [pl.BlockSpec((ranks, chunk, part), lambda step: (0, step, 0)), block] + [block] * len(result),
        ffn_weights_scratch(ranks, width, part),
        ([] if stream is None else [stream]) + list(jobs),
        collective_id,
        cost(4.8 * tokens * width * ranks * part, tokens * width * 14, tokens * ranks * part),
        "ffn_forward",
    )


def ffn_backward(up, down, grad, middle, branch, hidden, mod, cores=None, jobs=(), collective_id=None):
    tokens, width = middle.shape
    ranks, _, part = hidden.shape
    whole = fixed((tokens, width))
    made = [jax.ShapeDtypeStruct((2, ranks, width, part), jnp.bfloat16)] if cores is None else []
    return call(
        partial(ffn_backward_kernel, 2, cores),
        ranks,
        [up, down, grad, middle, branch, hidden, mod],
        anywhere(2) + [
            fixed(grad.shape), whole, whole,
            pl.BlockSpec((1, tokens, part), lambda step: (step, 0, 0)),
            fixed(mod.shape),
        ],
        [
            jax.ShapeDtypeStruct((tokens, width), jnp.float32),
            jax.ShapeDtypeStruct((ranks, 1, part), jnp.float32),
            jax.ShapeDtypeStruct((4, width), jnp.float32),
        ] + made,
        [
            whole,
            fixed((ranks, 1, part)),
            fixed((4, width)),
        ] + [pl.BlockSpec((2, 1, width, part), lambda step: (0, step, 0, 0))] * len(made),
        ffn_weights_scratch(ranks, width, part) + [
            pltpu.VMEM((width, tokens), jnp.bfloat16),
            pltpu.VMEM((tokens, width), jnp.bfloat16),
            pltpu.VMEM((width, tokens), jnp.bfloat16),
            pltpu.VMEM((tokens, part), jnp.bfloat16),
            pltpu.VMEM((tokens, part), jnp.bfloat16),
            pltpu.VMEM((tokens, width), jnp.float32),
        ],
        ([] if cores is None else [cores]) + list(jobs),
        collective_id,
        cost(9.6 * tokens * width * ranks * part, tokens * width * 20, tokens * ranks * part),
        "ffn_backward",
    )


def attention_backward(weight, grad, stream, saved, mod, stride, swap=None, cores=None, jobs=(), collective_id=None):
    project, mixed, branch = saved
    shape = stream.shape
    width = shape[-1]
    ranks = project.shape[0]
    tokens = shape[0] * shape[1] * shape[2]
    spec = group_spec(shape)
    result = [jax.ShapeDtypeStruct(shape, jnp.float32)] if swap is None else []
    made = [jax.ShapeDtypeStruct((ranks, width, 6 * PAIR), jnp.bfloat16)] if cores is None else []
    return call(
        partial(attention_backward_kernel, stride, swap, cores),
        shape[1],
        [weight, grad, stream, project, mixed, branch, mod],
        anywhere(1) + [
            spec, spec, rank_spec(project.shape), rank_spec(mixed.shape), spec, fixed(mod.shape),
        ],
        result + made + [
            jax.ShapeDtypeStruct((4, width), jnp.float32),
            jax.ShapeDtypeStruct((ranks, 5 * PAIR), jnp.float32),
        ],
        [spec] * len(result) + [fixed((ranks, width, 6 * PAIR))] * len(made) + [
            fixed((4, width)), fixed((ranks, 5 * PAIR)),
        ],
        [
            pltpu.VMEM((ranks, width, 6 * PAIR), jnp.bfloat16),
            pltpu.SemaphoreType.DMA((ranks,)),
            pltpu.VMEM((2, width, tokens), jnp.bfloat16),
            pltpu.VMEM((ranks, tokens, 5 * PAIR), jnp.bfloat16),
            pltpu.VMEM((ranks, tokens, 2 * PAIR), jnp.bfloat16),
        ],
        [job for job in (swap, cores) if job is not None] + list(jobs),
        collective_id,
        cost(16 * tokens * width * width * 1.5, tokens * width * 20),
        "attention_backward",
    )


def pack_heads(block):
    query, key, value, outer = block
    return jnp.concatenate(
        [query[:, :PAIR], key[:, :PAIR], value[:, :PAIR], query[:, PAIR:], key[:, PAIR:],
         value[:, PAIR:], outer[:, PAIR:], outer[:, :PAIR]], axis=1
    )


def unpack_heads(packed):
    part = lambda start, size: packed[:, start : start + size]
    join = lambda first, last: jnp.concatenate([part(first, PAIR), part(last, HD)], axis=1)
    return [join(0, 3 * PAIR), join(PAIR, 3 * PAIR + HD), join(2 * PAIR, 4 * PAIR), join(5 * PAIR, 4 * PAIR + HD)]


def pack_bias(query, value, ranks):
    query, value = query.reshape(ranks, -1), value.reshape(ranks, -1)
    none = jnp.zeros((ranks, PAIR), query.dtype)
    return jnp.concatenate(
        [query[:, :PAIR], none, value[:, :PAIR], query[:, PAIR:], none[:, :HD], value[:, PAIR:], none[:, :HD]],
        axis=1,
    )[:, None]


def unpack_bias(sums):
    query = jnp.concatenate([sums[:, :PAIR], sums[:, 3 * PAIR : 3 * PAIR + HD]], axis=1)
    value = jnp.concatenate([sums[:, 2 * PAIR : 3 * PAIR], sums[:, 4 * PAIR : 4 * PAIR + HD]], axis=1)
    return query.reshape(-1), value.reshape(-1)


def place():
    return lax.axis_index("dp"), lax.axis_index("tensor"), lax.axis_size("dp"), lax.axis_size("tensor")


def greet_all():
    device, rank, dp, tp = place()
    me, count = device * tp + rank, dp * tp
    barrier = pltpu.get_barrier_semaphore()

    def greet(index, carry):
        peer = lax.rem(me + index, count)
        pl.semaphore_signal(
            barrier, inc=1, device_id=(peer // tp, lax.rem(peer, tp)), device_id_type=pl.DeviceIdType.MESH
        )
        return carry

    lax.fori_loop(1, count, greet, 0)
    pl.semaphore_wait(barrier, count - 1)


def push(source, target, send, receive, device, rank):
    pltpu.make_async_remote_copy(
        src_ref=source, dst_ref=target, send_sem=send, recv_sem=receive,
        device_id=(device, rank), device_id_type=pl.DeviceIdType.MESH,
    ).start()


def wait_bytes(ref, semaphore):
    pltpu.make_async_copy(ref, ref, semaphore).wait()


class Where:
    def __init__(self):
        device, rank = lax.axis_index("dp"), lax.axis_index("tensor")
        self.count = lax.axis_size("dp") // 2
        self.device, self.rank = device, rank
        self.far, self.side = device // 2, lax.rem(device, 2)
        self.row, self.core = rank // 2, lax.rem(rank, 2)
        self.other_side = self.far * 2 + 1 - self.side
        self.other_row = (1 - self.row) * 2 + self.core
        self.other_core = self.row * 2 + 1 - self.core

    def ahead(self, step):
        return lax.rem(self.far + step, self.count)

    def line(self, step):
        return self.ahead(step) * 2 + self.side


def greet_neighbours(here):
    barrier = pltpu.get_barrier_semaphore()
    peers = [(here.other_side, here.rank), (here.device, here.other_row), (here.device, here.other_core)]
    peers += [(here.line(step), here.rank) for step in range(1, here.count)]
    for peer in peers:
        pl.semaphore_signal(barrier, inc=1, device_id=peer, device_id_type=pl.DeviceIdType.MESH)
    pl.semaphore_wait(barrier, len(peers))


def add_into(target, left, right):
    target[...] = left[...] + right[...]


class ScatterChain:
    def __init__(self, here, kept, line, lead, scratch):
        self.here, self.kept, self.line, self.lead = here, kept, line, lead
        self.keep, self.first_one, self.last_one, self.first_two, self.last_two, self.semaphores = scratch
        self.rows = line.shape[1]

    @staticmethod
    def scratch(width, columns, dp, lead):
        rows, far = width // dp, dp // 2
        low = lambda *shape: pltpu.VMEM(shape + (columns,), jnp.bfloat16)
        return [
            low(2, width),
            low(2, lead, rows), low(2 * (far - lead) * rows), low(lead, rows), low(far - lead, rows),
            pltpu.SemaphoreType.DMA((6, 2)),
        ]

    def chunk(self, row, far, side):
        return self.keep.at[row, pl.ds(pl.multiple_of((far * 2 + side) * self.rows, self.rows), self.rows)]

    def send(self, slot, source, target, device, rank):
        push(source, target, self.semaphores.at[slot, 0], self.semaphores.at[slot, 1], device, rank)

    def arrived(self, slot, ref):
        wait_bytes(ref, self.semaphores.at[slot, 1])

    def left(self, slot, ref):
        wait_bytes(ref, self.semaphores.at[slot, 0])

    def stage_one(self):
        here, lead = self.here, self.lead
        pltpu.make_async_copy(self.kept, self.keep, self.semaphores.at[5, 0]).start()
        for row in range(2):
            for far in range(lead):
                rows = pl.ds(pl.multiple_of((far * 2 + 1 - here.side) * self.rows, self.rows), self.rows)
                self.send(1, self.kept.at[row, rows], self.first_one.at[row, far], here.other_side, here.rank)
        start, size = lead * 2 * self.rows, (here.count - lead) * 2 * self.rows
        self.send(2, self.kept.at[1 - here.row, pl.ds(start, size)], self.last_one, here.device, here.other_row)

    def stage_two(self):
        here, lead = self.here, self.lead
        wait_bytes(self.keep, self.semaphores.at[5, 0])
        self.arrived(1, self.first_one)
        for row in range(2):
            for far in range(lead):
                mine = self.chunk(row, far, here.side)
                add_into(mine, mine, self.first_one.at[row, far])
        for far in range(lead):
            self.send(3, self.chunk(1 - here.row, far, here.side), self.first_two.at[far], here.device, here.other_row)
        self.arrived(2, self.last_one)
        for far in range(lead, here.count):
            for side in range(2):
                mine = self.chunk(here.row, far, side)
                add_into(mine, mine, self.last_one.at[pl.ds(((far - lead) * 2 + side) * self.rows, self.rows)])
        for far in range(lead, here.count):
            self.send(
                4, self.chunk(here.row, far, 1 - here.side), self.last_two.at[far - lead], here.other_side, here.rank
            )

    def merge(self):
        here = self.here
        self.arrived(3, self.first_two)
        self.arrived(4, self.last_two)
        for far in range(here.count):
            land = self.first_two.at[far] if far < self.lead else self.last_two.at[far - self.lead]
            add_into(self.line.at[far], self.chunk(here.row, far, here.side), land)

    def finish(self):
        self.left(1, self.first_one)
        self.left(2, self.last_one)
        self.left(3, self.first_two)
        self.left(4, self.last_two)


class LineChain:
    def __init__(self, here, line, out, land, semaphores):
        self.here, self.line, self.out, self.land, self.semaphores = here, line, out, land, semaphores

    @staticmethod
    def scratch(far, rows, columns):
        return [pltpu.VMEM((far - 1, rows, columns), jnp.bfloat16), pltpu.SemaphoreType.DMA((2,))]

    def start(self):
        here = self.here
        for step in range(1, here.count):
            push(
                self.line.at[here.ahead(step)], self.land.at[step - 1], self.semaphores.at[0],
                self.semaphores.at[1], here.line(step), here.rank,
            )

    def finish(self):
        wait_bytes(self.land, self.semaphores.at[1])
        total = self.line[self.here.far].astype(jnp.float32)
        for step in range(1, self.here.count):
            total = total + self.land[step - 1].astype(jnp.float32)
        self.out[...] = total
        wait_bytes(self.land, self.semaphores.at[0])


def leave_kernel(mod_start, *refs):
    refs = list(refs)
    scattering = len(refs) > 10
    kept, begun, *done = [refs.pop(0) for _ in range(6 if scattering else 2)]
    if not scattering:
        refs = [kept, begun] + refs
    small_ref, modulation_ref, *refs = refs
    heads_out, wide_out = (refs.pop(0), refs.pop(0)) if scattering else (None, None)
    sum_ref, act_ref, land_ref, acting_ref, semaphores, *space = refs
    device, rank, dp, tp = place()
    me, count = device * tp + rank, dp * tp
    greet_all()
    if scattering:
        here = Where()
        line_ref, out, *space = space
        pick = lambda number: [space.pop(0) for _ in range(number)]
        chains, trails = [], []
        for index in range(PARTS):
            size = out.shape[1] // PARTS
            part = pl.ds(index * size, size)
            line = line_ref.at[index]
            chains.append(ScatterChain(here, kept.at[0, :, :, part], line, here.count // 2, pick(6)))
            trails.append(LineChain(here, line, out.at[:, part], *pick(2)))
        others = [LineChain(here, begun.at[0], wide_out.at[0, 1], *pick(2))]
        chains[0].stage_one()
    for step in range(1, tp):
        there = lax.rem(rank + step, tp)
        push(small_ref.at[there], land_ref.at[rank], semaphores.at[0], semaphores.at[1], device, there)
    land_ref[rank] = small_ref[rank]
    wait_bytes(land_ref.at[pl.ds(0, tp - 1)], semaphores.at[1])
    mine = sum_ref.at[rank]
    mine[device] = jnp.sum(land_ref[...], axis=0)

    def one(step, carry):
        push(mine.at[device], mine.at[device], semaphores.at[2], semaphores.at[3], lax.rem(device + step, dp), rank)
        return carry

    lax.fori_loop(1, dp, one, 0)
    if scattering:
        for chain in chains[1:]:
            chain.stage_one()
        for chain in others:
            chain.start()
    wait_bytes(mine.at[pl.ds(0, dp - 1)], semaphores.at[3])
    for step in range(1, tp):
        push(mine, mine, semaphores.at[4], semaphores.at[5], device, lax.rem(rank + step, tp))
    if scattering:
        for chain in chains:
            chain.stage_two()
        for chain, line in zip(chains, trails):
            chain.merge()
            line.start()
    wait_bytes(sum_ref.at[pl.ds(0, tp - 1)], semaphores.at[5])
    layers, padded, columns = modulation_ref.shape
    lines = sum_ref.shape[2]
    total = jnp.zeros((dp, padded), jnp.float32)
    for layer in range(layers):
        for index in range(columns // PAIR):
            line = layer * (tp * lines // layers) + mod_start // PAIR + index
            low = sum_ref[line // lines, :, line % lines, :].astype(jnp.bfloat16)
            total += mm(low, modulation_ref[layer, :, index * PAIR : (index + 1) * PAIR], ((1,), (1,)))
    acting_ref[...] = jnp.concatenate([total, jnp.zeros((dp, PAIR - padded), jnp.float32)], axis=1)
    act_ref[me] = acting_ref[...]

    def tell(index, carry):
        peer = lax.rem(me + index, count)
        push(acting_ref, act_ref.at[me], semaphores.at[6], semaphores.at[7], peer // tp, lax.rem(peer, tp))
        return carry

    lax.fori_loop(1, count, tell, 0)
    if scattering:
        for chain in others:
            chain.finish()
    wait_bytes(act_ref.at[pl.ds(0, count - 1)], semaphores.at[7])
    wait_bytes(act_ref.at[pl.ds(0, count - 1)], semaphores.at[6])
    wait_bytes(land_ref.at[pl.ds(0, tp - 1)], semaphores.at[0])
    wait_bytes(mine.at[pl.ds(0, dp - 1)], semaphores.at[2])
    wait_bytes(sum_ref.at[pl.ds(0, tp - 1)], semaphores.at[4])
    if scattering:
        for chain in chains + trails:
            chain.finish()
        up_first, up_last, down_last, heads_last = done
        wide_out[0, 0], wide_out[1, 0], wide_out[1, 1] = up_first[0], up_last[0], down_last[0]
        for layer, packed in enumerate((out[...], heads_last[0])):
            parts = unpack_heads(packed)
            for kind in range(4):
                heads_out[layer, kind] = parts[kind]


def leave(small, modulation, mod_start, kept, begun, done, collective_id):
    tp, lines, lanes = small.shape
    dp = lax.axis_size("dp")
    inside = pl.BlockSpec(memory_space=pltpu.VMEM)
    shapes, space, extra = [], [], []
    if kept is not None:
        _, _, width, columns = kept.shape
        rows, far, part = width // dp, dp // 2, columns // PARTS
        extra = [kept, begun, *done]
        shapes = [
            jax.ShapeDtypeStruct((2, 4, rows, columns // 4), jnp.float32),
            jax.ShapeDtypeStruct((2, 2, rows, columns), jnp.float32),
        ]
        space = [pltpu.VMEM((PARTS, far, rows, part), jnp.bfloat16), pltpu.VMEM((rows, columns), jnp.float32)]
        for _ in range(PARTS):
            space += ScatterChain.scratch(width, part, dp, far // 2) + LineChain.scratch(far, rows, part)
        space += LineChain.scratch(far, rows, columns)
    return pl.pallas_call(
        partial(leave_kernel, mod_start),
        in_specs=([pl.BlockSpec(memory_space=pl.ANY)] + [inside] * 5)[: len(extra)] + [inside, inside],
        out_specs=[inside] * (len(shapes) + 2),
        out_shape=shapes + [
            jax.ShapeDtypeStruct((tp, dp, lines, lanes), jnp.float32),
            jax.ShapeDtypeStruct((dp * tp, dp, lanes), jnp.float32),
        ],
        scratch_shapes=[
            pltpu.VMEM((tp, lines, lanes), jnp.float32),
            pltpu.VMEM((dp, lanes), jnp.float32),
            pltpu.SemaphoreType.DMA((8,)),
        ] + space,
        compiler_params=pltpu.CompilerParams(
            collective_id=collective_id, has_side_effects=True, vmem_limit_bytes=VMEM_LIMIT
        ),
        name="leave",
    )(*extra, small, modulation)


class GatherChain:
    def __init__(self, here, source, out, semaphores, half=None):
        self.here, self.source, self.out, self.semaphores = here, source, out, semaphores
        self.half = here.count // 2 if half is None else half

    @staticmethod
    def scratch():
        return [pltpu.SemaphoreType.DMA((9, 2))]

    def pieces(self, rank, side, first=0, last=None):
        last = self.here.count if last is None else last
        return self.out.at[rank, pl.ds(first, last - first), side]

    def send(self, slot, pieces, device, rank):
        push(pieces, pieces, self.semaphores.at[slot, 0], self.semaphores.at[slot, 1], device, rank)

    def wait(self, slot, way, pieces):
        wait_bytes(self.pieces(0, 0, 0, pieces), self.semaphores.at[slot, way])

    def stage_line(self):
        here = self.here
        mine = self.out.at[here.rank, here.far, here.side]
        pltpu.make_async_copy(self.source, mine, self.semaphores.at[8, 0]).start()
        for step in range(1, here.count):
            push(
                self.source, mine, self.semaphores.at[0, 0], self.semaphores.at[0, 1], here.line(step), here.rank
            )

    def line_arrived(self):
        self.wait(8, 0, 1)
        self.wait(0, 1, self.here.count - 1)

    def line_left(self):
        self.wait(0, 0, self.here.count - 1)

    def stage_near(self):
        here = self.here
        mine = self.pieces(here.rank, here.side)
        self.send(1, mine, here.other_side, here.rank)
        self.send(2, mine, here.device, here.other_row)
        self.send(3, mine, here.device, here.other_core)

    def stage_across(self):
        here, count = self.here, self.here.count
        self.wait(1, 1, count)
        self.send(4, self.pieces(here.rank, 1 - here.side, 0, self.half), here.device, here.other_row)
        self.wait(2, 1, count)
        self.send(5, self.pieces(here.other_row, here.side, self.half, count), here.other_side, here.rank)
        self.send(6, self.pieces(here.rank, 1 - here.side), here.device, here.other_core)
        self.send(7, self.pieces(here.other_row, here.side), here.device, here.other_core)

    def stage_core(self):
        here, count = self.here, self.here.count
        self.wait(4, 1, self.half)
        self.wait(5, 1, count - self.half)
        self.send(8, self.pieces(here.other_row, 1 - here.side), here.device, here.other_core)

    def finish(self):
        count, half = self.here.count, self.half
        for slot in (3, 6, 7, 8):
            self.wait(slot, 1, count)
        for slot, pieces in ((1, count), (2, count), (3, count), (4, half), (5, count - half), (6, count), (7, count)):
            self.wait(slot, 0, pieces)
        self.wait(8, 0, count)


def column_parts(here, source, out, semaphores, half=None):
    size = out.shape[4] // PARTS
    chains = []
    for index, semaphore in enumerate(semaphores):
        part = pl.ds(index * size, size)
        shard = None if source is None else source.at[:, part]
        chains.append(GatherChain(here, shard, out.at[:, :, :, :, part], semaphore, half))
    return chains


class Job:
    operands, sources, shapes, specs, aliases, space = (), None, (), (), {}, ()
    stages, last = {}, ()


def anywhere(count):
    return [pl.BlockSpec(memory_space=pl.ANY)] * count


class CoreJob(Job):
    def __init__(self, kinds, width, columns):
        block = (kinds, width, columns)
        self.shapes, self.specs = [jax.ShapeDtypeStruct((kinds, 2, width, columns), jnp.bfloat16)], anywhere(1)
        self.space = [
            pltpu.VMEM((2,) + block, jnp.bfloat16),
            pltpu.VMEM((2,) + block, jnp.bfloat16),
            pltpu.SemaphoreType.DMA((4, kinds)),
        ]

    def bind(self, here, inputs, outputs, space):
        self.here, self.kept, (self.buffer, self.land, self.semaphores) = here, outputs[0], space
        self.stages = {}
        self.last = [
            partial(self.sent, own, kind) for own in range(2) for kind in range(self.buffer.shape[1])
        ]

    def sent(self, own, kind):
        wait_bytes(self.buffer.at[own, kind], self.semaphores.at[own, kind])

    def rank(self, turn):
        return turn_of(turn)

    def put(self, turn, kind, make):
        row, own = turn // 2, lax.rem(turn, 2)

        @pl.when(turn >= 2)
        def _():
            self.sent(own, kind)

        @pl.when(own == 0)
        def _():
            self.buffer[0, kind] = make().astype(jnp.bfloat16)

        @pl.when(own == 1)
        def _():
            wait_bytes(self.land.at[row, kind], self.semaphores.at[2 + row, kind])
            self.buffer[1, kind] = (make() + self.land[row, kind].astype(jnp.float32)).astype(jnp.bfloat16)

    def send(self, turn, kind):
        here, row, own = self.here, turn // 2, lax.rem(turn, 2)

        @pl.when(own == 0)
        def _():
            push(
                self.buffer.at[0, kind], self.land.at[row, kind], self.semaphores.at[0, kind],
                self.semaphores.at[2 + row, kind], here.device, here.other_core,
            )

        @pl.when(own == 1)
        def _():
            pltpu.make_async_copy(
                self.buffer.at[1, kind], self.kept.at[kind, row], self.semaphores.at[1, kind]
            ).start()


class ScatterJob(Job):
    def __init__(self, grads, lead, close=False):
        _, _, width, columns = grads[0][0].shape
        dp = lax.axis_size("dp")
        far, rows = dp // 2, width // dp
        self.lead, self.close, self.kinds = lead, close, [kind for _, kind in grads]
        self.operands = [array for array, _ in grads]
        shape = (len(grads) - close, far, rows, columns)
        self.shapes, self.specs = [jax.ShapeDtypeStruct(shape, jnp.bfloat16)], [fixed(shape)]
        self.space = ScatterChain.scratch(width, columns, dp, lead) * len(grads)
        if close:
            self.shapes.append(jax.ShapeDtypeStruct((1, rows, columns), jnp.float32))
            self.specs.append(fixed((1, rows, columns)))
            self.space = [pltpu.VMEM((far, rows, columns), jnp.bfloat16)] + LineChain.scratch(
                far, rows, columns
            ) + self.space

    def bind(self, here, inputs, outputs, space):
        lines = [outputs[0].at[index] for index in range(outputs[0].shape[0])]
        if self.close:
            own, land, semaphores, *space = space
            lines.insert(0, own)
            line = LineChain(here, own, outputs[1].at[0], land, semaphores)
        size = len(space) // len(inputs)
        chains = [
            ScatterChain(
                here, inputs[index].at[kind], lines[index], self.lead, space[index * size : (index + 1) * size]
            )
            for index, kind in enumerate(self.kinds)
        ]
        one = chains[0]
        if len(chains) == 1:
            self.stages = {(0, 0): [one.stage_one], (2, 0): [one.stage_two]}
            self.last = [one.merge, one.finish]
            return
        two = chains[1]
        if self.close:
            self.stages = {
                (0, 0): [one.stage_one], (1, 2): [one.stage_two], (2, 0): [one.merge, line.start, two.stage_one],
                (3, 2): [two.stage_two],
            }
            self.last = [line.finish, two.merge, one.finish, two.finish]
            return
        self.stages = {
            (0, 0): [one.stage_one, two.stage_one], (1, 3): [one.stage_two], (3, 1): [two.stage_two],
        }
        self.last = [one.merge, two.merge, one.finish, two.finish]


class LineJob(Job):
    def __init__(self, line):
        kinds, far, rows, columns = line.shape
        shape = (kinds, rows, columns)
        self.operands, self.sources = [line], [fixed(line.shape)]
        self.shapes, self.specs = [jax.ShapeDtypeStruct(shape, jnp.float32)], [fixed(shape)]
        self.space = LineChain.scratch(far, rows, columns) * kinds

    def bind(self, here, inputs, outputs, space):
        chains = [
            LineChain(here, inputs[0].at[kind], outputs[0].at[kind], *space[2 * kind : 2 * kind + 2])
            for kind in range(outputs[0].shape[0])
        ]
        self.stages = {(0, 0): [chain.start for chain in chains]}
        self.last = [chain.finish for chain in chains]


class FlowJob(Job):
    def __init__(self, spread, lines, half=None, late=()):
        dp, tp = lax.axis_size("dp"), lax.axis_size("tensor")
        self.counts, self.half = (len(spread), len(late)), half
        shards = list(late) + list(lines)
        self.operands = list(spread) + shards
        self.shapes = [jax.ShapeDtypeStruct(v.shape, v.dtype) for v in spread]
        self.shapes += [jax.ShapeDtypeStruct((tp, dp // 2, 2) + v.shape, v.dtype) for v in shards]
        self.specs = anywhere(len(self.shapes))
        self.aliases = {index: index for index in range(len(spread))}
        self.space = GatherChain.scratch() * (PARTS * len(self.shapes))

    def bind(self, here, inputs, outputs, space):
        first, late = self.counts
        chains = [
            column_parts(
                here, inputs[index] if index >= first else None, outputs[index],
                space[index * PARTS : (index + 1) * PARTS], self.half,
            )
            for index in range(len(inputs))
        ]
        spread, late, lines = (
            [chain for group in chosen for chain in group]
            for chosen in (chains[:first], chains[first : first + late], chains[first + late :])
        )
        self.stages = {(0, 0): [chain.stage_near for chain in spread]}
        self.stages[0, 0] += [chain.stage_line for chain in late + lines]
        for index, spot in zip(range(PARTS), ((1, 1), (2, 0), (3, 0))):
            self.stages[spot] = [chain.stage_across for chain in spread[index::PARTS]]
            for chain in late[index::PARTS]:
                self.stages[spot] += [chain.line_arrived, chain.stage_near]
        self.last = [chain.stage_across for chain in late]
        self.last += [chain.stage_core for chain in spread + late]
        self.last += [chain.finish for chain in spread + late]
        self.last += [chain.line_arrived for chain in lines]
        self.last += [chain.line_left for chain in late + lines]


class SwapJob(Job):
    def __init__(self, tokens, to_frames):
        self.to_frames = to_frames
        self.operands = [tokens]
        shape = tokens.shape
        shape = (shape[2], shape[0], shape[1]) + shape[3:] if to_frames else (shape[1], shape[2], shape[0]) + shape[3:]
        self.shapes, self.specs = [jax.ShapeDtypeStruct(shape, tokens.dtype)], anywhere(1)
        self.space = [pltpu.SemaphoreType.DMA((3,))]

    def bind(self, here, inputs, outputs, space):
        source, out, semaphores = inputs[0], outputs[0], space[0]
        frames, ranks = out.shape[:2] if self.to_frames else (out.shape[2], out.shape[0])
        few = pl.ds(0, ranks - 1)
        most, mine = (out.at[:, few], out.at[:, 0]) if self.to_frames else (out.at[few], out.at[0])

        def ends(frame, there):
            if self.to_frames:
                return source.at[there, :, frame], out.at[frame, here.rank]
            return source.at[frame, there], out.at[here.rank, :, frame]

        def start():
            for frame in range(frames):
                pltpu.make_async_copy(*ends(frame, here.rank), semaphores.at[2]).start()
            for step in range(1, ranks):
                there = lax.rem(here.rank + step, ranks)
                for frame in range(frames):
                    push(*ends(frame, there), semaphores.at[0], semaphores.at[1], here.device, there)

        def finish():
            wait_bytes(mine, semaphores.at[2])
            wait_bytes(most, semaphores.at[1])
            wait_bytes(most, semaphores.at[0])

        self.stages, self.last = {(0, 0): [start]}, [finish]


class StreamJob(Job):
    def __init__(self, shape, frames):
        self.shape, self.frames = shape, frames
        self.shapes, self.specs = [jax.ShapeDtypeStruct(shape, jnp.bfloat16)], anywhere(1)
        ranks, groups, rows, width = shape
        block = (groups, ranks, rows, width)
        if frames:
            block = (frames, ranks, groups, rows // frames, width)
        self.space = [pltpu.VMEM(block, jnp.bfloat16), pltpu.SemaphoreType.DMA((3,))]

    def bind(self, here, inputs, outputs, space):
        self.here, self.out = here, outputs[0]
        self.buffer, self.semaphores = space
        ranks = self.shape[0]

        def finish():
            wait_bytes(self.out.at[0], self.semaphores.at[2])
            wait_bytes(self.out.at[pl.ds(0, ranks - 1)], self.semaphores.at[1])
            wait_bytes(self.out.at[pl.ds(0, ranks - 1)], self.semaphores.at[0])

        self.stages, self.last = {}, [finish]

    def put(self, step, value):
        here, ranks = self.here, self.shape[0]
        size = self.buffer.size // self.buffer.shape[0] // value.shape[1]
        if value.shape[0] > size:
            count = value.shape[0] // size
            for index in range(count):
                self.put(step * count + index, value[index * size : (index + 1) * size])
            return
        self.buffer[step] = value.reshape(self.buffer.shape[1:]).astype(jnp.bfloat16)
        if self.frames:
            strip = self.buffer.shape[3]
            target = self.out.at[here.rank, :, pl.ds(pl.multiple_of(step * strip, strip), strip)]
        else:
            target = self.out.at[here.rank, step]
        pltpu.make_async_copy(self.buffer.at[step, here.rank], target, self.semaphores.at[2]).start()
        for ahead in range(1, ranks):
            there = lax.rem(here.rank + ahead, ranks)
            push(
                self.buffer.at[step, there], target, self.semaphores.at[0], self.semaphores.at[1],
                here.device, there,
            )


def greet_jobs(here):
    barrier = pltpu.get_barrier_semaphore()
    ranks = lax.axis_size("tensor")
    peers = [(here.other_side, here.rank)]
    peers += [(here.line(step), here.rank) for step in range(1, here.count)]
    peers += [(here.device, lax.rem(here.rank + step, ranks)) for step in range(1, ranks)]
    for peer in peers:
        pl.semaphore_signal(barrier, inc=1, device_id=peer, device_id_type=pl.DeviceIdType.MESH)
    pl.semaphore_wait(barrier, len(peers))


def call(body, steps, arguments, in_specs, out_shape, out_specs, scratch, jobs, collective_id, estimate, name):
    operands = [v for job in jobs for v in job.operands]
    sources = [v for job in jobs for v in (job.sources or anywhere(len(job.operands)))]
    shapes = [v for job in jobs for v in job.shapes]
    specs = [v for job in jobs for v in job.specs]
    space = [v for job in jobs for v in job.space]
    aliases, before, after = {}, len(arguments), len(out_shape)
    for job in jobs:
        for source, target in job.aliases.items():
            aliases[before + source] = after + target
        before, after = before + len(job.operands), after + len(job.shapes)

    def kernel(*refs):
        refs = list(refs)
        take = lambda number: [refs.pop(0) for _ in range(number)]
        inputs, job_inputs = take(len(arguments)), take(len(operands))
        outputs, job_outputs = take(len(out_shape)), take(len(shapes))
        own, job_space = take(len(scratch)), refs
        step = pl.program_id(0)
        if jobs:
            here = Where()
            for job in jobs:
                pick = lambda pool, number: [pool.pop(0) for _ in range(number)]
                job.bind(
                    here, pick(job_inputs, len(job.operands)), pick(job_outputs, len(job.shapes)),
                    pick(job_space, len(job.space)),
                )

        def hook(spot):
            for index in range(steps):
                todo = [
                    stage
                    for job in jobs
                    for (late, place), stages in sorted(job.stages.items())
                    if (late * 4 + place) * steps // 4 == index * 4 + spot
                    for stage in stages
                ]
                if todo or (jobs and spot == 0 and index == 0):

                    @pl.when(step == index)
                    def _():
                        if index == 0 and spot == 0:
                            greet_jobs(here)
                        for stage in todo:
                            stage()

        hook(0)
        body(lambda spot: hook(spot) if spot else None, *inputs, *outputs, *own)
        if jobs:

            @pl.when(step == steps - 1)
            def _():
                for job in jobs:
                    for stage in job.last:
                        stage()

    more = {"collective_id": collective_id, "has_side_effects": True} if jobs else {}
    return pl.pallas_call(
        kernel,
        grid=(steps,),
        in_specs=list(in_specs) + sources,
        out_specs=list(out_specs) + specs,
        out_shape=list(out_shape) + shapes,
        scratch_shapes=list(scratch) + space,
        input_output_aliases=aliases,
        compiler_params=pltpu.CompilerParams(
            vmem_limit_bytes=VMEM_LIMIT, dimension_semantics=("arbitrary",), **more
        ),
        cost_estimate=estimate,
        name=name,
    )(*arguments, *operands)


def entry_kernel(
    per_device, row_ref, modulation_ref, *refs
):
    gather = 2 if len(refs) > 5 else 0
    refs = list(refs)
    sources = [refs.pop(0) for _ in range(gather)]
    gathered_ref, mod_ref = refs.pop(0), refs.pop(0)
    targets = [refs.pop(0) for _ in range(gather)]
    part_ref, land_ref, semaphores, *space = refs
    device, rank, dp, tp = place()
    me, count = device * tp + rank, dp * tp
    lines = land_ref.shape[1]
    if gather:
        here = Where()
        parts = column_parts(here, sources[0], targets[0], space[:PARTS])
        following = GatherChain(here, sources[1], targets[1], space[PARTS])
    greet_all()

    def tell(index, carry):
        peer = lax.rem(me + index, count)
        push(
            row_ref, gathered_ref.at[me], semaphores.at[0], semaphores.at[1], peer // tp, lax.rem(peer, tp)
        )
        return carry

    lax.fori_loop(1, count, tell, 0)
    gathered_ref[me] = row_ref[...]
    if gather:
        for chain in parts:
            chain.stage_line()
    wait_bytes(gathered_ref.at[pl.ds(0, count - 1)], semaphores.at[1])
    padded = modulation_ref.shape[1]
    width = dp * tp * per_device
    chosen = jnp.zeros((count, padded), jnp.float32)
    row = lax.broadcasted_iota(jnp.int32, (PAIR, padded), 0)
    column = lax.broadcasted_iota(jnp.int32, (PAIR, padded), 1)
    for index in range(width // PAIR):
        match = (row + index * PAIR == column + me * per_device) & (column < per_device)
        chosen += mm(
            gathered_ref[:, index, :].astype(jnp.bfloat16), jnp.where(match, 1.0, 0.0).astype(jnp.bfloat16)
        )
    clip = lax.broadcasted_iota(jnp.int32, (dp, count), 0)
    member = lax.broadcasted_iota(jnp.int32, (dp, count), 1)
    leaders = jnp.where(member == clip * tp, 1.0, 0.0).astype(jnp.bfloat16)
    rows = mm(leaders, chosen.astype(jnp.bfloat16)).astype(jnp.bfloat16)
    for layer in range(modulation_ref.shape[0]):
        part = mm(rows, modulation_ref[layer])
        size = part.shape[1] // PAIR
        for index in range(size):
            line = layer * size + index
            part_ref[:, line // lines, line % lines, :] = part[:, index * PAIR : (index + 1) * PAIR]

    def share(index, carry):
        peer = lax.rem(me + index, count)
        there, lane = peer // tp, lax.rem(peer, tp)
        push(part_ref.at[there, lane], land_ref.at[me], semaphores.at[2], semaphores.at[3], there, lane)
        return carry

    lax.fori_loop(1, count, share, 0)
    land_ref[me] = part_ref[device, rank]
    if gather:
        for chain in parts:
            chain.line_arrived()
            chain.stage_near()
        following.stage_line()
        for chain in parts:
            chain.stage_across()
    wait_bytes(land_ref.at[pl.ds(0, count - 1)], semaphores.at[3])
    mod_ref[rank] = jnp.sum(land_ref[...], axis=0)
    for step in range(1, tp):
        push(
            mod_ref.at[rank], mod_ref.at[rank], semaphores.at[4], semaphores.at[5], device, lax.rem(rank + step, tp)
        )
    if gather:
        for chain in parts:
            chain.stage_core()
    wait_bytes(gathered_ref.at[pl.ds(0, count - 1)], semaphores.at[0])
    wait_bytes(land_ref.at[pl.ds(0, count - 1)], semaphores.at[2])
    wait_bytes(mod_ref.at[pl.ds(0, tp - 1)], semaphores.at[5])
    wait_bytes(mod_ref.at[pl.ds(0, tp - 1)], semaphores.at[4])
    if gather:
        following.line_arrived()
        for chain in parts:
            chain.finish()
        for chain in (*parts, following):
            chain.line_left()


def enter(row, modulation, per_device, weights, collective_id):
    dp, tp = lax.axis_size("dp"), lax.axis_size("tensor")
    count = dp * tp
    lines = modulation.shape[0] * modulation.shape[2] // (tp * PAIR)
    inside = pl.BlockSpec(memory_space=pltpu.VMEM)
    job = FlowJob((), weights) if weights else Job()
    return pl.pallas_call(
        partial(entry_kernel, per_device),
        in_specs=[inside, inside] + anywhere(len(job.operands)),
        out_specs=[inside, inside] + list(job.specs),
        out_shape=[
            jax.ShapeDtypeStruct((count,) + row.shape, jnp.float32),
            jax.ShapeDtypeStruct((tp, lines, PAIR), jnp.float32),
        ] + list(job.shapes),
        scratch_shapes=[
            pltpu.VMEM((dp, tp, lines, PAIR), jnp.float32),
            pltpu.VMEM((count, lines, PAIR), jnp.float32),
            pltpu.SemaphoreType.DMA((6,)),
        ] + (GatherChain.scratch() * (PARTS + 1) if weights else []),
        compiler_params=pltpu.CompilerParams(
            collective_id=collective_id, has_side_effects=True, vmem_limit_bytes=VMEM_LIMIT
        ),
        name="enter",
    )(row, modulation, *job.operands)


def adam_update(weight, first, second, grad, rate, decay):
    first_new = BETA_ONE * first + (1.0 - BETA_ONE) * grad
    second_new = BETA_TWO * second + (1.0 - BETA_TWO) * grad * grad
    corrected = (
        first_new
        / (1.0 - BETA_ONE**STEP)
        / (jnp.sqrt(second_new / (1.0 - BETA_TWO**STEP)) + ADAM_EPS)
    )
    weight_new = weight - rate * (corrected + decay * weight)
    return (weight_new, first_new, second_new, weight_new.astype(jnp.bfloat16))


def dot32(form, left, right):
    return jnp.einsum(form, left, right, preferred_element_type=jnp.float32)


def exchange(blocks):
    return lax.all_to_all(blocks, "tensor", split_axis=0, concat_axis=0, tiled=True)


def gather_plain(shard):
    rows, width = shard.shape
    whole = lax.all_gather(shard, ("tensor", "dp"), axis=0, tiled=True)
    return whole.reshape(-1, lax.axis_size("dp") * rows, width)


def scatter_plain(grads):
    kinds, ranks, width, cols = grads.shape
    flat = grads.reshape(kinds, ranks * width, cols)
    summed = lax.psum_scatter(flat, ("tensor", "dp"), scatter_dimension=1, tiled=True)
    return summed.astype(jnp.float32)


def per_device(
    clips, cotangent, timesteps, labels, time_table, class_table,
    attention_weights, attention_first, attention_second,
    ffn_weights, ffn_first, ffn_second,
    modulation_weights, modulation_first, modulation_second,
    bias_vectors, bias_first, bias_second,
):
    layers, kinds, rows, cols = attention_weights.shape
    _, frames, patches, width = clips.shape
    mod_rows = modulation_weights.shape[1]
    bias_cols = bias_vectors.shape[1]
    dp, tp = lax.axis_size("dp"), lax.axis_size("tensor")
    position = lax.axis_index("dp") * tp + lax.axis_index("tensor")
    tokens = frames * patches
    strip = patches // (tp * frames)
    blocks = (tp, frames, frames * strip, width)
    pieces = (tp * frames, frames, strip, width)

    embed = time_table[timesteps] + class_table[labels]
    cond_act = jax.nn.silu(embed).astype(jnp.bfloat16)
    fused = rows % 16 == 0
    shards = [
        (
            pack_heads(attention_weights[layer].astype(jnp.bfloat16)),
            ffn_weights[layer, 0].astype(jnp.bfloat16),
            ffn_weights[layer, 1].astype(jnp.bfloat16),
        )
        for layer in range(layers)
    ]
    low = bias_vectors.astype(jnp.bfloat16).reshape(-1)
    row = jnp.concatenate([cond_act[0], low]).astype(jnp.float32)
    row = jnp.pad(row, (0, -row.shape[0] % 1024)).reshape(-1, 128)
    modulation_low = modulation_weights.astype(jnp.bfloat16)
    modulation_low = jnp.pad(modulation_low, ((0, 0), (0, -mod_rows % 32), (0, 0)))
    gathered, mod, *begun = enter(row, modulation_low, mod_rows, shards[0][:2] if fused else None, 0)
    gathered = gathered.reshape(dp * tp, -1)
    cond_all = gathered[::tp, :width].astype(jnp.bfloat16)
    bias_low = gathered[:, width : width + layers * bias_cols].reshape(dp * tp, layers, bias_cols)
    bias_low = bias_low.transpose(1, 0, 2).reshape(layers, -1)
    cond_rows = lax.dynamic_slice_in_dim(cond_all, position * mod_rows, mod_rows, axis=1)
    cond_rows = jnp.pad(cond_rows, ((0, 0), (0, -mod_rows % 32)))
    mod = mod.reshape(layers, -1)
    mod_width = mod.shape[-1]
    mod = (mod + bias_low[:, -mod_width:]).reshape(layers, 6, width)
    hidden_width = bias_low.shape[1] - mod_width - 4 * width
    bias_up = bias_low[:, 3 * width : 3 * width + hidden_width].reshape(layers, tp, 1, -1)
    bias_out = bias_low[:, None, 2 * width : 3 * width]
    bias_down = bias_low[:, None, 3 * width + hidden_width : 4 * width + hidden_width]
    bias_project = [
        pack_bias(bias_low[layer, :width], bias_low[layer, width : 2 * width], tp) for layer in range(layers)
    ]

    by_patch = lambda v: v.reshape(frames, tp * frames, strip, width).transpose(1, 0, 2, 3)
    first = clips[0].reshape(1, frames, patches, width)

    whole = lambda weight: weight.reshape(tp, width, -1)
    attend = lambda layer, weight, stream, stride, *more: attention_forward(
        whole(weight), stream, mod[layer], bias_project[layer], bias_out[layer], stride, *more
    )
    expand = lambda layer, up, down, middle, *more: ffn_forward(
        whole(up), whole(down), middle.reshape(tokens, width), mod[layer], bias_down[layer], bias_up[layer], *more
    )
    if fused:
        attention_a, up_a = begun
        *heads_a, middle_a, up_a, down_a, attention_b = attend(
            0, attention_a, first, 0, [FlowJob([up_a], [shards[1][0]], None, [shards[0][2]])], 1
        )
        hidden_a, pushed_a, second, attention_b, up_b, down_b = expand(
            0, up_a, down_a, middle_a, StreamJob(blocks, frames),
            [FlowJob([attention_b], [shards[1][2]], dp // 8, [shards[1][1]])], 2, True,
        )
        *heads_b, middle_b, down_b = attend(1, attention_b, second, strip, [FlowJob([down_b], [])], 3)
        cot = cotangent.reshape(frames, tp, frames, strip, width)
        hidden_b, pushed_b, result, cot = expand(
            1, up_b, down_b, middle_b, None, [SwapJob(cot, False)], 4, True
        )
        attention_a, up_a, down_a = whole(attention_a), whole(up_a), whole(down_a)
        attention_b, up_b, down_b = whole(attention_b), whole(up_b), whole(down_b)
    else:
        (attention_a, up_a, down_a), (attention_b, up_b, down_b) = [[gather_plain(v) for v in group] for group in shards]
        *heads_a, middle_a = attend(0, attention_a, first, 0)
        hidden_a, pushed_a, second = expand(0, up_a, down_a, middle_a)
        second = exchange(by_patch(second).reshape(blocks))
        *heads_b, middle_b = attend(1, attention_b, second, strip)
        hidden_b, pushed_b, result = expand(1, up_b, down_b, middle_b)
        cot = exchange(by_patch(cotangent[0]).reshape(blocks))
    middle_a, middle_b = middle_a.reshape(tokens, width), middle_b.reshape(tokens, width)
    cot = cot.reshape(tokens, width)

    if fused:
        ffn_cores = lambda: CoreJob(2, width, ffn_weights.shape[-1])
        head_cores = lambda: CoreJob(1, width, kinds * cols)
        grad, *sums_b, kept, result = ffn_backward(
            up_b, down_b, cot, middle_b, pushed_b, hidden_b, mod[1], ffn_cores(),
            [SwapJob(result.reshape(tp, frames, frames, strip, width), True)], 5,
        )
        output = result.reshape(clips.shape)
        ffn_grad = kept
        *more_b, grad, kept, line_up = attention_backward(
            attention_b, grad.reshape(blocks), second, heads_b, mod[1], strip,
            StreamJob(blocks, 0), head_cores(), [ScatterJob([(ffn_grad, 0)], 3 * dp // 8)], 6,
        )
        waiting = [(ffn_grad, 1), (kept, 0)]
        grad, *sums_a, kept, done_up, line_b = ffn_backward(
            up_a, down_a, grad.reshape(pieces), middle_a, pushed_a, hidden_a, mod[0], ffn_cores(),
            [LineJob(line_up), ScatterJob(waiting, dp // 4)], 7,
        )
        ffn_grad = kept
        grad, *more_a, kept, done_b, line_ffn_a, done_up_a = attention_backward(
            attention_a, grad.reshape(first.shape), first, heads_a, mod[0], 0, None, head_cores(),
            [LineJob(line_b), ScatterJob([(ffn_grad, 0), (ffn_grad, 1)], dp // 4, True)], 8,
        )
        packed_a = kept
        done = (done_up_a, done_up, done_b[:1], done_b[1:])
    else:
        result = exchange(result.reshape(blocks)).reshape(pieces)
        output = result.transpose(1, 0, 2, 3).reshape(clips.shape)
        grad, *sums_b, ffn_grad = ffn_backward(up_b, down_b, cot, middle_b, pushed_b, hidden_b, mod[1])
        done_ffn_b = scatter_plain(ffn_grad)
        grad, packed_b, *more_b = attention_backward(
            attention_b, grad.reshape(blocks), second, heads_b, mod[1], strip
        )
        done_b = scatter_plain(packed_b[None])
        grad = exchange(grad.astype(jnp.bfloat16))
        grad, *sums_a, ffn_grad = ffn_backward(up_a, down_a, grad.reshape(pieces), middle_a, pushed_a, hidden_a, mod[0])
        done_ffn_a = scatter_plain(ffn_grad)
        grad, packed_a, *more_a = attention_backward(attention_a, grad.reshape(first.shape), first, heads_a, mod[0], 0)
        done_a = scatter_plain(packed_a[None])
    input_grad = grad.reshape(clips.shape)

    def gather_small(more, sums):
        attention_sums, project_sum = more
        up_sum, low_sums = sums
        return jnp.concatenate(
            [*unpack_bias(project_sum), attention_sums[0], up_sum.reshape(-1), low_sums[0],
             attention_sums[1:].reshape(-1), low_sums[1:].reshape(-1)]
        )

    small = jnp.stack([gather_small(more_a, sums_a), gather_small(more_b, sums_b)])
    token_width = small.shape[1] - mod_width
    *summed, small, grad_act = leave(
        small.reshape(tp, -1, 128), modulation_low, token_width,
        *((packed_a, line_ffn_a, done) if fused else (None, None, None)), 9,
    )
    small = small.transpose(1, 0, 2, 3).reshape(dp, layers, -1)
    grad_mod_low = small[..., token_width:].astype(jnp.bfloat16)
    grad_bias_all = jnp.concatenate(
        [small[..., :token_width], grad_mod_low.astype(jnp.float32)], axis=-1
    ).sum(axis=0)
    grad_bias = lax.dynamic_slice_in_dim(grad_bias_all, position * bias_cols, bias_cols, axis=1)
    grad_mod_weight = dot32("ck,cle->lke", cond_rows, grad_mod_low)[:, :mod_rows]
    grad_act = lax.dynamic_index_in_dim(
        grad_act[:, :, :mod_rows], lax.axis_index("dp"), axis=1, keepdims=False
    )
    if fused:
        grad_attention, grad_ffn = summed
    else:
        grad_attention = jnp.stack([jnp.stack(unpack_heads(done[0])) for done in (done_a, done_b)])
        grad_ffn = jnp.stack([done_ffn_a, done_ffn_b])
    silu_value, silu_pull = jax.vjp(jax.nn.silu, embed)
    cond_grad = silu_pull(grad_act.reshape(1, width))[0]

    return (output, input_grad, cond_grad) + (
        adam_update(attention_weights, attention_first, attention_second, grad_attention, MATRIX_RATE, MATRIX_DECAY)
        + adam_update(ffn_weights, ffn_first, ffn_second, grad_ffn, MATRIX_RATE, MATRIX_DECAY)
        + adam_update(modulation_weights, modulation_first, modulation_second, grad_mod_weight, MATRIX_RATE, MATRIX_DECAY)
        + adam_update(bias_vectors, bias_first, bias_second, grad_bias, VECTOR_RATE, 0.0)
    )


def solution(mesh):
    tokens = P("dp", "tensor", None, None)
    matrix = P(None, None, "dp", "tensor")
    modulation = P(None, BOTH, None)
    vector = P(None, BOTH)
    return jax.shard_map(
        per_device,
        mesh=mesh,
        in_specs=(tokens, tokens, P("dp"), P("dp"), P(), P())
        + (matrix,) * 6 + (modulation,) * 3 + (vector,) * 3,
        out_specs=(tokens, tokens, P("dp", None)) + (matrix,) * 8 + (modulation,) * 4 + (vector,) * 4,
        check_vma=False,
    )
```

```python
from functools import partial

import jax
import jax.numpy as jnp
from jax import lax
from jax.experimental import pallas as pl
from jax.experimental.pallas import tpu as pltpu
from jax.sharding import PartitionSpec as P

HD = 64
PAIR = 128
PARTS = 3
STEP = 10
BETA_ONE = 0.9
BETA_TWO = 0.999
ADAM_EPS = 1e-08
MATRIX_RATE = 0.04
VECTOR_RATE = 0.2
MATRIX_DECAY = 0.1
NORM_EPS = 1e-06
GELU_A = (2.0 / 3.141592653589793) ** 0.5
GELU_B = 0.044715
BLOCKED = -1e30
VMEM_LIMIT = 60 * 1024 * 1024
BOTH = ("dp", "tensor")


def mm(left, right, dims=((1,), (0,))):
    return lax.dot_general(left, right, (dims, ((), ())), preferred_element_type=jnp.float32)


def norm_parts(value):
    average = jnp.mean(value, axis=-1, keepdims=True)
    centred = value - average
    spread = jnp.mean(centred * centred, axis=-1, keepdims=True)
    inverse = lax.rsqrt(spread + NORM_EPS)
    return centred * inverse, inverse


def norm_back(grad, shape, inverse):
    first = jnp.mean(grad, axis=-1, keepdims=True)
    second = jnp.mean(grad * shape, axis=-1, keepdims=True)
    return inverse * (grad - first - shape * second)


def rows_of(ref):
    value = ref[...]
    return value.reshape(-1, value.shape[-1])


def put(ref, value):
    ref[...] = value.reshape(ref.shape).astype(ref.dtype)


def add_rows(ref, index, value):
    ref[pl.ds(index, 1), :] += jnp.sum(value, axis=0, keepdims=True)


def half_masks(rows):
    lane = lax.broadcasted_iota(jnp.int32, (rows, PAIR), 1)
    return lane < HD


def same_patch(tokens, stride):
    row = lax.broadcasted_iota(jnp.int32, (tokens, tokens), 0)
    column = lax.broadcasted_iota(jnp.int32, (tokens, tokens), 1)
    return lax.rem(row, stride) == lax.rem(column, stride)


def swap_halves(value):
    return pltpu.roll(value, HD, 1)


def start_loads(source, target, semaphores):
    for rank in range(target.shape[0]):
        pltpu.make_async_copy(source.at[rank], target.at[rank], semaphores.at[rank]).start()


def wait_loads(target, semaphores, rank):
    pltpu.make_async_copy(target.at[rank], target.at[rank], semaphores.at[rank]).wait()


def softmax_rows(scores, axis):
    raised = jnp.exp(scores - jnp.max(scores, axis=axis, keepdims=True))
    return raised * (1.0 / jnp.sum(raised, axis=axis, keepdims=True))


def attention_forward_kernel(
    stride, hook, source, stream_ref, mod_ref, bias_ref, bias_out_ref,
    project_ref, mixed_ref, branch_ref, middle_ref, weight_ref, semaphores,
):
    ranks = weight_ref.shape[0]

    @pl.when(pl.program_id(0) == 0)
    def _():
        start_loads(source, weight_ref, semaphores)

    stream = rows_of(stream_ref).astype(jnp.float32)
    tokens, width = stream.shape
    shape, _ = norm_parts(stream)
    normed = (shape * (1.0 + mod_ref[1:2]) + mod_ref[0:1]).astype(jnp.bfloat16)
    lower = half_masks(tokens)
    allowed = same_patch(tokens, stride) if stride else None

    @pl.when(pl.program_id(0) == 0)
    def _():
        for rank in range(ranks):
            wait_loads(weight_ref, semaphores, rank)

    def mix(heads):
        scores = [mm(chosen.astype(jnp.bfloat16), key, ((1,), (1,))) for chosen, key, _ in heads]
        outs = []
        for score, (_, _, value) in zip(scores, heads):
            if stride:
                score = jnp.where(allowed, score, BLOCKED)
            outs.append(mm(softmax_rows(score, -1).astype(jnp.bfloat16), value))
        return outs

    branch = None
    for rank in range(ranks):
        hook(rank)
        project = (mm(normed, weight_ref[rank, :, : 5 * PAIR]) + bias_ref[rank]).astype(jnp.bfloat16)
        project_ref[rank] = project.reshape(project_ref.shape[1:])
        query = project[:, :PAIR].astype(jnp.float32) * HD**-0.5
        key, value = project[:, PAIR : 2 * PAIR], project[:, 2 * PAIR : 3 * PAIR]
        both = project[:, 3 * PAIR : 4 * PAIR].astype(jnp.float32)
        first, second, last = mix(
            [
                (jnp.where(lower, query, 0.0), key, value),
                (jnp.where(lower, 0.0, query), key, value),
                (
                    jnp.where(lower, both * HD**-0.5, 0.0),
                    swap_halves(both).astype(jnp.bfloat16),
                    project[:, 4 * PAIR : 5 * PAIR],
                ),
            ]
        )
        mixed = jnp.concatenate(
            [jnp.where(lower, 0.0, swap_halves(last)), jnp.where(lower, first, second)], axis=1
        ).astype(jnp.bfloat16)
        mixed_ref[rank] = mixed.reshape(mixed_ref.shape[1:])
        term = mm(mixed, weight_ref[rank, :, 4 * PAIR :], ((1,), (1,)))
        branch = term if branch is None else branch + term
    branch = branch + bias_out_ref[...]
    put(branch_ref, branch)
    put(middle_ref, stream + mod_ref[2:3] * branch)


def gelu_parts(value):
    square = value * value
    bent = jnp.tanh(value * (GELU_A + (GELU_A * GELU_B) * square))
    half = 0.5 * (1.0 + bent)
    slope = half + (0.5 * value) * (1.0 - bent * bent) * (GELU_A + (3.0 * GELU_A * GELU_B) * square)
    return value * half, slope


def turn_of(rank):
    core = lax.rem(lax.axis_index("tensor"), 2)
    return rank + (1 - core) * (1 - 2 * (rank % 2))


def ffn_forward_kernel(
    stream, turned, hook, up_source, down_source, middle_ref, mod_ref, bias_ref, bias_up_ref, hidden_ref, branch_ref, *rest
):
    if stream is None:
        result_ref, *rest = rest
    up_ref, down_ref, up_semaphores, down_semaphores = rest
    step = pl.program_id(0)
    ranks = up_ref.shape[0]

    @pl.when(step == 0)
    def _():
        start_loads(up_source, up_ref, up_semaphores)
        start_loads(down_source, down_ref, down_semaphores)

    middle = middle_ref[...]
    shape, _ = norm_parts(middle)
    second = (shape * (1.0 + mod_ref[4:5]) + mod_ref[3:4]).astype(jnp.bfloat16)

    @pl.when(step == 0)
    def _():
        for rank in range(ranks):
            wait_loads(up_ref, up_semaphores, rank)
            wait_loads(down_ref, down_semaphores, rank)

    down = None
    for rank in range(ranks):
        hook(rank)
        hidden = mm(second, up_ref[rank]) + bias_up_ref[rank]
        hidden_ref[turn_of(rank) if turned else rank] = hidden.astype(jnp.bfloat16)
        active, _ = gelu_parts(hidden)
        part = mm(active.astype(jnp.bfloat16), down_ref[rank], ((1,), (1,)))
        down = part if down is None else down + part
    down = down + bias_ref[...]
    branch_ref[...] = down.astype(jnp.bfloat16)
    result = middle + mod_ref[5:6] * down
    if stream is None:
        result_ref[...] = result.astype(result_ref.dtype)
    else:
        stream.put(step, result)


def load_rows(ref, index, chunk):
    if len(ref.shape) == 2:
        return ref[index * chunk : (index + 1) * chunk, :].astype(jnp.float32)
    blocks, _, strip, width = ref.shape
    frames = chunk // (blocks * strip)
    parts = [ref[:, index * frames + frame].reshape(blocks * strip, width) for frame in range(frames)]
    return jnp.concatenate(parts, axis=0).astype(jnp.float32)


def ffn_backward_kernel(
    split, cores, hook, up_source, down_source, grad_ref, middle_ref, branch_ref, hidden_ref, mod_ref,
    grad_middle_ref, up_sum_ref, sums_ref, *refs
):
    if cores is None:
        weight_grad_ref, *refs = refs
    (up_ref, down_ref, up_semaphores, down_semaphores,
     second_ref, low_ref, low_across_ref, active_ref, slope_ref, total_ref) = refs
    step = pl.program_id(0)
    rank = step if cores is None else cores.rank(step)
    tokens, width = middle_ref.shape
    chunk = tokens // split

    @pl.when(step == 0)
    def _():
        start_loads(up_source, up_ref, up_semaphores)
        start_loads(down_source, down_ref, down_semaphores)
        sums_ref[...] = jnp.zeros_like(sums_ref)
        up_sum_ref[...] = jnp.zeros_like(up_sum_ref)
        for index in range(split):
            rows = slice(index * chunk, (index + 1) * chunk)
            grad = load_rows(grad_ref, index, chunk)
            low = (mod_ref[5:6] * grad).astype(jnp.bfloat16)
            low_ref[rows, :] = low
            low_across_ref[:, rows] = low.T
            add_rows(sums_ref, 0, low.astype(jnp.float32))
            add_rows(sums_ref, 3, grad * branch_ref[rows, :].astype(jnp.float32))
            shape, _ = norm_parts(middle_ref[rows, :])
            second = (shape * (1.0 + mod_ref[4:5]) + mod_ref[3:4]).astype(jnp.bfloat16)
            second_ref[:, rows] = second.T

    wait_loads(up_ref, up_semaphores, rank)
    wait_loads(down_ref, down_semaphores, rank)

    for index in range(split):
        hook(index)
        rows = slice(index * chunk, (index + 1) * chunk)
        active, slope = gelu_parts(hidden_ref[0, rows, :].astype(jnp.float32))
        active_ref[rows, :] = active.astype(jnp.bfloat16)
        low = (mm(low_ref[rows, :], down_ref[rank]) * slope).astype(jnp.bfloat16)
        slope_ref[rows, :] = low
        up_sum_ref[rank] += jnp.sum(low.astype(jnp.float32), axis=0, keepdims=True)
        part = mm(low, up_ref[rank], ((1,), (1,)))
        total_ref[rows, :] = jnp.where(step == 0, 0.0, total_ref[rows, :]) + part
    hook(2)
    make_up = lambda: mm(second_ref[...], slope_ref[...])
    if cores is None:
        weight_grad_ref[0, 0] = make_up().astype(jnp.bfloat16)
    else:
        cores.put(step, 0, make_up)
        cores.send(step, 0)
    hook(3)
    make_down = lambda: mm(low_across_ref[...], active_ref[...])
    if cores is None:
        weight_grad_ref[1, 0] = make_down().astype(jnp.bfloat16)
    else:
        cores.put(step, 1, make_down)
        cores.send(step, 1)

    @pl.when(step == pl.num_programs(0) - 1)
    def _():
        for index in range(split):
            rows = slice(index * chunk, (index + 1) * chunk)
            shape, inverse = norm_parts(middle_ref[rows, :])
            grad = total_ref[rows, :]
            add_rows(sums_ref, 1, grad)
            add_rows(sums_ref, 2, grad * shape)
            back = norm_back(grad * (1.0 + mod_ref[4:5]), shape, inverse)
            grad_middle_ref[rows, :] = load_rows(grad_ref, index, chunk) + back


def attention_backward_kernel(
    stride, swap, cores, hook, source, grad_ref, stream_ref, project_ref, mixed_ref, branch_ref, mod_ref, *refs
):
    if swap is None:
        grad_stream_ref, *refs = refs
    if cores is None:
        weight_grad_ref, *refs = refs
    (sums_ref, project_sum_ref,
     weight_ref, semaphores, left_ref, right_ref, outer_ref) = refs
    step = pl.program_id(0)
    ranks = weight_ref.shape[0]

    @pl.when(step == 0)
    def _():
        start_loads(source, weight_ref, semaphores)
        sums_ref[...] = jnp.zeros_like(sums_ref)
        project_sum_ref[...] = jnp.zeros_like(project_sum_ref)

    grad_middle = rows_of(grad_ref)
    tokens, width = grad_middle.shape
    stream = rows_of(stream_ref).astype(jnp.float32)
    shape, inverse = norm_parts(stream)
    rows = pl.ds(pl.multiple_of(step * tokens, tokens), tokens)
    normed = (shape * (1.0 + mod_ref[1:2]) + mod_ref[0:1]).astype(jnp.bfloat16)
    low = (mod_ref[2:3] * grad_middle).astype(jnp.bfloat16)
    left_ref[0, :, rows] = normed.T
    left_ref[1, :, rows] = low.T
    add_rows(sums_ref, 0, low.astype(jnp.float32))
    add_rows(sums_ref, 3, grad_middle * rows_of(branch_ref).astype(jnp.float32))
    lower = half_masks(tokens)
    allowed = same_patch(tokens, stride) if stride else None
    scale = HD**-0.5

    @pl.when(step == 0)
    def _():
        for rank in range(ranks):
            wait_loads(weight_ref, semaphores, rank)

    def score_grads(heads):
        scores = [mm(key, chosen.astype(jnp.bfloat16), ((1,), (1,))) for chosen, key, _, _ in heads]
        grad_probs = [mm(value, taken.astype(jnp.bfloat16), ((1,), (1,))) for _, _, value, taken in heads]
        outs = []
        for score, grad_prob in zip(scores, grad_probs):
            if stride:
                score = jnp.where(allowed, score, BLOCKED)
            probs = softmax_rows(score, 0)
            inner = jnp.sum(grad_prob * probs, axis=0, keepdims=True)
            outs.append((probs.astype(jnp.bfloat16), (probs * (grad_prob - inner)).astype(jnp.bfloat16)))
        return outs

    grad_normed = None
    for rank in range(ranks):
        hook(rank)
        project = project_ref[rank].reshape(tokens, 5 * PAIR)
        mixed = mixed_ref[rank].reshape(tokens, 2 * PAIR)
        outer_ref[rank, rows, :] = mixed
        grad_mixed = mm(low, weight_ref[rank, :, 4 * PAIR :]).astype(jnp.bfloat16)
        query, key, value = (project[:, n * PAIR : (n + 1) * PAIR] for n in range(3))
        query_wide = query.astype(jnp.float32) * scale
        pair = grad_mixed[:, PAIR:]
        pair_wide = pair.astype(jnp.float32)
        both = project[:, 3 * PAIR : 4 * PAIR].astype(jnp.float32)
        swapped = swap_halves(both).astype(jnp.bfloat16)
        single = swap_halves(grad_mixed[:, :PAIR].astype(jnp.float32))
        heads = [
            (jnp.where(keep, query_wide, 0.0), key, value, jnp.where(keep, pair_wide, 0.0)) for keep in (lower, ~lower)
        ]
        heads.append(
            (jnp.where(lower, both * scale, 0.0), swapped, project[:, 4 * PAIR :], jnp.where(lower, single, 0.0))
        )
        solved = score_grads(heads)
        outs = [
            (mm(grad_scores, key, ((0,), (0,))), mm(grad_scores, query), mm(probs, pair))
            for probs, grad_scores in solved[:2]
        ]
        parts = [
            jnp.where(lower, one, two) * factor
            for one, two, factor in zip(outs[0], outs[1], (scale, scale, 1.0))
        ]
        probs, grad_scores = solved[2]
        parts.append(
            jnp.where(lower, mm(grad_scores, swapped, ((0,), (0,))), mm(grad_scores, swapped)) * scale
        )
        parts.append(jnp.where(lower, mm(probs, single.astype(jnp.bfloat16)), 0.0))
        whole = jnp.concatenate(parts, axis=1).astype(jnp.bfloat16)
        right_ref[rank, rows, :] = whole
        add_rows(project_sum_ref, rank, whole.astype(jnp.float32))
        term = mm(whole, weight_ref[rank, :, : 5 * PAIR], ((1,), (1,)))
        grad_normed = term if grad_normed is None else grad_normed + term
    add_rows(sums_ref, 1, grad_normed)
    add_rows(sums_ref, 2, grad_normed * shape)
    back = norm_back(grad_normed * (1.0 + mod_ref[1:2]), shape, inverse)
    if swap is None:
        put(grad_stream_ref, grad_middle + back)
    else:
        swap.put(step, grad_middle + back)

    @pl.when(step == pl.num_programs(0) - 1)
    def _():
        def weights(turn, carry):
            rank = turn if cores is None else cores.rank(turn)
            inside = mm(left_ref[0], right_ref[rank])
            outside = mm(left_ref[1], outer_ref[rank])
            made = jnp.concatenate(
                [inside[:, : 4 * PAIR], inside[:, 4 * PAIR :] + outside[:, :PAIR], outside[:, PAIR:]], axis=1
            )
            if cores is None:
                weight_grad_ref[rank] = made.astype(jnp.bfloat16)
            else:
                cores.put(turn, 0, lambda: made)
                cores.send(turn, 0)
            return carry

        lax.fori_loop(0, ranks, weights, 0)


def fixed(shape):
    return pl.BlockSpec(shape, lambda step: (0,) * len(shape), pipeline_mode=pl.Buffered(1))


def cost(flops, moved, raised=0):
    return pl.CostEstimate(flops=int(flops), bytes_accessed=int(moved), transcendentals=int(raised))


def group_spec(shape):
    return pl.BlockSpec((shape[0], 1, shape[2], shape[3]), lambda step: (0, step, 0, 0))


def rank_spec(shape):
    return pl.BlockSpec((shape[0], shape[1], 1) + shape[3:], lambda step: (0, 0, step, 0, 0))


def attention_forward(weight, stream, mod, bias, bias_out, stride, jobs=(), collective_id=None):
    shape = stream.shape
    width = shape[-1]
    ranks = bias.shape[0]
    tokens = shape[0] * shape[1] * shape[2]
    spec = group_spec(shape)
    low = jax.ShapeDtypeStruct(shape, jnp.bfloat16)
    wide = jax.ShapeDtypeStruct(shape, jnp.float32)
    project = jax.ShapeDtypeStruct((ranks,) + shape[:3] + (5 * PAIR,), jnp.bfloat16)
    mixed = jax.ShapeDtypeStruct((ranks,) + shape[:3] + (2 * PAIR,), jnp.bfloat16)
    return call(
        partial(attention_forward_kernel, stride),
        shape[1],
        [weight, stream, mod, bias, bias_out],
        anywhere(1) + [spec, fixed(mod.shape), fixed(bias.shape), fixed(bias_out.shape)],
        [project, mixed, low, wide],
        [rank_spec(project.shape), rank_spec(mixed.shape), spec, spec],
        [pltpu.VMEM((ranks, width, 6 * PAIR), jnp.bfloat16), pltpu.SemaphoreType.DMA((ranks,))],
        jobs,
        collective_id,
        cost(8 * tokens * width * width * 1.5, tokens * width * 16),
        "attention_forward",
    )


def ffn_weights_scratch(ranks, width, part):
    return [
        pltpu.VMEM((ranks, width, part), jnp.bfloat16),
        pltpu.VMEM((ranks, width, part), jnp.bfloat16),
        pltpu.SemaphoreType.DMA((ranks,)),
        pltpu.SemaphoreType.DMA((ranks,)),
    ]


def ffn_forward(up, down, middle, mod, bias_down, bias_up, stream=None, jobs=(), collective_id=None, turned=False):
    tokens, width = middle.shape
    ranks, _, part = bias_up.shape
    steps = 4
    chunk = tokens // steps
    block = pl.BlockSpec((chunk, width), lambda step: (step, 0))
    result = [jax.ShapeDtypeStruct((tokens, width), jnp.bfloat16)] if stream is None else []
    return call(
        partial(ffn_forward_kernel, stream, turned),
        steps,
        [up, down, middle, mod, bias_down, bias_up],
        anywhere(2) + [block, fixed(mod.shape), fixed(bias_down.shape), fixed(bias_up.shape)],
        [
            jax.ShapeDtypeStruct((ranks, tokens, part), jnp.bfloat16),
            jax.ShapeDtypeStruct((tokens, width), jnp.bfloat16),
        ] + result,
        [pl.BlockSpec((ranks, chunk, part), lambda step: (0, step, 0)), block] + [block] * len(result),
        ffn_weights_scratch(ranks, width, part),
        ([] if stream is None else [stream]) + list(jobs),
        collective_id,
        cost(4.8 * tokens * width * ranks * part, tokens * width * 14, tokens * ranks * part),
        "ffn_forward",
    )


def ffn_backward(up, down, grad, middle, branch, hidden, mod, cores=None, jobs=(), collective_id=None):
    tokens, width = middle.shape
    ranks, _, part = hidden.shape
    whole = fixed((tokens, width))
    made = [jax.ShapeDtypeStruct((2, ranks, width, part), jnp.bfloat16)] if cores is None else []
    return call(
        partial(ffn_backward_kernel, 2, cores),
        ranks,
        [up, down, grad, middle, branch, hidden, mod],
        anywhere(2) + [
            fixed(grad.shape), whole, whole,
            pl.BlockSpec((1, tokens, part), lambda step: (step, 0, 0)),
            fixed(mod.shape),
        ],
        [
            jax.ShapeDtypeStruct((tokens, width), jnp.float32),
            jax.ShapeDtypeStruct((ranks, 1, part), jnp.float32),
            jax.ShapeDtypeStruct((4, width), jnp.float32),
        ] + made,
        [
            whole,
            fixed((ranks, 1, part)),
            fixed((4, width)),
        ] + [pl.BlockSpec((2, 1, width, part), lambda step: (0, step, 0, 0))] * len(made),
        ffn_weights_scratch(ranks, width, part) + [
            pltpu.VMEM((width, tokens), jnp.bfloat16),
            pltpu.VMEM((tokens, width), jnp.bfloat16),
            pltpu.VMEM((width, tokens), jnp.bfloat16),
            pltpu.VMEM((tokens, part), jnp.bfloat16),
            pltpu.VMEM((tokens, part), jnp.bfloat16),
            pltpu.VMEM((tokens, width), jnp.float32),
        ],
        ([] if cores is None else [cores]) + list(jobs),
        collective_id,
        cost(9.6 * tokens * width * ranks * part, tokens * width * 20, tokens * ranks * part),
        "ffn_backward",
    )


def attention_backward(weight, grad, stream, saved, mod, stride, swap=None, cores=None, jobs=(), collective_id=None):
    project, mixed, branch = saved
    shape = stream.shape
    width = shape[-1]
    ranks = project.shape[0]
    tokens = shape[0] * shape[1] * shape[2]
    spec = group_spec(shape)
    result = [jax.ShapeDtypeStruct(shape, jnp.float32)] if swap is None else []
    made = [jax.ShapeDtypeStruct((ranks, width, 6 * PAIR), jnp.bfloat16)] if cores is None else []
    return call(
        partial(attention_backward_kernel, stride, swap, cores),
        shape[1],
        [weight, grad, stream, project, mixed, branch, mod],
        anywhere(1) + [
            spec, spec, rank_spec(project.shape), rank_spec(mixed.shape), spec, fixed(mod.shape),
        ],
        result + made + [
            jax.ShapeDtypeStruct((4, width), jnp.float32),
            jax.ShapeDtypeStruct((ranks, 5 * PAIR), jnp.float32),
        ],
        [spec] * len(result) + [fixed((ranks, width, 6 * PAIR))] * len(made) + [
            fixed((4, width)), fixed((ranks, 5 * PAIR)),
        ],
        [
            pltpu.VMEM((ranks, width, 6 * PAIR), jnp.bfloat16),
            pltpu.SemaphoreType.DMA((ranks,)),
            pltpu.VMEM((2, width, tokens), jnp.bfloat16),
            pltpu.VMEM((ranks, tokens, 5 * PAIR), jnp.bfloat16),
            pltpu.VMEM((ranks, tokens, 2 * PAIR), jnp.bfloat16),
        ],
        [job for job in (swap, cores) if job is not None] + list(jobs),
        collective_id,
        cost(16 * tokens * width * width * 1.5, tokens * width * 20),
        "attention_backward",
    )


def pack_heads(block):
    query, key, value, outer = block
    return jnp.concatenate(
        [query[:, :PAIR], key[:, :PAIR], value[:, :PAIR], query[:, PAIR:], key[:, PAIR:],
         value[:, PAIR:], outer[:, PAIR:], outer[:, :PAIR]], axis=1
    )


def unpack_heads(packed):
    part = lambda start, size: packed[:, start : start + size]
    join = lambda first, last: jnp.concatenate([part(first, PAIR), part(last, HD)], axis=1)
    return [join(0, 3 * PAIR), join(PAIR, 3 * PAIR + HD), join(2 * PAIR, 4 * PAIR), join(5 * PAIR, 4 * PAIR + HD)]


def pack_bias(query, value, ranks):
    query, value = query.reshape(ranks, -1), value.reshape(ranks, -1)
    none = jnp.zeros((ranks, PAIR), query.dtype)
    return jnp.concatenate(
        [query[:, :PAIR], none, value[:, :PAIR], query[:, PAIR:], none[:, :HD], value[:, PAIR:], none[:, :HD]],
        axis=1,
    )[:, None]


def unpack_bias(sums):
    query = jnp.concatenate([sums[:, :PAIR], sums[:, 3 * PAIR : 3 * PAIR + HD]], axis=1)
    value = jnp.concatenate([sums[:, 2 * PAIR : 3 * PAIR], sums[:, 4 * PAIR : 4 * PAIR + HD]], axis=1)
    return query.reshape(-1), value.reshape(-1)


def place():
    return lax.axis_index("dp"), lax.axis_index("tensor"), lax.axis_size("dp"), lax.axis_size("tensor")


def greet_all():
    device, rank, dp, tp = place()
    me, count = device * tp + rank, dp * tp
    barrier = pltpu.get_barrier_semaphore()

    def greet(index, carry):
        peer = lax.rem(me + index, count)
        pl.semaphore_signal(
            barrier, inc=1, device_id=(peer // tp, lax.rem(peer, tp)), device_id_type=pl.DeviceIdType.MESH
        )
        return carry

    lax.fori_loop(1, count, greet, 0)
    pl.semaphore_wait(barrier, count - 1)


def push(source, target, send, receive, device, rank):
    pltpu.make_async_remote_copy(
        src_ref=source, dst_ref=target, send_sem=send, recv_sem=receive,
        device_id=(device, rank), device_id_type=pl.DeviceIdType.MESH,
    ).start()


def wait_bytes(ref, semaphore):
    pltpu.make_async_copy(ref, ref, semaphore).wait()


class Where:
    def __init__(self):
        device, rank = lax.axis_index("dp"), lax.axis_index("tensor")
        self.count = lax.axis_size("dp") // 2
        self.device, self.rank = device, rank
        self.far, self.side = device // 2, lax.rem(device, 2)
        self.row, self.core = rank // 2, lax.rem(rank, 2)
        self.other_side = self.far * 2 + 1 - self.side
        self.other_row = (1 - self.row) * 2 + self.core
        self.other_core = self.row * 2 + 1 - self.core

    def ahead(self, step):
        return lax.rem(self.far + step, self.count)

    def line(self, step):
        return self.ahead(step) * 2 + self.side


def greet_neighbours(here):
    barrier = pltpu.get_barrier_semaphore()
    peers = [(here.other_side, here.rank), (here.device, here.other_row), (here.device, here.other_core)]
    peers += [(here.line(step), here.rank) for step in range(1, here.count)]
    for peer in peers:
        pl.semaphore_signal(barrier, inc=1, device_id=peer, device_id_type=pl.DeviceIdType.MESH)
    pl.semaphore_wait(barrier, len(peers))


def add_into(target, left, right):
    target[...] = left[...] + right[...]


class ScatterChain:
    def __init__(self, here, kept, line, lead, scratch):
        self.here, self.kept, self.line, self.lead = here, kept, line, lead
        self.keep, self.first_one, self.last_one, self.first_two, self.last_two, self.semaphores = scratch
        self.rows = line.shape[1]

    @staticmethod
    def scratch(width, columns, dp, lead):
        rows, far = width // dp, dp // 2
        low = lambda *shape: pltpu.VMEM(shape + (columns,), jnp.bfloat16)
        return [
            low(2, width),
            low(2, lead, rows), low(2 * (far - lead) * rows), low(lead, rows), low(far - lead, rows),
            pltpu.SemaphoreType.DMA((6, 2)),
        ]

    def chunk(self, row, far, side):
        return self.keep.at[row, pl.ds(pl.multiple_of((far * 2 + side) * self.rows, self.rows), self.rows)]

    def send(self, slot, source, target, device, rank):
        push(source, target, self.semaphores.at[slot, 0], self.semaphores.at[slot, 1], device, rank)

    def arrived(self, slot, ref):
        wait_bytes(ref, self.semaphores.at[slot, 1])

    def left(self, slot, ref):
        wait_bytes(ref, self.semaphores.at[slot, 0])

    def stage_one(self):
        here, lead = self.here, self.lead
        pltpu.make_async_copy(self.kept, self.keep, self.semaphores.at[5, 0]).start()
        for row in range(2):
            for far in range(lead):
                rows = pl.ds(pl.multiple_of((far * 2 + 1 - here.side) * self.rows, self.rows), self.rows)
                self.send(1, self.kept.at[row, rows], self.first_one.at[row, far], here.other_side, here.rank)
        start, size = lead * 2 * self.rows, (here.count - lead) * 2 * self.rows
        self.send(2, self.kept.at[1 - here.row, pl.ds(start, size)], self.last_one, here.device, here.other_row)

    def stage_two(self):
        here, lead = self.here, self.lead
        wait_bytes(self.keep, self.semaphores.at[5, 0])
        self.arrived(1, self.first_one)
        for row in range(2):
            for far in range(lead):
                mine = self.chunk(row, far, here.side)
                add_into(mine, mine, self.first_one.at[row, far])
        for far in range(lead):
            self.send(3, self.chunk(1 - here.row, far, here.side), self.first_two.at[far], here.device, here.other_row)
        self.arrived(2, self.last_one)
        for far in range(lead, here.count):
            for side in range(2):
                mine = self.chunk(here.row, far, side)
                add_into(mine, mine, self.last_one.at[pl.ds(((far - lead) * 2 + side) * self.rows, self.rows)])
        for far in range(lead, here.count):
            self.send(
                4, self.chunk(here.row, far, 1 - here.side), self.last_two.at[far - lead], here.other_side, here.rank
            )

    def merge(self):
        here = self.here
        self.arrived(3, self.first_two)
        self.arrived(4, self.last_two)
        for far in range(here.count):
            land = self.first_two.at[far] if far < self.lead else self.last_two.at[far - self.lead]
            add_into(self.line.at[far], self.chunk(here.row, far, here.side), land)

    def finish(self):
        self.left(1, self.first_one)
        self.left(2, self.last_one)
        self.left(3, self.first_two)
        self.left(4, self.last_two)


class LineChain:
    def __init__(self, here, line, out, land, semaphores):
        self.here, self.line, self.out, self.land, self.semaphores = here, line, out, land, semaphores

    @staticmethod
    def scratch(far, rows, columns):
        return [pltpu.VMEM((far - 1, rows, columns), jnp.bfloat16), pltpu.SemaphoreType.DMA((2,))]

    def start(self):
        here = self.here
        for step in range(1, here.count):
            push(
                self.line.at[here.ahead(step)], self.land.at[step - 1], self.semaphores.at[0],
                self.semaphores.at[1], here.line(step), here.rank,
            )

    def finish(self):
        wait_bytes(self.land, self.semaphores.at[1])
        total = self.line[self.here.far].astype(jnp.float32)
        for step in range(1, self.here.count):
            total = total + self.land[step - 1].astype(jnp.float32)
        self.out[...] = total
        wait_bytes(self.land, self.semaphores.at[0])


def leave_kernel(mod_start, *refs):
    refs = list(refs)
    scattering = len(refs) > 10
    kept, begun, *done = [refs.pop(0) for _ in range(6 if scattering else 2)]
    if not scattering:
        refs = [kept, begun] + refs
    small_ref, modulation_ref, *refs = refs
    heads_out, wide_out = (refs.pop(0), refs.pop(0)) if scattering else (None, None)
    sum_ref, act_ref, land_ref, acting_ref, semaphores, *space = refs
    device, rank, dp, tp = place()
    me, count = device * tp + rank, dp * tp
    greet_all()
    if scattering:
        here = Where()
        line_ref, out, *space = space
        pick = lambda number: [space.pop(0) for _ in range(number)]
        chains, trails = [], []
        for index in range(PARTS):
            size = out.shape[1] // PARTS
            part = pl.ds(index * size, size)
            line = line_ref.at[index]
            chains.append(ScatterChain(here, kept.at[0, :, :, part], line, here.count // 2, pick(6)))
            trails.append(LineChain(here, line, out.at[:, part], *pick(2)))
        others = [LineChain(here, begun.at[0], wide_out.at[0, 1], *pick(2))]
    for step in range(1, tp):
        there = lax.rem(rank + step, tp)
        push(small_ref.at[there], land_ref.at[rank], semaphores.at[0], semaphores.at[1], device, there)
    land_ref[rank] = small_ref[rank]
    wait_bytes(land_ref.at[pl.ds(0, tp - 1)], semaphores.at[1])
    mine = sum_ref.at[rank]
    mine[device] = jnp.sum(land_ref[...], axis=0)

    def one(step, carry):
        push(mine.at[device], mine.at[device], semaphores.at[2], semaphores.at[3], lax.rem(device + step, dp), rank)
        return carry

    lax.fori_loop(1, dp, one, 0)
    if scattering:
        for chain in others:
            chain.start()
    wait_bytes(mine.at[pl.ds(0, dp - 1)], semaphores.at[3])
    for step in range(1, tp):
        push(mine, mine, semaphores.at[4], semaphores.at[5], device, lax.rem(rank + step, tp))
    if scattering:
        for chain in chains:
            chain.stage_one()
        up_first, up_last, down_last, heads_last = done
        wide_out[0, 0], wide_out[1, 0], wide_out[1, 1] = up_first[0], up_last[0], down_last[0]
        for kind, value in enumerate(unpack_heads(heads_last[0])):
            heads_out[1, kind] = value
        chains[0].stage_two()
    wait_bytes(sum_ref.at[pl.ds(0, tp - 1)], semaphores.at[5])
    layers, padded, columns = modulation_ref.shape
    lines = sum_ref.shape[2]
    total = jnp.zeros((dp, padded), jnp.float32)
    for layer in range(layers):
        for index in range(columns // PAIR):
            line = layer * (tp * lines // layers) + mod_start // PAIR + index
            low = sum_ref[line // lines, :, line % lines, :].astype(jnp.bfloat16)
            total += mm(low, modulation_ref[layer, :, index * PAIR : (index + 1) * PAIR], ((1,), (1,)))
    acting_ref[...] = jnp.concatenate([total, jnp.zeros((dp, PAIR - padded), jnp.float32)], axis=1)
    act_ref[me] = acting_ref[...]

    def tell(index, carry):
        peer = lax.rem(me + index, count)
        push(acting_ref, act_ref.at[me], semaphores.at[6], semaphores.at[7], peer // tp, lax.rem(peer, tp))
        return carry

    lax.fori_loop(1, count, tell, 0)
    if scattering:
        for chain in chains[1:]:
            chain.stage_two()
        for chain, line in zip(chains, trails):
            chain.merge()
            line.start()
        for chain in others:
            chain.finish()
    wait_bytes(act_ref.at[pl.ds(0, count - 1)], semaphores.at[7])
    wait_bytes(act_ref.at[pl.ds(0, count - 1)], semaphores.at[6])
    wait_bytes(land_ref.at[pl.ds(0, tp - 1)], semaphores.at[0])
    wait_bytes(mine.at[pl.ds(0, dp - 1)], semaphores.at[2])
    wait_bytes(sum_ref.at[pl.ds(0, tp - 1)], semaphores.at[4])
    if scattering:
        for chain in chains + trails:
            chain.finish()
        for kind, value in enumerate(unpack_heads(out[...])):
            heads_out[0, kind] = value


def leave(small, modulation, mod_start, kept, begun, done, collective_id):
    tp, lines, lanes = small.shape
    dp = lax.axis_size("dp")
    inside = pl.BlockSpec(memory_space=pltpu.VMEM)
    shapes, space, extra = [], [], []
    if kept is not None:
        _, _, width, columns = kept.shape
        rows, far, part = width // dp, dp // 2, columns // PARTS
        extra = [kept, begun, *done]
        shapes = [
            jax.ShapeDtypeStruct((2, 4, rows, columns // 4), jnp.float32),
            jax.ShapeDtypeStruct((2, 2, rows, columns), jnp.float32),
        ]
        space = [pltpu.VMEM((PARTS, far, rows, part), jnp.bfloat16), pltpu.VMEM((rows, columns), jnp.float32)]
        for _ in range(PARTS):
            space += ScatterChain.scratch(width, part, dp, far // 2) + LineChain.scratch(far, rows, part)
        space += LineChain.scratch(far, rows, columns)
    return pl.pallas_call(
        partial(leave_kernel, mod_start),
        in_specs=([pl.BlockSpec(memory_space=pl.ANY)] + [inside] * 5)[: len(extra)] + [inside, inside],
        out_specs=[inside] * (len(shapes) + 2),
        out_shape=shapes + [
            jax.ShapeDtypeStruct((tp, dp, lines, lanes), jnp.float32),
            jax.ShapeDtypeStruct((dp * tp, dp, lanes), jnp.float32),
        ],
        scratch_shapes=[
            pltpu.VMEM((tp, lines, lanes), jnp.float32),
            pltpu.VMEM((dp, lanes), jnp.float32),
            pltpu.SemaphoreType.DMA((8,)),
        ] + space,
        compiler_params=pltpu.CompilerParams(
            collective_id=collective_id, has_side_effects=True, vmem_limit_bytes=VMEM_LIMIT
        ),
        name="leave",
    )(*extra, small, modulation)


class GatherChain:
    def __init__(self, here, source, out, semaphores, half=None):
        self.here, self.source, self.out, self.semaphores = here, source, out, semaphores
        self.half = here.count // 2 if half is None else half

    @staticmethod
    def scratch():
        return [pltpu.SemaphoreType.DMA((9, 2))]

    def pieces(self, rank, side, first=0, last=None):
        last = self.here.count if last is None else last
        return self.out.at[rank, pl.ds(first, last - first), side]

    def send(self, slot, pieces, device, rank):
        push(pieces, pieces, self.semaphores.at[slot, 0], self.semaphores.at[slot, 1], device, rank)

    def wait(self, slot, way, pieces):
        wait_bytes(self.pieces(0, 0, 0, pieces), self.semaphores.at[slot, way])

    def stage_line(self):
        here = self.here
        mine = self.out.at[here.rank, here.far, here.side]
        pltpu.make_async_copy(self.source, mine, self.semaphores.at[8, 0]).start()
        for step in range(1, here.count):
            push(
                self.source, mine, self.semaphores.at[0, 0], self.semaphores.at[0, 1], here.line(step), here.rank
            )

    def line_arrived(self):
        self.wait(8, 0, 1)
        self.wait(0, 1, self.here.count - 1)

    def line_left(self):
        self.wait(0, 0, self.here.count - 1)

    def stage_near(self):
        here = self.here
        mine = self.pieces(here.rank, here.side)
        self.send(1, mine, here.other_side, here.rank)
        self.send(2, mine, here.device, here.other_row)
        self.send(3, mine, here.device, here.other_core)

    def stage_across(self):
        here, count = self.here, self.here.count
        self.wait(1, 1, count)
        self.send(4, self.pieces(here.rank, 1 - here.side, 0, self.half), here.device, here.other_row)
        self.wait(2, 1, count)
        self.send(5, self.pieces(here.other_row, here.side, self.half, count), here.other_side, here.rank)
        self.send(6, self.pieces(here.rank, 1 - here.side), here.device, here.other_core)
        self.send(7, self.pieces(here.other_row, here.side), here.device, here.other_core)

    def stage_core(self):
        here, count = self.here, self.here.count
        self.wait(4, 1, self.half)
        self.wait(5, 1, count - self.half)
        self.send(8, self.pieces(here.other_row, 1 - here.side), here.device, here.other_core)

    def finish(self):
        count, half = self.here.count, self.half
        for slot in (3, 6, 7, 8):
            self.wait(slot, 1, count)
        for slot, pieces in ((1, count), (2, count), (3, count), (4, half), (5, count - half), (6, count), (7, count)):
            self.wait(slot, 0, pieces)
        self.wait(8, 0, count)


def column_parts(here, source, out, semaphores, half=None):
    size = out.shape[4] // PARTS
    chains = []
    for index, semaphore in enumerate(semaphores):
        part = pl.ds(index * size, size)
        shard = None if source is None else source.at[:, part]
        chains.append(GatherChain(here, shard, out.at[:, :, :, :, part], semaphore, half))
    return chains


class Job:
    operands, sources, shapes, specs, aliases, space = (), None, (), (), {}, ()
    stages, last = {}, ()


def anywhere(count):
    return [pl.BlockSpec(memory_space=pl.ANY)] * count


class CoreJob(Job):
    def __init__(self, kinds, width, columns):
        block = (kinds, width, columns)
        self.shapes, self.specs = [jax.ShapeDtypeStruct((kinds, 2, width, columns), jnp.bfloat16)], anywhere(1)
        self.space = [
            pltpu.VMEM((2,) + block, jnp.bfloat16),
            pltpu.VMEM((2,) + block, jnp.bfloat16),
            pltpu.SemaphoreType.DMA((4, kinds)),
        ]

    def bind(self, here, inputs, outputs, space):
        self.here, self.kept, (self.buffer, self.land, self.semaphores) = here, outputs[0], space
        self.stages = {}
        self.last = [
            partial(self.sent, own, kind) for own in range(2) for kind in range(self.buffer.shape[1])
        ]

    def sent(self, own, kind):
        wait_bytes(self.buffer.at[own, kind], self.semaphores.at[own, kind])

    def rank(self, turn):
        return turn_of(turn)

    def put(self, turn, kind, make):
        row, own = turn // 2, lax.rem(turn, 2)

        @pl.when(turn >= 2)
        def _():
            self.sent(own, kind)

        @pl.when(own == 0)
        def _():
            self.buffer[0, kind] = make().astype(jnp.bfloat16)

        @pl.when(own == 1)
        def _():
            wait_bytes(self.land.at[row, kind], self.semaphores.at[2 + row, kind])
            self.buffer[1, kind] = (make() + self.land[row, kind].astype(jnp.float32)).astype(jnp.bfloat16)

    def send(self, turn, kind):
        here, row, own = self.here, turn // 2, lax.rem(turn, 2)

        @pl.when(own == 0)
        def _():
            push(
                self.buffer.at[0, kind], self.land.at[row, kind], self.semaphores.at[0, kind],
                self.semaphores.at[2 + row, kind], here.device, here.other_core,
            )

        @pl.when(own == 1)
        def _():
            pltpu.make_async_copy(
                self.buffer.at[1, kind], self.kept.at[kind, row], self.semaphores.at[1, kind]
            ).start()


class ScatterJob(Job):
    def __init__(self, grads, lead, close=False):
        _, _, width, columns = grads[0][0].shape
        dp = lax.axis_size("dp")
        far, rows = dp // 2, width // dp
        self.lead, self.close, self.kinds = lead, close, [kind for _, kind in grads]
        self.operands = [array for array, _ in grads]
        shape = (len(grads) - close, far, rows, columns)
        self.shapes, self.specs = [jax.ShapeDtypeStruct(shape, jnp.bfloat16)], [fixed(shape)]
        self.space = ScatterChain.scratch(width, columns, dp, lead) * len(grads)
        if close:
            self.shapes.append(jax.ShapeDtypeStruct((1, rows, columns), jnp.float32))
            self.specs.append(fixed((1, rows, columns)))
            self.space = [pltpu.VMEM((far, rows, columns), jnp.bfloat16)] + LineChain.scratch(
                far, rows, columns
            ) + self.space

    def bind(self, here, inputs, outputs, space):
        lines = [outputs[0].at[index] for index in range(outputs[0].shape[0])]
        if self.close:
            own, land, semaphores, *space = space
            lines.insert(0, own)
            line = LineChain(here, own, outputs[1].at[0], land, semaphores)
        size = len(space) // len(inputs)
        chains = [
            ScatterChain(
                here, inputs[index].at[kind], lines[index], self.lead, space[index * size : (index + 1) * size]
            )
            for index, kind in enumerate(self.kinds)
        ]
        one = chains[0]
        if len(chains) == 1:
            self.stages = {(0, 0): [one.stage_one], (2, 0): [one.stage_two]}
            self.last = [one.merge, one.finish]
            return
        two = chains[1]
        if self.close:
            self.stages = {
                (0, 0): [one.stage_one], (1, 1): [one.stage_two], (2, 0): [one.merge, line.start, two.stage_one],
                (3, 1): [two.stage_two],
            }
            self.last = [line.finish, two.merge, one.finish, two.finish]
            return
        self.stages = {
            (0, 0): [one.stage_one, two.stage_one], (1, 3): [one.stage_two], (3, 1): [two.stage_two],
        }
        self.last = [one.merge, two.merge, one.finish, two.finish]


class LineJob(Job):
    def __init__(self, line):
        kinds, far, rows, columns = line.shape
        shape = (kinds, rows, columns)
        self.operands, self.sources = [line], [fixed(line.shape)]
        self.shapes, self.specs = [jax.ShapeDtypeStruct(shape, jnp.float32)], [fixed(shape)]
        self.space = LineChain.scratch(far, rows, columns) * kinds

    def bind(self, here, inputs, outputs, space):
        chains = [
            LineChain(here, inputs[0].at[kind], outputs[0].at[kind], *space[2 * kind : 2 * kind + 2])
            for kind in range(outputs[0].shape[0])
        ]
        self.stages = {(0, 0): [chain.start for chain in chains]}
        self.last = [chain.finish for chain in chains]


class FlowJob(Job):
    def __init__(self, spread, lines, half=None, late=()):
        dp, tp = lax.axis_size("dp"), lax.axis_size("tensor")
        self.counts, self.half = (len(spread), len(late)), half
        shards = list(late) + list(lines)
        self.operands = list(spread) + shards
        self.shapes = [jax.ShapeDtypeStruct(v.shape, v.dtype) for v in spread]
        self.shapes += [jax.ShapeDtypeStruct((tp, dp // 2, 2) + v.shape, v.dtype) for v in shards]
        self.specs = anywhere(len(self.shapes))
        self.aliases = {index: index for index in range(len(spread))}
        self.space = GatherChain.scratch() * (PARTS * len(self.shapes))

    def bind(self, here, inputs, outputs, space):
        first, late = self.counts
        chains = [
            column_parts(
                here, inputs[index] if index >= first else None, outputs[index],
                space[index * PARTS : (index + 1) * PARTS], self.half,
            )
            for index in range(len(inputs))
        ]
        spread, late, lines = (
            [chain for group in chosen for chain in group]
            for chosen in (chains[:first], chains[first : first + late], chains[first + late :])
        )
        self.stages = {(0, 0): [chain.stage_near for chain in spread]}
        self.stages[0, 0] += [chain.stage_line for chain in late + lines]
        for index, spot in zip(range(PARTS), ((1, 1), (2, 0), (3, 0))):
            self.stages[spot] = [chain.stage_across for chain in spread[index::PARTS]]
            for chain in late[index::PARTS]:
                self.stages[spot] += [chain.line_arrived, chain.stage_near]
        self.last = [chain.stage_across for chain in late]
        self.last += [chain.stage_core for chain in spread + late]
        self.last += [chain.finish for chain in spread + late]
        self.last += [chain.line_arrived for chain in lines]
        self.last += [chain.line_left for chain in late + lines]


class SwapJob(Job):
    def __init__(self, tokens, to_frames):
        self.to_frames = to_frames
        self.operands = [tokens]
        shape = tokens.shape
        shape = (shape[2], shape[0], shape[1]) + shape[3:] if to_frames else (shape[1], shape[2], shape[0]) + shape[3:]
        self.shapes, self.specs = [jax.ShapeDtypeStruct(shape, tokens.dtype)], anywhere(1)
        self.space = [pltpu.SemaphoreType.DMA((3,))]

    def bind(self, here, inputs, outputs, space):
        source, out, semaphores = inputs[0], outputs[0], space[0]
        frames, ranks = out.shape[:2] if self.to_frames else (out.shape[2], out.shape[0])
        few = pl.ds(0, ranks - 1)
        most, mine = (out.at[:, few], out.at[:, 0]) if self.to_frames else (out.at[few], out.at[0])

        def ends(frame, there):
            if self.to_frames:
                return source.at[there, :, frame], out.at[frame, here.rank]
            return source.at[frame, there], out.at[here.rank, :, frame]

        def start():
            for frame in range(frames):
                pltpu.make_async_copy(*ends(frame, here.rank), semaphores.at[2]).start()
            for step in range(1, ranks):
                there = lax.rem(here.rank + step, ranks)
                for frame in range(frames):
                    push(*ends(frame, there), semaphores.at[0], semaphores.at[1], here.device, there)

        def finish():
            wait_bytes(mine, semaphores.at[2])
            wait_bytes(most, semaphores.at[1])
            wait_bytes(most, semaphores.at[0])

        self.stages, self.last = {(0, 0): [start]}, [finish]


class StreamJob(Job):
    def __init__(self, shape, frames):
        self.shape, self.frames = shape, frames
        self.shapes, self.specs = [jax.ShapeDtypeStruct(shape, jnp.bfloat16)], anywhere(1)
        ranks, groups, rows, width = shape
        block = (groups, ranks, rows, width)
        if frames:
            block = (frames, ranks, groups, rows // frames, width)
        self.space = [pltpu.VMEM(block, jnp.bfloat16), pltpu.SemaphoreType.DMA((3,))]

    def bind(self, here, inputs, outputs, space):
        self.here, self.out = here, outputs[0]
        self.buffer, self.semaphores = space
        ranks = self.shape[0]

        def finish():
            wait_bytes(self.out.at[0], self.semaphores.at[2])
            wait_bytes(self.out.at[pl.ds(0, ranks - 1)], self.semaphores.at[1])
            wait_bytes(self.out.at[pl.ds(0, ranks - 1)], self.semaphores.at[0])

        self.stages, self.last = {}, [finish]

    def put(self, step, value):
        here, ranks = self.here, self.shape[0]
        size = self.buffer.size // self.buffer.shape[0] // value.shape[1]
        if value.shape[0] > size:
            count = value.shape[0] // size
            for index in range(count):
                self.put(step * count + index, value[index * size : (index + 1) * size])
            return
        self.buffer[step] = value.reshape(self.buffer.shape[1:]).astype(jnp.bfloat16)
        if self.frames:
            strip = self.buffer.shape[3]
            target = self.out.at[here.rank, :, pl.ds(pl.multiple_of(step * strip, strip), strip)]
        else:
            target = self.out.at[here.rank, step]
        pltpu.make_async_copy(self.buffer.at[step, here.rank], target, self.semaphores.at[2]).start()
        for ahead in range(1, ranks):
            there = lax.rem(here.rank + ahead, ranks)
            push(
                self.buffer.at[step, there], target, self.semaphores.at[0], self.semaphores.at[1],
                here.device, there,
            )


def greet_jobs(here):
    barrier = pltpu.get_barrier_semaphore()
    ranks = lax.axis_size("tensor")
    peers = [(here.other_side, here.rank)]
    peers += [(here.line(step), here.rank) for step in range(1, here.count)]
    peers += [(here.device, lax.rem(here.rank + step, ranks)) for step in range(1, ranks)]
    for peer in peers:
        pl.semaphore_signal(barrier, inc=1, device_id=peer, device_id_type=pl.DeviceIdType.MESH)
    pl.semaphore_wait(barrier, len(peers))


def call(body, steps, arguments, in_specs, out_shape, out_specs, scratch, jobs, collective_id, estimate, name):
    operands = [v for job in jobs for v in job.operands]
    sources = [v for job in jobs for v in (job.sources or anywhere(len(job.operands)))]
    shapes = [v for job in jobs for v in job.shapes]
    specs = [v for job in jobs for v in job.specs]
    space = [v for job in jobs for v in job.space]
    aliases, before, after = {}, len(arguments), len(out_shape)
    for job in jobs:
        for source, target in job.aliases.items():
            aliases[before + source] = after + target
        before, after = before + len(job.operands), after + len(job.shapes)

    def kernel(*refs):
        refs = list(refs)
        take = lambda number: [refs.pop(0) for _ in range(number)]
        inputs, job_inputs = take(len(arguments)), take(len(operands))
        outputs, job_outputs = take(len(out_shape)), take(len(shapes))
        own, job_space = take(len(scratch)), refs
        step = pl.program_id(0)
        if jobs:
            here = Where()
            for job in jobs:
                pick = lambda pool, number: [pool.pop(0) for _ in range(number)]
                job.bind(
                    here, pick(job_inputs, len(job.operands)), pick(job_outputs, len(job.shapes)),
                    pick(job_space, len(job.space)),
                )

        def hook(spot):
            for index in range(steps):
                todo = [
                    stage
                    for job in jobs
                    for (late, place), stages in sorted(job.stages.items())
                    if (late * 4 + place) * steps // 4 == index * 4 + spot
                    for stage in stages
                ]
                if todo or (jobs and spot == 0 and index == 0):

                    @pl.when(step == index)
                    def _():
                        if index == 0 and spot == 0:
                            greet_jobs(here)
                        for stage in todo:
                            stage()

        hook(0)
        body(lambda spot: hook(spot) if spot else None, *inputs, *outputs, *own)
        if jobs:

            @pl.when(step == steps - 1)
            def _():
                for job in jobs:
                    for stage in job.last:
                        stage()

    more = {"collective_id": collective_id, "has_side_effects": True} if jobs else {}
    return pl.pallas_call(
        kernel,
        grid=(steps,),
        in_specs=list(in_specs) + sources,
        out_specs=list(out_specs) + specs,
        out_shape=list(out_shape) + shapes,
        scratch_shapes=list(scratch) + space,
        input_output_aliases=aliases,
        compiler_params=pltpu.CompilerParams(
            vmem_limit_bytes=VMEM_LIMIT, dimension_semantics=("arbitrary",), **more
        ),
        cost_estimate=estimate,
        name=name,
    )(*arguments, *operands)


def entry_kernel(
    per_device, row_ref, modulation_ref, *refs
):
    gather = 2 if len(refs) > 5 else 0
    refs = list(refs)
    sources = [refs.pop(0) for _ in range(gather)]
    gathered_ref, mod_ref = refs.pop(0), refs.pop(0)
    targets = [refs.pop(0) for _ in range(gather)]
    part_ref, land_ref, semaphores, *space = refs
    device, rank, dp, tp = place()
    me, count = device * tp + rank, dp * tp
    lines = land_ref.shape[1]
    if gather:
        here = Where()
        parts = column_parts(here, sources[0], targets[0], space[:PARTS])
        following = GatherChain(here, sources[1], targets[1], space[PARTS])
    greet_all()

    def tell(index, carry):
        peer = lax.rem(me + index, count)
        push(
            row_ref, gathered_ref.at[me], semaphores.at[0], semaphores.at[1], peer // tp, lax.rem(peer, tp)
        )
        return carry

    lax.fori_loop(1, count, tell, 0)
    gathered_ref[me] = row_ref[...]
    if gather:
        for chain in parts:
            chain.stage_line()
    wait_bytes(gathered_ref.at[pl.ds(0, count - 1)], semaphores.at[1])
    padded = modulation_ref.shape[1]
    width = dp * tp * per_device
    chosen = jnp.zeros((count, padded), jnp.float32)
    row = lax.broadcasted_iota(jnp.int32, (PAIR, padded), 0)
    column = lax.broadcasted_iota(jnp.int32, (PAIR, padded), 1)
    for index in range(width // PAIR):
        match = (row + index * PAIR == column + me * per_device) & (column < per_device)
        chosen += mm(
            gathered_ref[:, index, :].astype(jnp.bfloat16), jnp.where(match, 1.0, 0.0).astype(jnp.bfloat16)
        )
    clip = lax.broadcasted_iota(jnp.int32, (dp, count), 0)
    member = lax.broadcasted_iota(jnp.int32, (dp, count), 1)
    leaders = jnp.where(member == clip * tp, 1.0, 0.0).astype(jnp.bfloat16)
    rows = mm(leaders, chosen.astype(jnp.bfloat16)).astype(jnp.bfloat16)
    for layer in range(modulation_ref.shape[0]):
        part = mm(rows, modulation_ref[layer])
        size = part.shape[1] // PAIR
        for index in range(size):
            line = layer * size + index
            part_ref[:, line // lines, line % lines, :] = part[:, index * PAIR : (index + 1) * PAIR]

    def share(index, carry):
        peer = lax.rem(me + index, count)
        there, lane = peer // tp, lax.rem(peer, tp)
        push(part_ref.at[there, lane], land_ref.at[me], semaphores.at[2], semaphores.at[3], there, lane)
        return carry

    lax.fori_loop(1, count, share, 0)
    land_ref[me] = part_ref[device, rank]
    if gather:
        for chain in parts:
            chain.line_arrived()
            chain.stage_near()
        following.stage_line()
        for chain in parts:
            chain.stage_across()
    wait_bytes(land_ref.at[pl.ds(0, count - 1)], semaphores.at[3])
    mod_ref[rank] = jnp.sum(land_ref[...], axis=0)
    for step in range(1, tp):
        push(
            mod_ref.at[rank], mod_ref.at[rank], semaphores.at[4], semaphores.at[5], device, lax.rem(rank + step, tp)
        )
    if gather:
        for chain in parts:
            chain.stage_core()
    wait_bytes(gathered_ref.at[pl.ds(0, count - 1)], semaphores.at[0])
    wait_bytes(land_ref.at[pl.ds(0, count - 1)], semaphores.at[2])
    wait_bytes(mod_ref.at[pl.ds(0, tp - 1)], semaphores.at[5])
    wait_bytes(mod_ref.at[pl.ds(0, tp - 1)], semaphores.at[4])
    if gather:
        following.line_arrived()
        for chain in parts:
            chain.finish()
        for chain in (*parts, following):
            chain.line_left()


def enter(row, modulation, per_device, weights, collective_id):
    dp, tp = lax.axis_size("dp"), lax.axis_size("tensor")
    count = dp * tp
    lines = modulation.shape[0] * modulation.shape[2] // (tp * PAIR)
    inside = pl.BlockSpec(memory_space=pltpu.VMEM)
    job = FlowJob((), weights) if weights else Job()
    return pl.pallas_call(
        partial(entry_kernel, per_device),
        in_specs=[inside, inside] + anywhere(len(job.operands)),
        out_specs=[inside, inside] + list(job.specs),
        out_shape=[
            jax.ShapeDtypeStruct((count,) + row.shape, jnp.float32),
            jax.ShapeDtypeStruct((tp, lines, PAIR), jnp.float32),
        ] + list(job.shapes),
        scratch_shapes=[
            pltpu.VMEM((dp, tp, lines, PAIR), jnp.float32),
            pltpu.VMEM((count, lines, PAIR), jnp.float32),
            pltpu.SemaphoreType.DMA((6,)),
        ] + (GatherChain.scratch() * (PARTS + 1) if weights else []),
        compiler_params=pltpu.CompilerParams(
            collective_id=collective_id, has_side_effects=True, vmem_limit_bytes=VMEM_LIMIT
        ),
        name="enter",
    )(row, modulation, *job.operands)


def adam_update(weight, first, second, grad, rate, decay):
    first_new = BETA_ONE * first + (1.0 - BETA_ONE) * grad
    second_new = BETA_TWO * second + (1.0 - BETA_TWO) * grad * grad
    corrected = (
        first_new
        / (1.0 - BETA_ONE**STEP)
        / (jnp.sqrt(second_new / (1.0 - BETA_TWO**STEP)) + ADAM_EPS)
    )
    weight_new = weight - rate * (corrected + decay * weight)
    return (weight_new, first_new, second_new, weight_new.astype(jnp.bfloat16))


def dot32(form, left, right):
    return jnp.einsum(form, left, right, preferred_element_type=jnp.float32)


def exchange(blocks):
    return lax.all_to_all(blocks, "tensor", split_axis=0, concat_axis=0, tiled=True)


def gather_plain(shard):
    rows, width = shard.shape
    whole = lax.all_gather(shard, ("tensor", "dp"), axis=0, tiled=True)
    return whole.reshape(-1, lax.axis_size("dp") * rows, width)


def scatter_plain(grads):
    kinds, ranks, width, cols = grads.shape
    flat = grads.reshape(kinds, ranks * width, cols)
    summed = lax.psum_scatter(flat, ("tensor", "dp"), scatter_dimension=1, tiled=True)
    return summed.astype(jnp.float32)


def per_device(
    clips, cotangent, timesteps, labels, time_table, class_table,
    attention_weights, attention_first, attention_second,
    ffn_weights, ffn_first, ffn_second,
    modulation_weights, modulation_first, modulation_second,
    bias_vectors, bias_first, bias_second,
):
    layers, kinds, rows, cols = attention_weights.shape
    _, frames, patches, width = clips.shape
    mod_rows = modulation_weights.shape[1]
    bias_cols = bias_vectors.shape[1]
    dp, tp = lax.axis_size("dp"), lax.axis_size("tensor")
    position = lax.axis_index("dp") * tp + lax.axis_index("tensor")
    tokens = frames * patches
    strip = patches // (tp * frames)
    blocks = (tp, frames, frames * strip, width)
    pieces = (tp * frames, frames, strip, width)

    embed = time_table[timesteps] + class_table[labels]
    cond_act = jax.nn.silu(embed).astype(jnp.bfloat16)
    fused = rows % 16 == 0
    shards = [
        (
            pack_heads(attention_weights[layer].astype(jnp.bfloat16)),
            ffn_weights[layer, 0].astype(jnp.bfloat16),
            ffn_weights[layer, 1].astype(jnp.bfloat16),
        )
        for layer in range(layers)
    ]
    low = bias_vectors.astype(jnp.bfloat16).reshape(-1)
    row = jnp.concatenate([cond_act[0], low]).astype(jnp.float32)
    row = jnp.pad(row, (0, -row.shape[0] % 1024)).reshape(-1, 128)
    modulation_low = modulation_weights.astype(jnp.bfloat16)
    modulation_low = jnp.pad(modulation_low, ((0, 0), (0, -mod_rows % 32), (0, 0)))
    gathered, mod, *begun = enter(row, modulation_low, mod_rows, shards[0][:2] if fused else None, 0)
    gathered = gathered.reshape(dp * tp, -1)
    cond_all = gathered[::tp, :width].astype(jnp.bfloat16)
    bias_low = gathered[:, width : width + layers * bias_cols].reshape(dp * tp, layers, bias_cols)
    bias_low = bias_low.transpose(1, 0, 2).reshape(layers, -1)
    cond_rows = lax.dynamic_slice_in_dim(cond_all, position * mod_rows, mod_rows, axis=1)
    cond_rows = jnp.pad(cond_rows, ((0, 0), (0, -mod_rows % 32)))
    mod = mod.reshape(layers, -1)
    mod_width = mod.shape[-1]
    mod = (mod + bias_low[:, -mod_width:]).reshape(layers, 6, width)
    hidden_width = bias_low.shape[1] - mod_width - 4 * width
    bias_up = bias_low[:, 3 * width : 3 * width + hidden_width].reshape(layers, tp, 1, -1)
    bias_out = bias_low[:, None, 2 * width : 3 * width]
    bias_down = bias_low[:, None, 3 * width + hidden_width : 4 * width + hidden_width]
    bias_project = [
        pack_bias(bias_low[layer, :width], bias_low[layer, width : 2 * width], tp) for layer in range(layers)
    ]

    by_patch = lambda v: v.reshape(frames, tp * frames, strip, width).transpose(1, 0, 2, 3)
    first = clips[0].reshape(1, frames, patches, width)

    whole = lambda weight: weight.reshape(tp, width, -1)
    attend = lambda layer, weight, stream, stride, *more: attention_forward(
        whole(weight), stream, mod[layer], bias_project[layer], bias_out[layer], stride, *more
    )
    expand = lambda layer, up, down, middle, *more: ffn_forward(
        whole(up), whole(down), middle.reshape(tokens, width), mod[layer], bias_down[layer], bias_up[layer], *more
    )
    if fused:
        attention_a, up_a = begun
        *heads_a, middle_a, up_a, down_a, attention_b = attend(
            0, attention_a, first, 0, [FlowJob([up_a], [shards[1][0]], None, [shards[0][2]])], 1
        )
        hidden_a, pushed_a, second, attention_b, up_b, down_b = expand(
            0, up_a, down_a, middle_a, StreamJob(blocks, frames),
            [FlowJob([attention_b], [shards[1][2]], dp // 8, [shards[1][1]])], 2, True,
        )
        *heads_b, middle_b, down_b = attend(1, attention_b, second, strip, [FlowJob([down_b], [])], 3)
        cot = cotangent.reshape(frames, tp, frames, strip, width)
        hidden_b, pushed_b, result, cot = expand(
            1, up_b, down_b, middle_b, None, [SwapJob(cot, False)], 4, True
        )
        attention_a, up_a, down_a = whole(attention_a), whole(up_a), whole(down_a)
        attention_b, up_b, down_b = whole(attention_b), whole(up_b), whole(down_b)
    else:
        (attention_a, up_a, down_a), (attention_b, up_b, down_b) = [[gather_plain(v) for v in group] for group in shards]
        *heads_a, middle_a = attend(0, attention_a, first, 0)
        hidden_a, pushed_a, second = expand(0, up_a, down_a, middle_a)
        second = exchange(by_patch(second).reshape(blocks))
        *heads_b, middle_b = attend(1, attention_b, second, strip)
        hidden_b, pushed_b, result = expand(1, up_b, down_b, middle_b)
        cot = exchange(by_patch(cotangent[0]).reshape(blocks))
    middle_a, middle_b = middle_a.reshape(tokens, width), middle_b.reshape(tokens, width)
    cot = cot.reshape(tokens, width)

    if fused:
        ffn_cores = lambda: CoreJob(2, width, ffn_weights.shape[-1])
        head_cores = lambda: CoreJob(1, width, kinds * cols)
        grad, *sums_b, kept, result = ffn_backward(
            up_b, down_b, cot, middle_b, pushed_b, hidden_b, mod[1], ffn_cores(),
            [SwapJob(result.reshape(tp, frames, frames, strip, width), True)], 5,
        )
        output = result.reshape(clips.shape)
        ffn_grad = kept
        *more_b, grad, kept, line_up = attention_backward(
            attention_b, grad.reshape(blocks), second, heads_b, mod[1], strip,
            StreamJob(blocks, 0), head_cores(), [ScatterJob([(ffn_grad, 0)], 3 * dp // 8)], 6,
        )
        waiting = [(ffn_grad, 1), (kept, 0)]
        grad, *sums_a, kept, done_up, line_b = ffn_backward(
            up_a, down_a, grad.reshape(pieces), middle_a, pushed_a, hidden_a, mod[0], ffn_cores(),
            [LineJob(line_up), ScatterJob(waiting, dp // 4)], 7,
        )
        ffn_grad = kept
        grad, *more_a, kept, done_b, line_ffn_a, done_up_a = attention_backward(
            attention_a, grad.reshape(first.shape), first, heads_a, mod[0], 0, None, head_cores(),
            [LineJob(line_b), ScatterJob([(ffn_grad, 0), (ffn_grad, 1)], dp // 4, True)], 8,
        )
        packed_a = kept
        done = (done_up_a, done_up, done_b[:1], done_b[1:])
    else:
        result = exchange(result.reshape(blocks)).reshape(pieces)
        output = result.transpose(1, 0, 2, 3).reshape(clips.shape)
        grad, *sums_b, ffn_grad = ffn_backward(up_b, down_b, cot, middle_b, pushed_b, hidden_b, mod[1])
        done_ffn_b = scatter_plain(ffn_grad)
        grad, packed_b, *more_b = attention_backward(
            attention_b, grad.reshape(blocks), second, heads_b, mod[1], strip
        )
        done_b = scatter_plain(packed_b[None])
        grad = exchange(grad.astype(jnp.bfloat16))
        grad, *sums_a, ffn_grad = ffn_backward(up_a, down_a, grad.reshape(pieces), middle_a, pushed_a, hidden_a, mod[0])
        done_ffn_a = scatter_plain(ffn_grad)
        grad, packed_a, *more_a = attention_backward(attention_a, grad.reshape(first.shape), first, heads_a, mod[0], 0)
        done_a = scatter_plain(packed_a[None])
    input_grad = grad.reshape(clips.shape)

    def gather_small(more, sums):
        attention_sums, project_sum = more
        up_sum, low_sums = sums
        return jnp.concatenate(
            [*unpack_bias(project_sum), attention_sums[0], up_sum.reshape(-1), low_sums[0],
             attention_sums[1:].reshape(-1), low_sums[1:].reshape(-1)]
        )

    small = jnp.stack([gather_small(more_a, sums_a), gather_small(more_b, sums_b)])
    token_width = small.shape[1] - mod_width
    *summed, small, grad_act = leave(
        small.reshape(tp, -1, 128), modulation_low, token_width,
        *((packed_a, line_ffn_a, done) if fused else (None, None, None)), 9,
    )
    small = small.transpose(1, 0, 2, 3).reshape(dp, layers, -1)
    grad_mod_low = small[..., token_width:].astype(jnp.bfloat16)
    grad_bias_all = jnp.concatenate(
        [small[..., :token_width], grad_mod_low.astype(jnp.float32)], axis=-1
    ).sum(axis=0)
    grad_bias = lax.dynamic_slice_in_dim(grad_bias_all, position * bias_cols, bias_cols, axis=1)
    grad_mod_weight = dot32("ck,cle->lke", cond_rows, grad_mod_low)[:, :mod_rows]
    grad_act = lax.dynamic_index_in_dim(
        grad_act[:, :, :mod_rows], lax.axis_index("dp"), axis=1, keepdims=False
    )
    if fused:
        grad_attention, grad_ffn = summed
    else:
        grad_attention = jnp.stack([jnp.stack(unpack_heads(done[0])) for done in (done_a, done_b)])
        grad_ffn = jnp.stack([done_ffn_a, done_ffn_b])
    silu_value, silu_pull = jax.vjp(jax.nn.silu, embed)
    cond_grad = silu_pull(grad_act.reshape(1, width))[0]

    return (output, input_grad, cond_grad) + (
        adam_update(attention_weights, attention_first, attention_second, grad_attention, MATRIX_RATE, MATRIX_DECAY)
        + adam_update(ffn_weights, ffn_first, ffn_second, grad_ffn, MATRIX_RATE, MATRIX_DECAY)
        + adam_update(modulation_weights, modulation_first, modulation_second, grad_mod_weight, MATRIX_RATE, MATRIX_DECAY)
        + adam_update(bias_vectors, bias_first, bias_second, grad_bias, VECTOR_RATE, 0.0)
    )


def solution(mesh):
    tokens = P("dp", "tensor", None, None)
    matrix = P(None, None, "dp", "tensor")
    modulation = P(None, BOTH, None)
    vector = P(None, BOTH)
    return jax.shard_map(
        per_device,
        mesh=mesh,
        in_specs=(tokens, tokens, P("dp"), P("dp"), P(), P())
        + (matrix,) * 6 + (modulation,) * 3 + (vector,) * 3,
        out_specs=(tokens, tokens, P("dp", None)) + (matrix,) * 8 + (modulation,) * 4 + (vector,) * 4,
        check_vma=False,
    )
```

```python
from functools import partial

import jax
import jax.numpy as jnp
from jax import lax
from jax.experimental import pallas as pl
from jax.experimental.pallas import tpu as pltpu
from jax.sharding import PartitionSpec as P

HD = 64
PAIR = 128
PARTS = 3
STEP = 10
BETA_ONE = 0.9
BETA_TWO = 0.999
ADAM_EPS = 1e-08
MATRIX_RATE = 0.04
VECTOR_RATE = 0.2
MATRIX_DECAY = 0.1
NORM_EPS = 1e-06
GELU_A = (2.0 / 3.141592653589793) ** 0.5
GELU_B = 0.044715
BLOCKED = -1e30
VMEM_LIMIT = 60 * 1024 * 1024
BOTH = ("dp", "tensor")


def mm(left, right, dims=((1,), (0,))):
    return lax.dot_general(left, right, (dims, ((), ())), preferred_element_type=jnp.float32)


def norm_parts(value):
    average = jnp.mean(value, axis=-1, keepdims=True)
    centred = value - average
    spread = jnp.mean(centred * centred, axis=-1, keepdims=True)
    inverse = lax.rsqrt(spread + NORM_EPS)
    return centred * inverse, inverse


def norm_back(grad, shape, inverse):
    first = jnp.mean(grad, axis=-1, keepdims=True)
    second = jnp.mean(grad * shape, axis=-1, keepdims=True)
    return inverse * (grad - first - shape * second)


def rows_of(ref):
    value = ref[...]
    return value.reshape(-1, value.shape[-1])


def put(ref, value):
    ref[...] = value.reshape(ref.shape).astype(ref.dtype)


def add_rows(ref, index, value):
    ref[pl.ds(index, 1), :] += jnp.sum(value, axis=0, keepdims=True)


def half_masks(rows):
    lane = lax.broadcasted_iota(jnp.int32, (rows, PAIR), 1)
    return lane < HD


def same_patch(tokens, stride):
    row = lax.broadcasted_iota(jnp.int32, (tokens, tokens), 0)
    column = lax.broadcasted_iota(jnp.int32, (tokens, tokens), 1)
    return lax.rem(row, stride) == lax.rem(column, stride)


def swap_halves(value):
    return pltpu.roll(value, HD, 1)


def start_loads(source, target, semaphores):
    for rank in range(target.shape[0]):
        pltpu.make_async_copy(source.at[rank], target.at[rank], semaphores.at[rank]).start()


def wait_loads(target, semaphores, rank):
    pltpu.make_async_copy(target.at[rank], target.at[rank], semaphores.at[rank]).wait()


def softmax_rows(scores, axis):
    raised = jnp.exp(scores - jnp.max(scores, axis=axis, keepdims=True))
    return raised * (1.0 / jnp.sum(raised, axis=axis, keepdims=True))


def attention_forward_kernel(
    stride, hook, source, stream_ref, mod_ref, bias_ref, bias_out_ref,
    project_ref, mixed_ref, branch_ref, middle_ref, weight_ref, semaphores,
):
    ranks = weight_ref.shape[0]

    @pl.when(pl.program_id(0) == 0)
    def _():
        start_loads(source, weight_ref, semaphores)

    stream = rows_of(stream_ref).astype(jnp.float32)
    tokens, width = stream.shape
    shape, _ = norm_parts(stream)
    normed = (shape * (1.0 + mod_ref[1:2]) + mod_ref[0:1]).astype(jnp.bfloat16)
    lower = half_masks(tokens)
    allowed = same_patch(tokens, stride) if stride else None

    @pl.when(pl.program_id(0) == 0)
    def _():
        for rank in range(ranks):
            wait_loads(weight_ref, semaphores, rank)

    def mix(heads):
        scores = [mm(chosen.astype(jnp.bfloat16), key, ((1,), (1,))) for chosen, key, _ in heads]
        outs = []
        for score, (_, _, value) in zip(scores, heads):
            if stride:
                score = jnp.where(allowed, score, BLOCKED)
            outs.append(mm(softmax_rows(score, -1).astype(jnp.bfloat16), value))
        return outs

    branch = None
    for rank in range(ranks):
        hook(rank)
        project = (mm(normed, weight_ref[rank, :, : 5 * PAIR]) + bias_ref[rank]).astype(jnp.bfloat16)
        project_ref[rank] = project.reshape(project_ref.shape[1:])
        query = project[:, :PAIR].astype(jnp.float32) * HD**-0.5
        key, value = project[:, PAIR : 2 * PAIR], project[:, 2 * PAIR : 3 * PAIR]
        both = project[:, 3 * PAIR : 4 * PAIR].astype(jnp.float32)
        first, second, last = mix(
            [
                (jnp.where(lower, query, 0.0), key, value),
                (jnp.where(lower, 0.0, query), key, value),
                (
                    jnp.where(lower, both * HD**-0.5, 0.0),
                    swap_halves(both).astype(jnp.bfloat16),
                    project[:, 4 * PAIR : 5 * PAIR],
                ),
            ]
        )
        mixed = jnp.concatenate(
            [jnp.where(lower, 0.0, swap_halves(last)), jnp.where(lower, first, second)], axis=1
        ).astype(jnp.bfloat16)
        mixed_ref[rank] = mixed.reshape(mixed_ref.shape[1:])
        term = mm(mixed, weight_ref[rank, :, 4 * PAIR :], ((1,), (1,)))
        branch = term if branch is None else branch + term
    branch = branch + bias_out_ref[...]
    put(branch_ref, branch)
    put(middle_ref, stream + mod_ref[2:3] * branch)


def gelu_parts(value):
    square = value * value
    bent = jnp.tanh(value * (GELU_A + (GELU_A * GELU_B) * square))
    half = 0.5 * (1.0 + bent)
    slope = half + (0.5 * value) * (1.0 - bent * bent) * (GELU_A + (3.0 * GELU_A * GELU_B) * square)
    return value * half, slope


def turn_of(rank):
    core = lax.rem(lax.axis_index("tensor"), 2)
    return rank + (1 - core) * (1 - 2 * (rank % 2))


def ffn_forward_kernel(
    stream, turned, hook, up_source, down_source, middle_ref, mod_ref, bias_ref, bias_up_ref, hidden_ref, branch_ref, *rest
):
    if stream is None:
        result_ref, *rest = rest
    up_ref, down_ref, up_semaphores, down_semaphores = rest
    step = pl.program_id(0)
    ranks = up_ref.shape[0]

    @pl.when(step == 0)
    def _():
        start_loads(up_source, up_ref, up_semaphores)
        start_loads(down_source, down_ref, down_semaphores)

    middle = middle_ref[...]
    shape, _ = norm_parts(middle)
    second = (shape * (1.0 + mod_ref[4:5]) + mod_ref[3:4]).astype(jnp.bfloat16)

    @pl.when(step == 0)
    def _():
        for rank in range(ranks):
            wait_loads(up_ref, up_semaphores, rank)
            wait_loads(down_ref, down_semaphores, rank)

    down = None
    for rank in range(ranks):
        hook(rank)
        hidden = mm(second, up_ref[rank]) + bias_up_ref[rank]
        hidden_ref[turn_of(rank) if turned else rank] = hidden.astype(jnp.bfloat16)
        active, _ = gelu_parts(hidden)
        part = mm(active.astype(jnp.bfloat16), down_ref[rank], ((1,), (1,)))
        down = part if down is None else down + part
    down = down + bias_ref[...]
    branch_ref[...] = down.astype(jnp.bfloat16)
    result = middle + mod_ref[5:6] * down
    if stream is None:
        result_ref[...] = result.astype(result_ref.dtype)
    else:
        stream.put(step, result)


def load_rows(ref, index, chunk):
    if len(ref.shape) == 2:
        return ref[index * chunk : (index + 1) * chunk, :].astype(jnp.float32)
    blocks, _, strip, width = ref.shape
    frames = chunk // (blocks * strip)
    parts = [ref[:, index * frames + frame].reshape(blocks * strip, width) for frame in range(frames)]
    return jnp.concatenate(parts, axis=0).astype(jnp.float32)


def ffn_backward_kernel(
    split, cores, hook, up_source, down_source, grad_ref, middle_ref, branch_ref, hidden_ref, mod_ref,
    grad_middle_ref, up_sum_ref, sums_ref, *refs
):
    if cores is None:
        weight_grad_ref, *refs = refs
    (up_ref, down_ref, up_semaphores, down_semaphores,
     second_ref, low_ref, low_across_ref, active_ref, slope_ref, total_ref) = refs
    step = pl.program_id(0)
    rank = step if cores is None else cores.rank(step)
    tokens, width = middle_ref.shape
    chunk = tokens // split

    @pl.when(step == 0)
    def _():
        start_loads(up_source, up_ref, up_semaphores)
        start_loads(down_source, down_ref, down_semaphores)
        sums_ref[...] = jnp.zeros_like(sums_ref)
        up_sum_ref[...] = jnp.zeros_like(up_sum_ref)
        for index in range(split):
            rows = slice(index * chunk, (index + 1) * chunk)
            grad = load_rows(grad_ref, index, chunk)
            low = (mod_ref[5:6] * grad).astype(jnp.bfloat16)
            low_ref[rows, :] = low
            low_across_ref[:, rows] = low.T
            add_rows(sums_ref, 0, low.astype(jnp.float32))
            add_rows(sums_ref, 3, grad * branch_ref[rows, :].astype(jnp.float32))
            shape, _ = norm_parts(middle_ref[rows, :])
            second = (shape * (1.0 + mod_ref[4:5]) + mod_ref[3:4]).astype(jnp.bfloat16)
            second_ref[:, rows] = second.T

    wait_loads(up_ref, up_semaphores, rank)
    wait_loads(down_ref, down_semaphores, rank)

    for index in range(split):
        hook(index)
        rows = slice(index * chunk, (index + 1) * chunk)
        active, slope = gelu_parts(hidden_ref[0, rows, :].astype(jnp.float32))
        active_ref[rows, :] = active.astype(jnp.bfloat16)
        low = (mm(low_ref[rows, :], down_ref[rank]) * slope).astype(jnp.bfloat16)
        slope_ref[rows, :] = low
        up_sum_ref[rank] += jnp.sum(low.astype(jnp.float32), axis=0, keepdims=True)
        part = mm(low, up_ref[rank], ((1,), (1,)))
        total_ref[rows, :] = jnp.where(step == 0, 0.0, total_ref[rows, :]) + part
    hook(2)
    make_up = lambda: mm(second_ref[...], slope_ref[...])
    if cores is None:
        weight_grad_ref[0, 0] = make_up().astype(jnp.bfloat16)
    else:
        cores.put(step, 0, make_up)
        cores.send(step, 0)
    hook(3)
    make_down = lambda: mm(low_across_ref[...], active_ref[...])
    if cores is None:
        weight_grad_ref[1, 0] = make_down().astype(jnp.bfloat16)
    else:
        cores.put(step, 1, make_down)
        cores.send(step, 1)

    @pl.when(step == pl.num_programs(0) - 1)
    def _():
        for index in range(split):
            rows = slice(index * chunk, (index + 1) * chunk)
            shape, inverse = norm_parts(middle_ref[rows, :])
            grad = total_ref[rows, :]
            add_rows(sums_ref, 1, grad)
            add_rows(sums_ref, 2, grad * shape)
            back = norm_back(grad * (1.0 + mod_ref[4:5]), shape, inverse)
            grad_middle_ref[rows, :] = load_rows(grad_ref, index, chunk) + back


def attention_backward_kernel(
    stride, swap, cores, hook, source, grad_ref, stream_ref, project_ref, mixed_ref, branch_ref, mod_ref, *refs
):
    if swap is None:
        grad_stream_ref, *refs = refs
    if cores is None:
        weight_grad_ref, *refs = refs
    (sums_ref, project_sum_ref,
     weight_ref, semaphores, left_ref, right_ref, outer_ref) = refs
    step = pl.program_id(0)
    ranks = weight_ref.shape[0]

    @pl.when(step == 0)
    def _():
        start_loads(source, weight_ref, semaphores)
        sums_ref[...] = jnp.zeros_like(sums_ref)
        project_sum_ref[...] = jnp.zeros_like(project_sum_ref)

    grad_middle = rows_of(grad_ref)
    tokens, width = grad_middle.shape
    stream = rows_of(stream_ref).astype(jnp.float32)
    shape, inverse = norm_parts(stream)
    rows = pl.ds(pl.multiple_of(step * tokens, tokens), tokens)
    normed = (shape * (1.0 + mod_ref[1:2]) + mod_ref[0:1]).astype(jnp.bfloat16)
    low = (mod_ref[2:3] * grad_middle).astype(jnp.bfloat16)
    left_ref[0, :, rows] = normed.T
    left_ref[1, :, rows] = low.T
    add_rows(sums_ref, 0, low.astype(jnp.float32))
    add_rows(sums_ref, 3, grad_middle * rows_of(branch_ref).astype(jnp.float32))
    lower = half_masks(tokens)
    allowed = same_patch(tokens, stride) if stride else None
    scale = HD**-0.5

    @pl.when(step == 0)
    def _():
        for rank in range(ranks):
            wait_loads(weight_ref, semaphores, rank)

    def score_grads(heads):
        scores = [mm(key, chosen.astype(jnp.bfloat16), ((1,), (1,))) for chosen, key, _, _ in heads]
        grad_probs = [mm(value, taken.astype(jnp.bfloat16), ((1,), (1,))) for _, _, value, taken in heads]
        outs = []
        for score, grad_prob in zip(scores, grad_probs):
            if stride:
                score = jnp.where(allowed, score, BLOCKED)
            probs = softmax_rows(score, 0)
            inner = jnp.sum(grad_prob * probs, axis=0, keepdims=True)
            outs.append((probs.astype(jnp.bfloat16), (probs * (grad_prob - inner)).astype(jnp.bfloat16)))
        return outs

    grad_normed = None
    for rank in range(ranks):
        hook(rank)
        project = project_ref[rank].reshape(tokens, 5 * PAIR)
        mixed = mixed_ref[rank].reshape(tokens, 2 * PAIR)
        outer_ref[rank, rows, :] = mixed
        grad_mixed = mm(low, weight_ref[rank, :, 4 * PAIR :]).astype(jnp.bfloat16)
        query, key, value = (project[:, n * PAIR : (n + 1) * PAIR] for n in range(3))
        query_wide = query.astype(jnp.float32) * scale
        pair = grad_mixed[:, PAIR:]
        pair_wide = pair.astype(jnp.float32)
        both = project[:, 3 * PAIR : 4 * PAIR].astype(jnp.float32)
        swapped = swap_halves(both).astype(jnp.bfloat16)
        single = swap_halves(grad_mixed[:, :PAIR].astype(jnp.float32))
        heads = [
            (jnp.where(keep, query_wide, 0.0), key, value, jnp.where(keep, pair_wide, 0.0)) for keep in (lower, ~lower)
        ]
        heads.append(
            (jnp.where(lower, both * scale, 0.0), swapped, project[:, 4 * PAIR :], jnp.where(lower, single, 0.0))
        )
        solved = score_grads(heads)
        outs = [
            (mm(grad_scores, key, ((0,), (0,))), mm(grad_scores, query), mm(probs, pair))
            for probs, grad_scores in solved[:2]
        ]
        parts = [
            jnp.where(lower, one, two) * factor
            for one, two, factor in zip(outs[0], outs[1], (scale, scale, 1.0))
        ]
        probs, grad_scores = solved[2]
        parts.append(
            jnp.where(lower, mm(grad_scores, swapped, ((0,), (0,))), mm(grad_scores, swapped)) * scale
        )
        parts.append(jnp.where(lower, mm(probs, single.astype(jnp.bfloat16)), 0.0))
        whole = jnp.concatenate(parts, axis=1).astype(jnp.bfloat16)
        right_ref[rank, rows, :] = whole
        add_rows(project_sum_ref, rank, whole.astype(jnp.float32))
        term = mm(whole, weight_ref[rank, :, : 5 * PAIR], ((1,), (1,)))
        grad_normed = term if grad_normed is None else grad_normed + term
    add_rows(sums_ref, 1, grad_normed)
    add_rows(sums_ref, 2, grad_normed * shape)
    back = norm_back(grad_normed * (1.0 + mod_ref[1:2]), shape, inverse)
    if swap is None:
        put(grad_stream_ref, grad_middle + back)
    else:
        swap.put(step, grad_middle + back)

    @pl.when(step == pl.num_programs(0) - 1)
    def _():
        def weights(turn, carry):
            rank = turn if cores is None else cores.rank(turn)
            inside = mm(left_ref[0], right_ref[rank])
            outside = mm(left_ref[1], outer_ref[rank])
            made = jnp.concatenate(
                [inside[:, : 4 * PAIR], inside[:, 4 * PAIR :] + outside[:, :PAIR], outside[:, PAIR:]], axis=1
            )
            if cores is None:
                weight_grad_ref[rank] = made.astype(jnp.bfloat16)
            else:
                cores.put(turn, 0, lambda: made)
                cores.send(turn, 0)
            return carry

        lax.fori_loop(0, ranks, weights, 0)


def fixed(shape):
    return pl.BlockSpec(shape, lambda step: (0,) * len(shape), pipeline_mode=pl.Buffered(1))


def cost(flops, moved, raised=0):
    return pl.CostEstimate(flops=int(flops), bytes_accessed=int(moved), transcendentals=int(raised))


def group_spec(shape):
    return pl.BlockSpec((shape[0], 1, shape[2], shape[3]), lambda step: (0, step, 0, 0))


def rank_spec(shape):
    return pl.BlockSpec((shape[0], shape[1], 1) + shape[3:], lambda step: (0, 0, step, 0, 0))


def attention_forward(weight, stream, mod, bias, bias_out, stride, jobs=(), collective_id=None):
    shape = stream.shape
    width = shape[-1]
    ranks = bias.shape[0]
    tokens = shape[0] * shape[1] * shape[2]
    spec = group_spec(shape)
    low = jax.ShapeDtypeStruct(shape, jnp.bfloat16)
    wide = jax.ShapeDtypeStruct(shape, jnp.float32)
    project = jax.ShapeDtypeStruct((ranks,) + shape[:3] + (5 * PAIR,), jnp.bfloat16)
    mixed = jax.ShapeDtypeStruct((ranks,) + shape[:3] + (2 * PAIR,), jnp.bfloat16)
    return call(
        partial(attention_forward_kernel, stride),
        shape[1],
        [weight, stream, mod, bias, bias_out],
        anywhere(1) + [spec, fixed(mod.shape), fixed(bias.shape), fixed(bias_out.shape)],
        [project, mixed, low, wide],
        [rank_spec(project.shape), rank_spec(mixed.shape), spec, spec],
        [pltpu.VMEM((ranks, width, 6 * PAIR), jnp.bfloat16), pltpu.SemaphoreType.DMA((ranks,))],
        jobs,
        collective_id,
        cost(8 * tokens * width * width * 1.5, tokens * width * 16),
        "attention_forward",
    )


def ffn_weights_scratch(ranks, width, part):
    return [
        pltpu.VMEM((ranks, width, part), jnp.bfloat16),
        pltpu.VMEM((ranks, width, part), jnp.bfloat16),
        pltpu.SemaphoreType.DMA((ranks,)),
        pltpu.SemaphoreType.DMA((ranks,)),
    ]


def ffn_forward(up, down, middle, mod, bias_down, bias_up, stream=None, jobs=(), collective_id=None, turned=False):
    tokens, width = middle.shape
    ranks, _, part = bias_up.shape
    steps = 4
    chunk = tokens // steps
    block = pl.BlockSpec((chunk, width), lambda step: (step, 0))
    result = [jax.ShapeDtypeStruct((tokens, width), jnp.bfloat16)] if stream is None else []
    return call(
        partial(ffn_forward_kernel, stream, turned),
        steps,
        [up, down, middle, mod, bias_down, bias_up],
        anywhere(2) + [block, fixed(mod.shape), fixed(bias_down.shape), fixed(bias_up.shape)],
        [
            jax.ShapeDtypeStruct((ranks, tokens, part), jnp.bfloat16),
            jax.ShapeDtypeStruct((tokens, width), jnp.bfloat16),
        ] + result,
        [pl.BlockSpec((ranks, chunk, part), lambda step: (0, step, 0)), block] + [block] * len(result),
        ffn_weights_scratch(ranks, width, part),
        ([] if stream is None else [stream]) + list(jobs),
        collective_id,
        cost(4.8 * tokens * width * ranks * part, tokens * width * 14, tokens * ranks * part),
        "ffn_forward",
    )


def ffn_backward(up, down, grad, middle, branch, hidden, mod, cores=None, jobs=(), collective_id=None):
    tokens, width = middle.shape
    ranks, _, part = hidden.shape
    whole = fixed((tokens, width))
    made = [jax.ShapeDtypeStruct((2, ranks, width, part), jnp.bfloat16)] if cores is None else []
    return call(
        partial(ffn_backward_kernel, 2, cores),
        ranks,
        [up, down, grad, middle, branch, hidden, mod],
        anywhere(2) + [
            fixed(grad.shape), whole, whole,
            pl.BlockSpec((1, tokens, part), lambda step: (step, 0, 0)),
            fixed(mod.shape),
        ],
        [
            jax.ShapeDtypeStruct((tokens, width), jnp.float32),
            jax.ShapeDtypeStruct((ranks, 1, part), jnp.float32),
            jax.ShapeDtypeStruct((4, width), jnp.float32),
        ] + made,
        [
            whole,
            fixed((ranks, 1, part)),
            fixed((4, width)),
        ] + [pl.BlockSpec((2, 1, width, part), lambda step: (0, step, 0, 0))] * len(made),
        ffn_weights_scratch(ranks, width, part) + [
            pltpu.VMEM((width, tokens), jnp.bfloat16),
            pltpu.VMEM((tokens, width), jnp.bfloat16),
            pltpu.VMEM((width, tokens), jnp.bfloat16),
            pltpu.VMEM((tokens, part), jnp.bfloat16),
            pltpu.VMEM((tokens, part), jnp.bfloat16),
            pltpu.VMEM((tokens, width), jnp.float32),
        ],
        ([] if cores is None else [cores]) + list(jobs),
        collective_id,
        cost(9.6 * tokens * width * ranks * part, tokens * width * 20, tokens * ranks * part),
        "ffn_backward",
    )


def attention_backward(weight, grad, stream, saved, mod, stride, swap=None, cores=None, jobs=(), collective_id=None):
    project, mixed, branch = saved
    shape = stream.shape
    width = shape[-1]
    ranks = project.shape[0]
    tokens = shape[0] * shape[1] * shape[2]
    spec = group_spec(shape)
    result = [jax.ShapeDtypeStruct(shape, jnp.float32)] if swap is None else []
    made = [jax.ShapeDtypeStruct((ranks, width, 6 * PAIR), jnp.bfloat16)] if cores is None else []
    return call(
        partial(attention_backward_kernel, stride, swap, cores),
        shape[1],
        [weight, grad, stream, project, mixed, branch, mod],
        anywhere(1) + [
            spec, spec, rank_spec(project.shape), rank_spec(mixed.shape), spec, fixed(mod.shape),
        ],
        result + made + [
            jax.ShapeDtypeStruct((4, width), jnp.float32),
            jax.ShapeDtypeStruct((ranks, 5 * PAIR), jnp.float32),
        ],
        [spec] * len(result) + [fixed((ranks, width, 6 * PAIR))] * len(made) + [
            fixed((4, width)), fixed((ranks, 5 * PAIR)),
        ],
        [
            pltpu.VMEM((ranks, width, 6 * PAIR), jnp.bfloat16),
            pltpu.SemaphoreType.DMA((ranks,)),
            pltpu.VMEM((2, width, tokens), jnp.bfloat16),
            pltpu.VMEM((ranks, tokens, 5 * PAIR), jnp.bfloat16),
            pltpu.VMEM((ranks, tokens, 2 * PAIR), jnp.bfloat16),
        ],
        [job for job in (swap, cores) if job is not None] + list(jobs),
        collective_id,
        cost(16 * tokens * width * width * 1.5, tokens * width * 20),
        "attention_backward",
    )


def pack_heads(block):
    query, key, value, outer = block
    return jnp.concatenate(
        [query[:, :PAIR], key[:, :PAIR], value[:, :PAIR], query[:, PAIR:], key[:, PAIR:],
         value[:, PAIR:], outer[:, PAIR:], outer[:, :PAIR]], axis=1
    )


def unpack_heads(packed):
    part = lambda start, size: packed[:, start : start + size]
    join = lambda first, last: jnp.concatenate([part(first, PAIR), part(last, HD)], axis=1)
    return [join(0, 3 * PAIR), join(PAIR, 3 * PAIR + HD), join(2 * PAIR, 4 * PAIR), join(5 * PAIR, 4 * PAIR + HD)]


def pack_bias(query, value, ranks):
    query, value = query.reshape(ranks, -1), value.reshape(ranks, -1)
    none = jnp.zeros((ranks, PAIR), query.dtype)
    return jnp.concatenate(
        [query[:, :PAIR], none, value[:, :PAIR], query[:, PAIR:], none[:, :HD], value[:, PAIR:], none[:, :HD]],
        axis=1,
    )[:, None]


def unpack_bias(sums):
    query = jnp.concatenate([sums[:, :PAIR], sums[:, 3 * PAIR : 3 * PAIR + HD]], axis=1)
    value = jnp.concatenate([sums[:, 2 * PAIR : 3 * PAIR], sums[:, 4 * PAIR : 4 * PAIR + HD]], axis=1)
    return query.reshape(-1), value.reshape(-1)


def place():
    return lax.axis_index("dp"), lax.axis_index("tensor"), lax.axis_size("dp"), lax.axis_size("tensor")


def greet_all():
    device, rank, dp, tp = place()
    me, count = device * tp + rank, dp * tp
    barrier = pltpu.get_barrier_semaphore()

    def greet(index, carry):
        peer = lax.rem(me + index, count)
        pl.semaphore_signal(
            barrier, inc=1, device_id=(peer // tp, lax.rem(peer, tp)), device_id_type=pl.DeviceIdType.MESH
        )
        return carry

    lax.fori_loop(1, count, greet, 0)
    pl.semaphore_wait(barrier, count - 1)


def push(source, target, send, receive, device, rank):
    pltpu.make_async_remote_copy(
        src_ref=source, dst_ref=target, send_sem=send, recv_sem=receive,
        device_id=(device, rank), device_id_type=pl.DeviceIdType.MESH,
    ).start()


def wait_bytes(ref, semaphore):
    pltpu.make_async_copy(ref, ref, semaphore).wait()


class Where:
    def __init__(self):
        device, rank = lax.axis_index("dp"), lax.axis_index("tensor")
        self.count = lax.axis_size("dp") // 2
        self.device, self.rank = device, rank
        self.far, self.side = device // 2, lax.rem(device, 2)
        self.row, self.core = rank // 2, lax.rem(rank, 2)
        self.other_side = self.far * 2 + 1 - self.side
        self.other_row = (1 - self.row) * 2 + self.core
        self.other_core = self.row * 2 + 1 - self.core

    def ahead(self, step):
        return lax.rem(self.far + step, self.count)

    def line(self, step):
        return self.ahead(step) * 2 + self.side


def greet_neighbours(here):
    barrier = pltpu.get_barrier_semaphore()
    peers = [(here.other_side, here.rank), (here.device, here.other_row), (here.device, here.other_core)]
    peers += [(here.line(step), here.rank) for step in range(1, here.count)]
    for peer in peers:
        pl.semaphore_signal(barrier, inc=1, device_id=peer, device_id_type=pl.DeviceIdType.MESH)
    pl.semaphore_wait(barrier, len(peers))


def add_into(target, left, right):
    target[...] = left[...] + right[...]


class ScatterChain:
    def __init__(self, here, kept, line, lead, scratch):
        self.here, self.kept, self.line, self.lead = here, kept, line, lead
        self.keep, self.first_one, self.last_one, self.first_two, self.last_two, self.semaphores = scratch
        self.rows = line.shape[1]

    @staticmethod
    def scratch(width, columns, dp, lead):
        rows, far = width // dp, dp // 2
        low = lambda *shape: pltpu.VMEM(shape + (columns,), jnp.bfloat16)
        return [
            low(2, width),
            low(2, lead, rows), low(2 * (far - lead) * rows), low(lead, rows), low(far - lead, rows),
            pltpu.SemaphoreType.DMA((6, 2)),
        ]

    def chunk(self, row, far, side):
        return self.keep.at[row, pl.ds(pl.multiple_of((far * 2 + side) * self.rows, self.rows), self.rows)]

    def send(self, slot, source, target, device, rank):
        push(source, target, self.semaphores.at[slot, 0], self.semaphores.at[slot, 1], device, rank)

    def arrived(self, slot, ref):
        wait_bytes(ref, self.semaphores.at[slot, 1])

    def left(self, slot, ref):
        wait_bytes(ref, self.semaphores.at[slot, 0])

    def stage_one(self):
        here, lead = self.here, self.lead
        pltpu.make_async_copy(self.kept, self.keep, self.semaphores.at[5, 0]).start()
        for row in range(2):
            for far in range(lead):
                rows = pl.ds(pl.multiple_of((far * 2 + 1 - here.side) * self.rows, self.rows), self.rows)
                self.send(1, self.kept.at[row, rows], self.first_one.at[row, far], here.other_side, here.rank)
        start, size = lead * 2 * self.rows, (here.count - lead) * 2 * self.rows
        self.send(2, self.kept.at[1 - here.row, pl.ds(start, size)], self.last_one, here.device, here.other_row)

    def stage_two(self):
        here, lead = self.here, self.lead
        wait_bytes(self.keep, self.semaphores.at[5, 0])
        self.arrived(1, self.first_one)
        for row in range(2):
            for far in range(lead):
                mine = self.chunk(row, far, here.side)
                add_into(mine, mine, self.first_one.at[row, far])
        for far in range(lead):
            self.send(3, self.chunk(1 - here.row, far, here.side), self.first_two.at[far], here.device, here.other_row)
        self.arrived(2, self.last_one)
        for far in range(lead, here.count):
            for side in range(2):
                mine = self.chunk(here.row, far, side)
                add_into(mine, mine, self.last_one.at[pl.ds(((far - lead) * 2 + side) * self.rows, self.rows)])
        for far in range(lead, here.count):
            self.send(
                4, self.chunk(here.row, far, 1 - here.side), self.last_two.at[far - lead], here.other_side, here.rank
            )

    def merge(self):
        here = self.here
        self.arrived(3, self.first_two)
        self.arrived(4, self.last_two)
        for far in range(here.count):
            land = self.first_two.at[far] if far < self.lead else self.last_two.at[far - self.lead]
            add_into(self.line.at[far], self.chunk(here.row, far, here.side), land)

    def finish(self):
        self.left(1, self.first_one)
        self.left(2, self.last_one)
        self.left(3, self.first_two)
        self.left(4, self.last_two)


class LineChain:
    def __init__(self, here, line, out, land, semaphores):
        self.here, self.line, self.out, self.land, self.semaphores = here, line, out, land, semaphores

    @staticmethod
    def scratch(far, rows, columns):
        return [pltpu.VMEM((far - 1, rows, columns), jnp.bfloat16), pltpu.SemaphoreType.DMA((2,))]

    def start(self):
        here = self.here
        for step in range(1, here.count):
            push(
                self.line.at[here.ahead(step)], self.land.at[step - 1], self.semaphores.at[0],
                self.semaphores.at[1], here.line(step), here.rank,
            )

    def finish(self):
        wait_bytes(self.land, self.semaphores.at[1])
        total = self.line[self.here.far].astype(jnp.float32)
        for step in range(1, self.here.count):
            total = total + self.land[step - 1].astype(jnp.float32)
        self.out[...] = total
        wait_bytes(self.land, self.semaphores.at[0])


def leave_kernel(mod_start, *refs):
    refs = list(refs)
    scattering = len(refs) > 10
    kept, begun, *done = [refs.pop(0) for _ in range(6 if scattering else 2)]
    if not scattering:
        refs = [kept, begun] + refs
    small_ref, modulation_ref, *refs = refs
    heads_out, wide_out = (refs.pop(0), refs.pop(0)) if scattering else (None, None)
    sum_ref, act_ref, land_ref, acting_ref, semaphores, *space = refs
    device, rank, dp, tp = place()
    me, count = device * tp + rank, dp * tp
    greet_all()
    if scattering:
        here = Where()
        line_ref, out, *space = space
        pick = lambda number: [space.pop(0) for _ in range(number)]
        chains, trails = [], []
        for index in range(PARTS):
            size = out.shape[1] // PARTS
            part = pl.ds(index * size, size)
            line = line_ref.at[index]
            chains.append(ScatterChain(here, kept.at[0, :, :, part], line, here.count // 2, pick(6)))
            trails.append(LineChain(here, line, out.at[:, part], *pick(2)))
        others = [LineChain(here, begun.at[0], wide_out.at[0, 1], *pick(2))]
    for step in range(1, tp):
        there = lax.rem(rank + step, tp)
        push(small_ref.at[there], land_ref.at[rank], semaphores.at[0], semaphores.at[1], device, there)
    land_ref[rank] = small_ref[rank]
    wait_bytes(land_ref.at[pl.ds(0, tp - 1)], semaphores.at[1])
    mine = sum_ref.at[rank]
    mine[device] = jnp.sum(land_ref[...], axis=0)

    def one(step, carry):
        push(mine.at[device], mine.at[device], semaphores.at[2], semaphores.at[3], lax.rem(device + step, dp), rank)
        return carry

    lax.fori_loop(1, dp, one, 0)
    if scattering:
        for chain in others:
            chain.start()
    wait_bytes(mine.at[pl.ds(0, dp - 1)], semaphores.at[3])
    for step in range(1, tp):
        push(mine, mine, semaphores.at[4], semaphores.at[5], device, lax.rem(rank + step, tp))
    if scattering:
        for chain in chains:
            chain.stage_one()
        up_first, up_last, down_last, heads_last = done
        wide_out[0, 0], wide_out[1, 0], wide_out[1, 1] = up_first[0], up_last[0], down_last[0]
        for kind, value in enumerate(unpack_heads(heads_last[0])):
            heads_out[1, kind] = value
        chains[0].stage_two()
    wait_bytes(sum_ref.at[pl.ds(0, tp - 1)], semaphores.at[5])
    layers, padded, columns = modulation_ref.shape
    lines = sum_ref.shape[2]
    total = jnp.zeros((dp, padded), jnp.float32)
    for layer in range(layers):
        for index in range(columns // PAIR):
            line = layer * (tp * lines // layers) + mod_start // PAIR + index
            low = sum_ref[line // lines, :, line % lines, :].astype(jnp.bfloat16)
            total += mm(low, modulation_ref[layer, :, index * PAIR : (index + 1) * PAIR], ((1,), (1,)))
    acting_ref[...] = jnp.concatenate([total, jnp.zeros((dp, PAIR - padded), jnp.float32)], axis=1)
    act_ref[me] = acting_ref[...]

    def tell(index, carry):
        peer = lax.rem(me + index, count)
        push(acting_ref, act_ref.at[me], semaphores.at[6], semaphores.at[7], peer // tp, lax.rem(peer, tp))
        return carry

    lax.fori_loop(1, count, tell, 0)
    if scattering:
        for chain in chains[1:]:
            chain.stage_two()
        for chain, line in zip(chains, trails):
            chain.merge()
            line.start()
        for chain in others:
            chain.finish()
    wait_bytes(act_ref.at[pl.ds(0, count - 1)], semaphores.at[7])
    wait_bytes(act_ref.at[pl.ds(0, count - 1)], semaphores.at[6])
    wait_bytes(land_ref.at[pl.ds(0, tp - 1)], semaphores.at[0])
    wait_bytes(mine.at[pl.ds(0, dp - 1)], semaphores.at[2])
    wait_bytes(sum_ref.at[pl.ds(0, tp - 1)], semaphores.at[4])
    if scattering:
        for chain in chains + trails:
            chain.finish()
        for kind, value in enumerate(unpack_heads(out[...])):
            heads_out[0, kind] = value


def leave(small, modulation, mod_start, kept, begun, done, collective_id):
    tp, lines, lanes = small.shape
    dp = lax.axis_size("dp")
    inside = pl.BlockSpec(memory_space=pltpu.VMEM)
    shapes, space, extra = [], [], []
    if kept is not None:
        _, _, width, columns = kept.shape
        rows, far, part = width // dp, dp // 2, columns // PARTS
        extra = [kept, begun, *done]
        shapes = [
            jax.ShapeDtypeStruct((2, 4, rows, columns // 4), jnp.float32),
            jax.ShapeDtypeStruct((2, 2, rows, columns), jnp.float32),
        ]
        space = [pltpu.VMEM((PARTS, far, rows, part), jnp.bfloat16), pltpu.VMEM((rows, columns), jnp.float32)]
        for _ in range(PARTS):
            space += ScatterChain.scratch(width, part, dp, far // 2) + LineChain.scratch(far, rows, part)
        space += LineChain.scratch(far, rows, columns)
    return pl.pallas_call(
        partial(leave_kernel, mod_start),
        in_specs=([pl.BlockSpec(memory_space=pl.ANY)] + [inside] * 5)[: len(extra)] + [inside, inside],
        out_specs=[inside] * (len(shapes) + 2),
        out_shape=shapes + [
            jax.ShapeDtypeStruct((tp, dp, lines, lanes), jnp.float32),
            jax.ShapeDtypeStruct((dp * tp, dp, lanes), jnp.float32),
        ],
        scratch_shapes=[
            pltpu.VMEM((tp, lines, lanes), jnp.float32),
            pltpu.VMEM((dp, lanes), jnp.float32),
            pltpu.SemaphoreType.DMA((8,)),
        ] + space,
        compiler_params=pltpu.CompilerParams(
            collective_id=collective_id, has_side_effects=True, vmem_limit_bytes=VMEM_LIMIT
        ),
        name="leave",
    )(*extra, small, modulation)


class GatherChain:
    def __init__(self, here, source, out, semaphores, half=None):
        self.here, self.source, self.out, self.semaphores = here, source, out, semaphores
        self.half = here.count // 2 if half is None else half

    @staticmethod
    def scratch():
        return [pltpu.SemaphoreType.DMA((9, 2))]

    def pieces(self, rank, side, first=0, last=None):
        last = self.here.count if last is None else last
        return self.out.at[rank, pl.ds(first, last - first), side]

    def send(self, slot, pieces, device, rank):
        push(pieces, pieces, self.semaphores.at[slot, 0], self.semaphores.at[slot, 1], device, rank)

    def wait(self, slot, way, pieces):
        wait_bytes(self.pieces(0, 0, 0, pieces), self.semaphores.at[slot, way])

    def stage_line(self):
        here = self.here
        mine = self.out.at[here.rank, here.far, here.side]
        pltpu.make_async_copy(self.source, mine, self.semaphores.at[8, 0]).start()
        for step in range(1, here.count):
            push(
                self.source, mine, self.semaphores.at[0, 0], self.semaphores.at[0, 1], here.line(step), here.rank
            )

    def line_arrived(self):
        self.wait(8, 0, 1)
        self.wait(0, 1, self.here.count - 1)

    def line_left(self):
        self.wait(0, 0, self.here.count - 1)

    def stage_near(self):
        here = self.here
        mine = self.pieces(here.rank, here.side)
        self.send(1, mine, here.other_side, here.rank)
        self.send(2, mine, here.device, here.other_row)
        self.send(3, mine, here.device, here.other_core)

    def stage_across(self):
        here, count = self.here, self.here.count
        self.wait(1, 1, count)
        self.send(4, self.pieces(here.rank, 1 - here.side, 0, self.half), here.device, here.other_row)
        self.wait(2, 1, count)
        self.send(5, self.pieces(here.other_row, here.side, self.half, count), here.other_side, here.rank)
        self.send(6, self.pieces(here.rank, 1 - here.side), here.device, here.other_core)
        self.send(7, self.pieces(here.other_row, here.side), here.device, here.other_core)

    def stage_core(self):
        here, count = self.here, self.here.count
        self.wait(4, 1, self.half)
        self.wait(5, 1, count - self.half)
        self.send(8, self.pieces(here.other_row, 1 - here.side), here.device, here.other_core)

    def finish(self):
        count, half = self.here.count, self.half
        for slot in (3, 6, 7, 8):
            self.wait(slot, 1, count)
        for slot, pieces in ((1, count), (2, count), (3, count), (4, half), (5, count - half), (6, count), (7, count)):
            self.wait(slot, 0, pieces)
        self.wait(8, 0, count)


def column_parts(here, source, out, semaphores, half=None):
    size = out.shape[4] // PARTS
    chains = []
    for index, semaphore in enumerate(semaphores):
        part = pl.ds(index * size, size)
        shard = None if source is None else source.at[:, part]
        chains.append(GatherChain(here, shard, out.at[:, :, :, :, part], semaphore, half))
    return chains


class Job:
    operands, sources, shapes, specs, aliases, space = (), None, (), (), {}, ()
    stages, last = {}, ()


def anywhere(count):
    return [pl.BlockSpec(memory_space=pl.ANY)] * count


class CoreJob(Job):
    def __init__(self, kinds, width, columns):
        block = (kinds, width, columns)
        self.shapes, self.specs = [jax.ShapeDtypeStruct((kinds, 2, width, columns), jnp.bfloat16)], anywhere(1)
        self.space = [
            pltpu.VMEM((2,) + block, jnp.bfloat16),
            pltpu.VMEM((2,) + block, jnp.bfloat16),
            pltpu.SemaphoreType.DMA((4, kinds)),
        ]

    def bind(self, here, inputs, outputs, space):
        self.here, self.kept, (self.buffer, self.land, self.semaphores) = here, outputs[0], space
        self.stages = {}
        self.last = [
            partial(self.sent, own, kind) for own in range(2) for kind in range(self.buffer.shape[1])
        ]

    def sent(self, own, kind):
        wait_bytes(self.buffer.at[own, kind], self.semaphores.at[own, kind])

    def rank(self, turn):
        return turn_of(turn)

    def put(self, turn, kind, make):
        row, own = turn // 2, lax.rem(turn, 2)

        @pl.when(turn >= 2)
        def _():
            self.sent(own, kind)

        @pl.when(own == 0)
        def _():
            self.buffer[0, kind] = make().astype(jnp.bfloat16)

        @pl.when(own == 1)
        def _():
            wait_bytes(self.land.at[row, kind], self.semaphores.at[2 + row, kind])
            self.buffer[1, kind] = (make() + self.land[row, kind].astype(jnp.float32)).astype(jnp.bfloat16)

    def send(self, turn, kind):
        here, row, own = self.here, turn // 2, lax.rem(turn, 2)

        @pl.when(own == 0)
        def _():
            push(
                self.buffer.at[0, kind], self.land.at[row, kind], self.semaphores.at[0, kind],
                self.semaphores.at[2 + row, kind], here.device, here.other_core,
            )

        @pl.when(own == 1)
        def _():
            pltpu.make_async_copy(
                self.buffer.at[1, kind], self.kept.at[kind, row], self.semaphores.at[1, kind]
            ).start()


class ScatterJob(Job):
    def __init__(self, grads, lead, close=False):
        _, _, width, columns = grads[0][0].shape
        dp = lax.axis_size("dp")
        far, rows = dp // 2, width // dp
        self.lead, self.close, self.kinds = lead, close, [kind for _, kind in grads]
        self.operands = [array for array, _ in grads]
        shape = (len(grads) - close, far, rows, columns)
        self.shapes, self.specs = [jax.ShapeDtypeStruct(shape, jnp.bfloat16)], [fixed(shape)]
        self.space = ScatterChain.scratch(width, columns, dp, lead) * len(grads)
        if close:
            self.shapes.append(jax.ShapeDtypeStruct((1, rows, columns), jnp.float32))
            self.specs.append(fixed((1, rows, columns)))
            self.space = [pltpu.VMEM((far, rows, columns), jnp.bfloat16)] + LineChain.scratch(
                far, rows, columns
            ) + self.space

    def bind(self, here, inputs, outputs, space):
        lines = [outputs[0].at[index] for index in range(outputs[0].shape[0])]
        if self.close:
            own, land, semaphores, *space = space
            lines.insert(0, own)
            line = LineChain(here, own, outputs[1].at[0], land, semaphores)
        size = len(space) // len(inputs)
        chains = [
            ScatterChain(
                here, inputs[index].at[kind], lines[index], self.lead, space[index * size : (index + 1) * size]
            )
            for index, kind in enumerate(self.kinds)
        ]
        one = chains[0]
        if len(chains) == 1:
            self.stages = {(0, 0): [one.stage_one], (2, 0): [one.stage_two]}
            self.last = [one.merge, one.finish]
            return
        two = chains[1]
        if self.close:
            self.stages = {
                (0, 0): [one.stage_one], (1, 1): [one.stage_two], (2, 0): [one.merge, line.start, two.stage_one],
                (3, 1): [two.stage_two],
            }
            self.last = [line.finish, two.merge, one.finish, two.finish]
            return
        self.stages = {
            (0, 0): [one.stage_one, two.stage_one], (1, 3): [one.stage_two], (3, 1): [two.stage_two],
        }
        self.last = [one.merge, two.merge, one.finish, two.finish]


class LineJob(Job):
    def __init__(self, line):
        kinds, far, rows, columns = line.shape
        shape = (kinds, rows, columns)
        self.operands, self.sources = [line], [fixed(line.shape)]
        self.shapes, self.specs = [jax.ShapeDtypeStruct(shape, jnp.float32)], [fixed(shape)]
        self.space = LineChain.scratch(far, rows, columns) * kinds

    def bind(self, here, inputs, outputs, space):
        chains = [
            LineChain(here, inputs[0].at[kind], outputs[0].at[kind], *space[2 * kind : 2 * kind + 2])
            for kind in range(outputs[0].shape[0])
        ]
        self.stages = {(0, 0): [chain.start for chain in chains]}
        self.last = [chain.finish for chain in chains]


class FlowJob(Job):
    def __init__(self, spread, lines, half=None, late=()):
        dp, tp = lax.axis_size("dp"), lax.axis_size("tensor")
        self.counts, self.half = (len(spread), len(late)), half
        shards = list(late) + list(lines)
        self.operands = list(spread) + shards
        self.shapes = [jax.ShapeDtypeStruct(v.shape, v.dtype) for v in spread]
        self.shapes += [jax.ShapeDtypeStruct((tp, dp // 2, 2) + v.shape, v.dtype) for v in shards]
        self.specs = anywhere(len(self.shapes))
        self.aliases = {index: index for index in range(len(spread))}
        self.space = GatherChain.scratch() * (PARTS * len(self.shapes))

    def bind(self, here, inputs, outputs, space):
        first, late = self.counts
        chains = [
            column_parts(
                here, inputs[index] if index >= first else None, outputs[index],
                space[index * PARTS : (index + 1) * PARTS], self.half,
            )
            for index in range(len(inputs))
        ]
        spread, late, lines = (
            [chain for group in chosen for chain in group]
            for chosen in (chains[:first], chains[first : first + late], chains[first + late :])
        )
        self.stages = {(0, 0): [chain.stage_near for chain in spread]}
        self.stages[0, 0] += [chain.stage_line for chain in late + lines]
        for index, spot in zip(range(PARTS), ((1, 1), (2, 0), (3, 0))):
            self.stages[spot] = [chain.stage_across for chain in spread[index::PARTS]]
            for chain in late[index::PARTS]:
                self.stages[spot] += [chain.line_arrived, chain.stage_near]
        self.last = [chain.stage_across for chain in late]
        self.last += [chain.stage_core for chain in spread + late]
        self.last += [chain.finish for chain in spread + late]
        self.last += [chain.line_arrived for chain in lines]
        self.last += [chain.line_left for chain in late + lines]


class SwapJob(Job):
    def __init__(self, tokens, to_frames):
        self.to_frames = to_frames
        self.operands = [tokens]
        shape = tokens.shape
        shape = (shape[2], shape[0], shape[1]) + shape[3:] if to_frames else (shape[1], shape[2], shape[0]) + shape[3:]
        self.shapes, self.specs = [jax.ShapeDtypeStruct(shape, tokens.dtype)], anywhere(1)
        self.space = [pltpu.SemaphoreType.DMA((3,))]

    def bind(self, here, inputs, outputs, space):
        source, out, semaphores = inputs[0], outputs[0], space[0]
        frames, ranks = out.shape[:2] if self.to_frames else (out.shape[2], out.shape[0])
        few = pl.ds(0, ranks - 1)
        most, mine = (out.at[:, few], out.at[:, 0]) if self.to_frames else (out.at[few], out.at[0])

        def ends(frame, there):
            if self.to_frames:
                return source.at[there, :, frame], out.at[frame, here.rank]
            return source.at[frame, there], out.at[here.rank, :, frame]

        def start():
            for frame in range(frames):
                pltpu.make_async_copy(*ends(frame, here.rank), semaphores.at[2]).start()
            for step in range(1, ranks):
                there = lax.rem(here.rank + step, ranks)
                for frame in range(frames):
                    push(*ends(frame, there), semaphores.at[0], semaphores.at[1], here.device, there)

        def finish():
            wait_bytes(mine, semaphores.at[2])
            wait_bytes(most, semaphores.at[1])
            wait_bytes(most, semaphores.at[0])

        self.stages, self.last = {(0, 0): [start]}, [finish]


class StreamJob(Job):
    def __init__(self, shape, frames):
        self.shape, self.frames = shape, frames
        self.shapes, self.specs = [jax.ShapeDtypeStruct(shape, jnp.bfloat16)], anywhere(1)
        ranks, groups, rows, width = shape
        block = (groups, ranks, rows, width)
        if frames:
            block = (frames, ranks, groups, rows // frames, width)
        self.space = [pltpu.VMEM(block, jnp.bfloat16), pltpu.SemaphoreType.DMA((3,))]

    def bind(self, here, inputs, outputs, space):
        self.here, self.out = here, outputs[0]
        self.buffer, self.semaphores = space
        ranks = self.shape[0]

        def finish():
            wait_bytes(self.out.at[0], self.semaphores.at[2])
            wait_bytes(self.out.at[pl.ds(0, ranks - 1)], self.semaphores.at[1])
            wait_bytes(self.out.at[pl.ds(0, ranks - 1)], self.semaphores.at[0])

        self.stages, self.last = {}, [finish]

    def put(self, step, value):
        here, ranks = self.here, self.shape[0]
        size = self.buffer.size // self.buffer.shape[0] // value.shape[1]
        if value.shape[0] > size:
            count = value.shape[0] // size
            for index in range(count):
                self.put(step * count + index, value[index * size : (index + 1) * size])
            return
        self.buffer[step] = value.reshape(self.buffer.shape[1:]).astype(jnp.bfloat16)
        if self.frames:
            strip = self.buffer.shape[3]
            target = self.out.at[here.rank, :, pl.ds(pl.multiple_of(step * strip, strip), strip)]
        else:
            target = self.out.at[here.rank, step]
        pltpu.make_async_copy(self.buffer.at[step, here.rank], target, self.semaphores.at[2]).start()
        for ahead in range(1, ranks):
            there = lax.rem(here.rank + ahead, ranks)
            push(
                self.buffer.at[step, there], target, self.semaphores.at[0], self.semaphores.at[1],
                here.device, there,
            )


def greet_jobs(here):
    barrier = pltpu.get_barrier_semaphore()
    ranks = lax.axis_size("tensor")
    peers = [(here.other_side, here.rank)]
    peers += [(here.line(step), here.rank) for step in range(1, here.count)]
    peers += [(here.device, lax.rem(here.rank + step, ranks)) for step in range(1, ranks)]
    for peer in peers:
        pl.semaphore_signal(barrier, inc=1, device_id=peer, device_id_type=pl.DeviceIdType.MESH)
    pl.semaphore_wait(barrier, len(peers))


def call(body, steps, arguments, in_specs, out_shape, out_specs, scratch, jobs, collective_id, estimate, name):
    operands = [v for job in jobs for v in job.operands]
    sources = [v for job in jobs for v in (job.sources or anywhere(len(job.operands)))]
    shapes = [v for job in jobs for v in job.shapes]
    specs = [v for job in jobs for v in job.specs]
    space = [v for job in jobs for v in job.space]
    aliases, before, after = {}, len(arguments), len(out_shape)
    for job in jobs:
        for source, target in job.aliases.items():
            aliases[before + source] = after + target
        before, after = before + len(job.operands), after + len(job.shapes)

    def kernel(*refs):
        refs = list(refs)
        take = lambda number: [refs.pop(0) for _ in range(number)]
        inputs, job_inputs = take(len(arguments)), take(len(operands))
        outputs, job_outputs = take(len(out_shape)), take(len(shapes))
        own, job_space = take(len(scratch)), refs
        step = pl.program_id(0)
        if jobs:
            here = Where()
            for job in jobs:
                pick = lambda pool, number: [pool.pop(0) for _ in range(number)]
                job.bind(
                    here, pick(job_inputs, len(job.operands)), pick(job_outputs, len(job.shapes)),
                    pick(job_space, len(job.space)),
                )

        def hook(spot):
            for index in range(steps):
                todo = [
                    stage
                    for job in jobs
                    for (late, place), stages in sorted(job.stages.items())
                    if (late * 4 + place) * steps // 4 == index * 4 + spot
                    for stage in stages
                ]
                if todo or (jobs and spot == 0 and index == 0):

                    @pl.when(step == index)
                    def _():
                        if index == 0 and spot == 0:
                            greet_jobs(here)
                        for stage in todo:
                            stage()

        hook(0)
        body(lambda spot: hook(spot) if spot else None, *inputs, *outputs, *own)
        if jobs:

            @pl.when(step == steps - 1)
            def _():
                for job in jobs:
                    for stage in job.last:
                        stage()

    more = {"collective_id": collective_id, "has_side_effects": True} if jobs else {}
    return pl.pallas_call(
        kernel,
        grid=(steps,),
        in_specs=list(in_specs) + sources,
        out_specs=list(out_specs) + specs,
        out_shape=list(out_shape) + shapes,
        scratch_shapes=list(scratch) + space,
        input_output_aliases=aliases,
        compiler_params=pltpu.CompilerParams(
            vmem_limit_bytes=VMEM_LIMIT, dimension_semantics=("arbitrary",), **more
        ),
        cost_estimate=estimate,
        name=name,
    )(*arguments, *operands)


def entry_kernel(
    per_device, swap, row_ref, modulation_ref, *refs
):
    gather = 3 if len(refs) > 5 else 0
    refs = list(refs)
    sources = [refs.pop(0) for _ in range(gather)]
    gathered_ref, mod_ref = refs.pop(0), refs.pop(0)
    targets = [refs.pop(0) for _ in range(gather)]
    part_ref, land_ref, semaphores, *space = refs
    device, rank, dp, tp = place()
    me, count = device * tp + rank, dp * tp
    lines = land_ref.shape[1]
    if gather:
        here = Where()
        parts = column_parts(here, sources[0], targets[0], space[:PARTS])
        following = GatherChain(here, sources[1], targets[1], space[PARTS])
        swap.bind(here, sources[2:], targets[2:], space[PARTS + 1 :])
    greet_all()

    def tell(index, carry):
        peer = lax.rem(me + index, count)
        push(
            row_ref, gathered_ref.at[me], semaphores.at[0], semaphores.at[1], peer // tp, lax.rem(peer, tp)
        )
        return carry

    lax.fori_loop(1, count, tell, 0)
    gathered_ref[me] = row_ref[...]
    if gather:
        for chain in parts:
            chain.stage_line()
        for stage in swap.stages[0, 0]:
            stage()
    wait_bytes(gathered_ref.at[pl.ds(0, count - 1)], semaphores.at[1])
    padded = modulation_ref.shape[1]
    width = dp * tp * per_device
    chosen = jnp.zeros((count, padded), jnp.float32)
    row = lax.broadcasted_iota(jnp.int32, (PAIR, padded), 0)
    column = lax.broadcasted_iota(jnp.int32, (PAIR, padded), 1)
    for index in range(width // PAIR):
        match = (row + index * PAIR == column + me * per_device) & (column < per_device)
        chosen += mm(
            gathered_ref[:, index, :].astype(jnp.bfloat16), jnp.where(match, 1.0, 0.0).astype(jnp.bfloat16)
        )
    clip = lax.broadcasted_iota(jnp.int32, (dp, count), 0)
    member = lax.broadcasted_iota(jnp.int32, (dp, count), 1)
    leaders = jnp.where(member == clip * tp, 1.0, 0.0).astype(jnp.bfloat16)
    rows = mm(leaders, chosen.astype(jnp.bfloat16)).astype(jnp.bfloat16)
    for layer in range(modulation_ref.shape[0]):
        part = mm(rows, modulation_ref[layer])
        size = part.shape[1] // PAIR
        for index in range(size):
            line = layer * size + index
            part_ref[:, line // lines, line % lines, :] = part[:, index * PAIR : (index + 1) * PAIR]

    def share(index, carry):
        peer = lax.rem(me + index, count)
        there, lane = peer // tp, lax.rem(peer, tp)
        push(part_ref.at[there, lane], land_ref.at[me], semaphores.at[2], semaphores.at[3], there, lane)
        return carry

    lax.fori_loop(1, count, share, 0)
    land_ref[me] = part_ref[device, rank]
    if gather:
        for chain in parts:
            chain.line_arrived()
            chain.stage_near()
        following.stage_line()
        for chain in parts:
            chain.stage_across()
    wait_bytes(land_ref.at[pl.ds(0, count - 1)], semaphores.at[3])
    mod_ref[rank] = jnp.sum(land_ref[...], axis=0)
    for step in range(1, tp):
        push(
            mod_ref.at[rank], mod_ref.at[rank], semaphores.at[4], semaphores.at[5], device, lax.rem(rank + step, tp)
        )
    if gather:
        for chain in parts:
            chain.stage_core()
    wait_bytes(gathered_ref.at[pl.ds(0, count - 1)], semaphores.at[0])
    wait_bytes(land_ref.at[pl.ds(0, count - 1)], semaphores.at[2])
    wait_bytes(mod_ref.at[pl.ds(0, tp - 1)], semaphores.at[5])
    wait_bytes(mod_ref.at[pl.ds(0, tp - 1)], semaphores.at[4])
    if gather:
        following.line_arrived()
        for chain in parts:
            chain.finish()
        for chain in (*parts, following):
            chain.line_left()
        for stage in swap.last:
            stage()


def enter(row, modulation, per_device, weights, swap, collective_id):
    dp, tp = lax.axis_size("dp"), lax.axis_size("tensor")
    count = dp * tp
    lines = modulation.shape[0] * modulation.shape[2] // (tp * PAIR)
    inside = pl.BlockSpec(memory_space=pltpu.VMEM)
    job = FlowJob((), weights) if weights else Job()
    swap = swap if weights else Job()
    return pl.pallas_call(
        partial(entry_kernel, per_device, swap),
        in_specs=[inside, inside] + anywhere(len(job.operands) + len(swap.operands)),
        out_specs=[inside, inside] + list(job.specs) + list(swap.specs),
        out_shape=[
            jax.ShapeDtypeStruct((count,) + row.shape, jnp.float32),
            jax.ShapeDtypeStruct((tp, lines, PAIR), jnp.float32),
        ] + list(job.shapes) + list(swap.shapes),
        scratch_shapes=[
            pltpu.VMEM((dp, tp, lines, PAIR), jnp.float32),
            pltpu.VMEM((count, lines, PAIR), jnp.float32),
            pltpu.SemaphoreType.DMA((6,)),
        ] + (GatherChain.scratch() * (PARTS + 1) if weights else []) + list(swap.space),
        compiler_params=pltpu.CompilerParams(
            collective_id=collective_id, has_side_effects=True, vmem_limit_bytes=VMEM_LIMIT
        ),
        name="enter",
    )(row, modulation, *job.operands, *swap.operands)


def adam_update(weight, first, second, grad, rate, decay):
    first_new = BETA_ONE * first + (1.0 - BETA_ONE) * grad
    second_new = BETA_TWO * second + (1.0 - BETA_TWO) * grad * grad
    corrected = (
        first_new
        / (1.0 - BETA_ONE**STEP)
        / (jnp.sqrt(second_new / (1.0 - BETA_TWO**STEP)) + ADAM_EPS)
    )
    weight_new = weight - rate * (corrected + decay * weight)
    return (weight_new, first_new, second_new, weight_new.astype(jnp.bfloat16))


def dot32(form, left, right):
    return jnp.einsum(form, left, right, preferred_element_type=jnp.float32)


def exchange(blocks):
    return lax.all_to_all(blocks, "tensor", split_axis=0, concat_axis=0, tiled=True)


def gather_plain(shard):
    rows, width = shard.shape
    whole = lax.all_gather(shard, ("tensor", "dp"), axis=0, tiled=True)
    return whole.reshape(-1, lax.axis_size("dp") * rows, width)


def scatter_plain(grads):
    kinds, ranks, width, cols = grads.shape
    flat = grads.reshape(kinds, ranks * width, cols)
    summed = lax.psum_scatter(flat, ("tensor", "dp"), scatter_dimension=1, tiled=True)
    return summed.astype(jnp.float32)


def per_device(
    clips, cotangent, timesteps, labels, time_table, class_table,
    attention_weights, attention_first, attention_second,
    ffn_weights, ffn_first, ffn_second,
    modulation_weights, modulation_first, modulation_second,
    bias_vectors, bias_first, bias_second,
):
    layers, kinds, rows, cols = attention_weights.shape
    _, frames, patches, width = clips.shape
    mod_rows = modulation_weights.shape[1]
    bias_cols = bias_vectors.shape[1]
    dp, tp = lax.axis_size("dp"), lax.axis_size("tensor")
    position = lax.axis_index("dp") * tp + lax.axis_index("tensor")
    tokens = frames * patches
    strip = patches // (tp * frames)
    blocks = (tp, frames, frames * strip, width)
    pieces = (tp * frames, frames, strip, width)

    embed = time_table[timesteps] + class_table[labels]
    cond_act = jax.nn.silu(embed).astype(jnp.bfloat16)
    fused = rows % 16 == 0
    shards = [
        (
            pack_heads(attention_weights[layer].astype(jnp.bfloat16)),
            ffn_weights[layer, 0].astype(jnp.bfloat16),
            ffn_weights[layer, 1].astype(jnp.bfloat16),
        )
        for layer in range(layers)
    ]
    low = bias_vectors.astype(jnp.bfloat16).reshape(-1)
    row = jnp.concatenate([cond_act[0], low]).astype(jnp.float32)
    row = jnp.pad(row, (0, -row.shape[0] % 1024)).reshape(-1, 128)
    modulation_low = modulation_weights.astype(jnp.bfloat16)
    modulation_low = jnp.pad(modulation_low, ((0, 0), (0, -mod_rows % 32), (0, 0)))
    gathered, mod, *begun = enter(row, modulation_low, mod_rows, shards[0][:2] if fused else None,
        SwapJob(cotangent.reshape(frames, tp, frames, strip, width), False), 0,
    )
    gathered = gathered.reshape(dp * tp, -1)
    cond_all = gathered[::tp, :width].astype(jnp.bfloat16)
    bias_low = gathered[:, width : width + layers * bias_cols].reshape(dp * tp, layers, bias_cols)
    bias_low = bias_low.transpose(1, 0, 2).reshape(layers, -1)
    cond_rows = lax.dynamic_slice_in_dim(cond_all, position * mod_rows, mod_rows, axis=1)
    cond_rows = jnp.pad(cond_rows, ((0, 0), (0, -mod_rows % 32)))
    mod = mod.reshape(layers, -1)
    mod_width = mod.shape[-1]
    mod = (mod + bias_low[:, -mod_width:]).reshape(layers, 6, width)
    hidden_width = bias_low.shape[1] - mod_width - 4 * width
    bias_up = bias_low[:, 3 * width : 3 * width + hidden_width].reshape(layers, tp, 1, -1)
    bias_out = bias_low[:, None, 2 * width : 3 * width]
    bias_down = bias_low[:, None, 3 * width + hidden_width : 4 * width + hidden_width]
    bias_project = [
        pack_bias(bias_low[layer, :width], bias_low[layer, width : 2 * width], tp) for layer in range(layers)
    ]

    by_patch = lambda v: v.reshape(frames, tp * frames, strip, width).transpose(1, 0, 2, 3)
    first = clips[0].reshape(1, frames, patches, width)

    whole = lambda weight: weight.reshape(tp, width, -1)
    attend = lambda layer, weight, stream, stride, *more: attention_forward(
        whole(weight), stream, mod[layer], bias_project[layer], bias_out[layer], stride, *more
    )
    expand = lambda layer, up, down, middle, *more: ffn_forward(
        whole(up), whole(down), middle.reshape(tokens, width), mod[layer], bias_down[layer], bias_up[layer], *more
    )
    if fused:
        attention_a, up_a, cot = begun
        *heads_a, middle_a, up_a, down_a, attention_b = attend(
            0, attention_a, first, 0, [FlowJob([up_a], [shards[1][0]], None, [shards[0][2]])], 1
        )
        hidden_a, pushed_a, second, attention_b, up_b, down_b = expand(
            0, up_a, down_a, middle_a, StreamJob(blocks, frames),
            [FlowJob([attention_b], [shards[1][2]], dp // 8, [shards[1][1]])], 2, True,
        )
        *heads_b, middle_b, down_b = attend(1, attention_b, second, strip, [FlowJob([down_b], [])], 3)
        hidden_b, pushed_b, result = expand(1, up_b, down_b, middle_b, None, [], None, True)
        attention_a, up_a, down_a = whole(attention_a), whole(up_a), whole(down_a)
        attention_b, up_b, down_b = whole(attention_b), whole(up_b), whole(down_b)
    else:
        (attention_a, up_a, down_a), (attention_b, up_b, down_b) = [[gather_plain(v) for v in group] for group in shards]
        *heads_a, middle_a = attend(0, attention_a, first, 0)
        hidden_a, pushed_a, second = expand(0, up_a, down_a, middle_a)
        second = exchange(by_patch(second).reshape(blocks))
        *heads_b, middle_b = attend(1, attention_b, second, strip)
        hidden_b, pushed_b, result = expand(1, up_b, down_b, middle_b)
        cot = exchange(by_patch(cotangent[0]).reshape(blocks))
    middle_a, middle_b = middle_a.reshape(tokens, width), middle_b.reshape(tokens, width)
    cot = cot.reshape(tokens, width)

    if fused:
        ffn_cores = lambda: CoreJob(2, width, ffn_weights.shape[-1])
        head_cores = lambda: CoreJob(1, width, kinds * cols)
        grad, *sums_b, kept, result = ffn_backward(
            up_b, down_b, cot, middle_b, pushed_b, hidden_b, mod[1], ffn_cores(),
            [SwapJob(result.reshape(tp, frames, frames, strip, width), True)], 5,
        )
        output = result.reshape(clips.shape)
        ffn_grad = kept
        *more_b, grad, kept, line_up = attention_backward(
            attention_b, grad.reshape(blocks), second, heads_b, mod[1], strip,
            StreamJob(blocks, 0), head_cores(), [ScatterJob([(ffn_grad, 0)], 3 * dp // 8)], 6,
        )
        waiting = [(ffn_grad, 1), (kept, 0)]
        grad, *sums_a, kept, done_up, line_b = ffn_backward(
            up_a, down_a, grad.reshape(pieces), middle_a, pushed_a, hidden_a, mod[0], ffn_cores(),
            [LineJob(line_up), ScatterJob(waiting, dp // 4)], 7,
        )
        ffn_grad = kept
        grad, *more_a, kept, done_b, line_ffn_a, done_up_a = attention_backward(
            attention_a, grad.reshape(first.shape), first, heads_a, mod[0], 0, None, head_cores(),
            [LineJob(line_b), ScatterJob([(ffn_grad, 0), (ffn_grad, 1)], dp // 4, True)], 8,
        )
        packed_a = kept
        done = (done_up_a, done_up, done_b[:1], done_b[1:])
    else:
        result = exchange(result.reshape(blocks)).reshape(pieces)
        output = result.transpose(1, 0, 2, 3).reshape(clips.shape)
        grad, *sums_b, ffn_grad = ffn_backward(up_b, down_b, cot, middle_b, pushed_b, hidden_b, mod[1])
        done_ffn_b = scatter_plain(ffn_grad)
        grad, packed_b, *more_b = attention_backward(
            attention_b, grad.reshape(blocks), second, heads_b, mod[1], strip
        )
        done_b = scatter_plain(packed_b[None])
        grad = exchange(grad.astype(jnp.bfloat16))
        grad, *sums_a, ffn_grad = ffn_backward(up_a, down_a, grad.reshape(pieces), middle_a, pushed_a, hidden_a, mod[0])
        done_ffn_a = scatter_plain(ffn_grad)
        grad, packed_a, *more_a = attention_backward(attention_a, grad.reshape(first.shape), first, heads_a, mod[0], 0)
        done_a = scatter_plain(packed_a[None])
    input_grad = grad.reshape(clips.shape)

    def gather_small(more, sums):
        attention_sums, project_sum = more
        up_sum, low_sums = sums
        return jnp.concatenate(
            [*unpack_bias(project_sum), attention_sums[0], up_sum.reshape(-1), low_sums[0],
             attention_sums[1:].reshape(-1), low_sums[1:].reshape(-1)]
        )

    small = jnp.stack([gather_small(more_a, sums_a), gather_small(more_b, sums_b)])
    token_width = small.shape[1] - mod_width
    *summed, small, grad_act = leave(
        small.reshape(tp, -1, 128), modulation_low, token_width,
        *((packed_a, line_ffn_a, done) if fused else (None, None, None)), 9,
    )
    small = small.transpose(1, 0, 2, 3).reshape(dp, layers, -1)
    grad_mod_low = small[..., token_width:].astype(jnp.bfloat16)
    grad_bias_all = jnp.concatenate(
        [small[..., :token_width], grad_mod_low.astype(jnp.float32)], axis=-1
    ).sum(axis=0)
    grad_bias = lax.dynamic_slice_in_dim(grad_bias_all, position * bias_cols, bias_cols, axis=1)
    grad_mod_weight = dot32("ck,cle->lke", cond_rows, grad_mod_low)[:, :mod_rows]
    grad_act = lax.dynamic_index_in_dim(
        grad_act[:, :, :mod_rows], lax.axis_index("dp"), axis=1, keepdims=False
    )
    if fused:
        grad_attention, grad_ffn = summed
    else:
        grad_attention = jnp.stack([jnp.stack(unpack_heads(done[0])) for done in (done_a, done_b)])
        grad_ffn = jnp.stack([done_ffn_a, done_ffn_b])
    silu_value, silu_pull = jax.vjp(jax.nn.silu, embed)
    cond_grad = silu_pull(grad_act.reshape(1, width))[0]

    return (output, input_grad, cond_grad) + (
        adam_update(attention_weights, attention_first, attention_second, grad_attention, MATRIX_RATE, MATRIX_DECAY)
        + adam_update(ffn_weights, ffn_first, ffn_second, grad_ffn, MATRIX_RATE, MATRIX_DECAY)
        + adam_update(modulation_weights, modulation_first, modulation_second, grad_mod_weight, MATRIX_RATE, MATRIX_DECAY)
        + adam_update(bias_vectors, bias_first, bias_second, grad_bias, VECTOR_RATE, 0.0)
    )


def solution(mesh):
    tokens = P("dp", "tensor", None, None)
    matrix = P(None, None, "dp", "tensor")
    modulation = P(None, BOTH, None)
    vector = P(None, BOTH)
    return jax.shard_map(
        per_device,
        mesh=mesh,
        in_specs=(tokens, tokens, P("dp"), P("dp"), P(), P())
        + (matrix,) * 6 + (modulation,) * 3 + (vector,) * 3,
        out_specs=(tokens, tokens, P("dp", None)) + (matrix,) * 8 + (modulation,) * 4 + (vector,) * 4,
        check_vma=False,
    )
```
